128 devices in a mesh: section: 2 (over z_hi), dp: 64 (over z_lo, x, y, core).
Axes of the slice: x: 4, y: 4, z: 4 (z_hi: 2, z_lo: 2; z = z_hi * 2 + z_lo), core: 2. Of those that a mesh axis runs over, the one named last changes fastest.
Arguments:
- content_in: bfloat16 [16384, 768], P('dp'), may hold values from -6 to 6
- query_in: bfloat16 [2432, 768], P('dp'), may hold values from -6 to 6
- content_cot: bfloat16 [16384, 768], P('dp'), may hold values from -6 to 6
- query_cot: bfloat16 [2432, 768], P('dp'), may hold values from -6 to 6
- order_rank: int32 [128, 128], P('dp'), may hold values from 0 to 127, each once within a row
- query_pos: int32 [128, 19], P('dp'), may hold values from 0 to 127, as said below
- group_tag: int32 [128, 128], P('dp'), may hold values from 0 to 2, as said below
- w_query: bfloat16 [2, 768, 768], P('section'), may hold values from -0.3125 to 0.3125
- b_query: float32 [2, 768], P('section'), may hold values from -3 to 3
- w_key: bfloat16 [2, 768, 768], P('section'), may hold values from -0.21875 to 0.21875
- w_value: bfloat16 [2, 768, 768], P('section'), may hold values from -0.21875 to 0.21875
- b_value: float32 [2, 768], P('section'), may hold values from -3 to 3
- w_out: bfloat16 [2, 768, 768], P('section'), may hold values from -0.875 to 0.875
- b_out: float32 [2, 768], P('section'), may hold values from -3 to 3
- norm1_gain: float32 [2, 768], P('section'), may hold values from 0.5 to 1.5
- norm1_bias: float32 [2, 768], P('section'), may hold values from -2 to 2
- w_expand: bfloat16 [2, 768, 3072], P('section'), may hold values from -0.21875 to 0.21875
- b_expand: float32 [2, 3072], P('section'), may hold values from -3 to 3
- w_contract: bfloat16 [2, 3072, 768], P('section'), may hold values from -0.109375 to 0.109375
- b_contract: float32 [2, 768], P('section'), may hold values from -3 to 3
- norm2_gain: float32 [2, 768], P('section'), may hold values from 0.5 to 1.5
- norm2_bias: float32 [2, 768], P('section'), may hold values from -2 to 2
- rel_table: float32 [32, 12], replicated, may hold values from -6 to 6
Outputs:
- content_ends: float32 [2, 16384, 768], P('section', 'dp')
- query_ends: float32 [2, 2432, 768], P('section', 'dp')
- grad_w_query: float32 [2, 768, 768], P('section')
- grad_b_query: float32 [2, 768], P('section')
- grad_w_key: float32 [2, 768, 768], P('section')
- grad_w_value: float32 [2, 768, 768], P('section')
- grad_b_value: float32 [2, 768], P('section')
- grad_w_out: float32 [2, 768, 768], P('section')
- grad_b_out: float32 [2, 768], P('section')
- grad_norm1_gain: float32 [2, 768], P('section')
- grad_norm1_bias: float32 [2, 768], P('section')
- grad_w_expand: float32 [2, 768, 3072], P('section')
- grad_b_expand: float32 [2, 3072], P('section')
- grad_w_contract: float32 [2, 3072, 768], P('section')
- grad_b_contract: float32 [2, 768], P('section')
- grad_norm2_gain: float32 [2, 768], P('section')
- grad_norm2_bias: float32 [2, 768], P('section')
- grad_rel_table: float32 [32, 12], replicated
The draws below stay inside these ranges and needn't reach their ends.
Inputs may be any that keep to these rules, and one draw needn't show every extreme that they name: `query_pos`: each sequence's 19 entries are distinct positions. `group_tag`: tags never fall along a sequence; each sequence holds three groups of 32 or more positions.
All inputs are finite; a program needn't handle non-finite values.
Results may differ from the reference program's by a relative error of at most 0.025.
Values may be sent and summed in bfloat16 or wider, within the bound.
No kernel may reach another device: no remote copies, remote signals or barrier semaphores. Data moves between devices by JAX's collectives and lax.ppermute only.
A program may use at most 256 MiB of HBM per device.

```python
import math
import jax
import jax.numpy as jnp
from jax import lax

D = 768
H = 12
HD = 64
FF = 3072
NB = 32
L = 128
P_SIZE = 19
SEQS = 128
TOKENS = 16384
QROWS = 2432


def draw_query_pos(key, part):
    key = jax.random.fold_in(key, 11)
    row_keys = jax.random.split(key, SEQS)
    orders = jax.vmap(lambda row_key: jax.random.permutation(row_key, L))(row_keys)
    chosen = orders[:, :P_SIZE].astype(jnp.int32)
    leading = chosen[:, 0]
    row_ids = lax.iota(jnp.int32, SEQS)
    offsets = jnp.where(row_ids == 0, L - 1 - leading, jnp.where(row_ids == 1, L - leading, 0))
    return ((chosen + offsets[:, None]) % L).astype(jnp.int32)


def draw_group_tag(key, part):
    key = jax.random.fold_in(key, 23)
    first_key, second_key = jax.random.split(key)
    first_length = jax.random.randint(first_key, (SEQS, 1), L // 4, 3 * L // 8 + 1)
    second_length = jax.random.randint(second_key, (SEQS, 1), L // 4, 3 * L // 8 + 1)
    positions = lax.iota(jnp.int32, L)[None, :]
    return (positions >= first_length).astype(jnp.int32) + (positions >= first_length + second_length).astype(jnp.int32)


def levels(rng, dims, shards, low, top_value):
    factor_of = 1.0
    for axis_at, shards_of in shards:
        steps = jax.random.uniform(jax.random.fold_in(jax.random.fold_in(rng, 6), axis_at), (shards_of,), jnp.float32, low / len(shards), top_value / len(shards))
        factor_of = factor_of * jnp.repeat(jnp.exp(steps), dims[axis_at] // shards_of).reshape((-1,) + (1,) * (len(dims) - 1 - axis_at))
    return factor_of


def noise(stream_key, extent, scale, most, shards=(), kind=jnp.bfloat16):
    drawn = scale * jax.random.normal(stream_key, extent, jnp.float32)
    if shards:
        drawn = drawn * levels(stream_key, extent, shards, -0.22, 0.18)
    return jnp.clip(drawn, -most, most).astype(kind)


def setup_inputs(seed: int = 0) -> dict:
    arg_keys = jax.random.split(jax.random.key(seed), 24)
    return {
        "content_in": noise(arg_keys[0], (TOKENS, D), 1.0, 6.0, ((0, 64),)),
        "query_in": noise(arg_keys[1], (QROWS, D), 1.0, 6.0, ((0, 64),)),
        "content_cot": noise(arg_keys[2], (TOKENS, D), 1.0, 6.0, ((0, 64),)),
        "query_cot": noise(arg_keys[3], (QROWS, D), 1.0, 6.0, ((0, 64),)),
        "order_rank": jax.vmap(lambda own: jax.random.permutation(own, L))(jax.random.split(arg_keys[4], SEQS)).reshape((SEQS, L)).astype(jnp.int32),
        "query_pos": draw_query_pos(jax.random.fold_in(arg_keys[23], 71), 0),
        "group_tag": draw_group_tag(jax.random.fold_in(arg_keys[23], 71), 0),
        "w_query": noise(arg_keys[7], (2, D, D), (D // 2) ** -0.5, 0.3125, ((0, 2),)),
        "b_query": noise(arg_keys[8], (2, D), 0.5, 3.0, ((0, 2),), jnp.float32),
        "w_key": noise(arg_keys[9], (2, D, D), D ** -0.5, 0.21875, ((0, 2),)),
        "w_value": noise(arg_keys[10], (2, D, D), D ** -0.5, 0.21875, ((0, 2),)),
        "b_value": noise(arg_keys[11], (2, D), 0.5, 3.0, ((0, 2),), jnp.float32),
        "w_out": noise(arg_keys[12], (2, D, D), (D // 16) ** -0.5, 0.875, ((0, 2),)),
        "b_out": noise(arg_keys[13], (2, D), 0.5, 3.0, ((0, 2),), jnp.float32),
        "norm1_gain": jnp.clip(1.0 + 0.1 * jax.random.normal(arg_keys[14], (2, D), jnp.float32), 0.5, 1.5),
        "norm1_bias": noise(arg_keys[15], (2, D), 0.3, 2.0, ((0, 2),), jnp.float32),
        "w_expand": noise(arg_keys[16], (2, D, FF), D ** -0.5, 0.21875, ((0, 2),)),
        "b_expand": noise(arg_keys[17], (2, FF), 0.5, 3.0, ((0, 2),), jnp.float32),
        "w_contract": noise(arg_keys[18], (2, FF, D), FF ** -0.5, 0.109375, ((0, 2),)),
        "b_contract": noise(arg_keys[19], (2, D), 0.5, 3.0, ((0, 2),), jnp.float32),
        "norm2_gain": jnp.clip(1.0 + 0.1 * jax.random.normal(arg_keys[20], (2, D), jnp.float32), 0.5, 1.5),
        "norm2_bias": noise(arg_keys[21], (2, D), 0.3, 2.0, ((0, 2),), jnp.float32),
        "rel_table": noise(arg_keys[22], (NB, H), 1.0, 6.0, (), jnp.float32),
    }


@jax.custom_vjp
def low(v):
    return lax.optimization_barrier(v.astype(jnp.bfloat16)).astype(jnp.float32)

@jax.custom_vjp
def low_back(v):
    return v

def low_keep(v):
    return (low(v), None)

def low_pass(kept, grad):
    return (grad,)

def back_keep(v):
    return (v, None)

def back_low(kept, grad):
    return (low(grad),)
low.defvjp(low_keep, low_pass)
low_back.defvjp(back_keep, back_low)
TOP_PRECISION = lax.Precision.HIGHEST
EPSILON = 1e-05
LIMITS = (12, 16, 23, 32, 46, 64, 91)

def bucket_of(relative):
    distance = jnp.abs(relative)
    beyond = 8 + sum(((distance >= limit).astype(jnp.int32) for limit in LIMITS))
    within = jnp.where(distance < 8, distance, beyond)
    return within + 16 * (relative > 0).astype(jnp.int32)

def geometry(order_rows, pos_rows, tag_rows, table):
    positions = lax.iota(jnp.int32, L)
    matches = pos_rows[:, :, None] == positions[None, None, :]
    predicted = jnp.any(matches, axis=1)
    query_rank = jnp.take_along_axis(order_rows, pos_rows, axis=1)
    query_tag = jnp.take_along_axis(tag_rows, pos_rows, axis=1)
    row_rank = jnp.concatenate([order_rows, query_rank], axis=1)
    row_tag = jnp.concatenate([tag_rows, query_tag], axis=1)
    row_place = jnp.concatenate([jnp.broadcast_to(positions, order_rows.shape), pos_rows], axis=1)
    row_flag = jnp.concatenate([predicted, jnp.ones(pos_rows.shape, jnp.bool_)], axis=1)
    strict = jnp.concatenate([jnp.zeros(order_rows.shape, jnp.int32), jnp.ones(pos_rows.shape, jnp.int32)], axis=1)
    same_group = row_tag[:, :, None] == tag_rows[:, None, :]
    earlier = order_rows[:, None, :] + strict[:, :, None] <= row_rank[:, :, None]
    allowed = same_group & (~predicted[:, None, :] | row_flag[:, :, None] & earlier)
    buckets = bucket_of(positions[None, None, :] - row_place[:, :, None])
    score_bias = jnp.moveaxis(table[buckets], -1, 1)
    return (allowed, score_bias)

def matmul(former, latter):
    return jnp.einsum('srd,de->sre', former, latter, precision=TOP_PRECISION)

def normalize(values, gain, shift):
    centered = values - lax.optimization_barrier(jnp.mean(values, axis=-1, keepdims=True))
    variance = lax.optimization_barrier(jnp.mean(centered * centered, axis=-1, keepdims=True))
    return centered * lax.rsqrt(variance + EPSILON) * gain + shift

def split_into_heads(array):
    return array.reshape(array.shape[0], array.shape[1], H, HD)

def layer(rows, params, allowed, score_bias):
    weight_query, bias_query, weight_key, weight_value, bias_value, weight_out, bias_out, gain_first, shift_first, weight_expand, bias_expand, weight_contract, bias_contract, gain_second, shift_second = params
    inputs = low(rows)
    content = inputs[:, :L]
    query_matrix = low(low_back(matmul(inputs, weight_query) + bias_query))
    projected_key_rows = low(low_back(matmul(content, weight_key)))
    projected_value_rows = low(low_back(matmul(content, weight_value) + bias_value))
    unscaled_scores = jnp.einsum('fugy,fqgy->fguq', split_into_heads(query_matrix), split_into_heads(projected_key_rows), precision=TOP_PRECISION)
    scores = low_back(unscaled_scores * HD ** (-0.5) + score_bias)
    masked = jnp.where(allowed[:, None], scores, -1e+30)
    shifted = jnp.exp(masked - lax.optimization_barrier(jnp.max(masked, axis=-1, keepdims=True)))
    attention_weight_table = low(shifted / lax.optimization_barrier(jnp.sum(shifted, axis=-1, keepdims=True)))
    blended_rows = jnp.einsum('vgic,vcgw->vigw', attention_weight_table, split_into_heads(projected_value_rows), precision=TOP_PRECISION)
    blended_rows = low(low_back(blended_rows.reshape(rows.shape[0], rows.shape[1], D)))
    attended = low_back(matmul(blended_rows, weight_out) + bias_out)
    first = normalize(rows + attended, gain_first, shift_first)
    expanded = low_back(matmul(low(first), weight_expand) + bias_expand)
    activated = low(jax.nn.gelu(expanded, approximate=False))
    branch = low_back(matmul(activated, weight_contract) + bias_contract)
    return normalize(first + branch, gain_second, shift_second)

def block(rows, params, table, order_rows, pos_rows, tag_rows):
    allowed, score_bias = geometry(order_rows, pos_rows, tag_rows, table)
    middle = layer(rows, tuple((argument[0] for argument in params)), allowed, score_bias)
    middle = low(low_back(middle))
    return layer(middle, tuple((argument[1] for argument in params)), allowed, score_bias)

def reference(content_in, query_in, content_cot, query_cot, order_rank, query_pos, group_tag, w_query, b_query, w_key, w_value, b_value, w_out, b_out, norm1_gain, norm1_bias, w_expand, b_expand, w_contract, b_contract, norm2_gain, norm2_bias, rel_table):
    params = tuple((argument.astype(jnp.float32) for argument in (w_query, b_query, w_key, w_value, b_value, w_out, b_out, norm1_gain, norm1_bias, w_expand, b_expand, w_contract, b_contract, norm2_gain, norm2_bias)))
    table = rel_table.astype(jnp.float32)
    rows = jnp.concatenate([content_in.astype(jnp.float32).reshape(SEQS, L, D), query_in.astype(jnp.float32).reshape(SEQS, P_SIZE, D)], axis=1)
    cotangent = jnp.concatenate([content_cot.astype(jnp.float32).reshape(SEQS, L, D), query_cot.astype(jnp.float32).reshape(SEQS, P_SIZE, D)], axis=1)
    per_step = math.gcd(SEQS, max(1, 4096 // L))
    step_count = SEQS // per_step

    def regroup(argument):
        return argument.reshape((step_count, per_step) + argument.shape[1:])

    def scan_step(carry, inputs):
        block_rows, block_cotangent, block_rank, block_pos, block_tag = inputs

        def forward(rows_in, params_in, table_in):
            return block(rows_in, params_in, table_in, block_rank, block_pos, block_tag)
        outputs, pullback = jax.vjp(forward, block_rows, params, table)
        rows_grad, params_grad, table_grad = pullback(block_cotangent)
        carry_params, carry_table = carry
        carry = (tuple((running + fresh for running, fresh in zip(carry_params, params_grad))), carry_table + table_grad)
        return (carry, (outputs, rows_grad))
    initial = (tuple((jnp.zeros_like(argument) for argument in params)), jnp.zeros_like(table))
    (params_grad, table_grad), (outputs, rows_grad) = lax.scan(scan_step, initial, (regroup(rows), regroup(cotangent), regroup(order_rank), regroup(query_pos), regroup(group_tag)))
    outputs = outputs.reshape(SEQS, L + P_SIZE, D)
    rows_grad = rows_grad.reshape(SEQS, L + P_SIZE, D)
    content_ends = jnp.stack([rows_grad[:, :L].reshape(TOKENS, D), outputs[:, :L].reshape(TOKENS, D)])
    query_ends = jnp.stack([rows_grad[:, L:].reshape(QROWS, D), outputs[:, L:].reshape(QROWS, D)])
    query_weight_grad, query_bias_grad, key_weight_grad, value_weight_grad, value_bias_grad, out_weight_grad, out_bias_grad, first_gain_grad, first_shift_grad, expand_weight_grad, expand_bias_grad, contract_weight_grad, contract_bias_grad, second_gain_grad, second_shift_grad = params_grad
    return (content_ends, query_ends, query_weight_grad, query_bias_grad, key_weight_grad, value_weight_grad, value_bias_grad, out_weight_grad, out_bias_grad, first_gain_grad, first_shift_grad, expand_weight_grad, expand_bias_grad, contract_weight_grad, contract_bias_grad, second_gain_grad, second_shift_grad, table_grad)
```

```python
import jax
import jax.numpy as jnp
from jax import lax
from jax.sharding import PartitionSpec as P

D = 768
H = 12
HD = 64
NB = 32


TOP_PRECISION = lax.Precision.HIGHEST
EPSILON = 1e-05
LIMITS = (12, 16, 23, 32, 46, 64, 91)


def bucket_of(relative):
    distance = jnp.abs(relative)
    beyond = 8 + sum(((distance >= limit).astype(jnp.int32) for limit in LIMITS))
    within = jnp.where(distance < 8, distance, beyond)
    return within + 16 * (relative > 0).astype(jnp.int32)


def plain_dot(former, latter):
    return jnp.dot(former, latter, preferred_element_type=jnp.float32)


def outer_dot(former, latter):
    return lax.dot_general(
        former, latter, (((1,), (1,)), ((), ())), preferred_element_type=jnp.float32
    )


def inner_dot(former, latter):
    return lax.dot_general(
        former, latter, (((0,), (0,)), ((), ())), preferred_element_type=jnp.float32
    )


def geometry(order_row, pos_row, tag_row, table):
    length = order_row.shape[0]
    positions = lax.iota(jnp.int32, length)
    matches = pos_row[:, None] == positions[None, :]
    predicted = jnp.any(matches, axis=0)
    query_rank = jnp.sum(jnp.where(matches, order_row[None, :], 0), axis=1)
    query_tag = jnp.sum(jnp.where(matches, tag_row[None, :], 0), axis=1)
    row_rank = jnp.concatenate([order_row, query_rank])
    row_tag = jnp.concatenate([tag_row, query_tag])
    row_place = jnp.concatenate([positions, pos_row])
    row_flag = jnp.concatenate([predicted, jnp.ones(pos_row.shape, jnp.bool_)])
    strict = jnp.concatenate([jnp.zeros((length,), jnp.int32), jnp.ones(pos_row.shape, jnp.int32)])
    same_group = row_tag[:, None] == tag_row[None, :]
    earlier = order_row[None, :] + strict[:, None] <= row_rank[:, None]
    allowed = same_group & (~predicted[None, :] | row_flag[:, None] & earlier)
    buckets = bucket_of(positions[None, :] - row_place[:, None])
    one_hot = (buckets[None] == lax.iota(jnp.int32, NB)[:, None, None]).astype(jnp.float32)
    score_bias = jnp.einsum("krl,kh->hrl", one_hot, table, precision=TOP_PRECISION)
    return (allowed, score_bias, one_hot)


def normalize(values, gain, shift):
    centered = values - jnp.mean(values, axis=-1, keepdims=True)
    variance = jnp.mean(centered * centered, axis=-1, keepdims=True)
    inverse_root = lax.rsqrt(variance + EPSILON)
    normed = centered * inverse_root
    return (normed * gain + shift, normed, inverse_root)


def normalize_back(grad_out, gain, normed, inverse_root):
    gain_grad = jnp.sum(grad_out * normed, axis=0)
    shift_grad = jnp.sum(grad_out, axis=0)
    scaled = grad_out * gain
    grad_in = inverse_root * (
        scaled
        - jnp.mean(scaled, axis=-1, keepdims=True)
        - normed * jnp.mean(scaled * normed, axis=-1, keepdims=True)
    )
    return (grad_in, gain_grad, shift_grad)


def gelu_slope(values):
    return (
        0.5 * (1.0 + lax.erf(values * 0.7071067811865476))
        + values * jnp.exp(-0.5 * values * values) * 0.3989422804014327
    )


def forward_layer(rows, params, allowed, score_bias):
    (
        weight_query,
        bias_query,
        weight_key,
        weight_value,
        bias_value,
        weight_out,
        bias_out,
        gain_first,
        shift_first,
        weight_expand,
        bias_expand,
        weight_contract,
        bias_contract,
        gain_second,
        shift_second,
    ) = params
    seqs, row_count, _ = rows.shape
    length = allowed.shape[-1]
    flat = rows.reshape(seqs * row_count, D)
    content = rows[:, :length].reshape(seqs * length, D)
    query_matrix = (plain_dot(flat, weight_query) + bias_query).astype(jnp.bfloat16)
    key_matrix = plain_dot(content, weight_key).astype(jnp.bfloat16)
    value_matrix = (plain_dot(content, weight_value) + bias_value).astype(jnp.bfloat16)
    query_heads = query_matrix.reshape(seqs, row_count, H, HD)
    key_heads = key_matrix.reshape(seqs, length, H, HD)
    value_heads = value_matrix.reshape(seqs, length, H, HD)
    scores = (
        jnp.einsum("srhe,slhe->shrl", query_heads, key_heads, preferred_element_type=jnp.float32)
        * HD ** (-0.5)
        + score_bias
    )
    masked = jnp.where(allowed[:, None], scores, -1e30)
    shifted = jnp.exp(masked - jnp.max(masked, axis=-1, keepdims=True))
    attention = shifted / jnp.sum(shifted, axis=-1, keepdims=True)
    attention_low = attention.astype(jnp.bfloat16)
    blended = (
        jnp.einsum("shrl,slhe->srhe", attention_low, value_heads, preferred_element_type=jnp.float32)
        .reshape(seqs * row_count, D)
        .astype(jnp.bfloat16)
    )
    first_sum = flat.astype(jnp.float32) + plain_dot(blended, weight_out) + bias_out
    first, first_normed, first_root = normalize(first_sum, gain_first, shift_first)
    first_low = first.astype(jnp.bfloat16)
    expanded = plain_dot(first_low, weight_expand) + bias_expand
    activated = jax.nn.gelu(expanded, approximate=False).astype(jnp.bfloat16)
    second_sum = first + plain_dot(activated, weight_contract) + bias_contract
    output, second_normed, second_root = normalize(second_sum, gain_second, shift_second)
    saved = (
        query_heads,
        key_heads,
        value_heads,
        attention,
        attention_low,
        blended,
        first_normed,
        first_root,
        first_low,
        expanded,
        activated,
        second_normed,
        second_root,
    )
    return (output, saved)


def column_sum(gradient):
    return jnp.sum(gradient.astype(jnp.float32), axis=0)


def backward_layer(rows, params, saved, one_hot, grad_out):
    (
        weight_query,
        bias_query,
        weight_key,
        weight_value,
        bias_value,
        weight_out,
        bias_out,
        gain_first,
        shift_first,
        weight_expand,
        bias_expand,
        weight_contract,
        bias_contract,
        gain_second,
        shift_second,
    ) = params
    (
        query_heads,
        key_heads,
        value_heads,
        attention,
        attention_low,
        blended,
        first_normed,
        first_root,
        first_low,
        expanded,
        activated,
        second_normed,
        second_root,
    ) = saved
    seqs, row_count, _ = rows.shape
    length = key_heads.shape[1]
    flat = rows.reshape(seqs * row_count, D)
    content = rows[:, :length].reshape(seqs * length, D)
    second_grad, gain_second_grad, shift_second_grad = normalize_back(
        grad_out, gain_second, second_normed, second_root
    )
    branch_grad = second_grad.astype(jnp.bfloat16)
    expanded_grad = (outer_dot(branch_grad, weight_contract) * gelu_slope(expanded)).astype(
        jnp.bfloat16
    )
    first_total = second_grad + outer_dot(expanded_grad, weight_expand)
    first_grad, gain_first_grad, shift_first_grad = normalize_back(
        first_total, gain_first, first_normed, first_root
    )
    attended_grad = first_grad.astype(jnp.bfloat16)
    mixed_grad = (
        outer_dot(attended_grad, weight_out).astype(jnp.bfloat16).reshape(seqs, row_count, H, HD)
    )
    attention_grad = jnp.einsum(
        "srhe,slhe->shrl", mixed_grad, value_heads, preferred_element_type=jnp.float32
    )
    value_grad = (
        jnp.einsum("shrl,srhe->slhe", attention_low, mixed_grad, preferred_element_type=jnp.float32)
        .reshape(seqs * length, D)
        .astype(jnp.bfloat16)
    )
    score_grad = (
        attention * (attention_grad - jnp.sum(attention * attention_grad, axis=-1, keepdims=True))
    ).astype(jnp.bfloat16)
    table_grad = jnp.einsum(
        "skrl,shrl->kh", one_hot, score_grad.astype(jnp.float32), precision=TOP_PRECISION
    )
    query_grad = (
        (
            jnp.einsum("shrl,slhe->srhe", score_grad, key_heads, preferred_element_type=jnp.float32)
            * HD ** (-0.5)
        )
        .reshape(seqs * row_count, D)
        .astype(jnp.bfloat16)
    )
    key_grad = (
        (
            jnp.einsum("shrl,srhe->slhe", score_grad, query_heads, preferred_element_type=jnp.float32)
            * HD ** (-0.5)
        )
        .reshape(seqs * length, D)
        .astype(jnp.bfloat16)
    )
    content_grad = outer_dot(key_grad, weight_key) + outer_dot(value_grad, weight_value)
    rows_grad = (first_grad + outer_dot(query_grad, weight_query)).reshape(seqs, row_count, D)
    rows_grad = rows_grad + jnp.pad(
        content_grad.reshape(seqs, length, D), ((0, 0), (0, row_count - length), (0, 0))
    )
    small = jnp.concatenate(
        [
            column_sum(query_grad)[None],
            column_sum(value_grad)[None],
            column_sum(attended_grad)[None],
            gain_first_grad[None],
            shift_first_grad[None],
            column_sum(expanded_grad).reshape(4, D),
            column_sum(branch_grad)[None],
            gain_second_grad[None],
            shift_second_grad[None],
            jnp.pad(table_grad.reshape(1, NB * H), ((0, 0), (0, D - NB * H))),
            jnp.zeros((3, D), jnp.float32),
        ]
    )
    weight_groups = (
        inner_dot(activated, branch_grad).astype(jnp.bfloat16).reshape(2, 2, D, D),
        inner_dot(first_low, expanded_grad)
        .astype(jnp.bfloat16)
        .reshape(D, 2, 2, D)
        .transpose(1, 2, 0, 3),
        jnp.stack(
            [
                inner_dot(flat, query_grad).astype(jnp.bfloat16),
                inner_dot(content, key_grad).astype(jnp.bfloat16),
                inner_dot(content, value_grad).astype(jnp.bfloat16),
                inner_dot(blended, attended_grad).astype(jnp.bfloat16),
            ]
        ).reshape(2, 2, D, D),
    )
    return (rows_grad, small, weight_groups)


def shift(value, axis, by):
    size = lax.axis_size(axis)
    return lax.ppermute(value, axis, [(i, (i + by) % size) for i in range(size)])


def wide(value):
    return value.astype(jnp.float32)


def pick(parts, index):
    return lax.dynamic_index_in_dim(parts, index, 0, keepdims=False)


def ring_reduce(parts, axis):
    me = lax.axis_index(axis)
    own, after, across, before = (pick(parts, (me + k) % 4) for k in range(4))
    half = parts.shape[1] // 2
    from_left = shift(across[:half], axis, 1)
    from_right = shift(across[half:], axis, -1)
    to_right = jnp.concatenate(
        [(wide(after[:half]) + wide(from_left)).astype(jnp.bfloat16), after[half:]]
    )
    to_left = jnp.concatenate(
        [before[:half], (wide(before[half:]) + wide(from_right)).astype(jnp.bfloat16)]
    )
    left_sum = shift(to_right, axis, 1)
    right_sum = shift(to_left, axis, -1)
    return (wide(own) + wide(left_sum) + wide(right_sum)).astype(jnp.bfloat16)


def ring_gather(own, axis):
    me = lax.axis_index(axis)
    half = own.shape[0] // 2
    before = shift(own, axis, 1)
    after = shift(own, axis, -1)
    across = jnp.concatenate([shift(before[:half], axis, 1), shift(after[half:], axis, -1)])
    parts = jnp.zeros((4,) + own.shape, own.dtype)
    for k, part in enumerate((own, after, across, before)):
        parts = lax.dynamic_update_index_in_dim(parts, part, (me + k) % 4, 0)
    return parts


def pair_reduce(parts, axis):
    me = lax.axis_index(axis)
    arrived = shift(pick(parts, 1 - me), axis, 1)
    return (wide(pick(parts, me)) + wide(arrived)).astype(jnp.bfloat16)


def pair_gather(own, axis):
    me = lax.axis_index(axis)
    arrived = shift(own, axis, 1)
    return jnp.where(me == 0, jnp.stack([own, arrived]), jnp.stack([arrived, own]))


def reduce_block(block, outer, inner):
    part = ring_reduce(block.reshape(4, D // 4, D), outer)
    part = ring_reduce(part.reshape(4, D // 16, D), inner)
    part = pair_reduce(part.reshape(2, D // 32, D), "z")
    part = pair_gather(part, "z").reshape(D // 16, D)
    part = ring_gather(part, inner).reshape(D // 4, D)
    return ring_gather(part, outer).reshape(D, D)


def reduce_group(group):
    mine = pair_reduce(group, "c")
    along = jnp.stack([reduce_block(mine[0], "x", "y"), reduce_block(mine[1], "y", "x")])
    return wide(pair_gather(along, "c"))


def on_device(
    content_in,
    query_in,
    content_cot,
    query_cot,
    order_rank,
    query_pos,
    group_tag,
    *rest,
):
    params = tuple(argument[0] for argument in rest[:-1])
    rel_table = rest[-1]
    is_first = lax.axis_index("s") == 0
    sequences, length = order_rank.shape
    pick_count = query_pos.shape[1]
    row_count = length + pick_count

    def rows_of(content, query):
        return jnp.concatenate(
            [content.reshape(sequences, length, D), query.reshape(sequences, pick_count, D)], axis=1
        )

    allowed, score_bias, one_hot = jax.vmap(geometry, in_axes=(0, 0, 0, None))(
        order_rank, query_pos, group_tag, rel_table
    )
    own_rows = rows_of(content_in, query_in)
    cotangent = rows_of(content_cot, query_cot)
    first_out = forward_layer(own_rows, params, allowed, score_bias)[0]
    received = shift(first_out.astype(jnp.bfloat16), "s", 1).reshape(own_rows.shape)
    rows = jnp.where(is_first, own_rows, received)
    output, saved = forward_layer(rows, params, allowed, score_bias)
    flat_cotangent = wide(cotangent.reshape(-1, D))
    rows_grad = backward_layer(rows, params, saved, one_hot, flat_cotangent)[0]
    arrived = shift(rows_grad.astype(jnp.bfloat16), "s", 1)
    grad_out = jnp.where(is_first, wide(arrived.reshape(-1, D)), flat_cotangent)
    rows_grad, small, groups = backward_layer(rows, params, saved, one_hot, grad_out)
    ends = jnp.where(is_first, rows_grad, output.reshape(rows_grad.shape))
    content_ends = ends[:, :length].reshape(1, -1, D)
    query_ends = ends[:, length:].reshape(1, -1, D)
    smalls = lax.all_gather(small, DP, axis=0)
    small_sum = jnp.sum(smalls, axis=0)
    table_row = small_sum[12]
    table_total = (table_row + shift(table_row, "s", 1))[: NB * H].reshape(NB, H)
    contract, expand, heads = (reduce_group(group) for group in groups)
    contract = contract.reshape(1, 4 * D, D)
    expand = expand.reshape(4, D, D).transpose(1, 0, 2).reshape(1, D, 4 * D)
    heads = heads.reshape(4, 1, D, D)
    row = lambda k: small_sum[k][None]
    return (
        content_ends,
        query_ends,
        heads[0],
        row(0),
        heads[1],
        heads[2],
        row(1),
        heads[3],
        row(2),
        row(3),
        row(4),
        expand,
        small_sum[5:9].reshape(1, 4 * D),
        contract,
        row(9),
        row(10),
        row(11),
        table_total,
    )


DP = ("z", "x", "y", "c")


def solution(mesh):
    mesh = jax.sharding.Mesh(mesh.devices.reshape(2, 2, 4, 4, 2), ("s",) + DP)
    layer_specs = tuple(P("s", *([None] * (rank - 1))) for rank in (3, 2, 3, 3, 2, 3, 2, 2, 2, 3, 2, 3, 2, 2, 2))
    in_specs = (P(DP, None),) * 7 + layer_specs + (P(),)
    out_specs = (P("s", DP, None),) * 2 + layer_specs + (P(),)
    return jax.shard_map(
        on_device, mesh=mesh, in_specs=in_specs, out_specs=out_specs, check_vma=False
    )
```

```python
import jax
import jax.numpy as jnp
from jax import lax
from jax.experimental import pallas as pl
from jax.experimental.pallas import tpu as pltpu
from jax.sharding import PartitionSpec as P

D = 768
H = 12
HD = 64
FF = 3072
NB = 32
L = 128
PAIRS = H // 2
SEQS = 2
CONTENT = SEQS * L
PICKS = 32
ROWS = CONTENT + SEQS * PICKS
SEQ_ROWS = L + PICKS
EPSILON = 1e-05
SCALE = HD ** (-0.5)
TILE = 512
BAND = 32
LOW = jnp.bfloat16
WIDE = jnp.float32


def nn(former, latter):
    return lax.dot_general(
        former, latter, (((1,), (0,)), ((), ())), preferred_element_type=WIDE
    )


def nt(former, latter):
    return lax.dot_general(
        former, latter, (((1,), (1,)), ((), ())), preferred_element_type=WIDE
    )


def tn(former, latter):
    return lax.dot_general(
        former, latter, (((0,), (0,)), ((), ())), preferred_element_type=WIDE
    )


def seq_rows(ref, seq, lanes):
    return jnp.concatenate(
        [
            ref[seq * L : (seq + 1) * L, lanes],
            ref[CONTENT + seq * PICKS : CONTENT + (seq + 1) * PICKS, lanes],
        ]
    )


def store_rows(ref, seq, lanes, value):
    ref[seq * L : (seq + 1) * L, lanes] = value[:L]
    ref[CONTENT + seq * PICKS : CONTENT + (seq + 1) * PICKS, lanes] = value[L:]


def halves(value):
    even = lax.broadcasted_iota(jnp.int32, value.shape, 1) < HD
    zero = jnp.zeros_like(value)
    return jnp.concatenate([jnp.where(even, value, zero), jnp.where(even, zero, value)])


def side(value):
    count = value.shape[0] // 2
    return jnp.concatenate([value[:count], value[count:]], axis=1)


def bands(body):
    def step(index, carry):
        body(pl.ds(pl.multiple_of(index * BAND, BAND), BAND))
        return carry

    lax.fori_loop(0, ROWS // BAND, step, 0)


def pairs_loop(body):
    def step(pair, carry):
        body(pair, pl.ds(pl.multiple_of(pair * 128, 128), 128))
        return carry

    lax.fori_loop(0, PAIRS, step, 0)


def tiles_loop(body):
    def step(tile, carry):
        body(pl.ds(pl.multiple_of(tile * TILE, TILE), TILE))
        return carry

    lax.fori_loop(0, FF // TILE, step, 0)


def norm_rows(values):
    centered = values - jnp.mean(values, axis=-1, keepdims=True)
    variance = jnp.mean(centered * centered, axis=-1, keepdims=True)
    root = lax.rsqrt(variance + EPSILON)
    return (centered * root, root)


def norm_rows_back(scaled, normed, root):
    return root * (
        scaled
        - jnp.mean(scaled, axis=-1, keepdims=True)
        - normed * jnp.mean(scaled * normed, axis=-1, keepdims=True)
    )


B_QUERY, B_VALUE, B_OUT, GAIN1, SHIFT1, B_CONTRACT, GAIN2, SHIFT2 = range(8)


def forward(x, w, vec, b_expand, masks, s, keep, ready):
    row = lambda k: vec[k : k + 1, :]
    ready("query")
    s.query[...] = (nn(x[...], w.query[...]) + row(B_QUERY)).astype(LOW)
    ready("key")
    s.key[...] = nn(x[:CONTENT], w.key[...]).astype(LOW)
    ready("value")
    s.value[...] = (nn(x[:CONTENT], w.value[...]) + row(B_VALUE)).astype(LOW)
    ready("masks")

    def attend(pair, lanes):
        for seq in range(SEQS):
            own = pl.ds(seq * L, L)
            scores = (
                nt(halves(seq_rows(s.query, seq, lanes)), s.key[own, lanes]) * SCALE
                + masks[seq, pair]
            )
            shifted = jnp.exp(scores - jnp.max(scores, axis=-1, keepdims=True))
            probs = (shifted / jnp.sum(shifted, axis=-1, keepdims=True)).astype(LOW)
            if keep:
                s.probs[seq, pair] = probs
            mixed = nn(side(probs), halves(s.value[own, lanes]))
            store_rows(s.mixed, seq, lanes, mixed.astype(LOW))

    pairs_loop(attend)
    ready("out")
    s.total[...] = nn(s.mixed[...], w.out[...])

    def first_norm(band):
        normed, root = norm_rows(x[band].astype(WIDE) + s.total[band] + row(B_OUT))
        first = normed * row(GAIN1) + row(SHIFT1)
        s.first_low[band] = first.astype(LOW)
        s.total[band] = first + row(B_CONTRACT)
        if keep:
            s.normed1[band] = normed
            s.root1[band] = jnp.broadcast_to(root, (BAND, 128))

    bands(first_norm)
    ready("expand")
    ready("contract")

    def feed(tile):
        expanded = nn(s.first_low[...], w.expand[:, tile]) + b_expand[:, tile]
        cumulative = 0.5 * (1.0 + lax.erf(expanded * 0.7071067811865476))
        activated = (expanded * cumulative).astype(LOW)
        if keep:
            s.slope[:, tile] = (
                cumulative + expanded * jnp.exp(-0.5 * expanded * expanded) * 0.3989422804014327
            ).astype(LOW)
            s.activated[:, tile] = activated
        s.total[...] += nn(activated, w.contract[tile, :])

    tiles_loop(feed)

    def second_norm(band):
        normed, root = norm_rows(s.total[band])
        if keep:
            s.normed2[band] = normed
            s.root2[band] = jnp.broadcast_to(root, (BAND, 128))
        s.out[band] = (normed * row(GAIN2) + row(SHIFT2)).astype(s.out.dtype)

    bands(second_norm)


def backward_feed(grad, w, vec, s, sums=None):
    row = lambda k: vec[k : k + 1, :]

    def second_norm(band):
        upper = grad[band].astype(WIDE)
        normed = s.normed2[band]
        lower = norm_rows_back(upper * row(GAIN2), normed, s.root2[band, :1])
        s.total[band] = lower
        s.branch[band] = lower.astype(LOW)
        if sums is not None:
            sums(band, 10, upper * normed)
            sums(band, 11, upper)
            sums(band, 9, lower.astype(LOW).astype(WIDE))

    bands(second_norm)


def backward_expand(w, vec, s, sums=None, tile_sums=None):
    row = lambda k: vec[k : k + 1, :]

    def feed(tile):
        lower = (nt(s.branch[...], w.contract[tile, :]) * s.slope[:, tile].astype(WIDE)).astype(LOW)
        s.expanded[:, tile] = lower
        if tile_sums is not None:
            tile_sums(tile, lower)
        s.total[...] += nt(lower, w.expand[:, tile])

    tiles_loop(feed)

    def first_norm(band):
        upper = s.total[band]
        normed = s.normed1[band]
        lower = norm_rows_back(upper * row(GAIN1), normed, s.root1[band, :1])
        s.total[band] = lower
        s.attended[band] = lower.astype(LOW)
        if sums is not None:
            sums(band, 3, upper * normed)
            sums(band, 4, upper)
            sums(band, 2, lower.astype(LOW).astype(WIDE))

    bands(first_norm)


def backward_attend(w, s, table=None):
    s.dmixed[...] = nt(s.attended[...], w.out[...]).astype(LOW)

    def attend(pair, lanes):
        slopes = []
        for seq in range(SEQS):
            own = pl.ds(seq * L, L)
            probs = s.probs[seq, pair]
            below = halves(seq_rows(s.dmixed, seq, lanes))
            dprobs = nt(below, s.value[own, lanes])
            s.dvalue[own, lanes] = tn(probs, below).astype(LOW)
            weight = probs.astype(WIDE)
            dscores = (
                weight * (dprobs - jnp.sum(weight * dprobs, axis=-1, keepdims=True))
            ).astype(LOW)
            dquery = nn(side(dscores), halves(s.key[own, lanes])) * SCALE
            store_rows(s.dquery, seq, lanes, dquery.astype(LOW))
            dkey = tn(dscores, halves(seq_rows(s.query, seq, lanes))) * SCALE
            s.dkey[own, lanes] = dkey.astype(LOW)
            slopes.append(dscores)
        if table is not None:
            table(pair, slopes)

    pairs_loop(attend)
    s.total[...] += nt(s.dquery[...], w.query[...])
    s.total[:CONTENT] += nt(s.dkey[...], w.key[...]) + nt(s.dvalue[...], w.value[...])


class Names:
    def __init__(self, **named):
        self.__dict__.update(named)


MATRICES = ("query", "key", "value", "out", "expand", "contract")
MATRIX_SHAPES = {
    "query": (D, D),
    "key": (D, D),
    "value": (D, D),
    "out": (D, D),
    "expand": (D, FF),
    "contract": (FF, D),
}
MASK_SHAPE = (SEQS, PAIRS, 2 * SEQ_ROWS, L)
KEPT = {
    "query": ((ROWS, D), LOW),
    "key": ((CONTENT, D), LOW),
    "value": ((CONTENT, D), LOW),
    "probs": (MASK_SHAPE, LOW),
    "mixed": ((ROWS, D), LOW),
    "normed1": ((ROWS, D), WIDE),
    "root1": ((ROWS, 128), WIDE),
    "first_low": ((ROWS, D), LOW),
    "slope": ((ROWS, FF), LOW),
    "activated": ((ROWS, FF), LOW),
    "normed2": ((ROWS, D), WIDE),
    "root2": ((ROWS, 128), WIDE),
}
PASSED = {
    "branch": ((ROWS, D), LOW),
    "expanded": ((ROWS, FF), LOW),
    "attended": ((ROWS, D), LOW),
    "dmixed": ((ROWS, D), LOW),
    "dvalue": ((CONTENT, D), LOW),
    "dquery": ((ROWS, D), LOW),
    "dkey": ((CONTENT, D), LOW),
}
ANY = pl.BlockSpec(memory_space=pl.ANY)
VMEM = pl.BlockSpec(memory_space=pltpu.VMEM)
LIMIT = 60 * 1024 * 1024


def fetcher(pairs, sems):
    copies = {}
    for index, (name, source, target) in enumerate(pairs):
        copies[name] = pltpu.make_async_copy(source, target, sems.at[index])
        copies[name].start()
    return lambda name: copies[name].wait()


def front_kernel(x, *refs):
    matrices, (masks, vec, b_expand, out), rest = refs[:6], refs[6:10], refs[10:]
    held, (mask_buf, query, key, value, mixed, first_low, total, sems) = rest[:6], rest[6:]
    ready = fetcher(
        [(n, a, b) for n, a, b in zip(MATRICES[:3], matrices[:3], held[:3])]
        + [("masks", masks, mask_buf)]
        + [(n, a, b) for n, a, b in zip(MATRICES[3:], matrices[3:], held[3:])],
        sems,
    )
    s = Names(
        query=query, key=key, value=value, mixed=mixed, first_low=first_low, total=total, out=out
    )
    forward(x, Names(**dict(zip(MATRICES, held))), vec, b_expand, mask_buf, s, False, ready)


def front(x, matrices, masks, vec, b_expand):
    return pl.pallas_call(
        front_kernel,
        out_shape=jax.ShapeDtypeStruct((ROWS, D), LOW),
        in_specs=[VMEM] + [ANY] * 7 + [VMEM] * 2,
        out_specs=VMEM,
        scratch_shapes=[pltpu.VMEM(MATRIX_SHAPES[n], LOW) for n in MATRICES]
        + [pltpu.VMEM(MASK_SHAPE, WIDE)]
        + [pltpu.VMEM(*KEPT[n]) for n in ("query", "key", "value", "mixed", "first_low")]
        + [pltpu.VMEM((ROWS, D), WIDE), pltpu.SemaphoreType.DMA((7,))],
        compiler_params=pltpu.CompilerParams(vmem_limit_bytes=LIMIT),
        name="front",
    )(x, *matrices, masks, vec, b_expand)


def middle_kernel(x, cot, *refs):
    matrices, (masks, vec, b_expand), rest = refs[:6], refs[6:9], refs[9:]
    (out, grad), rest = rest[:2], rest[2:]
    kept_out, rest = rest[: len(KEPT)], rest[len(KEPT) :]
    held, (mask_buf,), rest = rest[:6], rest[6:7], rest[7:]
    kept, rest = rest[: len(KEPT)], rest[len(KEPT) :]
    passed, rest = rest[: len(PASSED)], rest[len(PASSED) :]
    total, sems, out_sems = rest
    ready = fetcher(
        [(n, a, b) for n, a, b in zip(MATRICES[:3], matrices[:3], held[:3])]
        + [("masks", masks, mask_buf)]
        + [(n, a, b) for n, a, b in zip(MATRICES[3:], matrices[3:], held[3:])],
        sems,
    )
    w = Names(**dict(zip(MATRICES, held)))
    s = Names(total=total, out=out, **dict(zip(KEPT, kept)), **dict(zip(PASSED, passed)))
    forward(x, w, vec, b_expand, mask_buf, s, True, ready)
    done = fetcher([(n, a, b) for n, a, b in zip(KEPT, kept, kept_out)], out_sems)
    backward_feed(cot, w, vec, s)
    backward_expand(w, vec, s)
    backward_attend(w, s)
    grad[...] = total[...].astype(LOW)
    for name in KEPT:
        done(name)


def middle(x, cot, matrices, masks, vec, b_expand):
    return pl.pallas_call(
        middle_kernel,
        out_shape=[
            jax.ShapeDtypeStruct((ROWS, D), WIDE),
            jax.ShapeDtypeStruct((ROWS, D), LOW),
        ]
        + [jax.ShapeDtypeStruct(*KEPT[n]) for n in KEPT],
        in_specs=[VMEM] * 2 + [ANY] * 7 + [VMEM] * 2,
        out_specs=[VMEM] * 2 + [ANY] * len(KEPT),
        scratch_shapes=[pltpu.VMEM(MATRIX_SHAPES[n], LOW) for n in MATRICES]
        + [pltpu.VMEM(MASK_SHAPE, WIDE)]
        + [pltpu.VMEM(*KEPT[n]) for n in KEPT]
        + [pltpu.VMEM(*PASSED[n]) for n in PASSED]
        + [
            pltpu.VMEM((ROWS, D), WIDE),
            pltpu.SemaphoreType.DMA((7,)),
            pltpu.SemaphoreType.DMA((len(KEPT),)),
        ],
        compiler_params=pltpu.CompilerParams(vmem_limit_bytes=LIMIT),
        name="middle",
    )(x, cot, *matrices, masks, vec, b_expand)


QUARTER = D // 4
BLOCKS = 6


def back_kernel(x, upper, spread, *refs):
    matrices, (vec,), rest = refs[:6], refs[6:7], refs[7:]
    kept_in, rest = rest[: len(KEPT)], rest[len(KEPT) :]
    (grad, small, table, groups), rest = rest[:4], rest[4:]
    held, rest = rest[:6], rest[6:]
    kept, rest = rest[: len(KEPT)], rest[len(KEPT) :]
    passed, rest = rest[: len(PASSED)], rest[len(PASSED) :]
    total, stage, sems, out_sems = rest
    first = ("normed2", "root2", "activated")
    later = [n for n in KEPT if n not in first]
    kept_pairs = {n: (n, a, b) for n, a, b in zip(KEPT, kept_in, kept)}
    matrix_pairs = {n: ("w_" + n, a, b) for n, a, b in zip(MATRICES, matrices, held)}
    ready = fetcher(
        [kept_pairs[n] for n in first]
        + [matrix_pairs["contract"], kept_pairs["slope"], matrix_pairs["expand"]]
        + [kept_pairs[n] for n in later if n != "slope"]
        + [matrix_pairs[n] for n in ("out", "query", "key", "value")],
        sems,
    )
    w = Names(**dict(zip(MATRICES, held)))
    s = Names(total=total, **dict(zip(KEPT, kept)), **dict(zip(PASSED, passed)))
    small[...] = jnp.zeros_like(small)

    def sums(band, place, value):
        small[place : place + 1, :] += jnp.sum(value, axis=0, keepdims=True)

    for name in first:
        ready(name)
    backward_feed(upper, w, vec, s, sums)

    pending = []

    def emit(core, quarter, block, value):
        slot = len(pending) % 2
        if len(pending) >= 2:
            pending[-2].wait()
        stage[slot] = value.astype(LOW)
        copy = pltpu.make_async_copy(
            stage.at[slot], groups.at[core, quarter, block], out_sems.at[slot]
        )
        copy.start()
        pending.append(copy)

    for index in range(FF // QUARTER):
        core, block, quarter = index // 8, index // 4 % 2, index % 4
        emit(
            core,
            quarter,
            block,
            tn(s.activated[:, index * QUARTER : (index + 1) * QUARTER], s.branch[...]),
        )

    def tile_sums(tile, value):
        pass

    ready("w_contract")
    ready("slope")
    ready("w_expand")
    for name in later:
        if name != "slope":
            ready(name)
    backward_expand(w, vec, s, sums, tile_sums)
    for column in range(4):
        part = jnp.sum(s.expanded[:, column * D : (column + 1) * D].astype(WIDE), axis=0, keepdims=True)
        small[5 + column : 6 + column, :] = part
        for quarter in range(4):
            emit(
                column // 2,
                quarter,
                2 + column % 2,
                tn(
                    s.first_low[:, quarter * QUARTER : (quarter + 1) * QUARTER],
                    s.expanded[:, column * D : (column + 1) * D],
                ),
            )
    for name in ("out", "query", "key", "value"):
        ready("w_" + name)

    def table_sum(pair, slopes):
        both = jnp.concatenate([slope[:SEQ_ROWS] for slope in slopes])
        table[2 * pair] = nn(spread[...], both)
        both = jnp.concatenate([slope[SEQ_ROWS:] for slope in slopes])
        table[2 * pair + 1] = nn(spread[...], both)

    backward_attend(w, s, table_sum)
    grad[...] = total[...]
    small[0:1, :] = jnp.sum(s.dquery[...].astype(WIDE), axis=0, keepdims=True)
    small[1:2, :] = jnp.sum(s.dvalue[...].astype(WIDE), axis=0, keepdims=True)
    for number, (former, latter) in enumerate(
        ((x, s.dquery), (x, s.dkey), (x, s.dvalue), (s.mixed, s.attended))
    ):
        count = latter.shape[0]
        for quarter in range(4):
            emit(
                number // 2,
                quarter,
                4 + number % 2,
                tn(former[:count, quarter * QUARTER : (quarter + 1) * QUARTER], latter[...]),
            )
    pending[-2].wait()
    pending[-1].wait()


def back(x, upper, spread, matrices, vec, kept):
    copies = len(KEPT) + len(MATRICES)
    return pl.pallas_call(
        back_kernel,
        out_shape=[
            jax.ShapeDtypeStruct((ROWS, D), WIDE),
            jax.ShapeDtypeStruct((16, D), WIDE),
            jax.ShapeDtypeStruct((H, L, L), WIDE),
            jax.ShapeDtypeStruct((2, 4, BLOCKS, QUARTER, D), LOW),
        ],
        in_specs=[VMEM] * 3 + [ANY] * 6 + [VMEM] + [ANY] * len(KEPT),
        out_specs=[VMEM] * 3 + [ANY],
        scratch_shapes=[pltpu.VMEM(MATRIX_SHAPES[n], LOW) for n in MATRICES]
        + [pltpu.VMEM(*KEPT[n]) for n in KEPT]
        + [pltpu.VMEM(*PASSED[n]) for n in PASSED]
        + [
            pltpu.VMEM((ROWS, D), WIDE),
            pltpu.VMEM((2, QUARTER, D), LOW),
            pltpu.SemaphoreType.DMA((copies,)),
            pltpu.SemaphoreType.DMA((2,)),
        ],
        compiler_params=pltpu.CompilerParams(vmem_limit_bytes=LIMIT),
        name="back",
    )(x, upper, spread, *matrices, vec, *kept)


LIMITS = (12, 16, 23, 32, 46, 64, 91)
TOP_PRECISION = lax.Precision.HIGHEST


def bucket_of(relative):
    distance = jnp.abs(relative)
    beyond = 8 + sum(((distance >= limit).astype(jnp.int32) for limit in LIMITS))
    within = jnp.where(distance < 8, distance, beyond)
    return within + 16 * (relative > 0).astype(jnp.int32)


def geometry(order_row, pos_row, tag_row, table):
    positions = lax.iota(jnp.int32, L)
    matches = pos_row[:, None] == positions[None, :]
    predicted = jnp.any(matches, axis=0)
    query_rank = jnp.sum(jnp.where(matches, order_row[None, :], 0), axis=1)
    query_tag = jnp.sum(jnp.where(matches, tag_row[None, :], 0), axis=1)
    row_rank = jnp.concatenate([order_row, query_rank])
    row_tag = jnp.concatenate([tag_row, query_tag])
    row_place = jnp.concatenate([positions, pos_row])
    row_flag = jnp.concatenate([predicted, jnp.ones(pos_row.shape, jnp.bool_)])
    strict = jnp.concatenate([jnp.zeros((L,), jnp.int32), jnp.ones(pos_row.shape, jnp.int32)])
    same_group = row_tag[:, None] == tag_row[None, :]
    earlier = order_row[None, :] + strict[:, None] <= row_rank[:, None]
    allowed = same_group & (~predicted[None, :] | row_flag[:, None] & earlier)
    buckets = bucket_of(positions[None, :] - row_place[:, None])
    one_hot = (buckets[None] == lax.iota(jnp.int32, NB)[:, None, None]).astype(WIDE)
    score_bias = jnp.einsum("krl,kh->hrl", one_hot, table, precision=TOP_PRECISION)
    masked = jnp.where(allowed[None], score_bias, -1e30)
    masked = jnp.pad(masked, ((0, 0), (0, SEQ_ROWS - masked.shape[1]), (0, 0)))
    padded = jnp.pad(matches.astype(LOW), ((0, PICKS - matches.shape[0]), (0, 0)))
    spread = jnp.concatenate([jnp.eye(L, dtype=LOW), padded.T], axis=1)
    return (masked, spread)


def diagonals():
    positions = lax.iota(jnp.int32, L)
    buckets = bucket_of(positions[None, :] - positions[:, None])
    return (buckets[None] == lax.iota(jnp.int32, NB)[:, None, None]).astype(WIDE)


PLANE = ("x", "y", "c")


def shift(value, axis, by):
    size = lax.axis_size(axis)
    return lax.ppermute(value, axis, [(i, (i + by) % size) for i in range(size)])


def turn(value, outer, by):
    pairs = []
    for i in range(4):
        for j in range(4):
            for c in range(2):
                if (c == 0) == outer:
                    target = ((i + by) % 4, j)
                else:
                    target = (i, (j + by) % 4)
                pairs.append(((i * 4 + j) * 2 + c, (target[0] * 4 + target[1]) * 2 + c))
    return lax.ppermute(value, PLANE, pairs)


def place(outer):
    return jnp.where(
        (lax.axis_index("c") == 0) == outer, lax.axis_index("x"), lax.axis_index("y")
    )


def wide(value):
    return value.astype(WIDE)


def pick(parts, index):
    return lax.dynamic_index_in_dim(parts, index, 0, keepdims=False)


def ring_reduce(parts, outer):
    me = place(outer)
    own, after, across, before = (pick(parts, (me + k) % 4) for k in range(4))
    half = parts.shape[1] // 2
    from_left = turn(across[:half], outer, 1)
    from_right = turn(across[half:], outer, -1)
    to_right = jnp.concatenate(
        [(wide(after[:half]) + wide(from_left)).astype(LOW), after[half:]]
    )
    to_left = jnp.concatenate(
        [before[:half], (wide(before[half:]) + wide(from_right)).astype(LOW)]
    )
    left_sum = turn(to_right, outer, 1)
    right_sum = turn(to_left, outer, -1)
    return (wide(own) + wide(left_sum) + wide(right_sum)).astype(LOW)


def direct_reduce(parts, outer):
    me = place(outer)
    total = wide(pick(parts, me))
    for by in (1, 2, -1):
        total += wide(turn(pick(parts, (me + by) % 4), outer, by))
    return total.astype(LOW)


def join(parts, outer):
    me = place(outer)
    whole = jnp.zeros((4,) + parts[0].shape, parts[0].dtype)
    for k, part in enumerate(parts):
        whole = lax.dynamic_update_index_in_dim(whole, part, (me + k) % 4, 0)
    return whole


def ring_gather(own, outer):
    half = own.shape[0] // 2
    before = turn(own, outer, 1)
    after = turn(own, outer, -1)
    across = jnp.concatenate([turn(before[:half], outer, 1), turn(after[half:], outer, -1)])
    return join((own, after, across, before), outer)


def direct_gather(own, outer):
    after, across, before = (turn(own, outer, by) for by in (-1, 2, 1))
    return join((own, after, across, before), outer)


def pair_reduce(parts, axis):
    me = lax.axis_index(axis)
    arrived = shift(pick(parts, 1 - me), axis, 1)
    return (wide(pick(parts, me)) + wide(arrived)).astype(LOW)


def pair_gather(own, axis):
    me = lax.axis_index(axis)
    arrived = shift(own, axis, 1)
    return jnp.where(me == 0, jnp.stack([own, arrived]), jnp.stack([arrived, own]))


def reduce_groups(groups):
    count = BLOCKS * QUARTER
    part = pair_reduce(groups.reshape(2, 4, count, D), "c")
    part = ring_reduce(part, True)
    part = direct_reduce(part.reshape(4, count // 4, D), False)
    part = pair_reduce(part.reshape(2, count // 8, D), "z")
    part = pair_gather(part, "z").reshape(count // 4, D)
    part = direct_gather(part, False).reshape(count, D)
    part = ring_gather(part, True)
    return pair_gather(part, "c").reshape(2, 4, BLOCKS, QUARTER, D)


def on_device(
    content_in,
    query_in,
    content_cot,
    query_cot,
    order_rank,
    query_pos,
    group_tag,
    *rest,
):
    (
        w_query,
        b_query,
        w_key,
        w_value,
        b_value,
        w_out,
        b_out,
        norm1_gain,
        norm1_bias,
        w_expand,
        b_expand,
        w_contract,
        b_contract,
        norm2_gain,
        norm2_bias,
    ) = (argument[0] for argument in rest[:-1])
    rel_table = rest[-1]
    is_first = lax.axis_index("s") == 0
    picks = query_pos.shape[1]

    def rows_of(content, query):
        query = jnp.pad(query.reshape(SEQS, picks, D), ((0, 0), (0, PICKS - picks), (0, 0)))
        return jnp.concatenate([content, query.reshape(SEQS * PICKS, D)])

    masks, spread = jax.vmap(geometry, in_axes=(0, 0, 0, None))(
        order_rank, query_pos, group_tag, rel_table
    )
    masks = masks.reshape(MASK_SHAPE)
    spread = jnp.concatenate([spread[0], spread[1]], axis=1)
    own_rows = rows_of(content_in, query_in)
    cotangent = rows_of(content_cot, query_cot)
    matrices = (w_query, w_key, w_value, w_out, w_expand, w_contract)
    vec = jnp.stack(
        [b_query, b_value, b_out, norm1_gain, norm1_bias, b_contract, norm2_gain, norm2_bias]
    )
    b_expand = b_expand[None]
    first_out = front(own_rows, matrices, masks, vec, b_expand)
    rows = jnp.where(is_first, own_rows, shift(first_out, "s", 1))
    output, rows_grad, *kept = middle(rows, cotangent, matrices, masks, vec, b_expand)
    upper = jnp.where(is_first, shift(rows_grad, "s", 1), cotangent)
    rows_grad, small, slopes, groups = back(rows, upper, spread, matrices, vec, kept)
    ends = jnp.where(is_first, rows_grad, output)
    content_ends = ends[None, :CONTENT]
    query_ends = ends[CONTENT:].reshape(SEQS, PICKS, D)[:, :picks].reshape(1, SEQS * picks, D)
    table = jnp.einsum("krl,hrl->kh", diagonals(), slopes, precision=TOP_PRECISION)
    table = jnp.pad(table.reshape(1, NB * H), ((0, 0), (0, D - NB * H)))
    small = jnp.concatenate([small[:12], table])
    small_sum = jnp.sum(lax.all_gather(small, DP, axis=0), axis=0)
    table_row = small_sum[12]
    table_total = (table_row + shift(table_row, "s", 1))[: NB * H].reshape(NB, H)
    groups = wide(reduce_groups(groups))
    contract = groups[:, :, 0:2].transpose(0, 2, 1, 3, 4).reshape(1, FF, D)
    expand = groups[:, :, 2:4].transpose(1, 3, 0, 2, 4).reshape(1, D, FF)
    heads = groups[:, :, 4:6].transpose(0, 2, 1, 3, 4).reshape(4, 1, D, D)
    row = lambda k: small_sum[k][None]
    return (
        content_ends,
        query_ends,
        heads[0],
        row(0),
        heads[1],
        heads[2],
        row(1),
        heads[3],
        row(2),
        row(3),
        row(4),
        expand,
        small_sum[5:9].reshape(1, FF),
        contract,
        row(9),
        row(10),
        row(11),
        table_total,
    )


DP = ("z", "x", "y", "c")


def solution(mesh):
    mesh = jax.sharding.Mesh(mesh.devices.reshape(2, 2, 4, 4, 2), ("s",) + DP)
    layer_specs = tuple(
        P("s", *([None] * (rank - 1))) for rank in (3, 2, 3, 3, 2, 3, 2, 2, 2, 3, 2, 3, 2, 2, 2)
    )
    in_specs = (P(DP, None),) * 7 + layer_specs + (P(),)
    out_specs = (P("s", DP, None),) * 2 + layer_specs + (P(),)
    return jax.shard_map(
        on_device, mesh=mesh, in_specs=in_specs, out_specs=out_specs, check_vma=False
    )
```

```python
import jax
import jax.numpy as jnp
from jax import lax
from jax.experimental import pallas as pl
from jax.experimental.pallas import tpu as pltpu
from jax.sharding import PartitionSpec as P

D = 768
H = 12
HD = 64
FF = 3072
NB = 32
L = 128
PAIRS = H // 2
SEQS = 2
CONTENT = SEQS * L
PICKS = 32
ROWS = CONTENT + SEQS * PICKS
SEQ_ROWS = L + PICKS
EPSILON = 1e-05
SCALE = HD ** (-0.5)
TILE = 768
BAND = 64
LOW = jnp.bfloat16
WIDE = jnp.float32


def nn(former, latter):
    return lax.dot_general(
        former, latter, (((1,), (0,)), ((), ())), preferred_element_type=WIDE
    )


def nt(former, latter):
    return lax.dot_general(
        former, latter, (((1,), (1,)), ((), ())), preferred_element_type=WIDE
    )


def tn(former, latter):
    return lax.dot_general(
        former, latter, (((0,), (0,)), ((), ())), preferred_element_type=WIDE
    )


def seq_rows(ref, seq, lanes):
    return jnp.concatenate(
        [
            ref[seq * L : (seq + 1) * L, lanes],
            ref[CONTENT + seq * PICKS : CONTENT + (seq + 1) * PICKS, lanes],
        ]
    )


def store_rows(ref, seq, lanes, value):
    ref[seq * L : (seq + 1) * L, lanes] = value[:L]
    ref[CONTENT + seq * PICKS : CONTENT + (seq + 1) * PICKS, lanes] = value[L:]


def halves(value):
    even = lax.broadcasted_iota(jnp.int32, value.shape, 1) < HD
    zero = jnp.zeros_like(value)
    return jnp.concatenate([jnp.where(even, value, zero), jnp.where(even, zero, value)])


def side(value):
    count = value.shape[0] // 2
    return jnp.concatenate([value[:count], value[count:]], axis=1)


def bands(body):
    for index in range(ROWS // BAND):
        body(slice(index * BAND, (index + 1) * BAND))


def pairs_loop(body):
    for pair in range(PAIRS):
        body(pair, slice(pair * 128, (pair + 1) * 128))


def tiles_loop(body):
    for tile in range(FF // TILE):
        body(slice(tile * TILE, (tile + 1) * TILE))


def norm_rows(values):
    centered = values - jnp.mean(values, axis=-1, keepdims=True)
    variance = jnp.mean(centered * centered, axis=-1, keepdims=True)
    root = lax.rsqrt(variance + EPSILON)
    return (centered * root, root)


def norm_rows_back(scaled, normed, root):
    return root * (
        scaled
        - jnp.mean(scaled, axis=-1, keepdims=True)
        - normed * jnp.mean(scaled * normed, axis=-1, keepdims=True)
    )


B_QUERY, B_VALUE, B_OUT, GAIN1, SHIFT1, B_CONTRACT, GAIN2, SHIFT2 = range(8)


def forward(x, w, vec, b_expand, masks, s, keep, ready):
    row = lambda k: vec[k : k + 1, :]
    ready("query")
    s.query[...] = (nn(x[...], w.query[...]) + row(B_QUERY)).astype(LOW)
    ready("key")
    s.key[...] = nn(x[:CONTENT], w.key[...]).astype(LOW)
    ready("value")
    s.value[...] = (nn(x[:CONTENT], w.value[...]) + row(B_VALUE)).astype(LOW)
    ready("masks")

    def attend(pair, lanes):
        for seq in range(SEQS):
            own = pl.ds(seq * L, L)
            scores = (
                nt(halves(seq_rows(s.query, seq, lanes)), s.key[own, lanes]) * SCALE
                + masks[seq, pair]
            )
            shifted = jnp.exp(scores - jnp.max(scores, axis=-1, keepdims=True))
            probs = (shifted / jnp.sum(shifted, axis=-1, keepdims=True)).astype(LOW)
            if keep:
                s.probs[seq, pair] = probs
            mixed = nn(side(probs), halves(s.value[own, lanes]))
            store_rows(s.mixed, seq, lanes, mixed.astype(LOW))

    pairs_loop(attend)
    ready("out")
    s.total[...] = nn(s.mixed[...], w.out[...])

    def first_norm(band):
        normed, root = norm_rows(x[band].astype(WIDE) + s.total[band] + row(B_OUT))
        first = normed * row(GAIN1) + row(SHIFT1)
        s.first_low[band] = first.astype(LOW)
        s.total[band] = first + row(B_CONTRACT)
        if keep:
            s.normed1[band] = normed
            s.root1[band] = jnp.broadcast_to(root, (BAND, 128))

    bands(first_norm)
    ready("expand")
    ready("contract")

    def feed(tile):
        expanded = nn(s.first_low[...], w.expand[:, tile]) + b_expand[:, tile]
        cumulative = 0.5 * (1.0 + lax.erf(expanded * 0.7071067811865476))
        activated = (expanded * cumulative).astype(LOW)
        if keep:
            s.slope[:, tile] = (
                cumulative + expanded * jnp.exp(-0.5 * expanded * expanded) * 0.3989422804014327
            ).astype(LOW)
            s.activated[:, tile] = activated
        s.total[...] += nn(activated, w.contract[tile, :])

    tiles_loop(feed)

    def second_norm(band):
        normed, root = norm_rows(s.total[band])
        if keep:
            s.normed2[band] = normed
            s.root2[band] = jnp.broadcast_to(root, (BAND, 128))
        s.out[band] = (normed * row(GAIN2) + row(SHIFT2)).astype(s.out.dtype)

    bands(second_norm)


def backward_feed(grad, w, vec, s, sums=None):
    row = lambda k: vec[k : k + 1, :]

    def second_norm(band):
        upper = grad[band].astype(WIDE)
        normed = s.normed2[band]
        lower = norm_rows_back(upper * row(GAIN2), normed, s.root2[band, :1])
        s.total[band] = lower
        s.branch[band] = lower.astype(LOW)
        if sums is not None:
            sums(band, 10, upper * normed)
            sums(band, 11, upper)
            sums(band, 9, lower.astype(LOW).astype(WIDE))

    bands(second_norm)


def backward_expand(w, vec, s, sums=None, tile_sums=None):
    row = lambda k: vec[k : k + 1, :]

    def feed(tile):
        lower = (nt(s.branch[...], w.contract[tile, :]) * s.slope[:, tile].astype(WIDE)).astype(LOW)
        s.expanded[:, tile] = lower
        if tile_sums is not None:
            tile_sums(tile, lower)
        s.total[...] += nt(lower, w.expand[:, tile])

    tiles_loop(feed)

    def first_norm(band):
        upper = s.total[band]
        normed = s.normed1[band]
        lower = norm_rows_back(upper * row(GAIN1), normed, s.root1[band, :1])
        s.total[band] = lower
        s.attended[band] = lower.astype(LOW)
        if sums is not None:
            sums(band, 3, upper * normed)
            sums(band, 4, upper)
            sums(band, 2, lower.astype(LOW).astype(WIDE))

    bands(first_norm)


def backward_attend_first(w, s, table=None):
    s.dmixed[...] = nt(s.attended[...], w.out[...]).astype(LOW)

    def attend(pair, lanes):
        slopes = []
        for seq in range(SEQS):
            own = pl.ds(seq * L, L)
            probs = s.probs[seq, pair]
            below = halves(seq_rows(s.dmixed, seq, lanes))
            dprobs = nt(below, s.value[own, lanes])
            s.dvalue[own, lanes] = tn(probs, below).astype(LOW)
            weight = probs.astype(WIDE)
            dscores = (
                weight * (dprobs - jnp.sum(weight * dprobs, axis=-1, keepdims=True))
            ).astype(LOW)
            dquery = nn(side(dscores), halves(s.key[own, lanes])) * SCALE
            store_rows(s.dquery, seq, lanes, dquery.astype(LOW))
            dkey = tn(dscores, halves(seq_rows(s.query, seq, lanes))) * SCALE
            s.dkey[own, lanes] = dkey.astype(LOW)
            slopes.append(dscores)
        if table is not None:
            table(pair, slopes)

    pairs_loop(attend)


def backward_attend_last(w, s):
    s.total[...] += nt(s.dquery[...], w.query[...])
    s.total[:CONTENT] += nt(s.dkey[...], w.key[...]) + nt(s.dvalue[...], w.value[...])


def backward_attend(w, s, table=None):
    backward_attend_first(w, s, table)
    backward_attend_last(w, s)


class Names:
    def __init__(self, **named):
        self.__dict__.update(named)


MATRICES = ("query", "key", "value", "out", "expand", "contract")
MATRIX_SHAPES = {
    "query": (D, D),
    "key": (D, D),
    "value": (D, D),
    "out": (D, D),
    "expand": (D, FF),
    "contract": (FF, D),
}
MASK_SHAPE = (SEQS, PAIRS, 2 * SEQ_ROWS, L)
KEPT = {
    "query": ((ROWS, D), LOW),
    "key": ((CONTENT, D), LOW),
    "value": ((CONTENT, D), LOW),
    "probs": (MASK_SHAPE, LOW),
    "mixed": ((ROWS, D), LOW),
    "normed1": ((ROWS, D), WIDE),
    "root1": ((ROWS, 128), WIDE),
    "first_low": ((ROWS, D), LOW),
    "slope": ((ROWS, FF), LOW),
    "activated": ((ROWS, FF), LOW),
    "normed2": ((ROWS, D), WIDE),
    "root2": ((ROWS, 128), WIDE),
}
PASSED = {
    "branch": ((ROWS, D), LOW),
    "expanded": ((ROWS, FF), LOW),
    "attended": ((ROWS, D), LOW),
    "dmixed": ((ROWS, D), LOW),
    "dvalue": ((CONTENT, D), LOW),
    "dquery": ((ROWS, D), LOW),
    "dkey": ((CONTENT, D), LOW),
}
ANY = pl.BlockSpec(memory_space=pl.ANY)
VMEM = pl.BlockSpec(memory_space=pltpu.VMEM)
LIMIT = 60 * 1024 * 1024


def fetcher(pairs, sems):
    copies = {}
    for index, (name, source, target) in enumerate(pairs):
        copies[name] = pltpu.make_async_copy(source, target, sems.at[index])
        copies[name].start()
    return lambda name: copies[name].wait()


def front_kernel(x, *refs):
    matrices, (masks, vec, b_expand, out), rest = refs[:6], refs[6:10], refs[10:]
    held, (mask_buf, query, key, value, mixed, first_low, total, sems) = rest[:6], rest[6:]
    ready = fetcher(
        [(n, a, b) for n, a, b in zip(MATRICES[:3], matrices[:3], held[:3])]
        + [("masks", masks, mask_buf)]
        + [(n, a, b) for n, a, b in zip(MATRICES[3:], matrices[3:], held[3:])],
        sems,
    )
    s = Names(
        query=query, key=key, value=value, mixed=mixed, first_low=first_low, total=total, out=out
    )
    forward(x, Names(**dict(zip(MATRICES, held))), vec, b_expand, mask_buf, s, False, ready)


def front(x, matrices, masks, vec, b_expand):
    return pl.pallas_call(
        front_kernel,
        out_shape=jax.ShapeDtypeStruct((ROWS, D), LOW),
        in_specs=[VMEM] + [ANY] * 7 + [VMEM] * 2,
        out_specs=VMEM,
        scratch_shapes=[pltpu.VMEM(MATRIX_SHAPES[n], LOW) for n in MATRICES]
        + [pltpu.VMEM(MASK_SHAPE, WIDE)]
        + [pltpu.VMEM(*KEPT[n]) for n in ("query", "key", "value", "mixed", "first_low")]
        + [pltpu.VMEM((ROWS, D), WIDE), pltpu.SemaphoreType.DMA((7,))],
        compiler_params=pltpu.CompilerParams(vmem_limit_bytes=LIMIT),
        name="front",
    )(x, *matrices, masks, vec, b_expand)


HALF = FF // 2
QUARTER = D // 4
EARLY = 3 * D + HALF
LATE = D + HALF
PIECE = CONTENT + ROWS
EXTRA = 32
SMEM = pl.BlockSpec(memory_space=pltpu.SMEM)
LATER = ("normed2", "root2", "slope", "normed1", "root1", "activated", "first_low")
SAVED = LATER + ("probs", "query", "key", "value")


def columns(ref, start, size):
    return ref.at[:, pl.ds(pl.multiple_of(start, 128), size)]


def rows_at(ref, start, size):
    return ref.at[pl.ds(pl.multiple_of(start, 64), size)]


def start_all(pairs, sems, base=0):
    copies = [
        pltpu.make_async_copy(source, target, sems.at[base + index])
        for index, (source, target) in enumerate(pairs)
    ]
    for copy in copies:
        copy.start()
    return copies


def middle_kernel(info, x, cot, *refs):
    matrices, (masks, vec, b_expand), rest = refs[:6], refs[6:9], refs[9:]
    (out, grad, early, pair_out), rest = rest[:4], rest[4:]
    saved_out, rest = rest[: len(SAVED)], rest[len(SAVED) :]
    held, (mask_buf,), rest = rest[:6], rest[6:7], rest[7:]
    kept, rest = rest[: len(KEPT)], rest[len(KEPT) :]
    passed, rest = rest[: len(PASSED)], rest[len(PASSED) :]
    total, sems, out_sems = rest
    ready = fetcher(
        [(n, a, b) for n, a, b in zip(MATRICES[:3], matrices[:3], held[:3])]
        + [("masks", masks, mask_buf)]
        + [(n, a, b) for n, a, b in zip(MATRICES[3:], matrices[3:], held[3:])],
        sems,
    )
    w = Names(**dict(zip(MATRICES, held)))
    s = Names(total=total, out=out, **dict(zip(KEPT, kept)), **dict(zip(PASSED, passed)))
    forward(x, w, vec, b_expand, mask_buf, s, True, ready)
    other = 1 - info[0]
    pairs = [
        (x, early.at[:, :D]),
        (s.mixed, early.at[:, D : 2 * D]),
        (s.first_low, early.at[:, 2 * D : 3 * D]),
        (columns(s.activated, other * HALF, HALF), early.at[:, 3 * D :]),
        (x, pair_out.at[0]),
        (s.mixed, pair_out.at[1]),
    ] + [(s.__dict__[n], ref) for n, ref in zip(SAVED, saved_out)]
    copies = start_all(pairs, out_sems)
    backward_feed(cot, w, vec, s)
    backward_expand(w, vec, s)
    backward_attend(w, s)
    grad[...] = total[...].astype(LOW)
    for copy in copies:
        copy.wait()


def middle(info, x, cot, matrices, masks, vec, b_expand):
    return pl.pallas_call(
        middle_kernel,
        out_shape=[
            jax.ShapeDtypeStruct((ROWS, D), WIDE),
            jax.ShapeDtypeStruct((ROWS, D), LOW),
            jax.ShapeDtypeStruct((ROWS, EARLY), LOW),
            jax.ShapeDtypeStruct((2, ROWS, D), LOW),
        ]
        + [jax.ShapeDtypeStruct(*KEPT[n]) for n in SAVED],
        in_specs=[SMEM] + [VMEM] * 2 + [ANY] * 7 + [VMEM] * 2,
        out_specs=[VMEM] * 2 + [ANY] * (2 + len(SAVED)),
        scratch_shapes=[pltpu.VMEM(MATRIX_SHAPES[n], LOW) for n in MATRICES]
        + [pltpu.VMEM(MASK_SHAPE, WIDE)]
        + [pltpu.VMEM(*KEPT[n]) for n in KEPT]
        + [pltpu.VMEM(*PASSED[n]) for n in PASSED]
        + [
            pltpu.VMEM((ROWS, D), WIDE),
            pltpu.SemaphoreType.DMA((7,)),
            pltpu.SemaphoreType.DMA((6 + len(SAVED),)),
        ],
        compiler_params=pltpu.CompilerParams(vmem_limit_bytes=LIMIT),
        name="middle",
    )(info, x, cot, *matrices, masks, vec, b_expand)


def feed_back_kernel(info, upper, vec, *refs):
    names = ("normed2", "root2", "contract", "slope", "expand", "normed1", "root1")
    sources, rest = refs[:7], refs[7:]
    (total, branch, attended, small, own, late), rest = rest[:6], rest[6:]
    held, (expanded, sems, out_sems) = rest[:7], rest[7:]
    ready = fetcher(list(zip(names, sources, held)), sems)
    buffers = dict(zip(names, held))
    w = Names(contract=buffers["contract"], expand=buffers["expand"])
    s = Names(
        total=total,
        branch=branch,
        attended=attended,
        expanded=expanded,
        **{n: buffers[n] for n in ("normed2", "root2", "slope", "normed1", "root1")},
    )
    small[...] = jnp.zeros_like(small)

    def sums(band, place, value):
        small[place : place + 1, :] += jnp.sum(value, axis=0, keepdims=True)

    ready("normed2")
    ready("root2")
    backward_feed(upper, w, vec, s, sums)
    copies = start_all([(branch, late.at[:, :D])], out_sems)
    for name in names[2:]:
        ready(name)

    def tile_sums(tile, value):
        place = 5 + tile.start // D
        small[place : place + 1, :] = jnp.sum(value.astype(WIDE), axis=0, keepdims=True)
        if tile.stop == FF:
            mine = info[0]
            copies.extend(
                start_all(
                    [
                        (columns(expanded, mine * HALF, HALF), own),
                        (columns(expanded, (1 - mine) * HALF, HALF), late.at[:, D:]),
                    ],
                    out_sems,
                    1,
                )
            )

    backward_expand(w, vec, s, sums, tile_sums)
    for copy in copies:
        copy.wait()


def feed_back(info, upper, vec, matrices, saved):
    shapes = [KEPT["normed2"], KEPT["root2"], (MATRIX_SHAPES["contract"], LOW), KEPT["slope"]]
    shapes += [(MATRIX_SHAPES["expand"], LOW), KEPT["normed1"], KEPT["root1"]]
    return pl.pallas_call(
        feed_back_kernel,
        out_shape=[
            jax.ShapeDtypeStruct((ROWS, D), WIDE),
            jax.ShapeDtypeStruct((ROWS, D), LOW),
            jax.ShapeDtypeStruct((ROWS, D), LOW),
            jax.ShapeDtypeStruct((16, D), WIDE),
            jax.ShapeDtypeStruct((ROWS, HALF), LOW),
            jax.ShapeDtypeStruct((ROWS, LATE), LOW),
        ],
        in_specs=[SMEM] + [VMEM] * 2 + [ANY] * 7,
        out_specs=[VMEM] * 4 + [ANY] * 2,
        scratch_shapes=[pltpu.VMEM(*shape) for shape in shapes]
        + [
            pltpu.VMEM((ROWS, FF), LOW),
            pltpu.SemaphoreType.DMA((7,)),
            pltpu.SemaphoreType.DMA((3,)),
        ],
        compiler_params=pltpu.CompilerParams(vmem_limit_bytes=LIMIT),
        name="feed_back",
    )(
        info,
        upper,
        vec,
        saved["normed2"],
        saved["root2"],
        matrices[5],
        saved["slope"],
        matrices[4],
        saved["normed1"],
        saved["root1"],
    )


def feed_grads_kernel(info, act, first_low, branch, own, early, late, *refs):
    outs, (a_act, a_first, b_branch, b_own, stage, sems, out_sems) = refs[:8], refs[8:]
    core, place = info[0], info[1]
    copies = start_all(
        [
            (columns(act, core * HALF, HALF), a_act.at[:ROWS]),
            (early.at[:, 3 * D :], a_act.at[ROWS:]),
            (branch, b_branch.at[:ROWS]),
            (late.at[:, :D], b_branch.at[ROWS:]),
            (first_low, a_first.at[:ROWS]),
            (early.at[:, 2 * D : 3 * D], a_first.at[ROWS:]),
            (own, b_own.at[:ROWS]),
            (late.at[:, D:], b_own.at[ROWS:]),
        ],
        sems,
    )
    sent = []

    def send(block):
        for k in range(4):
            quarter = lax.rem(place + k, 4)
            sent.extend(
                start_all(
                    [
                        (
                            rows_at(stage.at[block], quarter * QUARTER, QUARTER),
                            outs[2 * k + block // 2].at[
                                block % 2 * QUARTER : (block % 2 + 1) * QUARTER
                            ],
                        )
                    ],
                    out_sems,
                    block * 4 + k,
                )
            )

    for copy in copies[:4]:
        copy.wait()
    for block in range(2):
        for part in range(3):
            start = block * D + part * 256
            stage[block, part * 256 : (part + 1) * 256] = tn(
                a_act[:, start : start + 256], b_branch[...]
            ).astype(LOW)
        send(block)
    for copy in copies[4:]:
        copy.wait()
    for block in range(2):
        for part in range(3):
            stage[2 + block, part * 256 : (part + 1) * 256] = tn(
                a_first[:, part * 256 : (part + 1) * 256], b_own[:, block * D : (block + 1) * D]
            ).astype(LOW)
        send(2 + block)
    for copy in sent:
        copy.wait()


def feed_grads(info, act, first_low, branch, own, early, late):
    return pl.pallas_call(
        feed_grads_kernel,
        out_shape=[jax.ShapeDtypeStruct((2 * QUARTER, D), LOW)] * 8,
        in_specs=[SMEM] + [ANY] * 6,
        out_specs=[ANY] * 8,
        scratch_shapes=[
            pltpu.VMEM((2 * ROWS, HALF), LOW),
            pltpu.VMEM((2 * ROWS, D), LOW),
            pltpu.VMEM((2 * ROWS, D), LOW),
            pltpu.VMEM((2 * ROWS, HALF), LOW),
            pltpu.VMEM((4, D, D), LOW),
            pltpu.SemaphoreType.DMA((8,)),
            pltpu.SemaphoreType.DMA((16,)),
        ],
        compiler_params=pltpu.CompilerParams(vmem_limit_bytes=LIMIT),
        name="feed_grads",
    )(info, act, first_low, branch, own, early, late)


def attend_back_kernel(info, total_in, attended, small_in, spread, output, *refs):
    names = ("out", "value", "probs", "key", "query", "w_query", "w_key", "w_value")
    sources, rest = refs[:8], refs[8:]
    (content_ends, query_ends, small, table, own, send), rest = rest[:6], rest[6:]
    held, (total, dmixed, pieces, sems, out_sems) = rest[:8], rest[8:]
    ready = fetcher(list(zip(names, sources, held)), sems)
    buffers = dict(zip(names, held))
    w = Names(out=buffers["out"], query=buffers["w_query"], key=buffers["w_key"])
    w.value = buffers["w_value"]
    s = Names(
        total=total,
        attended=attended,
        dmixed=dmixed,
        dquery=pieces.at[0, :ROWS],
        dkey=pieces.at[0, ROWS:],
        dvalue=pieces.at[1, ROWS:],
        **{n: buffers[n] for n in ("probs", "query", "key", "value")},
    )
    total[...] = total_in[...]
    pieces[1, :ROWS] = attended[...]

    def table_sum(pair, slopes):
        for odd in range(2):
            both = jnp.concatenate(
                [slope[odd * SEQ_ROWS : (odd + 1) * SEQ_ROWS] for slope in slopes]
            )
            table[2 * pair + odd] = nn(spread[...], both)

    for name in names:
        ready(name)
    backward_attend_first(w, s, table_sum)
    copies = start_all([(pieces.at[info[0]], own), (pieces.at[1 - info[0]], send)], out_sems)
    small[...] = small_in[...]
    small[0:1, :] = jnp.sum(s.dquery[...].astype(WIDE), axis=0, keepdims=True)
    small[1:2, :] = jnp.sum(s.dvalue[...].astype(WIDE), axis=0, keepdims=True)
    backward_attend_last(w, s)
    first = info[2] == 1
    content_ends[...] = jnp.where(first, total[:CONTENT], output[:CONTENT])
    picks = query_ends.shape[0] // SEQS
    for seq in range(SEQS):
        band = slice(CONTENT + seq * PICKS, CONTENT + seq * PICKS + picks)
        query_ends[seq * picks : (seq + 1) * picks] = jnp.where(first, total[band], output[band])
    for copy in copies:
        copy.wait()


def attend_back(info, total, attended, small, spread, output, matrices, saved, picks):
    sources = [matrices[3], saved["value"], saved["probs"], saved["key"], saved["query"]]
    sources += [matrices[0], matrices[1], matrices[2]]
    return pl.pallas_call(
        attend_back_kernel,
        out_shape=[
            jax.ShapeDtypeStruct((CONTENT, D), WIDE),
            jax.ShapeDtypeStruct((SEQS * picks, D), WIDE),
            jax.ShapeDtypeStruct((16, D), WIDE),
            jax.ShapeDtypeStruct((H, L, L), WIDE),
            jax.ShapeDtypeStruct((PIECE, D), LOW),
            jax.ShapeDtypeStruct((PIECE, D), LOW),
        ],
        in_specs=[SMEM] + [VMEM] * 5 + [ANY] * 8,
        out_specs=[VMEM] * 4 + [ANY] * 2,
        scratch_shapes=[pltpu.VMEM(ref.shape, LOW) for ref in sources]
        + [
            pltpu.VMEM((ROWS, D), WIDE),
            pltpu.VMEM((ROWS, D), LOW),
            pltpu.VMEM((2, PIECE, D), LOW),
            pltpu.SemaphoreType.DMA((8,)),
            pltpu.SemaphoreType.DMA((2,)),
        ],
        compiler_params=pltpu.CompilerParams(vmem_limit_bytes=LIMIT),
        name="attend_back",
    )(info, total, attended, small, spread, output, *sources)


def attend_grads_kernel(info, pair, early, own, arrived, small, *refs):
    outs, rest = refs[:8], refs[8:]
    a_rows, a_content, b_rows, b_content, stage, extra, sems, out_sems = rest
    core, place = info[0], info[1]
    copies = start_all(
        [
            (pair.at[core], a_rows.at[:ROWS]),
            (columns(early, core * D, D), a_rows.at[ROWS:]),
            (own.at[:ROWS], b_rows.at[:ROWS]),
            (arrived.at[:ROWS], b_rows.at[ROWS:]),
            (pair.at[0, :CONTENT], a_content.at[:CONTENT]),
            (early.at[:CONTENT, :D], a_content.at[CONTENT:]),
            (own.at[ROWS:], b_content.at[:CONTENT]),
            (arrived.at[ROWS:], b_content.at[CONTENT:]),
        ],
        sems,
    )
    extra[...] = jnp.zeros_like(extra)
    part = small[pl.ds(pl.multiple_of(core * 8, 8), 8), :]
    extra[0] = jnp.concatenate([part, jnp.zeros((EXTRA - 8, D), WIDE)]).astype(LOW)
    sent = []
    for block, (former, latter) in enumerate(((a_rows, b_rows), (a_content, b_content))):
        for copy in copies[4 * block : 4 * block + 4]:
            copy.wait()
        for part in range(3):
            stage[block, part * 256 : (part + 1) * 256] = tn(
                former[:, part * 256 : (part + 1) * 256], latter[...]
            ).astype(LOW)
        for k in range(4):
            quarter = lax.rem(place + k, 4)
            target = outs[2 * k + block]
            sent.extend(
                start_all(
                    [
                        (rows_at(stage.at[block], quarter * QUARTER, QUARTER), target.at[:QUARTER]),
                        (extra.at[block], target.at[QUARTER:]),
                    ],
                    out_sems,
                    block * 8 + 2 * k,
                )
            )
    for copy in sent:
        copy.wait()


def attend_grads(info, pair, early, own, arrived, small):
    return pl.pallas_call(
        attend_grads_kernel,
        out_shape=[jax.ShapeDtypeStruct((QUARTER + EXTRA, D), LOW)] * 8,
        in_specs=[SMEM] + [ANY] * 4 + [VMEM],
        out_specs=[ANY] * 8,
        scratch_shapes=[
            pltpu.VMEM((2 * ROWS, D), LOW),
            pltpu.VMEM((2 * CONTENT, D), LOW),
            pltpu.VMEM((2 * ROWS, D), LOW),
            pltpu.VMEM((2 * CONTENT, D), LOW),
            pltpu.VMEM((2, D, D), LOW),
            pltpu.VMEM((2, EXTRA, D), LOW),
            pltpu.SemaphoreType.DMA((8,)),
            pltpu.SemaphoreType.DMA((16,)),
        ],
        compiler_params=pltpu.CompilerParams(vmem_limit_bytes=LIMIT),
        name="attend_grads",
    )(info, pair, early, own, arrived, small)


def spread_kernel(targets, keys, count, info, *refs):
    pieces = refs[: len(keys)]
    outs = refs[len(refs) - 2 * len(keys) - 2 - count : len(refs) - 2 * len(keys) - 2]
    held = refs[len(refs) - 2 * len(keys) - 2 : len(refs) - len(keys) - 2]
    wide_held = refs[len(refs) - len(keys) - 2 : len(refs) - 2]
    sems, out_sems = refs[-2:]
    copies = start_all(list(zip(pieces, held)), sems)
    finish = []
    for index, (sibling, k, half) in enumerate(keys):
        core = 1 - info[0] if sibling else info[0]
        quarter = lax.rem((info[3] if sibling else info[1]) + k, 4)
        copies[index].wait()
        wide_held[index][...] = held[index][...].astype(WIDE)
        finish.append(targets(outs, wide_held[index], half, core, quarter, out_sems, index))
    for action in finish:
        action()


def feed_targets(outs, source, half, core, quarter, sems, index):
    copies = []
    for block in range(2):
        part = source.at[block * QUARTER : (block + 1) * QUARTER]
        if half == 0:
            target = rows_at(outs[0], core * HALF + block * D + quarter * QUARTER, QUARTER)
        else:
            target = columns(
                rows_at(outs[1], quarter * QUARTER, QUARTER), (core * 2 + block) * D, D
            )
        copies.append((part, target))
    copies = start_all(copies, sems, 2 * index)

    def finish():
        for copy in copies:
            copy.wait()

    return finish


def attend_targets(outs, source, half, core, quarter, sems, index):
    part = source.at[:QUARTER]
    copies = [
        pltpu.make_async_copy(
            part, rows_at(outs[2 * number + half], quarter * QUARTER, QUARTER), sems.at[2 * index]
        )
        for number in range(2)
    ]
    for number in range(2):
        pl.when(core == number)(copies[number].start)

    def finish():
        for number in range(2):
            pl.when(core == number)(copies[number].wait)

    return finish


def spread_pieces(targets, shapes, info, pieces, outs, name):
    keys = tuple(pieces)
    arrays = [pieces[key] for key in keys]
    given = list(outs or ())

    def kernel(*refs):
        spread_kernel(targets, keys, len(shapes), *refs)

    return pl.pallas_call(
        kernel,
        out_shape=[jax.ShapeDtypeStruct(shape, WIDE) for shape in shapes],
        in_specs=[SMEM] + [ANY] * (len(keys) + len(given)),
        out_specs=[ANY] * len(shapes),
        scratch_shapes=[pltpu.VMEM(array.shape, LOW) for array in arrays]
        + [pltpu.VMEM(array.shape, WIDE) for array in arrays]
        + [pltpu.SemaphoreType.DMA((len(keys),)), pltpu.SemaphoreType.DMA((2 * len(keys),))],
        input_output_aliases={1 + len(keys) + i: i for i in range(len(given))},
        compiler_params=pltpu.CompilerParams(vmem_limit_bytes=LIMIT),
        cost_estimate=pl.CostEstimate(
            flops=0, bytes_accessed=sum(array.size * 6 for array in arrays), transcendentals=0
        ),
        name=name,
    )(info, *arrays, *given)


LIMITS = (12, 16, 23, 32, 46, 64, 91)
TOP_PRECISION = lax.Precision.HIGHEST


def bucket_of(relative):
    distance = jnp.abs(relative)
    beyond = 8 + sum(((distance >= limit).astype(jnp.int32) for limit in LIMITS))
    within = jnp.where(distance < 8, distance, beyond)
    return within + 16 * (relative > 0).astype(jnp.int32)


def geometry(order_row, pos_row, tag_row, table):
    positions = lax.iota(jnp.int32, L)
    matches = pos_row[:, None] == positions[None, :]
    predicted = jnp.any(matches, axis=0)
    query_rank = jnp.sum(jnp.where(matches, order_row[None, :], 0), axis=1)
    query_tag = jnp.sum(jnp.where(matches, tag_row[None, :], 0), axis=1)
    row_rank = jnp.concatenate([order_row, query_rank])
    row_tag = jnp.concatenate([tag_row, query_tag])
    row_place = jnp.concatenate([positions, pos_row])
    row_flag = jnp.concatenate([predicted, jnp.ones(pos_row.shape, jnp.bool_)])
    strict = jnp.concatenate([jnp.zeros((L,), jnp.int32), jnp.ones(pos_row.shape, jnp.int32)])
    same_group = row_tag[:, None] == tag_row[None, :]
    earlier = order_row[None, :] + strict[:, None] <= row_rank[:, None]
    allowed = same_group & (~predicted[None, :] | row_flag[:, None] & earlier)
    buckets = bucket_of(positions[None, :] - row_place[:, None])
    one_hot = (buckets[None] == lax.iota(jnp.int32, NB)[:, None, None]).astype(WIDE)
    score_bias = jnp.einsum("krl,kh->hrl", one_hot, table, precision=TOP_PRECISION)
    masked = jnp.where(allowed[None], score_bias, -1e30)
    masked = jnp.pad(masked, ((0, 0), (0, SEQ_ROWS - masked.shape[1]), (0, 0)))
    padded = jnp.pad(matches.astype(LOW), ((0, PICKS - matches.shape[0]), (0, 0)))
    spread = jnp.concatenate([jnp.eye(L, dtype=LOW), padded.T], axis=1)
    return (masked, spread)


def diagonals():
    positions = lax.iota(jnp.int32, L)
    buckets = bucket_of(positions[None, :] - positions[:, None])
    return (buckets[None] == lax.iota(jnp.int32, NB)[:, None, None]).astype(WIDE)


PLANE = ("x", "y", "c")


def shift(value, axis, by):
    size = lax.axis_size(axis)
    return lax.ppermute(value, axis, [(i, (i + by) % size) for i in range(size)])


def turn(value, outer, by):
    pairs = []
    for i in range(4):
        for j in range(4):
            for c in range(2):
                if (c == 0) == outer:
                    target = ((i + by) % 4, j)
                else:
                    target = (i, (j + by) % 4)
                pairs.append(((i * 4 + j) * 2 + c, (target[0] * 4 + target[1]) * 2 + c))
    return lax.ppermute(value, PLANE, pairs)


def place(outer):
    return jnp.where(
        (lax.axis_index("c") == 0) == outer, lax.axis_index("x"), lax.axis_index("y")
    )


def wide(value):
    return value.astype(WIDE)


def pick(parts, index):
    return lax.dynamic_index_in_dim(parts, index, 0, keepdims=False)


def total_of(*terms):
    return sum(wide(term) for term in terms).astype(LOW)


def chain_reduce(terms):
    (own0, own1), (after0, after1), (across0, across1), (before0, before1) = terms
    far0 = turn(across0, True, 1)
    far1 = turn(across1, True, -1)
    left1 = turn(after1, True, 1)
    right0 = turn(before0, True, -1)
    left0 = turn(total_of(after0, far0), True, 1)
    right1 = turn(total_of(before1, far1), True, -1)
    sums = [total_of(own0, left0, right0), total_of(own1, left1, right1)]
    count = own0.shape[0] // 4
    parts = jnp.concatenate([part.reshape(4, count, D) for part in sums], axis=1)
    me = place(False)
    arrived = [turn(pick(parts, (me + by) % 4), False, by) for by in (1, 2, -1)]
    part = total_of(pick(parts, me), *arrived).reshape(2, count, D)
    me = lax.axis_index("z")
    return total_of(pick(part, me), shift(pick(part, 1 - me), "z", 1))


def chain_gather(part):
    count = part.shape[0]
    arrived = shift(part, "z", 1)
    low = lax.axis_index("z") == 0
    part = jnp.concatenate([jnp.where(low, part, arrived), jnp.where(low, arrived, part)])
    me = place(False)
    whole = jnp.zeros((4, 2 * count, D), LOW)
    for k, piece in enumerate([part] + [turn(part, False, -by) for by in (1, 2, -1)]):
        whole = lax.dynamic_update_index_in_dim(whole, piece, (me + k) % 4, 0)
    own = [whole[:, half * count : (half + 1) * count].reshape(4 * count, D) for half in range(2)]
    pieces = {(0, 0): own[0], (0, 1): own[1]}
    pieces[3, 0] = turn(own[0], True, 1)
    pieces[1, 1] = turn(own[1], True, -1)
    pieces[3, 1] = turn(own[1], True, 1)
    pieces[1, 0] = turn(own[0], True, -1)
    pieces[2, 0] = turn(pieces[3, 0], True, 1)
    pieces[2, 1] = turn(pieces[1, 1], True, -1)
    near = {(0,) + key: piece for key, piece in pieces.items()}
    far = {(1,) + key: shift(piece, "c", 1) for key, piece in pieces.items()}
    return near | far


def settle(targets, shapes, info, pieces, name):
    outs = None
    for last in (False, True):
        some = {key: piece for key, piece in pieces.items() if (key[1] == 2) == last}
        outs = spread_pieces(targets, shapes, info, some, outs, name + "_" + "ab"[last])
    return outs


def send(value, by):
    return lax.ppermute(value, "s", [(0, 1)] if by > 0 else [(1, 0)])


def on_device(
    content_in,
    query_in,
    content_cot,
    query_cot,
    order_rank,
    query_pos,
    group_tag,
    *rest,
):
    (
        w_query,
        b_query,
        w_key,
        w_value,
        b_value,
        w_out,
        b_out,
        norm1_gain,
        norm1_bias,
        w_expand,
        b_expand,
        w_contract,
        b_contract,
        norm2_gain,
        norm2_bias,
    ) = (argument[0] for argument in rest[:-1])
    rel_table = rest[-1]
    is_first = lax.axis_index("s") == 0
    picks = query_pos.shape[1]

    def rows_of(content, query):
        query = jnp.pad(query.reshape(SEQS, picks, D), ((0, 0), (0, PICKS - picks), (0, 0)))
        return jnp.concatenate([content, query.reshape(SEQS * PICKS, D)])

    masks, spread = jax.vmap(geometry, in_axes=(0, 0, 0, None))(
        order_rank, query_pos, group_tag, rel_table
    )
    masks = masks.reshape(MASK_SHAPE)
    spread = jnp.concatenate([spread[0], spread[1]], axis=1)
    own_rows = rows_of(content_in, query_in)
    cotangent = rows_of(content_cot, query_cot)
    matrices = (w_query, w_key, w_value, w_out, w_expand, w_contract)
    vec = jnp.stack(
        [b_query, b_value, b_out, norm1_gain, norm1_bias, b_contract, norm2_gain, norm2_bias]
    )
    b_expand = b_expand[None]
    core = lax.axis_index("c")
    info = jnp.stack([core, place(True), is_first.astype(jnp.int32), place(False)])
    first_out = front(own_rows, matrices, masks, vec, b_expand)
    rows = jnp.where(is_first, own_rows, send(first_out, 1))
    output, rows_grad, early, pair, *kept = middle(
        info, rows, cotangent, matrices, masks, vec, b_expand
    )
    saved = dict(zip(SAVED, kept))
    upper = jnp.where(is_first, send(rows_grad, -1), cotangent)
    early = shift(early, "c", 1)
    total, branch, attended, small, own, late = feed_back(info, upper, vec, matrices, saved)
    late = shift(late, "c", 1)
    terms = feed_grads(info, saved["activated"], saved["first_low"], branch, own, early, late)
    feed_part = chain_reduce([terms[2 * k : 2 * k + 2] for k in range(4)])
    content_ends, query_ends, small, slopes, own, pass_on = attend_back(
        info, total, attended, small, spread, output, matrices, saved, picks
    )
    arrived = shift(pass_on, "c", 1)
    table = jnp.einsum("krl,hrl->kh", diagonals(), slopes, precision=TOP_PRECISION)
    table = jnp.pad(table.reshape(1, NB * H), ((0, 0), (0, D - NB * H)))
    small = jnp.concatenate([small[:12], table, small[13:]])
    small = small + shift(small, "c", 1)
    small = jnp.concatenate([small[:12], small[12:] + shift(small[12:], "s", 1)])
    terms = attend_grads(info, pair, early, own, arrived, small)
    attend_part = chain_reduce([terms[2 * k : 2 * k + 2] for k in range(4)])
    feed_pieces = chain_gather(feed_part)
    attend_pieces = chain_gather(attend_part)
    contract, expand = settle(feed_targets, ((FF, D), (D, FF)), info, feed_pieces, "feed_out")
    g_query, g_key, g_out, g_value = settle(
        attend_targets, ((D, D),) * 4, info, attend_pieces, "attend_out"
    )
    mine, other = (attend_pieces[far, 0, 0][QUARTER : QUARTER + 8] for far in (0, 1))
    small_sum = wide(
        jnp.concatenate([jnp.where(core == 0, mine, other), jnp.where(core == 0, other, mine)])
    )
    table_total = small_sum[12, : NB * H].reshape(NB, H)
    row = lambda k: small_sum[k][None]
    return (
        content_ends[None],
        query_ends[None],
        g_query[None],
        row(0),
        g_key[None],
        g_value[None],
        row(1),
        g_out[None],
        row(2),
        row(3),
        row(4),
        expand[None],
        small_sum[5:9].reshape(1, FF),
        contract[None],
        row(9),
        row(10),
        row(11),
        table_total,
    )


DP = ("z", "x", "y", "c")


def solution(mesh):
    mesh = jax.sharding.Mesh(mesh.devices.reshape(2, 2, 4, 4, 2), ("s",) + DP)
    layer_specs = tuple(
        P("s", *([None] * (rank - 1))) for rank in (3, 2, 3, 3, 2, 3, 2, 2, 2, 3, 2, 3, 2, 2, 2)
    )
    in_specs = (P(DP, None),) * 7 + layer_specs + (P(),)
    out_specs = (P("s", DP, None),) * 2 + layer_specs + (P(),)
    return jax.shard_map(
        on_device, mesh=mesh, in_specs=in_specs, out_specs=out_specs, check_vma=False
    )
```

```python
import jax
import jax.numpy as jnp
from jax import lax
from jax.experimental import pallas as pl
from jax.experimental.pallas import tpu as pltpu
from jax.sharding import PartitionSpec as P

D = 768
H = 12
HD = 64
FF = 3072
NB = 32
L = 128
PAIRS = H // 2
SEQS = 2
PICKS = 32
ROWS = L + PICKS
EPSILON = 1e-05
SCALE = HD ** (-0.5)
TILE = 1536
LOW = jnp.bfloat16
WIDE = jnp.float32
HALF = FF // 2
QUARTER = D // 4
EARLY = 3 * D + HALF
LATE = D + HALF
EXTRA = 32
ALL_ROWS = SEQS * ROWS
ALL_CONTENT = SEQS * L
PIECE = ALL_ROWS + ALL_CONTENT


def nn(former, latter):
    return lax.dot_general(
        former, latter, (((1,), (0,)), ((), ())), preferred_element_type=WIDE
    )


def nt(former, latter):
    return lax.dot_general(
        former, latter, (((1,), (1,)), ((), ())), preferred_element_type=WIDE
    )


def tn(former, latter):
    return lax.dot_general(
        former, latter, (((0,), (0,)), ((), ())), preferred_element_type=WIDE
    )


def halves(value):
    even = lax.broadcasted_iota(jnp.int32, value.shape, 1) < HD
    zero = jnp.zeros_like(value)
    return jnp.concatenate([jnp.where(even, value, zero), jnp.where(even, zero, value)])


def side(value):
    count = value.shape[0] // 2
    return jnp.concatenate([value[:count], value[count:]], axis=1)


def norm_rows(values):
    centered = values - jnp.mean(values, axis=-1, keepdims=True)
    variance = jnp.mean(centered * centered, axis=-1, keepdims=True)
    root = lax.rsqrt(variance + EPSILON)
    return (centered * root, root)


def norm_rows_back(scaled, normed, root):
    return root * (
        scaled
        - jnp.mean(scaled, axis=-1, keepdims=True)
        - normed * jnp.mean(scaled * normed, axis=-1, keepdims=True)
    )


B_QUERY, B_VALUE, B_OUT, GAIN1, SHIFT1, B_CONTRACT, GAIN2, SHIFT2 = range(8)
S_QUERY, S_VALUE, S_OUT, S_GAIN1, S_SHIFT1, S_EXPAND = range(6)
S_CONTRACT, S_GAIN2, S_SHIFT2, S_TABLE = 9, 10, 11, 12


def forward(x, w, vec, b_expand, masks, s, keep, ready):
    row = lambda k: vec[k : k + 1, :]
    ready("query")
    s.query[...] = (nn(x[...], w.query[...]) + row(B_QUERY)).astype(LOW)
    ready("key")
    s.key[...] = nn(x[:L], w.key[...]).astype(LOW)
    ready("value")
    s.value[...] = (nn(x[:L], w.value[...]) + row(B_VALUE)).astype(LOW)
    ready("masks")
    for pair in range(PAIRS):
        lanes = slice(pair * 128, (pair + 1) * 128)
        scores = nt(halves(s.query[:, lanes]), s.key[:, lanes]) * SCALE + masks[pair]
        shifted = jnp.exp(scores - jnp.max(scores, axis=-1, keepdims=True))
        probs = (shifted / jnp.sum(shifted, axis=-1, keepdims=True)).astype(LOW)
        if keep:
            s.probs[pair] = probs
        s.mixed[:, lanes] = nn(side(probs), halves(s.value[:, lanes])).astype(LOW)
    ready("out")
    total = x[...].astype(WIDE) + nn(s.mixed[...], w.out[...]) + row(B_OUT)
    normed, root = norm_rows(total)
    first = normed * row(GAIN1) + row(SHIFT1)
    s.first_low[...] = first.astype(LOW)
    s.total[...] = first + row(B_CONTRACT)
    if keep:
        s.normed1[...] = normed
        s.root1[...] = jnp.broadcast_to(root, (ROWS, 128))
    ready("expand")
    ready("contract")
    for tile in range(FF // TILE):
        tile = slice(tile * TILE, (tile + 1) * TILE)
        expanded = nn(s.first_low[...], w.expand[:, tile]) + b_expand[:, tile]
        cumulative = 0.5 * (1.0 + lax.erf(expanded * 0.7071067811865476))
        activated = (expanded * cumulative).astype(LOW)
        if keep:
            s.slope[:, tile] = (
                cumulative + expanded * jnp.exp(-0.5 * expanded * expanded) * 0.3989422804014327
            ).astype(LOW)
            s.activated[:, tile] = activated
        s.total[...] += nn(activated, w.contract[tile, :])
    normed, root = norm_rows(s.total[...])
    if keep:
        s.normed2[...] = normed
        s.root2[...] = jnp.broadcast_to(root, (ROWS, 128))
    s.out[...] = (normed * row(GAIN2) + row(SHIFT2)).astype(s.out.dtype)


def column_sum(value):
    return jnp.sum(value.astype(WIDE), axis=0, keepdims=True)


def back_second_norm(grad, vec, s, add=None):
    upper = grad.astype(WIDE)
    normed = s.normed2[...]
    lower = norm_rows_back(upper * vec[GAIN2 : GAIN2 + 1, :], normed, s.root2[:, :1])
    s.total[...] = lower
    s.branch[...] = lower.astype(LOW)
    if add is not None:
        add(S_GAIN2, column_sum(upper * normed))
        add(S_SHIFT2, column_sum(upper))
        add(S_CONTRACT, column_sum(lower.astype(LOW)))


def back_feed(w, vec, s, add=None):
    for tile in range(FF // TILE):
        tile = slice(tile * TILE, (tile + 1) * TILE)
        lower = (nt(s.branch[...], w.contract[tile, :]) * s.slope[:, tile].astype(WIDE)).astype(LOW)
        s.expanded[:, tile] = lower
        if add is not None:
            part = column_sum(lower)
            for column in range(TILE // D):
                add(
                    S_EXPAND + tile.start // D + column,
                    part[:, column * D : (column + 1) * D],
                )
        s.total[...] += nt(lower, w.expand[:, tile])
    upper = s.total[...]
    normed = s.normed1[...]
    lower = norm_rows_back(upper * vec[GAIN1 : GAIN1 + 1, :], normed, s.root1[:, :1])
    s.total[...] = lower
    s.attended[...] = lower.astype(LOW)
    if add is not None:
        add(S_GAIN1, column_sum(upper * normed))
        add(S_SHIFT1, column_sum(upper))
        add(S_OUT, column_sum(lower.astype(LOW)))


def back_attend(w, s, spread=None, table=None):
    for pair in range(PAIRS):
        lanes = slice(pair * 128, (pair + 1) * 128)
        probs = s.probs[pair]
        below = halves(s.dmixed[:, lanes])
        dprobs = nt(below, s.value[:, lanes])
        s.dvalue[:, lanes] = tn(probs, below).astype(LOW)
        weight = probs.astype(WIDE)
        dscores = (
            weight * (dprobs - jnp.sum(weight * dprobs, axis=-1, keepdims=True))
        ).astype(LOW)
        s.dquery[:, lanes] = (nn(side(dscores), halves(s.key[:, lanes])) * SCALE).astype(LOW)
        s.dkey[:, lanes] = (tn(dscores, halves(s.query[:, lanes])) * SCALE).astype(LOW)
        if table is not None:
            table(pair, dscores)


class Names:
    def __init__(self, **named):
        self.__dict__.update(named)


MATRICES = ("query", "key", "value", "out", "expand", "contract")
MATRIX_SHAPES = {
    "query": (D, D),
    "key": (D, D),
    "value": (D, D),
    "out": (D, D),
    "expand": (D, FF),
    "contract": (FF, D),
}
MASK_SHAPE = (PAIRS, 2 * ROWS, L)
KEPT = {
    "query": ((ROWS, D), LOW),
    "key": ((L, D), LOW),
    "value": ((L, D), LOW),
    "probs": (MASK_SHAPE, LOW),
    "mixed": ((ROWS, D), LOW),
    "normed1": ((ROWS, D), WIDE),
    "root1": ((ROWS, 128), WIDE),
    "first_low": ((ROWS, D), LOW),
    "slope": ((ROWS, FF), LOW),
    "activated": ((ROWS, FF), LOW),
    "normed2": ((ROWS, D), WIDE),
    "root2": ((ROWS, 128), WIDE),
}
SAVED = tuple(name for name in KEPT if name != "mixed")
ANY = pl.BlockSpec(memory_space=pl.ANY)
VMEM = pl.BlockSpec(memory_space=pltpu.VMEM)
SMEM = pl.BlockSpec(memory_space=pltpu.SMEM)
PARAMS = pltpu.CompilerParams(vmem_limit_bytes=60 * 1024 * 1024)
DMA = pltpu.SemaphoreType.DMA


def cost(microseconds):
    return pl.CostEstimate(flops=0, bytes_accessed=int(microseconds * 3.2e6), transcendentals=0)


def shaped(shape, kind):
    return jax.ShapeDtypeStruct(shape, kind)


def columns(ref, start, size):
    return ref.at[:, pl.ds(pl.multiple_of(start, 128), size)]


def rows_at(ref, start, size):
    return ref.at[pl.ds(pl.multiple_of(start, 64), size)]


def start_all(pairs, sems, base=0):
    copies = [
        pltpu.make_async_copy(source, target, sems.at[base + index])
        for index, (source, target) in enumerate(pairs)
    ]
    for copy in copies:
        copy.start()
    return copies


def wait_all(copies):
    for copy in copies:
        copy.wait()


def fetcher(names, sources, targets, sems, base=0):
    copies = dict(zip(names, start_all(list(zip(sources, targets)), sems, base)))
    return lambda name: copies[name].wait()


FORWARD_ORDER = ("query", "key", "value", "masks", "out", "expand", "contract")
FORWARD_SCRATCH = [
    pltpu.VMEM(MASK_SHAPE if n == "masks" else MATRIX_SHAPES[n], WIDE if n == "masks" else LOW)
    for n in FORWARD_ORDER
]


def fetch_rows(content, picks, seq, target, sems, base):
    return start_all(
        [
            (content.at[seq * L : (seq + 1) * L], target.at[:L]),
            (picks.at[seq * PICKS : (seq + 1) * PICKS], target.at[L:]),
        ],
        sems,
        base,
    )


def front(seq, content, picks, matrices, masks, vec, b_expand, after=()):
    def kernel(content, picks, masks, vec, b_expand, *refs):
        matrices, out, rest = refs[:6], refs[6 + len(after)], refs[7 + len(after) :]
        held, (x, query, key, value, mixed, first_low, total, sems) = rest[:7], rest[7:]
        rows = fetch_rows(content, picks, seq, x, sems, 7)
        sources = matrices[:3] + (masks.at[seq],) + matrices[3:]
        ready = fetcher(FORWARD_ORDER, sources, held, sems)
        s = Names(
            query=query,
            key=key,
            value=value,
            mixed=mixed,
            first_low=first_low,
            total=total,
            out=out,
        )
        w = Names(**dict(zip(FORWARD_ORDER, held)))
        wait_all(rows)
        forward(x, w, vec, b_expand, w.masks, s, False, ready)

    return pl.pallas_call(
        kernel,
        out_shape=shaped((ROWS, D), LOW),
        in_specs=[ANY] * 3 + [VMEM] * 2 + [ANY] * (6 + len(after)),
        out_specs=VMEM,
        scratch_shapes=FORWARD_SCRATCH
        + [pltpu.VMEM((ROWS, D), LOW)]
        + [pltpu.VMEM(*KEPT[n]) for n in ("query", "key", "value", "mixed", "first_low")]
        + [pltpu.VMEM((ROWS, D), WIDE), DMA((9,))],
        compiler_params=PARAMS,
        cost_estimate=cost(6),
        name="front",
    )(content, picks, masks, vec, b_expand, *matrices, *after)


def middle_forward(seq, info, content, picks, arrived, matrices, masks, vec, b_expand, after=()):
    def kernel(info, arrived, content, picks, masks, vec, b_expand, *refs):
        matrices, rest = refs[:6], refs[6 + len(after) :]
        (out, early, pair), saved_out = rest[:3], rest[3 : 3 + len(SAVED)]
        rest = rest[3 + len(SAVED) :]
        held, kept, (x, total, sems, out_sems) = rest[:7], rest[7 : 7 + len(KEPT)], rest[-4:]
        rows = fetch_rows(content, picks, seq, x, sems, 7)
        sources = matrices[:3] + (masks.at[seq],) + matrices[3:]
        ready = fetcher(FORWARD_ORDER, sources, held, sems)
        s = Names(total=total, out=out, **dict(zip(KEPT, kept)))
        w = Names(**dict(zip(FORWARD_ORDER, held)))
        wait_all(rows)
        x[...] = jnp.where(info[2] == 1, x[...], arrived[...])
        forward(x, w, vec, b_expand, w.masks, s, True, ready)
        wait_all(
            start_all(
                [
                    (x, early.at[:, :D]),
                    (s.mixed, early.at[:, D : 2 * D]),
                    (s.first_low, early.at[:, 2 * D : 3 * D]),
                    (columns(s.activated, (1 - info[0]) * HALF, HALF), early.at[:, 3 * D :]),
                    (x, pair.at[0]),
                    (s.mixed, pair.at[1]),
                ]
                + [(s.__dict__[n], ref) for n, ref in zip(SAVED, saved_out)],
                out_sems,
            )
        )

    out, early, pair, *saved = pl.pallas_call(
        kernel,
        out_shape=[
            shaped((ROWS, D), WIDE),
            shaped((ROWS, EARLY), LOW),
            shaped((2, ROWS, D), LOW),
        ]
        + [shaped(*KEPT[n]) for n in SAVED],
        in_specs=[SMEM, VMEM] + [ANY] * 3 + [VMEM] * 2 + [ANY] * (6 + len(after)),
        out_specs=[VMEM] + [ANY] * (2 + len(SAVED)),
        scratch_shapes=FORWARD_SCRATCH
        + [pltpu.VMEM(*KEPT[n]) for n in KEPT]
        + [
            pltpu.VMEM((ROWS, D), LOW),
            pltpu.VMEM((ROWS, D), WIDE),
            DMA((9,)),
            DMA((6 + len(SAVED),)),
        ],
        compiler_params=PARAMS,
        cost_estimate=cost(8),
        name="middle_forward",
    )(info, arrived, content, picks, masks, vec, b_expand, *matrices, *after)
    return (out, early, pair, dict(zip(SAVED, saved)))


FEED_SAVED = ("normed2", "root2", "slope", "normed1", "root1")
ATTEND_SAVED = ("value", "probs", "key", "query")


def middle_back(seq, content, picks, matrices, vec, saved):
    names = ("normed2", "root2", "contract", "slope", "expand", "normed1", "root1", "w_out")
    names += ATTEND_SAVED + ("w_query", "w_key", "w_value")
    weights = dict(zip(("w_query", "w_key", "w_value", "w_out", "expand", "contract"), matrices))
    sources = [weights[n] if n in weights else saved[n] for n in names]

    def kernel(content, picks, vec, *refs):
        sources, grad, rest = refs[: len(names)], refs[len(names)], refs[len(names) + 1 :]
        held, rest = rest[: len(names)], rest[len(names) :]
        cot, total, branch, expanded, attended, dmixed, dvalue, dquery, dkey, sems = rest
        rows = fetch_rows(content, picks, seq, cot, sems, len(names))
        ready = fetcher(names, sources, held, sems)
        w = Names(**dict(zip(names, held)))
        s = Names(
            total=total,
            branch=branch,
            expanded=expanded,
            attended=attended,
            dmixed=dmixed,
            dvalue=dvalue,
            dquery=dquery,
            dkey=dkey,
            **{n: w.__dict__[n] for n in FEED_SAVED + ATTEND_SAVED},
        )
        wait_all(rows)
        ready("normed2")
        ready("root2")
        back_second_norm(cot[...], vec, s)
        for name in names[2:7]:
            ready(name)
        back_feed(w, vec, s)
        for name in names[7:12]:
            ready(name)
        dmixed[...] = nt(attended[...], w.w_out[...]).astype(LOW)
        back_attend(w, s)
        for name in names[12:]:
            ready(name)
        lower = total[...] + nt(dquery[...], w.w_query[...])
        upper = nt(dkey[...], w.w_key[...]) + nt(dvalue[...], w.w_value[...])
        grad[:L] = (lower[:L] + upper).astype(LOW)
        grad[L:] = lower[L:].astype(LOW)

    return pl.pallas_call(
        kernel,
        out_shape=shaped((ROWS, D), LOW),
        in_specs=[ANY] * 2 + [VMEM] + [ANY] * len(names),
        out_specs=VMEM,
        scratch_shapes=[pltpu.VMEM(source.shape, source.dtype) for source in sources]
        + [
            pltpu.VMEM((ROWS, D), LOW),
            pltpu.VMEM((ROWS, D), WIDE),
            pltpu.VMEM((ROWS, D), LOW),
            pltpu.VMEM((ROWS, FF), LOW),
            pltpu.VMEM((ROWS, D), LOW),
            pltpu.VMEM((ROWS, D), LOW),
            pltpu.VMEM((L, D), LOW),
            pltpu.VMEM((ROWS, D), LOW),
            pltpu.VMEM((L, D), LOW),
            DMA((len(names) + 2,)),
        ],
        compiler_params=PARAMS,
        cost_estimate=cost(7),
        name="middle_back",
    )(content, picks, vec, *sources)


def feed_back(seq, info, arrived, content, picks, small_in, vec, matrices, saved):
    names = ("normed2", "root2", "contract", "slope", "expand", "normed1", "root1")
    weights = {"expand": matrices[4], "contract": matrices[5]}
    sources = [weights[n] if n in weights else saved[n] for n in names]

    def kernel(info, arrived, content, picks, small_in, vec, *refs):
        sources, rest = refs[:7], refs[7:]
        (total, branch, attended, small, own, late), rest = rest[:6], rest[6:]
        held, (upper, expanded, sems, out_sems) = rest[:7], rest[7:]
        rows = fetch_rows(content, picks, seq, upper, sems, 7)
        ready = fetcher(names, sources, held, sems)
        w = Names(**dict(zip(names, held)))
        s = Names(
            total=total,
            branch=branch,
            attended=attended,
            expanded=expanded,
            **{n: w.__dict__[n] for n in FEED_SAVED},
        )
        small[...] = small_in[...]

        def add(place, value):
            small[place : place + 1, :] += value

        wait_all(rows)
        ready("normed2")
        ready("root2")
        back_second_norm(jnp.where(info[2] == 1, arrived[...], upper[...]), vec, s, add)
        copies = start_all([(branch, late.at[:, :D])], out_sems)
        for name in names[2:]:
            ready(name)
        back_feed(w, vec, s, add)
        copies += start_all(
            [
                (columns(expanded, info[0] * HALF, HALF), own),
                (columns(expanded, (1 - info[0]) * HALF, HALF), late.at[:, D:]),
            ],
            out_sems,
            1,
        )
        wait_all(copies)

    return pl.pallas_call(
        kernel,
        out_shape=[
            shaped((ROWS, D), WIDE),
            shaped((ROWS, D), LOW),
            shaped((ROWS, D), LOW),
            shaped((16, D), WIDE),
            shaped((ROWS, HALF), LOW),
            shaped((ROWS, LATE), LOW),
        ],
        in_specs=[SMEM, VMEM] + [ANY] * 2 + [VMEM] * 2 + [ANY] * 7,
        out_specs=[VMEM] * 4 + [ANY] * 2,
        scratch_shapes=[pltpu.VMEM(source.shape, source.dtype) for source in sources]
        + [pltpu.VMEM((ROWS, D), LOW), pltpu.VMEM((ROWS, FF), LOW), DMA((9,)), DMA((3,))],
        compiler_params=PARAMS,
        cost_estimate=cost(6),
        name="feed_back",
    )(info, arrived, content, picks, small_in, vec, *sources)


PLACES = {
    (2, 0): (0, 0),
    (1, 1): (0, 1),
    (2, 1): (1, 0),
    (3, 0): (1, 1),
    (1, 0): (2, 0),
    (3, 1): (3, 0),
    (0, 0): (4, 0),
    (0, 1): (4, 1),
}


def term_shapes(count):
    return [shaped((n * count, D), LOW) for n in (2, 2, 1, 1, 2)]


def feed_grads(info, mine, branch, own, early, late):
    def kernel(info, *refs):
        acts, lows, branches, owns, earlies, lates = (refs[2 * i : 2 * i + 2] for i in range(6))
        outs, (a_act, a_first, b_branch, b_own, stage, sems, out_sems) = refs[12:17], refs[17:]
        core, place = info[0], info[1]
        own_at = [slice(seq * ROWS, (seq + 1) * ROWS) for seq in range(SEQS)]
        far_at = [slice((2 + seq) * ROWS, (3 + seq) * ROWS) for seq in range(SEQS)]
        pairs, later = [], []
        for seq in range(SEQS):
            pairs += [
                (columns(acts[seq], core * HALF, HALF), a_act.at[own_at[seq]]),
                (earlies[seq].at[:, 3 * D :], a_act.at[far_at[seq]]),
                (branches[seq], b_branch.at[own_at[seq]]),
                (lates[seq].at[:, :D], b_branch.at[far_at[seq]]),
            ]
            later += [
                (lows[seq], a_first.at[own_at[seq]]),
                (earlies[seq].at[:, 2 * D : 3 * D], a_first.at[far_at[seq]]),
                (owns[seq], b_own.at[own_at[seq]]),
                (lates[seq].at[:, D:], b_own.at[far_at[seq]]),
            ]
        copies = start_all(pairs + later, sems)
        sent = []

        def send(block):
            for k in range(4):
                quarter = lax.rem(place + k, 4)
                index, part = PLACES[k, block // 2]
                start = (2 * part + block % 2) * QUARTER
                sent.extend(
                    start_all(
                        [
                            (
                                rows_at(stage.at[block], quarter * QUARTER, QUARTER),
                                outs[index].at[start : start + QUARTER],
                            )
                        ],
                        out_sems,
                        block * 4 + k,
                    )
                )

        wait_all(copies[:8])
        for block in range(2):
            for part in range(3):
                start = block * D + part * 256
                stage[block, part * 256 : (part + 1) * 256] = tn(
                    a_act[:, start : start + 256], b_branch[...]
                ).astype(LOW)
            send(block)
        wait_all(copies[8:])
        for block in range(2):
            for part in range(3):
                stage[2 + block, part * 256 : (part + 1) * 256] = tn(
                    a_first[:, part * 256 : (part + 1) * 256], b_own[:, block * D : (block + 1) * D]
                ).astype(LOW)
            send(2 + block)
        wait_all(sent)

    acts = [saved["activated"] for saved in mine]
    lows = [saved["first_low"] for saved in mine]
    return pl.pallas_call(
        kernel,
        out_shape=term_shapes(2 * QUARTER),
        in_specs=[SMEM] + [ANY] * 12,
        out_specs=[ANY] * 5,
        scratch_shapes=[
            pltpu.VMEM((2 * ALL_ROWS, HALF), LOW),
            pltpu.VMEM((2 * ALL_ROWS, D), LOW),
            pltpu.VMEM((2 * ALL_ROWS, D), LOW),
            pltpu.VMEM((2 * ALL_ROWS, HALF), LOW),
            pltpu.VMEM((4, D, D), LOW),
            DMA((16,)),
            DMA((16,)),
        ],
        compiler_params=PARAMS,
        cost_estimate=cost(8),
        name="feed_grads",
    )(info, *acts, *lows, *branch, *own, *early, *late)


def attend_back(info, total, attended, small_in, spread, output, after, matrices, saved, picks):
    names = [n + str(seq) for n in ATTEND_SAVED for seq in range(SEQS)]
    names = ["w_out"] + names + ["w_query", "w_key", "w_value"]
    sources = [matrices[3]] + [saved[seq][n] for n in ATTEND_SAVED for seq in range(SEQS)]
    sources += list(matrices[:3])

    def kernel(info, small_in, spread, *refs):
        totals, attendeds, outputs = refs[0:2], refs[2:4], refs[4:6]
        sources, rest = refs[6 : 6 + len(names)], refs[6 + len(names) + len(after) :]
        (content_ends, query_ends, small, table, own, send), rest = rest[:6], rest[6:]
        held, (total, dmixed, pieces, sems, out_sems) = rest[: len(names)], rest[len(names) :]
        ready = fetcher(names, sources, held, sems)
        w = Names(**dict(zip(names, held)))
        at = [slice(seq * ROWS, (seq + 1) * ROWS) for seq in range(SEQS)]
        lower_at = [
            slice(ALL_ROWS + seq * L, ALL_ROWS + (seq + 1) * L) for seq in range(SEQS)
        ]
        for seq in range(SEQS):
            pieces[1, at[seq]] = attendeds[seq][...]
        ready("w_out")
        dmixed[...] = nt(pieces[1, :ALL_ROWS], w.w_out[...]).astype(LOW)
        for seq in range(SEQS):
            for name in ATTEND_SAVED:
                ready(name + str(seq))
            s = Names(
                dmixed=dmixed.at[at[seq]],
                dquery=pieces.at[0, at[seq]],
                dkey=pieces.at[0, lower_at[seq]],
                dvalue=pieces.at[1, lower_at[seq]],
                **{n: w.__dict__[n + str(seq)] for n in ATTEND_SAVED},
            )

            def table_sum(pair, dscores, seq=seq):
                for odd in range(2):
                    part = nn(
                        spread[:, seq * ROWS : (seq + 1) * ROWS],
                        dscores[odd * ROWS : (odd + 1) * ROWS],
                    )
                    if seq == 0:
                        table[2 * pair + odd] = part
                    else:
                        table[2 * pair + odd] += part

            back_attend(w, s, spread, table_sum)
        copies = start_all([(pieces.at[info[0]], own), (pieces.at[1 - info[0]], send)], out_sems)
        small[...] = small_in[...]
        small[S_QUERY : S_QUERY + 1, :] = column_sum(pieces[0, :ALL_ROWS])
        small[S_VALUE : S_VALUE + 1, :] = column_sum(pieces[1, ALL_ROWS:])
        for name in ("w_query", "w_key", "w_value"):
            ready(name)
        lower = nt(pieces[0, :ALL_ROWS], w.w_query[...])
        upper = nt(pieces[0, ALL_ROWS:], w.w_key[...]) + nt(pieces[1, ALL_ROWS:], w.w_value[...])
        first = info[2] == 1
        for seq in range(SEQS):
            base = seq * ROWS
            content_ends[seq * L : (seq + 1) * L] = jnp.where(
                first,
                totals[seq][:L] + lower[base : base + L] + upper[seq * L : (seq + 1) * L],
                outputs[seq][:L],
            )
            query_ends[seq * picks : (seq + 1) * picks] = jnp.where(
                first,
                totals[seq][L : L + picks] + lower[base + L : base + L + picks],
                outputs[seq][L : L + picks],
            )
        wait_all(copies)

    return pl.pallas_call(
        kernel,
        out_shape=[
            shaped((ALL_CONTENT, D), WIDE),
            shaped((SEQS * picks, D), WIDE),
            shaped((16, D), WIDE),
            shaped((H, L, L), WIDE),
            shaped((PIECE, D), LOW),
            shaped((PIECE, D), LOW),
        ],
        in_specs=[SMEM] + [VMEM] * 8 + [ANY] * (len(names) + len(after)),
        out_specs=[VMEM] * 4 + [ANY] * 2,
        scratch_shapes=[pltpu.VMEM(source.shape, LOW) for source in sources]
        + [
            pltpu.VMEM((ALL_ROWS, D), WIDE),
            pltpu.VMEM((ALL_ROWS, D), LOW),
            pltpu.VMEM((2, PIECE, D), LOW),
            DMA((len(names),)),
            DMA((2,)),
        ],
        compiler_params=PARAMS,
        cost_estimate=cost(12),
        name="attend_back",
    )(info, small_in, spread, *total, *attended, *output, *sources, *after)


def attend_grads(info, pair, early, own, arrived, small):
    def kernel(info, small, own, arrived, *refs):
        pairs_in, earlies, outs, rest = refs[0:2], refs[2:4], refs[4:9], refs[9:]
        a_rows, a_content, b_rows, b_content, stage, extra, sems, out_sems = rest
        core, place = info[0], info[1]
        pairs = [
            (own.at[:ALL_ROWS], b_rows.at[:ALL_ROWS]),
            (arrived.at[:ALL_ROWS], b_rows.at[ALL_ROWS:]),
        ]
        later = [
            (own.at[ALL_ROWS:], b_content.at[:ALL_CONTENT]),
            (arrived.at[ALL_ROWS:], b_content.at[ALL_CONTENT:]),
        ]
        for seq in range(SEQS):
            at, far = seq * ROWS, (2 + seq) * ROWS
            pairs += [
                (pairs_in[seq].at[core], a_rows.at[at : at + ROWS]),
                (columns(earlies[seq], core * D, D), a_rows.at[far : far + ROWS]),
            ]
            at, far = seq * L, (2 + seq) * L
            later += [
                (pairs_in[seq].at[0, :L], a_content.at[at : at + L]),
                (earlies[seq].at[:L, :D], a_content.at[far : far + L]),
            ]
        copies = start_all(pairs + later, sems)
        extra[...] = jnp.zeros_like(extra)
        part = small[pl.ds(pl.multiple_of(core * 8, 8), 8), :]
        extra[0] = jnp.concatenate([part, jnp.zeros((EXTRA - 8, D), WIDE)]).astype(LOW)
        sent = []
        for block, (former, latter) in enumerate(((a_rows, b_rows), (a_content, b_content))):
            wait_all(copies[6 * block : 6 * block + 6])
            for part in range(3):
                stage[block, part * 256 : (part + 1) * 256] = tn(
                    former[:, part * 256 : (part + 1) * 256], latter[...]
                ).astype(LOW)
            for k in range(4):
                quarter = lax.rem(place + k, 4)
                index, part = PLACES[k, block]
                start = part * (QUARTER + EXTRA)
                middle, stop = start + QUARTER, start + QUARTER + EXTRA
                sent += start_all(
                    [
                        (
                            rows_at(stage.at[block], quarter * QUARTER, QUARTER),
                            outs[index].at[start:middle],
                        ),
                        (extra.at[block], outs[index].at[middle:stop]),
                    ],
                    out_sems,
                    block * 8 + 2 * k,
                )
        wait_all(sent)

    return pl.pallas_call(
        kernel,
        out_shape=term_shapes(QUARTER + EXTRA),
        in_specs=[SMEM, VMEM] + [ANY] * 6,
        out_specs=[ANY] * 5,
        scratch_shapes=[
            pltpu.VMEM((2 * ALL_ROWS, D), LOW),
            pltpu.VMEM((2 * ALL_CONTENT, D), LOW),
            pltpu.VMEM((2 * ALL_ROWS, D), LOW),
            pltpu.VMEM((2 * ALL_CONTENT, D), LOW),
            pltpu.VMEM((2, D, D), LOW),
            pltpu.VMEM((2, EXTRA, D), LOW),
            DMA((12,)),
            DMA((16,)),
        ],
        compiler_params=PARAMS,
        cost_estimate=cost(5),
        name="attend_grads",
    )(info, small, own, arrived, *pair, *early)


def feed_targets(outs, source, half, core, quarter):
    pairs = []
    for block in range(2):
        part = source.at[block * QUARTER : (block + 1) * QUARTER]
        if half == 0:
            target = rows_at(outs[0], core * HALF + block * D + quarter * QUARTER, QUARTER)
        else:
            target = columns(
                rows_at(outs[1], quarter * QUARTER, QUARTER), (core * 2 + block) * D, D
            )
        pairs.append((None, part, target))
    return pairs


def attend_targets(outs, source, half, core, quarter):
    return [
        (
            core == number,
            source.at[:QUARTER],
            rows_at(outs[2 * number + half], quarter * QUARTER, QUARTER),
        )
        for number in range(2)
    ]


def settle(targets, shapes, count, info, pieces, outs, through, name):
    keys = tuple(pieces)
    arrays = [pieces[key] for key in keys]
    given = list(outs or ()) + list(through)
    first_alias = len(shapes) - len(outs or ())

    def kernel(info, *refs):
        parts, rest = refs[: len(keys)], refs[len(keys) + len(given) :]
        outs, rest = rest[: len(shapes)], rest[len(shapes) + len(through) :]
        held, wide_held, (sems, out_sems) = rest[: len(keys)], rest[len(keys) : -2], rest[-2:]
        copies = start_all(list(zip(parts, held)), sems)
        finish = []
        for index, (sibling, k, which) in enumerate(keys):
            core = 1 - info[0] if sibling else info[0]
            quarter = lax.rem((info[3] if sibling else info[1]) + k, 4)
            copies[index].wait()
            wide_held[index][...] = held[index][...].astype(WIDE)
            for number, half in enumerate(which):
                source = wide_held[index].at[number * count : (number + 1) * count]
                for place, (condition, part, target) in enumerate(
                    targets(outs, source, half, core, quarter)
                ):
                    copy = pltpu.make_async_copy(
                        part, target, out_sems.at[4 * index + 2 * number + place]
                    )
                    if condition is None:
                        copy.start()
                        finish.append(copy.wait)
                    else:
                        pl.when(condition)(copy.start)
                        finish.append(lambda copy=copy, condition=condition: pl.when(condition)(copy.wait))
        for action in finish:
            action()

    result = pl.pallas_call(
        kernel,
        out_shape=[shaped(shape, WIDE) for shape in shapes]
        + [shaped(array.shape, array.dtype) for array in through],
        in_specs=[SMEM] + [ANY] * (len(keys) + len(given)),
        out_specs=[ANY] * (len(shapes) + len(through)),
        scratch_shapes=[pltpu.VMEM(array.shape, LOW) for array in arrays]
        + [pltpu.VMEM(array.shape, WIDE) for array in arrays]
        + [DMA((len(keys),)), DMA((4 * len(keys),))],
        input_output_aliases={1 + len(keys) + i: first_alias + i for i in range(len(given))},
        compiler_params=PARAMS,
        cost_estimate=cost(sum(array.size for array in arrays) * 2e-6 + 1),
        name=name,
    )(info, *arrays, *given)
    return result[: len(shapes)], result[len(shapes) :]


LIMITS = (12, 16, 23, 32, 46, 64, 91)
TOP_PRECISION = lax.Precision.HIGHEST


def bucket_of(relative):
    distance = jnp.abs(relative)
    beyond = 8 + sum(((distance >= limit).astype(jnp.int32) for limit in LIMITS))
    within = jnp.where(distance < 8, distance, beyond)
    return within + 16 * (relative > 0).astype(jnp.int32)


def geometry(order_row, pos_row, tag_row, table):
    positions = lax.iota(jnp.int32, L)
    matches = pos_row[:, None] == positions[None, :]
    predicted = jnp.any(matches, axis=0)
    query_rank = jnp.sum(jnp.where(matches, order_row[None, :], 0), axis=1)
    query_tag = jnp.sum(jnp.where(matches, tag_row[None, :], 0), axis=1)
    row_rank = jnp.concatenate([order_row, query_rank])
    row_tag = jnp.concatenate([tag_row, query_tag])
    row_place = jnp.concatenate([positions, pos_row])
    row_flag = jnp.concatenate([predicted, jnp.ones(pos_row.shape, jnp.bool_)])
    strict = jnp.concatenate([jnp.zeros((L,), jnp.int32), jnp.ones(pos_row.shape, jnp.int32)])
    same_group = row_tag[:, None] == tag_row[None, :]
    earlier = order_row[None, :] + strict[:, None] <= row_rank[:, None]
    allowed = same_group & (~predicted[None, :] | row_flag[:, None] & earlier)
    buckets = bucket_of(positions[None, :] - row_place[:, None])
    one_hot = (buckets[None] == lax.iota(jnp.int32, NB)[:, None, None]).astype(WIDE)
    score_bias = jnp.einsum("krl,kh->hrl", one_hot, table, precision=TOP_PRECISION)
    masked = jnp.where(allowed[None], score_bias, -1e30)
    masked = jnp.pad(masked, ((0, 0), (0, ROWS - masked.shape[1]), (0, 0)))
    padded = jnp.pad(matches.astype(LOW), ((0, PICKS - matches.shape[0]), (0, 0)))
    spread = jnp.concatenate([jnp.eye(L, dtype=LOW), padded.T], axis=1)
    return (masked, spread)


def diagonals():
    positions = lax.iota(jnp.int32, L)
    buckets = bucket_of(positions[None, :] - positions[:, None])
    return (buckets[None] == lax.iota(jnp.int32, NB)[:, None, None]).astype(WIDE)


PLANE = ("x", "y", "c")


def shift(value, axis, by):
    size = lax.axis_size(axis)
    return lax.ppermute(value, axis, [(i, (i + by) % size) for i in range(size)])


def send(value, by):
    return lax.ppermute(value, "s", [(0, 1)] if by > 0 else [(1, 0)])


def turn(value, outer, by):
    pairs = []
    for i in range(4):
        for j in range(4):
            for c in range(2):
                if (c == 0) == outer:
                    target = ((i + by) % 4, j)
                else:
                    target = (i, (j + by) % 4)
                pairs.append(((i * 4 + j) * 2 + c, (target[0] * 4 + target[1]) * 2 + c))
    return lax.ppermute(value, PLANE, pairs)


def place(outer):
    return jnp.where(
        (lax.axis_index("c") == 0) == outer, lax.axis_index("x"), lax.axis_index("y")
    )


def wide(value):
    return value.astype(WIDE)


def pick(parts, index):
    return lax.dynamic_index_in_dim(parts, index, 0, keepdims=False)


def total_of(*terms):
    return sum(wide(term) for term in terms).astype(LOW)


def chain_reduce(terms):
    plus, minus, after0, before1, own = terms
    count = after0.shape[0]
    from_left = turn(plus, True, 1)
    from_right = turn(minus, True, -1)
    left = turn(total_of(after0, from_left[:count]), True, 1)
    right = turn(total_of(before1, from_right[:count]), True, -1)
    sums = [
        total_of(own[:count], left, from_right[count:]),
        total_of(own[count:], from_left[count:], right),
    ]
    parts = jnp.concatenate([part.reshape(4, count // 4, D) for part in sums], axis=1)
    me = place(False)
    arrived = [turn(pick(parts, (me + by) % 4), False, by) for by in (1, 2, -1)]
    part = total_of(pick(parts, me), *arrived)
    return total_of(part, shift(part, "z", 1))


def gather_inner(part):
    count = part.shape[0] // 2
    me = place(False)
    whole = jnp.zeros((2, 4, count, D), LOW)
    for k, piece in enumerate([part] + [turn(part, False, -by) for by in (1, 2, -1)]):
        whole = lax.dynamic_update_slice(
            whole, piece.reshape(2, 1, count, D), (0, (me + k) % 4, 0, 0)
        )
    return whole.reshape(8 * count, D)


def gather_outer(own):
    before = turn(own, True, 1)
    after = turn(own, True, -1)
    near = {(0, (0, 1)): own, (3, (0, 1)): before, (1, (0, 1)): after}
    both = {(0,) + key: piece for key, piece in near.items()}
    return both | {(1,) + key: shift(piece, "c", 1) for key, piece in near.items()}


def gather_across(pieces):
    before, after = pieces[0, 3, (0, 1)], pieces[0, 1, (0, 1)]
    count = before.shape[0] // 2
    far = {(2, (0,)): turn(before[:count], True, 1), (2, (1,)): turn(after[count:], True, -1)}
    both = {(0,) + key: piece for key, piece in far.items()}
    return both | {(1,) + key: shift(piece, "c", 1) for key, piece in far.items()}


def on_device(
    content_in,
    query_in,
    content_cot,
    query_cot,
    order_rank,
    query_pos,
    group_tag,
    *rest,
):
    (
        w_query,
        b_query,
        w_key,
        w_value,
        b_value,
        w_out,
        b_out,
        norm1_gain,
        norm1_bias,
        w_expand,
        b_expand,
        w_contract,
        b_contract,
        norm2_gain,
        norm2_bias,
    ) = (argument[0] for argument in rest[:-1])
    rel_table = rest[-1]
    core = lax.axis_index("c")
    first_section = (lax.axis_index("s") == 0).astype(jnp.int32)
    info = jnp.stack([core, place(True), first_section, place(False)])
    picks = query_pos.shape[1]

    def padded(query):
        query = jnp.pad(query.reshape(SEQS, picks, D), ((0, 0), (0, PICKS - picks), (0, 0)))
        return query.reshape(SEQS * PICKS, D)

    masks, spread = jax.vmap(geometry, in_axes=(0, 0, 0, None))(
        order_rank, query_pos, group_tag, rel_table
    )
    masks = masks.reshape((SEQS,) + MASK_SHAPE)
    spread = jnp.concatenate([spread[0], spread[1]], axis=1)
    query_in, query_cot = padded(query_in), padded(query_cot)
    matrices = (w_query, w_key, w_value, w_out, w_expand, w_contract)
    vec = jnp.stack(
        [b_query, b_value, b_out, norm1_gain, norm1_bias, b_contract, norm2_gain, norm2_bias]
    )
    b_expand = b_expand[None]

    fronts, arrived = [], []
    for seq in range(SEQS):
        fronts.append(
            front(seq, content_in, query_in, matrices, masks, vec, b_expand, tuple(fronts))
        )
        arrived.append(send(fronts[seq], 1))
    output, early, pair, saved, grads = [], [], [], [], []
    for seq in range(SEQS):
        results = middle_forward(
            seq, info, content_in, query_in, arrived[seq], matrices, masks, vec, b_expand, tuple(grads)
        )
        for collected, result in zip((output, early, pair, saved), results):
            collected.append(result)
        grads.append(middle_back(seq, content_cot, query_cot, matrices, vec, saved[seq]))
    early = [shift(value, "c", 1) for value in early]
    grads = [send(value, -1) for value in grads]
    small = jnp.zeros((16, D), WIDE)
    total, branch, attended, own, late = [], [], [], [], []
    for seq in range(SEQS):
        results = feed_back(
            seq, info, grads[seq], content_cot, query_cot, small, vec, matrices, saved[seq]
        )
        small = results[3]
        for collected, result in zip(
            (total, branch, attended, own, late), results[:3] + results[4:]
        ):
            collected.append(result)
    late = [shift(value, "c", 1) for value in late]
    terms = feed_grads(info, saved, branch, own, early, late)
    feed_part = chain_reduce(terms)
    content_ends, query_ends, small, slopes, own, pass_on = attend_back(
        info, total, attended, small, spread, output, (terms[4],), matrices, saved, picks
    )
    passed = shift(pass_on, "c", 1)
    table = jnp.einsum("krl,hrl->kh", diagonals(), slopes, precision=TOP_PRECISION)
    table = jnp.pad(table.reshape(1, NB * H), ((0, 0), (0, D - NB * H)))
    small = jnp.concatenate([small[:S_TABLE], table, small[S_TABLE + 1 :]])
    small = small + shift(small, "c", 1)
    small = jnp.concatenate([small[:8], small[8:] + shift_table(small[8:])])
    terms = attend_grads(info, pair, early, own, passed, small)
    attend_part = chain_reduce(terms)
    feed_own = gather_inner(feed_part)
    feed_near = gather_outer(feed_own)
    attend_own = gather_inner(attend_part)
    feed_shapes, attend_shapes = ((FF, D), (D, FF)), ((D, D),) * 4
    feed_outs, (attend_own,) = settle(
        feed_targets,
        feed_shapes,
        2 * QUARTER,
        info,
        feed_near,
        None,
        (attend_own,),
        "feed_out",
    )
    attend_near = gather_outer(attend_own)
    feed_outs, _ = settle(
        feed_targets,
        feed_shapes,
        2 * QUARTER,
        info,
        gather_across(feed_near),
        feed_outs,
        (),
        "feed_out_last",
    )
    attend_outs, _ = settle(
        attend_targets,
        attend_shapes,
        QUARTER + EXTRA,
        info,
        attend_near,
        None,
        (),
        "attend_out",
    )
    attend_outs, _ = settle(
        attend_targets,
        attend_shapes,
        QUARTER + EXTRA,
        info,
        gather_across(attend_near),
        attend_outs,
        (),
        "attend_out_last",
    )
    contract, expand = feed_outs
    g_query, g_key, g_out, g_value = attend_outs
    mine, other = (attend_near[far, 0, (0, 1)][QUARTER : QUARTER + 8] for far in (0, 1))
    small_sum = wide(
        jnp.concatenate([jnp.where(core == 0, mine, other), jnp.where(core == 0, other, mine)])
    )
    table_total = small_sum[S_TABLE, : NB * H].reshape(NB, H)
    row = lambda k: small_sum[k][None]
    return (
        content_ends[None],
        query_ends[None],
        g_query[None],
        row(S_QUERY),
        g_key[None],
        g_value[None],
        row(S_VALUE),
        g_out[None],
        row(S_OUT),
        row(S_GAIN1),
        row(S_SHIFT1),
        expand[None],
        small_sum[S_EXPAND : S_EXPAND + 4].reshape(1, FF),
        contract[None],
        row(S_CONTRACT),
        row(S_GAIN2),
        row(S_SHIFT2),
        table_total,
    )


def shift_table(rows):
    table = S_TABLE - 8
    arrived = shift(rows, "s", 1)
    return jnp.where(lax.iota(jnp.int32, 8)[:, None] == table, arrived, 0.0)


DP = ("z", "x", "y", "c")


def solution(mesh):
    mesh = jax.sharding.Mesh(mesh.devices.reshape(2, 2, 4, 4, 2), ("s",) + DP)
    layer_specs = tuple(
        P("s", *([None] * (rank - 1))) for rank in (3, 2, 3, 3, 2, 3, 2, 2, 2, 3, 2, 3, 2, 2, 2)
    )
    in_specs = (P(DP, None),) * 7 + layer_specs + (P(),)
    out_specs = (P("s", DP, None),) * 2 + layer_specs + (P(),)
    return jax.shard_map(
        on_device, mesh=mesh, in_specs=in_specs, out_specs=out_specs, check_vma=False
    )
```

```python
import jax
import jax.numpy as jnp
from jax import lax
from jax.experimental import pallas as pl
from jax.experimental.pallas import tpu as pltpu
from jax.sharding import PartitionSpec as P

D = 768
H = 12
HD = 64
FF = 3072
NB = 32
L = 128
PAIRS = H // 2
SEQS = 2
PICKS = 32
ROWS = L + PICKS
EPSILON = 1e-05
SCALE = HD ** (-0.5)
TILE = 1536
LOW = jnp.bfloat16
WIDE = jnp.float32
HALF = FF // 2
QUARTER = D // 4
EARLY = 3 * D + HALF
LATE = D + HALF
EXTRA = 32
SMALL = 32
ALL_ROWS = SEQS * ROWS
ALL_CONTENT = SEQS * L
PIECE = ALL_ROWS + ALL_CONTENT


def nn(former, latter):
    return lax.dot_general(
        former, latter, (((1,), (0,)), ((), ())), preferred_element_type=WIDE
    )


def nt(former, latter):
    return lax.dot_general(
        former, latter, (((1,), (1,)), ((), ())), preferred_element_type=WIDE
    )


def tn(former, latter):
    return lax.dot_general(
        former, latter, (((0,), (0,)), ((), ())), preferred_element_type=WIDE
    )


def halves(value):
    even = lax.broadcasted_iota(jnp.int32, value.shape, 1) < HD
    zero = jnp.zeros_like(value)
    return jnp.concatenate([jnp.where(even, value, zero), jnp.where(even, zero, value)])


def side(value):
    count = value.shape[0] // 2
    return jnp.concatenate([value[:count], value[count:]], axis=1)


def norm_rows(values):
    centered = values - jnp.mean(values, axis=-1, keepdims=True)
    variance = jnp.mean(centered * centered, axis=-1, keepdims=True)
    root = lax.rsqrt(variance + EPSILON)
    return (centered * root, root)


def norm_rows_back(scaled, normed, root):
    return root * (
        scaled
        - jnp.mean(scaled, axis=-1, keepdims=True)
        - normed * jnp.mean(scaled * normed, axis=-1, keepdims=True)
    )


B_QUERY, B_VALUE, B_OUT, GAIN1, SHIFT1, B_CONTRACT, GAIN2, SHIFT2 = range(8)
S_QUERY, S_VALUE, S_OUT, S_GAIN1, S_SHIFT1, S_EXPAND = range(6)
S_CONTRACT, S_GAIN2, S_SHIFT2, S_TABLE = 9, 10, 11, 16
LIMITS = (12, 16, 23, 32, 46, 64, 91)


def bucket_of(relative):
    distance = jnp.abs(relative)
    beyond = 8 + sum((distance >= limit).astype(jnp.int32) for limit in LIMITS)
    within = jnp.where(distance < 8, distance, beyond)
    return within + 16 * (relative > 0).astype(jnp.int32)


def forward(x, w, vec, b_expand, masks, s, keep):
    row = lambda k: vec[k : k + 1, :]
    s.query[...] = (nn(x[...], w.query[...]) + row(B_QUERY)).astype(LOW)
    s.key[...] = nn(x[:L], w.key[...]).astype(LOW)
    s.value[...] = (nn(x[:L], w.value[...]) + row(B_VALUE)).astype(LOW)
    for pair in range(PAIRS):
        lanes = slice(pair * 128, (pair + 1) * 128)
        scores = nt(halves(s.query[:, lanes]), s.key[:, lanes]) * SCALE + masks[pair]
        shifted = jnp.exp(scores - jnp.max(scores, axis=-1, keepdims=True))
        probs = (shifted / jnp.sum(shifted, axis=-1, keepdims=True)).astype(LOW)
        if keep:
            s.probs[pair] = probs
        s.mixed[:, lanes] = nn(side(probs), halves(s.value[:, lanes])).astype(LOW)
    total = x[...].astype(WIDE) + nn(s.mixed[...], w.out[...]) + row(B_OUT)
    normed, root = norm_rows(total)
    first = normed * row(GAIN1) + row(SHIFT1)
    s.first_low[...] = first.astype(LOW)
    s.total[...] = first + row(B_CONTRACT)
    if keep:
        s.normed1[...] = normed
        s.root1[...] = jnp.broadcast_to(root, (ROWS, 128))
    for tile in range(FF // TILE):
        tile = slice(tile * TILE, (tile + 1) * TILE)
        expanded = nn(s.first_low[...], w.expand[:, tile]) + b_expand[:, tile]
        cumulative = 0.5 * (1.0 + lax.erf(expanded * 0.7071067811865476))
        activated = (expanded * cumulative).astype(LOW)
        if keep:
            s.slope[:, tile] = (
                cumulative + expanded * jnp.exp(-0.5 * expanded * expanded) * 0.3989422804014327
            ).astype(LOW)
            s.activated[:, tile] = activated
        s.total[...] += nn(activated, w.contract[tile, :])
    normed, root = norm_rows(s.total[...])
    if keep:
        s.normed2[...] = normed
        s.root2[...] = jnp.broadcast_to(root, (ROWS, 128))
    s.out[...] = (normed * row(GAIN2) + row(SHIFT2)).astype(s.out.dtype)


def column_sum(value):
    return jnp.sum(value.astype(WIDE), axis=0, keepdims=True)


def back_second_norm(grad, vec, s, add=None):
    upper = grad.astype(WIDE)
    normed = s.normed2[...]
    lower = norm_rows_back(upper * vec[GAIN2 : GAIN2 + 1, :], normed, s.root2[:, :1])
    s.total[...] = lower
    s.branch[...] = lower.astype(LOW)
    if add is not None:
        add(S_GAIN2, column_sum(upper * normed))
        add(S_SHIFT2, column_sum(upper))
        add(S_CONTRACT, column_sum(lower.astype(LOW)))


def back_feed(w, vec, s, add=None):
    for tile in range(FF // TILE):
        tile = slice(tile * TILE, (tile + 1) * TILE)
        lower = (nt(s.branch[...], w.contract[tile, :]) * s.slope[:, tile].astype(WIDE)).astype(LOW)
        s.expanded[:, tile] = lower
        if add is not None:
            part = column_sum(lower)
            for column in range(TILE // D):
                add(
                    S_EXPAND + tile.start // D + column,
                    part[:, column * D : (column + 1) * D],
                )
        s.total[...] += nt(lower, w.expand[:, tile])
    upper = s.total[...]
    normed = s.normed1[...]
    lower = norm_rows_back(upper * vec[GAIN1 : GAIN1 + 1, :], normed, s.root1[:, :1])
    s.total[...] = lower
    s.attended[...] = lower.astype(LOW)
    if add is not None:
        add(S_GAIN1, column_sum(upper * normed))
        add(S_SHIFT1, column_sum(upper))
        add(S_OUT, column_sum(lower.astype(LOW)))


def back_attend(s, table=None):
    for pair in range(PAIRS):
        lanes = slice(pair * 128, (pair + 1) * 128)
        probs = s.probs[pair]
        below = halves(s.dmixed[:, lanes])
        dprobs = nt(below, s.value[:, lanes])
        s.dvalue[:, lanes] = tn(probs, below).astype(LOW)
        weight = probs.astype(WIDE)
        dscores = (
            weight * (dprobs - jnp.sum(weight * dprobs, axis=-1, keepdims=True))
        ).astype(LOW)
        s.dquery[:, lanes] = (nn(side(dscores), halves(s.key[:, lanes])) * SCALE).astype(LOW)
        s.dkey[:, lanes] = (tn(dscores, halves(s.query[:, lanes])) * SCALE).astype(LOW)
        if table is not None:
            table(pair, dscores)


class Names:
    def __init__(self, **named):
        self.__dict__.update(named)


MATRICES = ("query", "key", "value", "out", "expand", "contract")
MATRIX_SHAPES = {
    "query": (D, D),
    "key": (D, D),
    "value": (D, D),
    "out": (D, D),
    "expand": (D, FF),
    "contract": (FF, D),
}
MASK_SHAPE = (PAIRS, 2 * ROWS, L)
KEPT = {
    "query": ((ROWS, D), LOW),
    "key": ((L, D), LOW),
    "value": ((L, D), LOW),
    "probs": (MASK_SHAPE, LOW),
    "mixed": ((ROWS, D), LOW),
    "normed1": ((ROWS, D), WIDE),
    "root1": ((ROWS, 128), WIDE),
    "first_low": ((ROWS, D), LOW),
    "slope": ((ROWS, FF), LOW),
    "activated": ((ROWS, FF), LOW),
    "normed2": ((ROWS, D), WIDE),
    "root2": ((ROWS, 128), WIDE),
}
SAVED = tuple(name for name in KEPT if name != "mixed")
ANY = pl.BlockSpec(memory_space=pl.ANY)
VMEM = pl.BlockSpec(memory_space=pltpu.VMEM)
SMEM = pl.BlockSpec(memory_space=pltpu.SMEM)


def limit(megabytes):
    return pltpu.CompilerParams(vmem_limit_bytes=megabytes * 1024 * 1024)


DMA = pltpu.SemaphoreType.DMA


def cost(microseconds):
    return pl.CostEstimate(flops=0, bytes_accessed=int(microseconds * 3.2e6), transcendentals=0)


def shaped(shape, kind):
    return jax.ShapeDtypeStruct(shape, kind)


def columns(ref, start, size):
    return ref.at[:, pl.ds(pl.multiple_of(start, 128), size)]


def rows_at(ref, start, size):
    return ref.at[pl.ds(pl.multiple_of(start, 64), size)]


def start_all(pairs, sems, base=0):
    copies = [
        pltpu.make_async_copy(source, target, sems.at[base + index])
        for index, (source, target) in enumerate(pairs)
    ]
    for copy in copies:
        copy.start()
    return copies


def wait_all(copies):
    for copy in copies:
        copy.wait()


def fetcher(names, sources, targets, sems, base=0):
    copies = dict(zip(names, start_all(list(zip(sources, targets)), sems, base)))
    return lambda name: copies[name].wait()


def take_rows(content, picks, seq, target):
    target[:L] = content[seq * L : (seq + 1) * L]
    target[L:] = picks[seq * PICKS : (seq + 1) * PICKS]


def front(seq, content, picks, matrices, masks, vec, b_expand, after=()):
    def kernel(content, picks, masks, vec, b_expand, *refs):
        w = Names(**dict(zip(MATRICES, refs[:6])))
        out, x, query, key, value, mixed, first_low, total = refs[6 + len(after) :]
        s = Names(
            query=query,
            key=key,
            value=value,
            mixed=mixed,
            first_low=first_low,
            total=total,
            out=out,
        )
        take_rows(content, picks, seq, x)
        forward(x, w, vec, b_expand, masks.at[seq], s, False)

    return pl.pallas_call(
        kernel,
        out_shape=shaped((ROWS, D), LOW),
        in_specs=[VMEM] * 11 + [ANY] * len(after),
        out_specs=VMEM,
        scratch_shapes=[pltpu.VMEM((ROWS, D), LOW)]
        + [pltpu.VMEM(*KEPT[n]) for n in ("query", "key", "value", "mixed", "first_low")]
        + [pltpu.VMEM((ROWS, D), WIDE)],
        compiler_params=limit(12),
        cost_estimate=cost(5),
        name="front",
    )(content, picks, masks, vec, b_expand, *matrices, *after)


def middle_forward(seq, info, content, picks, arrived, matrices, masks, vec, b_expand, after=()):
    def kernel(info, arrived, content, picks, masks, vec, b_expand, *refs):
        w, rest = Names(**dict(zip(MATRICES, refs[:6]))), refs[6 + len(after) :]
        (out, early, pair), kept = rest[:3], rest[3 : 3 + len(SAVED)]
        mixed, total = rest[3 + len(SAVED) :]
        x = pair.at[0]
        s = Names(total=total, out=out, mixed=mixed, **dict(zip(SAVED, kept)))
        take_rows(content, picks, seq, x)
        x[...] = jnp.where(info[2] == 1, x[...], arrived[...])
        early[:, :D] = x[...]
        forward(x, w, vec, b_expand, masks.at[seq], s, True)
        pair[1] = mixed[...]
        early[:, D : 2 * D] = mixed[...]
        early[:, 2 * D : 3 * D] = s.first_low[...]
        early[:, 3 * D :] = columns(s.activated, (1 - info[0]) * HALF, HALF)[...]

    out, early, pair, *saved = pl.pallas_call(
        kernel,
        out_shape=[
            shaped((ROWS, D), WIDE),
            shaped((ROWS, EARLY), LOW),
            shaped((2, ROWS, D), LOW),
        ]
        + [shaped(*KEPT[n]) for n in SAVED],
        in_specs=[SMEM] + [VMEM] * 12 + [ANY] * len(after),
        out_specs=[VMEM] * (3 + len(SAVED)),
        scratch_shapes=[pltpu.VMEM(*KEPT["mixed"]), pltpu.VMEM((ROWS, D), WIDE)],
        compiler_params=limit(16),
        cost_estimate=cost(6),
        name="middle_forward",
    )(info, arrived, content, picks, masks, vec, b_expand, *matrices, *after)
    return (out, early, pair, dict(zip(SAVED, saved)))


FEED_SAVED = ("normed2", "root2", "slope", "normed1", "root1")
ATTEND_SAVED = ("value", "probs", "key", "query")


def middle_back(seq, content, picks, matrices, vec, saved):
    names = FEED_SAVED + ATTEND_SAVED

    def kernel(content, picks, vec, *refs):
        w, rest = Names(**dict(zip(MATRICES, refs[:6]))), refs[6:]
        kept, grad, rest = rest[: len(names)], rest[len(names)], rest[len(names) + 1 :]
        cot, total, branch, expanded, attended, dmixed, dvalue, dquery, dkey = rest
        s = Names(
            total=total,
            branch=branch,
            expanded=expanded,
            attended=attended,
            dmixed=dmixed,
            dvalue=dvalue,
            dquery=dquery,
            dkey=dkey,
            **dict(zip(names, kept)),
        )
        take_rows(content, picks, seq, cot)
        back_second_norm(cot[...], vec, s)
        back_feed(w, vec, s)
        dmixed[...] = nt(attended[...], w.out[...]).astype(LOW)
        back_attend(s)
        lower = total[...] + nt(dquery[...], w.query[...])
        upper = nt(dkey[...], w.key[...]) + nt(dvalue[...], w.value[...])
        grad[:L] = (lower[:L] + upper).astype(LOW)
        grad[L:] = lower[L:].astype(LOW)

    return pl.pallas_call(
        kernel,
        out_shape=shaped((ROWS, D), LOW),
        in_specs=[VMEM] * (9 + len(names)),
        out_specs=VMEM,
        scratch_shapes=[
            pltpu.VMEM((ROWS, D), LOW),
            pltpu.VMEM((ROWS, D), WIDE),
            pltpu.VMEM((ROWS, D), LOW),
            pltpu.VMEM((ROWS, FF), LOW),
            pltpu.VMEM((ROWS, D), LOW),
            pltpu.VMEM((ROWS, D), LOW),
            pltpu.VMEM((L, D), LOW),
            pltpu.VMEM((ROWS, D), LOW),
            pltpu.VMEM((L, D), LOW),
        ],
        compiler_params=limit(12),
        cost_estimate=cost(7),
        name="middle_back",
    )(content, picks, vec, *matrices, *(saved[n] for n in names))


def feed_back(seq, info, arrived, content, picks, small_in, vec, matrices, saved):
    def kernel(info, arrived, content, picks, small_in, vec, expand, contract, *refs):
        kept, rest = refs[:5], refs[5:]
        total, branch, attended, small, own, late, upper, expanded = rest
        w = Names(expand=expand, contract=contract)
        s = Names(
            total=total,
            branch=branch,
            attended=attended,
            expanded=expanded,
            **dict(zip(FEED_SAVED, kept)),
        )
        small[...] = small_in[...]

        def add(place, value):
            small[place : place + 1, :] += value

        take_rows(content, picks, seq, upper)
        back_second_norm(jnp.where(info[2] == 1, arrived[...], upper[...]), vec, s, add)
        late[:, :D] = branch[...]
        back_feed(w, vec, s, add)
        own[...] = columns(expanded, info[0] * HALF, HALF)[...]
        late[:, D:] = columns(expanded, (1 - info[0]) * HALF, HALF)[...]

    return pl.pallas_call(
        kernel,
        out_shape=[
            shaped((ROWS, D), WIDE),
            shaped((ROWS, D), LOW),
            shaped((ROWS, D), LOW),
            shaped((SMALL, D), WIDE),
            shaped((ROWS, HALF), LOW),
            shaped((ROWS, LATE), LOW),
        ],
        in_specs=[SMEM] + [VMEM] * 12,
        out_specs=[VMEM] * 6,
        scratch_shapes=[pltpu.VMEM((ROWS, D), LOW), pltpu.VMEM((ROWS, FF), LOW)],
        compiler_params=limit(12),
        cost_estimate=cost(4),
        name="feed_back",
    )(
        info,
        arrived,
        content,
        picks,
        small_in,
        vec,
        matrices[4],
        matrices[5],
        *(saved[n] for n in FEED_SAVED),
    )


PLACES = {
    (2, 0): (0, 0),
    (1, 1): (0, 1),
    (2, 1): (1, 0),
    (3, 0): (1, 1),
    (1, 0): (2, 0),
    (3, 1): (3, 0),
    (0, 0): (4, 0),
    (0, 1): (4, 1),
}


def term_shapes(count):
    return [shaped((n * count, D), LOW) for n in (2, 2, 1, 1, 2)]


def feed_grads(info, mine, branch, own, early, late):
    def kernel(info, *refs):
        acts, lows, branches, owns, earlies, lates = (refs[2 * i : 2 * i + 2] for i in range(6))
        outs, (a_act, a_first, b_branch, b_own, stage, sems, out_sems) = refs[12:17], refs[17:]
        core, place = info[0], info[1]
        own_at = [slice(seq * ROWS, (seq + 1) * ROWS) for seq in range(SEQS)]
        far_at = [slice((2 + seq) * ROWS, (3 + seq) * ROWS) for seq in range(SEQS)]
        pairs, later = [], []
        for seq in range(SEQS):
            pairs += [
                (columns(acts[seq], core * HALF, HALF), a_act.at[own_at[seq]]),
                (earlies[seq].at[:, 3 * D :], a_act.at[far_at[seq]]),
                (branches[seq], b_branch.at[own_at[seq]]),
                (lates[seq].at[:, :D], b_branch.at[far_at[seq]]),
            ]
            later += [
                (lows[seq], a_first.at[own_at[seq]]),
                (earlies[seq].at[:, 2 * D : 3 * D], a_first.at[far_at[seq]]),
                (owns[seq], b_own.at[own_at[seq]]),
                (lates[seq].at[:, D:], b_own.at[far_at[seq]]),
            ]
        copies = start_all(pairs + later, sems)
        sent = []

        def send(block):
            for k in range(4):
                quarter = lax.rem(place + k, 4)
                index, part = PLACES[k, block // 2]
                start = (2 * part + block % 2) * QUARTER
                sent.extend(
                    start_all(
                        [
                            (
                                rows_at(stage.at[block], quarter * QUARTER, QUARTER),
                                outs[index].at[start : start + QUARTER],
                            )
                        ],
                        out_sems,
                        block * 4 + k,
                    )
                )

        wait_all(copies[:8])
        for block in range(2):
            for part in range(3):
                start = block * D + part * 256
                stage[block, part * 256 : (part + 1) * 256] = tn(
                    a_act[:, start : start + 256], b_branch[...]
                ).astype(LOW)
            send(block)
        wait_all(copies[8:])
        for block in range(2):
            for part in range(3):
                stage[2 + block, part * 256 : (part + 1) * 256] = tn(
                    a_first[:, part * 256 : (part + 1) * 256], b_own[:, block * D : (block + 1) * D]
                ).astype(LOW)
            send(2 + block)
        wait_all(sent)

    acts = [saved["activated"] for saved in mine]
    lows = [saved["first_low"] for saved in mine]
    return pl.pallas_call(
        kernel,
        out_shape=term_shapes(2 * QUARTER),
        in_specs=[SMEM] + [ANY] * 12,
        out_specs=[ANY] * 5,
        scratch_shapes=[
            pltpu.VMEM((2 * ALL_ROWS, HALF), LOW),
            pltpu.VMEM((2 * ALL_ROWS, D), LOW),
            pltpu.VMEM((2 * ALL_ROWS, D), LOW),
            pltpu.VMEM((2 * ALL_ROWS, HALF), LOW),
            pltpu.VMEM((4, D, D), LOW),
            DMA((16,)),
            DMA((16,)),
        ],
        compiler_params=limit(24),
        cost_estimate=cost(8),
        name="feed_grads",
    )(info, *acts, *lows, *branch, *own, *early, *late)


def attend_back(info, total, attended, small_in, spread, output, after, matrices, saved, picks):
    names = ("out", "query", "key", "value")
    sources = [matrices[3]] + list(matrices[:3])
    kept_in = [saved[seq][n] for seq in range(SEQS) for n in ATTEND_SAVED]

    def kernel(info, small_in, spread, *refs):
        totals, attendeds, outputs = refs[0:2], refs[2:4], refs[4:6]
        w, kept, rest = Names(**dict(zip(names, refs[6:10]))), refs[10:18], refs[18 + len(after) :]
        content_ends, query_ends, small, own, send, dmixed, pieces, table, sums = rest
        at = [slice(seq * ROWS, (seq + 1) * ROWS) for seq in range(SEQS)]
        lower_at = [
            slice(ALL_ROWS + seq * L, ALL_ROWS + (seq + 1) * L) for seq in range(SEQS)
        ]
        for seq in range(SEQS):
            pieces[1, at[seq]] = attendeds[seq][...]
        dmixed[...] = nt(pieces[1, :ALL_ROWS], w.out[...]).astype(LOW)
        for seq in range(SEQS):
            s = Names(
                dmixed=dmixed.at[at[seq]],
                dquery=pieces.at[0, at[seq]],
                dkey=pieces.at[0, lower_at[seq]],
                dvalue=pieces.at[1, lower_at[seq]],
                **dict(zip(ATTEND_SAVED, kept[4 * seq : 4 * seq + 4])),
            )

            def table_sum(pair, dscores, seq=seq):
                for odd in range(2):
                    part = nn(spread[seq], dscores[odd * ROWS : (odd + 1) * ROWS])
                    if seq == 0:
                        table[2 * pair + odd] = part
                    else:
                        table[2 * pair + odd] += part

            back_attend(s, table_sum)
        own[...] = pieces[info[0]]
        send[...] = pieces[1 - info[0]]
        lower = nt(pieces[0, :ALL_ROWS], w.query[...])
        upper = nt(pieces[0, ALL_ROWS:], w.key[...]) + nt(pieces[1, ALL_ROWS:], w.value[...])
        first = info[2] == 1
        for seq in range(SEQS):
            base = seq * ROWS
            content_ends[seq * L : (seq + 1) * L] = jnp.where(
                first,
                totals[seq][:L] + lower[base : base + L] + upper[seq * L : (seq + 1) * L],
                outputs[seq][:L],
            )
            query_ends[seq * picks : (seq + 1) * picks] = jnp.where(
                first,
                totals[seq][L : L + picks] + lower[base + L : base + L + picks],
                outputs[seq][L : L + picks],
            )
        small[...] = small_in[...]
        small[S_QUERY : S_QUERY + 1, :] = column_sum(pieces[0, :ALL_ROWS])
        small[S_VALUE : S_VALUE + 1, :] = column_sum(pieces[1, ALL_ROWS:])
        sums[...] = jnp.zeros_like(sums)
        for head in range(H):
            both = jnp.concatenate([table[head], jnp.zeros((L, L), WIDE)], axis=1)
            turned = pltpu.roll(both, 0, 1, stride=1, stride_axis=0)
            sums[head : head + 1, :] = jnp.sum(turned, axis=0, keepdims=True)
        distance = lax.broadcasted_iota(jnp.int32, (2 * L, L), 0) - (L - 1)
        bucket = lax.broadcasted_iota(jnp.int32, (2 * L, L), 1)
        small[S_TABLE : S_TABLE + 16, :L] = lax.dot_general(
            sums[...],
            (bucket_of(distance) == bucket).astype(WIDE),
            (((1,), (0,)), ((), ())),
            precision=lax.Precision.HIGHEST,
            preferred_element_type=WIDE,
        )

    return pl.pallas_call(
        kernel,
        out_shape=[
            shaped((ALL_CONTENT, D), WIDE),
            shaped((SEQS * picks, D), WIDE),
            shaped((SMALL, D), WIDE),
            shaped((PIECE, D), LOW),
            shaped((PIECE, D), LOW),
        ],
        in_specs=[SMEM] + [VMEM] * 20 + [ANY] * len(after),
        out_specs=[VMEM] * 5,
        scratch_shapes=[
            pltpu.VMEM((ALL_ROWS, D), LOW),
            pltpu.VMEM((2, PIECE, D), LOW),
            pltpu.VMEM((H, L, L), WIDE),
            pltpu.VMEM((16, 2 * L), WIDE),
        ],
        compiler_params=limit(16),
        cost_estimate=cost(10),
        name="attend_back",
    )(info, small_in, spread, *total, *attended, *output, *sources, *kept_in, *after)


def attend_grads(info, pair, early, own, arrived, small, after=()):
    def kernel(info, small, own, arrived, *refs):
        pairs_in, earlies, refs = refs[0:2], refs[2:4], refs[4 + len(after) :]
        outs, rest = refs[:5], refs[5:]
        a_rows, a_content, b_rows, b_content, stage, extra, sems, out_sems = rest
        core, place = info[0], info[1]
        pairs = [
            (own.at[:ALL_ROWS], b_rows.at[:ALL_ROWS]),
            (arrived.at[:ALL_ROWS], b_rows.at[ALL_ROWS:]),
        ]
        later = [
            (own.at[ALL_ROWS:], b_content.at[:ALL_CONTENT]),
            (arrived.at[ALL_ROWS:], b_content.at[ALL_CONTENT:]),
        ]
        for seq in range(SEQS):
            at, far = seq * ROWS, (2 + seq) * ROWS
            pairs += [
                (pairs_in[seq].at[core], a_rows.at[at : at + ROWS]),
                (columns(earlies[seq], core * D, D), a_rows.at[far : far + ROWS]),
            ]
            at, far = seq * L, (2 + seq) * L
            later += [
                (pairs_in[seq].at[0, :L], a_content.at[at : at + L]),
                (earlies[seq].at[:L, :D], a_content.at[far : far + L]),
            ]
        copies = start_all(pairs + later, sems)
        extra[0] = small[...].astype(LOW)
        extra[1] = jnp.zeros((EXTRA, D), LOW)
        sent = []
        for block, (former, latter) in enumerate(((a_rows, b_rows), (a_content, b_content))):
            wait_all(copies[6 * block : 6 * block + 6])
            for part in range(3):
                stage[block, part * 256 : (part + 1) * 256] = tn(
                    former[:, part * 256 : (part + 1) * 256], latter[...]
                ).astype(LOW)
            for k in range(4):
                quarter = lax.rem(place + k, 4)
                index, part = PLACES[k, block]
                start = part * (QUARTER + EXTRA)
                middle, stop = start + QUARTER, start + QUARTER + EXTRA
                sent += start_all(
                    [
                        (
                            rows_at(stage.at[block], quarter * QUARTER, QUARTER),
                            outs[index].at[start:middle],
                        ),
                        (extra.at[block], outs[index].at[middle:stop]),
                    ],
                    out_sems,
                    block * 8 + 2 * k,
                )
        wait_all(sent)

    return pl.pallas_call(
        kernel,
        out_shape=term_shapes(QUARTER + EXTRA),
        in_specs=[SMEM, VMEM] + [ANY] * (6 + len(after)),
        out_specs=[ANY] * 5,
        scratch_shapes=[
            pltpu.VMEM((2 * ALL_ROWS, D), LOW),
            pltpu.VMEM((2 * ALL_CONTENT, D), LOW),
            pltpu.VMEM((2 * ALL_ROWS, D), LOW),
            pltpu.VMEM((2 * ALL_CONTENT, D), LOW),
            pltpu.VMEM((2, D, D), LOW),
            pltpu.VMEM((2, EXTRA, D), LOW),
            DMA((12,)),
            DMA((16,)),
        ],
        compiler_params=limit(20),
        cost_estimate=cost(5),
        name="attend_grads",
    )(info, small, own, arrived, *pair, *early, *after)


def feed_targets(outs, source, half, core, quarter):
    pairs = []
    for block in range(2):
        part = source.at[block * QUARTER : (block + 1) * QUARTER]
        if half == 0:
            target = rows_at(outs[0], core * HALF + block * D + quarter * QUARTER, QUARTER)
        else:
            target = columns(
                rows_at(outs[1], quarter * QUARTER, QUARTER), (core * 2 + block) * D, D
            )
        pairs.append((None, part, target))
    return pairs


def attend_targets(outs, source, half, core, quarter):
    return [
        (
            core == number,
            source.at[:QUARTER],
            rows_at(outs[2 * number + half], quarter * QUARTER, QUARTER),
        )
        for number in range(2)
    ]


def settle(targets, shapes, count, info, pieces, outs, through, name):
    keys = tuple(pieces)
    arrays = [pieces[key] for key in keys]
    given = list(outs or ()) + list(through)
    first_alias = len(shapes) - len(outs or ())

    def kernel(info, *refs):
        parts, rest = refs[: len(keys)], refs[len(keys) + len(given) :]
        outs, rest = rest[: len(shapes)], rest[len(shapes) + len(through) :]
        held, wide_held, (sems, out_sems) = rest[: len(keys)], rest[len(keys) : -2], rest[-2:]
        copies = start_all(list(zip(parts, held)), sems)
        finish = []
        for index, (sibling, k, which) in enumerate(keys):
            core = 1 - info[0] if sibling else info[0]
            quarter = lax.rem((info[3] if sibling else info[1]) + k, 4)
            copies[index].wait()
            wide_held[index][...] = held[index][...].astype(WIDE)
            for number, half in enumerate(which):
                source = wide_held[index].at[number * count : (number + 1) * count]
                for place, (condition, part, target) in enumerate(
                    targets(outs, source, half, core, quarter)
                ):
                    copy = pltpu.make_async_copy(
                        part, target, out_sems.at[4 * index + 2 * number + place]
                    )
                    if condition is None:
                        copy.start()
                        finish.append(copy.wait)
                    else:
                        pl.when(condition)(copy.start)
                        finish.append(lambda c=copy, when=condition: pl.when(when)(c.wait))
        for action in finish:
            action()

    result = pl.pallas_call(
        kernel,
        out_shape=[shaped(shape, WIDE) for shape in shapes]
        + [shaped(array.shape, array.dtype) for array in through],
        in_specs=[SMEM] + [ANY] * (len(keys) + len(given)),
        out_specs=[ANY] * (len(shapes) + len(through)),
        scratch_shapes=[pltpu.VMEM(array.shape, LOW) for array in arrays]
        + [pltpu.VMEM(array.shape, WIDE) for array in arrays]
        + [DMA((len(keys),)), DMA((4 * len(keys),))],
        input_output_aliases={1 + len(keys) + i: first_alias + i for i in range(len(given))},
        compiler_params=limit(32),
        cost_estimate=cost(sum(array.size for array in arrays) * 2e-6 + 1),
        name=name,
    )(info, *arrays, *given)
    return result[: len(shapes)], result[len(shapes) :]


TOP_PRECISION = lax.Precision.HIGHEST


def geometry(order_row, pos_row, tag_row, table):
    positions = lax.iota(jnp.int32, L)
    matches = pos_row[:, None] == positions[None, :]
    predicted = jnp.any(matches, axis=0)
    query_rank = jnp.sum(jnp.where(matches, order_row[None, :], 0), axis=1)
    query_tag = jnp.sum(jnp.where(matches, tag_row[None, :], 0), axis=1)
    row_rank = jnp.concatenate([order_row, query_rank])
    row_tag = jnp.concatenate([tag_row, query_tag])
    row_place = jnp.concatenate([positions, pos_row])
    row_flag = jnp.concatenate([predicted, jnp.ones(pos_row.shape, jnp.bool_)])
    strict = jnp.concatenate([jnp.zeros((L,), jnp.int32), jnp.ones(pos_row.shape, jnp.int32)])
    same_group = row_tag[:, None] == tag_row[None, :]
    earlier = order_row[None, :] + strict[:, None] <= row_rank[:, None]
    allowed = same_group & (~predicted[None, :] | row_flag[:, None] & earlier)
    buckets = bucket_of(positions[None, :] - row_place[:, None])
    one_hot = (buckets[None] == lax.iota(jnp.int32, NB)[:, None, None]).astype(WIDE)
    score_bias = jnp.einsum("krl,kh->hrl", one_hot, table, precision=TOP_PRECISION)
    masked = jnp.where(allowed[None], score_bias, -1e30)
    masked = jnp.pad(masked, ((0, 0), (0, ROWS - masked.shape[1]), (0, 0)))
    padded = jnp.pad(matches.astype(LOW), ((0, PICKS - matches.shape[0]), (0, 0)))
    spread = jnp.concatenate([jnp.eye(L, dtype=LOW), padded.T], axis=1)[::-1]
    return (masked, spread)


PLANE = ("x", "y", "c")


def shift(value, axis, by):
    size = lax.axis_size(axis)
    return lax.ppermute(value, axis, [(i, (i + by) % size) for i in range(size)])


def send(value, by):
    return lax.ppermute(value, "s", [(0, 1)] if by > 0 else [(1, 0)])


def turn(value, outer, by):
    pairs = []
    for i in range(4):
        for j in range(4):
            for c in range(2):
                if (c == 0) == outer:
                    target = ((i + by) % 4, j)
                else:
                    target = (i, (j + by) % 4)
                pairs.append(((i * 4 + j) * 2 + c, (target[0] * 4 + target[1]) * 2 + c))
    return lax.ppermute(value, PLANE, pairs)


def place(outer):
    return jnp.where(
        (lax.axis_index("c") == 0) == outer, lax.axis_index("x"), lax.axis_index("y")
    )


def wide(value):
    return value.astype(WIDE)


def pick(parts, index):
    return lax.dynamic_index_in_dim(parts, index, 0, keepdims=False)


def total_wide(*terms):
    return sum(wide(term) for term in terms)


def total_of(*terms):
    return total_wide(*terms).astype(LOW)


def chain_start(terms):
    plus, minus, after0, before1, own = terms
    count = after0.shape[0]
    from_left = turn(plus, True, 1)
    from_right = turn(minus, True, -1)
    to_right = total_of(after0, from_left[:count])
    to_left = total_of(before1, from_right[:count])
    return (to_right, to_left, from_left, from_right, own)


def chain_reduce(terms):
    to_right, to_left, from_left, from_right, own = terms
    count = to_right.shape[0]
    left = turn(to_right, True, 1)
    right = turn(to_left, True, -1)
    sums = [
        total_of(own[:count], left, from_right[count:]),
        total_of(own[count:], from_left[count:], right),
    ]
    parts = jnp.concatenate([part.reshape(4, count // 4, D) for part in sums], axis=1)
    me = place(False)
    arrived = [turn(pick(parts, (me + by) % 4), False, by) for by in (1, 2, -1)]
    part = total_of(pick(parts, me), *arrived)
    return total_of(part, shift(part, "z", 1))


def gather_inner(part):
    count = part.shape[0] // 2
    me = place(False)
    whole = jnp.zeros((2, 4, count, D), LOW)
    for k, piece in enumerate([part] + [turn(part, False, -by) for by in (1, 2, -1)]):
        whole = lax.dynamic_update_slice(
            whole, piece.reshape(2, 1, count, D), (0, (me + k) % 4, 0, 0)
        )
    return whole.reshape(8 * count, D)


def gather_outer(own):
    before = turn(own, True, 1)
    after = turn(own, True, -1)
    near = {(0, (0, 1)): own, (3, (0, 1)): before, (1, (0, 1)): after}
    both = {(0,) + key: piece for key, piece in near.items()}
    return both | {(1,) + key: shift(piece, "c", 1) for key, piece in near.items()}


def gather_across(pieces):
    before, after = pieces[0, 3, (0, 1)], pieces[0, 1, (0, 1)]
    count = before.shape[0] // 2
    far = {(2, (0,)): turn(before[:count], True, 1), (2, (1,)): turn(after[count:], True, -1)}
    both = {(0,) + key: piece for key, piece in far.items()}
    return both | {(1,) + key: shift(piece, "c", 1) for key, piece in far.items()}


def on_device(
    content_in,
    query_in,
    content_cot,
    query_cot,
    order_rank,
    query_pos,
    group_tag,
    *rest,
):
    (
        w_query,
        b_query,
        w_key,
        w_value,
        b_value,
        w_out,
        b_out,
        norm1_gain,
        norm1_bias,
        w_expand,
        b_expand,
        w_contract,
        b_contract,
        norm2_gain,
        norm2_bias,
    ) = (argument[0] for argument in rest[:-1])
    rel_table = rest[-1]
    core = lax.axis_index("c")
    first_section = (lax.axis_index("s") == 0).astype(jnp.int32)
    info = jnp.stack([core, place(True), first_section, place(False)])
    picks = query_pos.shape[1]

    def padded(query):
        query = jnp.pad(query.reshape(SEQS, picks, D), ((0, 0), (0, PICKS - picks), (0, 0)))
        return query.reshape(SEQS * PICKS, D)

    masks, spread = jax.vmap(geometry, in_axes=(0, 0, 0, None))(
        order_rank, query_pos, group_tag, rel_table
    )
    masks = masks.reshape((SEQS,) + MASK_SHAPE)
    query_in, query_cot = padded(query_in), padded(query_cot)
    matrices = (w_query, w_key, w_value, w_out, w_expand, w_contract)
    vec = jnp.stack(
        [b_query, b_value, b_out, norm1_gain, norm1_bias, b_contract, norm2_gain, norm2_bias]
    )
    b_expand = b_expand[None]

    fronts, arrived = [], []
    for seq in range(SEQS):
        fronts.append(
            front(seq, content_in, query_in, matrices, masks, vec, b_expand, tuple(fronts))
        )
        arrived.append(send(fronts[seq], 1))
    output, early, pair, saved, grads = [], [], [], [], []
    for seq in range(SEQS):
        results = middle_forward(
            seq, info, content_in, query_in, arrived[seq], matrices, masks, vec, b_expand, tuple(grads)
        )
        for collected, result in zip((output, early, pair, saved), results):
            collected.append(result)
        grads.append(middle_back(seq, content_cot, query_cot, matrices, vec, saved[seq]))
    early = [shift(value, "c", 1) for value in early]
    grads = [send(value, -1) for value in grads]
    small = jnp.zeros((SMALL, D), WIDE)
    total, branch, attended, own, late = [], [], [], [], []
    for seq in range(SEQS):
        results = feed_back(
            seq, info, grads[seq], content_cot, query_cot, small, vec, matrices, saved[seq]
        )
        small = results[3]
        for collected, result in zip(
            (total, branch, attended, own, late), results[:3] + results[4:]
        ):
            collected.append(result)
    late = [shift(value, "c", 1) for value in late]
    terms = feed_grads(info, saved, branch, own, early, late)
    feed_terms = chain_start(terms)
    content_ends, query_ends, small, own, pass_on = attend_back(
        info, total, attended, small, spread, output, (terms[4],), matrices, saved, picks
    )
    passed = shift(pass_on, "c", 1)
    feed_part = chain_reduce(feed_terms)
    attend_terms = attend_grads(info, pair, early, own, passed, small, feed_terms[:2])
    attend_part = chain_reduce(chain_start(attend_terms))
    feed_own = gather_inner(feed_part)
    feed_near = gather_outer(feed_own)
    attend_own = gather_inner(attend_part)
    feed_shapes, attend_shapes = ((FF, D), (D, FF)), ((D, D),) * 4
    attend_near = gather_outer(attend_own)
    feed_outs, through = settle(
        feed_targets,
        feed_shapes,
        2 * QUARTER,
        info,
        feed_near,
        None,
        tuple(attend_near[0, k, (0, 1)] for k in (1, 3)),
        "feed_out",
    )
    attend_near[0, 1, (0, 1)], attend_near[0, 3, (0, 1)] = through
    feed_outs, _ = settle(
        feed_targets,
        feed_shapes,
        2 * QUARTER,
        info,
        gather_across(feed_near),
        feed_outs,
        (),
        "feed_out_last",
    )
    attend_outs, _ = settle(
        attend_targets,
        attend_shapes,
        QUARTER + EXTRA,
        info,
        attend_near,
        None,
        (),
        "attend_out",
    )
    attend_outs, _ = settle(
        attend_targets,
        attend_shapes,
        QUARTER + EXTRA,
        info,
        gather_across(attend_near),
        attend_outs,
        (),
        "attend_out_last",
    )
    contract, expand = feed_outs
    g_query, g_key, g_out, g_value = attend_outs
    small_sum = total_wide(
        *(attend_near[far, 0, (0, 1)][QUARTER : QUARTER + SMALL] for far in (0, 1))
    )
    table = small_sum[S_TABLE : S_TABLE + H, :L]
    table_total = (table + shift(table, "s", 1))[:, :NB].T
    row = lambda k: small_sum[k][None]
    return (
        content_ends[None],
        query_ends[None],
        g_query[None],
        row(S_QUERY),
        g_key[None],
        g_value[None],
        row(S_VALUE),
        g_out[None],
        row(S_OUT),
        row(S_GAIN1),
        row(S_SHIFT1),
        expand[None],
        small_sum[S_EXPAND : S_EXPAND + 4].reshape(1, FF),
        contract[None],
        row(S_CONTRACT),
        row(S_GAIN2),
        row(S_SHIFT2),
        table_total,
    )


DP = ("z", "x", "y", "c")


def solution(mesh):
    mesh = jax.sharding.Mesh(mesh.devices.reshape(2, 2, 4, 4, 2), ("s",) + DP)
    layer_specs = tuple(
        P("s", *([None] * (rank - 1))) for rank in (3, 2, 3, 3, 2, 3, 2, 2, 2, 3, 2, 3, 2, 2, 2)
    )
    in_specs = (P(DP, None),) * 7 + layer_specs + (P(),)
    out_specs = (P("s", DP, None),) * 2 + layer_specs + (P(),)
    return jax.shard_map(
        on_device, mesh=mesh, in_specs=in_specs, out_specs=out_specs, check_vma=False
    )
```

```python
import jax
import jax.numpy as jnp
from jax import lax
from jax.experimental import pallas as pl
from jax.experimental.pallas import tpu as pltpu
from jax.sharding import PartitionSpec as P

D = 768
H = 12
HD = 64
FF = 3072
NB = 32
L = 128
PAIRS = H // 2
SEQS = 2
PICKS = 32
ROWS = L + PICKS
EPSILON = 1e-05
SCALE = HD ** (-0.5)
TILE = 1536
LOW = jnp.bfloat16
WIDE = jnp.float32
HALF = FF // 2
QUARTER = D // 4
EARLY = 3 * D + HALF
LATE = D + HALF
EXTRA = 32
SMALL = 32
ALL_ROWS = SEQS * ROWS
ALL_CONTENT = SEQS * L
PIECE = ALL_ROWS + ALL_CONTENT


def nn(former, latter):
    return lax.dot_general(
        former, latter, (((1,), (0,)), ((), ())), preferred_element_type=WIDE
    )


def nt(former, latter):
    return lax.dot_general(
        former, latter, (((1,), (1,)), ((), ())), preferred_element_type=WIDE
    )


def tn(former, latter):
    return lax.dot_general(
        former, latter, (((0,), (0,)), ((), ())), preferred_element_type=WIDE
    )


def halves(value):
    even = lax.broadcasted_iota(jnp.int32, value.shape, 1) < HD
    zero = jnp.zeros_like(value)
    return jnp.concatenate([jnp.where(even, value, zero), jnp.where(even, zero, value)])


def side(value):
    count = value.shape[0] // 2
    return jnp.concatenate([value[:count], value[count:]], axis=1)


def norm_rows(values):
    centered = values - jnp.mean(values, axis=-1, keepdims=True)
    variance = jnp.mean(centered * centered, axis=-1, keepdims=True)
    root = lax.rsqrt(variance + EPSILON)
    return (centered * root, root)


def norm_rows_back(scaled, normed, root):
    return root * (
        scaled
        - jnp.mean(scaled, axis=-1, keepdims=True)
        - normed * jnp.mean(scaled * normed, axis=-1, keepdims=True)
    )


B_QUERY, B_VALUE, B_OUT, GAIN1, SHIFT1, B_CONTRACT, GAIN2, SHIFT2 = range(8)
S_QUERY, S_VALUE, S_OUT, S_GAIN1, S_SHIFT1, S_EXPAND = range(6)
S_CONTRACT, S_GAIN2, S_SHIFT2, S_TABLE = 9, 10, 11, 16
LIMITS = (12, 16, 23, 32, 46, 64, 91)


def bucket_of(relative):
    distance = jnp.abs(relative)
    beyond = 8 + sum((distance >= limit).astype(jnp.int32) for limit in LIMITS)
    within = jnp.where(distance < 8, distance, beyond)
    return within + 16 * (relative > 0).astype(jnp.int32)


def forward(x, w, vec, b_expand, masks, s, keep):
    row = lambda k: vec[k : k + 1, :]
    s.query[...] = (nn(x[...], w.query[...]) + row(B_QUERY)).astype(LOW)
    s.key[...] = nn(x[:L], w.key[...]).astype(LOW)
    s.value[...] = (nn(x[:L], w.value[...]) + row(B_VALUE)).astype(LOW)
    for pair in range(PAIRS):
        lanes = slice(pair * 128, (pair + 1) * 128)
        scores = nt(halves(s.query[:, lanes]), s.key[:, lanes]) * SCALE + masks[pair]
        shifted = jnp.exp(scores - jnp.max(scores, axis=-1, keepdims=True))
        probs = (shifted / jnp.sum(shifted, axis=-1, keepdims=True)).astype(LOW)
        if keep:
            s.probs[pair] = probs
        s.mixed[:, lanes] = nn(side(probs), halves(s.value[:, lanes])).astype(LOW)
    total = x[...].astype(WIDE) + nn(s.mixed[...], w.out[...]) + row(B_OUT)
    normed, root = norm_rows(total)
    first = normed * row(GAIN1) + row(SHIFT1)
    s.first_low[...] = first.astype(LOW)
    s.total[...] = first + row(B_CONTRACT)
    if keep:
        s.normed1[...] = normed
        s.root1[...] = jnp.broadcast_to(root, (ROWS, 128))
    for tile in range(FF // TILE):
        tile = slice(tile * TILE, (tile + 1) * TILE)
        expanded = nn(s.first_low[...], w.expand[:, tile]) + b_expand[:, tile]
        cumulative = 0.5 * (1.0 + lax.erf(expanded * 0.7071067811865476))
        activated = (expanded * cumulative).astype(LOW)
        if keep:
            s.slope[:, tile] = (
                cumulative + expanded * jnp.exp(-0.5 * expanded * expanded) * 0.3989422804014327
            ).astype(LOW)
            s.activated[:, tile] = activated
        s.total[...] += nn(activated, w.contract[tile, :])
    normed, root = norm_rows(s.total[...])
    if keep:
        s.normed2[...] = normed
        s.root2[...] = jnp.broadcast_to(root, (ROWS, 128))
    s.out[...] = (normed * row(GAIN2) + row(SHIFT2)).astype(s.out.dtype)


def column_sum(value):
    return jnp.sum(value.astype(WIDE), axis=0, keepdims=True)


def back_second_norm(grad, vec, s, add=None):
    upper = grad.astype(WIDE)
    normed = s.normed2[...]
    lower = norm_rows_back(upper * vec[GAIN2 : GAIN2 + 1, :], normed, s.root2[:, :1])
    s.total[...] = lower
    s.branch[...] = lower.astype(LOW)
    if add is not None:
        add(S_GAIN2, column_sum(upper * normed))
        add(S_SHIFT2, column_sum(upper))
        add(S_CONTRACT, column_sum(lower.astype(LOW)))


def back_feed(w, vec, s, add=None):
    for tile in range(FF // TILE):
        tile = slice(tile * TILE, (tile + 1) * TILE)
        lower = (nt(s.branch[...], w.contract[tile, :]) * s.slope[:, tile].astype(WIDE)).astype(LOW)
        s.expanded[:, tile] = lower
        if add is not None:
            part = column_sum(lower)
            for column in range(TILE // D):
                add(
                    S_EXPAND + tile.start // D + column,
                    part[:, column * D : (column + 1) * D],
                )
        s.total[...] += nt(lower, w.expand[:, tile])
    upper = s.total[...]
    normed = s.normed1[...]
    lower = norm_rows_back(upper * vec[GAIN1 : GAIN1 + 1, :], normed, s.root1[:, :1])
    s.total[...] = lower
    s.attended[...] = lower.astype(LOW)
    if add is not None:
        add(S_GAIN1, column_sum(upper * normed))
        add(S_SHIFT1, column_sum(upper))
        add(S_OUT, column_sum(lower.astype(LOW)))


def back_attend(s, table=None):
    for pair in range(PAIRS):
        lanes = slice(pair * 128, (pair + 1) * 128)
        probs = s.probs[pair]
        below = halves(s.dmixed[:, lanes])
        dprobs = nt(below, s.value[:, lanes])
        s.dvalue[:, lanes] = tn(probs, below).astype(LOW)
        weight = probs.astype(WIDE)
        dscores = (
            weight * (dprobs - jnp.sum(weight * dprobs, axis=-1, keepdims=True))
        ).astype(LOW)
        s.dquery[:, lanes] = (nn(side(dscores), halves(s.key[:, lanes])) * SCALE).astype(LOW)
        s.dkey[:, lanes] = (tn(dscores, halves(s.query[:, lanes])) * SCALE).astype(LOW)
        if table is not None:
            table(pair, dscores)


class Names:
    def __init__(self, **named):
        self.__dict__.update(named)


MATRICES = ("query", "key", "value", "out", "expand", "contract")
MATRIX_SHAPES = {
    "query": (D, D),
    "key": (D, D),
    "value": (D, D),
    "out": (D, D),
    "expand": (D, FF),
    "contract": (FF, D),
}
MASK_SHAPE = (PAIRS, 2 * ROWS, L)
KEPT = {
    "query": ((ROWS, D), LOW),
    "key": ((L, D), LOW),
    "value": ((L, D), LOW),
    "probs": (MASK_SHAPE, LOW),
    "mixed": ((ROWS, D), LOW),
    "normed1": ((ROWS, D), WIDE),
    "root1": ((ROWS, 128), WIDE),
    "first_low": ((ROWS, D), LOW),
    "slope": ((ROWS, FF), LOW),
    "activated": ((ROWS, FF), LOW),
    "normed2": ((ROWS, D), WIDE),
    "root2": ((ROWS, 128), WIDE),
}
SAVED = tuple(name for name in KEPT if name != "mixed")
ANY = pl.BlockSpec(memory_space=pl.ANY)
VMEM = pl.BlockSpec(memory_space=pltpu.VMEM)
SMEM = pl.BlockSpec(memory_space=pltpu.SMEM)


def limit(megabytes):
    return pltpu.CompilerParams(vmem_limit_bytes=megabytes * 1024 * 1024)


DMA = pltpu.SemaphoreType.DMA


def cost(microseconds):
    return pl.CostEstimate(flops=0, bytes_accessed=int(microseconds * 3.2e6), transcendentals=0)


def shaped(shape, kind):
    return jax.ShapeDtypeStruct(shape, kind)


def columns(ref, start, size):
    return ref.at[:, pl.ds(pl.multiple_of(start, 128), size)]


def rows_at(ref, start, size):
    return ref.at[pl.ds(pl.multiple_of(start, 64), size)]


def start_all(pairs, sems, base=0):
    copies = [
        pltpu.make_async_copy(source, target, sems.at[base + index])
        for index, (source, target) in enumerate(pairs)
    ]
    for copy in copies:
        copy.start()
    return copies


def wait_all(copies):
    for copy in copies:
        copy.wait()


def fetcher(names, sources, targets, sems, base=0):
    copies = dict(zip(names, start_all(list(zip(sources, targets)), sems, base)))
    return lambda name: copies[name].wait()


def prepare(ranks, table, query_in, query_cot, picks, after):
    def kernel(ranks, table, query_in, query_cot, *refs):
        masks, spread, rows_in, rows_cot = refs[len(after) :]
        order, tag, pos = ranks[:, :L], ranks[:, L : 2 * L], ranks[:, 2 * L : 2 * L + picks]
        for source, target in ((query_in, rows_in), (query_cot, rows_cot)):
            values = source[...].astype(WIDE)
            blank = jnp.zeros((PICKS - picks, D), WIDE)
            target[...] = jnp.concatenate(
                [values[:picks], blank, values[picks:], blank]
            ).astype(LOW)
        lane = lax.broadcasted_iota(jnp.int32, (L, L), 1)
        level = lax.broadcasted_iota(jnp.int32, (L, L), 0)
        lane_q = lax.broadcasted_iota(jnp.int32, (PICKS, L), 1)
        upright = lambda row: jnp.sum(jnp.where(lane == level, row, 0.0), axis=1, keepdims=True)
        distance = lax.broadcasted_iota(jnp.int32, (2 * L, NB), 0) - (L - 1)
        bucket = lax.broadcasted_iota(jnp.int32, (2 * L, NB), 1)
        by_distance = lax.dot_general(
            table[...],
            (bucket_of(distance) == bucket).astype(WIDE),
            (((0,), (1,)), ((), ())),
            precision=lax.Precision.HIGHEST,
            preferred_element_type=WIDE,
        )
        allowed, hot = [], []
        for seq in range(SEQS):
            own_rank = order[seq : seq + 1, :].astype(WIDE)
            own_tag = tag[seq : seq + 1, :].astype(WIDE)
            own_pos = pos[seq : seq + 1, :].astype(WIDE)
            number = lax.broadcasted_iota(jnp.int32, (PICKS, picks), 0)
            same = number == lax.broadcasted_iota(jnp.int32, (PICKS, picks), 1)
            place = jnp.sum(jnp.where(same, own_pos, 0.0), axis=1, keepdims=True)
            filled = lax.broadcasted_iota(jnp.int32, (PICKS, 1), 0) < picks
            place = jnp.where(filled, place, -1.0).astype(jnp.int32)
            matches = place == lane_q
            marks = jnp.where(matches, 1.0, 0.0)
            predicted = jnp.max(marks, axis=0, keepdims=True)
            rank = jnp.sum(jnp.where(matches, own_rank, 0.0), axis=1, keepdims=True)
            group = jnp.sum(jnp.where(matches, own_tag, 0.0), axis=1, keepdims=True)
            earlier = (upright(predicted) > 0) & (own_rank <= upright(own_rank))
            content = (upright(own_tag) == own_tag) & ((predicted == 0) | earlier)
            query = (group == own_tag) & ((predicted == 0) | (own_rank + 1 <= rank))
            allowed.append((content, query))
            hot.append(marks)
            spread[seq, :L] = jnp.where(lane == L - 1 - level, 1.0, 0.0).astype(LOW)
            spread[seq, L:] = jnp.where(lane_q == L - 1 - place, 1.0, 0.0).astype(LOW)
        hot = jnp.concatenate(hot)
        for head in range(H):
            row = jnp.broadcast_to(by_distance[head : head + 1], (L, 2 * L))
            bias = pltpu.roll(row, L + 1, 1, stride=1, stride_axis=0)[:, :L]
            bias_q = lax.dot_general(
                hot,
                bias,
                (((1,), (0,)), ((), ())),
                precision=lax.Precision.HIGHEST,
                preferred_element_type=WIDE,
            )
            base = head % 2 * ROWS
            for seq in range(SEQS):
                content, query = allowed[seq]
                masks[seq, head // 2, base : base + L] = jnp.where(content, bias, -1e30)
                masks[seq, head // 2, base + L : base + ROWS] = jnp.where(
                    query, bias_q[seq * PICKS : (seq + 1) * PICKS], -1e30
                )

    return pl.pallas_call(
        kernel,
        out_shape=[
            shaped((SEQS,) + MASK_SHAPE, WIDE),
            shaped((SEQS, ROWS, L), LOW),
            shaped((SEQS * PICKS, D), LOW),
            shaped((SEQS * PICKS, D), LOW),
        ],
        in_specs=[VMEM] * 4 + [ANY] * len(after),
        out_specs=[VMEM] * 4,
        compiler_params=limit(8),
        cost_estimate=pl.CostEstimate(flops=int(3e10), bytes_accessed=0, transcendentals=0),
        name="prepare",
    )(ranks, table, query_in, query_cot, *after)


def take_rows(content, picks, seq, target):
    target[:L] = content[seq * L : (seq + 1) * L]
    target[L:] = picks[seq * PICKS : (seq + 1) * PICKS]


def front(seq, info, content, picks, matrices, masks, vec, b_expand, after=()):
    def kernel(info, content, picks, masks, vec, b_expand, *refs):
        w = Names(**dict(zip(MATRICES, refs[:6])))
        out, x, query, key, value, mixed, first_low, total = refs[6 + len(after) :]
        s = Names(
            query=query,
            key=key,
            value=value,
            mixed=mixed,
            first_low=first_low,
            total=total,
            out=out,
        )
        take_rows(content, picks, seq, x)
        forward(x, w, vec, b_expand, masks.at[seq], s, False)

    return pl.pallas_call(
        kernel,
        out_shape=shaped((ROWS, D), LOW),
        in_specs=[SMEM] + [VMEM] * 11 + [ANY] * len(after),
        out_specs=VMEM,
        scratch_shapes=[pltpu.VMEM((ROWS, D), LOW)]
        + [pltpu.VMEM(*KEPT[n]) for n in ("query", "key", "value", "mixed", "first_low")]
        + [pltpu.VMEM((ROWS, D), WIDE)],
        compiler_params=limit(12),
        cost_estimate=cost(5),
        name="front",
    )(info, content, picks, masks, vec, b_expand, *matrices, *after)


def middle_forward(seq, info, content, picks, arrived, matrices, masks, vec, b_expand, after=()):
    def kernel(info, arrived, content, picks, masks, vec, b_expand, *refs):
        w, rest = Names(**dict(zip(MATRICES, refs[:6]))), refs[6 + len(after) :]
        (out, early, pair), kept = rest[:3], rest[3 : 3 + len(SAVED)]
        mixed, total = rest[3 + len(SAVED) :]
        x = pair.at[0]
        s = Names(total=total, out=out, mixed=mixed, **dict(zip(SAVED, kept)))
        take_rows(content, picks, seq, x)
        x[...] = jnp.where(info[2] == 1, x[...], arrived[...])
        early[:, :D] = x[...]
        forward(x, w, vec, b_expand, masks.at[seq], s, True)
        pair[1] = mixed[...]
        early[:, D : 2 * D] = mixed[...]
        early[:, 2 * D : 3 * D] = s.first_low[...]
        early[:, 3 * D :] = columns(s.activated, (1 - info[0]) * HALF, HALF)[...]

    out, early, pair, *saved = pl.pallas_call(
        kernel,
        out_shape=[
            shaped((ROWS, D), WIDE),
            shaped((ROWS, EARLY), LOW),
            shaped((2, ROWS, D), LOW),
        ]
        + [shaped(*KEPT[n]) for n in SAVED],
        in_specs=[SMEM] + [VMEM] * 12 + [ANY] * len(after),
        out_specs=[VMEM] * (3 + len(SAVED)),
        scratch_shapes=[pltpu.VMEM(*KEPT["mixed"]), pltpu.VMEM((ROWS, D), WIDE)],
        compiler_params=limit(16),
        cost_estimate=cost(6),
        name="middle_forward",
    )(info, arrived, content, picks, masks, vec, b_expand, *matrices, *after)
    return (out, early, pair, dict(zip(SAVED, saved)))


FEED_SAVED = ("normed2", "root2", "slope", "normed1", "root1")
ATTEND_SAVED = ("value", "probs", "key", "query")


def middle_back(seq, content, picks, matrices, vec, saved):
    names = FEED_SAVED + ATTEND_SAVED

    def kernel(content, picks, vec, *refs):
        w, rest = Names(**dict(zip(MATRICES, refs[:6]))), refs[6:]
        kept, grad, rest = rest[: len(names)], rest[len(names)], rest[len(names) + 1 :]
        cot, total, branch, expanded, attended, dmixed, dvalue, dquery, dkey = rest
        s = Names(
            total=total,
            branch=branch,
            expanded=expanded,
            attended=attended,
            dmixed=dmixed,
            dvalue=dvalue,
            dquery=dquery,
            dkey=dkey,
            **dict(zip(names, kept)),
        )
        take_rows(content, picks, seq, cot)
        back_second_norm(cot[...], vec, s)
        back_feed(w, vec, s)
        dmixed[...] = nt(attended[...], w.out[...]).astype(LOW)
        back_attend(s)
        lower = total[...] + nt(dquery[...], w.query[...])
        upper = nt(dkey[...], w.key[...]) + nt(dvalue[...], w.value[...])
        grad[:L] = (lower[:L] + upper).astype(LOW)
        grad[L:] = lower[L:].astype(LOW)

    return pl.pallas_call(
        kernel,
        out_shape=shaped((ROWS, D), LOW),
        in_specs=[VMEM] * (9 + len(names)),
        out_specs=VMEM,
        scratch_shapes=[
            pltpu.VMEM((ROWS, D), LOW),
            pltpu.VMEM((ROWS, D), WIDE),
            pltpu.VMEM((ROWS, D), LOW),
            pltpu.VMEM((ROWS, FF), LOW),
            pltpu.VMEM((ROWS, D), LOW),
            pltpu.VMEM((ROWS, D), LOW),
            pltpu.VMEM((L, D), LOW),
            pltpu.VMEM((ROWS, D), LOW),
            pltpu.VMEM((L, D), LOW),
        ],
        compiler_params=limit(12),
        cost_estimate=cost(7),
        name="middle_back",
    )(content, picks, vec, *matrices, *(saved[n] for n in names))


def feed_back(seq, info, arrived, content, picks, small_in, vec, matrices, saved):
    given = [] if small_in is None else [small_in]

    def kernel(info, arrived, content, picks, vec, expand, contract, *refs):
        kept, rest = refs[:5], refs[5 + len(given) :]
        total, branch, attended, small, own, late, upper, expanded = rest
        w = Names(expand=expand, contract=contract)
        s = Names(
            total=total,
            branch=branch,
            attended=attended,
            expanded=expanded,
            **dict(zip(FEED_SAVED, kept)),
        )
        small[...] = refs[5][...] if given else jnp.zeros_like(small)

        def add(place, value):
            small[place : place + 1, :] += value

        take_rows(content, picks, seq, upper)
        back_second_norm(jnp.where(info[2] == 1, arrived[...], upper[...]), vec, s, add)
        late[:, :D] = branch[...]
        back_feed(w, vec, s, add)
        own[...] = columns(expanded, info[0] * HALF, HALF)[...]
        late[:, D:] = columns(expanded, (1 - info[0]) * HALF, HALF)[...]

    return pl.pallas_call(
        kernel,
        out_shape=[
            shaped((ROWS, D), WIDE),
            shaped((ROWS, D), LOW),
            shaped((ROWS, D), LOW),
            shaped((SMALL, D), WIDE),
            shaped((ROWS, HALF), LOW),
            shaped((ROWS, LATE), LOW),
        ],
        in_specs=[SMEM] + [VMEM] * (11 + len(given)),
        out_specs=[VMEM] * 6,
        scratch_shapes=[pltpu.VMEM((ROWS, D), LOW), pltpu.VMEM((ROWS, FF), LOW)],
        compiler_params=limit(12),
        cost_estimate=cost(4),
        name="feed_back",
    )(
        info,
        arrived,
        content,
        picks,
        vec,
        matrices[4],
        matrices[5],
        *(saved[n] for n in FEED_SAVED),
        *given,
    )


PLACES = {
    (2, 0): (0, 0),
    (1, 1): (0, 1),
    (2, 1): (1, 0),
    (3, 0): (1, 1),
    (1, 0): (2, 0),
    (3, 1): (3, 0),
    (0, 0): (4, 0),
    (0, 1): (4, 1),
}


def term_shapes(count):
    return [shaped((n * count, D), LOW) for n in (2, 2, 1, 1, 2)]


def feed_grads(info, mine, branch, own, early, late):
    def kernel(info, *refs):
        acts, lows, branches, owns, earlies, lates = (refs[2 * i : 2 * i + 2] for i in range(6))
        outs, (a_act, a_first, b_branch, b_own, stage, sems, out_sems) = refs[12:17], refs[17:]
        core, place = info[0], info[1]
        own_at = [slice(seq * ROWS, (seq + 1) * ROWS) for seq in range(SEQS)]
        far_at = [slice((2 + seq) * ROWS, (3 + seq) * ROWS) for seq in range(SEQS)]
        pairs, later = [], []
        for seq in range(SEQS):
            pairs += [
                (columns(acts[seq], core * HALF, HALF), a_act.at[own_at[seq]]),
                (earlies[seq].at[:, 3 * D :], a_act.at[far_at[seq]]),
                (branches[seq], b_branch.at[own_at[seq]]),
                (lates[seq].at[:, :D], b_branch.at[far_at[seq]]),
            ]
            later += [
                (lows[seq], a_first.at[own_at[seq]]),
                (earlies[seq].at[:, 2 * D : 3 * D], a_first.at[far_at[seq]]),
                (owns[seq], b_own.at[own_at[seq]]),
                (lates[seq].at[:, D:], b_own.at[far_at[seq]]),
            ]
        copies = start_all(pairs + later, sems)
        sent = []

        def send(block):
            for k in range(4):
                quarter = lax.rem(place + k, 4)
                index, part = PLACES[k, block // 2]
                start = (2 * part + block % 2) * QUARTER
                sent.extend(
                    start_all(
                        [
                            (
                                rows_at(stage.at[block], quarter * QUARTER, QUARTER),
                                outs[index].at[start : start + QUARTER],
                            )
                        ],
                        out_sems,
                        block * 4 + k,
                    )
                )

        wait_all(copies[:8])
        for block in range(2):
            for part in range(3):
                start = block * D + part * 256
                stage[block, part * 256 : (part + 1) * 256] = tn(
                    a_act[:, start : start + 256], b_branch[...]
                ).astype(LOW)
            send(block)
        wait_all(copies[8:])
        for block in range(2):
            for part in range(3):
                stage[2 + block, part * 256 : (part + 1) * 256] = tn(
                    a_first[:, part * 256 : (part + 1) * 256], b_own[:, block * D : (block + 1) * D]
                ).astype(LOW)
            send(2 + block)
        wait_all(sent)

    acts = [saved["activated"] for saved in mine]
    lows = [saved["first_low"] for saved in mine]
    return pl.pallas_call(
        kernel,
        out_shape=term_shapes(2 * QUARTER),
        in_specs=[SMEM] + [ANY] * 12,
        out_specs=[ANY] * 5,
        scratch_shapes=[
            pltpu.VMEM((2 * ALL_ROWS, HALF), LOW),
            pltpu.VMEM((2 * ALL_ROWS, D), LOW),
            pltpu.VMEM((2 * ALL_ROWS, D), LOW),
            pltpu.VMEM((2 * ALL_ROWS, HALF), LOW),
            pltpu.VMEM((4, D, D), LOW),
            DMA((16,)),
            DMA((16,)),
        ],
        compiler_params=limit(16),
        cost_estimate=cost(8),
        name="feed_grads",
    )(info, *acts, *lows, *branch, *own, *early, *late)


def attend_back(info, total, attended, small_in, spread, output, after, matrices, saved, picks):
    names = ("out", "query", "key", "value")
    sources = [matrices[3]] + list(matrices[:3])
    kept_in = [saved[seq][n] for seq in range(SEQS) for n in ATTEND_SAVED]

    def kernel(info, small_in, spread, *refs):
        totals, attendeds, outputs = refs[0:2], refs[2:4], refs[4:6]
        w, kept, rest = Names(**dict(zip(names, refs[6:10]))), refs[10:18], refs[18 + len(after) :]
        content_ends, query_ends, small, own, send, dmixed, pieces, table, sums = rest
        at = [slice(seq * ROWS, (seq + 1) * ROWS) for seq in range(SEQS)]
        lower_at = [
            slice(ALL_ROWS + seq * L, ALL_ROWS + (seq + 1) * L) for seq in range(SEQS)
        ]
        for seq in range(SEQS):
            pieces[1, at[seq]] = attendeds[seq][...]
        dmixed[...] = nt(pieces[1, :ALL_ROWS], w.out[...]).astype(LOW)
        for seq in range(SEQS):
            s = Names(
                dmixed=dmixed.at[at[seq]],
                dquery=pieces.at[0, at[seq]],
                dkey=pieces.at[0, lower_at[seq]],
                dvalue=pieces.at[1, lower_at[seq]],
                **dict(zip(ATTEND_SAVED, kept[4 * seq : 4 * seq + 4])),
            )

            def table_sum(pair, dscores, seq=seq):
                for odd in range(2):
                    part = tn(spread[seq], dscores[odd * ROWS : (odd + 1) * ROWS])
                    if seq == 0:
                        table[2 * pair + odd] = part
                    else:
                        table[2 * pair + odd] += part

            back_attend(s, table_sum)
        own[...] = pieces[info[0]]
        send[...] = pieces[1 - info[0]]
        lower = nt(pieces[0, :ALL_ROWS], w.query[...])
        upper = nt(pieces[0, ALL_ROWS:], w.key[...]) + nt(pieces[1, ALL_ROWS:], w.value[...])
        first = info[2] == 1
        for seq in range(SEQS):
            base = seq * ROWS
            content_ends[seq * L : (seq + 1) * L] = jnp.where(
                first,
                totals[seq][:L] + lower[base : base + L] + upper[seq * L : (seq + 1) * L],
                outputs[seq][:L],
            )
            query_ends[seq * picks : (seq + 1) * picks] = jnp.where(
                first,
                totals[seq][L : L + picks] + lower[base + L : base + L + picks],
                outputs[seq][L : L + picks],
            )
        small[...] = small_in[...]
        small[S_QUERY : S_QUERY + 1, :] = column_sum(pieces[0, :ALL_ROWS])
        small[S_VALUE : S_VALUE + 1, :] = column_sum(pieces[1, ALL_ROWS:])
        sums[...] = jnp.zeros_like(sums)
        for head in range(H):
            both = jnp.concatenate([table[head], jnp.zeros((L, L), WIDE)], axis=1)
            turned = pltpu.roll(both, 0, 1, stride=1, stride_axis=0)
            sums[head : head + 1, :] = jnp.sum(turned, axis=0, keepdims=True)
        distance = lax.broadcasted_iota(jnp.int32, (2 * L, L), 0) - (L - 1)
        bucket = lax.broadcasted_iota(jnp.int32, (2 * L, L), 1)
        small[S_TABLE : S_TABLE + 16, :L] = lax.dot_general(
            sums[...],
            (bucket_of(distance) == bucket).astype(WIDE),
            (((1,), (0,)), ((), ())),
            precision=lax.Precision.HIGHEST,
            preferred_element_type=WIDE,
        )

    return pl.pallas_call(
        kernel,
        out_shape=[
            shaped((ALL_CONTENT, D), WIDE),
            shaped((SEQS * picks, D), WIDE),
            shaped((SMALL, D), WIDE),
            shaped((PIECE, D), LOW),
            shaped((PIECE, D), LOW),
        ],
        in_specs=[SMEM] + [VMEM] * 20 + [ANY] * len(after),
        out_specs=[VMEM] * 5,
        scratch_shapes=[
            pltpu.VMEM((ALL_ROWS, D), LOW),
            pltpu.VMEM((2, PIECE, D), LOW),
            pltpu.VMEM((H, L, L), WIDE),
            pltpu.VMEM((16, 2 * L), WIDE),
        ],
        compiler_params=limit(16),
        cost_estimate=cost(10),
        name="attend_back",
    )(info, small_in, spread, *total, *attended, *output, *sources, *kept_in, *after)


def attend_grads(info, pair, early, own, arrived, small, after=()):
    def kernel(info, small, own, arrived, *refs):
        pairs_in, earlies, refs = refs[0:2], refs[2:4], refs[4 + len(after) :]
        outs, rest = refs[:5], refs[5:]
        a_rows, a_content, b_rows, b_content, stage, extra, sems, out_sems = rest
        core, place = info[0], info[1]
        pairs = [
            (own.at[:ALL_ROWS], b_rows.at[:ALL_ROWS]),
            (arrived.at[:ALL_ROWS], b_rows.at[ALL_ROWS:]),
        ]
        later = [
            (own.at[ALL_ROWS:], b_content.at[:ALL_CONTENT]),
            (arrived.at[ALL_ROWS:], b_content.at[ALL_CONTENT:]),
        ]
        for seq in range(SEQS):
            at, far = seq * ROWS, (2 + seq) * ROWS
            pairs += [
                (pairs_in[seq].at[core], a_rows.at[at : at + ROWS]),
                (columns(earlies[seq], core * D, D), a_rows.at[far : far + ROWS]),
            ]
            at, far = seq * L, (2 + seq) * L
            later += [
                (pairs_in[seq].at[0, :L], a_content.at[at : at + L]),
                (earlies[seq].at[:L, :D], a_content.at[far : far + L]),
            ]
        copies = start_all(pairs + later, sems)
        extra[0] = small[...].astype(LOW)
        extra[1] = jnp.zeros((EXTRA, D), LOW)
        sent = []
        for block, (former, latter) in enumerate(((a_rows, b_rows), (a_content, b_content))):
            wait_all(copies[6 * block : 6 * block + 6])
            for part in range(3):
                stage[block, part * 256 : (part + 1) * 256] = tn(
                    former[:, part * 256 : (part + 1) * 256], latter[...]
                ).astype(LOW)
            for k in range(4):
                quarter = lax.rem(place + k, 4)
                index, part = PLACES[k, block]
                start = part * (QUARTER + EXTRA)
                middle, stop = start + QUARTER, start + QUARTER + EXTRA
                sent += start_all(
                    [
                        (
                            rows_at(stage.at[block], quarter * QUARTER, QUARTER),
                            outs[index].at[start:middle],
                        ),
                        (extra.at[block], outs[index].at[middle:stop]),
                    ],
                    out_sems,
                    block * 8 + 2 * k,
                )
        wait_all(sent)

    return pl.pallas_call(
        kernel,
        out_shape=term_shapes(QUARTER + EXTRA),
        in_specs=[SMEM, VMEM] + [ANY] * (6 + len(after)),
        out_specs=[ANY] * 5,
        scratch_shapes=[
            pltpu.VMEM((2 * ALL_ROWS, D), LOW),
            pltpu.VMEM((2 * ALL_CONTENT, D), LOW),
            pltpu.VMEM((2 * ALL_ROWS, D), LOW),
            pltpu.VMEM((2 * ALL_CONTENT, D), LOW),
            pltpu.VMEM((2, D, D), LOW),
            pltpu.VMEM((2, EXTRA, D), LOW),
            DMA((12,)),
            DMA((16,)),
        ],
        compiler_params=limit(12),
        cost_estimate=cost(5),
        name="attend_grads",
    )(info, small, own, arrived, *pair, *early, *after)


def feed_targets(outs, source, half, core, quarter):
    pairs = []
    for block in range(2):
        part = source.at[block * QUARTER : (block + 1) * QUARTER]
        if half == 0:
            target = rows_at(outs[0], core * HALF + block * D + quarter * QUARTER, QUARTER)
        else:
            target = columns(
                rows_at(outs[1], quarter * QUARTER, QUARTER), (core * 2 + block) * D, D
            )
        pairs.append((None, part, target))
    return pairs


def attend_targets(outs, source, half, core, quarter):
    return [
        (
            core == number,
            source.at[:QUARTER],
            rows_at(outs[2 * number + half], quarter * QUARTER, QUARTER),
        )
        for number in range(2)
    ]


def settle(targets, shapes, count, info, pieces, outs, through, name):
    keys = tuple(pieces)
    arrays = [pieces[key] for key in keys]
    given = list(outs or ()) + list(through)
    first_alias = len(shapes) - len(outs or ())

    def kernel(info, *refs):
        parts, rest = refs[: len(keys)], refs[len(keys) + len(given) :]
        outs, rest = rest[: len(shapes)], rest[len(shapes) + len(through) :]
        held, wide_held, (sems, out_sems) = rest[: len(keys)], rest[len(keys) : -2], rest[-2:]
        copies = start_all(list(zip(parts, held)), sems)
        finish = []
        for index, (sibling, k, which) in enumerate(keys):
            core = 1 - info[0] if sibling else info[0]
            quarter = lax.rem((info[3] if sibling else info[1]) + k, 4)
            copies[index].wait()
            wide_held[index][...] = held[index][...].astype(WIDE)
            for number, half in enumerate(which):
                source = wide_held[index].at[number * count : (number + 1) * count]
                for place, (condition, part, target) in enumerate(
                    targets(outs, source, half, core, quarter)
                ):
                    copy = pltpu.make_async_copy(
                        part, target, out_sems.at[4 * index + 2 * number + place]
                    )
                    if condition is None:
                        copy.start()
                        finish.append(copy.wait)
                    else:
                        pl.when(condition)(copy.start)
                        finish.append(lambda c=copy, when=condition: pl.when(when)(c.wait))
        for action in finish:
            action()

    result = pl.pallas_call(
        kernel,
        out_shape=[shaped(shape, WIDE) for shape in shapes]
        + [shaped(array.shape, array.dtype) for array in through],
        in_specs=[SMEM] + [ANY] * (len(keys) + len(given)),
        out_specs=[ANY] * (len(shapes) + len(through)),
        scratch_shapes=[pltpu.VMEM(array.shape, LOW) for array in arrays]
        + [pltpu.VMEM(array.shape, WIDE) for array in arrays]
        + [DMA((len(keys),)), DMA((4 * len(keys),))],
        input_output_aliases={1 + len(keys) + i: first_alias + i for i in range(len(given))},
        compiler_params=limit(32),
        cost_estimate=cost(sum(array.size for array in arrays) * 2e-6 + 1),
        name=name,
    )(info, *arrays, *given)
    return result[: len(shapes)], result[len(shapes) :]


PLANE = ("x", "y", "c")


def shift(value, axis, by):
    size = lax.axis_size(axis)
    return lax.ppermute(value, axis, [(i, (i + by) % size) for i in range(size)])


def send(value, by):
    return lax.ppermute(value, "s", [(0, 1)] if by > 0 else [(1, 0)])


def turn(value, outer, by):
    pairs = []
    for i in range(4):
        for j in range(4):
            for c in range(2):
                if (c == 0) == outer:
                    target = ((i + by) % 4, j)
                else:
                    target = (i, (j + by) % 4)
                pairs.append(((i * 4 + j) * 2 + c, (target[0] * 4 + target[1]) * 2 + c))
    return lax.ppermute(value, PLANE, pairs)


def place(outer):
    return jnp.where(
        (lax.axis_index("c") == 0) == outer, lax.axis_index("x"), lax.axis_index("y")
    )


def wide(value):
    return value.astype(WIDE)


def pick(parts, index):
    return lax.dynamic_index_in_dim(parts, index, 0, keepdims=False)


def total_wide(*terms):
    return sum(wide(term) for term in terms)


def total_of(*terms):
    return total_wide(*terms).astype(LOW)


def chain_start(terms):
    plus, minus, after0, before1, own = terms
    count = after0.shape[0]
    from_left = turn(plus, True, 1)
    from_right = turn(minus, True, -1)
    to_right = total_of(after0, from_left[:count])
    to_left = total_of(before1, from_right[:count])
    return (to_right, to_left, from_left, from_right, own)


def chain_reduce(terms):
    to_right, to_left, from_left, from_right, own = terms
    count = to_right.shape[0]
    left = turn(to_right, True, 1)
    right = turn(to_left, True, -1)
    sums = [
        total_of(own[:count], left, from_right[count:]),
        total_of(own[count:], from_left[count:], right),
    ]
    parts = jnp.concatenate([part.reshape(4, count // 4, D) for part in sums], axis=1)
    me = place(False)
    arrived = [turn(pick(parts, (me + by) % 4), False, by) for by in (1, 2, -1)]
    part = total_of(pick(parts, me), *arrived)
    return total_of(part, shift(part, "z", 1))


def gather_inner(part):
    count = part.shape[0] // 2
    me = place(False)
    whole = jnp.zeros((2, 4, count, D), LOW)
    for k, piece in enumerate([part] + [turn(part, False, -by) for by in (1, 2, -1)]):
        whole = lax.dynamic_update_slice(
            whole, piece.reshape(2, 1, count, D), (0, (me + k) % 4, 0, 0)
        )
    return whole.reshape(8 * count, D)


def gather_outer(own):
    before = turn(own, True, 1)
    after = turn(own, True, -1)
    near = {(0, (0, 1)): own, (3, (0, 1)): before, (1, (0, 1)): after}
    both = {(0,) + key: piece for key, piece in near.items()}
    return both | {(1,) + key: shift(piece, "c", 1) for key, piece in near.items()}


def gather_across(pieces):
    before, after = pieces[0, 3, (0, 1)], pieces[0, 1, (0, 1)]
    count = before.shape[0] // 2
    far = {(2, (0,)): turn(before[:count], True, 1), (2, (1,)): turn(after[count:], True, -1)}
    both = {(0,) + key: piece for key, piece in far.items()}
    return both | {(1,) + key: shift(piece, "c", 1) for key, piece in far.items()}


def on_device(
    content_in,
    query_in,
    content_cot,
    query_cot,
    order_rank,
    query_pos,
    group_tag,
    *rest,
):
    (
        w_query,
        b_query,
        w_key,
        w_value,
        b_value,
        w_out,
        b_out,
        norm1_gain,
        norm1_bias,
        w_expand,
        b_expand,
        w_contract,
        b_contract,
        norm2_gain,
        norm2_bias,
    ) = (argument[0] for argument in rest[:-1])
    rel_table = rest[-1]
    core = lax.axis_index("c")
    first_section = (lax.axis_index("s") == 0).astype(jnp.int32)
    info = jnp.stack([core, place(True), first_section, place(False)])
    picks = query_pos.shape[1]

    matrices = (w_query, w_key, w_value, w_out, w_expand, w_contract)
    vec = jnp.stack(
        [b_query, b_value, b_out, norm1_gain, norm1_bias, b_contract, norm2_gain, norm2_bias]
    )
    ranks = jnp.concatenate([order_rank, group_tag, query_pos], axis=1)
    masks, spread, query_in, query_cot = prepare(
        ranks, rel_table, query_in, query_cot, picks, (vec, info)
    )
    b_expand = b_expand[None]

    fronts, arrived = [], []
    for seq in range(SEQS):
        fronts.append(
            front(seq, info, content_in, query_in, matrices, masks, vec, b_expand, tuple(fronts))
        )
        arrived.append(send(fronts[seq], 1))
    output, early, pair, saved, grads = [], [], [], [], []
    for seq in range(SEQS):
        results = middle_forward(
            seq, info, content_in, query_in, arrived[seq], matrices, masks, vec, b_expand, tuple(grads)
        )
        for collected, result in zip((output, early, pair, saved), results):
            collected.append(result)
        grads.append(middle_back(seq, content_cot, query_cot, matrices, vec, saved[seq]))
    early = [shift(value, "c", 1) for value in early]
    grads = [send(value, -1) for value in grads]
    small = None
    total, branch, attended, own, late = [], [], [], [], []
    for seq in range(SEQS):
        results = feed_back(
            seq, info, grads[seq], content_cot, query_cot, small, vec, matrices, saved[seq]
        )
        small = results[3]
        for collected, result in zip(
            (total, branch, attended, own, late), results[:3] + results[4:]
        ):
            collected.append(result)
    late = [shift(value, "c", 1) for value in late]
    terms = feed_grads(info, saved, branch, own, early, late)
    feed_terms = chain_start(terms)
    content_ends, query_ends, small, own, pass_on = attend_back(
        info, total, attended, small, spread, output, (terms[4],), matrices, saved, picks
    )
    passed = shift(pass_on, "c", 1)
    feed_part = chain_reduce(feed_terms)
    attend_terms = attend_grads(info, pair, early, own, passed, small, feed_terms[:2])
    attend_part = chain_reduce(chain_start(attend_terms))
    feed_own = gather_inner(feed_part)
    feed_near = gather_outer(feed_own)
    attend_own = gather_inner(attend_part)
    feed_shapes, attend_shapes = ((FF, D), (D, FF)), ((D, D),) * 4
    attend_near = gather_outer(attend_own)
    feed_outs, through = settle(
        feed_targets,
        feed_shapes,
        2 * QUARTER,
        info,
        feed_near,
        None,
        tuple(attend_near[0, k, (0, 1)] for k in (1, 3)),
        "feed_out",
    )
    attend_near[0, 1, (0, 1)], attend_near[0, 3, (0, 1)] = through
    feed_outs, _ = settle(
        feed_targets,
        feed_shapes,
        2 * QUARTER,
        info,
        gather_across(feed_near),
        feed_outs,
        (),
        "feed_out_last",
    )
    attend_outs, _ = settle(
        attend_targets,
        attend_shapes,
        QUARTER + EXTRA,
        info,
        attend_near,
        None,
        (),
        "attend_out",
    )
    attend_outs, _ = settle(
        attend_targets,
        attend_shapes,
        QUARTER + EXTRA,
        info,
        gather_across(attend_near),
        attend_outs,
        (),
        "attend_out_last",
    )
    contract, expand = feed_outs
    g_query, g_key, g_out, g_value = attend_outs
    small_sum = total_wide(
        *(attend_near[far, 0, (0, 1)][QUARTER : QUARTER + SMALL] for far in (0, 1))
    )
    table = small_sum[S_TABLE : S_TABLE + H, :L]
    table_total = (table + shift(table, "s", 1))[:, :NB].T
    row = lambda k: small_sum[k][None]
    return (
        content_ends[None],
        query_ends[None],
        g_query[None],
        row(S_QUERY),
        g_key[None],
        g_value[None],
        row(S_VALUE),
        g_out[None],
        row(S_OUT),
        row(S_GAIN1),
        row(S_SHIFT1),
        expand[None],
        small_sum[S_EXPAND : S_EXPAND + 4].reshape(1, FF),
        contract[None],
        row(S_CONTRACT),
        row(S_GAIN2),
        row(S_SHIFT2),
        table_total,
    )


DP = ("z", "x", "y", "c")


def solution(mesh):
    mesh = jax.sharding.Mesh(mesh.devices.reshape(2, 2, 4, 4, 2), ("s",) + DP)
    layer_specs = tuple(
        P("s", *([None] * (rank - 1))) for rank in (3, 2, 3, 3, 2, 3, 2, 2, 2, 3, 2, 3, 2, 2, 2)
    )
    in_specs = (P(DP, None),) * 7 + layer_specs + (P(),)
    out_specs = (P("s", DP, None),) * 2 + layer_specs + (P(),)
    return jax.shard_map(
        on_device, mesh=mesh, in_specs=in_specs, out_specs=out_specs, check_vma=False
    )
```

```python
import jax
import jax.numpy as jnp
from jax import lax
from jax.experimental import pallas as pl
from jax.experimental.pallas import tpu as pltpu
from jax.sharding import PartitionSpec as P

D = 768
H = 12
HD = 64
FF = 3072
NB = 32
L = 128
PAIRS = H // 2
SEQS = 2
PICKS = 32
ROWS = L + PICKS
EPSILON = 1e-05
SCALE = HD ** (-0.5)
TILE = 1536
LOW = jnp.bfloat16
WIDE = jnp.float32
HALF = FF // 2
QUARTER = D // 4
EARLY = 3 * D + HALF
LATE = D + HALF
EXTRA = 64
SMALL = 32
ALL_ROWS = SEQS * ROWS
ALL_CONTENT = SEQS * L
PIECE = ALL_ROWS + ALL_CONTENT


def nn(former, latter):
    return lax.dot_general(
        former, latter, (((1,), (0,)), ((), ())), preferred_element_type=WIDE
    )


def nt(former, latter):
    return lax.dot_general(
        former, latter, (((1,), (1,)), ((), ())), preferred_element_type=WIDE
    )


def tn(former, latter):
    return lax.dot_general(
        former, latter, (((0,), (0,)), ((), ())), preferred_element_type=WIDE
    )


def halves(value):
    even = lax.broadcasted_iota(jnp.int32, value.shape, 1) < HD
    zero = jnp.zeros_like(value)
    return jnp.concatenate([jnp.where(even, value, zero), jnp.where(even, zero, value)])


def side(value):
    count = value.shape[0] // 2
    return jnp.concatenate([value[:count], value[count:]], axis=1)


def norm_rows(values):
    centered = values - jnp.mean(values, axis=-1, keepdims=True)
    variance = jnp.mean(centered * centered, axis=-1, keepdims=True)
    root = lax.rsqrt(variance + EPSILON)
    return (centered * root, root)


def norm_rows_back(scaled, normed, root):
    return root * (
        scaled
        - jnp.mean(scaled, axis=-1, keepdims=True)
        - normed * jnp.mean(scaled * normed, axis=-1, keepdims=True)
    )


B_QUERY, B_VALUE, B_OUT, GAIN1, SHIFT1, B_CONTRACT, GAIN2, SHIFT2 = range(8)
S_QUERY, S_VALUE, S_OUT, S_GAIN1, S_SHIFT1, S_EXPAND = range(6)
S_CONTRACT, S_GAIN2, S_SHIFT2, S_TABLE = 9, 10, 11, 16
LIMITS = (12, 16, 23, 32, 46, 64, 91)


def bucket_of(relative):
    distance = jnp.abs(relative)
    beyond = 8 + sum((distance >= limit).astype(jnp.int32) for limit in LIMITS)
    within = jnp.where(distance < 8, distance, beyond)
    return within + 16 * (relative > 0).astype(jnp.int32)


def forward(x, w, vec, b_expand, masks, s, keep):
    row = lambda k: vec[k : k + 1, :]
    s.query[...] = (nn(x[...], w.query[...]) + row(B_QUERY)).astype(LOW)
    s.key[...] = nn(x[:L], w.key[...]).astype(LOW)
    s.value[...] = (nn(x[:L], w.value[...]) + row(B_VALUE)).astype(LOW)
    for pair in range(PAIRS):
        lanes = slice(pair * 128, (pair + 1) * 128)
        scores = nt(halves(s.query[:, lanes]), s.key[:, lanes]) * SCALE + masks[pair]
        shifted = jnp.exp(scores - jnp.max(scores, axis=-1, keepdims=True))
        probs = (shifted / jnp.sum(shifted, axis=-1, keepdims=True)).astype(LOW)
        if keep:
            s.probs[pair] = probs
        s.mixed[:, lanes] = nn(side(probs), halves(s.value[:, lanes])).astype(LOW)
    total = x[...].astype(WIDE) + nn(s.mixed[...], w.out[...]) + row(B_OUT)
    normed, root = norm_rows(total)
    first = normed * row(GAIN1) + row(SHIFT1)
    s.first_low[...] = first.astype(LOW)
    s.total[...] = first + row(B_CONTRACT)
    if keep:
        s.normed1[...] = normed
        s.root1[...] = jnp.broadcast_to(root, (ROWS, 128))
    for tile in range(FF // TILE):
        tile = slice(tile * TILE, (tile + 1) * TILE)
        expanded = nn(s.first_low[...], w.expand[:, tile]) + b_expand[:, tile]
        cumulative = 0.5 * (1.0 + lax.erf(expanded * 0.7071067811865476))
        activated = (expanded * cumulative).astype(LOW)
        if keep:
            s.slope[:, tile] = (
                cumulative + expanded * jnp.exp(-0.5 * expanded * expanded) * 0.3989422804014327
            ).astype(LOW)
            s.activated[:, tile] = activated
        s.total[...] += nn(activated, w.contract[tile, :])
    normed, root = norm_rows(s.total[...])
    if keep:
        s.normed2[...] = normed
        s.root2[...] = jnp.broadcast_to(root, (ROWS, 128))
    s.out[...] = (normed * row(GAIN2) + row(SHIFT2)).astype(s.out.dtype)


def column_sum(value):
    return jnp.sum(value.astype(WIDE), axis=0, keepdims=True)


def back_second_norm(grad, vec, s, add=None):
    upper = grad.astype(WIDE)
    normed = s.normed2[...]
    lower = norm_rows_back(upper * vec[GAIN2 : GAIN2 + 1, :], normed, s.root2[:, :1])
    s.total[...] = lower
    s.branch[...] = lower.astype(LOW)
    if add is not None:
        add(S_GAIN2, column_sum(upper * normed))
        add(S_SHIFT2, column_sum(upper))
        add(S_CONTRACT, column_sum(lower.astype(LOW)))


def back_feed(w, vec, s, add=None):
    for tile in range(FF // TILE):
        tile = slice(tile * TILE, (tile + 1) * TILE)
        lower = (nt(s.branch[...], w.contract[tile, :]) * s.slope[:, tile].astype(WIDE)).astype(LOW)
        s.expanded[:, tile] = lower
        if add is not None:
            part = column_sum(lower)
            for column in range(TILE // D):
                add(
                    S_EXPAND + tile.start // D + column,
                    part[:, column * D : (column + 1) * D],
                )
        s.total[...] += nt(lower, w.expand[:, tile])
    upper = s.total[...]
    normed = s.normed1[...]
    lower = norm_rows_back(upper * vec[GAIN1 : GAIN1 + 1, :], normed, s.root1[:, :1])
    s.total[...] = lower
    s.attended[...] = lower.astype(LOW)
    if add is not None:
        add(S_GAIN1, column_sum(upper * normed))
        add(S_SHIFT1, column_sum(upper))
        add(S_OUT, column_sum(lower.astype(LOW)))


def back_attend(s, table=None):
    for pair in range(PAIRS):
        lanes = slice(pair * 128, (pair + 1) * 128)
        probs = s.probs[pair]
        below = halves(s.dmixed[:, lanes])
        dprobs = nt(below, s.value[:, lanes])
        s.dvalue[:, lanes] = tn(probs, below).astype(LOW)
        weight = probs.astype(WIDE)
        dscores = (
            weight * (dprobs - jnp.sum(weight * dprobs, axis=-1, keepdims=True))
        ).astype(LOW)
        s.dquery[:, lanes] = (nn(side(dscores), halves(s.key[:, lanes])) * SCALE).astype(LOW)
        s.dkey[:, lanes] = (tn(dscores, halves(s.query[:, lanes])) * SCALE).astype(LOW)
        if table is not None:
            table(pair, dscores)


class Names:
    def __init__(self, **named):
        self.__dict__.update(named)


MATRICES = ("query", "key", "value", "out", "expand", "contract")
MATRIX_SHAPES = {
    "query": (D, D),
    "key": (D, D),
    "value": (D, D),
    "out": (D, D),
    "expand": (D, FF),
    "contract": (FF, D),
}
MASK_SHAPE = (PAIRS, 2 * ROWS, L)
KEPT = {
    "query": ((ROWS, D), LOW),
    "key": ((L, D), LOW),
    "value": ((L, D), LOW),
    "probs": (MASK_SHAPE, LOW),
    "mixed": ((ROWS, D), LOW),
    "normed1": ((ROWS, D), WIDE),
    "root1": ((ROWS, 128), WIDE),
    "first_low": ((ROWS, D), LOW),
    "slope": ((ROWS, FF), LOW),
    "activated": ((ROWS, FF), LOW),
    "normed2": ((ROWS, D), WIDE),
    "root2": ((ROWS, 128), WIDE),
}
SAVED = tuple(name for name in KEPT if name != "mixed")
ANY = pl.BlockSpec(memory_space=pl.ANY)
VMEM = pl.BlockSpec(memory_space=pltpu.VMEM)
SMEM = pl.BlockSpec(memory_space=pltpu.SMEM)


def limit(megabytes):
    return pltpu.CompilerParams(vmem_limit_bytes=megabytes * 1024 * 1024)


DMA = pltpu.SemaphoreType.DMA


def cost(microseconds):
    return pl.CostEstimate(flops=0, bytes_accessed=int(microseconds * 3.2e6), transcendentals=0)


def shaped(shape, kind):
    return jax.ShapeDtypeStruct(shape, kind)


TOKEN = shaped((8, 128), WIDE)


def columns(ref, start, size):
    return ref.at[:, pl.ds(pl.multiple_of(start, 128), size)]


def rows_at(ref, start, size):
    return ref.at[pl.ds(pl.multiple_of(start, 64), size)]


def start_all(pairs, sems, base=0):
    copies = [
        pltpu.make_async_copy(source, target, sems.at[base + index])
        for index, (source, target) in enumerate(pairs)
    ]
    for copy in copies:
        copy.start()
    return copies


def wait_all(copies):
    for copy in copies:
        copy.wait()


def fetcher(names, sources, targets, sems, base=0):
    copies = dict(zip(names, start_all(list(zip(sources, targets)), sems, base)))
    return lambda name: copies[name].wait()


def prepare(ranks, table, query_in, query_cot, picks, after):
    def kernel(ranks, table, query_in, query_cot, *refs):
        masks, spread, rows_in, rows_cot = refs[len(after) :]
        order, tag, pos = ranks[:, :L], ranks[:, L : 2 * L], ranks[:, 2 * L : 2 * L + picks]
        for source, target in ((query_in, rows_in), (query_cot, rows_cot)):
            values = source[...].astype(WIDE)
            blank = jnp.zeros((PICKS - picks, D), WIDE)
            target[...] = jnp.concatenate(
                [values[:picks], blank, values[picks:], blank]
            ).astype(LOW)
        lane = lax.broadcasted_iota(jnp.int32, (L, L), 1)
        level = lax.broadcasted_iota(jnp.int32, (L, L), 0)
        lane_q = lax.broadcasted_iota(jnp.int32, (PICKS, L), 1)
        upright = lambda row: jnp.sum(jnp.where(lane == level, row, 0.0), axis=1, keepdims=True)
        distance = lax.broadcasted_iota(jnp.int32, (2 * L, NB), 0) - (L - 1)
        bucket = lax.broadcasted_iota(jnp.int32, (2 * L, NB), 1)
        by_distance = lax.dot_general(
            table[...],
            (bucket_of(distance) == bucket).astype(WIDE),
            (((0,), (1,)), ((), ())),
            precision=lax.Precision.HIGHEST,
            preferred_element_type=WIDE,
        )
        allowed, hot = [], []
        for seq in range(SEQS):
            own_rank = order[seq : seq + 1, :].astype(WIDE)
            own_tag = tag[seq : seq + 1, :].astype(WIDE)
            own_pos = pos[seq : seq + 1, :].astype(WIDE)
            number = lax.broadcasted_iota(jnp.int32, (PICKS, picks), 0)
            same = number == lax.broadcasted_iota(jnp.int32, (PICKS, picks), 1)
            place = jnp.sum(jnp.where(same, own_pos, 0.0), axis=1, keepdims=True)
            filled = lax.broadcasted_iota(jnp.int32, (PICKS, 1), 0) < picks
            place = jnp.where(filled, place, -1.0).astype(jnp.int32)
            matches = place == lane_q
            marks = jnp.where(matches, 1.0, 0.0)
            predicted = jnp.max(marks, axis=0, keepdims=True)
            rank = jnp.sum(jnp.where(matches, own_rank, 0.0), axis=1, keepdims=True)
            group = jnp.sum(jnp.where(matches, own_tag, 0.0), axis=1, keepdims=True)
            earlier = (upright(predicted) > 0) & (own_rank <= upright(own_rank))
            content = (upright(own_tag) == own_tag) & ((predicted == 0) | earlier)
            query = (group == own_tag) & ((predicted == 0) | (own_rank + 1 <= rank))
            allowed.append((content, query))
            hot.append(marks)
            spread[seq, :L] = jnp.where(lane == L - 1 - level, 1.0, 0.0).astype(LOW)
            spread[seq, L:] = jnp.where(lane_q == L - 1 - place, 1.0, 0.0).astype(LOW)
        hot = jnp.concatenate(hot)
        for head in range(H):
            row = jnp.broadcast_to(by_distance[head : head + 1], (L, 2 * L))
            bias = pltpu.roll(row, L + 1, 1, stride=1, stride_axis=0)[:, :L]
            bias_q = lax.dot_general(
                hot,
                bias,
                (((1,), (0,)), ((), ())),
                precision=lax.Precision.HIGHEST,
                preferred_element_type=WIDE,
            )
            base = head % 2 * ROWS
            for seq in range(SEQS):
                content, query = allowed[seq]
                masks[seq, head // 2, base : base + L] = jnp.where(content, bias, -1e30)
                masks[seq, head // 2, base + L : base + ROWS] = jnp.where(
                    query, bias_q[seq * PICKS : (seq + 1) * PICKS], -1e30
                )

    return pl.pallas_call(
        kernel,
        out_shape=[
            shaped((SEQS,) + MASK_SHAPE, WIDE),
            shaped((SEQS, ROWS, L), LOW),
            shaped((SEQS * PICKS, D), LOW),
            shaped((SEQS * PICKS, D), LOW),
        ],
        in_specs=[VMEM] * 4 + [ANY] * len(after),
        out_specs=[VMEM] * 4,
        compiler_params=limit(8),
        cost_estimate=pl.CostEstimate(flops=int(3e10), bytes_accessed=0, transcendentals=0),
        name="prepare",
    )(ranks, table, query_in, query_cot, *after)


def take_rows(content, picks, seq, target):
    target[:L] = content[seq * L : (seq + 1) * L]
    target[L:] = picks[seq * PICKS : (seq + 1) * PICKS]


def front(seq, info, content, picks, matrices, masks, vec, b_expand, after=()):
    def kernel(info, content, picks, masks, vec, b_expand, *refs):
        w = Names(**dict(zip(MATRICES, refs[:6])))
        out, x, query, key, value, mixed, first_low, total = refs[6 + len(after) :]
        s = Names(
            query=query,
            key=key,
            value=value,
            mixed=mixed,
            first_low=first_low,
            total=total,
            out=out,
        )
        take_rows(content, picks, seq, x)
        forward(x, w, vec, b_expand, masks.at[seq], s, False)

    return pl.pallas_call(
        kernel,
        out_shape=shaped((ROWS, D), LOW),
        in_specs=[SMEM] + [VMEM] * 11 + [ANY] * len(after),
        out_specs=VMEM,
        scratch_shapes=[pltpu.VMEM((ROWS, D), LOW)]
        + [pltpu.VMEM(*KEPT[n]) for n in ("query", "key", "value", "mixed", "first_low")]
        + [pltpu.VMEM((ROWS, D), WIDE)],
        compiler_params=limit(12),
        cost_estimate=cost(5),
        name="front",
    )(info, content, picks, masks, vec, b_expand, *matrices, *after)


def middle_forward(seq, info, content, picks, arrived, matrices, masks, vec, b_expand, after=()):
    def kernel(info, arrived, content, picks, masks, vec, b_expand, *refs):
        w, rest = Names(**dict(zip(MATRICES, refs[:6]))), refs[6 + len(after) :]
        (out, early, pair), kept = rest[:3], rest[3 : 3 + len(SAVED)]
        mixed, total = rest[3 + len(SAVED) :]
        x = pair.at[0]
        s = Names(total=total, out=out, mixed=mixed, **dict(zip(SAVED, kept)))
        take_rows(content, picks, seq, x)
        x[...] = jnp.where(info[2] == 1, x[...], arrived[...])
        early[:, :D] = x[...]
        forward(x, w, vec, b_expand, masks.at[seq], s, True)
        pair[1] = mixed[...]
        early[:, D : 2 * D] = mixed[...]
        early[:, 2 * D : 3 * D] = s.first_low[...]
        early[:, 3 * D :] = columns(s.activated, (1 - info[0]) * HALF, HALF)[...]

    out, early, pair, *saved = pl.pallas_call(
        kernel,
        out_shape=[
            shaped((ROWS, D), WIDE),
            shaped((ROWS, EARLY), LOW),
            shaped((2, ROWS, D), LOW),
        ]
        + [shaped(*KEPT[n]) for n in SAVED],
        in_specs=[SMEM] + [VMEM] * 12 + [ANY] * len(after),
        out_specs=[VMEM] * (3 + len(SAVED)),
        scratch_shapes=[pltpu.VMEM(*KEPT["mixed"]), pltpu.VMEM((ROWS, D), WIDE)],
        compiler_params=limit(16),
        cost_estimate=cost(6),
        name="middle_forward",
    )(info, arrived, content, picks, masks, vec, b_expand, *matrices, *after)
    return (out, early, pair, dict(zip(SAVED, saved)))


FEED_SAVED = ("normed2", "root2", "slope", "normed1", "root1")
ATTEND_SAVED = ("value", "probs", "key", "query")


def middle_back(seq, content, picks, matrices, vec, saved):
    names = FEED_SAVED + ATTEND_SAVED

    def kernel(content, picks, vec, *refs):
        w, rest = Names(**dict(zip(MATRICES, refs[:6]))), refs[6:]
        kept, grad, rest = rest[: len(names)], rest[len(names)], rest[len(names) + 1 :]
        cot, total, branch, expanded, attended, dmixed, dvalue, dquery, dkey = rest
        s = Names(
            total=total,
            branch=branch,
            expanded=expanded,
            attended=attended,
            dmixed=dmixed,
            dvalue=dvalue,
            dquery=dquery,
            dkey=dkey,
            **dict(zip(names, kept)),
        )
        take_rows(content, picks, seq, cot)
        back_second_norm(cot[...], vec, s)
        back_feed(w, vec, s)
        dmixed[...] = nt(attended[...], w.out[...]).astype(LOW)
        back_attend(s)
        lower = total[...] + nt(dquery[...], w.query[...])
        upper = nt(dkey[...], w.key[...]) + nt(dvalue[...], w.value[...])
        grad[:L] = (lower[:L] + upper).astype(LOW)
        grad[L:] = lower[L:].astype(LOW)

    return pl.pallas_call(
        kernel,
        out_shape=shaped((ROWS, D), LOW),
        in_specs=[VMEM] * (9 + len(names)),
        out_specs=VMEM,
        scratch_shapes=[
            pltpu.VMEM((ROWS, D), LOW),
            pltpu.VMEM((ROWS, D), WIDE),
            pltpu.VMEM((ROWS, D), LOW),
            pltpu.VMEM((ROWS, FF), LOW),
            pltpu.VMEM((ROWS, D), LOW),
            pltpu.VMEM((ROWS, D), LOW),
            pltpu.VMEM((L, D), LOW),
            pltpu.VMEM((ROWS, D), LOW),
            pltpu.VMEM((L, D), LOW),
        ],
        compiler_params=limit(12),
        cost_estimate=cost(7),
        name="middle_back",
    )(content, picks, vec, *matrices, *(saved[n] for n in names))


def feed_back(seq, info, arrived, content, picks, small_in, vec, matrices, saved, after=()):
    given = [] if small_in is None else [small_in]

    def kernel(info, arrived, content, picks, vec, expand, contract, *refs):
        kept, rest = refs[:5], refs[5 + len(given) + len(after) :]
        total, branch, attended, small, own, late, upper, expanded = rest
        w = Names(expand=expand, contract=contract)
        s = Names(
            total=total,
            branch=branch,
            attended=attended,
            expanded=expanded,
            **dict(zip(FEED_SAVED, kept)),
        )
        small[...] = refs[5][...] if given else jnp.zeros_like(small)

        def add(place, value):
            small[place : place + 1, :] += value

        take_rows(content, picks, seq, upper)
        back_second_norm(jnp.where(info[2] == 1, arrived[...], upper[...]), vec, s, add)
        late[:, :D] = branch[...]
        back_feed(w, vec, s, add)
        own[...] = columns(expanded, info[0] * HALF, HALF)[...]
        late[:, D:] = columns(expanded, (1 - info[0]) * HALF, HALF)[...]

    return pl.pallas_call(
        kernel,
        out_shape=[
            shaped((ROWS, D), WIDE),
            shaped((ROWS, D), LOW),
            shaped((ROWS, D), LOW),
            shaped((SMALL, D), WIDE),
            shaped((ROWS, HALF), LOW),
            shaped((ROWS, LATE), LOW),
        ],
        in_specs=[SMEM] + [VMEM] * (11 + len(given)) + [ANY] * len(after),
        out_specs=[VMEM] * 6,
        scratch_shapes=[pltpu.VMEM((ROWS, D), LOW), pltpu.VMEM((ROWS, FF), LOW)],
        compiler_params=limit(12),
        cost_estimate=cost(4),
        name="feed_back",
    )(
        info,
        arrived,
        content,
        picks,
        vec,
        matrices[4],
        matrices[5],
        *(saved[n] for n in FEED_SAVED),
        *given,
        *after,
    )


PLACES = {
    (2, 0): (0, 0),
    (1, 1): (0, 1),
    (2, 1): (1, 0),
    (3, 0): (1, 1),
    (1, 0): (2, 0),
    (3, 1): (3, 0),
    (0, 0): (4, 0),
    (0, 1): (4, 1),
}


def term_shapes(count):
    return [shaped((n * count, D), LOW) for n in (2, 2, 1, 1, 2)]


def feed_grads(info, mine, branch, own, early, late):
    def kernel(info, *refs):
        acts, lows, branches, owns, earlies, lates = (refs[2 * i : 2 * i + 2] for i in range(6))
        outs, (a_act, a_first, b_branch, b_own, stage, sems, out_sems) = refs[12:17], refs[17:]
        core, place = info[0], info[1]
        own_at = [slice(seq * ROWS, (seq + 1) * ROWS) for seq in range(SEQS)]
        far_at = [slice((2 + seq) * ROWS, (3 + seq) * ROWS) for seq in range(SEQS)]
        pairs, later = [], []
        for seq in range(SEQS):
            pairs += [
                (columns(acts[seq], core * HALF, HALF), a_act.at[own_at[seq]]),
                (earlies[seq].at[:, 3 * D :], a_act.at[far_at[seq]]),
                (branches[seq], b_branch.at[own_at[seq]]),
                (lates[seq].at[:, :D], b_branch.at[far_at[seq]]),
            ]
            later += [
                (lows[seq], a_first.at[own_at[seq]]),
                (earlies[seq].at[:, 2 * D : 3 * D], a_first.at[far_at[seq]]),
                (owns[seq], b_own.at[own_at[seq]]),
                (lates[seq].at[:, D:], b_own.at[far_at[seq]]),
            ]
        copies = start_all(pairs + later, sems)
        sent = []

        def send(block):
            for k in range(4):
                quarter = lax.rem(place + k, 4)
                index, part = PLACES[k, block // 2]
                start = (2 * part + block % 2) * QUARTER
                sent.extend(
                    start_all(
                        [
                            (
                                rows_at(stage.at[block], quarter * QUARTER, QUARTER),
                                outs[index].at[start : start + QUARTER],
                            )
                        ],
                        out_sems,
                        block * 4 + k,
                    )
                )

        wait_all(copies[:8])
        for block in range(2):
            for part in range(3):
                start = block * D + part * 256
                stage[block, part * 256 : (part + 1) * 256] = tn(
                    a_act[:, start : start + 256], b_branch[...]
                ).astype(LOW)
            send(block)
        wait_all(copies[8:])
        for block in range(2):
            for part in range(3):
                stage[2 + block, part * 256 : (part + 1) * 256] = tn(
                    a_first[:, part * 256 : (part + 1) * 256], b_own[:, block * D : (block + 1) * D]
                ).astype(LOW)
            send(2 + block)
        wait_all(sent)

    acts = [saved["activated"] for saved in mine]
    lows = [saved["first_low"] for saved in mine]
    return pl.pallas_call(
        kernel,
        out_shape=term_shapes(2 * QUARTER),
        in_specs=[SMEM] + [ANY] * 12,
        out_specs=[ANY] * 5,
        scratch_shapes=[
            pltpu.VMEM((2 * ALL_ROWS, HALF), LOW),
            pltpu.VMEM((2 * ALL_ROWS, D), LOW),
            pltpu.VMEM((2 * ALL_ROWS, D), LOW),
            pltpu.VMEM((2 * ALL_ROWS, HALF), LOW),
            pltpu.VMEM((4, D, D), LOW),
            DMA((16,)),
            DMA((16,)),
        ],
        compiler_params=limit(16),
        cost_estimate=cost(8),
        name="feed_grads",
    )(info, *acts, *lows, *branch, *own, *early, *late)


def attend_back(seq, info, attended, small_in, spread, after, w_out, saved):
    def kernel(info, attended, small_in, spread, w_out, *refs):
        kept, (pieces, send, small, dmixed, sums) = refs[:4], refs[4 + len(after) :]
        small[...] = small_in[...]
        pieces[1, :ROWS] = attended[...]
        dmixed[...] = nt(attended[...], w_out[...]).astype(LOW)
        s = Names(
            dmixed=dmixed,
            dquery=pieces.at[0, :ROWS],
            dkey=pieces.at[0, ROWS:],
            dvalue=pieces.at[1, ROWS:],
            **dict(zip(ATTEND_SAVED, kept)),
        )
        sums[...] = jnp.zeros_like(sums)

        def table_sum(pair, dscores):
            for odd in range(2):
                part = tn(spread[seq], dscores[odd * ROWS : (odd + 1) * ROWS])
                both = jnp.concatenate([part, jnp.zeros((L, L), WIDE)], axis=1)
                turned = pltpu.roll(both, 0, 1, stride=1, stride_axis=0)
                head = 2 * pair + odd
                sums[head : head + 1, :] = jnp.sum(turned, axis=0, keepdims=True)

        back_attend(s, table_sum)
        send[...] = pieces[1 - info[0]]
        small[S_QUERY : S_QUERY + 1, :] += column_sum(pieces[0, :ROWS])
        small[S_VALUE : S_VALUE + 1, :] += column_sum(pieces[1, ROWS:])
        distance = lax.broadcasted_iota(jnp.int32, (2 * L, L), 0) - (L - 1)
        bucket = lax.broadcasted_iota(jnp.int32, (2 * L, L), 1)
        small[S_TABLE : S_TABLE + 16, :L] += lax.dot_general(
            sums[...],
            (bucket_of(distance) == bucket).astype(WIDE),
            (((1,), (0,)), ((), ())),
            precision=lax.Precision.HIGHEST,
            preferred_element_type=WIDE,
        )

    return pl.pallas_call(
        kernel,
        out_shape=[
            shaped((2, ROWS + L, D), LOW),
            shaped((ROWS + L, D), LOW),
            shaped((SMALL, D), WIDE),
        ],
        in_specs=[SMEM] + [VMEM] * 8 + [ANY] * len(after),
        out_specs=[VMEM] * 3,
        scratch_shapes=[pltpu.VMEM((ROWS, D), LOW), pltpu.VMEM((16, 2 * L), WIDE)],
        compiler_params=limit(12),
        cost_estimate=cost(4),
        name="attend_back",
    )(info, attended, small_in, spread, w_out, *(saved[n] for n in ATTEND_SAVED), *after)


def finish_rows(info, total, output, pieces, matrices, picks, after):
    def kernel(info, *refs):
        totals, outputs, pieces = refs[0:2], refs[2:4], refs[4:6]
        (query, key, value), refs = refs[6:9], refs[9 + len(after) :]
        content_ends, query_ends, done = refs
        done[...] = jnp.zeros_like(done)
        first = info[2] == 1
        for seq in range(SEQS):
            lower = totals[seq][...] + nt(pieces[seq][0, :ROWS], query[...])
            upper = nt(pieces[seq][0, ROWS:], key[...]) + nt(pieces[seq][1, ROWS:], value[...])
            content_ends[seq * L : (seq + 1) * L] = jnp.where(
                first, lower[:L] + upper, outputs[seq][:L]
            )
            query_ends[seq * picks : (seq + 1) * picks] = jnp.where(
                first, lower[L : L + picks], outputs[seq][L : L + picks]
            )

    return pl.pallas_call(
        kernel,
        out_shape=[shaped((ALL_CONTENT, D), WIDE), shaped((SEQS * picks, D), WIDE), TOKEN],
        in_specs=[SMEM] + [VMEM] * 9 + [ANY] * len(after),
        out_specs=[VMEM] * 3,
        compiler_params=limit(12),
        cost_estimate=cost(3),
        name="finish_rows",
    )(info, *total, *output, *pieces, *matrices[:3], *after)


def attend_grads(info, pair, early, mine, arrived, small, after=()):
    def kernel(info, small, *refs):
        pairs_in, earlies, mines, arriveds = (refs[2 * i : 2 * i + 2] for i in range(4))
        refs = refs[8 + len(after) :]
        outs, rest = refs[:5], refs[5:]
        a_rows, a_content, b_rows, b_content, stage, extra, sems, out_sems = rest
        core, place = info[0], info[1]
        pairs, later = [], []
        for seq in range(SEQS):
            at = slice(seq * ROWS, (seq + 1) * ROWS)
            far = slice((2 + seq) * ROWS, (3 + seq) * ROWS)
            pairs += [
                (pairs_in[seq].at[core], a_rows.at[at]),
                (columns(earlies[seq], core * D, D), a_rows.at[far]),
                (mines[seq].at[core, :ROWS], b_rows.at[at]),
                (arriveds[seq].at[:ROWS], b_rows.at[far]),
            ]
            at = slice(seq * L, (seq + 1) * L)
            far = slice((2 + seq) * L, (3 + seq) * L)
            later += [
                (pairs_in[seq].at[0, :L], a_content.at[at]),
                (earlies[seq].at[:L, :D], a_content.at[far]),
                (mines[seq].at[core, ROWS:], b_content.at[at]),
                (arriveds[seq].at[ROWS:], b_content.at[far]),
            ]
        copies = start_all(pairs + later, sems)
        blank = jnp.zeros((EXTRA, D), WIDE)
        extra[0] = jnp.concatenate([small[...], blank[SMALL:]]).astype(LOW)
        extra[1] = blank.astype(LOW)
        sent = []
        for block, (former, latter) in enumerate(((a_rows, b_rows), (a_content, b_content))):
            wait_all(copies[8 * block : 8 * block + 8])
            for part in range(3):
                stage[block, part * 256 : (part + 1) * 256] = tn(
                    former[:, part * 256 : (part + 1) * 256], latter[...]
                ).astype(LOW)
            for k in range(4):
                quarter = lax.rem(place + k, 4)
                index, part = PLACES[k, block]
                start = part * (QUARTER + EXTRA)
                middle, stop = start + QUARTER, start + QUARTER + EXTRA
                sent += start_all(
                    [
                        (
                            rows_at(stage.at[block], quarter * QUARTER, QUARTER),
                            outs[index].at[start:middle],
                        ),
                        (extra.at[block], outs[index].at[middle:stop]),
                    ],
                    out_sems,
                    block * 8 + 2 * k,
                )
        wait_all(sent)

    return pl.pallas_call(
        kernel,
        out_shape=term_shapes(QUARTER + EXTRA),
        in_specs=[SMEM, VMEM] + [ANY] * (8 + len(after)),
        out_specs=[ANY] * 5,
        scratch_shapes=[
            pltpu.VMEM((2 * ALL_ROWS, D), LOW),
            pltpu.VMEM((2 * ALL_CONTENT, D), LOW),
            pltpu.VMEM((2 * ALL_ROWS, D), LOW),
            pltpu.VMEM((2 * ALL_CONTENT, D), LOW),
            pltpu.VMEM((2, D, D), LOW),
            pltpu.VMEM((2, EXTRA, D), LOW),
            DMA((16,)),
            DMA((16,)),
        ],
        compiler_params=limit(12),
        cost_estimate=cost(5),
        name="attend_grads",
    )(info, small, *pair, *early, *mine, *arrived, *after)


def small_kernel(body, name, shapes, inputs, after=(), info=None, through=()):
    first = [] if info is None else [info]
    given = len(first) + len(inputs)

    def kernel(*refs):
        outs = refs[given + len(after) + len(through) :]
        body(*refs[:given], *outs[: len(shapes)])

    return pl.pallas_call(
        kernel,
        out_shape=[shaped(shape, LOW) for shape in shapes]
        + [shaped(array.shape, array.dtype) for array in through],
        in_specs=[SMEM] * len(first)
        + [VMEM] * len(inputs)
        + [ANY] * (len(after) + len(through)),
        out_specs=[VMEM] * len(shapes) + [ANY] * len(through),
        input_output_aliases={
            given + len(after) + i: len(shapes) + i for i in range(len(through))
        },
        compiler_params=limit(8),
        cost_estimate=cost(1),
        name=name,
    )(*first, *inputs, *after, *through)


def total_of(*terms):
    return sum(term.astype(WIDE) for term in terms).astype(LOW)


def ring_add(after0, before1, from_left, from_right, after=()):
    count = after0.shape[0]

    def body(after0, before1, from_left, from_right, right, left):
        right[...] = total_of(after0[...], from_left[:count])
        left[...] = total_of(before1[...], from_right[:count])

    return small_kernel(
        body, "ring_add", [after0.shape] * 2, (after0, before1, from_left, from_right), after
    )


def ring_sum(info, own, left, right, from_left, from_right, after=()):
    count = left.shape[0]
    part = count // 4

    def body(info, own, left, right, from_left, from_right, *outs):
        for k, out in enumerate(outs):
            at = pl.multiple_of(lax.rem(info[3] + k, 4) * part, 16)
            low, high = pl.ds(at, part), pl.ds(at + count, part)
            out[:part] = total_of(own[low], left[low], from_right[high])
            out[part:] = total_of(own[high], from_left[high], right[low])

    return small_kernel(
        body,
        "ring_sum",
        [(2 * part, D)] * 4,
        (own, left, right, from_left, from_right),
        after,
        info,
    )


def add_all(name, terms, after=()):
    def body(*refs):
        refs[-1][...] = total_of(*(ref[...] for ref in refs[:-1]))

    return small_kernel(body, name, [terms[0].shape], terms, after)[0]


def inner_join(info, parts, after=(), through=()):
    part = parts[0].shape[0] // 2

    def body(info, *refs):
        whole = refs[-1]
        for k, ref in enumerate(refs[:-1]):
            at = pl.multiple_of(lax.rem(info[3] + k, 4) * part, 16)
            whole[pl.ds(at, part)] = ref[:part]
            whole[pl.ds(at + 4 * part, part)] = ref[part:]

    return small_kernel(body, "inner_join", [(8 * part, D)], parts, after, info, through)


def cut(before, after_part, after=()):
    count = before.shape[0] // 2

    def body(before, after_part, right, left):
        right[...] = before[:count]
        left[...] = after_part[count:]

    return small_kernel(body, "cut", [(count, D)] * 2, (before, after_part), after)


def feed_targets(outs, source, half, core, quarter):
    pairs = []
    for block in range(2):
        part = source.at[block * QUARTER : (block + 1) * QUARTER]
        if half == 0:
            target = rows_at(outs[0], core * HALF + block * D + quarter * QUARTER, QUARTER)
        else:
            target = columns(
                rows_at(outs[1], quarter * QUARTER, QUARTER), (core * 2 + block) * D, D
            )
        pairs.append((None, part, target))
    return pairs


def attend_targets(outs, source, half, core, quarter):
    return [
        (
            core == number,
            source.at[:QUARTER],
            rows_at(outs[2 * number + half], quarter * QUARTER, QUARTER),
        )
        for number in range(2)
    ]


def settle(targets, shapes, count, info, pieces, outs, through, name):
    keys = tuple(pieces)
    arrays = [pieces[key] for key in keys]
    given = list(outs or ()) + list(through)
    first_alias = len(shapes) - len(outs or ())

    def kernel(info, *refs):
        parts, rest = refs[: len(keys)], refs[len(keys) + len(given) :]
        outs, rest = rest[: len(shapes)], rest[len(shapes) + len(through) :]
        done, rest = rest[0], rest[1:]
        done[...] = jnp.zeros_like(done)
        held, wide_held, (sems, out_sems) = rest[: len(keys)], rest[len(keys) : -2], rest[-2:]
        copies = start_all(list(zip(parts, held)), sems)
        finish = []
        for index, (sibling, k, which) in enumerate(keys):
            core = 1 - info[0] if sibling else info[0]
            quarter = lax.rem((info[3] if sibling else info[1]) + k, 4)
            copies[index].wait()
            wide_held[index][...] = held[index][...].astype(WIDE)
            for number, half in enumerate(which):
                source = wide_held[index].at[number * count : (number + 1) * count]
                for place, (condition, part, target) in enumerate(
                    targets(outs, source, half, core, quarter)
                ):
                    copy = pltpu.make_async_copy(
                        part, target, out_sems.at[4 * index + 2 * number + place]
                    )
                    if condition is None:
                        copy.start()
                        finish.append(copy.wait)
                    else:
                        pl.when(condition)(copy.start)
                        finish.append(lambda c=copy, when=condition: pl.when(when)(c.wait))
        for action in finish:
            action()

    result = pl.pallas_call(
        kernel,
        out_shape=[shaped(shape, WIDE) for shape in shapes]
        + [shaped(array.shape, array.dtype) for array in through]
        + [TOKEN],
        in_specs=[SMEM] + [ANY] * (len(keys) + len(given)),
        out_specs=[ANY] * (len(shapes) + len(through)) + [VMEM],
        scratch_shapes=[pltpu.VMEM(array.shape, LOW) for array in arrays]
        + [pltpu.VMEM(array.shape, WIDE) for array in arrays]
        + [DMA((len(keys),)), DMA((4 * len(keys),))],
        input_output_aliases={1 + len(keys) + i: first_alias + i for i in range(len(given))},
        compiler_params=limit(32),
        cost_estimate=cost(sum(array.size for array in arrays) * 2e-6 + 1),
        name=name,
    )(info, *arrays, *given)
    return result[: len(shapes)], result[len(shapes) : -1], result[-1]


PLANE = ("x", "y", "c")


def shift(value, axis, by):
    size = lax.axis_size(axis)
    return lax.ppermute(value, axis, [(i, (i + by) % size) for i in range(size)])


def send(value, by):
    return lax.ppermute(value, "s", [(0, 1)] if by > 0 else [(1, 0)])


def turn(value, outer, by):
    pairs = []
    for i in range(4):
        for j in range(4):
            for c in range(2):
                if (c == 0) == outer:
                    target = ((i + by) % 4, j)
                else:
                    target = (i, (j + by) % 4)
                pairs.append(((i * 4 + j) * 2 + c, (target[0] * 4 + target[1]) * 2 + c))
    return lax.ppermute(value, PLANE, pairs)


def place(outer):
    return jnp.where(
        (lax.axis_index("c") == 0) == outer, lax.axis_index("x"), lax.axis_index("y")
    )


def wide(value):
    return value.astype(WIDE)


def total_wide(*terms):
    return sum(wide(term) for term in terms)


def inner_turns(parts, sign):
    return [turn(part, False, sign * by) for part, by in zip(parts, (1, 2, -1))]


def both_cores(pieces):
    near = {(0,) + key: piece for key, piece in pieces.items()}
    return near | {(1,) + key: shift(piece, "c", 1) for key, piece in pieces.items()}


def gather_outer(own, after=()):
    before, after_part = turn(own, True, 1), turn(own, True, -1)
    to_right, to_left = cut(before, after_part, after)
    near = {(0, (0, 1)): own, (3, (0, 1)): before, (1, (0, 1)): after_part}
    across = {(2, (0,)): turn(to_right, True, 1), (2, (1,)): turn(to_left, True, -1)}
    return near, across, to_right


def on_device(
    content_in,
    query_in,
    content_cot,
    query_cot,
    order_rank,
    query_pos,
    group_tag,
    *rest,
):
    (
        w_query,
        b_query,
        w_key,
        w_value,
        b_value,
        w_out,
        b_out,
        norm1_gain,
        norm1_bias,
        w_expand,
        b_expand,
        w_contract,
        b_contract,
        norm2_gain,
        norm2_bias,
    ) = (argument[0] for argument in rest[:-1])
    rel_table = rest[-1]
    core = lax.axis_index("c")
    first_section = (lax.axis_index("s") == 0).astype(jnp.int32)
    info = jnp.stack([core, place(True), first_section, place(False)])
    picks = query_pos.shape[1]

    matrices = (w_query, w_key, w_value, w_out, w_expand, w_contract)
    w_out_held = w_out
    vec = jnp.stack(
        [b_query, b_value, b_out, norm1_gain, norm1_bias, b_contract, norm2_gain, norm2_bias]
    )
    ranks = jnp.concatenate([order_rank, group_tag, query_pos], axis=1)
    masks, spread, query_in, query_cot = prepare(
        ranks, rel_table, query_in, query_cot, picks, (vec, info)
    )
    b_expand = b_expand[None]

    fronts, arrived = [], []
    for seq in range(SEQS):
        fronts.append(
            front(seq, info, content_in, query_in, matrices, masks, vec, b_expand, tuple(fronts))
        )
        arrived.append(send(fronts[seq], 1))
    output, early, pair, saved, grads = [], [], [], [], []
    for seq in range(SEQS):
        results = middle_forward(
            seq, info, content_in, query_in, arrived[seq], matrices, masks, vec, b_expand, tuple(grads)
        )
        for collected, result in zip((output, early, pair, saved), results):
            collected.append(result)
        grads.append(middle_back(seq, content_cot, query_cot, matrices, vec, saved[seq]))
    early = [shift(value, "c", 1) for value in early]
    grads = [send(value, -1) for value in grads]
    small = None
    total, branch, attended, own, late, pieces, pass_on = [], [], [], [], [], [], []
    for seq in range(SEQS):
        results = feed_back(
            seq,
            info,
            grads[seq],
            content_cot,
            query_cot,
            small,
            vec,
            matrices,
            saved[seq],
            tuple(pass_on),
        )
        small = results[3]
        for collected, result in zip(
            (total, branch, attended, own, late), results[:3] + results[4:]
        ):
            collected.append(result)
        if seq == 0:
            late[0] = shift(late[0], "c", 1)
        else:
            late[1] = shift(late[1], "c", 1)
            feed_terms = feed_grads(info, saved, branch, own, early, late)
        results = attend_back(
            seq,
            info,
            attended[seq],
            small,
            spread,
            () if seq == 0 else (feed_terms[4],),
            w_out_held,
            saved[seq],
        )
        small = results[2]
        pieces.append(results[0])
        pass_on.append(results[1])
    passed = [shift(value, "c", 1) for value in pass_on]

    def outer_step(terms):
        return (turn(terms[0], True, 1), turn(terms[1], True, -1))

    f_left, f_right = outer_step(feed_terms)
    content_ends, query_ends, token = finish_rows(
        info, total, output, pieces, matrices, picks, (feed_terms[4],)
    )
    f_sent = ring_add(feed_terms[2], feed_terms[3], f_left, f_right, (token,))
    attend_terms = attend_grads(info, pair, early, pieces, passed, small, tuple(f_sent))
    a_left, a_right = outer_step(attend_terms)
    f_outer = outer_step(f_sent)
    f_parts = ring_sum(info, feed_terms[4], *f_outer, f_left, f_right, (attend_terms[2],))
    f_part = add_all("inner_sum", [f_parts[0]] + inner_turns(f_parts[1:], 1))
    f_far = shift(f_part, "z", 1)
    a_sent = ring_add(attend_terms[2], attend_terms[3], a_left, a_right, (f_part,))
    a_outer = outer_step(a_sent)
    f_part = add_all("z_sum", [f_part, f_far], (a_sent[0],))
    a_parts = ring_sum(info, attend_terms[4], *a_outer, a_left, a_right, (f_part,))
    f_others = inner_turns([f_part] * 3, -1)
    a_part = add_all("inner_sum", [a_parts[0]] + inner_turns(a_parts[1:], 1))
    a_far = shift(a_part, "z", 1)
    (feed_own,) = inner_join(info, [f_part] + f_others, (a_parts[0],))
    a_part = add_all("z_sum", [a_part, a_far])
    a_others = inner_turns([a_part] * 3, -1)
    feed_near, feed_across, sent = gather_outer(feed_own, tuple(a_others))
    attend_own, *arrays = inner_join(
        info, [a_part] + a_others, (sent,), tuple(feed_near.values())
    )
    feed_near = dict(zip(feed_near, arrays))
    feed_shapes, attend_shapes = ((FF, D), (D, FF)), ((D, D),) * 4
    feed_outs, _, token = settle(
        feed_targets,
        feed_shapes,
        2 * QUARTER,
        info,
        both_cores(feed_near),
        None,
        (),
        "feed_out",
    )
    attend_near, attend_across, _ = gather_outer(attend_own, (token,))
    feed_outs, _, _ = settle(
        feed_targets,
        feed_shapes,
        2 * QUARTER,
        info,
        both_cores(feed_across),
        feed_outs,
        (),
        "feed_out_last",
    )
    attend_near = both_cores(attend_near)
    attend_outs, _, _ = settle(
        attend_targets,
        attend_shapes,
        QUARTER + EXTRA,
        info,
        attend_near,
        None,
        (),
        "attend_out",
    )
    attend_outs, _, _ = settle(
        attend_targets,
        attend_shapes,
        QUARTER + EXTRA,
        info,
        both_cores(attend_across),
        attend_outs,
        (),
        "attend_out_last",
    )
    contract, expand = feed_outs
    g_query, g_key, g_out, g_value = attend_outs
    small_sum = total_wide(
        *(attend_near[far, 0, (0, 1)][QUARTER : QUARTER + SMALL] for far in (0, 1))
    )
    table = small_sum[S_TABLE : S_TABLE + H, :L]
    table_total = (table + shift(table, "s", 1))[:, :NB].T
    row = lambda k: small_sum[k][None]
    return (
        content_ends[None],
        query_ends[None],
        g_query[None],
        row(S_QUERY),
        g_key[None],
        g_value[None],
        row(S_VALUE),
        g_out[None],
        row(S_OUT),
        row(S_GAIN1),
        row(S_SHIFT1),
        expand[None],
        small_sum[S_EXPAND : S_EXPAND + 4].reshape(1, FF),
        contract[None],
        row(S_CONTRACT),
        row(S_GAIN2),
        row(S_SHIFT2),
        table_total,
    )


DP = ("z", "x", "y", "c")


def solution(mesh):
    mesh = jax.sharding.Mesh(mesh.devices.reshape(2, 2, 4, 4, 2), ("s",) + DP)
    layer_specs = tuple(
        P("s", *([None] * (rank - 1))) for rank in (3, 2, 3, 3, 2, 3, 2, 2, 2, 3, 2, 3, 2, 2, 2)
    )
    in_specs = (P(DP, None),) * 7 + layer_specs + (P(),)
    out_specs = (P("s", DP, None),) * 2 + layer_specs + (P(),)
    return jax.shard_map(
        on_device, mesh=mesh, in_specs=in_specs, out_specs=out_specs, check_vma=False
    )
```

```python
import jax
import jax.numpy as jnp
from jax import lax
from jax.experimental import pallas as pl
from jax.experimental.pallas import tpu as pltpu
from jax.sharding import PartitionSpec as P

D = 768
H = 12
HD = 64
FF = 3072
NB = 32
L = 128
PAIRS = H // 2
SEQS = 2
PICKS = 32
ROWS = L + PICKS
EPSILON = 1e-05
SCALE = HD ** (-0.5)
TILE = 1536
LOW = jnp.bfloat16
WIDE = jnp.float32
HALF = FF // 2
QUARTER = D // 4
EARLY = 3 * D + HALF
LATE = D + HALF
EXTRA = 64
SMALL = 32
ALL_ROWS = SEQS * ROWS
ALL_CONTENT = SEQS * L
PIECE = ALL_ROWS + ALL_CONTENT


def nn(former, latter):
    return lax.dot_general(
        former, latter, (((1,), (0,)), ((), ())), preferred_element_type=WIDE
    )


def nt(former, latter):
    return lax.dot_general(
        former, latter, (((1,), (1,)), ((), ())), preferred_element_type=WIDE
    )


def tn(former, latter):
    return lax.dot_general(
        former, latter, (((0,), (0,)), ((), ())), preferred_element_type=WIDE
    )


def halves(value):
    even = lax.broadcasted_iota(jnp.int32, value.shape, 1) < HD
    zero = jnp.zeros_like(value)
    return jnp.concatenate([jnp.where(even, value, zero), jnp.where(even, zero, value)])


def side(value):
    count = value.shape[0] // 2
    return jnp.concatenate([value[:count], value[count:]], axis=1)


def norm_rows(values):
    centered = values - jnp.mean(values, axis=-1, keepdims=True)
    variance = jnp.mean(centered * centered, axis=-1, keepdims=True)
    root = lax.rsqrt(variance + EPSILON)
    return (centered * root, root)


def norm_rows_back(scaled, normed, root):
    return root * (
        scaled
        - jnp.mean(scaled, axis=-1, keepdims=True)
        - normed * jnp.mean(scaled * normed, axis=-1, keepdims=True)
    )


B_QUERY, B_VALUE, B_OUT, GAIN1, SHIFT1, B_CONTRACT, GAIN2, SHIFT2 = range(8)
S_QUERY, S_VALUE, S_OUT, S_GAIN1, S_SHIFT1, S_EXPAND = range(6)
S_CONTRACT, S_GAIN2, S_SHIFT2, S_TABLE = 9, 10, 11, 16
LIMITS = (12, 16, 23, 32, 46, 64, 91)


def bucket_of(relative):
    distance = jnp.abs(relative)
    beyond = 8 + sum((distance >= limit).astype(jnp.int32) for limit in LIMITS)
    within = jnp.where(distance < 8, distance, beyond)
    return within + 16 * (relative > 0).astype(jnp.int32)


def forward(x, w, vec, b_expand, masks, s, keep):
    row = lambda k: vec[k : k + 1, :]
    s.query[...] = (nn(x[...], w.query[...]) + row(B_QUERY)).astype(LOW)
    s.key[...] = nn(x[:L], w.key[...]).astype(LOW)
    s.value[...] = (nn(x[:L], w.value[...]) + row(B_VALUE)).astype(LOW)
    for pair in range(PAIRS):
        lanes = slice(pair * 128, (pair + 1) * 128)
        scores = nt(halves(s.query[:, lanes]), s.key[:, lanes]) * SCALE + masks[pair]
        shifted = jnp.exp(scores - jnp.max(scores, axis=-1, keepdims=True))
        probs = (shifted / jnp.sum(shifted, axis=-1, keepdims=True)).astype(LOW)
        if keep:
            s.probs[pair] = probs
        s.mixed[:, lanes] = nn(side(probs), halves(s.value[:, lanes])).astype(LOW)
    total = x[...].astype(WIDE) + nn(s.mixed[...], w.out[...]) + row(B_OUT)
    normed, root = norm_rows(total)
    first = normed * row(GAIN1) + row(SHIFT1)
    s.first_low[...] = first.astype(LOW)
    s.total[...] = first + row(B_CONTRACT)
    if keep:
        s.normed1[...] = normed
        s.root1[...] = jnp.broadcast_to(root, (ROWS, 128))
    for tile in range(FF // TILE):
        tile = slice(tile * TILE, (tile + 1) * TILE)
        expanded = nn(s.first_low[...], w.expand[:, tile]) + b_expand[:, tile]
        cumulative = 0.5 * (1.0 + lax.erf(expanded * 0.7071067811865476))
        activated = (expanded * cumulative).astype(LOW)
        if keep:
            s.slope[:, tile] = (
                cumulative + expanded * jnp.exp(-0.5 * expanded * expanded) * 0.3989422804014327
            ).astype(LOW)
            s.activated[:, tile] = activated
        s.total[...] += nn(activated, w.contract[tile, :])
    normed, root = norm_rows(s.total[...])
    if keep:
        s.normed2[...] = normed
        s.root2[...] = jnp.broadcast_to(root, (ROWS, 128))
    s.out[...] = (normed * row(GAIN2) + row(SHIFT2)).astype(s.out.dtype)


def column_sum(value):
    return jnp.sum(value.astype(WIDE), axis=0, keepdims=True)


def back_second_norm(grad, vec, s, add=None):
    upper = grad.astype(WIDE)
    normed = s.normed2[...]
    lower = norm_rows_back(upper * vec[GAIN2 : GAIN2 + 1, :], normed, s.root2[:, :1])
    s.total[...] = lower
    s.branch[...] = lower.astype(LOW)
    if add is not None:
        add(S_GAIN2, column_sum(upper * normed))
        add(S_SHIFT2, column_sum(upper))
        add(S_CONTRACT, column_sum(lower.astype(LOW)))


def back_feed(w, vec, s, add=None):
    for tile in range(FF // TILE):
        tile = slice(tile * TILE, (tile + 1) * TILE)
        lower = (nt(s.branch[...], w.contract[tile, :]) * s.slope[:, tile].astype(WIDE)).astype(LOW)
        s.expanded[:, tile] = lower
        if add is not None:
            part = column_sum(lower)
            for column in range(TILE // D):
                add(
                    S_EXPAND + tile.start // D + column,
                    part[:, column * D : (column + 1) * D],
                )
        s.total[...] += nt(lower, w.expand[:, tile])
    upper = s.total[...]
    normed = s.normed1[...]
    lower = norm_rows_back(upper * vec[GAIN1 : GAIN1 + 1, :], normed, s.root1[:, :1])
    s.total[...] = lower
    s.attended[...] = lower.astype(LOW)
    if add is not None:
        add(S_GAIN1, column_sum(upper * normed))
        add(S_SHIFT1, column_sum(upper))
        add(S_OUT, column_sum(lower.astype(LOW)))


def back_attend(s, table=None):
    for pair in range(PAIRS):
        lanes = slice(pair * 128, (pair + 1) * 128)
        probs = s.probs[pair]
        below = halves(s.dmixed[:, lanes])
        dprobs = nt(below, s.value[:, lanes])
        s.dvalue[:, lanes] = tn(probs, below).astype(LOW)
        weight = probs.astype(WIDE)
        dscores = (
            weight * (dprobs - jnp.sum(weight * dprobs, axis=-1, keepdims=True))
        ).astype(LOW)
        s.dquery[:, lanes] = (nn(side(dscores), halves(s.key[:, lanes])) * SCALE).astype(LOW)
        s.dkey[:, lanes] = (tn(dscores, halves(s.query[:, lanes])) * SCALE).astype(LOW)
        if table is not None:
            table(pair, dscores)


class Names:
    def __init__(self, **named):
        self.__dict__.update(named)


MATRICES = ("query", "key", "value", "out", "expand", "contract")
MATRIX_SHAPES = {
    "query": (D, D),
    "key": (D, D),
    "value": (D, D),
    "out": (D, D),
    "expand": (D, FF),
    "contract": (FF, D),
}
MASK_SHAPE = (PAIRS, 2 * ROWS, L)
KEPT = {
    "query": ((ROWS, D), LOW),
    "key": ((L, D), LOW),
    "value": ((L, D), LOW),
    "probs": (MASK_SHAPE, LOW),
    "mixed": ((ROWS, D), LOW),
    "normed1": ((ROWS, D), WIDE),
    "root1": ((ROWS, 128), WIDE),
    "first_low": ((ROWS, D), LOW),
    "slope": ((ROWS, FF), LOW),
    "activated": ((ROWS, FF), LOW),
    "normed2": ((ROWS, D), WIDE),
    "root2": ((ROWS, 128), WIDE),
}
SAVED = tuple(name for name in KEPT if name != "mixed")
ANY = pl.BlockSpec(memory_space=pl.ANY)
VMEM = pl.BlockSpec(memory_space=pltpu.VMEM)
SMEM = pl.BlockSpec(memory_space=pltpu.SMEM)


def limit(megabytes):
    return pltpu.CompilerParams(vmem_limit_bytes=megabytes * 1024 * 1024)


DMA = pltpu.SemaphoreType.DMA


def cost(microseconds):
    return pl.CostEstimate(flops=0, bytes_accessed=int(microseconds * 3.2e6), transcendentals=0)


def shaped(shape, kind):
    return jax.ShapeDtypeStruct(shape, kind)


TOKEN = shaped((8, 128), WIDE)


def columns(ref, start, size):
    return ref.at[:, pl.ds(pl.multiple_of(start, 128), size)]


def rows_at(ref, start, size):
    return ref.at[pl.ds(pl.multiple_of(start, 64), size)]


def start_all(pairs, sems, base=0):
    copies = [
        pltpu.make_async_copy(source, target, sems.at[base + index])
        for index, (source, target) in enumerate(pairs)
    ]
    for copy in copies:
        copy.start()
    return copies


def wait_all(copies):
    for copy in copies:
        copy.wait()


def fetcher(names, sources, targets, sems, base=0):
    copies = dict(zip(names, start_all(list(zip(sources, targets)), sems, base)))
    return lambda name: copies[name].wait()


def prepare(ranks, table, query_in, query_cot, picks, after):
    def kernel(ranks, table, query_in, query_cot, *refs):
        masks, spread, rows_in, rows_cot = refs[len(after) :]
        order, tag, pos = ranks[:, :L], ranks[:, L : 2 * L], ranks[:, 2 * L : 2 * L + picks]
        for source, target in ((query_in, rows_in), (query_cot, rows_cot)):
            values = source[...].astype(WIDE)
            blank = jnp.zeros((PICKS - picks, D), WIDE)
            target[...] = jnp.concatenate(
                [values[:picks], blank, values[picks:], blank]
            ).astype(LOW)
        lane = lax.broadcasted_iota(jnp.int32, (L, L), 1)
        level = lax.broadcasted_iota(jnp.int32, (L, L), 0)
        lane_q = lax.broadcasted_iota(jnp.int32, (PICKS, L), 1)
        upright = lambda row: jnp.sum(jnp.where(lane == level, row, 0.0), axis=1, keepdims=True)
        distance = lax.broadcasted_iota(jnp.int32, (2 * L, NB), 0) - (L - 1)
        bucket = lax.broadcasted_iota(jnp.int32, (2 * L, NB), 1)
        by_distance = lax.dot_general(
            table[...],
            (bucket_of(distance) == bucket).astype(WIDE),
            (((0,), (1,)), ((), ())),
            precision=lax.Precision.HIGHEST,
            preferred_element_type=WIDE,
        )
        allowed, hot = [], []
        for seq in range(SEQS):
            own_rank = order[seq : seq + 1, :].astype(WIDE)
            own_tag = tag[seq : seq + 1, :].astype(WIDE)
            own_pos = pos[seq : seq + 1, :].astype(WIDE)
            number = lax.broadcasted_iota(jnp.int32, (PICKS, picks), 0)
            same = number == lax.broadcasted_iota(jnp.int32, (PICKS, picks), 1)
            place = jnp.sum(jnp.where(same, own_pos, 0.0), axis=1, keepdims=True)
            filled = lax.broadcasted_iota(jnp.int32, (PICKS, 1), 0) < picks
            place = jnp.where(filled, place, -1.0).astype(jnp.int32)
            matches = place == lane_q
            marks = jnp.where(matches, 1.0, 0.0)
            predicted = jnp.max(marks, axis=0, keepdims=True)
            rank = jnp.sum(jnp.where(matches, own_rank, 0.0), axis=1, keepdims=True)
            group = jnp.sum(jnp.where(matches, own_tag, 0.0), axis=1, keepdims=True)
            earlier = (upright(predicted) > 0) & (own_rank <= upright(own_rank))
            content = (upright(own_tag) == own_tag) & ((predicted == 0) | earlier)
            query = (group == own_tag) & ((predicted == 0) | (own_rank + 1 <= rank))
            allowed.append((content, query))
            hot.append(marks)
            spread[seq, :L] = jnp.where(lane == L - 1 - level, 1.0, 0.0).astype(LOW)
            spread[seq, L:] = jnp.where(lane_q == L - 1 - place, 1.0, 0.0).astype(LOW)
        hot = jnp.concatenate(hot)
        for head in range(H):
            row = jnp.broadcast_to(by_distance[head : head + 1], (L, 2 * L))
            bias = pltpu.roll(row, L + 1, 1, stride=1, stride_axis=0)[:, :L]
            bias_q = lax.dot_general(
                hot,
                bias,
                (((1,), (0,)), ((), ())),
                precision=lax.Precision.HIGHEST,
                preferred_element_type=WIDE,
            )
            base = head % 2 * ROWS
            for seq in range(SEQS):
                content, query = allowed[seq]
                masks[seq, head // 2, base : base + L] = jnp.where(content, bias, -1e30)
                masks[seq, head // 2, base + L : base + ROWS] = jnp.where(
                    query, bias_q[seq * PICKS : (seq + 1) * PICKS], -1e30
                )

    return pl.pallas_call(
        kernel,
        out_shape=[
            shaped((SEQS,) + MASK_SHAPE, WIDE),
            shaped((SEQS, ROWS, L), LOW),
            shaped((SEQS * PICKS, D), LOW),
            shaped((SEQS * PICKS, D), LOW),
        ],
        in_specs=[VMEM] * 4 + [ANY] * len(after),
        out_specs=[VMEM] * 4,
        compiler_params=limit(8),
        cost_estimate=pl.CostEstimate(flops=int(3e10), bytes_accessed=0, transcendentals=0),
        name="prepare",
    )(ranks, table, query_in, query_cot, *after)


def take_rows(content, picks, seq, target):
    target[:L] = content[seq * L : (seq + 1) * L]
    target[L:] = picks[seq * PICKS : (seq + 1) * PICKS]


def front(seq, info, content, picks, matrices, masks, vec, b_expand, after=()):
    def kernel(info, content, picks, masks, vec, b_expand, *refs):
        w = Names(**dict(zip(MATRICES, refs[:6])))
        out, x, query, key, value, mixed, first_low, total = refs[6 + len(after) :]
        s = Names(
            query=query,
            key=key,
            value=value,
            mixed=mixed,
            first_low=first_low,
            total=total,
            out=out,
        )
        take_rows(content, picks, seq, x)
        forward(x, w, vec, b_expand, masks.at[seq], s, False)

    return pl.pallas_call(
        kernel,
        out_shape=shaped((ROWS, D), LOW),
        in_specs=[SMEM] + [VMEM] * 11 + [ANY] * len(after),
        out_specs=VMEM,
        scratch_shapes=[pltpu.VMEM((ROWS, D), LOW)]
        + [pltpu.VMEM(*KEPT[n]) for n in ("query", "key", "value", "mixed", "first_low")]
        + [pltpu.VMEM((ROWS, D), WIDE)],
        compiler_params=limit(12),
        cost_estimate=cost(5),
        name="front",
    )(info, content, picks, masks, vec, b_expand, *matrices, *after)


def middle_forward(seq, info, content, picks, arrived, matrices, masks, vec, b_expand, after=()):
    def kernel(info, arrived, content, picks, masks, vec, b_expand, *refs):
        w, rest = Names(**dict(zip(MATRICES, refs[:6]))), refs[6 + len(after) :]
        (out, early, pair), kept = rest[:3], rest[3 : 3 + len(SAVED)]
        mixed, total = rest[3 + len(SAVED) :]
        x = pair.at[0]
        s = Names(total=total, out=out, mixed=mixed, **dict(zip(SAVED, kept)))
        take_rows(content, picks, seq, x)
        x[...] = jnp.where(info[2] == 1, x[...], arrived[...])
        early[:, :D] = x[...]
        forward(x, w, vec, b_expand, masks.at[seq], s, True)
        pair[1] = mixed[...]
        early[:, D : 2 * D] = mixed[...]
        early[:, 2 * D : 3 * D] = s.first_low[...]
        early[:, 3 * D :] = columns(s.activated, (1 - info[0]) * HALF, HALF)[...]

    out, early, pair, *saved = pl.pallas_call(
        kernel,
        out_shape=[
            shaped((ROWS, D), WIDE),
            shaped((ROWS, EARLY), LOW),
            shaped((2, ROWS, D), LOW),
        ]
        + [shaped(*KEPT[n]) for n in SAVED],
        in_specs=[SMEM] + [VMEM] * 12 + [ANY] * len(after),
        out_specs=[VMEM] * (3 + len(SAVED)),
        scratch_shapes=[pltpu.VMEM(*KEPT["mixed"]), pltpu.VMEM((ROWS, D), WIDE)],
        compiler_params=limit(16),
        cost_estimate=cost(6),
        name="middle_forward",
    )(info, arrived, content, picks, masks, vec, b_expand, *matrices, *after)
    return (out, early, pair, dict(zip(SAVED, saved)))


FEED_SAVED = ("normed2", "root2", "slope", "normed1", "root1")
ATTEND_SAVED = ("value", "probs", "key", "query")


def middle_back(seq, content, picks, matrices, vec, saved):
    names = FEED_SAVED + ATTEND_SAVED

    def kernel(content, picks, vec, *refs):
        w, rest = Names(**dict(zip(MATRICES, refs[:6]))), refs[6:]
        kept, grad, rest = rest[: len(names)], rest[len(names)], rest[len(names) + 1 :]
        cot, total, branch, expanded, attended, dmixed, dvalue, dquery, dkey = rest
        s = Names(
            total=total,
            branch=branch,
            expanded=expanded,
            attended=attended,
            dmixed=dmixed,
            dvalue=dvalue,
            dquery=dquery,
            dkey=dkey,
            **dict(zip(names, kept)),
        )
        take_rows(content, picks, seq, cot)
        back_second_norm(cot[...], vec, s)
        back_feed(w, vec, s)
        dmixed[...] = nt(attended[...], w.out[...]).astype(LOW)
        back_attend(s)
        lower = total[...] + nt(dquery[...], w.query[...])
        upper = nt(dkey[...], w.key[...]) + nt(dvalue[...], w.value[...])
        grad[:L] = (lower[:L] + upper).astype(LOW)
        grad[L:] = lower[L:].astype(LOW)

    return pl.pallas_call(
        kernel,
        out_shape=shaped((ROWS, D), LOW),
        in_specs=[VMEM] * (9 + len(names)),
        out_specs=VMEM,
        scratch_shapes=[
            pltpu.VMEM((ROWS, D), LOW),
            pltpu.VMEM((ROWS, D), WIDE),
            pltpu.VMEM((ROWS, D), LOW),
            pltpu.VMEM((ROWS, FF), LOW),
            pltpu.VMEM((ROWS, D), LOW),
            pltpu.VMEM((ROWS, D), LOW),
            pltpu.VMEM((L, D), LOW),
            pltpu.VMEM((ROWS, D), LOW),
            pltpu.VMEM((L, D), LOW),
        ],
        compiler_params=limit(12),
        cost_estimate=cost(7),
        name="middle_back",
    )(content, picks, vec, *matrices, *(saved[n] for n in names))


def feed_back(seq, info, arrived, content, picks, small_in, vec, matrices, saved, after=()):
    given = [] if small_in is None else [small_in]

    def kernel(info, arrived, content, picks, vec, expand, contract, *refs):
        kept, rest = refs[:5], refs[5 + len(given) + len(after) :]
        total, branch, attended, small, own, late, upper, expanded = rest
        w = Names(expand=expand, contract=contract)
        s = Names(
            total=total,
            branch=branch,
            attended=attended,
            expanded=expanded,
            **dict(zip(FEED_SAVED, kept)),
        )
        small[...] = refs[5][...] if given else jnp.zeros_like(small)

        def add(place, value):
            small[place : place + 1, :] += value

        take_rows(content, picks, seq, upper)
        back_second_norm(jnp.where(info[2] == 1, arrived[...], upper[...]), vec, s, add)
        late[:, :D] = branch[...]
        back_feed(w, vec, s, add)
        own[...] = columns(expanded, info[0] * HALF, HALF)[...]
        late[:, D:] = columns(expanded, (1 - info[0]) * HALF, HALF)[...]

    return pl.pallas_call(
        kernel,
        out_shape=[
            shaped((ROWS, D), WIDE),
            shaped((ROWS, D), LOW),
            shaped((ROWS, D), LOW),
            shaped((SMALL, D), WIDE),
            shaped((ROWS, HALF), LOW),
            shaped((ROWS, LATE), LOW),
        ],
        in_specs=[SMEM] + [VMEM] * (11 + len(given)) + [ANY] * len(after),
        out_specs=[VMEM] * 6,
        scratch_shapes=[pltpu.VMEM((ROWS, D), LOW), pltpu.VMEM((ROWS, FF), LOW)],
        compiler_params=limit(12),
        cost_estimate=cost(4),
        name="feed_back",
    )(
        info,
        arrived,
        content,
        picks,
        vec,
        matrices[4],
        matrices[5],
        *(saved[n] for n in FEED_SAVED),
        *given,
        *after,
    )


PLACES = {
    (2, 0): (0, 0),
    (1, 1): (0, 1),
    (2, 1): (1, 0),
    (3, 0): (1, 1),
    (1, 0): (2, 0),
    (3, 1): (3, 0),
    (0, 0): (4, 0),
    (0, 1): (4, 1),
}


def term_shapes(count):
    return [shaped((n * count, D), LOW) for n in (2, 2, 1, 1, 2)]


def feed_grads(info, mine, branch, own, early, late):
    def kernel(info, *refs):
        acts, lows, branches, owns, earlies, lates = (refs[2 * i : 2 * i + 2] for i in range(6))
        outs, (a_act, a_first, b_branch, b_own, stage, sems, out_sems) = refs[12:17], refs[17:]
        core, place = info[0], info[1]
        own_at = [slice(seq * ROWS, (seq + 1) * ROWS) for seq in range(SEQS)]
        far_at = [slice((2 + seq) * ROWS, (3 + seq) * ROWS) for seq in range(SEQS)]
        pairs, later = [], []
        for seq in range(SEQS):
            pairs += [
                (columns(acts[seq], core * HALF, HALF), a_act.at[own_at[seq]]),
                (earlies[seq].at[:, 3 * D :], a_act.at[far_at[seq]]),
                (branches[seq], b_branch.at[own_at[seq]]),
                (lates[seq].at[:, :D], b_branch.at[far_at[seq]]),
            ]
            later += [
                (lows[seq], a_first.at[own_at[seq]]),
                (earlies[seq].at[:, 2 * D : 3 * D], a_first.at[far_at[seq]]),
                (owns[seq], b_own.at[own_at[seq]]),
                (lates[seq].at[:, D:], b_own.at[far_at[seq]]),
            ]
        copies = start_all(pairs + later, sems)
        sent = []

        def send(block):
            for k in range(4):
                quarter = lax.rem(place + k, 4)
                index, part = PLACES[k, block // 2]
                start = (2 * part + block % 2) * QUARTER
                sent.extend(
                    start_all(
                        [
                            (
                                rows_at(stage.at[block], quarter * QUARTER, QUARTER),
                                outs[index].at[start : start + QUARTER],
                            )
                        ],
                        out_sems,
                        block * 4 + k,
                    )
                )

        wait_all(copies[:8])
        for block in range(2):
            for part in range(3):
                start = block * D + part * 256
                stage[block, part * 256 : (part + 1) * 256] = tn(
                    a_act[:, start : start + 256], b_branch[...]
                ).astype(LOW)
            send(block)
        wait_all(copies[8:])
        for block in range(2):
            for part in range(3):
                stage[2 + block, part * 256 : (part + 1) * 256] = tn(
                    a_first[:, part * 256 : (part + 1) * 256], b_own[:, block * D : (block + 1) * D]
                ).astype(LOW)
            send(2 + block)
        wait_all(sent)

    acts = [saved["activated"] for saved in mine]
    lows = [saved["first_low"] for saved in mine]
    return pl.pallas_call(
        kernel,
        out_shape=term_shapes(2 * QUARTER),
        in_specs=[SMEM] + [ANY] * 12,
        out_specs=[ANY] * 5,
        scratch_shapes=[
            pltpu.VMEM((2 * ALL_ROWS, HALF), LOW),
            pltpu.VMEM((2 * ALL_ROWS, D), LOW),
            pltpu.VMEM((2 * ALL_ROWS, D), LOW),
            pltpu.VMEM((2 * ALL_ROWS, HALF), LOW),
            pltpu.VMEM((4, D, D), LOW),
            DMA((16,)),
            DMA((16,)),
        ],
        compiler_params=limit(16),
        cost_estimate=cost(8),
        name="feed_grads",
    )(info, *acts, *lows, *branch, *own, *early, *late)


def attend_back(seq, info, attended, small_in, spread, after, w_out, saved):
    def kernel(info, attended, small_in, spread, w_out, *refs):
        kept, (pieces, send, small, dmixed, sums) = refs[:4], refs[4 + len(after) :]
        small[...] = small_in[...]
        pieces[1, :ROWS] = attended[...]
        dmixed[...] = nt(attended[...], w_out[...]).astype(LOW)
        s = Names(
            dmixed=dmixed,
            dquery=pieces.at[0, :ROWS],
            dkey=pieces.at[0, ROWS:],
            dvalue=pieces.at[1, ROWS:],
            **dict(zip(ATTEND_SAVED, kept)),
        )
        sums[...] = jnp.zeros_like(sums)

        def table_sum(pair, dscores):
            for odd in range(2):
                part = tn(spread[seq], dscores[odd * ROWS : (odd + 1) * ROWS])
                both = jnp.concatenate([part, jnp.zeros((L, L), WIDE)], axis=1)
                turned = pltpu.roll(both, 0, 1, stride=1, stride_axis=0)
                head = 2 * pair + odd
                sums[head : head + 1, :] = jnp.sum(turned, axis=0, keepdims=True)

        back_attend(s, table_sum)
        send[...] = pieces[1 - info[0]]
        small[S_QUERY : S_QUERY + 1, :] += column_sum(pieces[0, :ROWS])
        small[S_VALUE : S_VALUE + 1, :] += column_sum(pieces[1, ROWS:])
        distance = lax.broadcasted_iota(jnp.int32, (2 * L, L), 0) - (L - 1)
        bucket = lax.broadcasted_iota(jnp.int32, (2 * L, L), 1)
        small[S_TABLE : S_TABLE + 16, :L] += lax.dot_general(
            sums[...],
            (bucket_of(distance) == bucket).astype(WIDE),
            (((1,), (0,)), ((), ())),
            precision=lax.Precision.HIGHEST,
            preferred_element_type=WIDE,
        )

    return pl.pallas_call(
        kernel,
        out_shape=[
            shaped((2, ROWS + L, D), LOW),
            shaped((ROWS + L, D), LOW),
            shaped((SMALL, D), WIDE),
        ],
        in_specs=[SMEM] + [VMEM] * 8 + [ANY] * len(after),
        out_specs=[VMEM] * 3,
        scratch_shapes=[pltpu.VMEM((ROWS, D), LOW), pltpu.VMEM((16, 2 * L), WIDE)],
        compiler_params=limit(12),
        cost_estimate=cost(4),
        name="attend_back",
    )(info, attended, small_in, spread, w_out, *(saved[n] for n in ATTEND_SAVED), *after)


def finish_rows(info, total, output, pieces, matrices, picks, after):
    def kernel(info, *refs):
        totals, outputs, pieces = refs[0:2], refs[2:4], refs[4:6]
        (query, key, value), refs = refs[6:9], refs[9 + len(after) :]
        content_ends, query_ends, done = refs
        done[...] = jnp.zeros_like(done)
        first = info[2] == 1
        for seq in range(SEQS):
            lower = totals[seq][...] + nt(pieces[seq][0, :ROWS], query[...])
            upper = nt(pieces[seq][0, ROWS:], key[...]) + nt(pieces[seq][1, ROWS:], value[...])
            content_ends[seq * L : (seq + 1) * L] = jnp.where(
                first, lower[:L] + upper, outputs[seq][:L]
            )
            query_ends[seq * picks : (seq + 1) * picks] = jnp.where(
                first, lower[L : L + picks], outputs[seq][L : L + picks]
            )

    return pl.pallas_call(
        kernel,
        out_shape=[shaped((ALL_CONTENT, D), WIDE), shaped((SEQS * picks, D), WIDE), TOKEN],
        in_specs=[SMEM] + [VMEM] * 9 + [ANY] * len(after),
        out_specs=[VMEM] * 3,
        compiler_params=limit(12),
        cost_estimate=cost(3),
        name="finish_rows",
    )(info, *total, *output, *pieces, *matrices[:3], *after)


def attend_grads(info, pair, early, mine, arrived, small, after=()):
    def kernel(info, small, *refs):
        pairs_in, earlies, mines, arriveds = (refs[2 * i : 2 * i + 2] for i in range(4))
        refs = refs[8 + len(after) :]
        outs, rest = refs[:5], refs[5:]
        a_rows, a_content, b_rows, b_content, stage, extra, sems, out_sems = rest
        core, place = info[0], info[1]
        pairs, later = [], []
        for seq in range(SEQS):
            at = slice(seq * ROWS, (seq + 1) * ROWS)
            far = slice((2 + seq) * ROWS, (3 + seq) * ROWS)
            pairs += [
                (pairs_in[seq].at[core], a_rows.at[at]),
                (columns(earlies[seq], core * D, D), a_rows.at[far]),
                (mines[seq].at[core, :ROWS], b_rows.at[at]),
                (arriveds[seq].at[:ROWS], b_rows.at[far]),
            ]
            at = slice(seq * L, (seq + 1) * L)
            far = slice((2 + seq) * L, (3 + seq) * L)
            later += [
                (pairs_in[seq].at[0, :L], a_content.at[at]),
                (earlies[seq].at[:L, :D], a_content.at[far]),
                (mines[seq].at[core, ROWS:], b_content.at[at]),
                (arriveds[seq].at[ROWS:], b_content.at[far]),
            ]
        copies = start_all(pairs + later, sems)
        blank = jnp.zeros((EXTRA, D), WIDE)
        extra[0] = jnp.concatenate([small[...], blank[SMALL:]]).astype(LOW)
        extra[1] = blank.astype(LOW)
        sent = []
        for block, (former, latter) in enumerate(((a_rows, b_rows), (a_content, b_content))):
            wait_all(copies[8 * block : 8 * block + 8])
            for part in range(3):
                stage[block, part * 256 : (part + 1) * 256] = tn(
                    former[:, part * 256 : (part + 1) * 256], latter[...]
                ).astype(LOW)
            for k in range(4):
                quarter = lax.rem(place + k, 4)
                index, part = PLACES[k, block]
                start = part * (QUARTER + EXTRA)
                middle, stop = start + QUARTER, start + QUARTER + EXTRA
                sent += start_all(
                    [
                        (
                            rows_at(stage.at[block], quarter * QUARTER, QUARTER),
                            outs[index].at[start:middle],
                        ),
                        (extra.at[block], outs[index].at[middle:stop]),
                    ],
                    out_sems,
                    block * 8 + 2 * k,
                )
        wait_all(sent)

    return pl.pallas_call(
        kernel,
        out_shape=term_shapes(QUARTER + EXTRA),
        in_specs=[SMEM, VMEM] + [ANY] * (8 + len(after)),
        out_specs=[ANY] * 5,
        scratch_shapes=[
            pltpu.VMEM((2 * ALL_ROWS, D), LOW),
            pltpu.VMEM((2 * ALL_CONTENT, D), LOW),
            pltpu.VMEM((2 * ALL_ROWS, D), LOW),
            pltpu.VMEM((2 * ALL_CONTENT, D), LOW),
            pltpu.VMEM((2, D, D), LOW),
            pltpu.VMEM((2, EXTRA, D), LOW),
            DMA((16,)),
            DMA((16,)),
        ],
        compiler_params=limit(12),
        cost_estimate=cost(5),
        name="attend_grads",
    )(info, small, *pair, *early, *mine, *arrived, *after)


def small_kernel(body, name, shapes, inputs, after=(), info=None, through=()):
    first = [] if info is None else [info]
    given = len(first) + len(inputs)

    def kernel(*refs):
        outs = refs[given + len(after) + len(through) :]
        body(*refs[:given], *outs[: len(shapes)])

    return pl.pallas_call(
        kernel,
        out_shape=[shaped(shape, LOW) for shape in shapes]
        + [shaped(array.shape, array.dtype) for array in through],
        in_specs=[SMEM] * len(first)
        + [VMEM] * len(inputs)
        + [ANY] * (len(after) + len(through)),
        out_specs=[VMEM] * len(shapes) + [ANY] * len(through),
        input_output_aliases={
            given + len(after) + i: len(shapes) + i for i in range(len(through))
        },
        compiler_params=limit(8),
        cost_estimate=cost(1),
        name=name,
    )(*first, *inputs, *after, *through)


def total_of(*terms):
    return sum(term.astype(WIDE) for term in terms).astype(LOW)


def ring_add(after0, before1, from_left, from_right, after=()):
    count = after0.shape[0]

    def body(after0, before1, from_left, from_right, right, left):
        right[...] = total_of(after0[...], from_left[:count])
        left[...] = total_of(before1[...], from_right[:count])

    return small_kernel(
        body, "ring_add", [after0.shape] * 2, (after0, before1, from_left, from_right), after
    )


def ring_sum(info, own, left, right, from_left, from_right, after=()):
    count = left.shape[0]
    part = count // 4

    def body(info, own, left, right, from_left, from_right, *outs):
        for k, out in enumerate(outs):
            at = pl.multiple_of(lax.rem(info[3] + k, 4) * part, 16)
            low, high = pl.ds(at, part), pl.ds(at + count, part)
            out[:part] = total_of(own[low], left[low], from_right[high])
            out[part:] = total_of(own[high], from_left[high], right[low])

    return small_kernel(
        body,
        "ring_sum",
        [(2 * part, D)] * 4,
        (own, left, right, from_left, from_right),
        after,
        info,
    )


def add_all(name, terms, after=()):
    def body(*refs):
        refs[-1][...] = total_of(*(ref[...] for ref in refs[:-1]))

    return small_kernel(body, name, [terms[0].shape], terms, after)[0]


def inner_join(info, parts, after=(), through=()):
    part = parts[0].shape[0] // 2

    def body(info, *refs):
        whole = refs[-1]
        for k, ref in enumerate(refs[:-1]):
            at = pl.multiple_of(lax.rem(info[3] + k, 4) * part, 16)
            whole[pl.ds(at, part)] = ref[:part]
            whole[pl.ds(at + 4 * part, part)] = ref[part:]

    return small_kernel(body, "inner_join", [(8 * part, D)], parts, after, info, through)


def cut(arrays, after=()):
    rows = arrays[0].shape[0]
    count = rows // 2

    def body(*refs):
        arrays, (right, left, whole) = refs[:-3], refs[-3:]
        right[...] = arrays[0][:count]
        left[...] = arrays[1][count:]
        for index, ref in enumerate(arrays):
            whole[index * rows : (index + 1) * rows] = ref[...]

    shapes = [(count, D), (count, D), (len(arrays) * rows, D)]
    return small_kernel(body, "cut", shapes, arrays, after)


def feed_targets(outs, source, half, core, quarter):
    pairs = []
    for block in range(2):
        part = source.at[block * QUARTER : (block + 1) * QUARTER]
        if half == 0:
            target = rows_at(outs[0], core * HALF + block * D + quarter * QUARTER, QUARTER)
        else:
            target = columns(
                rows_at(outs[1], quarter * QUARTER, QUARTER), (core * 2 + block) * D, D
            )
        pairs.append((None, part, target))
    return pairs


def attend_targets(outs, source, half, core, quarter):
    return [
        (
            core == number,
            source.at[:QUARTER],
            rows_at(outs[2 * number + half], quarter * QUARTER, QUARTER),
        )
        for number in range(2)
    ]


def settle(targets, shapes, count, info, pieces, outs, name, after=()):
    keys = tuple(pieces)
    arrays = [pieces[key] for key in keys]
    given = list(after) + list(outs or ())

    def kernel(info, *refs):
        parts, rest = refs[: len(keys)], refs[len(keys) + len(given) :]
        outs, rest = rest[: len(shapes)], rest[len(shapes) :]
        done, rest = rest[0], rest[1:]
        done[...] = jnp.zeros_like(done)
        held, wide_held, (sems, out_sems) = rest[: len(keys)], rest[len(keys) : -2], rest[-2:]
        copies = start_all(list(zip(parts, held)), sems)
        finish = []
        for index, (sibling, places) in enumerate(keys):
            core = 1 - info[0] if sibling else info[0]
            copies[index].wait()
            for number, (k, half) in enumerate(places):
                quarter = lax.rem((info[3] if sibling else info[1]) + k, 4)
                source = wide_held[index].at[number * count : (number + 1) * count]
                source[...] = held[index][number * count : (number + 1) * count].astype(WIDE)
                for place, (condition, part, target) in enumerate(
                    targets(outs, source, half, core, quarter)
                ):
                    copy = pltpu.make_async_copy(
                        part, target, out_sems.at[12 * index + 2 * number + place]
                    )
                    if condition is None:
                        copy.start()
                        finish.append(copy.wait)
                    else:
                        pl.when(condition)(copy.start)
                        finish.append(lambda c=copy, when=condition: pl.when(when)(c.wait))
        for action in finish:
            action()

    result = pl.pallas_call(
        kernel,
        out_shape=[shaped(shape, WIDE) for shape in shapes]
        + [TOKEN],
        in_specs=[SMEM] + [ANY] * (len(keys) + len(given)),
        out_specs=[ANY] * len(shapes) + [VMEM],
        scratch_shapes=[pltpu.VMEM(array.shape, LOW) for array in arrays]
        + [pltpu.VMEM(array.shape, WIDE) for array in arrays]
        + [DMA((len(keys),)), DMA((12 * len(keys),))],
        input_output_aliases={
            1 + len(keys) + len(after) + i: i for i in range(len(outs or ()))
        },
        compiler_params=limit(32),
        cost_estimate=cost(sum(array.size for array in arrays) * 2e-6 + 1),
        name=name,
    )(info, *arrays, *given)
    return result[:-1], result[-1]


PLANE = ("x", "y", "c")


def shift(value, axis, by):
    size = lax.axis_size(axis)
    return lax.ppermute(value, axis, [(i, (i + by) % size) for i in range(size)])


def send(value, by):
    return lax.ppermute(value, "s", [(0, 1)] if by > 0 else [(1, 0)])


def turn(value, outer, by):
    pairs = []
    for i in range(4):
        for j in range(4):
            for c in range(2):
                if (c == 0) == outer:
                    target = ((i + by) % 4, j)
                else:
                    target = (i, (j + by) % 4)
                pairs.append(((i * 4 + j) * 2 + c, (target[0] * 4 + target[1]) * 2 + c))
    return lax.ppermute(value, PLANE, pairs)


def place(outer):
    return jnp.where(
        (lax.axis_index("c") == 0) == outer, lax.axis_index("x"), lax.axis_index("y")
    )


def wide(value):
    return value.astype(WIDE)


def total_wide(*terms):
    return sum(wide(term) for term in terms)


def inner_turns(parts, sign):
    return [turn(part, False, sign * by) for part, by in zip(parts, (1, 2, -1))]


OWN, ACROSS = ((0, 0), (0, 1)), (((2, 0),), ((2, 1),))
NEAR = ((3, 0), (3, 1), (1, 0), (1, 1))


def both_cores(places, piece):
    return {(0, places): piece, (1, places): shift(piece, "c", 1)}


def on_device(
    content_in,
    query_in,
    content_cot,
    query_cot,
    order_rank,
    query_pos,
    group_tag,
    *rest,
):
    (
        w_query,
        b_query,
        w_key,
        w_value,
        b_value,
        w_out,
        b_out,
        norm1_gain,
        norm1_bias,
        w_expand,
        b_expand,
        w_contract,
        b_contract,
        norm2_gain,
        norm2_bias,
    ) = (argument[0] for argument in rest[:-1])
    rel_table = rest[-1]
    core = lax.axis_index("c")
    first_section = (lax.axis_index("s") == 0).astype(jnp.int32)
    info = jnp.stack([core, place(True), first_section, place(False)])
    picks = query_pos.shape[1]

    matrices = (w_query, w_key, w_value, w_out, w_expand, w_contract)
    w_out_held = w_out
    vec = jnp.stack(
        [b_query, b_value, b_out, norm1_gain, norm1_bias, b_contract, norm2_gain, norm2_bias]
    )
    ranks = jnp.concatenate([order_rank, group_tag, query_pos], axis=1)
    masks, spread, query_in, query_cot = prepare(
        ranks, rel_table, query_in, query_cot, picks, (vec, info)
    )
    b_expand = b_expand[None]

    fronts, arrived = [], []
    for seq in range(SEQS):
        fronts.append(
            front(seq, info, content_in, query_in, matrices, masks, vec, b_expand, tuple(fronts))
        )
        arrived.append(send(fronts[seq], 1))
    output, early, pair, saved, grads = [], [], [], [], []
    for seq in range(SEQS):
        results = middle_forward(
            seq, info, content_in, query_in, arrived[seq], matrices, masks, vec, b_expand, tuple(grads)
        )
        for collected, result in zip((output, early, pair, saved), results):
            collected.append(result)
        grads.append(middle_back(seq, content_cot, query_cot, matrices, vec, saved[seq]))
    early = [shift(value, "c", 1) for value in early]
    grads = [send(value, -1) for value in grads]
    small = None
    total, branch, attended, own, late, pieces, pass_on = [], [], [], [], [], [], []
    for seq in range(SEQS):
        results = feed_back(
            seq,
            info,
            grads[seq],
            content_cot,
            query_cot,
            small,
            vec,
            matrices,
            saved[seq],
            tuple(pass_on),
        )
        small = results[3]
        for collected, result in zip(
            (total, branch, attended, own, late), results[:3] + results[4:]
        ):
            collected.append(result)
        if seq == 0:
            late[0] = shift(late[0], "c", 1)
        else:
            late[1] = shift(late[1], "c", 1)
            feed_terms = feed_grads(info, saved, branch, own, early, late)
        results = attend_back(
            seq,
            info,
            attended[seq],
            small,
            spread,
            () if seq == 0 else (feed_terms[4],),
            w_out_held,
            saved[seq],
        )
        small = results[2]
        pieces.append(results[0])
        pass_on.append(results[1])
    passed = [shift(value, "c", 1) for value in pass_on]

    def outer_step(terms):
        return (turn(terms[0], True, 1), turn(terms[1], True, -1))

    f_left, f_right = outer_step(feed_terms)
    content_ends, query_ends, token = finish_rows(
        info, total, output, pieces, matrices, picks, (feed_terms[4],)
    )
    f_sent = ring_add(feed_terms[2], feed_terms[3], f_left, f_right, (token,))
    attend_terms = attend_grads(info, pair, early, pieces, passed, small, tuple(f_sent))
    a_left, a_right = outer_step(attend_terms)
    f_outer = outer_step(f_sent)
    f_parts = ring_sum(info, feed_terms[4], *f_outer, f_left, f_right, (attend_terms[2],))
    f_part = add_all("inner_sum", [f_parts[0]] + inner_turns(f_parts[1:], 1))
    f_far = shift(f_part, "z", 1)
    a_sent = ring_add(attend_terms[2], attend_terms[3], a_left, a_right, (f_part,))
    a_outer = outer_step(a_sent)
    f_part = add_all("z_sum", [f_part, f_far])
    a_parts = ring_sum(info, attend_terms[4], *a_outer, a_left, a_right, (f_part,))
    f_others = inner_turns([f_part] * 3, -1)
    a_part = add_all("inner_sum", [a_parts[0]] + inner_turns(a_parts[1:], 1))
    (feed_own,) = inner_join(info, [f_part] + f_others, (a_part,))
    feed_outer = (turn(feed_own, True, 1), turn(feed_own, True, -1))
    a_part = add_all("z_sum", [a_part, shift(a_part, "z", 1)])
    a_others = inner_turns([a_part] * 3, -1)

    def feed_settle(pieces, outs, name):
        return settle(
            feed_targets, ((FF, D), (D, FF)), 2 * QUARTER, info, pieces, outs, "feed_" + name
        )

    def attend_settle(pieces, outs, name, after=()):
        return settle(
            attend_targets,
            ((D, D),) * 4,
            QUARTER + EXTRA,
            info,
            pieces,
            outs,
            "attend_" + name,
            after,
        )

    feed_outs, token = feed_settle(both_cores(OWN, feed_own), None, "own")
    to_right, to_left, feed_near = cut(feed_outer, (token, *a_others))
    feed_across = (turn(to_right, True, 1), turn(to_left, True, -1))
    (attend_own,) = inner_join(info, [a_part] + a_others, (to_right,))
    attend_outer = (turn(attend_own, True, 1), turn(attend_own, True, -1))
    feed_outs, token = feed_settle(both_cores(NEAR, feed_near), feed_outs, "near")
    to_right, to_left, attend_near = cut((*attend_outer, attend_own), (token, *feed_across))
    attend_across = (turn(to_right, True, 1), turn(to_left, True, -1))
    feed_outs, _ = feed_settle(
        both_cores(ACROSS[0], feed_across[0]) | both_cores(ACROSS[1], feed_across[1]),
        feed_outs,
        "across",
    )
    attend_both = both_cores(NEAR + OWN, attend_near)
    attend_outs, _ = attend_settle(attend_both, None, "near")
    attend_outs, _ = attend_settle(
        both_cores(ACROSS[0], attend_across[0]) | both_cores(ACROSS[1], attend_across[1]),
        attend_outs,
        "across",
    )
    contract, expand = feed_outs
    g_query, g_key, g_out, g_value = attend_outs
    start = 4 * (QUARTER + EXTRA) + QUARTER
    small_sum = total_wide(*(piece[start : start + SMALL] for piece in attend_both.values()))
    table = small_sum[S_TABLE : S_TABLE + H, :L]
    table_total = (table + shift(table, "s", 1))[:, :NB].T
    row = lambda k: small_sum[k][None]
    return (
        content_ends[None],
        query_ends[None],
        g_query[None],
        row(S_QUERY),
        g_key[None],
        g_value[None],
        row(S_VALUE),
        g_out[None],
        row(S_OUT),
        row(S_GAIN1),
        row(S_SHIFT1),
        expand[None],
        small_sum[S_EXPAND : S_EXPAND + 4].reshape(1, FF),
        contract[None],
        row(S_CONTRACT),
        row(S_GAIN2),
        row(S_SHIFT2),
        table_total,
    )


DP = ("z", "x", "y", "c")


def solution(mesh):
    mesh = jax.sharding.Mesh(mesh.devices.reshape(2, 2, 4, 4, 2), ("s",) + DP)
    layer_specs = tuple(
        P("s", *([None] * (rank - 1))) for rank in (3, 2, 3, 3, 2, 3, 2, 2, 2, 3, 2, 3, 2, 2, 2)
    )
    in_specs = (P(DP, None),) * 7 + layer_specs + (P(),)
    out_specs = (P("s", DP, None),) * 2 + layer_specs + (P(),)
    return jax.shard_map(
        on_device, mesh=mesh, in_specs=in_specs, out_specs=out_specs, check_vma=False
    )
```

```python
import jax
import jax.numpy as jnp
from jax import lax
from jax.experimental import pallas as pl
from jax.experimental.pallas import tpu as pltpu
from jax.sharding import PartitionSpec as P

D = 768
H = 12
HD = 64
FF = 3072
NB = 32
L = 128
PAIRS = H // 2
SEQS = 2
PICKS = 32
ROWS = L + PICKS
EPSILON = 1e-05
SCALE = HD ** (-0.5)
TILE = 1536
LOW = jnp.bfloat16
WIDE = jnp.float32
HALF = FF // 2
QUARTER = D // 4
EARLY = 3 * D + HALF
LATE = D + HALF
EXTRA = 64
SMALL = 32
ALL_ROWS = SEQS * ROWS
ALL_CONTENT = SEQS * L
PIECE = ALL_ROWS + ALL_CONTENT


def nn(former, latter):
    return lax.dot_general(
        former, latter, (((1,), (0,)), ((), ())), preferred_element_type=WIDE
    )


def nt(former, latter):
    return lax.dot_general(
        former, latter, (((1,), (1,)), ((), ())), preferred_element_type=WIDE
    )


def tn(former, latter):
    return lax.dot_general(
        former, latter, (((0,), (0,)), ((), ())), preferred_element_type=WIDE
    )


def halves(value):
    even = lax.broadcasted_iota(jnp.int32, value.shape, 1) < HD
    zero = jnp.zeros_like(value)
    return jnp.concatenate([jnp.where(even, value, zero), jnp.where(even, zero, value)])


def side(value):
    count = value.shape[0] // 2
    return jnp.concatenate([value[:count], value[count:]], axis=1)


def norm_rows(values):
    centered = values - jnp.mean(values, axis=-1, keepdims=True)
    variance = jnp.mean(centered * centered, axis=-1, keepdims=True)
    root = lax.rsqrt(variance + EPSILON)
    return (centered * root, root)


def norm_rows_back(scaled, normed, root):
    return root * (
        scaled
        - jnp.mean(scaled, axis=-1, keepdims=True)
        - normed * jnp.mean(scaled * normed, axis=-1, keepdims=True)
    )


B_QUERY, B_VALUE, B_OUT, GAIN1, SHIFT1, B_CONTRACT, GAIN2, SHIFT2 = range(8)
S_QUERY, S_VALUE, S_OUT, S_GAIN1, S_SHIFT1, S_EXPAND = range(6)
S_CONTRACT, S_GAIN2, S_SHIFT2, S_TABLE = 9, 10, 11, 16
LIMITS = (12, 16, 23, 32, 46, 64, 91)


def bucket_of(relative):
    distance = jnp.abs(relative)
    beyond = 8 + sum((distance >= limit).astype(jnp.int32) for limit in LIMITS)
    within = jnp.where(distance < 8, distance, beyond)
    return within + 16 * (relative > 0).astype(jnp.int32)


def forward(x, w, vec, b_expand, masks, s, keep):
    row = lambda k: vec[k : k + 1, :]
    s.query[...] = (nn(x[...], w.query[...]) + row(B_QUERY)).astype(LOW)
    s.key[...] = nn(x[:L], w.key[...]).astype(LOW)
    s.value[...] = (nn(x[:L], w.value[...]) + row(B_VALUE)).astype(LOW)
    for pair in range(PAIRS):
        lanes = slice(pair * 128, (pair + 1) * 128)
        scores = nt(halves(s.query[:, lanes]), s.key[:, lanes]) * SCALE + masks[pair]
        shifted = jnp.exp(scores - jnp.max(scores, axis=-1, keepdims=True))
        probs = (shifted / jnp.sum(shifted, axis=-1, keepdims=True)).astype(LOW)
        if keep:
            s.probs[pair] = probs
        s.mixed[:, lanes] = nn(side(probs), halves(s.value[:, lanes])).astype(LOW)
    total = x[...].astype(WIDE) + nn(s.mixed[...], w.out[...]) + row(B_OUT)
    normed, root = norm_rows(total)
    first = normed * row(GAIN1) + row(SHIFT1)
    s.first_low[...] = first.astype(LOW)
    s.total[...] = first + row(B_CONTRACT)
    if keep:
        s.normed1[...] = normed
        s.root1[...] = jnp.broadcast_to(root, (ROWS, 128))
    for tile in range(FF // TILE):
        tile = slice(tile * TILE, (tile + 1) * TILE)
        expanded = nn(s.first_low[...], w.expand[:, tile]) + b_expand[:, tile]
        cumulative = 0.5 * (1.0 + lax.erf(expanded * 0.7071067811865476))
        activated = (expanded * cumulative).astype(LOW)
        if keep:
            s.slope[:, tile] = (
                cumulative + expanded * jnp.exp(-0.5 * expanded * expanded) * 0.3989422804014327
            ).astype(LOW)
            s.activated[:, tile] = activated
        s.total[...] += nn(activated, w.contract[tile, :])
    normed, root = norm_rows(s.total[...])
    if keep:
        s.normed2[...] = normed
        s.root2[...] = jnp.broadcast_to(root, (ROWS, 128))
    s.out[...] = (normed * row(GAIN2) + row(SHIFT2)).astype(s.out.dtype)


def column_sum(value):
    return jnp.sum(value.astype(WIDE), axis=0, keepdims=True)


def back_second_norm(grad, vec, s, add=None):
    upper = grad.astype(WIDE)
    normed = s.normed2[...]
    lower = norm_rows_back(upper * vec[GAIN2 : GAIN2 + 1, :], normed, s.root2[:, :1])
    s.total[...] = lower
    s.branch[...] = lower.astype(LOW)
    if add is not None:
        add(S_GAIN2, column_sum(upper * normed))
        add(S_SHIFT2, column_sum(upper))
        add(S_CONTRACT, column_sum(lower.astype(LOW)))


def back_feed(w, vec, s, add=None):
    for tile in range(FF // TILE):
        tile = slice(tile * TILE, (tile + 1) * TILE)
        lower = (nt(s.branch[...], w.contract[tile, :]) * s.slope[:, tile].astype(WIDE)).astype(LOW)
        s.expanded[:, tile] = lower
        if add is not None:
            part = column_sum(lower)
            for column in range(TILE // D):
                add(
                    S_EXPAND + tile.start // D + column,
                    part[:, column * D : (column + 1) * D],
                )
        s.total[...] += nt(lower, w.expand[:, tile])
    upper = s.total[...]
    normed = s.normed1[...]
    lower = norm_rows_back(upper * vec[GAIN1 : GAIN1 + 1, :], normed, s.root1[:, :1])
    s.total[...] = lower
    s.attended[...] = lower.astype(LOW)
    if add is not None:
        add(S_GAIN1, column_sum(upper * normed))
        add(S_SHIFT1, column_sum(upper))
        add(S_OUT, column_sum(lower.astype(LOW)))


def back_attend(s, table=None):
    for pair in range(PAIRS):
        lanes = slice(pair * 128, (pair + 1) * 128)
        probs = s.probs[pair]
        below = halves(s.dmixed[:, lanes])
        dprobs = nt(below, s.value[:, lanes])
        s.dvalue[:, lanes] = tn(probs, below).astype(LOW)
        weight = probs.astype(WIDE)
        dscores = (
            weight * (dprobs - jnp.sum(weight * dprobs, axis=-1, keepdims=True))
        ).astype(LOW)
        s.dquery[:, lanes] = (nn(side(dscores), halves(s.key[:, lanes])) * SCALE).astype(LOW)
        s.dkey[:, lanes] = (tn(dscores, halves(s.query[:, lanes])) * SCALE).astype(LOW)
        if table is not None:
            table(pair, dscores)


class Names:
    def __init__(self, **named):
        self.__dict__.update(named)


MATRICES = ("query", "key", "value", "out", "expand", "contract")
MATRIX_SHAPES = {
    "query": (D, D),
    "key": (D, D),
    "value": (D, D),
    "out": (D, D),
    "expand": (D, FF),
    "contract": (FF, D),
}
MASK_SHAPE = (PAIRS, 2 * ROWS, L)
KEPT = {
    "query": ((ROWS, D), LOW),
    "key": ((L, D), LOW),
    "value": ((L, D), LOW),
    "probs": (MASK_SHAPE, LOW),
    "mixed": ((ROWS, D), LOW),
    "normed1": ((ROWS, D), WIDE),
    "root1": ((ROWS, 128), WIDE),
    "first_low": ((ROWS, D), LOW),
    "slope": ((ROWS, FF), LOW),
    "activated": ((ROWS, FF), LOW),
    "normed2": ((ROWS, D), WIDE),
    "root2": ((ROWS, 128), WIDE),
}
SAVED = tuple(name for name in KEPT if name != "mixed")
ANY = pl.BlockSpec(memory_space=pl.ANY)
VMEM = pl.BlockSpec(memory_space=pltpu.VMEM)
SMEM = pl.BlockSpec(memory_space=pltpu.SMEM)


def limit(megabytes):
    return pltpu.CompilerParams(vmem_limit_bytes=megabytes * 1024 * 1024)


DMA = pltpu.SemaphoreType.DMA


def cost(microseconds):
    return pl.CostEstimate(flops=0, bytes_accessed=int(microseconds * 3.2e6), transcendentals=0)


def shaped(shape, kind):
    return jax.ShapeDtypeStruct(shape, kind)


TOKEN = shaped((8, 128), WIDE)


def columns(ref, start, size):
    return ref.at[:, pl.ds(pl.multiple_of(start, 128), size)]


def rows_at(ref, start, size):
    return ref.at[pl.ds(pl.multiple_of(start, 64), size)]


def start_all(pairs, sems, base=0):
    copies = [
        pltpu.make_async_copy(source, target, sems.at[base + index])
        for index, (source, target) in enumerate(pairs)
    ]
    for copy in copies:
        copy.start()
    return copies


def wait_all(copies):
    for copy in copies:
        copy.wait()


def fetcher(names, sources, targets, sems, base=0):
    copies = dict(zip(names, start_all(list(zip(sources, targets)), sems, base)))
    return lambda name: copies[name].wait()


def prepare(ranks, table, query_in, query_cot, picks, after):
    def kernel(ranks, table, query_in, query_cot, *refs):
        masks, spread, rows_in, rows_cot = refs[len(after) :]
        order, tag, pos = ranks[:, :L], ranks[:, L : 2 * L], ranks[:, 2 * L : 2 * L + picks]
        for source, target in ((query_in, rows_in), (query_cot, rows_cot)):
            values = source[...].astype(WIDE)
            blank = jnp.zeros((PICKS - picks, D), WIDE)
            target[...] = jnp.concatenate(
                [values[:picks], blank, values[picks:], blank]
            ).astype(LOW)
        lane = lax.broadcasted_iota(jnp.int32, (L, L), 1)
        level = lax.broadcasted_iota(jnp.int32, (L, L), 0)
        lane_q = lax.broadcasted_iota(jnp.int32, (PICKS, L), 1)
        upright = lambda row: jnp.sum(jnp.where(lane == level, row, 0.0), axis=1, keepdims=True)
        distance = lax.broadcasted_iota(jnp.int32, (2 * L, NB), 0) - (L - 1)
        bucket = lax.broadcasted_iota(jnp.int32, (2 * L, NB), 1)
        by_distance = lax.dot_general(
            table[...],
            (bucket_of(distance) == bucket).astype(WIDE),
            (((0,), (1,)), ((), ())),
            precision=lax.Precision.HIGHEST,
            preferred_element_type=WIDE,
        )
        allowed, hot = [], []
        for seq in range(SEQS):
            own_rank = order[seq : seq + 1, :].astype(WIDE)
            own_tag = tag[seq : seq + 1, :].astype(WIDE)
            own_pos = pos[seq : seq + 1, :].astype(WIDE)
            number = lax.broadcasted_iota(jnp.int32, (PICKS, picks), 0)
            same = number == lax.broadcasted_iota(jnp.int32, (PICKS, picks), 1)
            place = jnp.sum(jnp.where(same, own_pos, 0.0), axis=1, keepdims=True)
            filled = lax.broadcasted_iota(jnp.int32, (PICKS, 1), 0) < picks
            place = jnp.where(filled, place, -1.0).astype(jnp.int32)
            matches = place == lane_q
            marks = jnp.where(matches, 1.0, 0.0)
            predicted = jnp.max(marks, axis=0, keepdims=True)
            rank = jnp.sum(jnp.where(matches, own_rank, 0.0), axis=1, keepdims=True)
            group = jnp.sum(jnp.where(matches, own_tag, 0.0), axis=1, keepdims=True)
            earlier = (upright(predicted) > 0) & (own_rank <= upright(own_rank))
            content = (upright(own_tag) == own_tag) & ((predicted == 0) | earlier)
            query = (group == own_tag) & ((predicted == 0) | (own_rank + 1 <= rank))
            allowed.append((content, query))
            hot.append(marks)
            spread[seq, :L] = jnp.where(lane == L - 1 - level, 1.0, 0.0).astype(LOW)
            spread[seq, L:] = jnp.where(lane_q == L - 1 - place, 1.0, 0.0).astype(LOW)
        hot = jnp.concatenate(hot)
        for head in range(H):
            row = jnp.broadcast_to(by_distance[head : head + 1], (L, 2 * L))
            bias = pltpu.roll(row, L + 1, 1, stride=1, stride_axis=0)[:, :L]
            bias_q = lax.dot_general(
                hot,
                bias,
                (((1,), (0,)), ((), ())),
                precision=lax.Precision.HIGHEST,
                preferred_element_type=WIDE,
            )
            base = head % 2 * ROWS
            for seq in range(SEQS):
                content, query = allowed[seq]
                masks[seq, head // 2, base : base + L] = jnp.where(content, bias, -1e30)
                masks[seq, head // 2, base + L : base + ROWS] = jnp.where(
                    query, bias_q[seq * PICKS : (seq + 1) * PICKS], -1e30
                )

    return pl.pallas_call(
        kernel,
        out_shape=[
            shaped((SEQS,) + MASK_SHAPE, WIDE),
            shaped((SEQS, ROWS, L), LOW),
            shaped((SEQS * PICKS, D), LOW),
            shaped((SEQS * PICKS, D), LOW),
        ],
        in_specs=[VMEM] * 4 + [ANY] * len(after),
        out_specs=[VMEM] * 4,
        compiler_params=limit(8),
        cost_estimate=pl.CostEstimate(flops=int(3e10), bytes_accessed=0, transcendentals=0),
        name="prepare",
    )(ranks, table, query_in, query_cot, *after)


def take_rows(content, picks, seq, target):
    target[:L] = content[seq * L : (seq + 1) * L]
    target[L:] = picks[seq * PICKS : (seq + 1) * PICKS]


def front(seq, info, content, picks, matrices, masks, vec, b_expand, after=()):
    def kernel(info, content, picks, masks, vec, b_expand, *refs):
        w = Names(**dict(zip(MATRICES, refs[:6])))
        out, x, query, key, value, mixed, first_low, total = refs[6 + len(after) :]
        s = Names(
            query=query,
            key=key,
            value=value,
            mixed=mixed,
            first_low=first_low,
            total=total,
            out=out,
        )
        take_rows(content, picks, seq, x)
        forward(x, w, vec, b_expand, masks.at[seq], s, False)

    return pl.pallas_call(
        kernel,
        out_shape=shaped((ROWS, D), LOW),
        in_specs=[SMEM] + [VMEM] * 11 + [ANY] * len(after),
        out_specs=VMEM,
        scratch_shapes=[pltpu.VMEM((ROWS, D), LOW)]
        + [pltpu.VMEM(*KEPT[n]) for n in ("query", "key", "value", "mixed", "first_low")]
        + [pltpu.VMEM((ROWS, D), WIDE)],
        compiler_params=limit(12),
        cost_estimate=cost(5),
        name="front",
    )(info, content, picks, masks, vec, b_expand, *matrices, *after)


def middle_forward(seq, info, content, picks, arrived, matrices, masks, vec, b_expand, after=()):
    def kernel(info, arrived, content, picks, masks, vec, b_expand, *refs):
        w, rest = Names(**dict(zip(MATRICES, refs[:6]))), refs[6 + len(after) :]
        (out, early, pair), kept = rest[:3], rest[3 : 3 + len(SAVED)]
        mixed, total = rest[3 + len(SAVED) :]
        x = pair.at[0]
        s = Names(total=total, out=out, mixed=mixed, **dict(zip(SAVED, kept)))
        take_rows(content, picks, seq, x)
        x[...] = jnp.where(info[2] == 1, x[...], arrived[...])
        early[:, :D] = x[...]
        forward(x, w, vec, b_expand, masks.at[seq], s, True)
        pair[1] = mixed[...]
        early[:, D : 2 * D] = mixed[...]
        early[:, 2 * D : 3 * D] = s.first_low[...]
        early[:, 3 * D :] = columns(s.activated, (1 - info[0]) * HALF, HALF)[...]

    out, early, pair, *saved = pl.pallas_call(
        kernel,
        out_shape=[
            shaped((ROWS, D), WIDE),
            shaped((ROWS, EARLY), LOW),
            shaped((2, ROWS, D), LOW),
        ]
        + [shaped(*KEPT[n]) for n in SAVED],
        in_specs=[SMEM] + [VMEM] * 12 + [ANY] * len(after),
        out_specs=[VMEM] * (3 + len(SAVED)),
        scratch_shapes=[pltpu.VMEM(*KEPT["mixed"]), pltpu.VMEM((ROWS, D), WIDE)],
        compiler_params=limit(16),
        cost_estimate=cost(6),
        name="middle_forward",
    )(info, arrived, content, picks, masks, vec, b_expand, *matrices, *after)
    return (out, early, pair, dict(zip(SAVED, saved)))


FEED_SAVED = ("normed2", "root2", "slope", "normed1", "root1")
ATTEND_SAVED = ("value", "probs", "key", "query")


def middle_back(seq, content, picks, matrices, vec, saved):
    names = FEED_SAVED + ATTEND_SAVED

    def kernel(content, picks, vec, *refs):
        w, rest = Names(**dict(zip(MATRICES, refs[:6]))), refs[6:]
        kept, grad, rest = rest[: len(names)], rest[len(names)], rest[len(names) + 1 :]
        cot, total, branch, expanded, attended, dmixed, dvalue, dquery, dkey = rest
        s = Names(
            total=total,
            branch=branch,
            expanded=expanded,
            attended=attended,
            dmixed=dmixed,
            dvalue=dvalue,
            dquery=dquery,
            dkey=dkey,
            **dict(zip(names, kept)),
        )
        take_rows(content, picks, seq, cot)
        back_second_norm(cot[...], vec, s)
        back_feed(w, vec, s)
        dmixed[...] = nt(attended[...], w.out[...]).astype(LOW)
        back_attend(s)
        lower = total[...] + nt(dquery[...], w.query[...])
        upper = nt(dkey[...], w.key[...]) + nt(dvalue[...], w.value[...])
        grad[:L] = (lower[:L] + upper).astype(LOW)
        grad[L:] = lower[L:].astype(LOW)

    return pl.pallas_call(
        kernel,
        out_shape=shaped((ROWS, D), LOW),
        in_specs=[VMEM] * (9 + len(names)),
        out_specs=VMEM,
        scratch_shapes=[
            pltpu.VMEM((ROWS, D), LOW),
            pltpu.VMEM((ROWS, D), WIDE),
            pltpu.VMEM((ROWS, D), LOW),
            pltpu.VMEM((ROWS, FF), LOW),
            pltpu.VMEM((ROWS, D), LOW),
            pltpu.VMEM((ROWS, D), LOW),
            pltpu.VMEM((L, D), LOW),
            pltpu.VMEM((ROWS, D), LOW),
            pltpu.VMEM((L, D), LOW),
        ],
        compiler_params=limit(12),
        cost_estimate=cost(7),
        name="middle_back",
    )(content, picks, vec, *matrices, *(saved[n] for n in names))


def feed_back(seq, info, arrived, content, picks, small_in, vec, matrices, saved, after=()):
    given = [] if small_in is None else [small_in]

    def kernel(info, arrived, content, picks, vec, expand, contract, *refs):
        kept, rest = refs[:5], refs[5 + len(given) + len(after) :]
        total, branch, attended, small, own, late, upper, expanded = rest
        w = Names(expand=expand, contract=contract)
        s = Names(
            total=total,
            branch=branch,
            attended=attended,
            expanded=expanded,
            **dict(zip(FEED_SAVED, kept)),
        )
        small[...] = refs[5][...] if given else jnp.zeros_like(small)

        def add(place, value):
            small[place : place + 1, :] += value

        take_rows(content, picks, seq, upper)
        back_second_norm(jnp.where(info[2] == 1, arrived[...], upper[...]), vec, s, add)
        late[:, :D] = branch[...]
        back_feed(w, vec, s, add)
        own[...] = columns(expanded, info[0] * HALF, HALF)[...]
        late[:, D:] = columns(expanded, (1 - info[0]) * HALF, HALF)[...]

    return pl.pallas_call(
        kernel,
        out_shape=[
            shaped((ROWS, D), WIDE),
            shaped((ROWS, D), LOW),
            shaped((ROWS, D), LOW),
            shaped((SMALL, D), WIDE),
            shaped((ROWS, HALF), LOW),
            shaped((ROWS, LATE), LOW),
        ],
        in_specs=[SMEM] + [VMEM] * (11 + len(given)) + [ANY] * len(after),
        out_specs=[VMEM] * 6,
        scratch_shapes=[pltpu.VMEM((ROWS, D), LOW), pltpu.VMEM((ROWS, FF), LOW)],
        compiler_params=limit(12),
        cost_estimate=cost(4),
        name="feed_back",
    )(
        info,
        arrived,
        content,
        picks,
        vec,
        matrices[4],
        matrices[5],
        *(saved[n] for n in FEED_SAVED),
        *given,
        *after,
    )


PLACES = {
    (2, 0): (0, 0),
    (1, 1): (0, 1),
    (2, 1): (1, 0),
    (3, 0): (1, 1),
    (1, 0): (2, 0),
    (3, 1): (3, 0),
    (0, 0): (4, 0),
    (0, 1): (4, 1),
}


def term_shapes(count):
    return [shaped((n * count, D), LOW) for n in (2, 2, 1, 1, 2)]


def feed_grads(info, mine, branch, own, early, late, after=()):
    def kernel(info, *refs):
        acts, lows, branches, owns, earlies, lates = (refs[2 * i : 2 * i + 2] for i in range(6))
        refs = refs[:12] + refs[12 + len(after) :]
        outs, (a_act, a_first, b_branch, b_own, stage, sems, out_sems) = refs[12:17], refs[17:]
        core, place = info[0], info[1]
        own_at = [slice(seq * ROWS, (seq + 1) * ROWS) for seq in range(SEQS)]
        far_at = [slice((2 + seq) * ROWS, (3 + seq) * ROWS) for seq in range(SEQS)]
        pairs, later = [], []
        for seq in range(SEQS):
            pairs += [
                (columns(acts[seq], core * HALF, HALF), a_act.at[own_at[seq]]),
                (earlies[seq].at[:, 3 * D :], a_act.at[far_at[seq]]),
                (branches[seq], b_branch.at[own_at[seq]]),
                (lates[seq].at[:, :D], b_branch.at[far_at[seq]]),
            ]
            later += [
                (lows[seq], a_first.at[own_at[seq]]),
                (earlies[seq].at[:, 2 * D : 3 * D], a_first.at[far_at[seq]]),
                (owns[seq], b_own.at[own_at[seq]]),
                (lates[seq].at[:, D:], b_own.at[far_at[seq]]),
            ]
        copies = start_all(pairs + later, sems)
        sent = []

        def send(block):
            for k in range(4):
                quarter = lax.rem(place + k, 4)
                index, part = PLACES[k, block // 2]
                start = (2 * part + block % 2) * QUARTER
                sent.extend(
                    start_all(
                        [
                            (
                                rows_at(stage.at[block], quarter * QUARTER, QUARTER),
                                outs[index].at[start : start + QUARTER],
                            )
                        ],
                        out_sems,
                        block * 4 + k,
                    )
                )

        wait_all(copies[:8])
        for block in range(2):
            for part in range(3):
                start = block * D + part * 256
                stage[block, part * 256 : (part + 1) * 256] = tn(
                    a_act[:, start : start + 256], b_branch[...]
                ).astype(LOW)
            send(block)
        wait_all(copies[8:])
        for block in range(2):
            for part in range(3):
                stage[2 + block, part * 256 : (part + 1) * 256] = tn(
                    a_first[:, part * 256 : (part + 1) * 256], b_own[:, block * D : (block + 1) * D]
                ).astype(LOW)
            send(2 + block)
        wait_all(sent)

    acts = [saved["activated"] for saved in mine]
    lows = [saved["first_low"] for saved in mine]
    return pl.pallas_call(
        kernel,
        out_shape=term_shapes(2 * QUARTER),
        in_specs=[SMEM] + [ANY] * (12 + len(after)),
        out_specs=[ANY] * 5,
        scratch_shapes=[
            pltpu.VMEM((2 * ALL_ROWS, HALF), LOW),
            pltpu.VMEM((2 * ALL_ROWS, D), LOW),
            pltpu.VMEM((2 * ALL_ROWS, D), LOW),
            pltpu.VMEM((2 * ALL_ROWS, HALF), LOW),
            pltpu.VMEM((4, D, D), LOW),
            DMA((16,)),
            DMA((16,)),
        ],
        compiler_params=limit(16),
        cost_estimate=cost(8),
        name="feed_grads",
    )(info, *acts, *lows, *branch, *own, *early, *late, *after)


def attend_back(seq, info, attended, small_in, spread, after, w_out, saved):
    def kernel(info, attended, small_in, spread, w_out, *refs):
        kept, (pieces, send, small, dmixed, sums) = refs[:4], refs[4 + len(after) :]
        small[...] = small_in[...]
        pieces[1, :ROWS] = attended[...]
        dmixed[...] = nt(attended[...], w_out[...]).astype(LOW)
        s = Names(
            dmixed=dmixed,
            dquery=pieces.at[0, :ROWS],
            dkey=pieces.at[0, ROWS:],
            dvalue=pieces.at[1, ROWS:],
            **dict(zip(ATTEND_SAVED, kept)),
        )
        sums[...] = jnp.zeros_like(sums)

        def table_sum(pair, dscores):
            for odd in range(2):
                part = tn(spread[seq], dscores[odd * ROWS : (odd + 1) * ROWS])
                both = jnp.concatenate([part, jnp.zeros((L, L), WIDE)], axis=1)
                turned = pltpu.roll(both, 0, 1, stride=1, stride_axis=0)
                head = 2 * pair + odd
                sums[head : head + 1, :] = jnp.sum(turned, axis=0, keepdims=True)

        back_attend(s, table_sum)
        send[...] = pieces[1 - info[0]]
        small[S_QUERY : S_QUERY + 1, :] += column_sum(pieces[0, :ROWS])
        small[S_VALUE : S_VALUE + 1, :] += column_sum(pieces[1, ROWS:])
        distance = lax.broadcasted_iota(jnp.int32, (2 * L, L), 0) - (L - 1)
        bucket = lax.broadcasted_iota(jnp.int32, (2 * L, L), 1)
        small[S_TABLE : S_TABLE + 16, :L] += lax.dot_general(
            sums[...],
            (bucket_of(distance) == bucket).astype(WIDE),
            (((1,), (0,)), ((), ())),
            precision=lax.Precision.HIGHEST,
            preferred_element_type=WIDE,
        )

    return pl.pallas_call(
        kernel,
        out_shape=[
            shaped((2, ROWS + L, D), LOW),
            shaped((ROWS + L, D), LOW),
            shaped((SMALL, D), WIDE),
        ],
        in_specs=[SMEM] + [VMEM] * 8 + [ANY] * len(after),
        out_specs=[VMEM] * 3,
        scratch_shapes=[pltpu.VMEM((ROWS, D), LOW), pltpu.VMEM((16, 2 * L), WIDE)],
        compiler_params=limit(12),
        cost_estimate=cost(4),
        name="attend_back",
    )(info, attended, small_in, spread, w_out, *(saved[n] for n in ATTEND_SAVED), *after)


def finish_rows(info, total, output, pieces, matrices, picks, after):
    def kernel(info, *refs):
        totals, outputs, pieces = refs[0:2], refs[2:4], refs[4:6]
        (query, key, value), refs = refs[6:9], refs[9 + len(after) :]
        content_ends, query_ends, done = refs
        done[...] = jnp.zeros_like(done)
        first = info[2] == 1
        for seq in range(SEQS):
            lower = totals[seq][...] + nt(pieces[seq][0, :ROWS], query[...])
            upper = nt(pieces[seq][0, ROWS:], key[...]) + nt(pieces[seq][1, ROWS:], value[...])
            content_ends[seq * L : (seq + 1) * L] = jnp.where(
                first, lower[:L] + upper, outputs[seq][:L]
            )
            query_ends[seq * picks : (seq + 1) * picks] = jnp.where(
                first, lower[L : L + picks], outputs[seq][L : L + picks]
            )

    return pl.pallas_call(
        kernel,
        out_shape=[shaped((ALL_CONTENT, D), WIDE), shaped((SEQS * picks, D), WIDE), TOKEN],
        in_specs=[SMEM] + [VMEM] * 9 + [ANY] * len(after),
        out_specs=[VMEM] * 3,
        compiler_params=limit(12),
        cost_estimate=cost(3),
        name="finish_rows",
    )(info, *total, *output, *pieces, *matrices[:3], *after)


def attend_grads(info, pair, early, mine, arrived, small, after=()):
    def kernel(info, small, *refs):
        pairs_in, earlies, mines, arriveds = (refs[2 * i : 2 * i + 2] for i in range(4))
        refs = refs[8 + len(after) :]
        outs, rest = refs[:5], refs[5:]
        a_rows, a_content, b_rows, b_content, stage, extra, sems, out_sems = rest
        core, place = info[0], info[1]
        pairs, later = [], []
        for seq in range(SEQS):
            at = slice(seq * ROWS, (seq + 1) * ROWS)
            far = slice((2 + seq) * ROWS, (3 + seq) * ROWS)
            pairs += [
                (pairs_in[seq].at[core], a_rows.at[at]),
                (columns(earlies[seq], core * D, D), a_rows.at[far]),
                (mines[seq].at[core, :ROWS], b_rows.at[at]),
                (arriveds[seq].at[:ROWS], b_rows.at[far]),
            ]
            at = slice(seq * L, (seq + 1) * L)
            far = slice((2 + seq) * L, (3 + seq) * L)
            later += [
                (pairs_in[seq].at[0, :L], a_content.at[at]),
                (earlies[seq].at[:L, :D], a_content.at[far]),
                (mines[seq].at[core, ROWS:], b_content.at[at]),
                (arriveds[seq].at[ROWS:], b_content.at[far]),
            ]
        copies = start_all(pairs + later, sems)
        blank = jnp.zeros((EXTRA, D), WIDE)
        extra[0] = jnp.concatenate([small[...], blank[SMALL:]]).astype(LOW)
        extra[1] = blank.astype(LOW)
        sent = []
        for block, (former, latter) in enumerate(((a_rows, b_rows), (a_content, b_content))):
            wait_all(copies[8 * block : 8 * block + 8])
            for part in range(3):
                stage[block, part * 256 : (part + 1) * 256] = tn(
                    former[:, part * 256 : (part + 1) * 256], latter[...]
                ).astype(LOW)
            for k in range(4):
                quarter = lax.rem(place + k, 4)
                index, part = PLACES[k, block]
                start = part * (QUARTER + EXTRA)
                middle, stop = start + QUARTER, start + QUARTER + EXTRA
                sent += start_all(
                    [
                        (
                            rows_at(stage.at[block], quarter * QUARTER, QUARTER),
                            outs[index].at[start:middle],
                        ),
                        (extra.at[block], outs[index].at[middle:stop]),
                    ],
                    out_sems,
                    block * 8 + 2 * k,
                )
        wait_all(sent)

    return pl.pallas_call(
        kernel,
        out_shape=term_shapes(QUARTER + EXTRA),
        in_specs=[SMEM, VMEM] + [ANY] * (8 + len(after)),
        out_specs=[ANY] * 5,
        scratch_shapes=[
            pltpu.VMEM((2 * ALL_ROWS, D), LOW),
            pltpu.VMEM((2 * ALL_CONTENT, D), LOW),
            pltpu.VMEM((2 * ALL_ROWS, D), LOW),
            pltpu.VMEM((2 * ALL_CONTENT, D), LOW),
            pltpu.VMEM((2, D, D), LOW),
            pltpu.VMEM((2, EXTRA, D), LOW),
            DMA((16,)),
            DMA((16,)),
        ],
        compiler_params=limit(12),
        cost_estimate=cost(5),
        name="attend_grads",
    )(info, small, *pair, *early, *mine, *arrived, *after)


def small_kernel(body, name, shapes, inputs, after=(), info=None, through=()):
    first = [] if info is None else [info]
    given = len(first) + len(inputs)

    def kernel(*refs):
        outs = refs[given + len(after) + len(through) :]
        body(*refs[:given], *outs[: len(shapes)])

    return pl.pallas_call(
        kernel,
        out_shape=[shaped(shape, LOW) for shape in shapes]
        + [shaped(array.shape, array.dtype) for array in through],
        in_specs=[SMEM] * len(first)
        + [VMEM] * len(inputs)
        + [ANY] * (len(after) + len(through)),
        out_specs=[VMEM] * len(shapes) + [ANY] * len(through),
        input_output_aliases={
            given + len(after) + i: len(shapes) + i for i in range(len(through))
        },
        compiler_params=limit(8),
        cost_estimate=cost(1),
        name=name,
    )(*first, *inputs, *after, *through)


def total_of(*terms):
    return sum(term.astype(WIDE) for term in terms).astype(LOW)


def ring_add(after0, before1, from_left, from_right, after=()):
    count = after0.shape[0]

    def body(after0, before1, from_left, from_right, right, left):
        right[...] = total_of(after0[...], from_left[:count])
        left[...] = total_of(before1[...], from_right[:count])

    return small_kernel(
        body, "ring_add", [after0.shape] * 2, (after0, before1, from_left, from_right), after
    )


def ring_sum(info, own, left, right, from_left, from_right, after=()):
    count = left.shape[0]
    part = count // 4

    def body(info, own, left, right, from_left, from_right, *outs):
        for k, out in enumerate(outs):
            at = pl.multiple_of(lax.rem(info[3] + k, 4) * part, 16)
            low, high = pl.ds(at, part), pl.ds(at + count, part)
            out[:part] = total_of(own[low], left[low], from_right[high])
            out[part:] = total_of(own[high], from_left[high], right[low])

    return small_kernel(
        body,
        "ring_sum",
        [(2 * part, D)] * 4,
        (own, left, right, from_left, from_right),
        after,
        info,
    )


def add_all(name, terms, after=()):
    def body(*refs):
        refs[-1][...] = total_of(*(ref[...] for ref in refs[:-1]))

    return small_kernel(body, name, [terms[0].shape], terms, after)[0]


def inner_join(info, parts, after=(), through=()):
    part = parts[0].shape[0] // 2

    def body(info, *refs):
        whole = refs[-1]
        for k, ref in enumerate(refs[:-1]):
            at = pl.multiple_of(lax.rem(info[3] + k, 4) * part, 16)
            whole[pl.ds(at, part)] = ref[:part]
            whole[pl.ds(at + 4 * part, part)] = ref[part:]

    return small_kernel(body, "inner_join", [(8 * part, D)], parts, after, info, through)


def cut(arrays, after=()):
    rows = arrays[0].shape[0]
    count = rows // 2

    def body(*refs):
        arrays, (right, left, whole) = refs[:-3], refs[-3:]
        right[...] = arrays[0][:count]
        left[...] = arrays[1][count:]
        for index, ref in enumerate(arrays):
            whole[index * rows : (index + 1) * rows] = ref[...]

    shapes = [(count, D), (count, D), (len(arrays) * rows, D)]
    return small_kernel(body, "cut", shapes, arrays, after)


def feed_targets(outs, source, half, core, quarter):
    pairs = []
    for block in range(2):
        part = source.at[block * QUARTER : (block + 1) * QUARTER]
        if half == 0:
            target = rows_at(outs[0], core * HALF + block * D + quarter * QUARTER, QUARTER)
        else:
            target = columns(
                rows_at(outs[1], quarter * QUARTER, QUARTER), (core * 2 + block) * D, D
            )
        pairs.append((None, part, target))
    return pairs


def attend_targets(outs, source, half, core, quarter):
    return [
        (
            core == number,
            source.at[:QUARTER],
            rows_at(outs[2 * number + half], quarter * QUARTER, QUARTER),
        )
        for number in range(2)
    ]


def settle(targets, shapes, count, info, pieces, outs, name, after=()):
    keys = tuple(pieces)
    arrays = [pieces[key] for key in keys]
    given = list(after) + list(outs or ())

    def kernel(info, *refs):
        parts, rest = refs[: len(keys)], refs[len(keys) + len(given) :]
        outs, rest = rest[: len(shapes)], rest[len(shapes) :]
        done, rest = rest[0], rest[1:]
        done[...] = jnp.zeros_like(done)
        held, wide_held, (sems, out_sems) = rest[: len(keys)], rest[len(keys) : -2], rest[-2:]
        copies = start_all(list(zip(parts, held)), sems)
        finish = []
        for index, (sibling, places) in enumerate(keys):
            core = 1 - info[0] if sibling else info[0]
            copies[index].wait()
            for number, (k, half) in enumerate(places):
                quarter = lax.rem((info[3] if sibling else info[1]) + k, 4)
                source = wide_held[index].at[number * count : (number + 1) * count]
                source[...] = held[index][number * count : (number + 1) * count].astype(WIDE)
                for place, (condition, part, target) in enumerate(
                    targets(outs, source, half, core, quarter)
                ):
                    copy = pltpu.make_async_copy(
                        part, target, out_sems.at[12 * index + 2 * number + place]
                    )
                    if condition is None:
                        copy.start()
                        finish.append(copy.wait)
                    else:
                        pl.when(condition)(copy.start)
                        finish.append(lambda c=copy, when=condition: pl.when(when)(c.wait))
        for action in finish:
            action()

    result = pl.pallas_call(
        kernel,
        out_shape=[shaped(shape, WIDE) for shape in shapes]
        + [TOKEN],
        in_specs=[SMEM] + [ANY] * (len(keys) + len(given)),
        out_specs=[ANY] * len(shapes) + [VMEM],
        scratch_shapes=[pltpu.VMEM(array.shape, LOW) for array in arrays]
        + [pltpu.VMEM(array.shape, WIDE) for array in arrays]
        + [DMA((len(keys),)), DMA((12 * len(keys),))],
        input_output_aliases={
            1 + len(keys) + len(after) + i: i for i in range(len(outs or ()))
        },
        compiler_params=limit(32),
        cost_estimate=cost(sum(array.size for array in arrays) * 2e-6 + 1),
        name=name,
    )(info, *arrays, *given)
    return result[:-1], result[-1]


PLANE = ("x", "y", "c")


def shift(value, axis, by):
    size = lax.axis_size(axis)
    return lax.ppermute(value, axis, [(i, (i + by) % size) for i in range(size)])


def send(value, by):
    return lax.ppermute(value, "s", [(0, 1)] if by > 0 else [(1, 0)])


def turn(value, outer, by):
    pairs = []
    for i in range(4):
        for j in range(4):
            for c in range(2):
                if (c == 0) == outer:
                    target = ((i + by) % 4, j)
                else:
                    target = (i, (j + by) % 4)
                pairs.append(((i * 4 + j) * 2 + c, (target[0] * 4 + target[1]) * 2 + c))
    return lax.ppermute(value, PLANE, pairs)


def place(outer):
    return jnp.where(
        (lax.axis_index("c") == 0) == outer, lax.axis_index("x"), lax.axis_index("y")
    )


def wide(value):
    return value.astype(WIDE)


def total_wide(*terms):
    return sum(wide(term) for term in terms)


def inner_turns(parts, sign):
    return [turn(part, False, sign * by) for part, by in zip(parts, (1, 2, -1))]


OWN, ACROSS = ((0, 0), (0, 1)), (((2, 0),), ((2, 1),))
NEAR = ((3, 0), (3, 1), (1, 0), (1, 1))


def both_cores(places, piece):
    return {(0, places): piece, (1, places): shift(piece, "c", 1)}


def on_device(
    content_in,
    query_in,
    content_cot,
    query_cot,
    order_rank,
    query_pos,
    group_tag,
    *rest,
):
    (
        w_query,
        b_query,
        w_key,
        w_value,
        b_value,
        w_out,
        b_out,
        norm1_gain,
        norm1_bias,
        w_expand,
        b_expand,
        w_contract,
        b_contract,
        norm2_gain,
        norm2_bias,
    ) = (argument[0] for argument in rest[:-1])
    rel_table = rest[-1]
    core = lax.axis_index("c")
    first_section = (lax.axis_index("s") == 0).astype(jnp.int32)
    info = jnp.stack([core, place(True), first_section, place(False)])
    picks = query_pos.shape[1]

    matrices = (w_query, w_key, w_value, w_out, w_expand, w_contract)
    w_out_held = w_out
    vec = jnp.stack(
        [b_query, b_value, b_out, norm1_gain, norm1_bias, b_contract, norm2_gain, norm2_bias]
    )
    ranks = jnp.concatenate([order_rank, group_tag, query_pos], axis=1)
    masks, spread, query_in, query_cot = prepare(
        ranks, rel_table, query_in, query_cot, picks, (vec, info)
    )
    b_expand = b_expand[None]

    fronts, arrived = [], []
    for seq in range(SEQS):
        fronts.append(
            front(seq, info, content_in, query_in, matrices, masks, vec, b_expand, tuple(fronts))
        )
        arrived.append(send(fronts[seq], 1))
    output, early, pair, saved, grads = [], [], [], [], []
    for seq in range(SEQS):
        results = middle_forward(
            seq, info, content_in, query_in, arrived[seq], matrices, masks, vec, b_expand, tuple(grads)
        )
        for collected, result in zip((output, early, pair, saved), results):
            collected.append(result)
        grads.append(middle_back(seq, content_cot, query_cot, matrices, vec, saved[seq]))
    early = [shift(value, "c", 1) for value in early]
    grads = [send(value, -1) for value in grads]
    small = None
    total, branch, attended, own, late, pieces, pass_on = [], [], [], [], [], [], []
    for seq in range(SEQS):
        results = feed_back(
            seq,
            info,
            grads[seq],
            content_cot,
            query_cot,
            small,
            vec,
            matrices,
            saved[seq],
            tuple(pass_on),
        )
        small = results[3]
        for collected, result in zip(
            (total, branch, attended, own, late), results[:3] + results[4:]
        ):
            collected.append(result)
        late[seq] = shift(late[seq], "c", 1)
        results = attend_back(
            seq,
            info,
            attended[seq],
            small,
            spread,
            (),
            w_out_held,
            saved[seq],
        )
        small = results[2]
        pieces.append(results[0])
        pass_on.append(results[1])
    feed_terms = feed_grads(info, saved, branch, own, early, late, (small,))
    passed = [shift(value, "c", 1) for value in pass_on]

    def outer_step(terms):
        return (turn(terms[0], True, 1), turn(terms[1], True, -1))

    f_left, f_right = outer_step(feed_terms)
    attend_terms = attend_grads(info, pair, early, pieces, passed, small, (feed_terms[4],))
    content_ends, query_ends, token = finish_rows(
        info, total, output, pieces, matrices, picks, (attend_terms[2],)
    )
    f_sent = ring_add(feed_terms[2], feed_terms[3], f_left, f_right, (token,))
    a_left, a_right = outer_step(attend_terms)
    f_outer = outer_step(f_sent)
    f_parts = ring_sum(info, feed_terms[4], *f_outer, f_left, f_right)
    f_others = inner_turns(f_parts[1:], 1)
    a_sent = ring_add(attend_terms[2], attend_terms[3], a_left, a_right, (f_parts[0],))
    f_part = add_all("inner_sum", [f_parts[0]] + f_others, (a_sent[0],))
    f_far = shift(f_part, "z", 1)
    a_parts = ring_sum(info, attend_terms[4], *outer_step(a_sent), a_left, a_right, (f_part,))
    f_part = add_all("z_sum", [f_part, f_far])
    f_others = inner_turns([f_part] * 3, -1)
    a_part = add_all("inner_sum", [a_parts[0]] + inner_turns(a_parts[1:], 1))
    (feed_own,) = inner_join(info, [f_part] + f_others, (a_part,))
    feed_outer = (turn(feed_own, True, 1), turn(feed_own, True, -1))
    a_part = add_all("z_sum", [a_part, shift(a_part, "z", 1)])
    a_others = inner_turns([a_part] * 3, -1)

    def feed_settle(pieces, outs, name):
        return settle(
            feed_targets, ((FF, D), (D, FF)), 2 * QUARTER, info, pieces, outs, "feed_" + name
        )

    def attend_settle(pieces, outs, name, after=()):
        return settle(
            attend_targets,
            ((D, D),) * 4,
            QUARTER + EXTRA,
            info,
            pieces,
            outs,
            "attend_" + name,
            after,
        )

    feed_outs, token = feed_settle(both_cores(OWN, feed_own), None, "own")
    to_right, to_left, feed_near = cut(feed_outer, (token, *a_others))
    feed_across = (turn(to_right, True, 1), turn(to_left, True, -1))
    (attend_own,) = inner_join(info, [a_part] + a_others, (to_right,))
    attend_outer = (turn(attend_own, True, 1), turn(attend_own, True, -1))
    feed_outs, token = feed_settle(both_cores(NEAR, feed_near), feed_outs, "near")
    to_right, to_left, attend_near = cut((*attend_outer, attend_own), (token, *feed_across))
    attend_across = (turn(to_right, True, 1), turn(to_left, True, -1))
    feed_outs, _ = feed_settle(
        both_cores(ACROSS[0], feed_across[0]) | both_cores(ACROSS[1], feed_across[1]),
        feed_outs,
        "across",
    )
    attend_both = both_cores(NEAR + OWN, attend_near)
    attend_outs, _ = attend_settle(attend_both, None, "near")
    attend_outs, _ = attend_settle(
        both_cores(ACROSS[0], attend_across[0]) | both_cores(ACROSS[1], attend_across[1]),
        attend_outs,
        "across",
    )
    contract, expand = feed_outs
    g_query, g_key, g_out, g_value = attend_outs
    start = 4 * (QUARTER + EXTRA) + QUARTER
    small_sum = total_wide(*(piece[start : start + SMALL] for piece in attend_both.values()))
    table = small_sum[S_TABLE : S_TABLE + H, :L]
    table_total = (table + shift(table, "s", 1))[:, :NB].T
    row = lambda k: small_sum[k][None]
    return (
        content_ends[None],
        query_ends[None],
        g_query[None],
        row(S_QUERY),
        g_key[None],
        g_value[None],
        row(S_VALUE),
        g_out[None],
        row(S_OUT),
        row(S_GAIN1),
        row(S_SHIFT1),
        expand[None],
        small_sum[S_EXPAND : S_EXPAND + 4].reshape(1, FF),
        contract[None],
        row(S_CONTRACT),
        row(S_GAIN2),
        row(S_SHIFT2),
        table_total,
    )


DP = ("z", "x", "y", "c")


def solution(mesh):
    mesh = jax.sharding.Mesh(mesh.devices.reshape(2, 2, 4, 4, 2), ("s",) + DP)
    layer_specs = tuple(
        P("s", *([None] * (rank - 1))) for rank in (3, 2, 3, 3, 2, 3, 2, 2, 2, 3, 2, 3, 2, 2, 2)
    )
    in_specs = (P(DP, None),) * 7 + layer_specs + (P(),)
    out_specs = (P("s", DP, None),) * 2 + layer_specs + (P(),)
    return jax.shard_map(
        on_device, mesh=mesh, in_specs=in_specs, out_specs=out_specs, check_vma=False
    )
```

```python
import jax
import jax.numpy as jnp
from jax import lax
from jax.experimental import pallas as pl
from jax.experimental.pallas import tpu as pltpu
from jax.sharding import PartitionSpec as P

D = 768
H = 12
HD = 64
FF = 3072
NB = 32
L = 128
PAIRS = H // 2
SEQS = 2
PICKS = 32
ROWS = L + PICKS
EPSILON = 1e-05
SCALE = HD ** (-0.5)
TILE = 1536
LOW = jnp.bfloat16
WIDE = jnp.float32
HALF = FF // 2
QUARTER = D // 4
EARLY = 3 * D + HALF
LATE = D + HALF
SMALL = 16
ALL_ROWS = SEQS * ROWS
ALL_CONTENT = SEQS * L
PIECE = ALL_ROWS + ALL_CONTENT


def nn(former, latter):
    return lax.dot_general(
        former, latter, (((1,), (0,)), ((), ())), preferred_element_type=WIDE
    )


def nt(former, latter):
    return lax.dot_general(
        former, latter, (((1,), (1,)), ((), ())), preferred_element_type=WIDE
    )


def tn(former, latter):
    return lax.dot_general(
        former, latter, (((0,), (0,)), ((), ())), preferred_element_type=WIDE
    )


def halves(value):
    even = lax.broadcasted_iota(jnp.int32, value.shape, 1) < HD
    zero = jnp.zeros_like(value)
    return jnp.concatenate([jnp.where(even, value, zero), jnp.where(even, zero, value)])


def side(value):
    count = value.shape[0] // 2
    return jnp.concatenate([value[:count], value[count:]], axis=1)


def norm_rows(values):
    centered = values - jnp.mean(values, axis=-1, keepdims=True)
    variance = jnp.mean(centered * centered, axis=-1, keepdims=True)
    root = lax.rsqrt(variance + EPSILON)
    return (centered * root, root)


def norm_rows_back(scaled, normed, root):
    return root * (
        scaled
        - jnp.mean(scaled, axis=-1, keepdims=True)
        - normed * jnp.mean(scaled * normed, axis=-1, keepdims=True)
    )


B_QUERY, B_VALUE, B_OUT, GAIN1, SHIFT1, B_CONTRACT, GAIN2, SHIFT2 = range(8)
S_QUERY, S_VALUE, S_OUT, S_GAIN1, S_SHIFT1, S_EXPAND = range(6)
S_CONTRACT, S_GAIN2, S_SHIFT2, S_TABLE = 9, 10, 11, 12
LIMITS = (12, 16, 23, 32, 46, 64, 91)


def bucket_of(relative):
    distance = jnp.abs(relative)
    beyond = 8 + sum((distance >= limit).astype(jnp.int32) for limit in LIMITS)
    within = jnp.where(distance < 8, distance, beyond)
    return within + 16 * (relative > 0).astype(jnp.int32)


def forward(x, w, vec, b_expand, masks, s, keep):
    row = lambda k: vec[k : k + 1, :]
    s.query[...] = (nn(x[...], w.query[...]) + row(B_QUERY)).astype(LOW)
    s.key[...] = nn(x[:L], w.key[...]).astype(LOW)
    s.value[...] = (nn(x[:L], w.value[...]) + row(B_VALUE)).astype(LOW)
    for pair in range(PAIRS):
        lanes = slice(pair * 128, (pair + 1) * 128)
        scores = nt(halves(s.query[:, lanes]), s.key[:, lanes]) * SCALE + masks[pair]
        shifted = jnp.exp(scores - jnp.max(scores, axis=-1, keepdims=True))
        probs = (shifted / jnp.sum(shifted, axis=-1, keepdims=True)).astype(LOW)
        if keep:
            s.probs[pair] = probs
        s.mixed[:, lanes] = nn(side(probs), halves(s.value[:, lanes])).astype(LOW)
    total = x[...].astype(WIDE) + nn(s.mixed[...], w.out[...]) + row(B_OUT)
    normed, root = norm_rows(total)
    first = normed * row(GAIN1) + row(SHIFT1)
    s.first_low[...] = first.astype(LOW)
    s.total[...] = first + row(B_CONTRACT)
    if keep:
        s.normed1[...] = normed
        s.root1[...] = jnp.broadcast_to(root, (ROWS, 128))
    for tile in range(FF // TILE):
        tile = slice(tile * TILE, (tile + 1) * TILE)
        expanded = nn(s.first_low[...], w.expand[:, tile]) + b_expand[:, tile]
        cumulative = 0.5 * (1.0 + lax.erf(expanded * 0.7071067811865476))
        activated = (expanded * cumulative).astype(LOW)
        if keep:
            s.slope[:, tile] = (
                cumulative + expanded * jnp.exp(-0.5 * expanded * expanded) * 0.3989422804014327
            ).astype(LOW)
            s.activated[:, tile] = activated
        s.total[...] += nn(activated, w.contract[tile, :])
    normed, root = norm_rows(s.total[...])
    if keep:
        s.normed2[...] = normed
        s.root2[...] = jnp.broadcast_to(root, (ROWS, 128))
    s.out[...] = (normed * row(GAIN2) + row(SHIFT2)).astype(s.out.dtype)


def column_sum(value):
    return jnp.sum(value.astype(WIDE), axis=0, keepdims=True)


def back_second_norm(grad, vec, s, add=None):
    upper = grad.astype(WIDE)
    normed = s.normed2[...]
    lower = norm_rows_back(upper * vec[GAIN2 : GAIN2 + 1, :], normed, s.root2[:, :1])
    s.total[...] = lower
    s.branch[...] = lower.astype(LOW)
    if add is not None:
        add(S_GAIN2, column_sum(upper * normed))
        add(S_SHIFT2, column_sum(upper))
        add(S_CONTRACT, column_sum(lower.astype(LOW)))


def back_feed(w, vec, s, add=None):
    for tile in range(FF // TILE):
        tile = slice(tile * TILE, (tile + 1) * TILE)
        lower = (nt(s.branch[...], w.contract[tile, :]) * s.slope[:, tile].astype(WIDE)).astype(LOW)
        s.expanded[:, tile] = lower
        if add is not None:
            part = column_sum(lower)
            for column in range(TILE // D):
                add(
                    S_EXPAND + tile.start // D + column,
                    part[:, column * D : (column + 1) * D],
                )
        s.total[...] += nt(lower, w.expand[:, tile])
    upper = s.total[...]
    normed = s.normed1[...]
    lower = norm_rows_back(upper * vec[GAIN1 : GAIN1 + 1, :], normed, s.root1[:, :1])
    s.total[...] = lower
    s.attended[...] = lower.astype(LOW)
    if add is not None:
        add(S_GAIN1, column_sum(upper * normed))
        add(S_SHIFT1, column_sum(upper))
        add(S_OUT, column_sum(lower.astype(LOW)))


def back_attend(s, table=None):
    for pair in range(PAIRS):
        lanes = slice(pair * 128, (pair + 1) * 128)
        probs = s.probs[pair]
        below = halves(s.dmixed[:, lanes])
        dprobs = nt(below, s.value[:, lanes])
        s.dvalue[:, lanes] = tn(probs, below).astype(LOW)
        weight = probs.astype(WIDE)
        dscores = (
            weight * (dprobs - jnp.sum(weight * dprobs, axis=-1, keepdims=True))
        ).astype(LOW)
        s.dquery[:, lanes] = (nn(side(dscores), halves(s.key[:, lanes])) * SCALE).astype(LOW)
        s.dkey[:, lanes] = (tn(dscores, halves(s.query[:, lanes])) * SCALE).astype(LOW)
        if table is not None:
            table(pair, dscores)


class Names:
    def __init__(self, **named):
        self.__dict__.update(named)


MATRICES = ("query", "key", "value", "out", "expand", "contract")
MATRIX_SHAPES = {
    "query": (D, D),
    "key": (D, D),
    "value": (D, D),
    "out": (D, D),
    "expand": (D, FF),
    "contract": (FF, D),
}
MASK_SHAPE = (PAIRS, 2 * ROWS, L)
KEPT = {
    "query": ((ROWS, D), LOW),
    "key": ((L, D), LOW),
    "value": ((L, D), LOW),
    "probs": (MASK_SHAPE, LOW),
    "mixed": ((ROWS, D), LOW),
    "normed1": ((ROWS, D), WIDE),
    "root1": ((ROWS, 128), WIDE),
    "first_low": ((ROWS, D), LOW),
    "slope": ((ROWS, FF), LOW),
    "activated": ((ROWS, FF), LOW),
    "normed2": ((ROWS, D), WIDE),
    "root2": ((ROWS, 128), WIDE),
}
SAVED = tuple(name for name in KEPT if name != "mixed")
ANY = pl.BlockSpec(memory_space=pl.ANY)
HBM = pl.BlockSpec(memory_space=pltpu.HBM)
VMEM = pl.BlockSpec(memory_space=pltpu.VMEM)
SMEM = pl.BlockSpec(memory_space=pltpu.SMEM)


def limit(megabytes):
    return pltpu.CompilerParams(vmem_limit_bytes=megabytes * 1024 * 1024)


DMA = pltpu.SemaphoreType.DMA


def cost(microseconds):
    return pl.CostEstimate(flops=0, bytes_accessed=int(microseconds * 3.2e6), transcendentals=0)


def shaped(shape, kind):
    return jax.ShapeDtypeStruct(shape, kind)


TOKEN = shaped((8, 128), WIDE)


def columns(ref, start, size):
    return ref.at[:, pl.ds(pl.multiple_of(start, 128), size)]


def rows_at(ref, start, size):
    return ref.at[pl.ds(pl.multiple_of(start, 64), size)]


def start_all(pairs, sems, base=0):
    copies = [
        pltpu.make_async_copy(source, target, sems.at[base + index])
        for index, (source, target) in enumerate(pairs)
    ]
    for copy in copies:
        copy.start()
    return copies


def wait_all(copies):
    for copy in copies:
        copy.wait()


def fetcher(names, sources, targets, sems, base=0):
    copies = dict(zip(names, start_all(list(zip(sources, targets)), sems, base)))
    return lambda name: copies[name].wait()


def prepare(ranks, table, query_in, query_cot, picks, after):
    def kernel(ranks, table, query_in, query_cot, *refs):
        masks, spread, rows_in, rows_cot = refs[len(after) :]
        order, tag, pos = ranks[:, :L], ranks[:, L : 2 * L], ranks[:, 2 * L : 2 * L + picks]
        for source, target in ((query_in, rows_in), (query_cot, rows_cot)):
            values = source[...].astype(WIDE)
            blank = jnp.zeros((PICKS - picks, D), WIDE)
            target[...] = jnp.concatenate(
                [values[:picks], blank, values[picks:], blank]
            ).astype(LOW)
        lane = lax.broadcasted_iota(jnp.int32, (L, L), 1)
        level = lax.broadcasted_iota(jnp.int32, (L, L), 0)
        lane_q = lax.broadcasted_iota(jnp.int32, (PICKS, L), 1)
        upright = lambda row: jnp.sum(jnp.where(lane == level, row, 0.0), axis=1, keepdims=True)
        distance = lax.broadcasted_iota(jnp.int32, (2 * L, NB), 0) - (L - 1)
        bucket = lax.broadcasted_iota(jnp.int32, (2 * L, NB), 1)
        by_distance = lax.dot_general(
            table[...],
            (bucket_of(distance) == bucket).astype(WIDE),
            (((0,), (1,)), ((), ())),
            precision=lax.Precision.HIGHEST,
            preferred_element_type=WIDE,
        )
        allowed, hot = [], []
        for seq in range(SEQS):
            own_rank = order[seq : seq + 1, :].astype(WIDE)
            own_tag = tag[seq : seq + 1, :].astype(WIDE)
            own_pos = pos[seq : seq + 1, :].astype(WIDE)
            number = lax.broadcasted_iota(jnp.int32, (PICKS, picks), 0)
            same = number == lax.broadcasted_iota(jnp.int32, (PICKS, picks), 1)
            place = jnp.sum(jnp.where(same, own_pos, 0.0), axis=1, keepdims=True)
            filled = lax.broadcasted_iota(jnp.int32, (PICKS, 1), 0) < picks
            place = jnp.where(filled, place, -1.0).astype(jnp.int32)
            matches = place == lane_q
            marks = jnp.where(matches, 1.0, 0.0)
            predicted = jnp.max(marks, axis=0, keepdims=True)
            rank = jnp.sum(jnp.where(matches, own_rank, 0.0), axis=1, keepdims=True)
            group = jnp.sum(jnp.where(matches, own_tag, 0.0), axis=1, keepdims=True)
            earlier = (upright(predicted) > 0) & (own_rank <= upright(own_rank))
            content = (upright(own_tag) == own_tag) & ((predicted == 0) | earlier)
            query = (group == own_tag) & ((predicted == 0) | (own_rank + 1 <= rank))
            allowed.append((content, query))
            hot.append(marks)
            spread[seq, :L] = jnp.where(lane == L - 1 - level, 1.0, 0.0).astype(LOW)
            spread[seq, L:] = jnp.where(lane_q == L - 1 - place, 1.0, 0.0).astype(LOW)
        hot = jnp.concatenate(hot)
        for head in range(H):
            row = jnp.broadcast_to(by_distance[head : head + 1], (L, 2 * L))
            bias = pltpu.roll(row, L + 1, 1, stride=1, stride_axis=0)[:, :L]
            bias_q = lax.dot_general(
                hot,
                bias,
                (((1,), (0,)), ((), ())),
                precision=lax.Precision.HIGHEST,
                preferred_element_type=WIDE,
            )
            base = head % 2 * ROWS
            for seq in range(SEQS):
                content, query = allowed[seq]
                masks[seq, head // 2, base : base + L] = jnp.where(content, bias, -1e30)
                masks[seq, head // 2, base + L : base + ROWS] = jnp.where(
                    query, bias_q[seq * PICKS : (seq + 1) * PICKS], -1e30
                )

    return pl.pallas_call(
        kernel,
        out_shape=[
            shaped((SEQS,) + MASK_SHAPE, WIDE),
            shaped((SEQS, ROWS, L), LOW),
            shaped((SEQS * PICKS, D), LOW),
            shaped((SEQS * PICKS, D), LOW),
        ],
        in_specs=[VMEM] * 4 + [ANY] * len(after),
        out_specs=[VMEM] * 4,
        compiler_params=limit(8),
        cost_estimate=pl.CostEstimate(flops=int(3e10), bytes_accessed=0, transcendentals=0),
        name="prepare",
    )(ranks, table, query_in, query_cot, *after)


def take_rows(content, picks, seq, target):
    target[:L] = content[seq * L : (seq + 1) * L]
    target[L:] = picks[seq * PICKS : (seq + 1) * PICKS]


def front(seq, info, content, picks, matrices, masks, vec, b_expand, after=()):
    def kernel(info, content, picks, masks, vec, b_expand, *refs):
        w = Names(**dict(zip(MATRICES, refs[:6])))
        out, x, query, key, value, mixed, first_low, total = refs[6 + len(after) :]
        s = Names(
            query=query,
            key=key,
            value=value,
            mixed=mixed,
            first_low=first_low,
            total=total,
            out=out,
        )
        take_rows(content, picks, seq, x)
        forward(x, w, vec, b_expand, masks.at[seq], s, False)

    return pl.pallas_call(
        kernel,
        out_shape=shaped((ROWS, D), LOW),
        in_specs=[SMEM] + [VMEM] * 11 + [ANY] * len(after),
        out_specs=VMEM,
        scratch_shapes=[pltpu.VMEM((ROWS, D), LOW)]
        + [pltpu.VMEM(*KEPT[n]) for n in ("query", "key", "value", "mixed", "first_low")]
        + [pltpu.VMEM((ROWS, D), WIDE)],
        compiler_params=limit(12),
        cost_estimate=cost(5),
        name="front",
    )(info, content, picks, masks, vec, b_expand, *matrices, *after)


def middle_forward(seq, info, content, picks, arrived, matrices, masks, vec, b_expand, after=()):
    def kernel(info, arrived, content, picks, masks, vec, b_expand, *refs):
        w, rest = Names(**dict(zip(MATRICES, refs[:6]))), refs[6 + len(after) :]
        (out, early, pair), kept = rest[:3], rest[3 : 3 + len(SAVED)]
        mixed, total = rest[3 + len(SAVED) :]
        x = pair.at[0]
        s = Names(total=total, out=out, mixed=mixed, **dict(zip(SAVED, kept)))
        take_rows(content, picks, seq, x)
        x[...] = jnp.where(info[2] == 1, x[...], arrived[...])
        early[:, :D] = x[...]
        forward(x, w, vec, b_expand, masks.at[seq], s, True)
        pair[1] = mixed[...]
        early[:, D : 2 * D] = mixed[...]
        early[:, 2 * D : 3 * D] = s.first_low[...]
        early[:, 3 * D :] = columns(s.activated, (1 - info[0]) * HALF, HALF)[...]

    out, early, pair, *saved = pl.pallas_call(
        kernel,
        out_shape=[
            shaped((ROWS, D), WIDE),
            shaped((ROWS, EARLY), LOW),
            shaped((2, ROWS, D), LOW),
        ]
        + [shaped(*KEPT[n]) for n in SAVED],
        in_specs=[SMEM] + [VMEM] * 12 + [ANY] * len(after),
        out_specs=[VMEM] * (3 + len(SAVED)),
        scratch_shapes=[pltpu.VMEM(*KEPT["mixed"]), pltpu.VMEM((ROWS, D), WIDE)],
        compiler_params=limit(16),
        cost_estimate=cost(6),
        name="middle_forward",
    )(info, arrived, content, picks, masks, vec, b_expand, *matrices, *after)
    return (out, early, pair, dict(zip(SAVED, saved)))


FEED_SAVED = ("normed2", "root2", "slope", "normed1", "root1")
ATTEND_SAVED = ("value", "probs", "key", "query")


def middle_back(seq, content, picks, matrices, vec, saved):
    names = FEED_SAVED + ATTEND_SAVED

    def kernel(content, picks, vec, *refs):
        w, rest = Names(**dict(zip(MATRICES, refs[:6]))), refs[6:]
        kept, grad, rest = rest[: len(names)], rest[len(names)], rest[len(names) + 1 :]
        cot, total, branch, expanded, attended, dmixed, dvalue, dquery, dkey = rest
        s = Names(
            total=total,
            branch=branch,
            expanded=expanded,
            attended=attended,
            dmixed=dmixed,
            dvalue=dvalue,
            dquery=dquery,
            dkey=dkey,
            **dict(zip(names, kept)),
        )
        take_rows(content, picks, seq, cot)
        back_second_norm(cot[...], vec, s)
        back_feed(w, vec, s)
        dmixed[...] = nt(attended[...], w.out[...]).astype(LOW)
        back_attend(s)
        lower = total[...] + nt(dquery[...], w.query[...])
        upper = nt(dkey[...], w.key[...]) + nt(dvalue[...], w.value[...])
        grad[:L] = (lower[:L] + upper).astype(LOW)
        grad[L:] = lower[L:].astype(LOW)

    return pl.pallas_call(
        kernel,
        out_shape=shaped((ROWS, D), LOW),
        in_specs=[VMEM] * (9 + len(names)),
        out_specs=VMEM,
        scratch_shapes=[
            pltpu.VMEM((ROWS, D), LOW),
            pltpu.VMEM((ROWS, D), WIDE),
            pltpu.VMEM((ROWS, D), LOW),
            pltpu.VMEM((ROWS, FF), LOW),
            pltpu.VMEM((ROWS, D), LOW),
            pltpu.VMEM((ROWS, D), LOW),
            pltpu.VMEM((L, D), LOW),
            pltpu.VMEM((ROWS, D), LOW),
            pltpu.VMEM((L, D), LOW),
        ],
        compiler_params=limit(12),
        cost_estimate=cost(7),
        name="middle_back",
    )(content, picks, vec, *matrices, *(saved[n] for n in names))


def feed_back(seq, info, arrived, content, picks, small_in, vec, matrices, saved, after=()):
    given = [] if small_in is None else [small_in]

    def kernel(info, arrived, content, picks, vec, expand, contract, *refs):
        kept, rest = refs[:5], refs[5 + len(given) + len(after) :]
        total, branch, attended, small, own, late, upper, expanded = rest
        w = Names(expand=expand, contract=contract)
        s = Names(
            total=total,
            branch=branch,
            attended=attended,
            expanded=expanded,
            **dict(zip(FEED_SAVED, kept)),
        )
        small[...] = refs[5][...] if given else jnp.zeros_like(small)

        def add(place, value):
            small[place : place + 1, :] += value

        take_rows(content, picks, seq, upper)
        back_second_norm(jnp.where(info[2] == 1, arrived[...], upper[...]), vec, s, add)
        late[:, :D] = branch[...]
        back_feed(w, vec, s, add)
        own[...] = columns(expanded, info[0] * HALF, HALF)[...]
        late[:, D:] = columns(expanded, (1 - info[0]) * HALF, HALF)[...]

    return pl.pallas_call(
        kernel,
        out_shape=[
            shaped((ROWS, D), WIDE),
            shaped((ROWS, D), LOW),
            shaped((ROWS, D), LOW),
            shaped((SMALL, D), WIDE),
            shaped((ROWS, HALF), LOW),
            shaped((ROWS, LATE), LOW),
        ],
        in_specs=[SMEM] + [VMEM] * (11 + len(given)) + [ANY] * len(after),
        out_specs=[VMEM] * 6,
        scratch_shapes=[pltpu.VMEM((ROWS, D), LOW), pltpu.VMEM((ROWS, FF), LOW)],
        compiler_params=limit(12),
        cost_estimate=cost(4),
        name="feed_back",
    )(
        info,
        arrived,
        content,
        picks,
        vec,
        matrices[4],
        matrices[5],
        *(saved[n] for n in FEED_SAVED),
        *given,
        *after,
    )


PLACES = {
    (2, 0): (0, 0),
    (1, 1): (0, 1),
    (2, 1): (1, 0),
    (3, 0): (1, 1),
    (1, 0): (2, 0),
    (3, 1): (3, 0),
    (0, 0): (4, 0),
    (0, 1): (4, 1),
}


def term_shapes(count, extra=0):
    rows = (2 * count + extra, 2 * count + extra, count, count, 2 * count)
    return [shaped((n, D), LOW) for n in rows]


def feed_grads(info, mine, branch, own, early, late, after=()):
    def kernel(info, *refs):
        acts, lows, branches, owns, earlies, lates = (refs[2 * i : 2 * i + 2] for i in range(6))
        refs = refs[:12] + refs[12 + len(after) :]
        outs, (a_act, a_first, b_branch, b_own, stage, sems, out_sems) = refs[12:17], refs[17:]
        core, place = info[0], info[1]
        own_at = [slice(seq * ROWS, (seq + 1) * ROWS) for seq in range(SEQS)]
        far_at = [slice((2 + seq) * ROWS, (3 + seq) * ROWS) for seq in range(SEQS)]
        pairs, later = [], []
        for seq in range(SEQS):
            pairs += [
                (columns(acts[seq], core * HALF, HALF), a_act.at[own_at[seq]]),
                (earlies[seq].at[:, 3 * D :], a_act.at[far_at[seq]]),
                (branches[seq], b_branch.at[own_at[seq]]),
                (lates[seq].at[:, :D], b_branch.at[far_at[seq]]),
            ]
            later += [
                (lows[seq], a_first.at[own_at[seq]]),
                (earlies[seq].at[:, 2 * D : 3 * D], a_first.at[far_at[seq]]),
                (owns[seq], b_own.at[own_at[seq]]),
                (lates[seq].at[:, D:], b_own.at[far_at[seq]]),
            ]
        copies = start_all(pairs + later, sems)
        sent = []

        def send(block):
            for k in range(4):
                quarter = lax.rem(place + k, 4)
                index, part = PLACES[k, block // 2]
                start = (2 * part + block % 2) * QUARTER
                sent.extend(
                    start_all(
                        [
                            (
                                rows_at(stage.at[block], quarter * QUARTER, QUARTER),
                                outs[index].at[start : start + QUARTER],
                            )
                        ],
                        out_sems,
                        block * 4 + k,
                    )
                )

        wait_all(copies[:8])
        for block in range(2):
            for part in range(3):
                start = block * D + part * 256
                stage[block, part * 256 : (part + 1) * 256] = tn(
                    a_act[:, start : start + 256], b_branch[...]
                ).astype(LOW)
            send(block)
        wait_all(copies[8:])
        for block in range(2):
            for part in range(3):
                stage[2 + block, part * 256 : (part + 1) * 256] = tn(
                    a_first[:, part * 256 : (part + 1) * 256], b_own[:, block * D : (block + 1) * D]
                ).astype(LOW)
            send(2 + block)
        wait_all(sent)

    acts = [saved["activated"] for saved in mine]
    lows = [saved["first_low"] for saved in mine]
    return pl.pallas_call(
        kernel,
        out_shape=term_shapes(2 * QUARTER),
        in_specs=[SMEM] + [ANY] * (12 + len(after)),
        out_specs=[ANY] * 5,
        scratch_shapes=[
            pltpu.VMEM((2 * ALL_ROWS, HALF), LOW),
            pltpu.VMEM((2 * ALL_ROWS, D), LOW),
            pltpu.VMEM((2 * ALL_ROWS, D), LOW),
            pltpu.VMEM((2 * ALL_ROWS, HALF), LOW),
            pltpu.VMEM((4, D, D), LOW),
            DMA((16,)),
            DMA((16,)),
        ],
        compiler_params=limit(16),
        cost_estimate=cost(8),
        name="feed_grads",
    )(info, *acts, *lows, *branch, *own, *early, *late, *after)


def attend_back(seq, info, attended, small_in, spread, after, w_out, saved):
    def kernel(info, attended, small_in, spread, w_out, *refs):
        kept, (pieces, send, small, dmixed, sums) = refs[:4], refs[4 + len(after) :]
        small[...] = small_in[...]
        pieces[1, :ROWS] = attended[...]
        dmixed[...] = nt(attended[...], w_out[...]).astype(LOW)
        s = Names(
            dmixed=dmixed,
            dquery=pieces.at[0, :ROWS],
            dkey=pieces.at[0, ROWS:],
            dvalue=pieces.at[1, ROWS:],
            **dict(zip(ATTEND_SAVED, kept)),
        )
        sums[...] = jnp.zeros_like(sums)

        def table_sum(pair, dscores):
            for odd in range(2):
                part = tn(spread[seq], dscores[odd * ROWS : (odd + 1) * ROWS])
                both = jnp.concatenate([part, jnp.zeros((L, L), WIDE)], axis=1)
                turned = pltpu.roll(both, 0, 1, stride=1, stride_axis=0)
                head = 2 * pair + odd
                sums[head : head + 1, :] = jnp.sum(turned, axis=0, keepdims=True)

        back_attend(s, table_sum)
        send[: ROWS + L] = pieces[1 - info[0]]
        small[S_QUERY : S_QUERY + 1, :] += column_sum(pieces[0, :ROWS])
        small[S_VALUE : S_VALUE + 1, :] += column_sum(pieces[1, ROWS:])
        distance = lax.broadcasted_iota(jnp.int32, (2 * L, L), 0) - (L - 1)
        bucket = lax.broadcasted_iota(jnp.int32, (2 * L, L), 1)
        table = lax.dot_general(
            sums[...],
            (bucket_of(distance) == bucket).astype(WIDE),
            (((1,), (0,)), ((), ())),
            precision=lax.Precision.HIGHEST,
            preferred_element_type=WIDE,
        )
        for column in range(H // 4):
            lanes = slice(column * L, (column + 1) * L)
            small[S_TABLE : S_TABLE + 4, lanes] += table[4 * column : 4 * column + 4]
        send[ROWS + L :] = small[...].astype(LOW)

    return pl.pallas_call(
        kernel,
        out_shape=[
            shaped((2, ROWS + L, D), LOW),
            shaped((ROWS + L + SMALL, D), LOW),
            shaped((SMALL, D), WIDE),
        ],
        in_specs=[SMEM] + [VMEM] * 8 + [ANY] * len(after),
        out_specs=[VMEM] * 3,
        scratch_shapes=[pltpu.VMEM((ROWS, D), LOW), pltpu.VMEM((16, 2 * L), WIDE)],
        compiler_params=limit(12),
        cost_estimate=cost(4),
        name="attend_back",
    )(info, attended, small_in, spread, w_out, *(saved[n] for n in ATTEND_SAVED), *after)


def finish_rows(info, total, output, pieces, matrices, picks, after):
    def kernel(info, *refs):
        totals, outputs, pieces = refs[0:2], refs[2:4], refs[4:6]
        (query, key, value), refs = refs[6:9], refs[9 + len(after) :]
        content_ends, query_out, done, query_ends, sem = refs
        done[...] = jnp.zeros_like(done)
        first = info[2] == 1
        for seq in range(SEQS):
            lower = totals[seq][...] + nt(pieces[seq][0, :ROWS], query[...])
            upper = nt(pieces[seq][0, ROWS:], key[...]) + nt(pieces[seq][1, ROWS:], value[...])
            content_ends[seq * L : (seq + 1) * L] = jnp.where(
                first, lower[:L] + upper, outputs[seq][:L]
            )
            query_ends[seq * picks : (seq + 1) * picks] = jnp.where(
                first, lower[L : L + picks], outputs[seq][L : L + picks]
            )
        copy = pltpu.make_async_copy(query_ends, query_out, sem)
        copy.start()
        copy.wait()

    return pl.pallas_call(
        kernel,
        out_shape=[shaped((ALL_CONTENT, D), WIDE), shaped((SEQS * picks, D), WIDE), TOKEN],
        in_specs=[SMEM] + [VMEM] * 9 + [ANY] * len(after),
        out_specs=[VMEM, HBM, VMEM],
        scratch_shapes=[pltpu.VMEM((SEQS * picks, D), WIDE), DMA],
        compiler_params=limit(12),
        cost_estimate=cost(3),
        name="finish_rows",
    )(info, *total, *output, *pieces, *matrices[:3], *after)


def attend_grads(info, pair, early, mine, arrived, small, after=()):
    def kernel(info, small, *refs):
        pairs_in, earlies, mines, arriveds = (refs[2 * i : 2 * i + 2] for i in range(4))
        refs = refs[8 + len(after) :]
        outs, extra, rest = refs[:5], refs[5], refs[6:]
        a_rows, a_content, b_rows, b_content, stage, far_small, sems, out_sems = rest
        core, place = info[0], info[1]
        pairs, later = [], []
        for seq in range(SEQS):
            at = slice(seq * ROWS, (seq + 1) * ROWS)
            far = slice((2 + seq) * ROWS, (3 + seq) * ROWS)
            pairs += [
                (pairs_in[seq].at[core], a_rows.at[at]),
                (columns(earlies[seq], core * D, D), a_rows.at[far]),
                (mines[seq].at[core, :ROWS], b_rows.at[at]),
                (arriveds[seq].at[:ROWS], b_rows.at[far]),
            ]
            at = slice(seq * L, (seq + 1) * L)
            far = slice((2 + seq) * L, (3 + seq) * L)
            later += [
                (pairs_in[seq].at[0, :L], a_content.at[at]),
                (earlies[seq].at[:L, :D], a_content.at[far]),
                (mines[seq].at[core, ROWS:], b_content.at[at]),
                (arriveds[seq].at[ROWS : ROWS + L], b_content.at[far]),
            ]
        copies = start_all([(arriveds[1].at[ROWS + L :], far_small)] + pairs + later, sems)
        copies.pop(0).wait()
        extra[...] = (small[...] + far_small[...].astype(WIDE)).astype(LOW)
        sent = start_all([(extra, outs[i].at[2 * QUARTER :]) for i in range(2)], out_sems, 8)
        for block, (former, latter) in enumerate(((a_rows, b_rows), (a_content, b_content))):
            wait_all(copies[8 * block : 8 * block + 8])
            for part in range(3):
                stage[block, part * 256 : (part + 1) * 256] = tn(
                    former[:, part * 256 : (part + 1) * 256], latter[...]
                ).astype(LOW)
            for k in range(4):
                quarter = lax.rem(place + k, 4)
                index, part = PLACES[k, block]
                start = part * QUARTER
                sent += start_all(
                    [
                        (
                            rows_at(stage.at[block], quarter * QUARTER, QUARTER),
                            outs[index].at[start : start + QUARTER],
                        )
                    ],
                    out_sems,
                    block * 4 + k,
                )
        wait_all(sent)

    return pl.pallas_call(
        kernel,
        out_shape=term_shapes(QUARTER, SMALL) + [shaped((SMALL, D), LOW)],
        in_specs=[SMEM, VMEM] + [ANY] * (8 + len(after)),
        out_specs=[ANY] * 5 + [VMEM],
        scratch_shapes=[
            pltpu.VMEM((2 * ALL_ROWS, D), LOW),
            pltpu.VMEM((2 * ALL_CONTENT, D), LOW),
            pltpu.VMEM((2 * ALL_ROWS, D), LOW),
            pltpu.VMEM((2 * ALL_CONTENT, D), LOW),
            pltpu.VMEM((2, D, D), LOW),
            pltpu.VMEM((SMALL, D), LOW),
            DMA((17,)),
            DMA((10,)),
        ],
        compiler_params=limit(12),
        cost_estimate=cost(5),
        name="attend_grads",
    )(info, small, *pair, *early, *mine, *arrived, *after)


def small_kernel(body, name, shapes, inputs, after=(), info=None, through=()):
    first = [] if info is None else [info]
    given = len(first) + len(inputs)

    def kernel(*refs):
        outs = refs[given + len(after) + len(through) :]
        body(*refs[:given], *outs[: len(shapes)])

    return pl.pallas_call(
        kernel,
        out_shape=[shaped(shape, LOW) for shape in shapes]
        + [shaped(array.shape, array.dtype) for array in through],
        in_specs=[SMEM] * len(first)
        + [VMEM] * len(inputs)
        + [ANY] * (len(after) + len(through)),
        out_specs=[VMEM] * len(shapes) + [ANY] * len(through),
        input_output_aliases={
            given + len(after) + i: len(shapes) + i for i in range(len(through))
        },
        compiler_params=limit(8),
        cost_estimate=cost(1),
        name=name,
    )(*first, *inputs, *after, *through)


def total_of(*terms):
    return sum(term.astype(WIDE) for term in terms).astype(LOW)


def ring_add(after0, before1, from_left, from_right, after=()):
    count = after0.shape[0]
    extra = from_left.shape[0] - 2 * count

    def body(after0, before1, from_left, from_right, right, left):
        right[:count] = total_of(after0[...], from_left[:count])
        left[:count] = total_of(before1[...], from_right[:count])
        if extra:
            right[count:] = from_left[2 * count :]
            left[count:] = from_right[2 * count :]

    return small_kernel(
        body,
        "ring_add",
        [(count + extra, D)] * 2,
        (after0, before1, from_left, from_right),
        after,
    )


def ring_sum(info, own, left, right, from_left, from_right, after=(), small=()):
    count = own.shape[0] // 2
    part = count // 4
    extra = sum(array.shape[0] for array in small)

    def body(info, own, left, right, from_left, from_right, *outs):
        if extra:
            small, outs = outs[0], outs[1:]
            total = total_of(
                small[...], from_left[2 * count :], from_right[2 * count :], left[count:]
            )
        for k, out in enumerate(outs):
            at = pl.multiple_of(lax.rem(info[3] + k, 4) * part, 16)
            low, high = pl.ds(at, part), pl.ds(at + count, part)
            out[:part] = total_of(own[low], left[low], from_right[high])
            out[part : 2 * part] = total_of(own[high], from_left[high], right[low])
            if extra:
                out[2 * part :] = total

    return small_kernel(
        body,
        "ring_sum",
        [(2 * part + extra, D)] * 4,
        (own, left, right, from_left, from_right, *small),
        after,
        info,
    )


def add_all(name, terms, after=()):
    def body(*refs):
        refs[-1][...] = total_of(*(ref[...] for ref in refs[:-1]))

    return small_kernel(body, name, [terms[0].shape], terms, after)[0]


def split_sum(one, two, count):
    middle = count + S_TABLE

    def body(one, two, *outs):
        total = total_of(one[...], two[...])
        outs[0][...] = total[:count]
        outs[1][...] = total[count:middle]
        outs[2][...] = total[middle:]

    shapes = [(count, D), (S_TABLE, D), (SMALL - S_TABLE, D)]
    return small_kernel(body, "z_sum", shapes, (one, two))


def finish_small(small, table, far, after=()):
    places = [n for n in range(S_TABLE) if not S_EXPAND <= n < S_EXPAND + 4]

    def kernel(small, table, far, *refs):
        vectors, (b_expand, whole, done) = refs[len(after) : -3], refs[-3:]
        done[...] = jnp.zeros_like(done)
        values = small[...].astype(WIDE)
        for place, vector in zip(places, vectors):
            vector[...] = values[place : place + 1]
        for column in range(4):
            lanes = slice(column * D, (column + 1) * D)
            b_expand[:, lanes] = values[S_EXPAND + column : S_EXPAND + column + 1]
        total = table[...].astype(WIDE) + far[...].astype(WIDE)
        heads = [total[:, column * L : (column + 1) * L] for column in range(4)]
        whole[...] = jnp.concatenate(heads).T[:NB, :H]

    *vectors, b_expand, whole, done = pl.pallas_call(
        kernel,
        out_shape=[shaped((1, D), WIDE)] * len(places)
        + [shaped((1, FF), WIDE), shaped((NB, H), WIDE), TOKEN],
        in_specs=[VMEM] * 3 + [ANY] * len(after),
        out_specs=[VMEM] * (len(places) + 3),
        compiler_params=limit(4),
        cost_estimate=cost(1),
        name="finish_small",
    )(small, table, far, *after)
    return dict(zip(places, vectors)), b_expand, whole, done


def inner_join(info, parts, after=(), through=()):
    part = parts[0].shape[0] // 2

    def body(info, *refs):
        whole = refs[-1]
        for k, ref in enumerate(refs[:-1]):
            at = pl.multiple_of(lax.rem(info[3] + k, 4) * part, 16)
            whole[pl.ds(at, part)] = ref[:part]
            whole[pl.ds(at + 4 * part, part)] = ref[part:]

    return small_kernel(body, "inner_join", [(8 * part, D)], parts, after, info, through)


def cut(arrays, after=()):
    rows = arrays[0].shape[0]
    count = rows // 2

    def body(*refs):
        arrays, (right, left, whole) = refs[:-3], refs[-3:]
        right[...] = arrays[0][:count]
        left[...] = arrays[1][count:]
        for index, ref in enumerate(arrays):
            whole[index * rows : (index + 1) * rows] = ref[...]

    shapes = [(count, D), (count, D), (len(arrays) * rows, D)]
    return small_kernel(body, "cut", shapes, arrays, after)


def feed_targets(outs, source, half, core, quarter):
    pairs = []
    for block in range(2):
        part = source.at[block * QUARTER : (block + 1) * QUARTER]
        if half == 0:
            target = rows_at(outs[0], core * HALF + block * D + quarter * QUARTER, QUARTER)
        else:
            target = columns(
                rows_at(outs[1], quarter * QUARTER, QUARTER), (core * 2 + block) * D, D
            )
        pairs.append((None, part, target))
    return pairs


def attend_targets(outs, source, half, core, quarter):
    return [
        (
            core == number,
            source.at[:QUARTER],
            rows_at(outs[2 * number + half], quarter * QUARTER, QUARTER),
        )
        for number in range(2)
    ]


def settle(targets, shapes, count, info, pieces, outs, name, after=()):
    keys = tuple(pieces)
    arrays = [pieces[key] for key in keys]
    given = list(after) + list(outs or ())

    def kernel(info, *refs):
        parts, rest = refs[: len(keys)], refs[len(keys) + len(given) :]
        outs, rest = rest[: len(shapes)], rest[len(shapes) :]
        done, rest = rest[0], rest[1:]
        done[...] = jnp.zeros_like(done)
        wide_held, out_sems = rest[:-1], rest[-1]
        finish = []
        for index, (sibling, places) in enumerate(keys):
            core = 1 - info[0] if sibling else info[0]
            for number, (k, half) in enumerate(places):
                quarter = lax.rem((info[3] if sibling else info[1]) + k, 4)
                source = wide_held[index].at[number * count : (number + 1) * count]
                source[...] = parts[index][number * count : (number + 1) * count].astype(WIDE)
                for place, (condition, part, target) in enumerate(
                    targets(outs, source, half, core, quarter)
                ):
                    copy = pltpu.make_async_copy(
                        part, target, out_sems.at[12 * index + 2 * number + place]
                    )
                    if condition is None:
                        copy.start()
                        finish.append(copy.wait)
                    else:
                        pl.when(condition)(copy.start)
                        finish.append(lambda c=copy, when=condition: pl.when(when)(c.wait))
        for action in finish:
            action()

    result = pl.pallas_call(
        kernel,
        out_shape=[shaped(shape, WIDE) for shape in shapes]
        + [TOKEN],
        in_specs=[SMEM] + [VMEM] * len(keys) + [ANY] * len(given),
        out_specs=[ANY] * len(shapes) + [VMEM],
        scratch_shapes=[pltpu.VMEM(array.shape, WIDE) for array in arrays]
        + [DMA((12 * len(keys),))],
        input_output_aliases={
            1 + len(keys) + len(after) + i: i for i in range(len(outs or ()))
        },
        compiler_params=limit(20),
        cost_estimate=cost(sum(array.size for array in arrays) * 2e-6 + 1),
        name=name,
    )(info, *arrays, *given)
    return result[:-1], result[-1]


PLANE = ("x", "y", "c")


def shift(value, axis, by):
    size = lax.axis_size(axis)
    return lax.ppermute(value, axis, [(i, (i + by) % size) for i in range(size)])


def send(value, by):
    return lax.ppermute(value, "s", [(0, 1)] if by > 0 else [(1, 0)])


def turn(value, outer, by):
    pairs = []
    for i in range(4):
        for j in range(4):
            for c in range(2):
                if (c == 0) == outer:
                    target = ((i + by) % 4, j)
                else:
                    target = (i, (j + by) % 4)
                pairs.append(((i * 4 + j) * 2 + c, (target[0] * 4 + target[1]) * 2 + c))
    return lax.ppermute(value, PLANE, pairs)


def place(outer):
    return jnp.where(
        (lax.axis_index("c") == 0) == outer, lax.axis_index("x"), lax.axis_index("y")
    )


def wide(value):
    return value.astype(WIDE)


def total_wide(*terms):
    return sum(wide(term) for term in terms)


def inner_turns(parts, sign):
    return [turn(part, False, sign * by) for part, by in zip(parts, (1, 2, -1))]


OWN, ACROSS = ((0, 0), (0, 1)), (((2, 0),), ((2, 1),))
NEAR = ((3, 0), (3, 1), (1, 0), (1, 1))


def both_cores(places, piece):
    return {(0, places): piece, (1, places): shift(piece, "c", 1)}


def on_device(
    content_in,
    query_in,
    content_cot,
    query_cot,
    order_rank,
    query_pos,
    group_tag,
    *rest,
):
    (
        w_query,
        b_query,
        w_key,
        w_value,
        b_value,
        w_out,
        b_out,
        norm1_gain,
        norm1_bias,
        w_expand,
        b_expand,
        w_contract,
        b_contract,
        norm2_gain,
        norm2_bias,
    ) = (argument[0] for argument in rest[:-1])
    rel_table = rest[-1]
    core = lax.axis_index("c")
    first_section = (lax.axis_index("s") == 0).astype(jnp.int32)
    info = jnp.stack([core, place(True), first_section, place(False)])
    picks = query_pos.shape[1]

    matrices = (w_query, w_key, w_value, w_out, w_expand, w_contract)
    w_out_held = w_out
    vec = jnp.stack(
        [b_query, b_value, b_out, norm1_gain, norm1_bias, b_contract, norm2_gain, norm2_bias]
    )
    ranks = jnp.concatenate([order_rank, group_tag, query_pos], axis=1)
    masks, spread, query_in, query_cot = prepare(
        ranks, rel_table, query_in, query_cot, picks, (vec, info)
    )
    b_expand = b_expand[None]

    fronts, arrived = [], []
    for seq in range(SEQS):
        fronts.append(
            front(seq, info, content_in, query_in, matrices, masks, vec, b_expand, tuple(fronts))
        )
        arrived.append(send(fronts[seq], 1))
    output, early, pair, saved, grads = [], [], [], [], []
    for seq in range(SEQS):
        results = middle_forward(
            seq, info, content_in, query_in, arrived[seq], matrices, masks, vec, b_expand, tuple(grads)
        )
        for collected, result in zip((output, early, pair, saved), results):
            collected.append(result)
        grads.append(middle_back(seq, content_cot, query_cot, matrices, vec, saved[seq]))
    early = [shift(value, "c", 1) for value in early]
    grads = [send(value, -1) for value in grads]
    small = None
    total, branch, attended, own, late, pieces, pass_on = [], [], [], [], [], [], []
    for seq in range(SEQS):
        results = feed_back(
            seq,
            info,
            grads[seq],
            content_cot,
            query_cot,
            small,
            vec,
            matrices,
            saved[seq],
            tuple(pass_on),
        )
        small = results[3]
        for collected, result in zip(
            (total, branch, attended, own, late), results[:3] + results[4:]
        ):
            collected.append(result)
        late[seq] = shift(late[seq], "c", 1)
        results = attend_back(
            seq,
            info,
            attended[seq],
            small,
            spread,
            (),
            w_out_held,
            saved[seq],
        )
        small = results[2]
        pieces.append(results[0])
        pass_on.append(results[1])
    feed_terms = feed_grads(info, saved, branch, own, early, late, (small,))
    passed = [shift(value, "c", 1) for value in pass_on]

    def outer_step(terms):
        return (turn(terms[0], True, 1), turn(terms[1], True, -1))

    f_left, f_right = outer_step(feed_terms)
    *attend_terms, extra = attend_grads(info, pair, early, pieces, passed, small, (feed_terms[4],))
    a_left, a_right = outer_step(attend_terms)
    f_sent = ring_add(feed_terms[2], feed_terms[3], f_left, f_right, (extra,))
    f_parts = ring_sum(info, feed_terms[4], *outer_step(f_sent), f_left, f_right)
    f_others = inner_turns(f_parts[1:], 1)
    a_sent = ring_add(attend_terms[2], attend_terms[3], a_left, a_right, (f_parts[0],))
    content_ends, query_ends, token = finish_rows(
        info, total, output, pieces, matrices, picks, (a_sent[0],)
    )
    f_part = add_all("inner_sum", [f_parts[0]] + f_others, (token,))
    f_far = shift(f_part, "z", 1)
    a_parts = ring_sum(
        info, attend_terms[4], *outer_step(a_sent), a_left, a_right, (f_part,), (extra,)
    )
    f_part = add_all("z_sum", [f_part, f_far])
    f_others = inner_turns([f_part] * 3, -1)
    a_part = add_all("inner_sum", [a_parts[0]] + inner_turns(a_parts[1:], 1))
    (feed_own,) = inner_join(info, [f_part] + f_others, (a_part,))
    feed_outer = (turn(feed_own, True, 1), turn(feed_own, True, -1))
    a_part, small, table = split_sum(a_part, shift(a_part, "z", 1), 2 * QUARTER // 4)
    a_others = inner_turns([a_part] * 3, -1)

    def feed_settle(pieces, outs, name):
        return settle(
            feed_targets, ((FF, D), (D, FF)), 2 * QUARTER, info, pieces, outs, "feed_" + name
        )

    def attend_settle(pieces, outs, name, after=()):
        return settle(
            attend_targets,
            ((D, D),) * 4,
            QUARTER,
            info,
            pieces,
            outs,
            "attend_" + name,
            after,
        )

    feed_outs, token = feed_settle(both_cores(OWN, feed_own), None, "own")
    to_right, to_left, feed_near = cut(feed_outer, (token, *a_others))
    feed_across = (turn(to_right, True, 1), turn(to_left, True, -1))
    (attend_own,) = inner_join(info, [a_part] + a_others, (to_right,))
    attend_outer = (turn(attend_own, True, 1), turn(attend_own, True, -1))
    feed_outs, token = feed_settle(both_cores(NEAR, feed_near), feed_outs, "near")
    row, b_expand, table, small_token = finish_small(small, table, shift(table, "s", 1), (token,))
    to_right, to_left, attend_near = cut(
        (*attend_outer, attend_own), (token, small_token, *feed_across)
    )
    attend_across = (turn(to_right, True, 1), turn(to_left, True, -1))
    feed_outs, _ = feed_settle(
        both_cores(ACROSS[0], feed_across[0]) | both_cores(ACROSS[1], feed_across[1]),
        feed_outs,
        "across",
    )
    attend_both = both_cores(NEAR + OWN, attend_near)
    attend_outs, _ = attend_settle(attend_both, None, "near")
    attend_outs, _ = attend_settle(
        both_cores(ACROSS[0], attend_across[0]) | both_cores(ACROSS[1], attend_across[1]),
        attend_outs,
        "across",
    )
    contract, expand = feed_outs
    g_query, g_key, g_out, g_value = attend_outs
    return (
        content_ends[None],
        query_ends[None],
        g_query[None],
        row[S_QUERY],
        g_key[None],
        g_value[None],
        row[S_VALUE],
        g_out[None],
        row[S_OUT],
        row[S_GAIN1],
        row[S_SHIFT1],
        expand[None],
        b_expand,
        contract[None],
        row[S_CONTRACT],
        row[S_GAIN2],
        row[S_SHIFT2],
        table,
    )


DP = ("z", "x", "y", "c")


def solution(mesh):
    mesh = jax.sharding.Mesh(mesh.devices.reshape(2, 2, 4, 4, 2), ("s",) + DP)
    layer_specs = tuple(
        P("s", *([None] * (rank - 1))) for rank in (3, 2, 3, 3, 2, 3, 2, 2, 2, 3, 2, 3, 2, 2, 2)
    )
    in_specs = (P(DP, None),) * 7 + layer_specs + (P(),)
    out_specs = (P("s", DP, None),) * 2 + layer_specs + (P(),)
    return jax.shard_map(
        on_device, mesh=mesh, in_specs=in_specs, out_specs=out_specs, check_vma=False
    )
```

```python
import jax
import jax.numpy as jnp
from jax import lax
from jax.experimental import pallas as pl
from jax.experimental.pallas import tpu as pltpu
from jax.sharding import PartitionSpec as P

D = 768
H = 12
HD = 64
FF = 3072
NB = 32
L = 128
PAIRS = H // 2
SEQS = 2
PICKS = 32
ROWS = L + PICKS
EPSILON = 1e-05
SCALE = HD ** (-0.5)
TILE = 1536
LOW = jnp.bfloat16
WIDE = jnp.float32
HALF = FF // 2
QUARTER = D // 4
EARLY = 3 * D + HALF
LATE = D + HALF
SMALL = 16
ALL_ROWS = SEQS * ROWS
ALL_CONTENT = SEQS * L
PIECE = ALL_ROWS + ALL_CONTENT


def nn(former, latter):
    return lax.dot_general(
        former, latter, (((1,), (0,)), ((), ())), preferred_element_type=WIDE
    )


def nt(former, latter):
    return lax.dot_general(
        former, latter, (((1,), (1,)), ((), ())), preferred_element_type=WIDE
    )


def tn(former, latter):
    return lax.dot_general(
        former, latter, (((0,), (0,)), ((), ())), preferred_element_type=WIDE
    )


def halves(value):
    even = lax.broadcasted_iota(jnp.int32, value.shape, 1) < HD
    zero = jnp.zeros_like(value)
    return jnp.concatenate([jnp.where(even, value, zero), jnp.where(even, zero, value)])


def side(value):
    count = value.shape[0] // 2
    return jnp.concatenate([value[:count], value[count:]], axis=1)


def norm_rows(values):
    centered = values - jnp.mean(values, axis=-1, keepdims=True)
    variance = jnp.mean(centered * centered, axis=-1, keepdims=True)
    root = lax.rsqrt(variance + EPSILON)
    return (centered * root, root)


def norm_rows_back(scaled, normed, root):
    return root * (
        scaled
        - jnp.mean(scaled, axis=-1, keepdims=True)
        - normed * jnp.mean(scaled * normed, axis=-1, keepdims=True)
    )


B_QUERY, B_VALUE, B_OUT, GAIN1, SHIFT1, B_CONTRACT, GAIN2, SHIFT2 = range(8)
S_QUERY, S_VALUE, S_OUT, S_GAIN1, S_SHIFT1, S_EXPAND = range(6)
S_CONTRACT, S_GAIN2, S_SHIFT2, S_TABLE = 9, 10, 11, 12
LIMITS = (12, 16, 23, 32, 46, 64, 91)


def bucket_of(relative):
    distance = jnp.abs(relative)
    beyond = 8 + sum((distance >= limit).astype(jnp.int32) for limit in LIMITS)
    within = jnp.where(distance < 8, distance, beyond)
    return within + 16 * (relative > 0).astype(jnp.int32)


def forward(x, w, vec, b_expand, masks, s, keep):
    row = lambda k: vec[k : k + 1, :]
    s.query[...] = (nn(x[...], w.query[...]) + row(B_QUERY)).astype(LOW)
    s.key[...] = nn(x[:L], w.key[...]).astype(LOW)
    s.value[...] = (nn(x[:L], w.value[...]) + row(B_VALUE)).astype(LOW)
    for pair in range(PAIRS):
        lanes = slice(pair * 128, (pair + 1) * 128)
        scores = nt(halves(s.query[:, lanes]), s.key[:, lanes]) * SCALE + masks[pair]
        shifted = jnp.exp(scores - jnp.max(scores, axis=-1, keepdims=True))
        probs = (shifted / jnp.sum(shifted, axis=-1, keepdims=True)).astype(LOW)
        if keep:
            s.probs[pair] = probs
        s.mixed[:, lanes] = nn(side(probs), halves(s.value[:, lanes])).astype(LOW)
    total = x[...].astype(WIDE) + nn(s.mixed[...], w.out[...]) + row(B_OUT)
    normed, root = norm_rows(total)
    first = normed * row(GAIN1) + row(SHIFT1)
    s.first_low[...] = first.astype(LOW)
    s.total[...] = first + row(B_CONTRACT)
    if keep:
        s.normed1[...] = normed
        s.root1[...] = jnp.broadcast_to(root, (ROWS, 128))
    for tile in range(FF // TILE):
        tile = slice(tile * TILE, (tile + 1) * TILE)
        expanded = nn(s.first_low[...], w.expand[:, tile]) + b_expand[:, tile]
        cumulative = 0.5 * (1.0 + lax.erf(expanded * 0.7071067811865476))
        activated = (expanded * cumulative).astype(LOW)
        if keep:
            s.slope[:, tile] = (
                cumulative + expanded * jnp.exp(-0.5 * expanded * expanded) * 0.3989422804014327
            ).astype(LOW)
            s.activated[:, tile] = activated
        s.total[...] += nn(activated, w.contract[tile, :])
    normed, root = norm_rows(s.total[...])
    if keep:
        s.normed2[...] = normed
        s.root2[...] = jnp.broadcast_to(root, (ROWS, 128))
    s.out[...] = (normed * row(GAIN2) + row(SHIFT2)).astype(s.out.dtype)


def column_sum(value):
    return jnp.sum(value.astype(WIDE), axis=0, keepdims=True)


def back_second_norm(grad, vec, s, add=None):
    upper = grad.astype(WIDE)
    normed = s.normed2[...]
    lower = norm_rows_back(upper * vec[GAIN2 : GAIN2 + 1, :], normed, s.root2[:, :1])
    s.total[...] = lower
    s.branch[...] = lower.astype(LOW)
    if add is not None:
        add(S_GAIN2, column_sum(upper * normed))
        add(S_SHIFT2, column_sum(upper))
        add(S_CONTRACT, column_sum(lower.astype(LOW)))


def back_feed(w, vec, s, add=None):
    for tile in range(FF // TILE):
        tile = slice(tile * TILE, (tile + 1) * TILE)
        lower = (nt(s.branch[...], w.contract[tile, :]) * s.slope[:, tile].astype(WIDE)).astype(LOW)
        s.expanded[:, tile] = lower
        if add is not None:
            part = column_sum(lower)
            for column in range(TILE // D):
                add(
                    S_EXPAND + tile.start // D + column,
                    part[:, column * D : (column + 1) * D],
                )
        s.total[...] += nt(lower, w.expand[:, tile])
    upper = s.total[...]
    normed = s.normed1[...]
    lower = norm_rows_back(upper * vec[GAIN1 : GAIN1 + 1, :], normed, s.root1[:, :1])
    s.total[...] = lower
    s.attended[...] = lower.astype(LOW)
    if add is not None:
        add(S_GAIN1, column_sum(upper * normed))
        add(S_SHIFT1, column_sum(upper))
        add(S_OUT, column_sum(lower.astype(LOW)))


def back_attend(s, table=None):
    for pair in range(PAIRS):
        lanes = slice(pair * 128, (pair + 1) * 128)
        probs = s.probs[pair]
        below = halves(s.dmixed[:, lanes])
        dprobs = nt(below, s.value[:, lanes])
        s.dvalue[:, lanes] = tn(probs, below).astype(LOW)
        weight = probs.astype(WIDE)
        dscores = (
            weight * (dprobs - jnp.sum(weight * dprobs, axis=-1, keepdims=True))
        ).astype(LOW)
        s.dquery[:, lanes] = (nn(side(dscores), halves(s.key[:, lanes])) * SCALE).astype(LOW)
        s.dkey[:, lanes] = (tn(dscores, halves(s.query[:, lanes])) * SCALE).astype(LOW)
        if table is not None:
            table(pair, dscores)


class Names:
    def __init__(self, **named):
        self.__dict__.update(named)


MATRICES = ("query", "key", "value", "out", "expand", "contract")
MATRIX_SHAPES = {
    "query": (D, D),
    "key": (D, D),
    "value": (D, D),
    "out": (D, D),
    "expand": (D, FF),
    "contract": (FF, D),
}
MASK_SHAPE = (PAIRS, 2 * ROWS, L)
KEPT = {
    "query": ((ROWS, D), LOW),
    "key": ((L, D), LOW),
    "value": ((L, D), LOW),
    "probs": (MASK_SHAPE, LOW),
    "mixed": ((ROWS, D), LOW),
    "normed1": ((ROWS, D), WIDE),
    "root1": ((ROWS, 128), WIDE),
    "first_low": ((ROWS, D), LOW),
    "slope": ((ROWS, FF), LOW),
    "activated": ((ROWS, FF), LOW),
    "normed2": ((ROWS, D), WIDE),
    "root2": ((ROWS, 128), WIDE),
}
SAVED = tuple(name for name in KEPT if name != "mixed")
ANY = pl.BlockSpec(memory_space=pl.ANY)
HBM = pl.BlockSpec(memory_space=pltpu.HBM)
VMEM = pl.BlockSpec(memory_space=pltpu.VMEM)
SMEM = pl.BlockSpec(memory_space=pltpu.SMEM)


def limit(megabytes):
    return pltpu.CompilerParams(vmem_limit_bytes=megabytes * 1024 * 1024)


DMA = pltpu.SemaphoreType.DMA


def cost(microseconds):
    return pl.CostEstimate(flops=0, bytes_accessed=int(microseconds * 3.2e6), transcendentals=0)


def shaped(shape, kind):
    return jax.ShapeDtypeStruct(shape, kind)


TOKEN = shaped((8, 128), WIDE)


def columns(ref, start, size):
    return ref.at[:, pl.ds(pl.multiple_of(start, 128), size)]


def rows_at(ref, start, size):
    return ref.at[pl.ds(pl.multiple_of(start, 64), size)]


def start_all(pairs, sems, base=0):
    copies = [
        pltpu.make_async_copy(source, target, sems.at[base + index])
        for index, (source, target) in enumerate(pairs)
    ]
    for copy in copies:
        copy.start()
    return copies


def wait_all(copies):
    for copy in copies:
        copy.wait()


def fetcher(names, sources, targets, sems, base=0):
    copies = dict(zip(names, start_all(list(zip(sources, targets)), sems, base)))
    return lambda name: copies[name].wait()


def prepare(ranks, table, queries, picks, after):
    def kernel(ranks, table, queries, *refs):
        masks, spread, rows_in, rows_cot = refs[len(after) :]
        order, tag, pos = ranks[:, :L], ranks[:, L : 2 * L], ranks[:, 2 * L : 2 * L + picks]
        values = queries[...].astype(WIDE)
        blank = jnp.zeros((PICKS - picks, D), WIDE)
        for index, target in enumerate((rows_in, rows_cot)):
            own = values[2 * index * picks : 2 * (index + 1) * picks]
            target[...] = jnp.concatenate([own[:picks], blank, own[picks:], blank]).astype(LOW)
        lane = lax.broadcasted_iota(jnp.int32, (L, L), 1)
        level = lax.broadcasted_iota(jnp.int32, (L, L), 0)
        lane_q = lax.broadcasted_iota(jnp.int32, (PICKS, L), 1)
        upright = lambda row: jnp.sum(jnp.where(lane == level, row, 0.0), axis=1, keepdims=True)
        distance = lax.broadcasted_iota(jnp.int32, (2 * L, NB), 0) - (L - 1)
        bucket = lax.broadcasted_iota(jnp.int32, (2 * L, NB), 1)
        by_distance = lax.dot_general(
            table[...],
            (bucket_of(distance) == bucket).astype(WIDE),
            (((0,), (1,)), ((), ())),
            precision=lax.Precision.HIGHEST,
            preferred_element_type=WIDE,
        )
        allowed, hot = [], []
        for seq in range(SEQS):
            own_rank = order[seq : seq + 1, :].astype(WIDE)
            own_tag = tag[seq : seq + 1, :].astype(WIDE)
            own_pos = pos[seq : seq + 1, :].astype(WIDE)
            number = lax.broadcasted_iota(jnp.int32, (PICKS, picks), 0)
            same = number == lax.broadcasted_iota(jnp.int32, (PICKS, picks), 1)
            place = jnp.sum(jnp.where(same, own_pos, 0.0), axis=1, keepdims=True)
            filled = lax.broadcasted_iota(jnp.int32, (PICKS, 1), 0) < picks
            place = jnp.where(filled, place, -1.0).astype(jnp.int32)
            matches = place == lane_q
            marks = jnp.where(matches, 1.0, 0.0)
            predicted = jnp.max(marks, axis=0, keepdims=True)
            rank = jnp.sum(jnp.where(matches, own_rank, 0.0), axis=1, keepdims=True)
            group = jnp.sum(jnp.where(matches, own_tag, 0.0), axis=1, keepdims=True)
            earlier = (upright(predicted) > 0) & (own_rank <= upright(own_rank))
            content = (upright(own_tag) == own_tag) & ((predicted == 0) | earlier)
            query = (group == own_tag) & ((predicted == 0) | (own_rank + 1 <= rank))
            allowed.append((content, query))
            hot.append(marks)
            spread[seq, :L] = jnp.where(lane == L - 1 - level, 1.0, 0.0).astype(LOW)
            spread[seq, L:] = jnp.where(lane_q == L - 1 - place, 1.0, 0.0).astype(LOW)
        hot = jnp.concatenate(hot)
        for head in range(H):
            row = jnp.broadcast_to(by_distance[head : head + 1], (L, 2 * L))
            bias = pltpu.roll(row, L + 1, 1, stride=1, stride_axis=0)[:, :L]
            bias_q = lax.dot_general(
                hot,
                bias,
                (((1,), (0,)), ((), ())),
                precision=lax.Precision.HIGHEST,
                preferred_element_type=WIDE,
            )
            base = head % 2 * ROWS
            for seq in range(SEQS):
                content, query = allowed[seq]
                masks[seq, head // 2, base : base + L] = jnp.where(content, bias, -1e30)
                masks[seq, head // 2, base + L : base + ROWS] = jnp.where(
                    query, bias_q[seq * PICKS : (seq + 1) * PICKS], -1e30
                )

    return pl.pallas_call(
        kernel,
        out_shape=[
            shaped((SEQS,) + MASK_SHAPE, WIDE),
            shaped((SEQS, ROWS, L), LOW),
            shaped((SEQS * PICKS, D), LOW),
            shaped((SEQS * PICKS, D), LOW),
        ],
        in_specs=[VMEM] * 3 + [ANY] * len(after),
        out_specs=[VMEM] * 4,
        compiler_params=limit(8),
        cost_estimate=pl.CostEstimate(flops=int(3e10), bytes_accessed=0, transcendentals=0),
        name="prepare",
    )(ranks, table, queries, *after)


def take_rows(content, picks, seq, target):
    target[:L] = content[seq * L : (seq + 1) * L]
    target[L:] = picks[seq * PICKS : (seq + 1) * PICKS]


def front(seq, info, content, picks, matrices, masks, vec, b_expand, after=()):
    def kernel(info, content, picks, masks, vec, b_expand, *refs):
        w = Names(**dict(zip(MATRICES, refs[:6])))
        out, x, query, key, value, mixed, first_low, total = refs[6 + len(after) :]
        s = Names(
            query=query,
            key=key,
            value=value,
            mixed=mixed,
            first_low=first_low,
            total=total,
            out=out,
        )
        take_rows(content, picks, seq, x)
        forward(x, w, vec, b_expand, masks.at[seq], s, False)

    return pl.pallas_call(
        kernel,
        out_shape=shaped((ROWS, D), LOW),
        in_specs=[SMEM] + [VMEM] * 11 + [ANY] * len(after),
        out_specs=VMEM,
        scratch_shapes=[pltpu.VMEM((ROWS, D), LOW)]
        + [pltpu.VMEM(*KEPT[n]) for n in ("query", "key", "value", "mixed", "first_low")]
        + [pltpu.VMEM((ROWS, D), WIDE)],
        compiler_params=limit(12),
        cost_estimate=cost(5),
        name="front",
    )(info, content, picks, masks, vec, b_expand, *matrices, *after)


def middle_forward(seq, info, content, picks, arrived, matrices, masks, vec, b_expand, after=()):
    def kernel(info, arrived, content, picks, masks, vec, b_expand, *refs):
        w, rest = Names(**dict(zip(MATRICES, refs[:6]))), refs[6 + len(after) :]
        (out, early, pair), kept = rest[:3], rest[3 : 3 + len(SAVED)]
        mixed, total = rest[3 + len(SAVED) :]
        x = pair.at[0]
        s = Names(total=total, out=out, mixed=mixed, **dict(zip(SAVED, kept)))
        take_rows(content, picks, seq, x)
        x[...] = jnp.where(info[2] == 1, x[...], arrived[...])
        early[:, :D] = x[...]
        forward(x, w, vec, b_expand, masks.at[seq], s, True)
        pair[1] = mixed[...]
        early[:, D : 2 * D] = mixed[...]
        early[:, 2 * D : 3 * D] = s.first_low[...]
        early[:, 3 * D :] = columns(s.activated, (1 - info[0]) * HALF, HALF)[...]

    out, early, pair, *saved = pl.pallas_call(
        kernel,
        out_shape=[
            shaped((ROWS, D), WIDE),
            shaped((ROWS, EARLY), LOW),
            shaped((2, ROWS, D), LOW),
        ]
        + [shaped(*KEPT[n]) for n in SAVED],
        in_specs=[SMEM] + [VMEM] * 12 + [ANY] * len(after),
        out_specs=[VMEM] * (3 + len(SAVED)),
        scratch_shapes=[pltpu.VMEM(*KEPT["mixed"]), pltpu.VMEM((ROWS, D), WIDE)],
        compiler_params=limit(16),
        cost_estimate=cost(6),
        name="middle_forward",
    )(info, arrived, content, picks, masks, vec, b_expand, *matrices, *after)
    return (out, early, pair, dict(zip(SAVED, saved)))


FEED_SAVED = ("normed2", "root2", "slope", "normed1", "root1")
ATTEND_SAVED = ("value", "probs", "key", "query")


def middle_back(seq, content, picks, matrices, vec, saved):
    names = FEED_SAVED + ATTEND_SAVED

    def kernel(content, picks, vec, *refs):
        w, rest = Names(**dict(zip(MATRICES, refs[:6]))), refs[6:]
        kept, grad, rest = rest[: len(names)], rest[len(names)], rest[len(names) + 1 :]
        cot, total, branch, expanded, attended, dmixed, dvalue, dquery, dkey = rest
        s = Names(
            total=total,
            branch=branch,
            expanded=expanded,
            attended=attended,
            dmixed=dmixed,
            dvalue=dvalue,
            dquery=dquery,
            dkey=dkey,
            **dict(zip(names, kept)),
        )
        take_rows(content, picks, seq, cot)
        back_second_norm(cot[...], vec, s)
        back_feed(w, vec, s)
        dmixed[...] = nt(attended[...], w.out[...]).astype(LOW)
        back_attend(s)
        lower = total[...] + nt(dquery[...], w.query[...])
        upper = nt(dkey[...], w.key[...]) + nt(dvalue[...], w.value[...])
        grad[:L] = (lower[:L] + upper).astype(LOW)
        grad[L:] = lower[L:].astype(LOW)

    return pl.pallas_call(
        kernel,
        out_shape=shaped((ROWS, D), LOW),
        in_specs=[VMEM] * (9 + len(names)),
        out_specs=VMEM,
        scratch_shapes=[
            pltpu.VMEM((ROWS, D), LOW),
            pltpu.VMEM((ROWS, D), WIDE),
            pltpu.VMEM((ROWS, D), LOW),
            pltpu.VMEM((ROWS, FF), LOW),
            pltpu.VMEM((ROWS, D), LOW),
            pltpu.VMEM((ROWS, D), LOW),
            pltpu.VMEM((L, D), LOW),
            pltpu.VMEM((ROWS, D), LOW),
            pltpu.VMEM((L, D), LOW),
        ],
        compiler_params=limit(12),
        cost_estimate=cost(7),
        name="middle_back",
    )(content, picks, vec, *matrices, *(saved[n] for n in names))


def feed_back(seq, info, arrived, content, picks, small_in, vec, matrices, saved, after=()):
    given = [] if small_in is None else [small_in]

    def kernel(info, arrived, content, picks, vec, expand, contract, *refs):
        kept, rest = refs[:5], refs[5 + len(given) + len(after) :]
        total, branch, attended, small, own, late, upper, expanded = rest
        w = Names(expand=expand, contract=contract)
        s = Names(
            total=total,
            branch=branch,
            attended=attended,
            expanded=expanded,
            **dict(zip(FEED_SAVED, kept)),
        )
        small[...] = refs[5][...] if given else jnp.zeros_like(small)

        def add(place, value):
            small[place : place + 1, :] += value

        take_rows(content, picks, seq, upper)
        back_second_norm(jnp.where(info[2] == 1, arrived[...], upper[...]), vec, s, add)
        late[:, :D] = branch[...]
        back_feed(w, vec, s, add)
        own[...] = columns(expanded, info[0] * HALF, HALF)[...]
        late[:, D:] = columns(expanded, (1 - info[0]) * HALF, HALF)[...]

    return pl.pallas_call(
        kernel,
        out_shape=[
            shaped((ROWS, D), WIDE),
            shaped((ROWS, D), LOW),
            shaped((ROWS, D), LOW),
            shaped((SMALL, D), WIDE),
            shaped((ROWS, HALF), LOW),
            shaped((ROWS, LATE), LOW),
        ],
        in_specs=[SMEM] + [VMEM] * (11 + len(given)) + [ANY] * len(after),
        out_specs=[VMEM] * 6,
        scratch_shapes=[pltpu.VMEM((ROWS, D), LOW), pltpu.VMEM((ROWS, FF), LOW)],
        compiler_params=limit(12),
        cost_estimate=cost(4),
        name="feed_back",
    )(
        info,
        arrived,
        content,
        picks,
        vec,
        matrices[4],
        matrices[5],
        *(saved[n] for n in FEED_SAVED),
        *given,
        *after,
    )


PLACES = {
    (2, 0): (0, 0),
    (1, 1): (0, 1),
    (2, 1): (1, 0),
    (3, 0): (1, 1),
    (1, 0): (2, 0),
    (3, 1): (3, 0),
    (0, 0): (4, 0),
    (0, 1): (4, 1),
}


def term_shapes(count, extra=0):
    rows = (2 * count + extra, 2 * count + extra, count, count, 2 * count)
    return [shaped((n, D), LOW) for n in rows]


def feed_grads(info, mine, branch, own, early, late, after=()):
    def kernel(info, *refs):
        acts, lows, branches, owns, earlies, lates = (refs[2 * i : 2 * i + 2] for i in range(6))
        refs = refs[:12] + refs[12 + len(after) :]
        outs, (a_act, a_first, b_branch, b_own, stage, out_sems) = refs[12:17], refs[17:]
        core, place = info[0], info[1]
        own_at = [slice(seq * ROWS, (seq + 1) * ROWS) for seq in range(SEQS)]
        far_at = [slice((2 + seq) * ROWS, (3 + seq) * ROWS) for seq in range(SEQS)]
        for seq in range(SEQS):
            at, far = own_at[seq], far_at[seq]
            a_act[at] = columns(acts[seq], core * HALF, HALF)[...]
            a_act[far] = earlies[seq][:, 3 * D :]
            b_branch[at] = branches[seq][...]
            b_branch[far] = lates[seq][:, :D]
        sent = []

        def send(block):
            for k in range(4):
                quarter = lax.rem(place + k, 4)
                index, part = PLACES[k, block // 2]
                start = (2 * part + block % 2) * QUARTER
                sent.extend(
                    start_all(
                        [
                            (
                                rows_at(stage.at[block], quarter * QUARTER, QUARTER),
                                outs[index].at[start : start + QUARTER],
                            )
                        ],
                        out_sems,
                        block * 4 + k,
                    )
                )

        for block in range(2):
            for part in range(3):
                start = block * D + part * 256
                stage[block, part * 256 : (part + 1) * 256] = tn(
                    a_act[:, start : start + 256], b_branch[...]
                ).astype(LOW)
            send(block)
        for seq in range(SEQS):
            at, far = own_at[seq], far_at[seq]
            a_first[at] = lows[seq][...]
            a_first[far] = earlies[seq][:, 2 * D : 3 * D]
            b_own[at] = owns[seq][...]
            b_own[far] = lates[seq][:, D:]
        for block in range(2):
            for part in range(3):
                stage[2 + block, part * 256 : (part + 1) * 256] = tn(
                    a_first[:, part * 256 : (part + 1) * 256], b_own[:, block * D : (block + 1) * D]
                ).astype(LOW)
            send(2 + block)
        wait_all(sent)

    acts = [saved["activated"] for saved in mine]
    lows = [saved["first_low"] for saved in mine]
    return pl.pallas_call(
        kernel,
        out_shape=term_shapes(2 * QUARTER),
        in_specs=[SMEM] + [VMEM] * 12 + [ANY] * len(after),
        out_specs=[ANY] * 5,
        scratch_shapes=[
            pltpu.VMEM((2 * ALL_ROWS, HALF), LOW),
            pltpu.VMEM((2 * ALL_ROWS, D), LOW),
            pltpu.VMEM((2 * ALL_ROWS, D), LOW),
            pltpu.VMEM((2 * ALL_ROWS, HALF), LOW),
            pltpu.VMEM((4, D, D), LOW),
            DMA((16,)),
        ],
        compiler_params=limit(16),
        cost_estimate=cost(8),
        name="feed_grads",
    )(info, *acts, *lows, *branch, *own, *early, *late, *after)


def attend_back(seq, info, attended, small_in, spread, after, w_out, saved):
    def kernel(info, attended, small_in, spread, w_out, *refs):
        kept, (pieces, send, small, dmixed, sums) = refs[:4], refs[4 + len(after) :]
        small[...] = small_in[...]
        pieces[1, :ROWS] = attended[...]
        dmixed[...] = nt(attended[...], w_out[...]).astype(LOW)
        s = Names(
            dmixed=dmixed,
            dquery=pieces.at[0, :ROWS],
            dkey=pieces.at[0, ROWS:],
            dvalue=pieces.at[1, ROWS:],
            **dict(zip(ATTEND_SAVED, kept)),
        )
        sums[...] = jnp.zeros_like(sums)

        def table_sum(pair, dscores):
            for odd in range(2):
                part = tn(spread[seq], dscores[odd * ROWS : (odd + 1) * ROWS])
                both = jnp.concatenate([part, jnp.zeros((L, L), WIDE)], axis=1)
                turned = pltpu.roll(both, 0, 1, stride=1, stride_axis=0)
                head = 2 * pair + odd
                sums[head : head + 1, :] = jnp.sum(turned, axis=0, keepdims=True)

        back_attend(s, table_sum)
        send[: ROWS + L] = pieces[1 - info[0]]
        small[S_QUERY : S_QUERY + 1, :] += column_sum(pieces[0, :ROWS])
        small[S_VALUE : S_VALUE + 1, :] += column_sum(pieces[1, ROWS:])
        distance = lax.broadcasted_iota(jnp.int32, (2 * L, L), 0) - (L - 1)
        bucket = lax.broadcasted_iota(jnp.int32, (2 * L, L), 1)
        table = lax.dot_general(
            sums[...],
            (bucket_of(distance) == bucket).astype(WIDE),
            (((1,), (0,)), ((), ())),
            precision=lax.Precision.HIGHEST,
            preferred_element_type=WIDE,
        )
        for column in range(H // 4):
            lanes = slice(column * L, (column + 1) * L)
            small[S_TABLE : S_TABLE + 4, lanes] += table[4 * column : 4 * column + 4]
        send[ROWS + L :] = small[...].astype(LOW)

    return pl.pallas_call(
        kernel,
        out_shape=[
            shaped((2, ROWS + L, D), LOW),
            shaped((ROWS + L + SMALL, D), LOW),
            shaped((SMALL, D), WIDE),
        ],
        in_specs=[SMEM] + [VMEM] * 8 + [ANY] * len(after),
        out_specs=[VMEM] * 3,
        scratch_shapes=[pltpu.VMEM((ROWS, D), LOW), pltpu.VMEM((16, 2 * L), WIDE)],
        compiler_params=limit(12),
        cost_estimate=cost(4),
        name="attend_back",
    )(info, attended, small_in, spread, w_out, *(saved[n] for n in ATTEND_SAVED), *after)


def finish_rows(info, total, output, pieces, matrices, picks, after):
    def kernel(info, *refs):
        totals, outputs, pieces = refs[0:2], refs[2:4], refs[4:6]
        (query, key, value), refs = refs[6:9], refs[9 + len(after) :]
        content_ends, query_out, done, query_ends, sem = refs
        done[...] = jnp.zeros_like(done)
        first = info[2] == 1
        for seq in range(SEQS):
            lower = totals[seq][...] + nt(pieces[seq][0, :ROWS], query[...])
            upper = nt(pieces[seq][0, ROWS:], key[...]) + nt(pieces[seq][1, ROWS:], value[...])
            content_ends[seq * L : (seq + 1) * L] = jnp.where(
                first, lower[:L] + upper, outputs[seq][:L]
            )
            query_ends[seq * picks : (seq + 1) * picks] = jnp.where(
                first, lower[L : L + picks], outputs[seq][L : L + picks]
            )
        copy = pltpu.make_async_copy(query_ends, query_out, sem)
        copy.start()
        copy.wait()

    return pl.pallas_call(
        kernel,
        out_shape=[shaped((ALL_CONTENT, D), WIDE), shaped((SEQS * picks, D), WIDE), TOKEN],
        in_specs=[SMEM] + [VMEM] * 9 + [ANY] * len(after),
        out_specs=[VMEM, HBM, VMEM],
        scratch_shapes=[pltpu.VMEM((SEQS * picks, D), WIDE), DMA],
        compiler_params=limit(12),
        cost_estimate=cost(3),
        name="finish_rows",
    )(info, *total, *output, *pieces, *matrices[:3], *after)


def attend_grads(info, pair, early, mine, arrived, small, after=()):
    def kernel(info, small, *refs):
        pairs_in, earlies, mines, arriveds = (refs[2 * i : 2 * i + 2] for i in range(4))
        refs = refs[8 + len(after) :]
        outs, extra, rest = refs[:5], refs[5], refs[6:]
        a_rows, a_content, b_rows, b_content, stage, out_sems = rest
        core, place = info[0], info[1]
        for seq in range(SEQS):
            at = slice(seq * ROWS, (seq + 1) * ROWS)
            far = slice((2 + seq) * ROWS, (3 + seq) * ROWS)
            a_rows[at] = pairs_in[seq][core]
            a_rows[far] = columns(earlies[seq], core * D, D)[...]
            b_rows[at] = mines[seq][core, :ROWS]
            b_rows[far] = arriveds[seq][:ROWS]
            at = slice(seq * L, (seq + 1) * L)
            far = slice((2 + seq) * L, (3 + seq) * L)
            a_content[at] = pairs_in[seq][0, :L]
            a_content[far] = earlies[seq][:L, :D]
            b_content[at] = mines[seq][core, ROWS:]
            b_content[far] = arriveds[seq][ROWS : ROWS + L]
        far_small = arriveds[1][ROWS + L :]
        extra[...] = (small[...] + far_small.astype(WIDE)).astype(LOW)
        sent = start_all([(extra, outs[i].at[2 * QUARTER :]) for i in range(2)], out_sems, 8)
        for block, (former, latter) in enumerate(((a_rows, b_rows), (a_content, b_content))):
            for part in range(3):
                stage[block, part * 256 : (part + 1) * 256] = tn(
                    former[:, part * 256 : (part + 1) * 256], latter[...]
                ).astype(LOW)
            for k in range(4):
                quarter = lax.rem(place + k, 4)
                index, part = PLACES[k, block]
                start = part * QUARTER
                sent += start_all(
                    [
                        (
                            rows_at(stage.at[block], quarter * QUARTER, QUARTER),
                            outs[index].at[start : start + QUARTER],
                        )
                    ],
                    out_sems,
                    block * 4 + k,
                )
        wait_all(sent)

    return pl.pallas_call(
        kernel,
        out_shape=term_shapes(QUARTER, SMALL) + [shaped((SMALL, D), LOW)],
        in_specs=[SMEM] + [VMEM] * 9 + [ANY] * len(after),
        out_specs=[ANY] * 5 + [VMEM],
        scratch_shapes=[
            pltpu.VMEM((2 * ALL_ROWS, D), LOW),
            pltpu.VMEM((2 * ALL_CONTENT, D), LOW),
            pltpu.VMEM((2 * ALL_ROWS, D), LOW),
            pltpu.VMEM((2 * ALL_CONTENT, D), LOW),
            pltpu.VMEM((2, D, D), LOW),
            DMA((10,)),
        ],
        compiler_params=limit(12),
        cost_estimate=cost(5),
        name="attend_grads",
    )(info, small, *pair, *early, *mine, *arrived, *after)


def small_kernel(body, name, shapes, inputs, after=(), info=None, through=()):
    first = [] if info is None else [info]
    given = len(first) + len(inputs)

    def kernel(*refs):
        outs = refs[given + len(after) + len(through) :]
        body(*refs[:given], *outs[: len(shapes)])

    return pl.pallas_call(
        kernel,
        out_shape=[shaped(shape, LOW) for shape in shapes]
        + [shaped(array.shape, array.dtype) for array in through],
        in_specs=[SMEM] * len(first)
        + [VMEM] * len(inputs)
        + [ANY] * (len(after) + len(through)),
        out_specs=[VMEM] * len(shapes) + [ANY] * len(through),
        input_output_aliases={
            given + len(after) + i: len(shapes) + i for i in range(len(through))
        },
        compiler_params=limit(8),
        cost_estimate=cost(1),
        name=name,
    )(*first, *inputs, *after, *through)


def total_of(*terms):
    return sum(term.astype(WIDE) for term in terms).astype(LOW)


def ring_add(after0, before1, from_left, from_right, after=()):
    count = after0.shape[0]
    extra = from_left.shape[0] - 2 * count

    def body(after0, before1, from_left, from_right, right, left):
        right[:count] = total_of(after0[...], from_left[:count])
        left[:count] = total_of(before1[...], from_right[:count])
        if extra:
            right[count:] = from_left[2 * count :]
            left[count:] = from_right[2 * count :]

    return small_kernel(
        body,
        "ring_add",
        [(count + extra, D)] * 2,
        (after0, before1, from_left, from_right),
        after,
    )


def ring_sum(info, own, left, right, from_left, from_right, after=(), small=()):
    count = own.shape[0] // 2
    part = count // 4
    extra = sum(array.shape[0] for array in small)

    def body(info, own, left, right, from_left, from_right, *outs):
        if extra:
            small, outs = outs[0], outs[1:]
            total = total_of(
                small[...], from_left[2 * count :], from_right[2 * count :], left[count:]
            )
        for k, out in enumerate(outs):
            at = pl.multiple_of(lax.rem(info[3] + k, 4) * part, 16)
            low, high = pl.ds(at, part), pl.ds(at + count, part)
            out[:part] = total_of(own[low], left[low], from_right[high])
            out[part : 2 * part] = total_of(own[high], from_left[high], right[low])
            if extra:
                out[2 * part :] = total

    return small_kernel(
        body,
        "ring_sum",
        [(2 * part + extra, D)] * 4,
        (own, left, right, from_left, from_right, *small),
        after,
        info,
    )


def add_all(name, terms, after=()):
    def body(*refs):
        refs[-1][...] = total_of(*(ref[...] for ref in refs[:-1]))

    return small_kernel(body, name, [terms[0].shape], terms, after)[0]


def hand_on(arrays, after):
    return small_kernel(lambda *refs: None, "hand_on", [], (), after, None, arrays)


def split_sum(one, two, count, after=()):
    middle = count + S_TABLE

    def body(one, two, *outs):
        total = total_of(one[...], two[...])
        outs[0][...] = total[:count]
        outs[1][...] = total[count:middle]
        outs[2][...] = total[middle:]

    shapes = [(count, D), (S_TABLE, D), (SMALL - S_TABLE, D)]
    return small_kernel(body, "z_sum", shapes, (one, two), after)


def finish_small(small, table, far, after=()):
    places = [n for n in range(S_TABLE) if not S_EXPAND <= n < S_EXPAND + 4]

    def kernel(small, table, far, *refs):
        vectors, (b_expand, whole, done) = refs[len(after) : -3], refs[-3:]
        done[...] = jnp.zeros_like(done)
        values = small[...].astype(WIDE)
        for place, vector in zip(places, vectors):
            vector[...] = values[place : place + 1]
        for column in range(4):
            lanes = slice(column * D, (column + 1) * D)
            b_expand[:, lanes] = values[S_EXPAND + column : S_EXPAND + column + 1]
        total = table[...].astype(WIDE) + far[...].astype(WIDE)
        heads = [total[:, column * L : (column + 1) * L] for column in range(4)]
        whole[...] = jnp.concatenate(heads).T[:NB, :H]

    *vectors, b_expand, whole, done = pl.pallas_call(
        kernel,
        out_shape=[shaped((1, D), WIDE)] * len(places)
        + [shaped((1, FF), WIDE), shaped((NB, H), WIDE), TOKEN],
        in_specs=[VMEM] * 3 + [ANY] * len(after),
        out_specs=[VMEM] * (len(places) + 3),
        compiler_params=limit(4),
        cost_estimate=cost(1),
        name="finish_small",
    )(small, table, far, *after)
    return dict(zip(places, vectors)), b_expand, whole, done


def inner_join(info, parts, after=(), through=()):
    part = parts[0].shape[0] // 2

    def body(info, *refs):
        whole = refs[-1]
        for k, ref in enumerate(refs[:-1]):
            at = pl.multiple_of(lax.rem(info[3] + k, 4) * part, 16)
            whole[pl.ds(at, part)] = ref[:part]
            whole[pl.ds(at + 4 * part, part)] = ref[part:]

    return small_kernel(body, "inner_join", [(8 * part, D)], parts, after, info, through)


def cut(arrays, after=()):
    rows = arrays[0].shape[0]
    count = rows // 2

    def body(*refs):
        arrays, (right, left, whole) = refs[:-3], refs[-3:]
        right[...] = arrays[0][:count]
        left[...] = arrays[1][count:]
        for index, ref in enumerate(arrays):
            whole[index * rows : (index + 1) * rows] = ref[...]

    shapes = [(count, D), (count, D), (len(arrays) * rows, D)]
    return small_kernel(body, "cut", shapes, arrays, after)


def feed_targets(outs, source, half, core, quarter):
    pairs = []
    for block in range(2):
        part = source.at[block * QUARTER : (block + 1) * QUARTER]
        if half == 0:
            target = rows_at(outs[0], core * HALF + block * D + quarter * QUARTER, QUARTER)
        else:
            target = columns(
                rows_at(outs[1], quarter * QUARTER, QUARTER), (core * 2 + block) * D, D
            )
        pairs.append((None, part, target))
    return pairs


def attend_targets(outs, source, half, core, quarter):
    return [
        (
            core == number,
            source.at[:QUARTER],
            rows_at(outs[2 * number + half], quarter * QUARTER, QUARTER),
        )
        for number in range(2)
    ]


def settle(targets, shapes, count, info, pieces, outs, name, after=()):
    keys = tuple(pieces)
    arrays = [pieces[key] for key in keys]
    given = list(after) + list(outs or ())

    def kernel(info, *refs):
        parts, rest = refs[: len(keys)], refs[len(keys) + len(given) :]
        outs, rest = rest[: len(shapes)], rest[len(shapes) :]
        done, rest = rest[0], rest[1:]
        done[...] = jnp.zeros_like(done)
        wide_held, out_sems = rest[:-1], rest[-1]
        finish = []
        for index, (sibling, places) in enumerate(keys):
            core = 1 - info[0] if sibling else info[0]
            for number, (k, half) in enumerate(places):
                quarter = lax.rem((info[3] if sibling else info[1]) + k, 4)
                source = wide_held[index].at[number * count : (number + 1) * count]
                source[...] = parts[index][number * count : (number + 1) * count].astype(WIDE)
                for place, (condition, part, target) in enumerate(
                    targets(outs, source, half, core, quarter)
                ):
                    copy = pltpu.make_async_copy(
                        part, target, out_sems.at[12 * index + 2 * number + place]
                    )
                    if condition is None:
                        copy.start()
                        finish.append(copy.wait)
                    else:
                        pl.when(condition)(copy.start)
                        finish.append(lambda c=copy, when=condition: pl.when(when)(c.wait))
        for action in finish:
            action()

    result = pl.pallas_call(
        kernel,
        out_shape=[shaped(shape, WIDE) for shape in shapes]
        + [TOKEN],
        in_specs=[SMEM] + [VMEM] * len(keys) + [ANY] * len(given),
        out_specs=[ANY] * len(shapes) + [VMEM],
        scratch_shapes=[pltpu.VMEM(array.shape, WIDE) for array in arrays]
        + [DMA((12 * len(keys),))],
        input_output_aliases={
            1 + len(keys) + len(after) + i: i for i in range(len(outs or ()))
        },
        compiler_params=limit(20),
        cost_estimate=cost(sum(array.size for array in arrays) * 2e-6 + 1),
        name=name,
    )(info, *arrays, *given)
    return result[:-1], result[-1]


PLANE = ("x", "y", "c")


def shift(value, axis, by):
    size = lax.axis_size(axis)
    return lax.ppermute(value, axis, [(i, (i + by) % size) for i in range(size)])


def send(value, by):
    return lax.ppermute(value, "s", [(0, 1)] if by > 0 else [(1, 0)])


def turn(value, outer, by):
    pairs = []
    for i in range(4):
        for j in range(4):
            for c in range(2):
                if (c == 0) == outer:
                    target = ((i + by) % 4, j)
                else:
                    target = (i, (j + by) % 4)
                pairs.append(((i * 4 + j) * 2 + c, (target[0] * 4 + target[1]) * 2 + c))
    return lax.ppermute(value, PLANE, pairs)


def place(outer):
    return jnp.where(
        (lax.axis_index("c") == 0) == outer, lax.axis_index("x"), lax.axis_index("y")
    )


def wide(value):
    return value.astype(WIDE)


def total_wide(*terms):
    return sum(wide(term) for term in terms)


def inner_turns(parts, sign):
    return [turn(part, False, sign * by) for part, by in zip(parts, (1, 2, -1))]


OWN, ACROSS = ((0, 0), (0, 1)), (((2, 0),), ((2, 1),))
NEAR = ((3, 0), (3, 1), (1, 0), (1, 1))


def both_cores(places, piece):
    return {(0, places): piece, (1, places): shift(piece, "c", 1)}


def on_device(
    content_in,
    query_in,
    content_cot,
    query_cot,
    order_rank,
    query_pos,
    group_tag,
    *rest,
):
    (
        w_query,
        b_query,
        w_key,
        w_value,
        b_value,
        w_out,
        b_out,
        norm1_gain,
        norm1_bias,
        w_expand,
        b_expand,
        w_contract,
        b_contract,
        norm2_gain,
        norm2_bias,
    ) = (argument[0] for argument in rest[:-1])
    rel_table = rest[-1]
    core = lax.axis_index("c")
    first_section = (lax.axis_index("s") == 0).astype(jnp.int32)
    info = jnp.stack([core, place(True), first_section, place(False)])
    picks = query_pos.shape[1]

    matrices = (w_query, w_key, w_value, w_out, w_expand, w_contract)
    w_out_held = w_out
    vec = jnp.stack(
        [b_query, b_value, b_out, norm1_gain, norm1_bias, b_contract, norm2_gain, norm2_bias]
    )
    ranks = jnp.concatenate([order_rank, group_tag, query_pos], axis=1)
    masks, spread, query_in, query_cot = prepare(
        ranks, rel_table, jnp.concatenate([query_in, query_cot]), picks, (vec, info)
    )
    b_expand = b_expand[None]

    fronts, arrived = [], []
    for seq in range(SEQS):
        fronts.append(
            front(seq, info, content_in, query_in, matrices, masks, vec, b_expand, tuple(fronts))
        )
        arrived.append(send(fronts[seq], 1))
    output, early, pair, saved, grads = [], [], [], [], []
    for seq in range(SEQS):
        results = middle_forward(
            seq, info, content_in, query_in, arrived[seq], matrices, masks, vec, b_expand, tuple(grads)
        )
        for collected, result in zip((output, early, pair, saved), results):
            collected.append(result)
        grads.append(middle_back(seq, content_cot, query_cot, matrices, vec, saved[seq]))
    early = [shift(value, "c", 1) for value in early]
    grads = [send(value, -1) for value in grads]
    small = None
    total, branch, attended, own, late, pieces, pass_on = [], [], [], [], [], [], []
    for seq in range(SEQS):
        results = feed_back(
            seq,
            info,
            grads[seq],
            content_cot,
            query_cot,
            small,
            vec,
            matrices,
            saved[seq],
            tuple(pass_on),
        )
        small = results[3]
        for collected, result in zip(
            (total, branch, attended, own, late), results[:3] + results[4:]
        ):
            collected.append(result)
        late[seq] = shift(late[seq], "c", 1)
        results = attend_back(
            seq,
            info,
            attended[seq],
            small,
            spread,
            (),
            w_out_held,
            saved[seq],
        )
        small = results[2]
        pieces.append(results[0])
        pass_on.append(results[1])
    feed_terms = feed_grads(info, saved, branch, own, early, late, (small,))
    passed = [shift(value, "c", 1) for value in pass_on]

    def outer_step(terms):
        return (turn(terms[0], True, 1), turn(terms[1], True, -1))

    f_left, f_right = outer_step(feed_terms)
    *attend_terms, extra = attend_grads(info, pair, early, pieces, passed, small, (feed_terms[4],))
    a_left, a_right = outer_step(attend_terms)
    f_sent = ring_add(feed_terms[2], feed_terms[3], f_left, f_right, (extra,))
    f_parts = ring_sum(info, feed_terms[4], *outer_step(f_sent), f_left, f_right)
    f_others = inner_turns(f_parts[1:], 1)
    a_sent = ring_add(attend_terms[2], attend_terms[3], a_left, a_right, (f_parts[0],))
    f_part = add_all("inner_sum", [f_parts[0]] + f_others, (a_sent[0],))
    f_far = shift(f_part, "z", 1)
    a_parts = ring_sum(
        info, attend_terms[4], *outer_step(a_sent), a_left, a_right, (f_part,), (extra,)
    )
    f_part = add_all("z_sum", [f_part, f_far])
    f_others = inner_turns([f_part] * 3, -1)
    a_part = add_all("inner_sum", [a_parts[0]] + inner_turns(a_parts[1:], 1))
    (feed_own,) = inner_join(info, [f_part] + f_others, (a_part,))
    feed_outer = (turn(feed_own, True, 1), turn(feed_own, True, -1))
    content_ends, query_ends, token = finish_rows(
        info, total, output, pieces, matrices, picks, (feed_own,)
    )
    a_part, small, table = split_sum(
        a_part, shift(a_part, "z", 1), 2 * QUARTER // 4, (token,)
    )
    a_others = inner_turns([a_part] * 3, -1)

    def feed_settle(pieces, outs, name):
        return settle(
            feed_targets, ((FF, D), (D, FF)), 2 * QUARTER, info, pieces, outs, "feed_" + name
        )

    def attend_settle(pieces, outs, name, after=()):
        return settle(
            attend_targets,
            ((D, D),) * 4,
            QUARTER,
            info,
            pieces,
            outs,
            "attend_" + name,
            after,
        )

    feed_outs, token = feed_settle(both_cores(OWN, feed_own), None, "own")
    to_right, to_left, feed_near = cut(feed_outer, (token, *a_others))
    feed_across = (turn(to_right, True, 1), turn(to_left, True, -1))
    (attend_own,) = inner_join(info, [a_part] + a_others, (to_right,))
    attend_outer = (turn(attend_own, True, 1), turn(attend_own, True, -1))
    feed_outs, token = feed_settle(both_cores(NEAR, feed_near), feed_outs, "near")
    row, b_expand, table, small_token = finish_small(small, table, shift(table, "s", 1), (token,))
    to_right, to_left, attend_near = cut(
        (*attend_outer, attend_own), (token, small_token, *feed_across)
    )
    attend_across = (turn(to_right, True, 1), turn(to_left, True, -1))
    feed_outs, token = feed_settle(
        both_cores(ACROSS[0], feed_across[0]) | both_cores(ACROSS[1], feed_across[1]),
        feed_outs,
        "across",
    )
    attend_outs, near_token = attend_settle(both_cores(NEAR + OWN, attend_near), None, "near")
    attend_across = hand_on(attend_across, (token, near_token))
    attend_outs, _ = attend_settle(
        both_cores(ACROSS[0], attend_across[0]) | both_cores(ACROSS[1], attend_across[1]),
        attend_outs,
        "across",
    )
    contract, expand = feed_outs
    g_query, g_key, g_out, g_value = attend_outs
    return (
        content_ends[None],
        query_ends[None],
        g_query[None],
        row[S_QUERY],
        g_key[None],
        g_value[None],
        row[S_VALUE],
        g_out[None],
        row[S_OUT],
        row[S_GAIN1],
        row[S_SHIFT1],
        expand[None],
        b_expand,
        contract[None],
        row[S_CONTRACT],
        row[S_GAIN2],
        row[S_SHIFT2],
        table,
    )


DP = ("z", "x", "y", "c")


def solution(mesh):
    mesh = jax.sharding.Mesh(mesh.devices.reshape(2, 2, 4, 4, 2), ("s",) + DP)
    layer_specs = tuple(
        P("s", *([None] * (rank - 1))) for rank in (3, 2, 3, 3, 2, 3, 2, 2, 2, 3, 2, 3, 2, 2, 2)
    )
    in_specs = (P(DP, None),) * 7 + layer_specs + (P(),)
    out_specs = (P("s", DP, None),) * 2 + layer_specs + (P(),)
    return jax.shard_map(
        on_device, mesh=mesh, in_specs=in_specs, out_specs=out_specs, check_vma=False
    )
```

```python
import jax
import jax.numpy as jnp
from jax import lax
from jax.experimental import pallas as pl
from jax.experimental.pallas import tpu as pltpu
from jax.sharding import PartitionSpec as P

D = 768
H = 12
HD = 64
FF = 3072
NB = 32
L = 128
PAIRS = H // 2
SEQS = 2
PICKS = 32
ROWS = L + PICKS
EPSILON = 1e-05
SCALE = HD ** (-0.5)
TILE = 1536
LOW = jnp.bfloat16
WIDE = jnp.float32
HALF = FF // 2
QUARTER = D // 4
EARLY = 3 * D + HALF
LATE = D + HALF
SMALL = 16
ALL_ROWS = SEQS * ROWS
ALL_CONTENT = SEQS * L
PIECE = ALL_ROWS + ALL_CONTENT


def nn(former, latter):
    return lax.dot_general(
        former, latter, (((1,), (0,)), ((), ())), preferred_element_type=WIDE
    )


def nt(former, latter):
    return lax.dot_general(
        former, latter, (((1,), (1,)), ((), ())), preferred_element_type=WIDE
    )


def tn(former, latter):
    return lax.dot_general(
        former, latter, (((0,), (0,)), ((), ())), preferred_element_type=WIDE
    )


def halves(value):
    even = lax.broadcasted_iota(jnp.int32, value.shape, 1) < HD
    zero = jnp.zeros_like(value)
    return jnp.concatenate([jnp.where(even, value, zero), jnp.where(even, zero, value)])


def side(value):
    count = value.shape[0] // 2
    return jnp.concatenate([value[:count], value[count:]], axis=1)


def norm_rows(values):
    centered = values - jnp.mean(values, axis=-1, keepdims=True)
    variance = jnp.mean(centered * centered, axis=-1, keepdims=True)
    root = lax.rsqrt(variance + EPSILON)
    return (centered * root, root)


def norm_rows_back(scaled, normed, root):
    return root * (
        scaled
        - jnp.mean(scaled, axis=-1, keepdims=True)
        - normed * jnp.mean(scaled * normed, axis=-1, keepdims=True)
    )


B_QUERY, B_VALUE, B_OUT, GAIN1, SHIFT1, B_CONTRACT, GAIN2, SHIFT2 = range(8)
S_QUERY, S_VALUE, S_OUT, S_GAIN1, S_SHIFT1, S_EXPAND = range(6)
S_CONTRACT, S_GAIN2, S_SHIFT2, S_TABLE = 9, 10, 11, 12
LIMITS = (12, 16, 23, 32, 46, 64, 91)


def bucket_of(relative):
    distance = jnp.abs(relative)
    beyond = 8 + sum((distance >= limit).astype(jnp.int32) for limit in LIMITS)
    within = jnp.where(distance < 8, distance, beyond)
    return within + 16 * (relative > 0).astype(jnp.int32)


def forward(x, w, vec, b_expand, masks, s, keep):
    row = lambda k: vec[k : k + 1, :]
    s.query[...] = (nn(x[...], w.query[...]) + row(B_QUERY)).astype(LOW)
    s.key[...] = nn(x[:L], w.key[...]).astype(LOW)
    s.value[...] = (nn(x[:L], w.value[...]) + row(B_VALUE)).astype(LOW)
    for pair in range(PAIRS):
        lanes = slice(pair * 128, (pair + 1) * 128)
        scores = nt(halves(s.query[:, lanes]), s.key[:, lanes]) * SCALE + masks[pair]
        shifted = jnp.exp(scores - jnp.max(scores, axis=-1, keepdims=True))
        probs = (shifted / jnp.sum(shifted, axis=-1, keepdims=True)).astype(LOW)
        if keep:
            s.probs[pair] = probs
        s.mixed[:, lanes] = nn(side(probs), halves(s.value[:, lanes])).astype(LOW)
    total = x[...].astype(WIDE) + nn(s.mixed[...], w.out[...]) + row(B_OUT)
    normed, root = norm_rows(total)
    first = normed * row(GAIN1) + row(SHIFT1)
    s.first_low[...] = first.astype(LOW)
    s.total[...] = first + row(B_CONTRACT)
    if keep:
        s.normed1[...] = normed
        s.root1[...] = jnp.broadcast_to(root, (ROWS, 128))
    for tile in range(FF // TILE):
        tile = slice(tile * TILE, (tile + 1) * TILE)
        expanded = nn(s.first_low[...], w.expand[:, tile]) + b_expand[:, tile]
        cumulative = 0.5 * (1.0 + lax.erf(expanded * 0.7071067811865476))
        activated = (expanded * cumulative).astype(LOW)
        if keep:
            s.slope[:, tile] = (
                cumulative + expanded * jnp.exp(-0.5 * expanded * expanded) * 0.3989422804014327
            ).astype(LOW)
            s.activated[:, tile] = activated
        s.total[...] += nn(activated, w.contract[tile, :])
    normed, root = norm_rows(s.total[...])
    if keep:
        s.normed2[...] = normed
        s.root2[...] = jnp.broadcast_to(root, (ROWS, 128))
    s.out[...] = (normed * row(GAIN2) + row(SHIFT2)).astype(s.out.dtype)


def column_sum(value):
    return jnp.sum(value.astype(WIDE), axis=0, keepdims=True)


def back_second_norm(grad, vec, s, add=None):
    upper = grad.astype(WIDE)
    normed = s.normed2[...]
    lower = norm_rows_back(upper * vec[GAIN2 : GAIN2 + 1, :], normed, s.root2[:, :1])
    s.total[...] = lower
    s.branch[...] = lower.astype(LOW)
    if add is not None:
        add(S_GAIN2, column_sum(upper * normed))
        add(S_SHIFT2, column_sum(upper))
        add(S_CONTRACT, column_sum(lower.astype(LOW)))


def back_feed(w, vec, s, add=None):
    for tile in range(FF // TILE):
        tile = slice(tile * TILE, (tile + 1) * TILE)
        lower = (nt(s.branch[...], w.contract[tile, :]) * s.slope[:, tile].astype(WIDE)).astype(LOW)
        s.expanded[:, tile] = lower
        if add is not None:
            part = column_sum(lower)
            for column in range(TILE // D):
                add(
                    S_EXPAND + tile.start // D + column,
                    part[:, column * D : (column + 1) * D],
                )
        s.total[...] += nt(lower, w.expand[:, tile])
    upper = s.total[...]
    normed = s.normed1[...]
    lower = norm_rows_back(upper * vec[GAIN1 : GAIN1 + 1, :], normed, s.root1[:, :1])
    s.total[...] = lower
    s.attended[...] = lower.astype(LOW)
    if add is not None:
        add(S_GAIN1, column_sum(upper * normed))
        add(S_SHIFT1, column_sum(upper))
        add(S_OUT, column_sum(lower.astype(LOW)))


def back_attend(s, table=None):
    for pair in range(PAIRS):
        lanes = slice(pair * 128, (pair + 1) * 128)
        probs = s.probs[pair]
        below = halves(s.dmixed[:, lanes])
        dprobs = nt(below, s.value[:, lanes])
        s.dvalue[:, lanes] = tn(probs, below).astype(LOW)
        weight = probs.astype(WIDE)
        dscores = (
            weight * (dprobs - jnp.sum(weight * dprobs, axis=-1, keepdims=True))
        ).astype(LOW)
        s.dquery[:, lanes] = (nn(side(dscores), halves(s.key[:, lanes])) * SCALE).astype(LOW)
        s.dkey[:, lanes] = (tn(dscores, halves(s.query[:, lanes])) * SCALE).astype(LOW)
        if table is not None:
            table(pair, dscores)


class Names:
    def __init__(self, **named):
        self.__dict__.update(named)


MATRICES = ("query", "key", "value", "out", "expand", "contract")
MATRIX_SHAPES = {
    "query": (D, D),
    "key": (D, D),
    "value": (D, D),
    "out": (D, D),
    "expand": (D, FF),
    "contract": (FF, D),
}
MASK_SHAPE = (PAIRS, 2 * ROWS, L)
KEPT = {
    "query": ((ROWS, D), LOW),
    "key": ((L, D), LOW),
    "value": ((L, D), LOW),
    "probs": (MASK_SHAPE, LOW),
    "mixed": ((ROWS, D), LOW),
    "normed1": ((ROWS, D), WIDE),
    "root1": ((ROWS, 128), WIDE),
    "first_low": ((ROWS, D), LOW),
    "slope": ((ROWS, FF), LOW),
    "activated": ((ROWS, FF), LOW),
    "normed2": ((ROWS, D), WIDE),
    "root2": ((ROWS, 128), WIDE),
}
SAVED = tuple(name for name in KEPT if name != "mixed")
ANY = pl.BlockSpec(memory_space=pl.ANY)
HBM = pl.BlockSpec(memory_space=pltpu.HBM)
VMEM = pl.BlockSpec(memory_space=pltpu.VMEM)
SMEM = pl.BlockSpec(memory_space=pltpu.SMEM)


def limit(megabytes):
    return pltpu.CompilerParams(vmem_limit_bytes=megabytes * 1024 * 1024)


DMA = pltpu.SemaphoreType.DMA


def cost(microseconds):
    return pl.CostEstimate(flops=0, bytes_accessed=int(microseconds * 3.2e6), transcendentals=0)


def shaped(shape, kind):
    return jax.ShapeDtypeStruct(shape, kind)


TOKEN = shaped((8, 128), WIDE)


def columns(ref, start, size):
    return ref.at[:, pl.ds(pl.multiple_of(start, 128), size)]


def rows_at(ref, start, size):
    return ref.at[pl.ds(pl.multiple_of(start, 64), size)]


def start_all(pairs, sems, base=0):
    copies = [
        pltpu.make_async_copy(source, target, sems.at[base + index])
        for index, (source, target) in enumerate(pairs)
    ]
    for copy in copies:
        copy.start()
    return copies


def wait_all(copies):
    for copy in copies:
        copy.wait()


def fetcher(names, sources, targets, sems, base=0):
    copies = dict(zip(names, start_all(list(zip(sources, targets)), sems, base)))
    return lambda name: copies[name].wait()


def prepare(ranks, table, queries, picks, after):
    def kernel(ranks, table, queries, *refs):
        masks, spread, rows_in, rows_cot = refs[len(after) :]
        order, tag, pos = ranks[:, :L], ranks[:, L : 2 * L], ranks[:, 2 * L : 2 * L + picks]
        values = queries[...].astype(WIDE)
        blank = jnp.zeros((PICKS - picks, D), WIDE)
        for index, target in enumerate((rows_in, rows_cot)):
            own = values[2 * index * picks : 2 * (index + 1) * picks]
            target[...] = jnp.concatenate([own[:picks], blank, own[picks:], blank]).astype(LOW)
        lane = lax.broadcasted_iota(jnp.int32, (L, L), 1)
        level = lax.broadcasted_iota(jnp.int32, (L, L), 0)
        lane_q = lax.broadcasted_iota(jnp.int32, (PICKS, L), 1)
        upright = lambda row: jnp.sum(jnp.where(lane == level, row, 0.0), axis=1, keepdims=True)
        distance = lax.broadcasted_iota(jnp.int32, (2 * L, NB), 0) - (L - 1)
        bucket = lax.broadcasted_iota(jnp.int32, (2 * L, NB), 1)
        by_distance = lax.dot_general(
            table[...],
            (bucket_of(distance) == bucket).astype(WIDE),
            (((0,), (1,)), ((), ())),
            precision=lax.Precision.HIGHEST,
            preferred_element_type=WIDE,
        )
        allowed, hot = [], []
        for seq in range(SEQS):
            own_rank = order[seq : seq + 1, :].astype(WIDE)
            own_tag = tag[seq : seq + 1, :].astype(WIDE)
            own_pos = pos[seq : seq + 1, :].astype(WIDE)
            number = lax.broadcasted_iota(jnp.int32, (PICKS, picks), 0)
            same = number == lax.broadcasted_iota(jnp.int32, (PICKS, picks), 1)
            place = jnp.sum(jnp.where(same, own_pos, 0.0), axis=1, keepdims=True)
            filled = lax.broadcasted_iota(jnp.int32, (PICKS, 1), 0) < picks
            place = jnp.where(filled, place, -1.0).astype(jnp.int32)
            matches = place == lane_q
            marks = jnp.where(matches, 1.0, 0.0)
            predicted = jnp.max(marks, axis=0, keepdims=True)
            rank = jnp.sum(jnp.where(matches, own_rank, 0.0), axis=1, keepdims=True)
            group = jnp.sum(jnp.where(matches, own_tag, 0.0), axis=1, keepdims=True)
            earlier = (upright(predicted) > 0) & (own_rank <= upright(own_rank))
            content = (upright(own_tag) == own_tag) & ((predicted == 0) | earlier)
            query = (group == own_tag) & ((predicted == 0) | (own_rank + 1 <= rank))
            allowed.append((content, query))
            hot.append(marks)
            spread[seq, :L] = jnp.where(lane == L - 1 - level, 1.0, 0.0).astype(LOW)
            spread[seq, L:] = jnp.where(lane_q == L - 1 - place, 1.0, 0.0).astype(LOW)
        hot = jnp.concatenate(hot)
        for head in range(H):
            row = jnp.broadcast_to(by_distance[head : head + 1], (L, 2 * L))
            bias = pltpu.roll(row, L + 1, 1, stride=1, stride_axis=0)[:, :L]
            bias_q = lax.dot_general(
                hot,
                bias,
                (((1,), (0,)), ((), ())),
                precision=lax.Precision.HIGHEST,
                preferred_element_type=WIDE,
            )
            base = head % 2 * ROWS
            for seq in range(SEQS):
                content, query = allowed[seq]
                masks[seq, head // 2, base : base + L] = jnp.where(content, bias, -1e30)
                masks[seq, head // 2, base + L : base + ROWS] = jnp.where(
                    query, bias_q[seq * PICKS : (seq + 1) * PICKS], -1e30
                )

    return pl.pallas_call(
        kernel,
        out_shape=[
            shaped((SEQS,) + MASK_SHAPE, WIDE),
            shaped((SEQS, ROWS, L), LOW),
            shaped((SEQS * PICKS, D), LOW),
            shaped((SEQS * PICKS, D), LOW),
        ],
        in_specs=[VMEM] * 3 + [ANY] * len(after),
        out_specs=[VMEM] * 4,
        compiler_params=limit(8),
        cost_estimate=pl.CostEstimate(flops=int(3e10), bytes_accessed=0, transcendentals=0),
        name="prepare",
    )(ranks, table, queries, *after)


def take_rows(content, picks, seq, target):
    target[:L] = content[seq * L : (seq + 1) * L]
    target[L:] = picks[seq * PICKS : (seq + 1) * PICKS]


def front(seq, info, content, picks, matrices, masks, vec, b_expand, after=()):
    def kernel(info, content, picks, masks, vec, b_expand, *refs):
        w = Names(**dict(zip(MATRICES, refs[:6])))
        out, x, query, key, value, mixed, first_low, total = refs[6 + len(after) :]
        s = Names(
            query=query,
            key=key,
            value=value,
            mixed=mixed,
            first_low=first_low,
            total=total,
            out=out,
        )
        take_rows(content, picks, seq, x)
        forward(x, w, vec, b_expand, masks.at[seq], s, False)

    return pl.pallas_call(
        kernel,
        out_shape=shaped((ROWS, D), LOW),
        in_specs=[SMEM] + [VMEM] * 11 + [ANY] * len(after),
        out_specs=VMEM,
        scratch_shapes=[pltpu.VMEM((ROWS, D), LOW)]
        + [pltpu.VMEM(*KEPT[n]) for n in ("query", "key", "value", "mixed", "first_low")]
        + [pltpu.VMEM((ROWS, D), WIDE)],
        compiler_params=limit(12),
        cost_estimate=cost(5),
        name="front",
    )(info, content, picks, masks, vec, b_expand, *matrices, *after)


def middle_forward(seq, info, content, picks, arrived, matrices, masks, vec, b_expand, after=()):
    def kernel(info, arrived, content, picks, masks, vec, b_expand, *refs):
        w, rest = Names(**dict(zip(MATRICES, refs[:6]))), refs[6 + len(after) :]
        (out, early, pair), kept = rest[:3], rest[3 : 3 + len(SAVED)]
        mixed, total = rest[3 + len(SAVED) :]
        x = pair.at[0]
        s = Names(total=total, out=out, mixed=mixed, **dict(zip(SAVED, kept)))
        take_rows(content, picks, seq, x)
        x[...] = jnp.where(info[2] == 1, x[...], arrived[...])
        early[:, :D] = x[...]
        forward(x, w, vec, b_expand, masks.at[seq], s, True)
        pair[1] = mixed[...]
        early[:, D : 2 * D] = mixed[...]
        early[:, 2 * D : 3 * D] = s.first_low[...]
        early[:, 3 * D :] = columns(s.activated, (1 - info[0]) * HALF, HALF)[...]

    out, early, pair, *saved = pl.pallas_call(
        kernel,
        out_shape=[
            shaped((ROWS, D), WIDE),
            shaped((ROWS, EARLY), LOW),
            shaped((2, ROWS, D), LOW),
        ]
        + [shaped(*KEPT[n]) for n in SAVED],
        in_specs=[SMEM] + [VMEM] * 12 + [ANY] * len(after),
        out_specs=[VMEM] * (3 + len(SAVED)),
        scratch_shapes=[pltpu.VMEM(*KEPT["mixed"]), pltpu.VMEM((ROWS, D), WIDE)],
        compiler_params=limit(16),
        cost_estimate=cost(6),
        name="middle_forward",
    )(info, arrived, content, picks, masks, vec, b_expand, *matrices, *after)
    return (out, early, pair, dict(zip(SAVED, saved)))


FEED_SAVED = ("normed2", "root2", "slope", "normed1", "root1")
ATTEND_SAVED = ("value", "probs", "key", "query")


def middle_back(seq, content, picks, matrices, vec, saved):
    names = FEED_SAVED + ATTEND_SAVED

    def kernel(content, picks, vec, *refs):
        w, rest = Names(**dict(zip(MATRICES, refs[:6]))), refs[6:]
        kept, grad, rest = rest[: len(names)], rest[len(names)], rest[len(names) + 1 :]
        cot, total, branch, expanded, attended, dmixed, dvalue, dquery, dkey = rest
        s = Names(
            total=total,
            branch=branch,
            expanded=expanded,
            attended=attended,
            dmixed=dmixed,
            dvalue=dvalue,
            dquery=dquery,
            dkey=dkey,
            **dict(zip(names, kept)),
        )
        take_rows(content, picks, seq, cot)
        back_second_norm(cot[...], vec, s)
        back_feed(w, vec, s)
        dmixed[...] = nt(attended[...], w.out[...]).astype(LOW)
        back_attend(s)
        lower = total[...] + nt(dquery[...], w.query[...])
        upper = nt(dkey[...], w.key[...]) + nt(dvalue[...], w.value[...])
        grad[:L] = (lower[:L] + upper).astype(LOW)
        grad[L:] = lower[L:].astype(LOW)

    return pl.pallas_call(
        kernel,
        out_shape=shaped((ROWS, D), LOW),
        in_specs=[VMEM] * (9 + len(names)),
        out_specs=VMEM,
        scratch_shapes=[
            pltpu.VMEM((ROWS, D), LOW),
            pltpu.VMEM((ROWS, D), WIDE),
            pltpu.VMEM((ROWS, D), LOW),
            pltpu.VMEM((ROWS, FF), LOW),
            pltpu.VMEM((ROWS, D), LOW),
            pltpu.VMEM((ROWS, D), LOW),
            pltpu.VMEM((L, D), LOW),
            pltpu.VMEM((ROWS, D), LOW),
            pltpu.VMEM((L, D), LOW),
        ],
        compiler_params=limit(12),
        cost_estimate=cost(7),
        name="middle_back",
    )(content, picks, vec, *matrices, *(saved[n] for n in names))


def feed_back(seq, info, arrived, content, picks, small_in, vec, matrices, saved, after=()):
    given = [] if small_in is None else [small_in]

    def kernel(info, arrived, content, picks, vec, expand, contract, *refs):
        kept, rest = refs[:5], refs[5 + len(given) + len(after) :]
        total, branch, attended, small, own, late, upper, expanded = rest
        w = Names(expand=expand, contract=contract)
        s = Names(
            total=total,
            branch=branch,
            attended=attended,
            expanded=expanded,
            **dict(zip(FEED_SAVED, kept)),
        )
        small[...] = refs[5][...] if given else jnp.zeros_like(small)

        def add(place, value):
            small[place : place + 1, :] += value

        take_rows(content, picks, seq, upper)
        back_second_norm(jnp.where(info[2] == 1, arrived[...], upper[...]), vec, s, add)
        late[:, :D] = branch[...]
        back_feed(w, vec, s, add)
        own[...] = columns(expanded, info[0] * HALF, HALF)[...]
        late[:, D:] = columns(expanded, (1 - info[0]) * HALF, HALF)[...]

    return pl.pallas_call(
        kernel,
        out_shape=[
            shaped((ROWS, D), WIDE),
            shaped((ROWS, D), LOW),
            shaped((ROWS, D), LOW),
            shaped((SMALL, D), WIDE),
            shaped((ROWS, HALF), LOW),
            shaped((ROWS, LATE), LOW),
        ],
        in_specs=[SMEM] + [VMEM] * (11 + len(given)) + [ANY] * len(after),
        out_specs=[VMEM] * 6,
        scratch_shapes=[pltpu.VMEM((ROWS, D), LOW), pltpu.VMEM((ROWS, FF), LOW)],
        compiler_params=limit(12),
        cost_estimate=cost(4),
        name="feed_back",
    )(
        info,
        arrived,
        content,
        picks,
        vec,
        matrices[4],
        matrices[5],
        *(saved[n] for n in FEED_SAVED),
        *given,
        *after,
    )


PLACES = {
    (2, 0): (0, 0),
    (1, 1): (0, 1),
    (2, 1): (1, 0),
    (3, 0): (1, 1),
    (1, 0): (2, 0),
    (3, 1): (3, 0),
    (0, 0): (4, 0),
    (0, 1): (4, 1),
}


def term_shapes(count, extra=0):
    rows = (2 * count + extra, 2 * count + extra, count, count, 2 * count)
    return [shaped((n, D), LOW) for n in rows]


def feed_grads(info, mine, branch, own, early, late, after=()):
    def kernel(info, *refs):
        acts, lows, branches, owns, earlies, lates = (refs[2 * i : 2 * i + 2] for i in range(6))
        refs = refs[:12] + refs[12 + len(after) :]
        outs, (a_act, a_first, b_branch, b_own, stage, out_sems) = refs[12:17], refs[17:]
        core, place = info[0], info[1]
        own_at = [slice(seq * ROWS, (seq + 1) * ROWS) for seq in range(SEQS)]
        far_at = [slice((2 + seq) * ROWS, (3 + seq) * ROWS) for seq in range(SEQS)]
        for seq in range(SEQS):
            at, far = own_at[seq], far_at[seq]
            a_act[at] = columns(acts[seq], core * HALF, HALF)[...]
            a_act[far] = earlies[seq][:, 3 * D :]
            b_branch[at] = branches[seq][...]
            b_branch[far] = lates[seq][:, :D]
        sent = []

        def send(block):
            for k in range(4):
                quarter = lax.rem(place + k, 4)
                index, part = PLACES[k, block // 2]
                start = (2 * part + block % 2) * QUARTER
                sent.extend(
                    start_all(
                        [
                            (
                                rows_at(stage.at[block], quarter * QUARTER, QUARTER),
                                outs[index].at[start : start + QUARTER],
                            )
                        ],
                        out_sems,
                        block * 4 + k,
                    )
                )

        for block in range(2):
            for part in range(3):
                start = block * D + part * 256
                stage[block, part * 256 : (part + 1) * 256] = tn(
                    a_act[:, start : start + 256], b_branch[...]
                ).astype(LOW)
            send(block)
        for seq in range(SEQS):
            at, far = own_at[seq], far_at[seq]
            a_first[at] = lows[seq][...]
            a_first[far] = earlies[seq][:, 2 * D : 3 * D]
            b_own[at] = owns[seq][...]
            b_own[far] = lates[seq][:, D:]
        for block in range(2):
            for part in range(3):
                stage[2 + block, part * 256 : (part + 1) * 256] = tn(
                    a_first[:, part * 256 : (part + 1) * 256], b_own[:, block * D : (block + 1) * D]
                ).astype(LOW)
            send(2 + block)
        wait_all(sent)

    acts = [saved["activated"] for saved in mine]
    lows = [saved["first_low"] for saved in mine]
    return pl.pallas_call(
        kernel,
        out_shape=term_shapes(2 * QUARTER),
        in_specs=[SMEM] + [VMEM] * 12 + [ANY] * len(after),
        out_specs=[ANY] * 5,
        scratch_shapes=[
            pltpu.VMEM((2 * ALL_ROWS, HALF), LOW),
            pltpu.VMEM((2 * ALL_ROWS, D), LOW),
            pltpu.VMEM((2 * ALL_ROWS, D), LOW),
            pltpu.VMEM((2 * ALL_ROWS, HALF), LOW),
            pltpu.VMEM((4, D, D), LOW),
            DMA((16,)),
        ],
        compiler_params=limit(16),
        cost_estimate=cost(8),
        name="feed_grads",
    )(info, *acts, *lows, *branch, *own, *early, *late, *after)


def attend_back(seq, info, attended, small_in, spread, after, w_out, saved):
    def kernel(info, attended, small_in, spread, w_out, *refs):
        kept, (pieces, send, small, dmixed, sums) = refs[:4], refs[4 + len(after) :]
        small[...] = small_in[...]
        pieces[1, :ROWS] = attended[...]
        dmixed[...] = nt(attended[...], w_out[...]).astype(LOW)
        s = Names(
            dmixed=dmixed,
            dquery=pieces.at[0, :ROWS],
            dkey=pieces.at[0, ROWS:],
            dvalue=pieces.at[1, ROWS:],
            **dict(zip(ATTEND_SAVED, kept)),
        )
        sums[...] = jnp.zeros_like(sums)

        def table_sum(pair, dscores):
            for odd in range(2):
                part = tn(spread[seq], dscores[odd * ROWS : (odd + 1) * ROWS])
                both = jnp.concatenate([part, jnp.zeros((L, L), WIDE)], axis=1)
                turned = pltpu.roll(both, 0, 1, stride=1, stride_axis=0)
                head = 2 * pair + odd
                sums[head : head + 1, :] = jnp.sum(turned, axis=0, keepdims=True)

        back_attend(s, table_sum)
        send[: ROWS + L] = pieces[1 - info[0]]
        small[S_QUERY : S_QUERY + 1, :] += column_sum(pieces[0, :ROWS])
        small[S_VALUE : S_VALUE + 1, :] += column_sum(pieces[1, ROWS:])
        distance = lax.broadcasted_iota(jnp.int32, (2 * L, L), 0) - (L - 1)
        bucket = lax.broadcasted_iota(jnp.int32, (2 * L, L), 1)
        table = lax.dot_general(
            sums[...],
            (bucket_of(distance) == bucket).astype(WIDE),
            (((1,), (0,)), ((), ())),
            precision=lax.Precision.HIGHEST,
            preferred_element_type=WIDE,
        )
        for column in range(H // 4):
            lanes = slice(column * L, (column + 1) * L)
            small[S_TABLE : S_TABLE + 4, lanes] += table[4 * column : 4 * column + 4]
        send[ROWS + L :] = small[...].astype(LOW)

    return pl.pallas_call(
        kernel,
        out_shape=[
            shaped((2, ROWS + L, D), LOW),
            shaped((ROWS + L + SMALL, D), LOW),
            shaped((SMALL, D), WIDE),
        ],
        in_specs=[SMEM] + [VMEM] * 8 + [ANY] * len(after),
        out_specs=[VMEM] * 3,
        scratch_shapes=[pltpu.VMEM((ROWS, D), LOW), pltpu.VMEM((16, 2 * L), WIDE)],
        compiler_params=limit(12),
        cost_estimate=cost(4),
        name="attend_back",
    )(info, attended, small_in, spread, w_out, *(saved[n] for n in ATTEND_SAVED), *after)


def finish_rows(info, total, output, pieces, matrices, picks, after):
    def kernel(info, *refs):
        totals, outputs, pieces = refs[0:2], refs[2:4], refs[4:6]
        (query, key, value), refs = refs[6:9], refs[9 + len(after) :]
        content_ends, query_out, done, query_ends, sem = refs
        done[...] = jnp.zeros_like(done)
        first = info[2] == 1
        for seq in range(SEQS):
            lower = totals[seq][...] + nt(pieces[seq][0, :ROWS], query[...])
            upper = nt(pieces[seq][0, ROWS:], key[...]) + nt(pieces[seq][1, ROWS:], value[...])
            content_ends[seq * L : (seq + 1) * L] = jnp.where(
                first, lower[:L] + upper, outputs[seq][:L]
            )
            query_ends[seq * picks : (seq + 1) * picks] = jnp.where(
                first, lower[L : L + picks], outputs[seq][L : L + picks]
            )
        copy = pltpu.make_async_copy(query_ends, query_out, sem)
        copy.start()
        copy.wait()

    return pl.pallas_call(
        kernel,
        out_shape=[shaped((ALL_CONTENT, D), WIDE), shaped((SEQS * picks, D), WIDE), TOKEN],
        in_specs=[SMEM] + [VMEM] * 9 + [ANY] * len(after),
        out_specs=[VMEM, HBM, VMEM],
        scratch_shapes=[pltpu.VMEM((SEQS * picks, D), WIDE), DMA],
        compiler_params=limit(12),
        cost_estimate=cost(3),
        name="finish_rows",
    )(info, *total, *output, *pieces, *matrices[:3], *after)


def attend_grads(info, pair, early, mine, arrived, small, after=()):
    def kernel(info, small, *refs):
        pairs_in, earlies, mines, arriveds = (refs[2 * i : 2 * i + 2] for i in range(4))
        refs = refs[8 + len(after) :]
        outs, extra, rest = refs[:5], refs[5], refs[6:]
        a_rows, a_content, b_rows, b_content, stage, out_sems = rest
        core, place = info[0], info[1]
        for seq in range(SEQS):
            at = slice(seq * ROWS, (seq + 1) * ROWS)
            far = slice((2 + seq) * ROWS, (3 + seq) * ROWS)
            a_rows[at] = pairs_in[seq][core]
            a_rows[far] = columns(earlies[seq], core * D, D)[...]
            b_rows[at] = mines[seq][core, :ROWS]
            b_rows[far] = arriveds[seq][:ROWS]
            at = slice(seq * L, (seq + 1) * L)
            far = slice((2 + seq) * L, (3 + seq) * L)
            a_content[at] = pairs_in[seq][0, :L]
            a_content[far] = earlies[seq][:L, :D]
            b_content[at] = mines[seq][core, ROWS:]
            b_content[far] = arriveds[seq][ROWS : ROWS + L]
        far_small = arriveds[1][ROWS + L :]
        extra[...] = (small[...] + far_small.astype(WIDE)).astype(LOW)
        sent = start_all([(extra, outs[i].at[2 * QUARTER :]) for i in range(2)], out_sems, 8)
        for block, (former, latter) in enumerate(((a_rows, b_rows), (a_content, b_content))):
            for part in range(3):
                stage[block, part * 256 : (part + 1) * 256] = tn(
                    former[:, part * 256 : (part + 1) * 256], latter[...]
                ).astype(LOW)
            for k in range(4):
                quarter = lax.rem(place + k, 4)
                index, part = PLACES[k, block]
                start = part * QUARTER
                sent += start_all(
                    [
                        (
                            rows_at(stage.at[block], quarter * QUARTER, QUARTER),
                            outs[index].at[start : start + QUARTER],
                        )
                    ],
                    out_sems,
                    block * 4 + k,
                )
        wait_all(sent)

    return pl.pallas_call(
        kernel,
        out_shape=term_shapes(QUARTER, SMALL) + [shaped((SMALL, D), LOW)],
        in_specs=[SMEM] + [VMEM] * 9 + [ANY] * len(after),
        out_specs=[ANY] * 5 + [VMEM],
        scratch_shapes=[
            pltpu.VMEM((2 * ALL_ROWS, D), LOW),
            pltpu.VMEM((2 * ALL_CONTENT, D), LOW),
            pltpu.VMEM((2 * ALL_ROWS, D), LOW),
            pltpu.VMEM((2 * ALL_CONTENT, D), LOW),
            pltpu.VMEM((2, D, D), LOW),
            DMA((10,)),
        ],
        compiler_params=limit(12),
        cost_estimate=cost(5),
        name="attend_grads",
    )(info, small, *pair, *early, *mine, *arrived, *after)


def small_kernel(body, name, shapes, inputs, after=(), info=None, through=()):
    first = [] if info is None else [info]
    given = len(first) + len(inputs)

    def kernel(*refs):
        outs = refs[given + len(after) + len(through) :]
        body(*refs[:given], *outs[: len(shapes)])

    return pl.pallas_call(
        kernel,
        out_shape=[shaped(shape, LOW) for shape in shapes]
        + [shaped(array.shape, array.dtype) for array in through],
        in_specs=[SMEM] * len(first)
        + [VMEM] * len(inputs)
        + [ANY] * (len(after) + len(through)),
        out_specs=[VMEM] * len(shapes) + [ANY] * len(through),
        input_output_aliases={
            given + len(after) + i: len(shapes) + i for i in range(len(through))
        },
        compiler_params=limit(8),
        cost_estimate=cost(1),
        name=name,
    )(*first, *inputs, *after, *through)


def total_of(*terms):
    return sum(term.astype(WIDE) for term in terms).astype(LOW)


def ring_add(after0, before1, from_left, from_right, after=()):
    count = after0.shape[0]
    extra = from_left.shape[0] - 2 * count

    def body(after0, before1, from_left, from_right, right, left):
        right[:count] = total_of(after0[...], from_left[:count])
        left[:count] = total_of(before1[...], from_right[:count])
        if extra:
            right[count:] = from_left[2 * count :]
            left[count:] = from_right[2 * count :]

    return small_kernel(
        body,
        "ring_add",
        [(count + extra, D)] * 2,
        (after0, before1, from_left, from_right),
        after,
    )


def ring_sum(info, own, left, right, from_left, from_right, after=(), small=()):
    count = own.shape[0] // 2
    part = count // 4
    extra = sum(array.shape[0] for array in small)

    def body(info, own, left, right, from_left, from_right, *outs):
        if extra:
            small, outs = outs[0], outs[1:]
            total = total_of(
                small[...], from_left[2 * count :], from_right[2 * count :], left[count:]
            )
        for k, out in enumerate(outs):
            at = pl.multiple_of(lax.rem(info[3] + k, 4) * part, 16)
            low, high = pl.ds(at, part), pl.ds(at + count, part)
            out[:part] = total_of(own[low], left[low], from_right[high])
            out[part : 2 * part] = total_of(own[high], from_left[high], right[low])
            if extra:
                out[2 * part :] = total

    return small_kernel(
        body,
        "ring_sum",
        [(2 * part + extra, D)] * 4,
        (own, left, right, from_left, from_right, *small),
        after,
        info,
    )


def add_all(name, terms, after=()):
    def body(*refs):
        refs[-1][...] = total_of(*(ref[...] for ref in refs[:-1]))

    return small_kernel(body, name, [terms[0].shape], terms, after)[0]


def hand_on(arrays, after):
    return small_kernel(lambda *refs: None, "hand_on", [], (), after, None, arrays)


def split_sum(one, two, count, after=()):
    middle = count + S_TABLE

    def body(one, two, *outs):
        total = total_of(one[...], two[...])
        outs[0][...] = total[:count]
        outs[1][...] = total[count:middle]
        outs[2][...] = total[middle:]

    shapes = [(count, D), (S_TABLE, D), (SMALL - S_TABLE, D)]
    return small_kernel(body, "z_sum", shapes, (one, two), after)


def finish_small(small, table, far, after=()):
    places = [n for n in range(S_TABLE) if not S_EXPAND <= n < S_EXPAND + 4]

    def kernel(small, table, far, *refs):
        vectors, (b_expand, whole, done) = refs[len(after) : -3], refs[-3:]
        done[...] = jnp.zeros_like(done)
        values = small[...].astype(WIDE)
        for place, vector in zip(places, vectors):
            vector[...] = values[place : place + 1]
        for column in range(4):
            lanes = slice(column * D, (column + 1) * D)
            b_expand[:, lanes] = values[S_EXPAND + column : S_EXPAND + column + 1]
        total = table[...].astype(WIDE) + far[...].astype(WIDE)
        heads = [total[:, column * L : (column + 1) * L] for column in range(4)]
        whole[...] = jnp.concatenate(heads).T[:NB, :H]

    *vectors, b_expand, whole, done = pl.pallas_call(
        kernel,
        out_shape=[shaped((1, D), WIDE)] * len(places)
        + [shaped((1, FF), WIDE), shaped((NB, H), WIDE), TOKEN],
        in_specs=[VMEM] * 3 + [ANY] * len(after),
        out_specs=[VMEM] * (len(places) + 3),
        compiler_params=limit(4),
        cost_estimate=cost(1),
        name="finish_small",
    )(small, table, far, *after)
    return dict(zip(places, vectors)), b_expand, whole, done


def inner_join(info, parts, after=(), through=()):
    part = parts[0].shape[0] // 2

    def body(info, *refs):
        whole = refs[-1]
        for k, ref in enumerate(refs[:-1]):
            at = pl.multiple_of(lax.rem(info[3] + k, 4) * part, 16)
            whole[pl.ds(at, part)] = ref[:part]
            whole[pl.ds(at + 4 * part, part)] = ref[part:]

    return small_kernel(body, "inner_join", [(8 * part, D)], parts, after, info, through)


def cut(arrays, after=()):
    rows = arrays[0].shape[0]
    count = rows // 2

    def body(*refs):
        arrays, (right, left, whole) = refs[:-3], refs[-3:]
        right[...] = arrays[0][:count]
        left[...] = arrays[1][count:]
        for index, ref in enumerate(arrays):
            whole[index * rows : (index + 1) * rows] = ref[...]

    shapes = [(count, D), (count, D), (len(arrays) * rows, D)]
    return small_kernel(body, "cut", shapes, arrays, after)


def feed_targets(outs, source, half, core, quarter):
    pairs = []
    for block in range(2):
        part = source.at[block * QUARTER : (block + 1) * QUARTER]
        if half == 0:
            target = rows_at(outs[0], core * HALF + block * D + quarter * QUARTER, QUARTER)
        else:
            target = columns(
                rows_at(outs[1], quarter * QUARTER, QUARTER), (core * 2 + block) * D, D
            )
        pairs.append((None, part, target))
    return pairs


def attend_targets(outs, source, half, core, quarter):
    return [
        (
            core == number,
            source.at[:QUARTER],
            rows_at(outs[2 * number + half], quarter * QUARTER, QUARTER),
        )
        for number in range(2)
    ]


def settle(targets, shapes, count, info, pieces, outs, name, after=()):
    keys = tuple(pieces)
    arrays = [pieces[key] for key in keys]
    given = list(after) + list(outs or ())

    def kernel(info, *refs):
        parts, rest = refs[: len(keys)], refs[len(keys) + len(given) :]
        outs, rest = rest[: len(shapes)], rest[len(shapes) :]
        done, rest = rest[0], rest[1:]
        done[...] = jnp.zeros_like(done)
        wide_held, out_sems = rest[:-1], rest[-1]
        finish = []
        for index, (sibling, places) in enumerate(keys):
            core = 1 - info[0] if sibling else info[0]
            for number, (k, half) in enumerate(places):
                quarter = lax.rem((info[3] if sibling else info[1]) + k, 4)
                source = wide_held[index].at[number * count : (number + 1) * count]
                source[...] = parts[index][number * count : (number + 1) * count].astype(WIDE)
                for place, (condition, part, target) in enumerate(
                    targets(outs, source, half, core, quarter)
                ):
                    copy = pltpu.make_async_copy(
                        part, target, out_sems.at[12 * index + 2 * number + place]
                    )
                    if condition is None:
                        copy.start()
                        finish.append(copy.wait)
                    else:
                        pl.when(condition)(copy.start)
                        finish.append(lambda c=copy, when=condition: pl.when(when)(c.wait))
        for action in finish:
            action()

    result = pl.pallas_call(
        kernel,
        out_shape=[shaped(shape, WIDE) for shape in shapes]
        + [TOKEN],
        in_specs=[SMEM] + [VMEM] * len(keys) + [ANY] * len(given),
        out_specs=[ANY] * len(shapes) + [VMEM],
        scratch_shapes=[pltpu.VMEM(array.shape, WIDE) for array in arrays]
        + [DMA((12 * len(keys),))],
        input_output_aliases={
            1 + len(keys) + len(after) + i: i for i in range(len(outs or ()))
        },
        compiler_params=limit(20),
        cost_estimate=cost(sum(array.size for array in arrays) * 2e-6 + 1),
        name=name,
    )(info, *arrays, *given)
    return result[:-1], result[-1]


PLANE = ("x", "y", "c")


def shift(value, axis, by):
    size = lax.axis_size(axis)
    return lax.ppermute(value, axis, [(i, (i + by) % size) for i in range(size)])


def send(value, by):
    return lax.ppermute(value, "s", [(0, 1)] if by > 0 else [(1, 0)])


def turn(value, outer, by):
    pairs = []
    for i in range(4):
        for j in range(4):
            for c in range(2):
                if (c == 0) == outer:
                    target = ((i + by) % 4, j)
                else:
                    target = (i, (j + by) % 4)
                pairs.append(((i * 4 + j) * 2 + c, (target[0] * 4 + target[1]) * 2 + c))
    return lax.ppermute(value, PLANE, pairs)


def place(outer):
    return jnp.where(
        (lax.axis_index("c") == 0) == outer, lax.axis_index("x"), lax.axis_index("y")
    )


def wide(value):
    return value.astype(WIDE)


def total_wide(*terms):
    return sum(wide(term) for term in terms)


def inner_turns(parts, sign):
    return [turn(part, False, sign * by) for part, by in zip(parts, (1, 2, -1))]


OWN, ACROSS = ((0, 0), (0, 1)), (((2, 0),), ((2, 1),))
NEAR = ((3, 0), (3, 1), (1, 0), (1, 1))


def both_cores(places, piece):
    return {(0, places): piece, (1, places): shift(piece, "c", 1)}


def on_device(
    content_in,
    query_in,
    content_cot,
    query_cot,
    order_rank,
    query_pos,
    group_tag,
    *rest,
):
    (
        w_query,
        b_query,
        w_key,
        w_value,
        b_value,
        w_out,
        b_out,
        norm1_gain,
        norm1_bias,
        w_expand,
        b_expand,
        w_contract,
        b_contract,
        norm2_gain,
        norm2_bias,
    ) = (argument[0] for argument in rest[:-1])
    rel_table = rest[-1]
    core = lax.axis_index("c")
    first_section = (lax.axis_index("s") == 0).astype(jnp.int32)
    info = jnp.stack([core, place(True), first_section, place(False)])
    picks = query_pos.shape[1]

    matrices = (w_query, w_key, w_value, w_out, w_expand, w_contract)
    w_out_held = w_out
    vec = jnp.stack(
        [b_query, b_value, b_out, norm1_gain, norm1_bias, b_contract, norm2_gain, norm2_bias]
    )
    ranks = jnp.concatenate([order_rank, group_tag, query_pos], axis=1)
    masks, spread, query_in, query_cot = prepare(
        ranks, rel_table, jnp.concatenate([query_in, query_cot]), picks, (vec, info)
    )
    b_expand = b_expand[None]

    fronts, arrived = [], []
    for seq in range(SEQS):
        fronts.append(
            front(seq, info, content_in, query_in, matrices, masks, vec, b_expand, tuple(fronts))
        )
        arrived.append(send(fronts[seq], 1))
    output, early, pair, saved, grads = [], [], [], [], []
    for seq in range(SEQS):
        results = middle_forward(
            seq, info, content_in, query_in, arrived[seq], matrices, masks, vec, b_expand, tuple(grads)
        )
        for collected, result in zip((output, early, pair, saved), results):
            collected.append(result)
        grads.append(middle_back(seq, content_cot, query_cot, matrices, vec, saved[seq]))
    early = [shift(value, "c", 1) for value in early]
    grads = [send(value, -1) for value in grads]
    small = None
    total, branch, attended, own, late, pieces, pass_on = [], [], [], [], [], [], []
    for seq in range(SEQS):
        results = feed_back(
            seq,
            info,
            grads[seq],
            content_cot,
            query_cot,
            small,
            vec,
            matrices,
            saved[seq],
            tuple(pass_on),
        )
        small = results[3]
        for collected, result in zip(
            (total, branch, attended, own, late), results[:3] + results[4:]
        ):
            collected.append(result)
        late[seq] = shift(late[seq], "c", 1)
        results = attend_back(
            seq,
            info,
            attended[seq],
            small,
            spread,
            (),
            w_out_held,
            saved[seq],
        )
        small = results[2]
        pieces.append(results[0])
        pass_on.append(results[1])
    feed_terms = feed_grads(info, saved, branch, own, early, late, (small,))
    passed = [shift(value, "c", 1) for value in pass_on]

    def outer_step(terms):
        return (turn(terms[0], True, 1), turn(terms[1], True, -1))

    f_left, f_right = outer_step(feed_terms)
    *attend_terms, extra = attend_grads(info, pair, early, pieces, passed, small, (feed_terms[4],))
    a_left, a_right = outer_step(attend_terms)
    f_sent = ring_add(feed_terms[2], feed_terms[3], f_left, f_right, (extra,))
    f_outer = outer_step(f_sent)
    a_sent = ring_add(attend_terms[2], attend_terms[3], a_left, a_right)
    f_parts = ring_sum(info, feed_terms[4], *f_outer, f_left, f_right, (a_sent[0],))
    f_others = inner_turns(f_parts[1:], 1)
    a_parts = ring_sum(
        info, attend_terms[4], *outer_step(a_sent), a_left, a_right, (f_parts[0],), (extra,)
    )
    f_part = add_all("inner_sum", [f_parts[0]] + f_others, (a_parts[0],))
    f_far = shift(f_part, "z", 1)
    a_part = add_all("inner_sum", [a_parts[0]] + inner_turns(a_parts[1:], 1), (f_part,))
    a_far = shift(a_part, "z", 1)
    f_part = add_all("z_sum", [f_part, f_far])
    f_others = inner_turns([f_part] * 3, -1)
    a_part, small, table = split_sum(a_part, a_far, 2 * QUARTER // 4, (f_part,))
    a_others = inner_turns([a_part] * 3, -1)
    (feed_own,) = inner_join(info, [f_part] + f_others, (a_part,))
    feed_outer = (turn(feed_own, True, 1), turn(feed_own, True, -1))
    (attend_own,) = inner_join(info, [a_part] + a_others, (feed_own,))
    attend_outer = (turn(attend_own, True, 1), turn(attend_own, True, -1))
    content_ends, query_ends, token = finish_rows(
        info, total, output, pieces, matrices, picks, (attend_own,)
    )

    def feed_settle(pieces, outs, name):
        return settle(
            feed_targets, ((FF, D), (D, FF)), 2 * QUARTER, info, pieces, outs, "feed_" + name
        )

    def attend_settle(pieces, outs, name, after=()):
        return settle(
            attend_targets,
            ((D, D),) * 4,
            QUARTER,
            info,
            pieces,
            outs,
            "attend_" + name,
            after,
        )

    feed_outs, own_token = feed_settle(both_cores(OWN, feed_own), None, "own")
    to_right, to_left, feed_near = cut(feed_outer, (token, own_token))
    feed_across = (turn(to_right, True, 1), turn(to_left, True, -1))
    feed_outs, token = feed_settle(both_cores(NEAR, feed_near), feed_outs, "near")
    row, b_expand, table, small_token = finish_small(small, table, shift(table, "s", 1), (token,))
    to_right, to_left, attend_near = cut(
        (*attend_outer, attend_own), (token, small_token, *feed_across)
    )
    attend_across = (turn(to_right, True, 1), turn(to_left, True, -1))
    feed_outs, token = feed_settle(
        both_cores(ACROSS[0], feed_across[0]) | both_cores(ACROSS[1], feed_across[1]),
        feed_outs,
        "across",
    )
    attend_outs, near_token = attend_settle(both_cores(NEAR + OWN, attend_near), None, "near")
    attend_across = hand_on(attend_across, (token, near_token))
    attend_outs, _ = attend_settle(
        both_cores(ACROSS[0], attend_across[0]) | both_cores(ACROSS[1], attend_across[1]),
        attend_outs,
        "across",
    )
    contract, expand = feed_outs
    g_query, g_key, g_out, g_value = attend_outs
    return (
        content_ends[None],
        query_ends[None],
        g_query[None],
        row[S_QUERY],
        g_key[None],
        g_value[None],
        row[S_VALUE],
        g_out[None],
        row[S_OUT],
        row[S_GAIN1],
        row[S_SHIFT1],
        expand[None],
        b_expand,
        contract[None],
        row[S_CONTRACT],
        row[S_GAIN2],
        row[S_SHIFT2],
        table,
    )


DP = ("z", "x", "y", "c")


def solution(mesh):
    mesh = jax.sharding.Mesh(mesh.devices.reshape(2, 2, 4, 4, 2), ("s",) + DP)
    layer_specs = tuple(
        P("s", *([None] * (rank - 1))) for rank in (3, 2, 3, 3, 2, 3, 2, 2, 2, 3, 2, 3, 2, 2, 2)
    )
    in_specs = (P(DP, None),) * 7 + layer_specs + (P(),)
    out_specs = (P("s", DP, None),) * 2 + layer_specs + (P(),)
    return jax.shard_map(
        on_device, mesh=mesh, in_specs=in_specs, out_specs=out_specs, check_vma=False
    )
```

```python
import jax
import jax.numpy as jnp
from jax import lax
from jax.experimental import pallas as pl
from jax.experimental.pallas import tpu as pltpu
from jax.sharding import PartitionSpec as P

D = 768
H = 12
HD = 64
FF = 3072
NB = 32
L = 128
PAIRS = H // 2
SEQS = 2
PICKS = 32
ROWS = L + PICKS
EPSILON = 1e-05
SCALE = HD ** (-0.5)
TILE = 1536
LOW = jnp.bfloat16
WIDE = jnp.float32
HALF = FF // 2
QUARTER = D // 4
EARLY = 3 * D + HALF
LATE = D + HALF
SMALL = 16
ALL_ROWS = SEQS * ROWS
ALL_CONTENT = SEQS * L
PIECE = ALL_ROWS + ALL_CONTENT


def nn(former, latter):
    return lax.dot_general(
        former, latter, (((1,), (0,)), ((), ())), preferred_element_type=WIDE
    )


def nt(former, latter):
    return lax.dot_general(
        former, latter, (((1,), (1,)), ((), ())), preferred_element_type=WIDE
    )


def tn(former, latter):
    return lax.dot_general(
        former, latter, (((0,), (0,)), ((), ())), preferred_element_type=WIDE
    )


def halves(value):
    even = lax.broadcasted_iota(jnp.int32, value.shape, 1) < HD
    zero = jnp.zeros_like(value)
    return jnp.concatenate([jnp.where(even, value, zero), jnp.where(even, zero, value)])


def side(value):
    count = value.shape[0] // 2
    return jnp.concatenate([value[:count], value[count:]], axis=1)


def norm_rows(values):
    centered = values - jnp.mean(values, axis=-1, keepdims=True)
    variance = jnp.mean(centered * centered, axis=-1, keepdims=True)
    root = lax.rsqrt(variance + EPSILON)
    return (centered * root, root)


def norm_rows_back(scaled, normed, root):
    return root * (
        scaled
        - jnp.mean(scaled, axis=-1, keepdims=True)
        - normed * jnp.mean(scaled * normed, axis=-1, keepdims=True)
    )


B_QUERY, B_VALUE, B_OUT, GAIN1, SHIFT1, B_CONTRACT, GAIN2, SHIFT2 = range(8)
S_QUERY, S_VALUE, S_OUT, S_GAIN1, S_SHIFT1, S_EXPAND = range(6)
S_CONTRACT, S_GAIN2, S_SHIFT2, S_TABLE = 9, 10, 11, 12
LIMITS = (12, 16, 23, 32, 46, 64, 91)


def bucket_of(relative):
    distance = jnp.abs(relative)
    beyond = 8 + sum((distance >= limit).astype(jnp.int32) for limit in LIMITS)
    within = jnp.where(distance < 8, distance, beyond)
    return within + 16 * (relative > 0).astype(jnp.int32)


def forward(x, w, vec, b_expand, masks, s, keep):
    row = lambda k: vec[k : k + 1, :]
    s.query[...] = (nn(x[...], w.query[...]) + row(B_QUERY)).astype(LOW)
    s.key[...] = nn(x[:L], w.key[...]).astype(LOW)
    s.value[...] = (nn(x[:L], w.value[...]) + row(B_VALUE)).astype(LOW)
    for pair in range(PAIRS):
        lanes = slice(pair * 128, (pair + 1) * 128)
        scores = nt(halves(s.query[:, lanes]), s.key[:, lanes]) * SCALE + masks[pair]
        shifted = jnp.exp(scores - jnp.max(scores, axis=-1, keepdims=True))
        probs = (shifted / jnp.sum(shifted, axis=-1, keepdims=True)).astype(LOW)
        if keep:
            s.probs[pair] = probs
        s.mixed[:, lanes] = nn(side(probs), halves(s.value[:, lanes])).astype(LOW)
    total = x[...].astype(WIDE) + nn(s.mixed[...], w.out[...]) + row(B_OUT)
    normed, root = norm_rows(total)
    first = normed * row(GAIN1) + row(SHIFT1)
    s.first_low[...] = first.astype(LOW)
    s.total[...] = first + row(B_CONTRACT)
    if keep:
        s.normed1[...] = normed
        s.root1[...] = jnp.broadcast_to(root, (ROWS, 128))
    for tile in range(FF // TILE):
        tile = slice(tile * TILE, (tile + 1) * TILE)
        expanded = nn(s.first_low[...], w.expand[:, tile]) + b_expand[:, tile]
        cumulative = 0.5 * (1.0 + lax.erf(expanded * 0.7071067811865476))
        activated = (expanded * cumulative).astype(LOW)
        if keep:
            s.slope[:, tile] = (
                cumulative + expanded * jnp.exp(-0.5 * expanded * expanded) * 0.3989422804014327
            ).astype(LOW)
            s.activated[:, tile] = activated
        s.total[...] += nn(activated, w.contract[tile, :])
    normed, root = norm_rows(s.total[...])
    if keep:
        s.normed2[...] = normed
        s.root2[...] = jnp.broadcast_to(root, (ROWS, 128))
    s.out[...] = (normed * row(GAIN2) + row(SHIFT2)).astype(s.out.dtype)


def column_sum(value):
    return jnp.sum(value.astype(WIDE), axis=0, keepdims=True)


def back_second_norm(grad, vec, s, add=None):
    upper = grad.astype(WIDE)
    normed = s.normed2[...]
    lower = norm_rows_back(upper * vec[GAIN2 : GAIN2 + 1, :], normed, s.root2[:, :1])
    s.total[...] = lower
    s.branch[...] = lower.astype(LOW)
    if add is not None:
        add(S_GAIN2, column_sum(upper * normed))
        add(S_SHIFT2, column_sum(upper))
        add(S_CONTRACT, column_sum(lower.astype(LOW)))


def back_feed(w, vec, s, add=None):
    for tile in range(FF // TILE):
        tile = slice(tile * TILE, (tile + 1) * TILE)
        lower = (nt(s.branch[...], w.contract[tile, :]) * s.slope[:, tile].astype(WIDE)).astype(LOW)
        s.expanded[:, tile] = lower
        if add is not None:
            part = column_sum(lower)
            for column in range(TILE // D):
                add(
                    S_EXPAND + tile.start // D + column,
                    part[:, column * D : (column + 1) * D],
                )
        s.total[...] += nt(lower, w.expand[:, tile])
    upper = s.total[...]
    normed = s.normed1[...]
    lower = norm_rows_back(upper * vec[GAIN1 : GAIN1 + 1, :], normed, s.root1[:, :1])
    s.total[...] = lower
    s.attended[...] = lower.astype(LOW)
    if add is not None:
        add(S_GAIN1, column_sum(upper * normed))
        add(S_SHIFT1, column_sum(upper))
        add(S_OUT, column_sum(lower.astype(LOW)))


def back_attend(s, table=None):
    for pair in range(PAIRS):
        lanes = slice(pair * 128, (pair + 1) * 128)
        probs = s.probs[pair]
        below = halves(s.dmixed[:, lanes])
        dprobs = nt(below, s.value[:, lanes])
        s.dvalue[:, lanes] = tn(probs, below).astype(LOW)
        weight = probs.astype(WIDE)
        dscores = (
            weight * (dprobs - jnp.sum(weight * dprobs, axis=-1, keepdims=True))
        ).astype(LOW)
        s.dquery[:, lanes] = (nn(side(dscores), halves(s.key[:, lanes])) * SCALE).astype(LOW)
        s.dkey[:, lanes] = (tn(dscores, halves(s.query[:, lanes])) * SCALE).astype(LOW)
        if table is not None:
            table(pair, dscores)


class Names:
    def __init__(self, **named):
        self.__dict__.update(named)


MATRICES = ("query", "key", "value", "out", "expand", "contract")
MATRIX_SHAPES = {
    "query": (D, D),
    "key": (D, D),
    "value": (D, D),
    "out": (D, D),
    "expand": (D, FF),
    "contract": (FF, D),
}
MASK_SHAPE = (PAIRS, 2 * ROWS, L)
KEPT = {
    "query": ((ROWS, D), LOW),
    "key": ((L, D), LOW),
    "value": ((L, D), LOW),
    "probs": (MASK_SHAPE, LOW),
    "mixed": ((ROWS, D), LOW),
    "normed1": ((ROWS, D), WIDE),
    "root1": ((ROWS, 128), WIDE),
    "first_low": ((ROWS, D), LOW),
    "slope": ((ROWS, FF), LOW),
    "activated": ((ROWS, FF), LOW),
    "normed2": ((ROWS, D), WIDE),
    "root2": ((ROWS, 128), WIDE),
}
SAVED = tuple(name for name in KEPT if name != "mixed")
ANY = pl.BlockSpec(memory_space=pl.ANY)
HBM = pl.BlockSpec(memory_space=pltpu.HBM)
VMEM = pl.BlockSpec(memory_space=pltpu.VMEM)
SMEM = pl.BlockSpec(memory_space=pltpu.SMEM)


def limit(megabytes):
    return pltpu.CompilerParams(vmem_limit_bytes=megabytes * 1024 * 1024)


DMA = pltpu.SemaphoreType.DMA


def cost(microseconds):
    return pl.CostEstimate(flops=0, bytes_accessed=int(microseconds * 3.2e6), transcendentals=0)


def shaped(shape, kind):
    return jax.ShapeDtypeStruct(shape, kind)


TOKEN = shaped((8, 128), WIDE)


def columns(ref, start, size):
    return ref.at[:, pl.ds(pl.multiple_of(start, 128), size)]


def rows_at(ref, start, size):
    return ref.at[pl.ds(pl.multiple_of(start, 64), size)]


def start_all(pairs, sems, base=0):
    copies = [
        pltpu.make_async_copy(source, target, sems.at[base + index])
        for index, (source, target) in enumerate(pairs)
    ]
    for copy in copies:
        copy.start()
    return copies


def wait_all(copies):
    for copy in copies:
        copy.wait()


def fetcher(names, sources, targets, sems, base=0):
    copies = dict(zip(names, start_all(list(zip(sources, targets)), sems, base)))
    return lambda name: copies[name].wait()


def prepare(ranks, table, queries, picks, after):
    def kernel(ranks, table, queries, *refs):
        masks, spread, rows_in, rows_cot = refs[len(after) :]
        order, tag, pos = ranks[:, :L], ranks[:, L : 2 * L], ranks[:, 2 * L : 2 * L + picks]
        values = queries[...].astype(WIDE)
        blank = jnp.zeros((PICKS - picks, D), WIDE)
        for index, target in enumerate((rows_in, rows_cot)):
            own = values[2 * index * picks : 2 * (index + 1) * picks]
            target[...] = jnp.concatenate([own[:picks], blank, own[picks:], blank]).astype(LOW)
        lane = lax.broadcasted_iota(jnp.int32, (L, L), 1)
        level = lax.broadcasted_iota(jnp.int32, (L, L), 0)
        lane_q = lax.broadcasted_iota(jnp.int32, (PICKS, L), 1)
        upright = lambda row: jnp.sum(jnp.where(lane == level, row, 0.0), axis=1, keepdims=True)
        distance = lax.broadcasted_iota(jnp.int32, (2 * L, NB), 0) - (L - 1)
        bucket = lax.broadcasted_iota(jnp.int32, (2 * L, NB), 1)
        by_distance = lax.dot_general(
            table[...],
            (bucket_of(distance) == bucket).astype(WIDE),
            (((0,), (1,)), ((), ())),
            precision=lax.Precision.HIGHEST,
            preferred_element_type=WIDE,
        )
        allowed, hot = [], []
        for seq in range(SEQS):
            own_rank = order[seq : seq + 1, :].astype(WIDE)
            own_tag = tag[seq : seq + 1, :].astype(WIDE)
            own_pos = pos[seq : seq + 1, :].astype(WIDE)
            number = lax.broadcasted_iota(jnp.int32, (PICKS, picks), 0)
            same = number == lax.broadcasted_iota(jnp.int32, (PICKS, picks), 1)
            place = jnp.sum(jnp.where(same, own_pos, 0.0), axis=1, keepdims=True)
            filled = lax.broadcasted_iota(jnp.int32, (PICKS, 1), 0) < picks
            place = jnp.where(filled, place, -1.0).astype(jnp.int32)
            matches = place == lane_q
            marks = jnp.where(matches, 1.0, 0.0)
            predicted = jnp.max(marks, axis=0, keepdims=True)
            rank = jnp.sum(jnp.where(matches, own_rank, 0.0), axis=1, keepdims=True)
            group = jnp.sum(jnp.where(matches, own_tag, 0.0), axis=1, keepdims=True)
            earlier = (upright(predicted) > 0) & (own_rank <= upright(own_rank))
            content = (upright(own_tag) == own_tag) & ((predicted == 0) | earlier)
            query = (group == own_tag) & ((predicted == 0) | (own_rank + 1 <= rank))
            allowed.append((content, query))
            hot.append(marks)
            spread[seq, :L] = jnp.where(lane == L - 1 - level, 1.0, 0.0).astype(LOW)
            spread[seq, L:] = jnp.where(lane_q == L - 1 - place, 1.0, 0.0).astype(LOW)
        hot = jnp.concatenate(hot)
        for head in range(H):
            row = jnp.broadcast_to(by_distance[head : head + 1], (L, 2 * L))
            bias = pltpu.roll(row, L + 1, 1, stride=1, stride_axis=0)[:, :L]
            bias_q = lax.dot_general(
                hot,
                bias,
                (((1,), (0,)), ((), ())),
                precision=lax.Precision.HIGHEST,
                preferred_element_type=WIDE,
            )
            base = head % 2 * ROWS
            for seq in range(SEQS):
                content, query = allowed[seq]
                masks[seq, head // 2, base : base + L] = jnp.where(content, bias, -1e30)
                masks[seq, head // 2, base + L : base + ROWS] = jnp.where(
                    query, bias_q[seq * PICKS : (seq + 1) * PICKS], -1e30
                )

    return pl.pallas_call(
        kernel,
        out_shape=[
            shaped((SEQS,) + MASK_SHAPE, WIDE),
            shaped((SEQS, ROWS, L), LOW),
            shaped((SEQS * PICKS, D), LOW),
            shaped((SEQS * PICKS, D), LOW),
        ],
        in_specs=[VMEM] * 3 + [ANY] * len(after),
        out_specs=[VMEM] * 4,
        compiler_params=limit(8),
        cost_estimate=pl.CostEstimate(flops=int(3e10), bytes_accessed=0, transcendentals=0),
        name="prepare",
    )(ranks, table, queries, *after)


def take_rows(content, picks, seq, target):
    target[:L] = content[seq * L : (seq + 1) * L]
    target[L:] = picks[seq * PICKS : (seq + 1) * PICKS]


def front(seq, info, content, picks, matrices, masks, vec, b_expand, after=()):
    def kernel(info, content, picks, masks, vec, b_expand, *refs):
        w = Names(**dict(zip(MATRICES, refs[:6])))
        out, x, query, key, value, mixed, first_low, total = refs[6 + len(after) :]
        s = Names(
            query=query,
            key=key,
            value=value,
            mixed=mixed,
            first_low=first_low,
            total=total,
            out=out,
        )
        take_rows(content, picks, seq, x)
        forward(x, w, vec, b_expand, masks.at[seq], s, False)

    return pl.pallas_call(
        kernel,
        out_shape=shaped((ROWS, D), LOW),
        in_specs=[SMEM] + [VMEM] * 11 + [ANY] * len(after),
        out_specs=VMEM,
        scratch_shapes=[pltpu.VMEM((ROWS, D), LOW)]
        + [pltpu.VMEM(*KEPT[n]) for n in ("query", "key", "value", "mixed", "first_low")]
        + [pltpu.VMEM((ROWS, D), WIDE)],
        compiler_params=limit(12),
        cost_estimate=cost(5),
        name="front",
    )(info, content, picks, masks, vec, b_expand, *matrices, *after)


def middle_forward(seq, info, content, picks, arrived, matrices, masks, vec, b_expand, after=()):
    def kernel(info, arrived, content, picks, masks, vec, b_expand, *refs):
        w, rest = Names(**dict(zip(MATRICES, refs[:6]))), refs[6 + len(after) :]
        (out, early, pair), kept = rest[:3], rest[3 : 3 + len(SAVED)]
        mixed, total = rest[3 + len(SAVED) :]
        x = pair.at[0]
        s = Names(total=total, out=out, mixed=mixed, **dict(zip(SAVED, kept)))
        take_rows(content, picks, seq, x)
        x[...] = jnp.where(info[2] == 1, x[...], arrived[...])
        early[:, :D] = x[...]
        forward(x, w, vec, b_expand, masks.at[seq], s, True)
        pair[1] = mixed[...]
        early[:, D : 2 * D] = mixed[...]
        early[:, 2 * D : 3 * D] = s.first_low[...]
        early[:, 3 * D :] = columns(s.activated, (1 - info[0]) * HALF, HALF)[...]

    out, early, pair, *saved = pl.pallas_call(
        kernel,
        out_shape=[
            shaped((ROWS, D), WIDE),
            shaped((ROWS, EARLY), LOW),
            shaped((2, ROWS, D), LOW),
        ]
        + [shaped(*KEPT[n]) for n in SAVED],
        in_specs=[SMEM] + [VMEM] * 12 + [ANY] * len(after),
        out_specs=[VMEM] * (3 + len(SAVED)),
        scratch_shapes=[pltpu.VMEM(*KEPT["mixed"]), pltpu.VMEM((ROWS, D), WIDE)],
        compiler_params=limit(16),
        cost_estimate=cost(6),
        name="middle_forward",
    )(info, arrived, content, picks, masks, vec, b_expand, *matrices, *after)
    return (out, early, pair, dict(zip(SAVED, saved)))


FEED_SAVED = ("normed2", "root2", "slope", "normed1", "root1")
ATTEND_SAVED = ("value", "probs", "key", "query")


def middle_back(seq, content, picks, matrices, vec, saved):
    names = FEED_SAVED + ATTEND_SAVED

    def kernel(content, picks, vec, *refs):
        w, rest = Names(**dict(zip(MATRICES, refs[:6]))), refs[6:]
        kept, grad, rest = rest[: len(names)], rest[len(names)], rest[len(names) + 1 :]
        cot, total, branch, expanded, attended, dmixed, dvalue, dquery, dkey = rest
        s = Names(
            total=total,
            branch=branch,
            expanded=expanded,
            attended=attended,
            dmixed=dmixed,
            dvalue=dvalue,
            dquery=dquery,
            dkey=dkey,
            **dict(zip(names, kept)),
        )
        take_rows(content, picks, seq, cot)
        back_second_norm(cot[...], vec, s)
        back_feed(w, vec, s)
        dmixed[...] = nt(attended[...], w.out[...]).astype(LOW)
        back_attend(s)
        lower = total[...] + nt(dquery[...], w.query[...])
        upper = nt(dkey[...], w.key[...]) + nt(dvalue[...], w.value[...])
        grad[:L] = (lower[:L] + upper).astype(LOW)
        grad[L:] = lower[L:].astype(LOW)

    return pl.pallas_call(
        kernel,
        out_shape=shaped((ROWS, D), LOW),
        in_specs=[VMEM] * (9 + len(names)),
        out_specs=VMEM,
        scratch_shapes=[
            pltpu.VMEM((ROWS, D), LOW),
            pltpu.VMEM((ROWS, D), WIDE),
            pltpu.VMEM((ROWS, D), LOW),
            pltpu.VMEM((ROWS, FF), LOW),
            pltpu.VMEM((ROWS, D), LOW),
            pltpu.VMEM((ROWS, D), LOW),
            pltpu.VMEM((L, D), LOW),
            pltpu.VMEM((ROWS, D), LOW),
            pltpu.VMEM((L, D), LOW),
        ],
        compiler_params=limit(12),
        cost_estimate=cost(7),
        name="middle_back",
    )(content, picks, vec, *matrices, *(saved[n] for n in names))


def feed_back(seq, info, arrived, content, picks, small_in, vec, matrices, saved, after=()):
    given = [] if small_in is None else [small_in]

    def kernel(info, arrived, content, picks, vec, expand, contract, *refs):
        kept, rest = refs[:5], refs[5 + len(given) + len(after) :]
        total, branch, attended, small, own, late, upper, expanded = rest
        w = Names(expand=expand, contract=contract)
        s = Names(
            total=total,
            branch=branch,
            attended=attended,
            expanded=expanded,
            **dict(zip(FEED_SAVED, kept)),
        )
        small[...] = refs[5][...] if given else jnp.zeros_like(small)

        def add(place, value):
            small[place : place + 1, :] += value

        take_rows(content, picks, seq, upper)
        back_second_norm(jnp.where(info[2] == 1, arrived[...], upper[...]), vec, s, add)
        late[:, :D] = branch[...]
        back_feed(w, vec, s, add)
        own[...] = columns(expanded, info[0] * HALF, HALF)[...]
        late[:, D:] = columns(expanded, (1 - info[0]) * HALF, HALF)[...]

    return pl.pallas_call(
        kernel,
        out_shape=[
            shaped((ROWS, D), WIDE),
            shaped((ROWS, D), LOW),
            shaped((ROWS, D), LOW),
            shaped((SMALL, D), WIDE),
            shaped((ROWS, HALF), LOW),
            shaped((ROWS, LATE), LOW),
        ],
        in_specs=[SMEM] + [VMEM] * (11 + len(given)) + [ANY] * len(after),
        out_specs=[VMEM] * 6,
        scratch_shapes=[pltpu.VMEM((ROWS, D), LOW), pltpu.VMEM((ROWS, FF), LOW)],
        compiler_params=limit(12),
        cost_estimate=cost(4),
        name="feed_back",
    )(
        info,
        arrived,
        content,
        picks,
        vec,
        matrices[4],
        matrices[5],
        *(saved[n] for n in FEED_SAVED),
        *given,
        *after,
    )


PLACES = {
    (2, 0): (0, 0),
    (1, 1): (0, 1),
    (2, 1): (1, 0),
    (3, 0): (1, 1),
    (1, 0): (2, 0),
    (3, 1): (3, 0),
    (0, 0): (4, 0),
    (0, 1): (4, 1),
}


def term_shapes(count, extra=0):
    rows = (2 * count + extra, 2 * count + extra, count, count, 2 * count)
    return [shaped((n, D), LOW) for n in rows]


def feed_grads(info, mine, branch, own, early, late, after=()):
    def kernel(info, *refs):
        acts, lows, branches, owns, earlies, lates = (refs[2 * i : 2 * i + 2] for i in range(6))
        refs = refs[:12] + refs[12 + len(after) :]
        outs, (a_act, a_first, b_branch, b_own, stage, out_sems) = refs[12:17], refs[17:]
        core, place = info[0], info[1]
        own_at = [slice(seq * ROWS, (seq + 1) * ROWS) for seq in range(SEQS)]
        far_at = [slice((2 + seq) * ROWS, (3 + seq) * ROWS) for seq in range(SEQS)]
        for seq in range(SEQS):
            at, far = own_at[seq], far_at[seq]
            a_act[at] = columns(acts[seq], core * HALF, HALF)[...]
            a_act[far] = earlies[seq][:, 3 * D :]
            b_branch[at] = branches[seq][...]
            b_branch[far] = lates[seq][:, :D]
        sent = []

        def send(block):
            for k in range(4):
                quarter = lax.rem(place + k, 4)
                index, part = PLACES[k, block // 2]
                start = (2 * part + block % 2) * QUARTER
                sent.extend(
                    start_all(
                        [
                            (
                                rows_at(stage.at[block], quarter * QUARTER, QUARTER),
                                outs[index].at[start : start + QUARTER],
                            )
                        ],
                        out_sems,
                        block * 4 + k,
                    )
                )

        for block in range(2):
            for part in range(3):
                start = block * D + part * 256
                stage[block, part * 256 : (part + 1) * 256] = tn(
                    a_act[:, start : start + 256], b_branch[...]
                ).astype(LOW)
            send(block)
        for seq in range(SEQS):
            at, far = own_at[seq], far_at[seq]
            a_first[at] = lows[seq][...]
            a_first[far] = earlies[seq][:, 2 * D : 3 * D]
            b_own[at] = owns[seq][...]
            b_own[far] = lates[seq][:, D:]
        for block in range(2):
            for part in range(3):
                stage[2 + block, part * 256 : (part + 1) * 256] = tn(
                    a_first[:, part * 256 : (part + 1) * 256], b_own[:, block * D : (block + 1) * D]
                ).astype(LOW)
            send(2 + block)
        wait_all(sent)

    acts = [saved["activated"] for saved in mine]
    lows = [saved["first_low"] for saved in mine]
    return pl.pallas_call(
        kernel,
        out_shape=term_shapes(2 * QUARTER),
        in_specs=[SMEM] + [VMEM] * 12 + [ANY] * len(after),
        out_specs=[ANY] * 5,
        scratch_shapes=[
            pltpu.VMEM((2 * ALL_ROWS, HALF), LOW),
            pltpu.VMEM((2 * ALL_ROWS, D), LOW),
            pltpu.VMEM((2 * ALL_ROWS, D), LOW),
            pltpu.VMEM((2 * ALL_ROWS, HALF), LOW),
            pltpu.VMEM((4, D, D), LOW),
            DMA((16,)),
        ],
        compiler_params=limit(16),
        cost_estimate=cost(8),
        name="feed_grads",
    )(info, *acts, *lows, *branch, *own, *early, *late, *after)


def attend_back(seq, info, attended, small_in, spread, after, w_out, saved):
    def kernel(info, attended, small_in, spread, w_out, *refs):
        kept, (pieces, send, small, dmixed, sums) = refs[:4], refs[4 + len(after) :]
        small[...] = small_in[...]
        pieces[1, :ROWS] = attended[...]
        dmixed[...] = nt(attended[...], w_out[...]).astype(LOW)
        s = Names(
            dmixed=dmixed,
            dquery=pieces.at[0, :ROWS],
            dkey=pieces.at[0, ROWS:],
            dvalue=pieces.at[1, ROWS:],
            **dict(zip(ATTEND_SAVED, kept)),
        )
        sums[...] = jnp.zeros_like(sums)

        def table_sum(pair, dscores):
            for odd in range(2):
                part = tn(spread[seq], dscores[odd * ROWS : (odd + 1) * ROWS])
                both = jnp.concatenate([part, jnp.zeros((L, L), WIDE)], axis=1)
                turned = pltpu.roll(both, 0, 1, stride=1, stride_axis=0)
                head = 2 * pair + odd
                sums[head : head + 1, :] = jnp.sum(turned, axis=0, keepdims=True)

        back_attend(s, table_sum)
        send[: ROWS + L] = pieces[1 - info[0]]
        small[S_QUERY : S_QUERY + 1, :] += column_sum(pieces[0, :ROWS])
        small[S_VALUE : S_VALUE + 1, :] += column_sum(pieces[1, ROWS:])
        distance = lax.broadcasted_iota(jnp.int32, (2 * L, L), 0) - (L - 1)
        bucket = lax.broadcasted_iota(jnp.int32, (2 * L, L), 1)
        table = lax.dot_general(
            sums[...],
            (bucket_of(distance) == bucket).astype(WIDE),
            (((1,), (0,)), ((), ())),
            precision=lax.Precision.HIGHEST,
            preferred_element_type=WIDE,
        )
        for column in range(H // 4):
            lanes = slice(column * L, (column + 1) * L)
            small[S_TABLE : S_TABLE + 4, lanes] += table[4 * column : 4 * column + 4]
        send[ROWS + L :] = small[...].astype(LOW)

    return pl.pallas_call(
        kernel,
        out_shape=[
            shaped((2, ROWS + L, D), LOW),
            shaped((ROWS + L + SMALL, D), LOW),
            shaped((SMALL, D), WIDE),
        ],
        in_specs=[SMEM] + [VMEM] * 8 + [ANY] * len(after),
        out_specs=[VMEM] * 3,
        scratch_shapes=[pltpu.VMEM((ROWS, D), LOW), pltpu.VMEM((16, 2 * L), WIDE)],
        compiler_params=limit(12),
        cost_estimate=cost(4),
        name="attend_back",
    )(info, attended, small_in, spread, w_out, *(saved[n] for n in ATTEND_SAVED), *after)


def finish_rows(info, total, output, pieces, matrices, picks, after):
    def kernel(info, *refs):
        totals, outputs, pieces = refs[0:2], refs[2:4], refs[4:6]
        (query, key, value), refs = refs[6:9], refs[9 + len(after) :]
        content_ends, query_out, done, query_ends, sem = refs
        done[...] = jnp.zeros_like(done)
        first = info[2] == 1
        for seq in range(SEQS):
            lower = totals[seq][...] + nt(pieces[seq][0, :ROWS], query[...])
            upper = nt(pieces[seq][0, ROWS:], key[...]) + nt(pieces[seq][1, ROWS:], value[...])
            content_ends[seq * L : (seq + 1) * L] = jnp.where(
                first, lower[:L] + upper, outputs[seq][:L]
            )
            query_ends[seq * picks : (seq + 1) * picks] = jnp.where(
                first, lower[L : L + picks], outputs[seq][L : L + picks]
            )
        copy = pltpu.make_async_copy(query_ends, query_out, sem)
        copy.start()
        copy.wait()

    return pl.pallas_call(
        kernel,
        out_shape=[shaped((ALL_CONTENT, D), WIDE), shaped((SEQS * picks, D), WIDE), TOKEN],
        in_specs=[SMEM] + [VMEM] * 9 + [ANY] * len(after),
        out_specs=[VMEM, HBM, VMEM],
        scratch_shapes=[pltpu.VMEM((SEQS * picks, D), WIDE), DMA],
        compiler_params=limit(12),
        cost_estimate=cost(3),
        name="finish_rows",
    )(info, *total, *output, *pieces, *matrices[:3], *after)


def attend_grads(info, pair, early, mine, arrived, small, after=()):
    def kernel(info, small, *refs):
        pairs_in, earlies, mines, arriveds = (refs[2 * i : 2 * i + 2] for i in range(4))
        refs = refs[8 + len(after) :]
        outs, extra, rest = refs[:5], refs[5], refs[6:]
        a_rows, a_content, b_rows, b_content, stage, out_sems = rest
        core, place = info[0], info[1]
        for seq in range(SEQS):
            at = slice(seq * ROWS, (seq + 1) * ROWS)
            far = slice((2 + seq) * ROWS, (3 + seq) * ROWS)
            a_rows[at] = pairs_in[seq][core]
            a_rows[far] = columns(earlies[seq], core * D, D)[...]
            b_rows[at] = mines[seq][core, :ROWS]
            b_rows[far] = arriveds[seq][:ROWS]
            at = slice(seq * L, (seq + 1) * L)
            far = slice((2 + seq) * L, (3 + seq) * L)
            a_content[at] = pairs_in[seq][0, :L]
            a_content[far] = earlies[seq][:L, :D]
            b_content[at] = mines[seq][core, ROWS:]
            b_content[far] = arriveds[seq][ROWS : ROWS + L]
        far_small = arriveds[1][ROWS + L :]
        extra[...] = (small[...] + far_small.astype(WIDE)).astype(LOW)
        sent = start_all([(extra, outs[i].at[2 * QUARTER :]) for i in range(2)], out_sems, 8)
        for block, (former, latter) in enumerate(((a_rows, b_rows), (a_content, b_content))):
            for part in range(3):
                stage[block, part * 256 : (part + 1) * 256] = tn(
                    former[:, part * 256 : (part + 1) * 256], latter[...]
                ).astype(LOW)
            for k in range(4):
                quarter = lax.rem(place + k, 4)
                index, part = PLACES[k, block]
                start = part * QUARTER
                sent += start_all(
                    [
                        (
                            rows_at(stage.at[block], quarter * QUARTER, QUARTER),
                            outs[index].at[start : start + QUARTER],
                        )
                    ],
                    out_sems,
                    block * 4 + k,
                )
        wait_all(sent)

    return pl.pallas_call(
        kernel,
        out_shape=term_shapes(QUARTER, SMALL) + [shaped((SMALL, D), LOW)],
        in_specs=[SMEM] + [VMEM] * 9 + [ANY] * len(after),
        out_specs=[ANY] * 5 + [VMEM],
        scratch_shapes=[
            pltpu.VMEM((2 * ALL_ROWS, D), LOW),
            pltpu.VMEM((2 * ALL_CONTENT, D), LOW),
            pltpu.VMEM((2 * ALL_ROWS, D), LOW),
            pltpu.VMEM((2 * ALL_CONTENT, D), LOW),
            pltpu.VMEM((2, D, D), LOW),
            DMA((10,)),
        ],
        compiler_params=limit(12),
        cost_estimate=cost(5),
        name="attend_grads",
    )(info, small, *pair, *early, *mine, *arrived, *after)


def small_kernel(body, name, shapes, inputs, after=(), info=None, through=()):
    first = [] if info is None else [info]
    given = len(first) + len(inputs)

    def kernel(*refs):
        outs = refs[given + len(after) + len(through) :]
        body(*refs[:given], *outs[: len(shapes)])

    return pl.pallas_call(
        kernel,
        out_shape=[shaped(shape, LOW) for shape in shapes]
        + [shaped(array.shape, array.dtype) for array in through],
        in_specs=[SMEM] * len(first)
        + [VMEM] * len(inputs)
        + [ANY] * (len(after) + len(through)),
        out_specs=[VMEM] * len(shapes) + [ANY] * len(through),
        input_output_aliases={
            given + len(after) + i: len(shapes) + i for i in range(len(through))
        },
        compiler_params=limit(8),
        cost_estimate=cost(1),
        name=name,
    )(*first, *inputs, *after, *through)


def total_of(*terms):
    return sum(term.astype(WIDE) for term in terms).astype(LOW)


def ring_add(after0, before1, from_left, from_right, after=()):
    count = after0.shape[0]
    extra = from_left.shape[0] - 2 * count

    def body(after0, before1, from_left, from_right, right, left):
        right[:count] = total_of(after0[...], from_left[:count])
        left[:count] = total_of(before1[...], from_right[:count])
        if extra:
            right[count:] = from_left[2 * count :]
            left[count:] = from_right[2 * count :]

    return small_kernel(
        body,
        "ring_add",
        [(count + extra, D)] * 2,
        (after0, before1, from_left, from_right),
        after,
    )


def ring_sum(info, own, left, right, from_left, from_right, after=(), small=()):
    count = own.shape[0] // 2
    part = count // 4
    extra = sum(array.shape[0] for array in small)

    def body(info, own, left, right, from_left, from_right, *outs):
        if extra:
            small, outs = outs[0], outs[1:]
            total = total_of(
                small[...], from_left[2 * count :], from_right[2 * count :], left[count:]
            )
        for k, out in enumerate(outs):
            at = pl.multiple_of(lax.rem(info[3] + k, 4) * part, 16)
            low, high = pl.ds(at, part), pl.ds(at + count, part)
            out[:part] = total_of(own[low], left[low], from_right[high])
            out[part : 2 * part] = total_of(own[high], from_left[high], right[low])
            if extra:
                out[2 * part :] = total

    return small_kernel(
        body,
        "ring_sum",
        [(2 * part + extra, D)] * 4,
        (own, left, right, from_left, from_right, *small),
        after,
        info,
    )


def add_all(name, terms, after=()):
    def body(*refs):
        refs[-1][...] = total_of(*(ref[...] for ref in refs[:-1]))

    return small_kernel(body, name, [terms[0].shape], terms, after)[0]


def hand_on(arrays, after):
    return small_kernel(lambda *refs: None, "hand_on", [], (), after, None, arrays)


def z_join(feed, feed_far, attend, attend_far):
    first = feed.shape[0]
    count = attend.shape[0] - SMALL

    def body(feed, feed_far, attend, attend_far, whole, small, table):
        whole[:first] = total_of(feed[...], feed_far[...])
        total = total_of(attend[...], attend_far[...])
        whole[first:] = total[:count]
        small[...] = total[count : count + S_TABLE]
        table[...] = total[count + S_TABLE :]

    shapes = [(first + count, D), (S_TABLE, D), (SMALL - S_TABLE, D)]
    return small_kernel(body, "z_join", shapes, (feed, feed_far, attend, attend_far))


def finish_small(small, table, far, after=()):
    places = [n for n in range(S_TABLE) if not S_EXPAND <= n < S_EXPAND + 4]

    def kernel(small, table, far, *refs):
        vectors, (b_expand, whole, done) = refs[len(after) : -3], refs[-3:]
        done[...] = jnp.zeros_like(done)
        values = small[...].astype(WIDE)
        for place, vector in zip(places, vectors):
            vector[...] = values[place : place + 1]
        for column in range(4):
            lanes = slice(column * D, (column + 1) * D)
            b_expand[:, lanes] = values[S_EXPAND + column : S_EXPAND + column + 1]
        total = table[...].astype(WIDE) + far[...].astype(WIDE)
        heads = [total[:, column * L : (column + 1) * L] for column in range(4)]
        whole[...] = jnp.concatenate(heads).T[:NB, :H]

    *vectors, b_expand, whole, done = pl.pallas_call(
        kernel,
        out_shape=[shaped((1, D), WIDE)] * len(places)
        + [shaped((1, FF), WIDE), shaped((NB, H), WIDE), TOKEN],
        in_specs=[VMEM] * 3 + [ANY] * len(after),
        out_specs=[VMEM] * (len(places) + 3),
        compiler_params=limit(4),
        cost_estimate=cost(1),
        name="finish_small",
    )(small, table, far, *after)
    return dict(zip(places, vectors)), b_expand, whole, done


def inner_join(info, parts):
    counts = (QUARTER // 2, QUARTER // 4)
    half = 4 * sum(counts)

    def body(info, *refs):
        whole = refs[-1]
        start, given = 0, 0
        for count in counts:
            for k, ref in enumerate(refs[:-1]):
                at = pl.multiple_of(lax.rem(info[3] + k, 4) * count, 16) + start
                whole[pl.ds(at, count)] = ref[given : given + count]
                whole[pl.ds(at + half, count)] = ref[given + count : given + 2 * count]
            start, given = start + 4 * count, given + 2 * count

    return small_kernel(body, "inner_join", [(2 * half, D)], parts, (), info)[0]


def cut(before, after_part, after=()):
    count = before.shape[0] // 2

    def body(before, after_part, right, left, both):
        right[...] = before[:count]
        left[...] = after_part[count:]
        both[: 2 * count] = before[...]
        both[2 * count :] = after_part[...]

    shapes = [(count, D), (count, D), (4 * count, D)]
    return small_kernel(body, "cut", shapes, (before, after_part), after)


OUT_SHAPES = ((FF, D), (D, FF)) + ((D, D),) * 4


def out_places(outs, source, half, core, quarter):
    pairs = []
    for block in range(2):
        part = source.at[block * QUARTER : (block + 1) * QUARTER]
        if half == 0:
            target = rows_at(outs[0], core * HALF + block * D + quarter * QUARTER, QUARTER)
        else:
            target = columns(
                rows_at(outs[1], quarter * QUARTER, QUARTER), (core * 2 + block) * D, D
            )
        pairs.append((None, part, target))
    part = source.at[2 * QUARTER :]
    for number in range(2):
        target = rows_at(outs[2 + 2 * number + half], quarter * QUARTER, QUARTER)
        pairs.append((core == number, part, target))
    return pairs


def settle(info, pieces, outs, name, after=()):
    shapes, count = OUT_SHAPES, 3 * QUARTER
    keys = tuple(pieces)
    arrays = [pieces[key] for key in keys]
    given = list(after) + list(outs or ())

    def kernel(info, *refs):
        parts, rest = refs[: len(keys)], refs[len(keys) + len(given) :]
        outs, rest = rest[: len(shapes)], rest[len(shapes) :]
        done, rest = rest[0], rest[1:]
        done[...] = jnp.zeros_like(done)
        wide_held, out_sems = rest[:-1], rest[-1]
        finish = []
        for index, (sibling, places) in enumerate(keys):
            core = 1 - info[0] if sibling else info[0]
            for number, (k, half) in enumerate(places):
                quarter = lax.rem((info[3] if sibling else info[1]) + k, 4)
                source = wide_held[index].at[number * count : (number + 1) * count]
                source[...] = parts[index][number * count : (number + 1) * count].astype(WIDE)
                for place, (condition, part, target) in enumerate(
                    out_places(outs, source, half, core, quarter)
                ):
                    copy = pltpu.make_async_copy(
                        part, target, out_sems.at[16 * index + 4 * number + place]
                    )
                    if condition is None:
                        copy.start()
                        finish.append(copy.wait)
                    else:
                        pl.when(condition)(copy.start)
                        finish.append(lambda c=copy, when=condition: pl.when(when)(c.wait))
        for action in finish:
            action()

    result = pl.pallas_call(
        kernel,
        out_shape=[shaped(shape, WIDE) for shape in shapes]
        + [TOKEN],
        in_specs=[SMEM] + [VMEM] * len(keys) + [ANY] * len(given),
        out_specs=[ANY] * len(shapes) + [VMEM],
        scratch_shapes=[pltpu.VMEM(array.shape, WIDE) for array in arrays]
        + [DMA((16 * len(keys),))],
        input_output_aliases={
            1 + len(keys) + len(after) + i: i for i in range(len(outs or ()))
        },
        compiler_params=limit(20),
        cost_estimate=cost(sum(array.size for array in arrays) * 2e-6 + 1),
        name=name,
    )(info, *arrays, *given)
    return result[:-1], result[-1]


PLANE = ("x", "y", "c")


def shift(value, axis, by):
    size = lax.axis_size(axis)
    return lax.ppermute(value, axis, [(i, (i + by) % size) for i in range(size)])


def send(value, by):
    return lax.ppermute(value, "s", [(0, 1)] if by > 0 else [(1, 0)])


def turn(value, outer, by):
    pairs = []
    for i in range(4):
        for j in range(4):
            for c in range(2):
                if (c == 0) == outer:
                    target = ((i + by) % 4, j)
                else:
                    target = (i, (j + by) % 4)
                pairs.append(((i * 4 + j) * 2 + c, (target[0] * 4 + target[1]) * 2 + c))
    return lax.ppermute(value, PLANE, pairs)


def place(outer):
    return jnp.where(
        (lax.axis_index("c") == 0) == outer, lax.axis_index("x"), lax.axis_index("y")
    )


def wide(value):
    return value.astype(WIDE)


def total_wide(*terms):
    return sum(wide(term) for term in terms)


def inner_turns(parts, sign):
    return [turn(part, False, sign * by) for part, by in zip(parts, (1, 2, -1))]


OWN, ACROSS = ((0, 0), (0, 1)), (((2, 0),), ((2, 1),))
NEAR = ((3, 0), (3, 1), (1, 0), (1, 1))


def both_cores(places, piece):
    return {(0, places): piece, (1, places): shift(piece, "c", 1)}


def on_device(
    content_in,
    query_in,
    content_cot,
    query_cot,
    order_rank,
    query_pos,
    group_tag,
    *rest,
):
    (
        w_query,
        b_query,
        w_key,
        w_value,
        b_value,
        w_out,
        b_out,
        norm1_gain,
        norm1_bias,
        w_expand,
        b_expand,
        w_contract,
        b_contract,
        norm2_gain,
        norm2_bias,
    ) = (argument[0] for argument in rest[:-1])
    rel_table = rest[-1]
    core = lax.axis_index("c")
    first_section = (lax.axis_index("s") == 0).astype(jnp.int32)
    info = jnp.stack([core, place(True), first_section, place(False)])
    picks = query_pos.shape[1]

    matrices = (w_query, w_key, w_value, w_out, w_expand, w_contract)
    w_out_held = w_out
    vec = jnp.stack(
        [b_query, b_value, b_out, norm1_gain, norm1_bias, b_contract, norm2_gain, norm2_bias]
    )
    ranks = jnp.concatenate([order_rank, group_tag, query_pos], axis=1)
    masks, spread, query_in, query_cot = prepare(
        ranks, rel_table, jnp.concatenate([query_in, query_cot]), picks, (vec, info)
    )
    b_expand = b_expand[None]

    fronts, arrived = [], []
    for seq in range(SEQS):
        fronts.append(
            front(seq, info, content_in, query_in, matrices, masks, vec, b_expand, tuple(fronts))
        )
        arrived.append(send(fronts[seq], 1))
    output, early, pair, saved, grads = [], [], [], [], []
    for seq in range(SEQS):
        results = middle_forward(
            seq, info, content_in, query_in, arrived[seq], matrices, masks, vec, b_expand, tuple(grads)
        )
        for collected, result in zip((output, early, pair, saved), results):
            collected.append(result)
        grads.append(middle_back(seq, content_cot, query_cot, matrices, vec, saved[seq]))
    early = [shift(value, "c", 1) for value in early]
    grads = [send(value, -1) for value in grads]
    small = None
    total, branch, attended, own, late, pieces, pass_on = [], [], [], [], [], [], []
    for seq in range(SEQS):
        results = feed_back(
            seq,
            info,
            grads[seq],
            content_cot,
            query_cot,
            small,
            vec,
            matrices,
            saved[seq],
            tuple(pass_on),
        )
        small = results[3]
        for collected, result in zip(
            (total, branch, attended, own, late), results[:3] + results[4:]
        ):
            collected.append(result)
        late[seq] = shift(late[seq], "c", 1)
        results = attend_back(
            seq,
            info,
            attended[seq],
            small,
            spread,
            (),
            w_out_held,
            saved[seq],
        )
        small = results[2]
        pieces.append(results[0])
        pass_on.append(results[1])
    feed_terms = feed_grads(info, saved, branch, own, early, late, (small,))
    passed = [shift(value, "c", 1) for value in pass_on]

    def outer_step(terms):
        return (turn(terms[0], True, 1), turn(terms[1], True, -1))

    f_left, f_right = outer_step(feed_terms)
    *attend_terms, extra = attend_grads(info, pair, early, pieces, passed, small, (feed_terms[4],))
    a_left, a_right = outer_step(attend_terms)
    f_sent = ring_add(feed_terms[2], feed_terms[3], f_left, f_right, (extra,))
    f_outer = outer_step(f_sent)
    a_sent = ring_add(attend_terms[2], attend_terms[3], a_left, a_right)
    f_parts = ring_sum(info, feed_terms[4], *f_outer, f_left, f_right, (a_sent[0],))
    f_others = inner_turns(f_parts[1:], 1)
    a_parts = ring_sum(
        info, attend_terms[4], *outer_step(a_sent), a_left, a_right, (f_parts[0],), (extra,)
    )
    f_part = add_all("inner_sum", [f_parts[0]] + f_others, (a_parts[0],))
    f_far = shift(f_part, "z", 1)
    a_part = add_all("inner_sum", [a_parts[0]] + inner_turns(a_parts[1:], 1), (f_part,))
    a_far = shift(a_part, "z", 1)
    part, small, table = z_join(f_part, f_far, a_part, a_far)
    own = inner_join(info, [part] + inner_turns([part] * 3, -1))
    before, after_part = turn(own, True, 1), turn(own, True, -1)
    content_ends, query_ends, token = finish_rows(
        info, total, output, pieces, matrices, picks, (own,)
    )
    row, b_expand, table, small_token = finish_small(small, table, shift(table, "s", 1), (own,))
    outs, own_token = settle(info, both_cores(OWN, own), None, "own_out")
    to_right, to_left, near = cut(before, after_part, (token, small_token, own_token))
    across = (turn(to_right, True, 1), turn(to_left, True, -1))
    outs, near_token = settle(info, {(0, NEAR): near}, outs, "near_out")
    outs, far_token = settle(info, {(1, NEAR): shift(near, "c", 1)}, outs, "near_out")
    across = hand_on(across, (near_token, far_token))
    outs, _ = settle(
        info,
        both_cores(ACROSS[0], across[0]) | both_cores(ACROSS[1], across[1]),
        outs,
        "across_out",
    )
    contract, expand, g_query, g_key, g_out, g_value = outs
    return (
        content_ends[None],
        query_ends[None],
        g_query[None],
        row[S_QUERY],
        g_key[None],
        g_value[None],
        row[S_VALUE],
        g_out[None],
        row[S_OUT],
        row[S_GAIN1],
        row[S_SHIFT1],
        expand[None],
        b_expand,
        contract[None],
        row[S_CONTRACT],
        row[S_GAIN2],
        row[S_SHIFT2],
        table,
    )


DP = ("z", "x", "y", "c")


def solution(mesh):
    mesh = jax.sharding.Mesh(mesh.devices.reshape(2, 2, 4, 4, 2), ("s",) + DP)
    layer_specs = tuple(
        P("s", *([None] * (rank - 1))) for rank in (3, 2, 3, 3, 2, 3, 2, 2, 2, 3, 2, 3, 2, 2, 2)
    )
    in_specs = (P(DP, None),) * 7 + layer_specs + (P(),)
    out_specs = (P("s", DP, None),) * 2 + layer_specs + (P(),)
    return jax.shard_map(
        on_device, mesh=mesh, in_specs=in_specs, out_specs=out_specs, check_vma=False
    )
```

```python
import jax
import jax.numpy as jnp
from jax import lax
from jax.experimental import pallas as pl
from jax.experimental.pallas import tpu as pltpu
from jax.sharding import PartitionSpec as P

D = 768
H = 12
HD = 64
FF = 3072
NB = 32
L = 128
PAIRS = H // 2
SEQS = 2
PICKS = 32
ROWS = L + PICKS
EPSILON = 1e-05
SCALE = HD ** (-0.5)
TILE = 1536
LOW = jnp.bfloat16
WIDE = jnp.float32
HALF = FF // 2
QUARTER = D // 4
EARLY = 3 * D + HALF
LATE = D + HALF
SMALL = 16
ALL_ROWS = SEQS * ROWS
ALL_CONTENT = SEQS * L
PIECE = ALL_ROWS + ALL_CONTENT


def nn(former, latter):
    return lax.dot_general(
        former, latter, (((1,), (0,)), ((), ())), preferred_element_type=WIDE
    )


def nt(former, latter):
    return lax.dot_general(
        former, latter, (((1,), (1,)), ((), ())), preferred_element_type=WIDE
    )


def tn(former, latter):
    return lax.dot_general(
        former, latter, (((0,), (0,)), ((), ())), preferred_element_type=WIDE
    )


def halves(value):
    even = lax.broadcasted_iota(jnp.int32, value.shape, 1) < HD
    zero = jnp.zeros_like(value)
    return jnp.concatenate([jnp.where(even, value, zero), jnp.where(even, zero, value)])


def side(value):
    count = value.shape[0] // 2
    return jnp.concatenate([value[:count], value[count:]], axis=1)


def norm_rows(values):
    centered = values - jnp.mean(values, axis=-1, keepdims=True)
    variance = jnp.mean(centered * centered, axis=-1, keepdims=True)
    root = lax.rsqrt(variance + EPSILON)
    return (centered * root, root)


def norm_rows_back(scaled, normed, root):
    return root * (
        scaled
        - jnp.mean(scaled, axis=-1, keepdims=True)
        - normed * jnp.mean(scaled * normed, axis=-1, keepdims=True)
    )


B_QUERY, B_VALUE, B_OUT, GAIN1, SHIFT1, B_CONTRACT, GAIN2, SHIFT2 = range(8)
S_QUERY, S_VALUE, S_OUT, S_GAIN1, S_SHIFT1, S_EXPAND = range(6)
S_CONTRACT, S_GAIN2, S_SHIFT2, S_TABLE = 9, 10, 11, 12
LIMITS = (12, 16, 23, 32, 46, 64, 91)


def bucket_of(relative):
    distance = jnp.abs(relative)
    beyond = 8 + sum((distance >= limit).astype(jnp.int32) for limit in LIMITS)
    within = jnp.where(distance < 8, distance, beyond)
    return within + 16 * (relative > 0).astype(jnp.int32)


def forward(x, w, vec, b_expand, masks, s, keep):
    row = lambda k: vec[k : k + 1, :]
    s.query[...] = (nn(x[...], w.query[...]) + row(B_QUERY)).astype(LOW)
    s.key[...] = nn(x[:L], w.key[...]).astype(LOW)
    s.value[...] = (nn(x[:L], w.value[...]) + row(B_VALUE)).astype(LOW)
    for pair in range(PAIRS):
        lanes = slice(pair * 128, (pair + 1) * 128)
        scores = nt(halves(s.query[:, lanes]), s.key[:, lanes]) * SCALE + masks[pair]
        shifted = jnp.exp(scores - jnp.max(scores, axis=-1, keepdims=True))
        probs = (shifted / jnp.sum(shifted, axis=-1, keepdims=True)).astype(LOW)
        if keep:
            s.probs[pair] = probs
        s.mixed[:, lanes] = nn(side(probs), halves(s.value[:, lanes])).astype(LOW)
    total = x[...].astype(WIDE) + nn(s.mixed[...], w.out[...]) + row(B_OUT)
    normed, root = norm_rows(total)
    first = normed * row(GAIN1) + row(SHIFT1)
    s.first_low[...] = first.astype(LOW)
    s.total[...] = first + row(B_CONTRACT)
    if keep:
        s.normed1[...] = normed
        s.root1[...] = jnp.broadcast_to(root, (ROWS, 128))
    for tile in range(FF // TILE):
        tile = slice(tile * TILE, (tile + 1) * TILE)
        expanded = nn(s.first_low[...], w.expand[:, tile]) + b_expand[:, tile]
        cumulative = 0.5 * (1.0 + lax.erf(expanded * 0.7071067811865476))
        activated = (expanded * cumulative).astype(LOW)
        if keep:
            s.slope[:, tile] = (
                cumulative + expanded * jnp.exp(-0.5 * expanded * expanded) * 0.3989422804014327
            ).astype(LOW)
            s.activated[:, tile] = activated
        s.total[...] += nn(activated, w.contract[tile, :])
    normed, root = norm_rows(s.total[...])
    if keep:
        s.normed2[...] = normed
        s.root2[...] = jnp.broadcast_to(root, (ROWS, 128))
    s.out[...] = (normed * row(GAIN2) + row(SHIFT2)).astype(s.out.dtype)


def column_sum(value):
    return jnp.sum(value.astype(WIDE), axis=0, keepdims=True)


def back_second_norm(grad, vec, s, add=None):
    upper = grad.astype(WIDE)
    normed = s.normed2[...]
    lower = norm_rows_back(upper * vec[GAIN2 : GAIN2 + 1, :], normed, s.root2[:, :1])
    s.total[...] = lower
    s.branch[...] = lower.astype(LOW)
    if add is not None:
        add(S_GAIN2, column_sum(upper * normed))
        add(S_SHIFT2, column_sum(upper))
        add(S_CONTRACT, column_sum(lower.astype(LOW)))


def back_feed(w, vec, s, add=None):
    for tile in range(FF // TILE):
        tile = slice(tile * TILE, (tile + 1) * TILE)
        lower = (nt(s.branch[...], w.contract[tile, :]) * s.slope[:, tile].astype(WIDE)).astype(LOW)
        s.expanded[:, tile] = lower
        if add is not None:
            part = column_sum(lower)
            for column in range(TILE // D):
                add(
                    S_EXPAND + tile.start // D + column,
                    part[:, column * D : (column + 1) * D],
                )
        s.total[...] += nt(lower, w.expand[:, tile])
    upper = s.total[...]
    normed = s.normed1[...]
    lower = norm_rows_back(upper * vec[GAIN1 : GAIN1 + 1, :], normed, s.root1[:, :1])
    s.total[...] = lower
    s.attended[...] = lower.astype(LOW)
    if add is not None:
        add(S_GAIN1, column_sum(upper * normed))
        add(S_SHIFT1, column_sum(upper))
        add(S_OUT, column_sum(lower.astype(LOW)))


def back_attend(s, table=None):
    for pair in range(PAIRS):
        lanes = slice(pair * 128, (pair + 1) * 128)
        probs = s.probs[pair]
        below = halves(s.dmixed[:, lanes])
        dprobs = nt(below, s.value[:, lanes])
        s.dvalue[:, lanes] = tn(probs, below).astype(LOW)
        weight = probs.astype(WIDE)
        dscores = (
            weight * (dprobs - jnp.sum(weight * dprobs, axis=-1, keepdims=True))
        ).astype(LOW)
        s.dquery[:, lanes] = (nn(side(dscores), halves(s.key[:, lanes])) * SCALE).astype(LOW)
        s.dkey[:, lanes] = (tn(dscores, halves(s.query[:, lanes])) * SCALE).astype(LOW)
        if table is not None:
            table(pair, dscores)


class Names:
    def __init__(self, **named):
        self.__dict__.update(named)


MATRICES = ("query", "key", "value", "out", "expand", "contract")
MATRIX_SHAPES = {
    "query": (D, D),
    "key": (D, D),
    "value": (D, D),
    "out": (D, D),
    "expand": (D, FF),
    "contract": (FF, D),
}
MASK_SHAPE = (PAIRS, 2 * ROWS, L)
KEPT = {
    "query": ((ROWS, D), LOW),
    "key": ((L, D), LOW),
    "value": ((L, D), LOW),
    "probs": (MASK_SHAPE, LOW),
    "mixed": ((ROWS, D), LOW),
    "normed1": ((ROWS, D), WIDE),
    "root1": ((ROWS, 128), WIDE),
    "first_low": ((ROWS, D), LOW),
    "slope": ((ROWS, FF), LOW),
    "activated": ((ROWS, FF), LOW),
    "normed2": ((ROWS, D), WIDE),
    "root2": ((ROWS, 128), WIDE),
}
SAVED = tuple(name for name in KEPT if name != "mixed")
ANY = pl.BlockSpec(memory_space=pl.ANY)
HBM = pl.BlockSpec(memory_space=pltpu.HBM)
VMEM = pl.BlockSpec(memory_space=pltpu.VMEM)
SMEM = pl.BlockSpec(memory_space=pltpu.SMEM)


def limit(megabytes):
    return pltpu.CompilerParams(vmem_limit_bytes=megabytes * 1024 * 1024)


DMA = pltpu.SemaphoreType.DMA


def cost(microseconds):
    return pl.CostEstimate(flops=0, bytes_accessed=int(microseconds * 3.2e6), transcendentals=0)


def shaped(shape, kind):
    return jax.ShapeDtypeStruct(shape, kind)


TOKEN = shaped((8, 128), WIDE)


def columns(ref, start, size):
    return ref.at[:, pl.ds(pl.multiple_of(start, 128), size)]


def rows_at(ref, start, size):
    return ref.at[pl.ds(pl.multiple_of(start, 64), size)]


def start_all(pairs, sems, base=0):
    copies = [
        pltpu.make_async_copy(source, target, sems.at[base + index])
        for index, (source, target) in enumerate(pairs)
    ]
    for copy in copies:
        copy.start()
    return copies


def wait_all(copies):
    for copy in copies:
        copy.wait()


def fetcher(names, sources, targets, sems, base=0):
    copies = dict(zip(names, start_all(list(zip(sources, targets)), sems, base)))
    return lambda name: copies[name].wait()


def prepare(ranks, table, queries, picks, after):
    def kernel(ranks, table, queries, *refs):
        masks, spread, rows_in, rows_cot = refs[len(after) :]
        order, tag, pos = ranks[:, :L], ranks[:, L : 2 * L], ranks[:, 2 * L : 2 * L + picks]
        values = queries[...].astype(WIDE)
        blank = jnp.zeros((PICKS - picks, D), WIDE)
        for index, target in enumerate((rows_in, rows_cot)):
            own = values[2 * index * picks : 2 * (index + 1) * picks]
            target[...] = jnp.concatenate([own[:picks], blank, own[picks:], blank]).astype(LOW)
        lane = lax.broadcasted_iota(jnp.int32, (L, L), 1)
        level = lax.broadcasted_iota(jnp.int32, (L, L), 0)
        lane_q = lax.broadcasted_iota(jnp.int32, (PICKS, L), 1)
        upright = lambda row: jnp.sum(jnp.where(lane == level, row, 0.0), axis=1, keepdims=True)
        distance = lax.broadcasted_iota(jnp.int32, (2 * L, NB), 0) - (L - 1)
        bucket = lax.broadcasted_iota(jnp.int32, (2 * L, NB), 1)
        by_distance = lax.dot_general(
            table[...],
            (bucket_of(distance) == bucket).astype(WIDE),
            (((0,), (1,)), ((), ())),
            precision=lax.Precision.HIGHEST,
            preferred_element_type=WIDE,
        )
        allowed, hot = [], []
        for seq in range(SEQS):
            own_rank = order[seq : seq + 1, :].astype(WIDE)
            own_tag = tag[seq : seq + 1, :].astype(WIDE)
            own_pos = pos[seq : seq + 1, :].astype(WIDE)
            number = lax.broadcasted_iota(jnp.int32, (PICKS, picks), 0)
            same = number == lax.broadcasted_iota(jnp.int32, (PICKS, picks), 1)
            place = jnp.sum(jnp.where(same, own_pos, 0.0), axis=1, keepdims=True)
            filled = lax.broadcasted_iota(jnp.int32, (PICKS, 1), 0) < picks
            place = jnp.where(filled, place, -1.0).astype(jnp.int32)
            matches = place == lane_q
            marks = jnp.where(matches, 1.0, 0.0)
            predicted = jnp.max(marks, axis=0, keepdims=True)
            rank = jnp.sum(jnp.where(matches, own_rank, 0.0), axis=1, keepdims=True)
            group = jnp.sum(jnp.where(matches, own_tag, 0.0), axis=1, keepdims=True)
            earlier = (upright(predicted) > 0) & (own_rank <= upright(own_rank))
            content = (upright(own_tag) == own_tag) & ((predicted == 0) | earlier)
            query = (group == own_tag) & ((predicted == 0) | (own_rank + 1 <= rank))
            allowed.append((content, query))
            hot.append(marks)
            spread[seq, :L] = jnp.where(lane == L - 1 - level, 1.0, 0.0).astype(LOW)
            spread[seq, L:] = jnp.where(lane_q == L - 1 - place, 1.0, 0.0).astype(LOW)
        hot = jnp.concatenate(hot)
        for head in range(H):
            row = jnp.broadcast_to(by_distance[head : head + 1], (L, 2 * L))
            bias = pltpu.roll(row, L + 1, 1, stride=1, stride_axis=0)[:, :L]
            bias_q = lax.dot_general(
                hot,
                bias,
                (((1,), (0,)), ((), ())),
                precision=lax.Precision.HIGHEST,
                preferred_element_type=WIDE,
            )
            base = head % 2 * ROWS
            for seq in range(SEQS):
                content, query = allowed[seq]
                masks[seq, head // 2, base : base + L] = jnp.where(content, bias, -1e30)
                masks[seq, head // 2, base + L : base + ROWS] = jnp.where(
                    query, bias_q[seq * PICKS : (seq + 1) * PICKS], -1e30
                )

    return pl.pallas_call(
        kernel,
        out_shape=[
            shaped((SEQS,) + MASK_SHAPE, WIDE),
            shaped((SEQS, ROWS, L), LOW),
            shaped((SEQS * PICKS, D), LOW),
            shaped((SEQS * PICKS, D), LOW),
        ],
        in_specs=[VMEM] * 3 + [ANY] * len(after),
        out_specs=[VMEM] * 4,
        compiler_params=limit(8),
        cost_estimate=pl.CostEstimate(flops=int(3e10), bytes_accessed=0, transcendentals=0),
        name="prepare",
    )(ranks, table, queries, *after)


def take_rows(content, picks, seq, target):
    target[:L] = content[seq * L : (seq + 1) * L]
    target[L:] = picks[seq * PICKS : (seq + 1) * PICKS]


def front(seq, info, content, picks, matrices, masks, vec, b_expand, after=()):
    def kernel(info, content, picks, masks, vec, b_expand, *refs):
        w = Names(**dict(zip(MATRICES, refs[:6])))
        out, x, query, key, value, mixed, first_low, total = refs[6 + len(after) :]
        s = Names(
            query=query,
            key=key,
            value=value,
            mixed=mixed,
            first_low=first_low,
            total=total,
            out=out,
        )
        take_rows(content, picks, seq, x)
        forward(x, w, vec, b_expand, masks.at[seq], s, False)

    return pl.pallas_call(
        kernel,
        out_shape=shaped((ROWS, D), LOW),
        in_specs=[SMEM] + [VMEM] * 11 + [ANY] * len(after),
        out_specs=VMEM,
        scratch_shapes=[pltpu.VMEM((ROWS, D), LOW)]
        + [pltpu.VMEM(*KEPT[n]) for n in ("query", "key", "value", "mixed", "first_low")]
        + [pltpu.VMEM((ROWS, D), WIDE)],
        compiler_params=limit(12),
        cost_estimate=cost(5),
        name="front",
    )(info, content, picks, masks, vec, b_expand, *matrices, *after)


def middle_forward(seq, info, content, picks, arrived, matrices, masks, vec, b_expand, after=()):
    def kernel(info, arrived, content, picks, masks, vec, b_expand, *refs):
        w, rest = Names(**dict(zip(MATRICES, refs[:6]))), refs[6 + len(after) :]
        (out, early, pair), kept = rest[:3], rest[3 : 3 + len(SAVED)]
        mixed, total = rest[3 + len(SAVED) :]
        x = pair.at[0]
        s = Names(total=total, out=out, mixed=mixed, **dict(zip(SAVED, kept)))
        take_rows(content, picks, seq, x)
        x[...] = jnp.where(info[2] == 1, x[...], arrived[...])
        early[:, :D] = x[...]
        forward(x, w, vec, b_expand, masks.at[seq], s, True)
        pair[1] = mixed[...]
        early[:, D : 2 * D] = mixed[...]
        early[:, 2 * D : 3 * D] = s.first_low[...]
        early[:, 3 * D :] = columns(s.activated, (1 - info[0]) * HALF, HALF)[...]

    out, early, pair, *saved = pl.pallas_call(
        kernel,
        out_shape=[
            shaped((ROWS, D), WIDE),
            shaped((ROWS, EARLY), LOW),
            shaped((2, ROWS, D), LOW),
        ]
        + [shaped(*KEPT[n]) for n in SAVED],
        in_specs=[SMEM] + [VMEM] * 12 + [ANY] * len(after),
        out_specs=[VMEM] * (3 + len(SAVED)),
        scratch_shapes=[pltpu.VMEM(*KEPT["mixed"]), pltpu.VMEM((ROWS, D), WIDE)],
        compiler_params=limit(16),
        cost_estimate=cost(6),
        name="middle_forward",
    )(info, arrived, content, picks, masks, vec, b_expand, *matrices, *after)
    return (out, early, pair, dict(zip(SAVED, saved)))


FEED_SAVED = ("normed2", "root2", "slope", "normed1", "root1")
ATTEND_SAVED = ("value", "probs", "key", "query")


def middle_back(seq, content, picks, matrices, vec, saved):
    names = FEED_SAVED + ATTEND_SAVED

    def kernel(content, picks, vec, *refs):
        w, rest = Names(**dict(zip(MATRICES, refs[:6]))), refs[6:]
        kept, grad, rest = rest[: len(names)], rest[len(names)], rest[len(names) + 1 :]
        cot, total, branch, expanded, attended, dmixed, dvalue, dquery, dkey = rest
        s = Names(
            total=total,
            branch=branch,
            expanded=expanded,
            attended=attended,
            dmixed=dmixed,
            dvalue=dvalue,
            dquery=dquery,
            dkey=dkey,
            **dict(zip(names, kept)),
        )
        take_rows(content, picks, seq, cot)
        back_second_norm(cot[...], vec, s)
        back_feed(w, vec, s)
        dmixed[...] = nt(attended[...], w.out[...]).astype(LOW)
        back_attend(s)
        lower = total[...] + nt(dquery[...], w.query[...])
        upper = nt(dkey[...], w.key[...]) + nt(dvalue[...], w.value[...])
        grad[:L] = (lower[:L] + upper).astype(LOW)
        grad[L:] = lower[L:].astype(LOW)

    return pl.pallas_call(
        kernel,
        out_shape=shaped((ROWS, D), LOW),
        in_specs=[VMEM] * (9 + len(names)),
        out_specs=VMEM,
        scratch_shapes=[
            pltpu.VMEM((ROWS, D), LOW),
            pltpu.VMEM((ROWS, D), WIDE),
            pltpu.VMEM((ROWS, D), LOW),
            pltpu.VMEM((ROWS, FF), LOW),
            pltpu.VMEM((ROWS, D), LOW),
            pltpu.VMEM((ROWS, D), LOW),
            pltpu.VMEM((L, D), LOW),
            pltpu.VMEM((ROWS, D), LOW),
            pltpu.VMEM((L, D), LOW),
        ],
        compiler_params=limit(12),
        cost_estimate=cost(7),
        name="middle_back",
    )(content, picks, vec, *matrices, *(saved[n] for n in names))


def feed_back(seq, info, arrived, content, picks, small_in, vec, matrices, saved, after=()):
    given = [] if small_in is None else [small_in]

    def kernel(info, arrived, content, picks, vec, expand, contract, *refs):
        kept, rest = refs[:5], refs[5 + len(given) + len(after) :]
        total, branch, attended, small, own, late, upper, expanded = rest
        w = Names(expand=expand, contract=contract)
        s = Names(
            total=total,
            branch=branch,
            attended=attended,
            expanded=expanded,
            **dict(zip(FEED_SAVED, kept)),
        )
        small[...] = refs[5][...] if given else jnp.zeros_like(small)

        def add(place, value):
            small[place : place + 1, :] += value

        take_rows(content, picks, seq, upper)
        back_second_norm(jnp.where(info[2] == 1, arrived[...], upper[...]), vec, s, add)
        late[:, :D] = branch[...]
        back_feed(w, vec, s, add)
        own[...] = columns(expanded, info[0] * HALF, HALF)[...]
        late[:, D:] = columns(expanded, (1 - info[0]) * HALF, HALF)[...]

    return pl.pallas_call(
        kernel,
        out_shape=[
            shaped((ROWS, D), WIDE),
            shaped((ROWS, D), LOW),
            shaped((ROWS, D), LOW),
            shaped((SMALL, D), WIDE),
            shaped((ROWS, HALF), LOW),
            shaped((ROWS, LATE), LOW),
        ],
        in_specs=[SMEM] + [VMEM] * (11 + len(given)) + [ANY] * len(after),
        out_specs=[VMEM] * 6,
        scratch_shapes=[pltpu.VMEM((ROWS, D), LOW), pltpu.VMEM((ROWS, FF), LOW)],
        compiler_params=limit(12),
        cost_estimate=cost(4),
        name="feed_back",
    )(
        info,
        arrived,
        content,
        picks,
        vec,
        matrices[4],
        matrices[5],
        *(saved[n] for n in FEED_SAVED),
        *given,
        *after,
    )


PLACES = {
    (2, 0): (0, 0),
    (1, 1): (0, 1),
    (2, 1): (1, 0),
    (3, 0): (1, 1),
    (1, 0): (2, 0),
    (3, 1): (3, 0),
    (0, 0): (4, 0),
    (0, 1): (4, 1),
}


def term_shapes(count, extra=0):
    rows = (2 * count + extra, 2 * count + extra, count, count, 2 * count)
    return [shaped((n, D), LOW) for n in rows]


def feed_grads(info, mine, branch, own, early, late, after=()):
    def kernel(info, *refs):
        acts, lows, branches, owns, earlies, lates = (refs[2 * i : 2 * i + 2] for i in range(6))
        refs = refs[:12] + refs[12 + len(after) :]
        outs, (a_act, a_first, b_branch, b_own, stage, out_sems) = refs[12:17], refs[17:]
        core, place = info[0], info[1]
        own_at = [slice(seq * ROWS, (seq + 1) * ROWS) for seq in range(SEQS)]
        far_at = [slice((2 + seq) * ROWS, (3 + seq) * ROWS) for seq in range(SEQS)]
        for seq in range(SEQS):
            at, far = own_at[seq], far_at[seq]
            a_act[at] = columns(acts[seq], core * HALF, HALF)[...]
            a_act[far] = earlies[seq][:, 3 * D :]
            b_branch[at] = branches[seq][...]
            b_branch[far] = lates[seq][:, :D]
        sent = []

        def send(block):
            for k in range(4):
                quarter = lax.rem(place + k, 4)
                index, part = PLACES[k, block // 2]
                start = (2 * part + block % 2) * QUARTER
                sent.extend(
                    start_all(
                        [
                            (
                                rows_at(stage.at[block], quarter * QUARTER, QUARTER),
                                outs[index].at[start : start + QUARTER],
                            )
                        ],
                        out_sems,
                        block * 4 + k,
                    )
                )

        for block in range(2):
            for part in range(3):
                start = block * D + part * 256
                stage[block, part * 256 : (part + 1) * 256] = tn(
                    a_act[:, start : start + 256], b_branch[...]
                ).astype(LOW)
            send(block)
        for seq in range(SEQS):
            at, far = own_at[seq], far_at[seq]
            a_first[at] = lows[seq][...]
            a_first[far] = earlies[seq][:, 2 * D : 3 * D]
            b_own[at] = owns[seq][...]
            b_own[far] = lates[seq][:, D:]
        for block in range(2):
            for part in range(3):
                stage[2 + block, part * 256 : (part + 1) * 256] = tn(
                    a_first[:, part * 256 : (part + 1) * 256], b_own[:, block * D : (block + 1) * D]
                ).astype(LOW)
            send(2 + block)
        wait_all(sent)

    acts = [saved["activated"] for saved in mine]
    lows = [saved["first_low"] for saved in mine]
    return pl.pallas_call(
        kernel,
        out_shape=term_shapes(2 * QUARTER),
        in_specs=[SMEM] + [VMEM] * 12 + [ANY] * len(after),
        out_specs=[ANY] * 5,
        scratch_shapes=[
            pltpu.VMEM((2 * ALL_ROWS, HALF), LOW),
            pltpu.VMEM((2 * ALL_ROWS, D), LOW),
            pltpu.VMEM((2 * ALL_ROWS, D), LOW),
            pltpu.VMEM((2 * ALL_ROWS, HALF), LOW),
            pltpu.VMEM((4, D, D), LOW),
            DMA((16,)),
        ],
        compiler_params=limit(16),
        cost_estimate=cost(8),
        name="feed_grads",
    )(info, *acts, *lows, *branch, *own, *early, *late, *after)


def attend_back(seq, info, attended, small_in, spread, after, w_out, saved):
    def kernel(info, attended, small_in, spread, w_out, *refs):
        kept, (pieces, send, small, dmixed, sums) = refs[:4], refs[4 + len(after) :]
        small[...] = small_in[...]
        pieces[1, :ROWS] = attended[...]
        dmixed[...] = nt(attended[...], w_out[...]).astype(LOW)
        s = Names(
            dmixed=dmixed,
            dquery=pieces.at[0, :ROWS],
            dkey=pieces.at[0, ROWS:],
            dvalue=pieces.at[1, ROWS:],
            **dict(zip(ATTEND_SAVED, kept)),
        )
        sums[...] = jnp.zeros_like(sums)

        def table_sum(pair, dscores):
            for odd in range(2):
                part = tn(spread[seq], dscores[odd * ROWS : (odd + 1) * ROWS])
                both = jnp.concatenate([part, jnp.zeros((L, L), WIDE)], axis=1)
                turned = pltpu.roll(both, 0, 1, stride=1, stride_axis=0)
                head = 2 * pair + odd
                sums[head : head + 1, :] = jnp.sum(turned, axis=0, keepdims=True)

        back_attend(s, table_sum)
        send[: ROWS + L] = pieces[1 - info[0]]
        small[S_QUERY : S_QUERY + 1, :] += column_sum(pieces[0, :ROWS])
        small[S_VALUE : S_VALUE + 1, :] += column_sum(pieces[1, ROWS:])
        distance = lax.broadcasted_iota(jnp.int32, (2 * L, L), 0) - (L - 1)
        bucket = lax.broadcasted_iota(jnp.int32, (2 * L, L), 1)
        table = lax.dot_general(
            sums[...],
            (bucket_of(distance) == bucket).astype(WIDE),
            (((1,), (0,)), ((), ())),
            precision=lax.Precision.HIGHEST,
            preferred_element_type=WIDE,
        )
        for column in range(H // 4):
            lanes = slice(column * L, (column + 1) * L)
            small[S_TABLE : S_TABLE + 4, lanes] += table[4 * column : 4 * column + 4]
        send[ROWS + L :] = small[...].astype(LOW)

    return pl.pallas_call(
        kernel,
        out_shape=[
            shaped((2, ROWS + L, D), LOW),
            shaped((ROWS + L + SMALL, D), LOW),
            shaped((SMALL, D), WIDE),
        ],
        in_specs=[SMEM] + [VMEM] * 8 + [ANY] * len(after),
        out_specs=[VMEM] * 3,
        scratch_shapes=[pltpu.VMEM((ROWS, D), LOW), pltpu.VMEM((16, 2 * L), WIDE)],
        compiler_params=limit(12),
        cost_estimate=cost(4),
        name="attend_back",
    )(info, attended, small_in, spread, w_out, *(saved[n] for n in ATTEND_SAVED), *after)


def finish_rows(info, total, output, pieces, matrices, picks, after):
    def kernel(info, *refs):
        totals, outputs, pieces = refs[0:2], refs[2:4], refs[4:6]
        (query, key, value), refs = refs[6:9], refs[9 + len(after) :]
        content_ends, query_out, done, query_ends, sem = refs
        done[...] = jnp.zeros_like(done)
        first = info[2] == 1
        for seq in range(SEQS):
            lower = totals[seq][...] + nt(pieces[seq][0, :ROWS], query[...])
            upper = nt(pieces[seq][0, ROWS:], key[...]) + nt(pieces[seq][1, ROWS:], value[...])
            content_ends[seq * L : (seq + 1) * L] = jnp.where(
                first, lower[:L] + upper, outputs[seq][:L]
            )
            query_ends[seq * picks : (seq + 1) * picks] = jnp.where(
                first, lower[L : L + picks], outputs[seq][L : L + picks]
            )
        copy = pltpu.make_async_copy(query_ends, query_out, sem)
        copy.start()
        copy.wait()

    return pl.pallas_call(
        kernel,
        out_shape=[shaped((ALL_CONTENT, D), WIDE), shaped((SEQS * picks, D), WIDE), TOKEN],
        in_specs=[SMEM] + [VMEM] * 9 + [ANY] * len(after),
        out_specs=[VMEM, HBM, VMEM],
        scratch_shapes=[pltpu.VMEM((SEQS * picks, D), WIDE), DMA],
        compiler_params=limit(12),
        cost_estimate=cost(3),
        name="finish_rows",
    )(info, *total, *output, *pieces, *matrices[:3], *after)


def attend_grads(info, pair, early, mine, arrived, small, after=()):
    def kernel(info, small, *refs):
        pairs_in, earlies, mines, arriveds = (refs[2 * i : 2 * i + 2] for i in range(4))
        refs = refs[8 + len(after) :]
        outs, extra, rest = refs[:5], refs[5], refs[6:]
        a_rows, a_content, b_rows, b_content, stage, out_sems = rest
        core, place = info[0], info[1]
        for seq in range(SEQS):
            at = slice(seq * ROWS, (seq + 1) * ROWS)
            far = slice((2 + seq) * ROWS, (3 + seq) * ROWS)
            a_rows[at] = pairs_in[seq][core]
            a_rows[far] = columns(earlies[seq], core * D, D)[...]
            b_rows[at] = mines[seq][core, :ROWS]
            b_rows[far] = arriveds[seq][:ROWS]
            at = slice(seq * L, (seq + 1) * L)
            far = slice((2 + seq) * L, (3 + seq) * L)
            a_content[at] = pairs_in[seq][0, :L]
            a_content[far] = earlies[seq][:L, :D]
            b_content[at] = mines[seq][core, ROWS:]
            b_content[far] = arriveds[seq][ROWS : ROWS + L]
        far_small = arriveds[1][ROWS + L :]
        extra[...] = (small[...] + far_small.astype(WIDE)).astype(LOW)
        sent = start_all([(extra, outs[i].at[2 * QUARTER :]) for i in range(2)], out_sems, 8)
        for block, (former, latter) in enumerate(((a_rows, b_rows), (a_content, b_content))):
            for part in range(3):
                stage[block, part * 256 : (part + 1) * 256] = tn(
                    former[:, part * 256 : (part + 1) * 256], latter[...]
                ).astype(LOW)
            for k in range(4):
                quarter = lax.rem(place + k, 4)
                index, part = PLACES[k, block]
                start = part * QUARTER
                sent += start_all(
                    [
                        (
                            rows_at(stage.at[block], quarter * QUARTER, QUARTER),
                            outs[index].at[start : start + QUARTER],
                        )
                    ],
                    out_sems,
                    block * 4 + k,
                )
        wait_all(sent)

    return pl.pallas_call(
        kernel,
        out_shape=term_shapes(QUARTER, SMALL) + [shaped((SMALL, D), LOW)],
        in_specs=[SMEM] + [VMEM] * 9 + [ANY] * len(after),
        out_specs=[ANY] * 5 + [VMEM],
        scratch_shapes=[
            pltpu.VMEM((2 * ALL_ROWS, D), LOW),
            pltpu.VMEM((2 * ALL_CONTENT, D), LOW),
            pltpu.VMEM((2 * ALL_ROWS, D), LOW),
            pltpu.VMEM((2 * ALL_CONTENT, D), LOW),
            pltpu.VMEM((2, D, D), LOW),
            DMA((10,)),
        ],
        compiler_params=limit(12),
        cost_estimate=cost(5),
        name="attend_grads",
    )(info, small, *pair, *early, *mine, *arrived, *after)


def small_kernel(body, name, shapes, inputs, after=(), info=None, through=()):
    first = [] if info is None else [info]
    given = len(first) + len(inputs)

    def kernel(*refs):
        outs = refs[given + len(after) + len(through) :]
        body(*refs[:given], *outs[: len(shapes)])

    return pl.pallas_call(
        kernel,
        out_shape=[shaped(shape, LOW) for shape in shapes]
        + [shaped(array.shape, array.dtype) for array in through],
        in_specs=[SMEM] * len(first)
        + [VMEM] * len(inputs)
        + [ANY] * (len(after) + len(through)),
        out_specs=[VMEM] * len(shapes) + [ANY] * len(through),
        input_output_aliases={
            given + len(after) + i: len(shapes) + i for i in range(len(through))
        },
        compiler_params=limit(8),
        cost_estimate=cost(1),
        name=name,
    )(*first, *inputs, *after, *through)


def total_of(*terms):
    return sum(term.astype(WIDE) for term in terms).astype(LOW)


def ring_add(after0, before1, from_left, from_right, after=()):
    count = after0.shape[0]
    extra = from_left.shape[0] - 2 * count

    def body(after0, before1, from_left, from_right, right, left):
        right[:count] = total_of(after0[...], from_left[:count])
        left[:count] = total_of(before1[...], from_right[:count])
        if extra:
            right[count:] = from_left[2 * count :]
            left[count:] = from_right[2 * count :]

    return small_kernel(
        body,
        "ring_add",
        [(count + extra, D)] * 2,
        (after0, before1, from_left, from_right),
        after,
    )


def ring_sum(info, own, left, right, from_left, from_right, after=(), small=()):
    count = own.shape[0] // 2
    part = count // 4
    extra = sum(array.shape[0] for array in small)

    def body(info, own, left, right, from_left, from_right, *outs):
        if extra:
            small, outs = outs[0], outs[1:]
            total = total_of(
                small[...], from_left[2 * count :], from_right[2 * count :], left[count:]
            )
        for k, out in enumerate(outs):
            at = pl.multiple_of(lax.rem(info[3] + k, 4) * part, 16)
            low, high = pl.ds(at, part), pl.ds(at + count, part)
            out[:part] = total_of(own[low], left[low], from_right[high])
            out[part : 2 * part] = total_of(own[high], from_left[high], right[low])
            if extra:
                out[2 * part :] = total

    return small_kernel(
        body,
        "ring_sum",
        [(2 * part + extra, D)] * 4,
        (own, left, right, from_left, from_right, *small),
        after,
        info,
    )


def add_all(name, terms, after=()):
    def body(*refs):
        refs[-1][...] = total_of(*(ref[...] for ref in refs[:-1]))

    return small_kernel(body, name, [terms[0].shape], terms, after)[0]


def hand_on(arrays, after):
    return small_kernel(lambda *refs: None, "hand_on", [], (), after, None, arrays)


def z_join(feed, feed_far, attend, attend_far):
    first = feed.shape[0]
    count = attend.shape[0] - SMALL

    def body(feed, feed_far, attend, attend_far, whole, small, table):
        whole[:first] = total_of(feed[...], feed_far[...])
        total = total_of(attend[...], attend_far[...])
        whole[first:] = total[:count]
        small[...] = total[count : count + S_TABLE]
        table[...] = total[count + S_TABLE :]

    shapes = [(first + count, D), (S_TABLE, D), (SMALL - S_TABLE, D)]
    return small_kernel(body, "z_join", shapes, (feed, feed_far, attend, attend_far))


def finish_small(small, table, far, after=()):
    places = [n for n in range(S_TABLE) if not S_EXPAND <= n < S_EXPAND + 4]

    def kernel(small, table, far, *refs):
        vectors, (b_expand, whole, done) = refs[len(after) : -3], refs[-3:]
        done[...] = jnp.zeros_like(done)
        values = small[...].astype(WIDE)
        for place, vector in zip(places, vectors):
            vector[...] = values[place : place + 1]
        for column in range(4):
            lanes = slice(column * D, (column + 1) * D)
            b_expand[:, lanes] = values[S_EXPAND + column : S_EXPAND + column + 1]
        total = table[...].astype(WIDE) + far[...].astype(WIDE)
        heads = [total[:, column * L : (column + 1) * L] for column in range(4)]
        whole[...] = jnp.concatenate(heads).T[:NB, :H]

    *vectors, b_expand, whole, done = pl.pallas_call(
        kernel,
        out_shape=[shaped((1, D), WIDE)] * len(places)
        + [shaped((1, FF), WIDE), shaped((NB, H), WIDE), TOKEN],
        in_specs=[VMEM] * 3 + [ANY] * len(after),
        out_specs=[VMEM] * (len(places) + 3),
        compiler_params=limit(4),
        cost_estimate=cost(1),
        name="finish_small",
    )(small, table, far, *after)
    return dict(zip(places, vectors)), b_expand, whole, done


def inner_join(info, parts):
    counts = (QUARTER // 2, QUARTER // 4)
    half = 4 * sum(counts)

    def body(info, *refs):
        refs, halves_out = refs[:-2], refs[-2:]
        start, given = 0, 0
        for count in counts:
            for k, ref in enumerate(refs):
                at = pl.ds(pl.multiple_of(lax.rem(info[3] + k, 4) * count, 16) + start, count)
                for out in halves_out:
                    out[at] = ref[given : given + count]
                    given += count
                given -= 2 * count
            start, given = start + 4 * count, given + 2 * count

    return small_kernel(body, "inner_join", [(half, D)] * 2, parts, (), info)


OUT_SHAPES = ((FF, D), (D, FF)) + ((D, D),) * 4


def out_places(outs, source, half, core, quarter):
    pairs = []
    for block in range(2):
        part = source.at[block * QUARTER : (block + 1) * QUARTER]
        if half == 0:
            target = rows_at(outs[0], core * HALF + block * D + quarter * QUARTER, QUARTER)
        else:
            target = columns(
                rows_at(outs[1], quarter * QUARTER, QUARTER), (core * 2 + block) * D, D
            )
        pairs.append((None, part, target))
    part = source.at[2 * QUARTER :]
    for number in range(2):
        target = rows_at(outs[2 + 2 * number + half], quarter * QUARTER, QUARTER)
        pairs.append((core == number, part, target))
    return pairs


def settle(info, pieces, outs, name, after=()):
    shapes = OUT_SHAPES
    keys = tuple(pieces)
    arrays = [pieces[key] for key in keys]
    given = list(after) + list(outs or ())

    def kernel(info, *refs):
        parts, rest = refs[: len(keys)], refs[len(keys) + len(given) :]
        outs, rest = rest[: len(shapes)], rest[len(shapes) :]
        done, rest = rest[0], rest[1:]
        done[...] = jnp.zeros_like(done)
        wide_held, out_sems = rest[:-1], rest[-1]
        finish = []
        for index, (sibling, k, half) in enumerate(keys):
            core = 1 - info[0] if sibling else info[0]
            quarter = lax.rem((info[3] if sibling else info[1]) + k, 4)
            source = wide_held[index]
            source[...] = parts[index][...].astype(WIDE)
            for place, (condition, part, target) in enumerate(
                out_places(outs, source, half, core, quarter)
            ):
                copy = pltpu.make_async_copy(part, target, out_sems.at[4 * index + place])
                if condition is None:
                    copy.start()
                    finish.append(copy.wait)
                else:
                    pl.when(condition)(copy.start)
                    finish.append(lambda c=copy, when=condition: pl.when(when)(c.wait))
        for action in finish:
            action()

    result = pl.pallas_call(
        kernel,
        out_shape=[shaped(shape, WIDE) for shape in shapes]
        + [TOKEN],
        in_specs=[SMEM] + [VMEM] * len(keys) + [ANY] * len(given),
        out_specs=[ANY] * len(shapes) + [VMEM],
        scratch_shapes=[pltpu.VMEM(array.shape, WIDE) for array in arrays]
        + [DMA((4 * len(keys),))],
        input_output_aliases={
            1 + len(keys) + len(after) + i: i for i in range(len(outs or ()))
        },
        compiler_params=limit(20),
        cost_estimate=cost(sum(array.size for array in arrays) * 2e-6 + 1),
        name=name,
    )(info, *arrays, *given)
    return result[:-1], result[-1]


PLANE = ("x", "y", "c")


def shift(value, axis, by):
    size = lax.axis_size(axis)
    return lax.ppermute(value, axis, [(i, (i + by) % size) for i in range(size)])


def send(value, by):
    return lax.ppermute(value, "s", [(0, 1)] if by > 0 else [(1, 0)])


def turn(value, outer, by):
    pairs = []
    for i in range(4):
        for j in range(4):
            for c in range(2):
                if (c == 0) == outer:
                    target = ((i + by) % 4, j)
                else:
                    target = (i, (j + by) % 4)
                pairs.append(((i * 4 + j) * 2 + c, (target[0] * 4 + target[1]) * 2 + c))
    return lax.ppermute(value, PLANE, pairs)


def place(outer):
    return jnp.where(
        (lax.axis_index("c") == 0) == outer, lax.axis_index("x"), lax.axis_index("y")
    )


def wide(value):
    return value.astype(WIDE)


def total_wide(*terms):
    return sum(wide(term) for term in terms)


def inner_turns(parts, sign):
    return [turn(part, False, sign * by) for part, by in zip(parts, (1, 2, -1))]


def other_core(pieces):
    return {(1,) + key[1:]: shift(piece, "c", 1) for key, piece in pieces.items()}


def on_device(
    content_in,
    query_in,
    content_cot,
    query_cot,
    order_rank,
    query_pos,
    group_tag,
    *rest,
):
    (
        w_query,
        b_query,
        w_key,
        w_value,
        b_value,
        w_out,
        b_out,
        norm1_gain,
        norm1_bias,
        w_expand,
        b_expand,
        w_contract,
        b_contract,
        norm2_gain,
        norm2_bias,
    ) = (argument[0] for argument in rest[:-1])
    rel_table = rest[-1]
    core = lax.axis_index("c")
    first_section = (lax.axis_index("s") == 0).astype(jnp.int32)
    info = jnp.stack([core, place(True), first_section, place(False)])
    picks = query_pos.shape[1]

    matrices = (w_query, w_key, w_value, w_out, w_expand, w_contract)
    w_out_held = w_out
    vec = jnp.stack(
        [b_query, b_value, b_out, norm1_gain, norm1_bias, b_contract, norm2_gain, norm2_bias]
    )
    ranks = jnp.concatenate([order_rank, group_tag, query_pos], axis=1)
    masks, spread, query_in, query_cot = prepare(
        ranks, rel_table, jnp.concatenate([query_in, query_cot]), picks, (vec, info)
    )
    b_expand = b_expand[None]

    fronts, arrived = [], []
    for seq in range(SEQS):
        fronts.append(
            front(seq, info, content_in, query_in, matrices, masks, vec, b_expand, tuple(fronts))
        )
        arrived.append(send(fronts[seq], 1))
    output, early, pair, saved, grads = [], [], [], [], []
    for seq in range(SEQS):
        results = middle_forward(
            seq, info, content_in, query_in, arrived[seq], matrices, masks, vec, b_expand, tuple(grads)
        )
        for collected, result in zip((output, early, pair, saved), results):
            collected.append(result)
        grads.append(middle_back(seq, content_cot, query_cot, matrices, vec, saved[seq]))
    early = [shift(value, "c", 1) for value in early]
    grads = [send(value, -1) for value in grads]
    small = None
    total, branch, attended, own, late, pieces, pass_on = [], [], [], [], [], [], []
    for seq in range(SEQS):
        results = feed_back(
            seq,
            info,
            grads[seq],
            content_cot,
            query_cot,
            small,
            vec,
            matrices,
            saved[seq],
            tuple(pass_on),
        )
        small = results[3]
        for collected, result in zip(
            (total, branch, attended, own, late), results[:3] + results[4:]
        ):
            collected.append(result)
        late[seq] = shift(late[seq], "c", 1)
        results = attend_back(
            seq,
            info,
            attended[seq],
            small,
            spread,
            (),
            w_out_held,
            saved[seq],
        )
        small = results[2]
        pieces.append(results[0])
        pass_on.append(results[1])
    feed_terms = feed_grads(info, saved, branch, own, early, late, (small,))
    passed = [shift(value, "c", 1) for value in pass_on]

    def outer_step(terms):
        return (turn(terms[0], True, 1), turn(terms[1], True, -1))

    f_left, f_right = outer_step(feed_terms)
    *attend_terms, extra = attend_grads(info, pair, early, pieces, passed, small, (feed_terms[4],))
    a_left, a_right = outer_step(attend_terms)
    f_sent = ring_add(feed_terms[2], feed_terms[3], f_left, f_right, (extra,))
    f_outer = outer_step(f_sent)
    a_sent = ring_add(attend_terms[2], attend_terms[3], a_left, a_right)
    f_parts = ring_sum(info, feed_terms[4], *f_outer, f_left, f_right, (a_sent[0],))
    f_others = inner_turns(f_parts[1:], 1)
    a_parts = ring_sum(
        info, attend_terms[4], *outer_step(a_sent), a_left, a_right, (f_parts[0],), (extra,)
    )
    f_part = add_all("inner_sum", [f_parts[0]] + f_others, (a_parts[0],))
    f_far = shift(f_part, "z", 1)
    a_part = add_all("inner_sum", [a_parts[0]] + inner_turns(a_parts[1:], 1), (f_part,))
    a_far = shift(a_part, "z", 1)
    part, small, table = z_join(f_part, f_far, a_part, a_far)
    own0, own1 = inner_join(info, [part] + inner_turns([part] * 3, -1))
    first = (turn(own0, True, 1), turn(own1, True, -1))
    content_ends, query_ends, token = finish_rows(
        info, total, output, pieces, matrices, picks, (own0,)
    )
    row, b_expand, table, small_token = finish_small(small, table, shift(table, "s", 1), (own0,))
    own = {(0, 0, 0): own0, (0, 0, 1): own1}
    outs, own_token = settle(info, own | other_core(own), None, "own_out")
    *first, own0, own1 = hand_on((*first, own0, own1), (token, small_token, own_token))
    across = (turn(first[0], True, 1), turn(first[1], True, -1))
    second = (turn(own1, True, 1), turn(own0, True, -1))
    near = {(0, 3, 0): first[0], (0, 1, 1): first[1]}
    outs, token = settle(info, near | other_core(near), outs, "near_out")
    last = hand_on((*second, *across), (token,))
    last = dict(zip(((0, 3, 1), (0, 1, 0), (0, 2, 0), (0, 2, 1)), last))
    outs, _ = settle(info, last, outs, "last_out")
    outs, _ = settle(info, other_core(last), outs, "last_out")
    contract, expand, g_query, g_key, g_out, g_value = outs
    return (
        content_ends[None],
        query_ends[None],
        g_query[None],
        row[S_QUERY],
        g_key[None],
        g_value[None],
        row[S_VALUE],
        g_out[None],
        row[S_OUT],
        row[S_GAIN1],
        row[S_SHIFT1],
        expand[None],
        b_expand,
        contract[None],
        row[S_CONTRACT],
        row[S_GAIN2],
        row[S_SHIFT2],
        table,
    )


DP = ("z", "x", "y", "c")


def solution(mesh):
    mesh = jax.sharding.Mesh(mesh.devices.reshape(2, 2, 4, 4, 2), ("s",) + DP)
    layer_specs = tuple(
        P("s", *([None] * (rank - 1))) for rank in (3, 2, 3, 3, 2, 3, 2, 2, 2, 3, 2, 3, 2, 2, 2)
    )
    in_specs = (P(DP, None),) * 7 + layer_specs + (P(),)
    out_specs = (P("s", DP, None),) * 2 + layer_specs + (P(),)
    return jax.shard_map(
        on_device, mesh=mesh, in_specs=in_specs, out_specs=out_specs, check_vma=False
    )
```

```python
import jax
import jax.numpy as jnp
from jax import lax
from jax.experimental import pallas as pl
from jax.experimental.pallas import tpu as pltpu
from jax.sharding import PartitionSpec as P

D = 768
H = 12
HD = 64
FF = 3072
NB = 32
L = 128
PAIRS = H // 2
SEQS = 2
PICKS = 32
ROWS = L + PICKS
EPSILON = 1e-05
SCALE = HD ** (-0.5)
TILE = 1536
LOW = jnp.bfloat16
WIDE = jnp.float32
HALF = FF // 2
QUARTER = D // 4
EARLY = 3 * D + HALF
LATE = D + HALF
SMALL = 16
ALL_ROWS = SEQS * ROWS
ALL_CONTENT = SEQS * L
PIECE = ALL_ROWS + ALL_CONTENT


def nn(former, latter):
    return lax.dot_general(
        former, latter, (((1,), (0,)), ((), ())), preferred_element_type=WIDE
    )


def nt(former, latter):
    return lax.dot_general(
        former, latter, (((1,), (1,)), ((), ())), preferred_element_type=WIDE
    )


def tn(former, latter):
    return lax.dot_general(
        former, latter, (((0,), (0,)), ((), ())), preferred_element_type=WIDE
    )


def halves(value):
    even = lax.broadcasted_iota(jnp.int32, value.shape, 1) < HD
    zero = jnp.zeros_like(value)
    return jnp.concatenate([jnp.where(even, value, zero), jnp.where(even, zero, value)])


def side(value):
    count = value.shape[0] // 2
    return jnp.concatenate([value[:count], value[count:]], axis=1)


def norm_rows(values):
    centered = values - jnp.mean(values, axis=-1, keepdims=True)
    variance = jnp.mean(centered * centered, axis=-1, keepdims=True)
    root = lax.rsqrt(variance + EPSILON)
    return (centered * root, root)


def norm_rows_back(scaled, normed, root):
    return root * (
        scaled
        - jnp.mean(scaled, axis=-1, keepdims=True)
        - normed * jnp.mean(scaled * normed, axis=-1, keepdims=True)
    )


B_QUERY, B_VALUE, B_OUT, GAIN1, SHIFT1, B_CONTRACT, GAIN2, SHIFT2 = range(8)
S_QUERY, S_VALUE, S_OUT, S_GAIN1, S_SHIFT1, S_EXPAND = range(6)
S_CONTRACT, S_GAIN2, S_SHIFT2, S_TABLE = 9, 10, 11, 12
LIMITS = (12, 16, 23, 32, 46, 64, 91)


def bucket_of(relative):
    distance = jnp.abs(relative)
    beyond = 8 + sum((distance >= limit).astype(jnp.int32) for limit in LIMITS)
    within = jnp.where(distance < 8, distance, beyond)
    return within + 16 * (relative > 0).astype(jnp.int32)


def forward_attend(x, w, vec, masks, s, keep):
    row = lambda k: vec[k : k + 1, :]
    s.query[...] = (nn(x[...], w.query[...]) + row(B_QUERY)).astype(LOW)
    s.key[...] = nn(x[:L], w.key[...]).astype(LOW)
    s.value[...] = (nn(x[:L], w.value[...]) + row(B_VALUE)).astype(LOW)
    for pair in range(PAIRS):
        lanes = slice(pair * 128, (pair + 1) * 128)
        scores = nt(halves(s.query[:, lanes]), s.key[:, lanes]) * SCALE + masks[pair]
        shifted = jnp.exp(scores - jnp.max(scores, axis=-1, keepdims=True))
        probs = (shifted / jnp.sum(shifted, axis=-1, keepdims=True)).astype(LOW)
        if keep:
            s.probs[pair] = probs
        s.mixed[:, lanes] = nn(side(probs), halves(s.value[:, lanes])).astype(LOW)
    total = x[...].astype(WIDE) + nn(s.mixed[...], w.out[...]) + row(B_OUT)
    normed, root = norm_rows(total)
    first = normed * row(GAIN1) + row(SHIFT1)
    s.first_low[...] = first.astype(LOW)
    s.total[...] = first + row(B_CONTRACT)
    if keep:
        s.normed1[...] = normed
        s.root1[...] = jnp.broadcast_to(root, (ROWS, 128))


def forward_feed(w, vec, b_expand, s, keep):
    row = lambda k: vec[k : k + 1, :]
    for tile in range(FF // TILE):
        tile = slice(tile * TILE, (tile + 1) * TILE)
        expanded = nn(s.first_low[...], w.expand[:, tile]) + b_expand[:, tile]
        cumulative = 0.5 * (1.0 + lax.erf(expanded * 0.7071067811865476))
        activated = (expanded * cumulative).astype(LOW)
        if keep:
            s.slope[:, tile] = (
                cumulative + expanded * jnp.exp(-0.5 * expanded * expanded) * 0.3989422804014327
            ).astype(LOW)
            s.activated[:, tile] = activated
        s.total[...] += nn(activated, w.contract[tile, :])
    normed, root = norm_rows(s.total[...])
    if keep:
        s.normed2[...] = normed
        s.root2[...] = jnp.broadcast_to(root, (ROWS, 128))
    s.out[...] = (normed * row(GAIN2) + row(SHIFT2)).astype(s.out.dtype)


def column_sum(value):
    return jnp.sum(value.astype(WIDE), axis=0, keepdims=True)


def back_second_norm(grad, vec, s, add=None):
    upper = grad.astype(WIDE)
    normed = s.normed2[...]
    lower = norm_rows_back(upper * vec[GAIN2 : GAIN2 + 1, :], normed, s.root2[:, :1])
    s.total[...] = lower
    s.branch[...] = lower.astype(LOW)
    if add is not None:
        add(S_GAIN2, column_sum(upper * normed))
        add(S_SHIFT2, column_sum(upper))
        add(S_CONTRACT, column_sum(lower.astype(LOW)))


def back_feed(w, vec, s, add=None):
    for tile in range(FF // TILE):
        tile = slice(tile * TILE, (tile + 1) * TILE)
        lower = (nt(s.branch[...], w.contract[tile, :]) * s.slope[:, tile].astype(WIDE)).astype(LOW)
        s.expanded[:, tile] = lower
        if add is not None:
            part = column_sum(lower)
            for column in range(TILE // D):
                add(
                    S_EXPAND + tile.start // D + column,
                    part[:, column * D : (column + 1) * D],
                )
        s.total[...] += nt(lower, w.expand[:, tile])
    upper = s.total[...]
    normed = s.normed1[...]
    lower = norm_rows_back(upper * vec[GAIN1 : GAIN1 + 1, :], normed, s.root1[:, :1])
    s.total[...] = lower
    s.attended[...] = lower.astype(LOW)
    if add is not None:
        add(S_GAIN1, column_sum(upper * normed))
        add(S_SHIFT1, column_sum(upper))
        add(S_OUT, column_sum(lower.astype(LOW)))


def back_attend(s, table=None):
    for pair in range(PAIRS):
        lanes = slice(pair * 128, (pair + 1) * 128)
        probs = s.probs[pair]
        below = halves(s.dmixed[:, lanes])
        dprobs = nt(below, s.value[:, lanes])
        s.dvalue[:, lanes] = tn(probs, below).astype(LOW)
        weight = probs.astype(WIDE)
        dscores = (
            weight * (dprobs - jnp.sum(weight * dprobs, axis=-1, keepdims=True))
        ).astype(LOW)
        s.dquery[:, lanes] = (nn(side(dscores), halves(s.key[:, lanes])) * SCALE).astype(LOW)
        s.dkey[:, lanes] = (tn(dscores, halves(s.query[:, lanes])) * SCALE).astype(LOW)
        if table is not None:
            table(pair, dscores)


class Names:
    def __init__(self, **named):
        self.__dict__.update(named)


MATRICES = ("query", "key", "value", "out", "expand", "contract")
MATRIX_SHAPES = {
    "query": (D, D),
    "key": (D, D),
    "value": (D, D),
    "out": (D, D),
    "expand": (D, FF),
    "contract": (FF, D),
}
MASK_SHAPE = (PAIRS, 2 * ROWS, L)
KEPT = {
    "query": ((ROWS, D), LOW),
    "key": ((L, D), LOW),
    "value": ((L, D), LOW),
    "probs": (MASK_SHAPE, LOW),
    "mixed": ((ROWS, D), LOW),
    "normed1": ((ROWS, D), WIDE),
    "root1": ((ROWS, 128), WIDE),
    "first_low": ((ROWS, D), LOW),
    "slope": ((ROWS, FF), LOW),
    "activated": ((ROWS, FF), LOW),
    "normed2": ((ROWS, D), WIDE),
    "root2": ((ROWS, 128), WIDE),
}
SAVED = tuple(name for name in KEPT if name != "mixed")
ANY = pl.BlockSpec(memory_space=pl.ANY)
HBM = pl.BlockSpec(memory_space=pltpu.HBM)
VMEM = pl.BlockSpec(memory_space=pltpu.VMEM)
SMEM = pl.BlockSpec(memory_space=pltpu.SMEM)


def limit(megabytes):
    return pltpu.CompilerParams(vmem_limit_bytes=megabytes * 1024 * 1024)


DMA = pltpu.SemaphoreType.DMA


def cost(microseconds):
    return pl.CostEstimate(flops=0, bytes_accessed=int(microseconds * 3.2e6), transcendentals=0)


def shaped(shape, kind):
    return jax.ShapeDtypeStruct(shape, kind)


TOKEN = shaped((8, 128), WIDE)


def columns(ref, start, size):
    return ref.at[:, pl.ds(pl.multiple_of(start, 128), size)]


def rows_at(ref, start, size):
    return ref.at[pl.ds(pl.multiple_of(start, 64), size)]


def start_all(pairs, sems, base=0):
    copies = [
        pltpu.make_async_copy(source, target, sems.at[base + index])
        for index, (source, target) in enumerate(pairs)
    ]
    for copy in copies:
        copy.start()
    return copies


def wait_all(copies):
    for copy in copies:
        copy.wait()


def fetcher(names, sources, targets, sems, base=0):
    copies = dict(zip(names, start_all(list(zip(sources, targets)), sems, base)))
    return lambda name: copies[name].wait()


def prepare(ranks, table, queries, picks, after):
    def kernel(ranks, table, queries, *refs):
        masks, spread, rows_in, rows_cot = refs[len(after) :]
        order, tag, pos = ranks[:, :L], ranks[:, L : 2 * L], ranks[:, 2 * L : 2 * L + picks]
        values = queries[...].astype(WIDE)
        blank = jnp.zeros((PICKS - picks, D), WIDE)
        for index, target in enumerate((rows_in, rows_cot)):
            own = values[2 * index * picks : 2 * (index + 1) * picks]
            target[...] = jnp.concatenate([own[:picks], blank, own[picks:], blank]).astype(LOW)
        lane = lax.broadcasted_iota(jnp.int32, (L, L), 1)
        level = lax.broadcasted_iota(jnp.int32, (L, L), 0)
        lane_q = lax.broadcasted_iota(jnp.int32, (PICKS, L), 1)
        upright = lambda row: jnp.sum(jnp.where(lane == level, row, 0.0), axis=1, keepdims=True)
        distance = lax.broadcasted_iota(jnp.int32, (2 * L, NB), 0) - (L - 1)
        bucket = lax.broadcasted_iota(jnp.int32, (2 * L, NB), 1)
        by_distance = lax.dot_general(
            table[...],
            (bucket_of(distance) == bucket).astype(WIDE),
            (((1,), (1,)), ((), ())),
            precision=lax.Precision.HIGHEST,
            preferred_element_type=WIDE,
        )
        allowed, hot = [], []
        for seq in range(SEQS):
            own_rank = order[seq : seq + 1, :].astype(WIDE)
            own_tag = tag[seq : seq + 1, :].astype(WIDE)
            own_pos = pos[seq : seq + 1, :].astype(WIDE)
            number = lax.broadcasted_iota(jnp.int32, (PICKS, picks), 0)
            same = number == lax.broadcasted_iota(jnp.int32, (PICKS, picks), 1)
            place = jnp.sum(jnp.where(same, own_pos, 0.0), axis=1, keepdims=True)
            filled = lax.broadcasted_iota(jnp.int32, (PICKS, 1), 0) < picks
            place = jnp.where(filled, place, -1.0).astype(jnp.int32)
            matches = place == lane_q
            marks = jnp.where(matches, 1.0, 0.0)
            predicted = jnp.max(marks, axis=0, keepdims=True)
            rank = jnp.sum(jnp.where(matches, own_rank, 0.0), axis=1, keepdims=True)
            group = jnp.sum(jnp.where(matches, own_tag, 0.0), axis=1, keepdims=True)
            earlier = (upright(predicted) > 0) & (own_rank <= upright(own_rank))
            content = (upright(own_tag) == own_tag) & ((predicted == 0) | earlier)
            query = (group == own_tag) & ((predicted == 0) | (own_rank + 1 <= rank))
            allowed.append((content, query))
            hot.append(marks)
            spread[seq, :L] = jnp.where(lane == L - 1 - level, 1.0, 0.0).astype(LOW)
            spread[seq, L:] = jnp.where(lane_q == L - 1 - place, 1.0, 0.0).astype(LOW)
        hot = jnp.concatenate(hot)
        for head in range(H):
            row = jnp.broadcast_to(by_distance[head : head + 1], (L, 2 * L))
            bias = pltpu.roll(row, L + 1, 1, stride=1, stride_axis=0)[:, :L]
            bias_q = lax.dot_general(
                hot,
                bias,
                (((1,), (0,)), ((), ())),
                precision=lax.Precision.HIGHEST,
                preferred_element_type=WIDE,
            )
            base = head % 2 * ROWS
            for seq in range(SEQS):
                content, query = allowed[seq]
                masks[seq, head // 2, base : base + L] = jnp.where(content, bias, -1e30)
                masks[seq, head // 2, base + L : base + ROWS] = jnp.where(
                    query, bias_q[seq * PICKS : (seq + 1) * PICKS], -1e30
                )

    return pl.pallas_call(
        kernel,
        out_shape=[
            shaped((SEQS,) + MASK_SHAPE, WIDE),
            shaped((SEQS, ROWS, L), LOW),
            shaped((SEQS * PICKS, D), LOW),
            shaped((SEQS * PICKS, D), LOW),
        ],
        in_specs=[VMEM] * 3 + [ANY] * len(after),
        out_specs=[VMEM] * 4,
        compiler_params=limit(8),
        cost_estimate=pl.CostEstimate(flops=int(3e10), bytes_accessed=0, transcendentals=0),
        name="prepare",
    )(ranks, table, queries, *after)


def take_rows(content, picks, seq, target):
    target[:L] = content[seq * L : (seq + 1) * L]
    target[L:] = picks[seq * PICKS : (seq + 1) * PICKS]


def front(seq, info, content, picks, matrices, masks, vec, b_expand, after=()):
    def kernel(info, content, picks, masks, vec, b_expand, *refs):
        w = Names(**dict(zip(MATRICES, refs[:6])))
        out, x, query, key, value, mixed, first_low, total = refs[6 + len(after) :]
        s = Names(
            query=query,
            key=key,
            value=value,
            mixed=mixed,
            first_low=first_low,
            total=total,
            out=out,
        )
        take_rows(content, picks, seq, x)
        forward_attend(x, w, vec, masks.at[seq], s, False)
        forward_feed(w, vec, b_expand, s, False)

    return pl.pallas_call(
        kernel,
        out_shape=shaped((ROWS, D), LOW),
        in_specs=[SMEM] + [VMEM] * 11 + [ANY] * len(after),
        out_specs=VMEM,
        scratch_shapes=[pltpu.VMEM((ROWS, D), LOW)]
        + [pltpu.VMEM(*KEPT[n]) for n in ("query", "key", "value", "mixed", "first_low")]
        + [pltpu.VMEM((ROWS, D), WIDE)],
        compiler_params=limit(12),
        cost_estimate=cost(5),
        name="front",
    )(info, content, picks, masks, vec, b_expand, *matrices, *after)


def front_parts(seq, info, content, picks, matrices, masks, vec, b_expand):
    def first(info, content, picks, masks, vec, *refs):
        w = Names(**dict(zip(MATRICES[:4], refs[:4])))
        first_low, total, x, query, key, value, mixed = refs[4:]
        s = Names(
            query=query, key=key, value=value, mixed=mixed, first_low=first_low, total=total
        )
        take_rows(content, picks, seq, x)
        forward_attend(x, w, vec, masks.at[seq], s, False)

    def second(first_low, total_in, vec, b_expand, expand, contract, out, total):
        total[...] = total_in[...]
        s = Names(first_low=first_low, total=total, out=out)
        forward_feed(Names(expand=expand, contract=contract), vec, b_expand, s, False)

    first_low, total = pl.pallas_call(
        first,
        out_shape=[shaped((ROWS, D), LOW), shaped((ROWS, D), WIDE)],
        in_specs=[SMEM] + [VMEM] * 8,
        out_specs=[VMEM] * 2,
        scratch_shapes=[pltpu.VMEM((ROWS, D), LOW)]
        + [pltpu.VMEM(*KEPT[n]) for n in ("query", "key", "value", "mixed")],
        compiler_params=limit(8),
        cost_estimate=pl.CostEstimate(flops=int(1e10), bytes_accessed=0, transcendentals=0),
        name="front_attend",
    )(info, content, picks, masks, vec, *matrices[:4])
    return pl.pallas_call(
        second,
        out_shape=shaped((ROWS, D), LOW),
        in_specs=[VMEM] * 6,
        out_specs=VMEM,
        scratch_shapes=[pltpu.VMEM((ROWS, D), WIDE)],
        compiler_params=limit(12),
        cost_estimate=cost(2),
        name="front_feed",
    )(first_low, total, vec, b_expand, *matrices[4:])


def middle_forward(seq, info, content, picks, arrived, matrices, masks, vec, b_expand, after=()):
    def kernel(info, arrived, content, picks, masks, vec, b_expand, *refs):
        w, rest = Names(**dict(zip(MATRICES, refs[:6]))), refs[6 + len(after) :]
        (out, early, pair), kept = rest[:3], rest[3 : 3 + len(SAVED)]
        mixed, total = rest[3 + len(SAVED) :]
        x = pair.at[0]
        s = Names(total=total, out=out, mixed=mixed, **dict(zip(SAVED, kept)))
        take_rows(content, picks, seq, x)
        x[...] = jnp.where(info[2] == 1, x[...], arrived[...])
        early[:, :D] = x[...]
        forward_attend(x, w, vec, masks.at[seq], s, True)
        forward_feed(w, vec, b_expand, s, True)
        pair[1] = mixed[...]
        early[:, D : 2 * D] = mixed[...]
        early[:, 2 * D : 3 * D] = s.first_low[...]
        early[:, 3 * D :] = columns(s.activated, (1 - info[0]) * HALF, HALF)[...]

    out, early, pair, *saved = pl.pallas_call(
        kernel,
        out_shape=[
            shaped((ROWS, D), WIDE),
            shaped((ROWS, EARLY), LOW),
            shaped((2, ROWS, D), LOW),
        ]
        + [shaped(*KEPT[n]) for n in SAVED],
        in_specs=[SMEM] + [VMEM] * 12 + [ANY] * len(after),
        out_specs=[VMEM] * (3 + len(SAVED)),
        scratch_shapes=[pltpu.VMEM(*KEPT["mixed"]), pltpu.VMEM((ROWS, D), WIDE)],
        compiler_params=limit(16),
        cost_estimate=cost(6),
        name="middle_forward",
    )(info, arrived, content, picks, masks, vec, b_expand, *matrices, *after)
    return (out, early, pair, dict(zip(SAVED, saved)))


FEED_SAVED = ("normed2", "root2", "slope", "normed1", "root1")
ATTEND_SAVED = ("value", "probs", "key", "query")


def middle_back(seq, content, picks, matrices, vec, saved):
    names = FEED_SAVED + ATTEND_SAVED

    def kernel(content, picks, vec, *refs):
        w, rest = Names(**dict(zip(MATRICES, refs[:6]))), refs[6:]
        kept, grad, rest = rest[: len(names)], rest[len(names)], rest[len(names) + 1 :]
        cot, total, branch, expanded, attended, dmixed, dvalue, dquery, dkey = rest
        s = Names(
            total=total,
            branch=branch,
            expanded=expanded,
            attended=attended,
            dmixed=dmixed,
            dvalue=dvalue,
            dquery=dquery,
            dkey=dkey,
            **dict(zip(names, kept)),
        )
        take_rows(content, picks, seq, cot)
        back_second_norm(cot[...], vec, s)
        back_feed(w, vec, s)
        dmixed[...] = nt(attended[...], w.out[...]).astype(LOW)
        back_attend(s)
        lower = total[...] + nt(dquery[...], w.query[...])
        upper = nt(dkey[...], w.key[...]) + nt(dvalue[...], w.value[...])
        grad[:L] = (lower[:L] + upper).astype(LOW)
        grad[L:] = lower[L:].astype(LOW)

    return pl.pallas_call(
        kernel,
        out_shape=shaped((ROWS, D), LOW),
        in_specs=[VMEM] * (9 + len(names)),
        out_specs=VMEM,
        scratch_shapes=[
            pltpu.VMEM((ROWS, D), LOW),
            pltpu.VMEM((ROWS, D), WIDE),
            pltpu.VMEM((ROWS, D), LOW),
            pltpu.VMEM((ROWS, FF), LOW),
            pltpu.VMEM((ROWS, D), LOW),
            pltpu.VMEM((ROWS, D), LOW),
            pltpu.VMEM((L, D), LOW),
            pltpu.VMEM((ROWS, D), LOW),
            pltpu.VMEM((L, D), LOW),
        ],
        compiler_params=limit(12),
        cost_estimate=cost(7),
        name="middle_back",
    )(content, picks, vec, *matrices, *(saved[n] for n in names))


def feed_back(seq, info, arrived, content, picks, small_in, vec, matrices, saved, after=()):
    given = [] if small_in is None else [small_in]

    def kernel(info, arrived, content, picks, vec, expand, contract, *refs):
        kept, rest = refs[:5], refs[5 + len(given) + len(after) :]
        total, branch, attended, small, own, late, upper, expanded = rest
        w = Names(expand=expand, contract=contract)
        s = Names(
            total=total,
            branch=branch,
            attended=attended,
            expanded=expanded,
            **dict(zip(FEED_SAVED, kept)),
        )
        small[...] = refs[5][...] if given else jnp.zeros_like(small)

        def add(place, value):
            small[place : place + 1, :] += value

        take_rows(content, picks, seq, upper)
        back_second_norm(jnp.where(info[2] == 1, arrived[...], upper[...]), vec, s, add)
        late[:, :D] = branch[...]
        back_feed(w, vec, s, add)
        own[...] = columns(expanded, info[0] * HALF, HALF)[...]
        late[:, D:] = columns(expanded, (1 - info[0]) * HALF, HALF)[...]

    return pl.pallas_call(
        kernel,
        out_shape=[
            shaped((ROWS, D), WIDE),
            shaped((ROWS, D), LOW),
            shaped((ROWS, D), LOW),
            shaped((SMALL, D), WIDE),
            shaped((ROWS, HALF), LOW),
            shaped((ROWS, LATE), LOW),
        ],
        in_specs=[SMEM] + [VMEM] * (11 + len(given)) + [ANY] * len(after),
        out_specs=[VMEM] * 6,
        scratch_shapes=[pltpu.VMEM((ROWS, D), LOW), pltpu.VMEM((ROWS, FF), LOW)],
        compiler_params=limit(12),
        cost_estimate=cost(4),
        name="feed_back",
    )(
        info,
        arrived,
        content,
        picks,
        vec,
        matrices[4],
        matrices[5],
        *(saved[n] for n in FEED_SAVED),
        *given,
        *after,
    )


PLACES = {
    (2, 0): (0, 0),
    (1, 1): (0, 1),
    (2, 1): (1, 0),
    (3, 0): (1, 1),
    (1, 0): (2, 0),
    (3, 1): (3, 0),
    (0, 0): (4, 0),
    (0, 1): (4, 1),
}


def term_shapes(count, extra=0):
    rows = (2 * count + extra, 2 * count + extra, count, count, 2 * count)
    return [shaped((n, D), LOW) for n in rows]


def feed_grads(info, mine, branch, own, early, late, after=()):
    def kernel(info, *refs):
        acts, lows, branches, owns, earlies, lates = (refs[2 * i : 2 * i + 2] for i in range(6))
        refs = refs[:12] + refs[12 + len(after) :]
        outs, (a_act, a_first, b_branch, b_own, stage, out_sems) = refs[12:17], refs[17:]
        core, place = info[0], info[1]
        own_at = [slice(seq * ROWS, (seq + 1) * ROWS) for seq in range(SEQS)]
        far_at = [slice((2 + seq) * ROWS, (3 + seq) * ROWS) for seq in range(SEQS)]
        for seq in range(SEQS):
            at, far = own_at[seq], far_at[seq]
            a_act[at] = columns(acts[seq], core * HALF, HALF)[...]
            a_act[far] = earlies[seq][:, 3 * D :]
            b_branch[at] = branches[seq][...]
            b_branch[far] = lates[seq][:, :D]
        sent = []

        def send(block):
            for k in range(4):
                quarter = lax.rem(place + k, 4)
                index, part = PLACES[k, block // 2]
                start = (2 * part + block % 2) * QUARTER
                sent.extend(
                    start_all(
                        [
                            (
                                rows_at(stage.at[block], quarter * QUARTER, QUARTER),
                                outs[index].at[start : start + QUARTER],
                            )
                        ],
                        out_sems,
                        block * 4 + k,
                    )
                )

        for block in range(2):
            for part in range(3):
                start = block * D + part * 256
                stage[block, part * 256 : (part + 1) * 256] = tn(
                    a_act[:, start : start + 256], b_branch[...]
                ).astype(LOW)
            send(block)
        for seq in range(SEQS):
            at, far = own_at[seq], far_at[seq]
            a_first[at] = lows[seq][...]
            a_first[far] = earlies[seq][:, 2 * D : 3 * D]
            b_own[at] = owns[seq][...]
            b_own[far] = lates[seq][:, D:]
        for block in range(2):
            for part in range(3):
                stage[2 + block, part * 256 : (part + 1) * 256] = tn(
                    a_first[:, part * 256 : (part + 1) * 256], b_own[:, block * D : (block + 1) * D]
                ).astype(LOW)
            send(2 + block)
        wait_all(sent)

    acts = [saved["activated"] for saved in mine]
    lows = [saved["first_low"] for saved in mine]
    return pl.pallas_call(
        kernel,
        out_shape=term_shapes(2 * QUARTER),
        in_specs=[SMEM] + [VMEM] * 12 + [ANY] * len(after),
        out_specs=[ANY] * 5,
        scratch_shapes=[
            pltpu.VMEM((2 * ALL_ROWS, HALF), LOW),
            pltpu.VMEM((2 * ALL_ROWS, D), LOW),
            pltpu.VMEM((2 * ALL_ROWS, D), LOW),
            pltpu.VMEM((2 * ALL_ROWS, HALF), LOW),
            pltpu.VMEM((4, D, D), LOW),
            DMA((16,)),
        ],
        compiler_params=limit(16),
        cost_estimate=cost(8),
        name="feed_grads",
    )(info, *acts, *lows, *branch, *own, *early, *late, *after)


def attend_back(seq, info, attended, small_in, spread, after, w_out, saved):
    def kernel(info, attended, small_in, spread, w_out, *refs):
        kept, (pieces, send, small, dmixed, sums) = refs[:4], refs[4 + len(after) :]
        small[...] = small_in[...]
        pieces[1, :ROWS] = attended[...]
        dmixed[...] = nt(attended[...], w_out[...]).astype(LOW)
        s = Names(
            dmixed=dmixed,
            dquery=pieces.at[0, :ROWS],
            dkey=pieces.at[0, ROWS:],
            dvalue=pieces.at[1, ROWS:],
            **dict(zip(ATTEND_SAVED, kept)),
        )
        sums[...] = jnp.zeros_like(sums)

        def table_sum(pair, dscores):
            for odd in range(2):
                part = tn(spread[seq], dscores[odd * ROWS : (odd + 1) * ROWS])
                both = jnp.concatenate([part, jnp.zeros((L, L), WIDE)], axis=1)
                turned = pltpu.roll(both, 0, 1, stride=1, stride_axis=0)
                head = 2 * pair + odd
                sums[head : head + 1, :] = jnp.sum(turned, axis=0, keepdims=True)

        back_attend(s, table_sum)
        send[: ROWS + L] = pieces[1 - info[0]]
        small[S_QUERY : S_QUERY + 1, :] += column_sum(pieces[0, :ROWS])
        small[S_VALUE : S_VALUE + 1, :] += column_sum(pieces[1, ROWS:])
        distance = lax.broadcasted_iota(jnp.int32, (2 * L, L), 0) - (L - 1)
        bucket = lax.broadcasted_iota(jnp.int32, (2 * L, L), 1)
        table = lax.dot_general(
            sums[...],
            (bucket_of(distance) == bucket).astype(WIDE),
            (((1,), (0,)), ((), ())),
            precision=lax.Precision.HIGHEST,
            preferred_element_type=WIDE,
        )
        for column in range(H // 4):
            lanes = slice(column * L, (column + 1) * L)
            small[S_TABLE : S_TABLE + 4, lanes] += table[4 * column : 4 * column + 4]
        send[ROWS + L :] = small[...].astype(LOW)

    return pl.pallas_call(
        kernel,
        out_shape=[
            shaped((2, ROWS + L, D), LOW),
            shaped((ROWS + L + SMALL, D), LOW),
            shaped((SMALL, D), WIDE),
        ],
        in_specs=[SMEM] + [VMEM] * 8 + [ANY] * len(after),
        out_specs=[VMEM] * 3,
        scratch_shapes=[pltpu.VMEM((ROWS, D), LOW), pltpu.VMEM((16, 2 * L), WIDE)],
        compiler_params=limit(12),
        cost_estimate=cost(4),
        name="attend_back",
    )(info, attended, small_in, spread, w_out, *(saved[n] for n in ATTEND_SAVED), *after)


def finish_rows(info, total, output, pieces, matrices, picks, after):
    def kernel(info, *refs):
        totals, outputs, pieces = refs[0:2], refs[2:4], refs[4:6]
        (query, key, value), refs = refs[6:9], refs[9 + len(after) :]
        content_ends, query_ends, done = refs
        done[...] = jnp.zeros_like(done)
        first = info[2] == 1
        for seq in range(SEQS):
            lower = totals[seq][...] + nt(pieces[seq][0, :ROWS], query[...])
            upper = nt(pieces[seq][0, ROWS:], key[...]) + nt(pieces[seq][1, ROWS:], value[...])
            content_ends[seq * L : (seq + 1) * L] = jnp.where(
                first, lower[:L] + upper, outputs[seq][:L]
            )
            ends = jnp.where(first, lower[L : L + picks], outputs[seq][L : L + picks])
            for row in range(picks):
                query_ends[seq * picks + row] = ends[row : row + 1]

    return pl.pallas_call(
        kernel,
        out_shape=[shaped((ALL_CONTENT, D), WIDE), shaped((SEQS * picks, 1, D), WIDE), TOKEN],
        in_specs=[SMEM] + [VMEM] * 9 + [ANY] * len(after),
        out_specs=[VMEM] * 3,
        compiler_params=limit(12),
        cost_estimate=cost(3),
        name="finish_rows",
    )(info, *total, *output, *pieces, *matrices[:3], *after)


def attend_grads(info, pair, early, mine, arrived, small, after=()):
    def kernel(info, small, *refs):
        pairs_in, earlies, mines, arriveds = (refs[2 * i : 2 * i + 2] for i in range(4))
        refs = refs[8 + len(after) :]
        outs, extra, rest = refs[:5], refs[5], refs[6:]
        a_rows, a_content, b_rows, b_content, stage, out_sems = rest
        core, place = info[0], info[1]
        for seq in range(SEQS):
            at = slice(seq * ROWS, (seq + 1) * ROWS)
            far = slice((2 + seq) * ROWS, (3 + seq) * ROWS)
            a_rows[at] = pairs_in[seq][core]
            a_rows[far] = columns(earlies[seq], core * D, D)[...]
            b_rows[at] = mines[seq][core, :ROWS]
            b_rows[far] = arriveds[seq][:ROWS]
            at = slice(seq * L, (seq + 1) * L)
            far = slice((2 + seq) * L, (3 + seq) * L)
            a_content[at] = pairs_in[seq][0, :L]
            a_content[far] = earlies[seq][:L, :D]
            b_content[at] = mines[seq][core, ROWS:]
            b_content[far] = arriveds[seq][ROWS : ROWS + L]
        far_small = arriveds[1][ROWS + L :]
        extra[...] = (small[...] + far_small.astype(WIDE)).astype(LOW)
        sent = start_all([(extra, outs[i].at[2 * QUARTER :]) for i in range(2)], out_sems, 8)
        for block, (former, latter) in enumerate(((a_rows, b_rows), (a_content, b_content))):
            for part in range(3):
                stage[block, part * 256 : (part + 1) * 256] = tn(
                    former[:, part * 256 : (part + 1) * 256], latter[...]
                ).astype(LOW)
            for k in range(4):
                quarter = lax.rem(place + k, 4)
                index, part = PLACES[k, block]
                start = part * QUARTER
                sent += start_all(
                    [
                        (
                            rows_at(stage.at[block], quarter * QUARTER, QUARTER),
                            outs[index].at[start : start + QUARTER],
                        )
                    ],
                    out_sems,
                    block * 4 + k,
                )
        wait_all(sent)

    return pl.pallas_call(
        kernel,
        out_shape=term_shapes(QUARTER, SMALL) + [shaped((SMALL, D), LOW)],
        in_specs=[SMEM] + [VMEM] * 9 + [ANY] * len(after),
        out_specs=[ANY] * 5 + [VMEM],
        scratch_shapes=[
            pltpu.VMEM((2 * ALL_ROWS, D), LOW),
            pltpu.VMEM((2 * ALL_CONTENT, D), LOW),
            pltpu.VMEM((2 * ALL_ROWS, D), LOW),
            pltpu.VMEM((2 * ALL_CONTENT, D), LOW),
            pltpu.VMEM((2, D, D), LOW),
            DMA((10,)),
        ],
        compiler_params=limit(12),
        cost_estimate=cost(5),
        name="attend_grads",
    )(info, small, *pair, *early, *mine, *arrived, *after)


def small_kernel(body, name, shapes, inputs, after=(), info=None, through=()):
    first = [] if info is None else [info]
    given = len(first) + len(inputs)

    def kernel(*refs):
        outs = refs[given + len(after) + len(through) :]
        body(*refs[:given], *outs[: len(shapes)])

    return pl.pallas_call(
        kernel,
        out_shape=[shaped(shape, LOW) for shape in shapes]
        + [shaped(array.shape, array.dtype) for array in through],
        in_specs=[SMEM] * len(first)
        + [VMEM] * len(inputs)
        + [ANY] * (len(after) + len(through)),
        out_specs=[VMEM] * len(shapes) + [ANY] * len(through),
        input_output_aliases={
            given + len(after) + i: len(shapes) + i for i in range(len(through))
        },
        compiler_params=limit(8),
        cost_estimate=cost(1),
        name=name,
    )(*first, *inputs, *after, *through)


def total_of(*terms):
    return sum(term.astype(WIDE) for term in terms).astype(LOW)


def ring_add(after0, before1, from_left, from_right, after=()):
    count = after0.shape[0]
    extra = from_left.shape[0] - 2 * count

    def body(after0, before1, from_left, from_right, right, left):
        right[:count] = total_of(after0[...], from_left[:count])
        left[:count] = total_of(before1[...], from_right[:count])
        if extra:
            right[count:] = from_left[2 * count :]
            left[count:] = from_right[2 * count :]

    return small_kernel(
        body,
        "ring_add",
        [(count + extra, D)] * 2,
        (after0, before1, from_left, from_right),
        after,
    )


def ring_sum(info, own, left, right, from_left, from_right, after=(), small=()):
    count = own.shape[0] // 2
    part = count // 4
    extra = sum(array.shape[0] for array in small)

    def body(info, own, left, right, from_left, from_right, *outs):
        if extra:
            small, outs = outs[0], outs[1:]
            total = total_of(
                small[...], from_left[2 * count :], from_right[2 * count :], left[count:]
            )
        for k, out in enumerate(outs):
            at = pl.multiple_of(lax.rem(info[3] + k, 4) * part, 16)
            low, high = pl.ds(at, part), pl.ds(at + count, part)
            out[:part] = total_of(own[low], left[low], from_right[high])
            out[part : 2 * part] = total_of(own[high], from_left[high], right[low])
            if extra:
                out[2 * part :] = total

    return small_kernel(
        body,
        "ring_sum",
        [(2 * part + extra, D)] * 4,
        (own, left, right, from_left, from_right, *small),
        after,
        info,
    )


def add_all(name, terms, after=()):
    def body(*refs):
        refs[-1][...] = total_of(*(ref[...] for ref in refs[:-1]))

    return small_kernel(body, name, [terms[0].shape], terms, after)[0]


def hand_on(arrays, after):
    return small_kernel(lambda *refs: None, "hand_on", [], (), after, None, arrays)


def z_join(feed, feed_far, attend, attend_far):
    first = feed.shape[0]
    count = attend.shape[0] - SMALL

    def body(feed, feed_far, attend, attend_far, whole, small, table):
        whole[:first] = total_of(feed[...], feed_far[...])
        total = total_of(attend[...], attend_far[...])
        whole[first:] = total[:count]
        small[...] = total[count : count + S_TABLE]
        table[...] = total[count + S_TABLE :]

    shapes = [(first + count, D), (S_TABLE, D), (SMALL - S_TABLE, D)]
    return small_kernel(body, "z_join", shapes, (feed, feed_far, attend, attend_far))


def finish_small(small, table, far, after=()):
    places = [n for n in range(S_TABLE) if not S_EXPAND <= n < S_EXPAND + 4]

    def kernel(small, table, far, *refs):
        vectors, (b_expand, whole, done) = refs[len(after) : -3], refs[-3:]
        done[...] = jnp.zeros_like(done)
        values = small[...].astype(WIDE)
        for place, vector in zip(places, vectors):
            vector[...] = values[place : place + 1]
        for column in range(4):
            lanes = slice(column * D, (column + 1) * D)
            b_expand[:, lanes] = values[S_EXPAND + column : S_EXPAND + column + 1]
        total = table[...].astype(WIDE) + far[...].astype(WIDE)
        heads = [total[:, column * L : (column + 1) * L] for column in range(4)]
        whole[...] = jnp.concatenate(heads)[:H, :NB]

    *vectors, b_expand, whole, done = pl.pallas_call(
        kernel,
        out_shape=[shaped((1, D), WIDE)] * len(places)
        + [shaped((1, FF), WIDE), shaped((H, NB), WIDE), TOKEN],
        in_specs=[VMEM] * 3 + [ANY] * len(after),
        out_specs=[VMEM] * (len(places) + 3),
        compiler_params=limit(4),
        cost_estimate=cost(1),
        name="finish_small",
    )(small, table, far, *after)
    return dict(zip(places, vectors)), b_expand, whole, done


def inner_join(info, parts):
    counts = (QUARTER // 2, QUARTER // 4)
    half = 4 * sum(counts)

    def body(info, *refs):
        whole = refs[-1]
        start, given = 0, 0
        for count in counts:
            for k, ref in enumerate(refs[:-1]):
                at = pl.multiple_of(lax.rem(info[3] + k, 4) * count, 16) + start
                whole[pl.ds(at, count)] = ref[given : given + count]
                whole[pl.ds(at + half, count)] = ref[given + count : given + 2 * count]
            start, given = start + 4 * count, given + 2 * count

    return small_kernel(body, "inner_join", [(2 * half, D)], parts, (), info)[0]


def cut(before, after_part, after=()):
    count = before.shape[0] // 2

    def body(before, after_part, right, left, both):
        right[...] = before[:count]
        left[...] = after_part[count:]
        both[: 2 * count] = before[...]
        both[2 * count :] = after_part[...]

    shapes = [(count, D), (count, D), (4 * count, D)]
    return small_kernel(body, "cut", shapes, (before, after_part), after)


OUT_SHAPES = ((FF, D), (D, FF)) + ((D, D),) * 4


def out_places(outs, source, half, core, quarter):
    pairs = []
    for block in range(2):
        part = source.at[block * QUARTER : (block + 1) * QUARTER]
        if half == 0:
            target = rows_at(outs[0], core * HALF + block * D + quarter * QUARTER, QUARTER)
        else:
            target = columns(
                rows_at(outs[1], quarter * QUARTER, QUARTER), (core * 2 + block) * D, D
            )
        pairs.append((None, part, target))
    part = source.at[2 * QUARTER :]
    for number in range(2):
        target = rows_at(outs[2 + 2 * number + half], quarter * QUARTER, QUARTER)
        pairs.append((core == number, part, target))
    return pairs


def settle(info, pieces, outs, name, after=()):
    shapes, count = OUT_SHAPES, 3 * QUARTER
    keys = tuple(pieces)
    arrays = [pieces[key] for key in keys]
    given = list(after) + list(outs or ())

    def kernel(info, *refs):
        parts, rest = refs[: len(keys)], refs[len(keys) + len(given) :]
        outs, rest = rest[: len(shapes)], rest[len(shapes) :]
        done, rest = rest[0], rest[1:]
        done[...] = jnp.zeros_like(done)
        wide_held, out_sems = rest[:-1], rest[-1]
        finish = []
        for index, (sibling, places) in enumerate(keys):
            core = 1 - info[0] if sibling else info[0]
            for number, (k, half) in enumerate(places):
                quarter = lax.rem((info[3] if sibling else info[1]) + k, 4)
                source = wide_held[index].at[number * count : (number + 1) * count]
                source[...] = parts[index][number * count : (number + 1) * count].astype(WIDE)
                for place, (condition, part, target) in enumerate(
                    out_places(outs, source, half, core, quarter)
                ):
                    copy = pltpu.make_async_copy(
                        part, target, out_sems.at[16 * index + 4 * number + place]
                    )
                    if condition is None:
                        copy.start()
                        finish.append(copy.wait)
                    else:
                        pl.when(condition)(copy.start)
                        finish.append(lambda c=copy, when=condition: pl.when(when)(c.wait))
        for action in finish:
            action()

    result = pl.pallas_call(
        kernel,
        out_shape=[shaped(shape, WIDE) for shape in shapes]
        + [TOKEN],
        in_specs=[SMEM] + [VMEM] * len(keys) + [ANY] * len(given),
        out_specs=[ANY] * len(shapes) + [VMEM],
        scratch_shapes=[pltpu.VMEM(array.shape, WIDE) for array in arrays]
        + [DMA((16 * len(keys),))],
        input_output_aliases={
            1 + len(keys) + len(after) + i: i for i in range(len(outs or ()))
        },
        compiler_params=limit(20),
        cost_estimate=cost(sum(array.size for array in arrays) * 2e-6 + 1),
        name=name,
    )(info, *arrays, *given)
    return result[:-1], result[-1]


PLANE = ("x", "y", "c")


def shift(value, axis, by):
    size = lax.axis_size(axis)
    return lax.ppermute(value, axis, [(i, (i + by) % size) for i in range(size)])


def send(value, by):
    return lax.ppermute(value, "s", [(0, 1)] if by > 0 else [(1, 0)])


def turn(value, outer, by):
    pairs = []
    for i in range(4):
        for j in range(4):
            for c in range(2):
                if (c == 0) == outer:
                    target = ((i + by) % 4, j)
                else:
                    target = (i, (j + by) % 4)
                pairs.append(((i * 4 + j) * 2 + c, (target[0] * 4 + target[1]) * 2 + c))
    return lax.ppermute(value, PLANE, pairs)


def place(outer):
    return jnp.where(
        (lax.axis_index("c") == 0) == outer, lax.axis_index("x"), lax.axis_index("y")
    )


def wide(value):
    return value.astype(WIDE)


def total_wide(*terms):
    return sum(wide(term) for term in terms)


def inner_turns(parts, sign):
    return [turn(part, False, sign * by) for part, by in zip(parts, (1, 2, -1))]


OWN, ACROSS = ((0, 0), (0, 1)), (((2, 0),), ((2, 1),))
NEAR = ((3, 0), (3, 1), (1, 0), (1, 1))


def both_cores(places, piece):
    return {(0, places): piece, (1, places): shift(piece, "c", 1)}


def on_device(
    content_in,
    query_in,
    content_cot,
    query_cot,
    order_rank,
    query_pos,
    group_tag,
    *rest,
):
    (
        w_query,
        b_query,
        w_key,
        w_value,
        b_value,
        w_out,
        b_out,
        norm1_gain,
        norm1_bias,
        w_expand,
        b_expand,
        w_contract,
        b_contract,
        norm2_gain,
        norm2_bias,
    ) = (argument[0] for argument in rest[:-1])
    rel_table = rest[-1]
    core = lax.axis_index("c")
    first_section = (lax.axis_index("s") == 0).astype(jnp.int32)
    info = jnp.stack([core, place(True), first_section, place(False)])
    picks = query_pos.shape[1]

    matrices = (w_query, w_key, w_value, w_out, w_expand, w_contract)
    w_out_held = w_out
    vec = jnp.stack(
        [b_query, b_value, b_out, norm1_gain, norm1_bias, b_contract, norm2_gain, norm2_bias]
    )
    ranks = jnp.concatenate([order_rank, group_tag, query_pos], axis=1)
    masks, spread, query_in, query_cot = prepare(
        ranks, rel_table.T, jnp.concatenate([query_in, query_cot]), picks, (vec, info)
    )
    b_expand = b_expand[None]

    fronts, arrived = [], []
    for seq in range(SEQS):
        given = (seq, info, content_in, query_in, matrices, masks, vec, b_expand)
        fronts.append(front(*given, tuple(fronts)) if fronts else front_parts(*given))
        arrived.append(send(fronts[seq], 1))
    output, early, pair, saved, grads = [], [], [], [], []
    for seq in range(SEQS):
        results = middle_forward(
            seq, info, content_in, query_in, arrived[seq], matrices, masks, vec, b_expand, tuple(grads)
        )
        for collected, result in zip((output, early, pair, saved), results):
            collected.append(result)
        grads.append(middle_back(seq, content_cot, query_cot, matrices, vec, saved[seq]))
    early = [shift(value, "c", 1) for value in early]
    grads = [send(value, -1) for value in grads]
    small = None
    total, branch, attended, own, late, pieces, pass_on = [], [], [], [], [], [], []
    for seq in range(SEQS):
        results = feed_back(
            seq,
            info,
            grads[seq],
            content_cot,
            query_cot,
            small,
            vec,
            matrices,
            saved[seq],
            tuple(pass_on),
        )
        small = results[3]
        for collected, result in zip(
            (total, branch, attended, own, late), results[:3] + results[4:]
        ):
            collected.append(result)
        late[seq] = shift(late[seq], "c", 1)
        results = attend_back(
            seq,
            info,
            attended[seq],
            small,
            spread,
            (),
            w_out_held,
            saved[seq],
        )
        small = results[2]
        pieces.append(results[0])
        pass_on.append(results[1])
    feed_terms = feed_grads(info, saved, branch, own, early, late, (small,))
    passed = [shift(value, "c", 1) for value in pass_on]

    def outer_step(terms):
        return (turn(terms[0], True, 1), turn(terms[1], True, -1))

    f_left, f_right = outer_step(feed_terms)
    *attend_terms, extra = attend_grads(info, pair, early, pieces, passed, small, (feed_terms[4],))
    a_left, a_right = outer_step(attend_terms)
    f_sent = ring_add(feed_terms[2], feed_terms[3], f_left, f_right, (extra,))
    f_outer = outer_step(f_sent)
    a_sent = ring_add(attend_terms[2], attend_terms[3], a_left, a_right)
    f_parts = ring_sum(info, feed_terms[4], *f_outer, f_left, f_right, (a_sent[0],))
    f_others = inner_turns(f_parts[1:], 1)
    a_parts = ring_sum(
        info, attend_terms[4], *outer_step(a_sent), a_left, a_right, (f_parts[0],), (extra,)
    )
    f_part = add_all("inner_sum", [f_parts[0]] + f_others, (a_parts[0],))
    f_far = shift(f_part, "z", 1)
    a_part = add_all("inner_sum", [a_parts[0]] + inner_turns(a_parts[1:], 1), (f_part,))
    a_far = shift(a_part, "z", 1)
    part, small, table = z_join(f_part, f_far, a_part, a_far)
    own = inner_join(info, [part] + inner_turns([part] * 3, -1))
    before, after_part = turn(own, True, 1), turn(own, True, -1)
    content_ends, query_ends, token = finish_rows(
        info, total, output, pieces, matrices, picks, (own,)
    )
    row, b_expand, table, small_token = finish_small(small, table, shift(table, "s", 1), (own,))
    outs, own_token = settle(info, both_cores(OWN, own), None, "own_out")
    to_right, to_left, near = cut(before, after_part, (token, small_token, own_token))
    across = (turn(to_right, True, 1), turn(to_left, True, -1))
    outs, near_token = settle(info, {(0, NEAR): near}, outs, "near_out")
    outs, far_token = settle(info, {(1, NEAR): shift(near, "c", 1)}, outs, "near_out")
    across = hand_on(across, (near_token, far_token))
    own = {(0, places): piece for places, piece in zip(ACROSS, across)}
    far = {(1, places): shift(piece, "c", 1) for places, piece in zip(ACROSS, across)}
    outs, _ = settle(info, own, outs, "across_out")
    outs, _ = settle(info, far, outs, "across_out")
    contract, expand, g_query, g_key, g_out, g_value = outs
    return (
        content_ends[None],
        query_ends.transpose(1, 0, 2),
        g_query[None],
        row[S_QUERY],
        g_key[None],
        g_value[None],
        row[S_VALUE],
        g_out[None],
        row[S_OUT],
        row[S_GAIN1],
        row[S_SHIFT1],
        expand[None],
        b_expand,
        contract[None],
        row[S_CONTRACT],
        row[S_GAIN2],
        row[S_SHIFT2],
        table.T,
    )


DP = ("z", "x", "y", "c")


def solution(mesh):
    mesh = jax.sharding.Mesh(mesh.devices.reshape(2, 2, 4, 4, 2), ("s",) + DP)
    layer_specs = tuple(
        P("s", *([None] * (rank - 1))) for rank in (3, 2, 3, 3, 2, 3, 2, 2, 2, 3, 2, 3, 2, 2, 2)
    )
    in_specs = (P(DP, None),) * 7 + layer_specs + (P(),)
    out_specs = (P("s", DP, None),) * 2 + layer_specs + (P(),)
    return jax.shard_map(
        on_device, mesh=mesh, in_specs=in_specs, out_specs=out_specs, check_vma=False
    )
```

```python
import jax
import jax.numpy as jnp
from jax import lax
from jax.experimental import pallas as pl
from jax.experimental.pallas import tpu as pltpu
from jax.sharding import PartitionSpec as P

D = 768
H = 12
HD = 64
FF = 3072
NB = 32
L = 128
PAIRS = H // 2
SEQS = 2
PICKS = 32
ROWS = L + PICKS
EPSILON = 1e-05
SCALE = HD ** (-0.5)
TILE = 1536
LOW = jnp.bfloat16
WIDE = jnp.float32
HALF = FF // 2
QUARTER = D // 4
EARLY = 3 * D + HALF
LATE = D + HALF
SMALL = 16
ALL_ROWS = SEQS * ROWS
ALL_CONTENT = SEQS * L
PIECE = ALL_ROWS + ALL_CONTENT


def nn(former, latter):
    return lax.dot_general(
        former, latter, (((1,), (0,)), ((), ())), preferred_element_type=WIDE
    )


def nt(former, latter):
    return lax.dot_general(
        former, latter, (((1,), (1,)), ((), ())), preferred_element_type=WIDE
    )


def tn(former, latter):
    return lax.dot_general(
        former, latter, (((0,), (0,)), ((), ())), preferred_element_type=WIDE
    )


def halves(value):
    even = lax.broadcasted_iota(jnp.int32, value.shape, 1) < HD
    zero = jnp.zeros_like(value)
    return jnp.concatenate([jnp.where(even, value, zero), jnp.where(even, zero, value)])


def side(value):
    count = value.shape[0] // 2
    return jnp.concatenate([value[:count], value[count:]], axis=1)


def norm_rows(values):
    centered = values - jnp.mean(values, axis=-1, keepdims=True)
    variance = jnp.mean(centered * centered, axis=-1, keepdims=True)
    root = lax.rsqrt(variance + EPSILON)
    return (centered * root, root)


def norm_rows_back(scaled, normed, root):
    return root * (
        scaled
        - jnp.mean(scaled, axis=-1, keepdims=True)
        - normed * jnp.mean(scaled * normed, axis=-1, keepdims=True)
    )


B_QUERY, B_VALUE, B_OUT, GAIN1, SHIFT1, B_CONTRACT, GAIN2, SHIFT2 = range(8)
S_QUERY, S_VALUE, S_OUT, S_GAIN1, S_SHIFT1, S_EXPAND = range(6)
S_CONTRACT, S_GAIN2, S_SHIFT2, S_TABLE = 9, 10, 11, 12
LIMITS = (12, 16, 23, 32, 46, 64, 91)


def bucket_of(relative):
    distance = jnp.abs(relative)
    beyond = 8 + sum((distance >= limit).astype(jnp.int32) for limit in LIMITS)
    within = jnp.where(distance < 8, distance, beyond)
    return within + 16 * (relative > 0).astype(jnp.int32)


def forward_attend(x, w, vec, masks, s, keep):
    row = lambda k: vec[k : k + 1, :]
    s.query[...] = (nn(x[...], w.query[...]) + row(B_QUERY)).astype(LOW)
    s.key[...] = nn(x[:L], w.key[...]).astype(LOW)
    s.value[...] = (nn(x[:L], w.value[...]) + row(B_VALUE)).astype(LOW)
    for pair in range(PAIRS):
        lanes = slice(pair * 128, (pair + 1) * 128)
        scores = nt(halves(s.query[:, lanes]), s.key[:, lanes]) * SCALE + masks[pair]
        shifted = jnp.exp(scores - jnp.max(scores, axis=-1, keepdims=True))
        probs = (shifted / jnp.sum(shifted, axis=-1, keepdims=True)).astype(LOW)
        if keep:
            s.probs[pair] = probs
        s.mixed[:, lanes] = nn(side(probs), halves(s.value[:, lanes])).astype(LOW)
    total = x[...].astype(WIDE) + nn(s.mixed[...], w.out[...]) + row(B_OUT)
    normed, root = norm_rows(total)
    first = normed * row(GAIN1) + row(SHIFT1)
    s.first_low[...] = first.astype(LOW)
    s.total[...] = first + row(B_CONTRACT)
    if keep:
        s.normed1[...] = normed
        s.root1[...] = jnp.broadcast_to(root, (ROWS, 128))


def forward_feed(w, vec, b_expand, s, keep):
    row = lambda k: vec[k : k + 1, :]
    for tile in range(FF // TILE):
        tile = slice(tile * TILE, (tile + 1) * TILE)
        expanded = nn(s.first_low[...], w.expand[:, tile]) + b_expand[:, tile]
        cumulative = 0.5 * (1.0 + lax.erf(expanded * 0.7071067811865476))
        activated = (expanded * cumulative).astype(LOW)
        if keep:
            s.slope[:, tile] = (
                cumulative + expanded * jnp.exp(-0.5 * expanded * expanded) * 0.3989422804014327
            ).astype(LOW)
            s.activated[:, tile] = activated
        s.total[...] += nn(activated, w.contract[tile, :])
    normed, root = norm_rows(s.total[...])
    if keep:
        s.normed2[...] = normed
        s.root2[...] = jnp.broadcast_to(root, (ROWS, 128))
    s.out[...] = (normed * row(GAIN2) + row(SHIFT2)).astype(s.out.dtype)


def column_sum(value):
    return jnp.sum(value.astype(WIDE), axis=0, keepdims=True)


def back_second_norm(grad, vec, s, add=None):
    upper = grad.astype(WIDE)
    normed = s.normed2[...]
    lower = norm_rows_back(upper * vec[GAIN2 : GAIN2 + 1, :], normed, s.root2[:, :1])
    s.total[...] = lower
    s.branch[...] = lower.astype(LOW)
    if add is not None:
        add(S_GAIN2, column_sum(upper * normed))
        add(S_SHIFT2, column_sum(upper))
        add(S_CONTRACT, column_sum(lower.astype(LOW)))


def back_feed(w, vec, s, add=None):
    for tile in range(FF // TILE):
        tile = slice(tile * TILE, (tile + 1) * TILE)
        lower = (nt(s.branch[...], w.contract[tile, :]) * s.slope[:, tile].astype(WIDE)).astype(LOW)
        s.expanded[:, tile] = lower
        if add is not None:
            part = column_sum(lower)
            for column in range(TILE // D):
                add(
                    S_EXPAND + tile.start // D + column,
                    part[:, column * D : (column + 1) * D],
                )
        s.total[...] += nt(lower, w.expand[:, tile])
    upper = s.total[...]
    normed = s.normed1[...]
    lower = norm_rows_back(upper * vec[GAIN1 : GAIN1 + 1, :], normed, s.root1[:, :1])
    s.total[...] = lower
    s.attended[...] = lower.astype(LOW)
    if add is not None:
        add(S_GAIN1, column_sum(upper * normed))
        add(S_SHIFT1, column_sum(upper))
        add(S_OUT, column_sum(lower.astype(LOW)))


def back_attend(s, table=None):
    for pair in range(PAIRS):
        lanes = slice(pair * 128, (pair + 1) * 128)
        probs = s.probs[pair]
        below = halves(s.dmixed[:, lanes])
        dprobs = nt(below, s.value[:, lanes])
        s.dvalue[:, lanes] = tn(probs, below).astype(LOW)
        weight = probs.astype(WIDE)
        dscores = (
            weight * (dprobs - jnp.sum(weight * dprobs, axis=-1, keepdims=True))
        ).astype(LOW)
        s.dquery[:, lanes] = (nn(side(dscores), halves(s.key[:, lanes])) * SCALE).astype(LOW)
        s.dkey[:, lanes] = (tn(dscores, halves(s.query[:, lanes])) * SCALE).astype(LOW)
        if table is not None:
            table(pair, dscores)


class Names:
    def __init__(self, **named):
        self.__dict__.update(named)


MATRICES = ("query", "key", "value", "out", "expand", "contract")
MATRIX_SHAPES = {
    "query": (D, D),
    "key": (D, D),
    "value": (D, D),
    "out": (D, D),
    "expand": (D, FF),
    "contract": (FF, D),
}
MASK_SHAPE = (PAIRS, 2 * ROWS, L)
KEPT = {
    "query": ((ROWS, D), LOW),
    "key": ((L, D), LOW),
    "value": ((L, D), LOW),
    "probs": (MASK_SHAPE, LOW),
    "mixed": ((ROWS, D), LOW),
    "normed1": ((ROWS, D), WIDE),
    "root1": ((ROWS, 128), WIDE),
    "first_low": ((ROWS, D), LOW),
    "slope": ((ROWS, FF), LOW),
    "activated": ((ROWS, FF), LOW),
    "normed2": ((ROWS, D), WIDE),
    "root2": ((ROWS, 128), WIDE),
}
SAVED = tuple(name for name in KEPT if name != "mixed")
ANY = pl.BlockSpec(memory_space=pl.ANY)
HBM = pl.BlockSpec(memory_space=pltpu.HBM)
VMEM = pl.BlockSpec(memory_space=pltpu.VMEM)
SMEM = pl.BlockSpec(memory_space=pltpu.SMEM)


def limit(megabytes):
    return pltpu.CompilerParams(vmem_limit_bytes=megabytes * 1024 * 1024)


DMA = pltpu.SemaphoreType.DMA


def cost(microseconds):
    return pl.CostEstimate(flops=0, bytes_accessed=int(microseconds * 3.2e6), transcendentals=0)


def shaped(shape, kind):
    return jax.ShapeDtypeStruct(shape, kind)


TOKEN = shaped((8, 128), WIDE)


def columns(ref, start, size):
    return ref.at[:, pl.ds(pl.multiple_of(start, 128), size)]


def rows_at(ref, start, size):
    return ref.at[pl.ds(pl.multiple_of(start, 64), size)]


def start_all(pairs, sems, base=0):
    copies = [
        pltpu.make_async_copy(source, target, sems.at[base + index])
        for index, (source, target) in enumerate(pairs)
    ]
    for copy in copies:
        copy.start()
    return copies


def wait_all(copies):
    for copy in copies:
        copy.wait()


def fetcher(names, sources, targets, sems, base=0):
    copies = dict(zip(names, start_all(list(zip(sources, targets)), sems, base)))
    return lambda name: copies[name].wait()


def prepare(ranks, table, queries, picks, after):
    def kernel(ranks, table, queries, *refs):
        masks, spread, rows_in, rows_cot = refs[len(after) :]
        order, tag, pos = ranks[:, :L], ranks[:, L : 2 * L], ranks[:, 2 * L : 2 * L + picks]
        values = queries[...].astype(WIDE)
        blank = jnp.zeros((PICKS - picks, D), WIDE)
        for index, target in enumerate((rows_in, rows_cot)):
            own = values[2 * index * picks : 2 * (index + 1) * picks]
            target[...] = jnp.concatenate([own[:picks], blank, own[picks:], blank]).astype(LOW)
        lane = lax.broadcasted_iota(jnp.int32, (L, L), 1)
        level = lax.broadcasted_iota(jnp.int32, (L, L), 0)
        lane_q = lax.broadcasted_iota(jnp.int32, (PICKS, L), 1)
        upright = lambda row: jnp.sum(jnp.where(lane == level, row, 0.0), axis=1, keepdims=True)
        distance = lax.broadcasted_iota(jnp.int32, (2 * L, NB), 0) - (L - 1)
        bucket = lax.broadcasted_iota(jnp.int32, (2 * L, NB), 1)
        by_distance = lax.dot_general(
            table[...],
            (bucket_of(distance) == bucket).astype(WIDE),
            (((1,), (1,)), ((), ())),
            precision=lax.Precision.HIGHEST,
            preferred_element_type=WIDE,
        )
        allowed, hot = [], []
        for seq in range(SEQS):
            own_rank = order[seq : seq + 1, :].astype(WIDE)
            own_tag = tag[seq : seq + 1, :].astype(WIDE)
            own_pos = pos[seq : seq + 1, :].astype(WIDE)
            number = lax.broadcasted_iota(jnp.int32, (PICKS, picks), 0)
            same = number == lax.broadcasted_iota(jnp.int32, (PICKS, picks), 1)
            place = jnp.sum(jnp.where(same, own_pos, 0.0), axis=1, keepdims=True)
            filled = lax.broadcasted_iota(jnp.int32, (PICKS, 1), 0) < picks
            place = jnp.where(filled, place, -1.0).astype(jnp.int32)
            matches = place == lane_q
            marks = jnp.where(matches, 1.0, 0.0)
            predicted = jnp.max(marks, axis=0, keepdims=True)
            rank = jnp.sum(jnp.where(matches, own_rank, 0.0), axis=1, keepdims=True)
            group = jnp.sum(jnp.where(matches, own_tag, 0.0), axis=1, keepdims=True)
            earlier = (upright(predicted) > 0) & (own_rank <= upright(own_rank))
            content = (upright(own_tag) == own_tag) & ((predicted == 0) | earlier)
            query = (group == own_tag) & ((predicted == 0) | (own_rank + 1 <= rank))
            allowed.append((content, query))
            hot.append(marks)
            spread[seq, :L] = jnp.where(lane == L - 1 - level, 1.0, 0.0).astype(LOW)
            spread[seq, L:] = jnp.where(lane_q == L - 1 - place, 1.0, 0.0).astype(LOW)
        hot = jnp.concatenate(hot)
        for head in range(H):
            row = jnp.broadcast_to(by_distance[head : head + 1], (L, 2 * L))
            bias = pltpu.roll(row, L + 1, 1, stride=1, stride_axis=0)[:, :L]
            bias_q = lax.dot_general(
                hot,
                bias,
                (((1,), (0,)), ((), ())),
                precision=lax.Precision.HIGHEST,
                preferred_element_type=WIDE,
            )
            base = head % 2 * ROWS
            for seq in range(SEQS):
                content, query = allowed[seq]
                masks[seq, head // 2, base : base + L] = jnp.where(content, bias, -1e30)
                masks[seq, head // 2, base + L : base + ROWS] = jnp.where(
                    query, bias_q[seq * PICKS : (seq + 1) * PICKS], -1e30
                )

    return pl.pallas_call(
        kernel,
        out_shape=[
            shaped((SEQS,) + MASK_SHAPE, WIDE),
            shaped((SEQS, ROWS, L), LOW),
            shaped((SEQS * PICKS, D), LOW),
            shaped((SEQS * PICKS, D), LOW),
        ],
        in_specs=[VMEM] * 3 + [ANY] * len(after),
        out_specs=[VMEM] * 4,
        compiler_params=limit(8),
        cost_estimate=pl.CostEstimate(flops=int(3e10), bytes_accessed=0, transcendentals=0),
        name="prepare",
    )(ranks, table, queries, *after)


def only(condition, work, *outs):
    pl.when(condition)(work)

    @pl.when(jnp.logical_not(condition))
    def _():
        for out in outs:
            out[...] = jnp.zeros_like(out)


def take_rows(content, picks, seq, target):
    target[:L] = content[seq * L : (seq + 1) * L]
    target[L:] = picks[seq * PICKS : (seq + 1) * PICKS]


def front(seq, info, content, picks, matrices, masks, vec, b_expand, after=()):
    def kernel(info, content, picks, masks, vec, b_expand, *refs):
        w = Names(**dict(zip(MATRICES, refs[:6])))
        out, x, query, key, value, mixed, first_low, total = refs[6 + len(after) :]
        s = Names(
            query=query,
            key=key,
            value=value,
            mixed=mixed,
            first_low=first_low,
            total=total,
            out=out,
        )

        def work():
            take_rows(content, picks, seq, x)
            forward_attend(x, w, vec, masks.at[seq], s, False)
            forward_feed(w, vec, b_expand, s, False)

        only(info[2] == 1, work, out)

    return pl.pallas_call(
        kernel,
        out_shape=shaped((ROWS, D), LOW),
        in_specs=[SMEM] + [VMEM] * 11 + [ANY] * len(after),
        out_specs=VMEM,
        scratch_shapes=[pltpu.VMEM((ROWS, D), LOW)]
        + [pltpu.VMEM(*KEPT[n]) for n in ("query", "key", "value", "mixed", "first_low")]
        + [pltpu.VMEM((ROWS, D), WIDE)],
        compiler_params=limit(12),
        cost_estimate=cost(5),
        name="front",
    )(info, content, picks, masks, vec, b_expand, *matrices, *after)


def front_parts(seq, info, content, picks, matrices, masks, vec, b_expand):
    def first(info, content, picks, masks, vec, *refs):
        w = Names(**dict(zip(MATRICES[:4], refs[:4])))
        first_low, total, x, query, key, value, mixed = refs[4:]
        s = Names(
            query=query, key=key, value=value, mixed=mixed, first_low=first_low, total=total
        )

        def work():
            take_rows(content, picks, seq, x)
            forward_attend(x, w, vec, masks.at[seq], s, False)

        only(info[2] == 1, work, first_low, total)

    def second(info, first_low, total_in, vec, b_expand, expand, contract, out, total):
        s = Names(first_low=first_low, total=total, out=out)

        def work():
            total[...] = total_in[...]
            forward_feed(Names(expand=expand, contract=contract), vec, b_expand, s, False)

        only(info[2] == 1, work, out)

    first_low, total = pl.pallas_call(
        first,
        out_shape=[shaped((ROWS, D), LOW), shaped((ROWS, D), WIDE)],
        in_specs=[SMEM] + [VMEM] * 8,
        out_specs=[VMEM] * 2,
        scratch_shapes=[pltpu.VMEM((ROWS, D), LOW)]
        + [pltpu.VMEM(*KEPT[n]) for n in ("query", "key", "value", "mixed")],
        compiler_params=limit(8),
        cost_estimate=pl.CostEstimate(flops=int(1e10), bytes_accessed=0, transcendentals=0),
        name="front_attend",
    )(info, content, picks, masks, vec, *matrices[:4])
    return pl.pallas_call(
        second,
        out_shape=shaped((ROWS, D), LOW),
        in_specs=[SMEM] + [VMEM] * 6,
        out_specs=VMEM,
        scratch_shapes=[pltpu.VMEM((ROWS, D), WIDE)],
        compiler_params=limit(12),
        cost_estimate=cost(2),
        name="front_feed",
    )(info, first_low, total, vec, b_expand, *matrices[4:])


def middle_forward(seq, info, content, picks, arrived, matrices, masks, vec, b_expand, after=()):
    def kernel(info, arrived, content, picks, masks, vec, b_expand, *refs):
        w, rest = Names(**dict(zip(MATRICES, refs[:6]))), refs[6 + len(after) :]
        (out, early, pair), kept = rest[:3], rest[3 : 3 + len(SAVED)]
        mixed, total = rest[3 + len(SAVED) :]
        x = pair.at[0]
        s = Names(total=total, out=out, mixed=mixed, **dict(zip(SAVED, kept)))
        take_rows(content, picks, seq, x)
        x[...] = jnp.where(info[2] == 1, x[...], arrived[...])
        early[:, :D] = x[...]
        forward_attend(x, w, vec, masks.at[seq], s, True)
        forward_feed(w, vec, b_expand, s, True)
        pair[1] = mixed[...]
        early[:, D : 2 * D] = mixed[...]
        early[:, 2 * D : 3 * D] = s.first_low[...]
        early[:, 3 * D :] = columns(s.activated, (1 - info[0]) * HALF, HALF)[...]

    out, early, pair, *saved = pl.pallas_call(
        kernel,
        out_shape=[
            shaped((ROWS, D), WIDE),
            shaped((ROWS, EARLY), LOW),
            shaped((2, ROWS, D), LOW),
        ]
        + [shaped(*KEPT[n]) for n in SAVED],
        in_specs=[SMEM] + [VMEM] * 12 + [ANY] * len(after),
        out_specs=[VMEM] * (3 + len(SAVED)),
        scratch_shapes=[pltpu.VMEM(*KEPT["mixed"]), pltpu.VMEM((ROWS, D), WIDE)],
        compiler_params=limit(16),
        cost_estimate=cost(6),
        name="middle_forward",
    )(info, arrived, content, picks, masks, vec, b_expand, *matrices, *after)
    return (out, early, pair, dict(zip(SAVED, saved)))


FEED_SAVED = ("normed2", "root2", "slope", "normed1", "root1")
ATTEND_SAVED = ("value", "probs", "key", "query")


def middle_back(seq, info, content, picks, matrices, vec, saved):
    names = FEED_SAVED + ATTEND_SAVED

    def kernel(info, content, picks, vec, *refs):
        w, rest = Names(**dict(zip(MATRICES, refs[:6]))), refs[6:]
        kept, grad, rest = rest[: len(names)], rest[len(names)], rest[len(names) + 1 :]
        cot, total, branch, expanded, attended, dmixed, dvalue, dquery, dkey = rest
        s = Names(
            total=total,
            branch=branch,
            expanded=expanded,
            attended=attended,
            dmixed=dmixed,
            dvalue=dvalue,
            dquery=dquery,
            dkey=dkey,
            **dict(zip(names, kept)),
        )

        def work():
            take_rows(content, picks, seq, cot)
            back_second_norm(cot[...], vec, s)
            back_feed(w, vec, s)
            dmixed[...] = nt(attended[...], w.out[...]).astype(LOW)
            back_attend(s)
            lower = total[...] + nt(dquery[...], w.query[...])
            upper = nt(dkey[...], w.key[...]) + nt(dvalue[...], w.value[...])
            grad[:L] = (lower[:L] + upper).astype(LOW)
            grad[L:] = lower[L:].astype(LOW)

        only(info[2] == 0, work, grad)

    return pl.pallas_call(
        kernel,
        out_shape=shaped((ROWS, D), LOW),
        in_specs=[SMEM] + [VMEM] * (9 + len(names)),
        out_specs=VMEM,
        scratch_shapes=[
            pltpu.VMEM((ROWS, D), LOW),
            pltpu.VMEM((ROWS, D), WIDE),
            pltpu.VMEM((ROWS, D), LOW),
            pltpu.VMEM((ROWS, FF), LOW),
            pltpu.VMEM((ROWS, D), LOW),
            pltpu.VMEM((ROWS, D), LOW),
            pltpu.VMEM((L, D), LOW),
            pltpu.VMEM((ROWS, D), LOW),
            pltpu.VMEM((L, D), LOW),
        ],
        compiler_params=limit(12),
        cost_estimate=cost(7),
        name="middle_back",
    )(info, content, picks, vec, *matrices, *(saved[n] for n in names))


def feed_back(seq, info, arrived, content, picks, small_in, vec, matrices, saved, after=()):
    given = [] if small_in is None else [small_in]

    def kernel(info, arrived, content, picks, vec, expand, contract, *refs):
        kept, rest = refs[:5], refs[5 + len(given) + len(after) :]
        total, branch, attended, small, own, late, upper, expanded = rest
        w = Names(expand=expand, contract=contract)
        s = Names(
            total=total,
            branch=branch,
            attended=attended,
            expanded=expanded,
            **dict(zip(FEED_SAVED, kept)),
        )
        small[...] = refs[5][...] if given else jnp.zeros_like(small)

        def add(place, value):
            small[place : place + 1, :] += value

        take_rows(content, picks, seq, upper)
        back_second_norm(jnp.where(info[2] == 1, arrived[...], upper[...]), vec, s, add)
        late[:, :D] = branch[...]
        back_feed(w, vec, s, add)
        own[...] = columns(expanded, info[0] * HALF, HALF)[...]
        late[:, D:] = columns(expanded, (1 - info[0]) * HALF, HALF)[...]

    return pl.pallas_call(
        kernel,
        out_shape=[
            shaped((ROWS, D), WIDE),
            shaped((ROWS, D), LOW),
            shaped((ROWS, D), LOW),
            shaped((SMALL, D), WIDE),
            shaped((ROWS, HALF), LOW),
            shaped((ROWS, LATE), LOW),
        ],
        in_specs=[SMEM] + [VMEM] * (11 + len(given)) + [ANY] * len(after),
        out_specs=[VMEM] * 6,
        scratch_shapes=[pltpu.VMEM((ROWS, D), LOW), pltpu.VMEM((ROWS, FF), LOW)],
        compiler_params=limit(12),
        cost_estimate=cost(4),
        name="feed_back",
    )(
        info,
        arrived,
        content,
        picks,
        vec,
        matrices[4],
        matrices[5],
        *(saved[n] for n in FEED_SAVED),
        *given,
        *after,
    )


PLACES = {
    (2, 0): (0, 0),
    (1, 1): (0, 1),
    (2, 1): (1, 0),
    (3, 0): (1, 1),
    (1, 0): (2, 0),
    (3, 1): (3, 0),
    (0, 0): (4, 0),
    (0, 1): (4, 1),
}


def term_shapes(count, extra=0):
    rows = (2 * count + extra, 2 * count + extra, count, count, 2 * count)
    return [shaped((n, D), LOW) for n in rows]


def feed_grads(info, mine, branch, own, early, late, after=()):
    def kernel(info, *refs):
        acts, lows, branches, owns, earlies, lates = (refs[2 * i : 2 * i + 2] for i in range(6))
        refs = refs[:12] + refs[12 + len(after) :]
        outs, (a_act, a_first, b_branch, b_own, stage, out_sems) = refs[12:17], refs[17:]
        core, place = info[0], info[1]
        own_at = [slice(seq * ROWS, (seq + 1) * ROWS) for seq in range(SEQS)]
        far_at = [slice((2 + seq) * ROWS, (3 + seq) * ROWS) for seq in range(SEQS)]
        for seq in range(SEQS):
            at, far = own_at[seq], far_at[seq]
            a_act[at] = columns(acts[seq], core * HALF, HALF)[...]
            a_act[far] = earlies[seq][:, 3 * D :]
            b_branch[at] = branches[seq][...]
            b_branch[far] = lates[seq][:, :D]
        sent = []

        def send(block):
            for k in range(4):
                quarter = lax.rem(place + k, 4)
                index, part = PLACES[k, block // 2]
                start = (2 * part + block % 2) * QUARTER
                sent.extend(
                    start_all(
                        [
                            (
                                rows_at(stage.at[block], quarter * QUARTER, QUARTER),
                                outs[index].at[start : start + QUARTER],
                            )
                        ],
                        out_sems,
                        block * 4 + k,
                    )
                )

        for block in range(2):
            for part in range(3):
                start = block * D + part * 256
                stage[block, part * 256 : (part + 1) * 256] = tn(
                    a_act[:, start : start + 256], b_branch[...]
                ).astype(LOW)
            send(block)
        for seq in range(SEQS):
            at, far = own_at[seq], far_at[seq]
            a_first[at] = lows[seq][...]
            a_first[far] = earlies[seq][:, 2 * D : 3 * D]
            b_own[at] = owns[seq][...]
            b_own[far] = lates[seq][:, D:]
        for block in range(2):
            for part in range(3):
                stage[2 + block, part * 256 : (part + 1) * 256] = tn(
                    a_first[:, part * 256 : (part + 1) * 256], b_own[:, block * D : (block + 1) * D]
                ).astype(LOW)
            send(2 + block)
        wait_all(sent)

    acts = [saved["activated"] for saved in mine]
    lows = [saved["first_low"] for saved in mine]
    return pl.pallas_call(
        kernel,
        out_shape=term_shapes(2 * QUARTER),
        in_specs=[SMEM] + [VMEM] * 12 + [ANY] * len(after),
        out_specs=[ANY] * 5,
        scratch_shapes=[
            pltpu.VMEM((2 * ALL_ROWS, HALF), LOW),
            pltpu.VMEM((2 * ALL_ROWS, D), LOW),
            pltpu.VMEM((2 * ALL_ROWS, D), LOW),
            pltpu.VMEM((2 * ALL_ROWS, HALF), LOW),
            pltpu.VMEM((4, D, D), LOW),
            DMA((16,)),
        ],
        compiler_params=limit(16),
        cost_estimate=cost(8),
        name="feed_grads",
    )(info, *acts, *lows, *branch, *own, *early, *late, *after)


def attend_back(seq, info, attended, small_in, spread, after, w_out, saved):
    def kernel(info, attended, small_in, spread, w_out, *refs):
        kept, (pieces, send, small, dmixed, sums) = refs[:4], refs[4 + len(after) :]
        small[...] = small_in[...]
        pieces[1, :ROWS] = attended[...]
        dmixed[...] = nt(attended[...], w_out[...]).astype(LOW)
        s = Names(
            dmixed=dmixed,
            dquery=pieces.at[0, :ROWS],
            dkey=pieces.at[0, ROWS:],
            dvalue=pieces.at[1, ROWS:],
            **dict(zip(ATTEND_SAVED, kept)),
        )
        sums[...] = jnp.zeros_like(sums)

        def table_sum(pair, dscores):
            for odd in range(2):
                part = tn(spread[seq], dscores[odd * ROWS : (odd + 1) * ROWS])
                both = jnp.concatenate([part, jnp.zeros((L, L), WIDE)], axis=1)
                turned = pltpu.roll(both, 0, 1, stride=1, stride_axis=0)
                head = 2 * pair + odd
                sums[head : head + 1, :] = jnp.sum(turned, axis=0, keepdims=True)

        back_attend(s, table_sum)
        send[: ROWS + L] = pieces[1 - info[0]]
        small[S_QUERY : S_QUERY + 1, :] += column_sum(pieces[0, :ROWS])
        small[S_VALUE : S_VALUE + 1, :] += column_sum(pieces[1, ROWS:])
        distance = lax.broadcasted_iota(jnp.int32, (2 * L, L), 0) - (L - 1)
        bucket = lax.broadcasted_iota(jnp.int32, (2 * L, L), 1)
        table = lax.dot_general(
            sums[...],
            (bucket_of(distance) == bucket).astype(WIDE),
            (((1,), (0,)), ((), ())),
            precision=lax.Precision.HIGHEST,
            preferred_element_type=WIDE,
        )
        for column in range(H // 4):
            lanes = slice(column * L, (column + 1) * L)
            small[S_TABLE : S_TABLE + 4, lanes] += table[4 * column : 4 * column + 4]
        send[ROWS + L :] = small[...].astype(LOW)

    return pl.pallas_call(
        kernel,
        out_shape=[
            shaped((2, ROWS + L, D), LOW),
            shaped((ROWS + L + SMALL, D), LOW),
            shaped((SMALL, D), WIDE),
        ],
        in_specs=[SMEM] + [VMEM] * 8 + [ANY] * len(after),
        out_specs=[VMEM] * 3,
        scratch_shapes=[pltpu.VMEM((ROWS, D), LOW), pltpu.VMEM((16, 2 * L), WIDE)],
        compiler_params=limit(12),
        cost_estimate=cost(4),
        name="attend_back",
    )(info, attended, small_in, spread, w_out, *(saved[n] for n in ATTEND_SAVED), *after)


def finish_rows(info, total, output, pieces, matrices, picks, after):
    def kernel(info, *refs):
        totals, outputs, pieces = refs[0:2], refs[2:4], refs[4:6]
        (query, key, value), refs = refs[6:9], refs[9 + len(after) :]
        content_ends, query_ends, done = refs
        done[...] = jnp.zeros_like(done)
        first = info[2] == 1
        for seq in range(SEQS):
            lower = totals[seq][...] + nt(pieces[seq][0, :ROWS], query[...])
            upper = nt(pieces[seq][0, ROWS:], key[...]) + nt(pieces[seq][1, ROWS:], value[...])
            content_ends[seq * L : (seq + 1) * L] = jnp.where(
                first, lower[:L] + upper, outputs[seq][:L]
            )
            ends = jnp.where(first, lower[L : L + picks], outputs[seq][L : L + picks])
            for row in range(picks):
                query_ends[seq * picks + row] = ends[row : row + 1]

    return pl.pallas_call(
        kernel,
        out_shape=[shaped((ALL_CONTENT, D), WIDE), shaped((SEQS * picks, 1, D), WIDE), TOKEN],
        in_specs=[SMEM] + [VMEM] * 9 + [ANY] * len(after),
        out_specs=[VMEM] * 3,
        compiler_params=limit(12),
        cost_estimate=cost(3),
        name="finish_rows",
    )(info, *total, *output, *pieces, *matrices[:3], *after)


def attend_grads(info, pair, early, mine, arrived, small, after=()):
    def kernel(info, small, *refs):
        pairs_in, earlies, mines, arriveds = (refs[2 * i : 2 * i + 2] for i in range(4))
        refs = refs[8 + len(after) :]
        outs, extra, rest = refs[:5], refs[5], refs[6:]
        a_rows, a_content, b_rows, b_content, stage, out_sems = rest
        core, place = info[0], info[1]
        for seq in range(SEQS):
            at = slice(seq * ROWS, (seq + 1) * ROWS)
            far = slice((2 + seq) * ROWS, (3 + seq) * ROWS)
            a_rows[at] = pairs_in[seq][core]
            a_rows[far] = columns(earlies[seq], core * D, D)[...]
            b_rows[at] = mines[seq][core, :ROWS]
            b_rows[far] = arriveds[seq][:ROWS]
            at = slice(seq * L, (seq + 1) * L)
            far = slice((2 + seq) * L, (3 + seq) * L)
            a_content[at] = pairs_in[seq][0, :L]
            a_content[far] = earlies[seq][:L, :D]
            b_content[at] = mines[seq][core, ROWS:]
            b_content[far] = arriveds[seq][ROWS : ROWS + L]
        far_small = arriveds[1][ROWS + L :]
        extra[...] = (small[...] + far_small.astype(WIDE)).astype(LOW)
        sent = start_all([(extra, outs[i].at[2 * QUARTER :]) for i in range(2)], out_sems, 8)
        for block, (former, latter) in enumerate(((a_rows, b_rows), (a_content, b_content))):
            for part in range(3):
                stage[block, part * 256 : (part + 1) * 256] = tn(
                    former[:, part * 256 : (part + 1) * 256], latter[...]
                ).astype(LOW)
            for k in range(4):
                quarter = lax.rem(place + k, 4)
                index, part = PLACES[k, block]
                start = part * QUARTER
                sent += start_all(
                    [
                        (
                            rows_at(stage.at[block], quarter * QUARTER, QUARTER),
                            outs[index].at[start : start + QUARTER],
                        )
                    ],
                    out_sems,
                    block * 4 + k,
                )
        wait_all(sent)

    return pl.pallas_call(
        kernel,
        out_shape=term_shapes(QUARTER, SMALL) + [shaped((SMALL, D), LOW)],
        in_specs=[SMEM] + [VMEM] * 9 + [ANY] * len(after),
        out_specs=[ANY] * 5 + [VMEM],
        scratch_shapes=[
            pltpu.VMEM((2 * ALL_ROWS, D), LOW),
            pltpu.VMEM((2 * ALL_CONTENT, D), LOW),
            pltpu.VMEM((2 * ALL_ROWS, D), LOW),
            pltpu.VMEM((2 * ALL_CONTENT, D), LOW),
            pltpu.VMEM((2, D, D), LOW),
            DMA((10,)),
        ],
        compiler_params=limit(12),
        cost_estimate=cost(5),
        name="attend_grads",
    )(info, small, *pair, *early, *mine, *arrived, *after)


def small_kernel(body, name, shapes, inputs, after=(), info=None, through=()):
    first = [] if info is None else [info]
    given = len(first) + len(inputs)

    def kernel(*refs):
        outs = refs[given + len(after) + len(through) :]
        body(*refs[:given], *outs[: len(shapes)])

    return pl.pallas_call(
        kernel,
        out_shape=[shaped(shape, LOW) for shape in shapes]
        + [shaped(array.shape, array.dtype) for array in through],
        in_specs=[SMEM] * len(first)
        + [VMEM] * len(inputs)
        + [ANY] * (len(after) + len(through)),
        out_specs=[VMEM] * len(shapes) + [ANY] * len(through),
        input_output_aliases={
            given + len(after) + i: len(shapes) + i for i in range(len(through))
        },
        compiler_params=limit(8),
        cost_estimate=cost(1),
        name=name,
    )(*first, *inputs, *after, *through)


def total_of(*terms):
    return sum(term.astype(WIDE) for term in terms).astype(LOW)


def ring_add(after0, before1, from_left, from_right, after=()):
    count = after0.shape[0]
    extra = from_left.shape[0] - 2 * count

    def body(after0, before1, from_left, from_right, right, left):
        right[:count] = total_of(after0[...], from_left[:count])
        left[:count] = total_of(before1[...], from_right[:count])
        if extra:
            right[count:] = from_left[2 * count :]
            left[count:] = from_right[2 * count :]

    return small_kernel(
        body,
        "ring_add",
        [(count + extra, D)] * 2,
        (after0, before1, from_left, from_right),
        after,
    )


def ring_sum(info, own, left, right, from_left, from_right, after=(), small=()):
    count = own.shape[0] // 2
    part = count // 4
    extra = sum(array.shape[0] for array in small)

    def body(info, own, left, right, from_left, from_right, *outs):
        if extra:
            small, outs = outs[0], outs[1:]
            total = total_of(
                small[...], from_left[2 * count :], from_right[2 * count :], left[count:]
            )
        for k, out in enumerate(outs):
            at = pl.multiple_of(lax.rem(info[3] + k, 4) * part, 16)
            low, high = pl.ds(at, part), pl.ds(at + count, part)
            out[:part] = total_of(own[low], left[low], from_right[high])
            out[part : 2 * part] = total_of(own[high], from_left[high], right[low])
            if extra:
                out[2 * part :] = total

    return small_kernel(
        body,
        "ring_sum",
        [(2 * part + extra, D)] * 4,
        (own, left, right, from_left, from_right, *small),
        after,
        info,
    )


def add_all(name, terms, after=()):
    def body(*refs):
        refs[-1][...] = total_of(*(ref[...] for ref in refs[:-1]))

    return small_kernel(body, name, [terms[0].shape], terms, after)[0]


def hand_on(arrays, after):
    return small_kernel(lambda *refs: None, "hand_on", [], (), after, None, arrays)


def z_join(feed, feed_far, attend, attend_far):
    first = feed.shape[0]
    count = attend.shape[0] - SMALL

    def body(feed, feed_far, attend, attend_far, whole, small, table):
        whole[:first] = total_of(feed[...], feed_far[...])
        total = total_of(attend[...], attend_far[...])
        whole[first:] = total[:count]
        small[...] = total[count : count + S_TABLE]
        table[...] = total[count + S_TABLE :]

    shapes = [(first + count, D), (S_TABLE, D), (SMALL - S_TABLE, D)]
    return small_kernel(body, "z_join", shapes, (feed, feed_far, attend, attend_far))


def finish_small(small, table, far, after=()):
    places = [n for n in range(S_TABLE) if not S_EXPAND <= n < S_EXPAND + 4]

    def kernel(small, table, far, *refs):
        vectors, (b_expand, whole, done) = refs[len(after) : -3], refs[-3:]
        done[...] = jnp.zeros_like(done)
        values = small[...].astype(WIDE)
        for place, vector in zip(places, vectors):
            vector[...] = values[place : place + 1]
        for column in range(4):
            lanes = slice(column * D, (column + 1) * D)
            b_expand[:, lanes] = values[S_EXPAND + column : S_EXPAND + column + 1]
        total = table[...].astype(WIDE) + far[...].astype(WIDE)
        heads = [total[:, column * L : (column + 1) * L] for column in range(4)]
        whole[...] = jnp.concatenate(heads)[:H, :NB]

    *vectors, b_expand, whole, done = pl.pallas_call(
        kernel,
        out_shape=[shaped((1, D), WIDE)] * len(places)
        + [shaped((1, FF), WIDE), shaped((H, NB), WIDE), TOKEN],
        in_specs=[VMEM] * 3 + [ANY] * len(after),
        out_specs=[VMEM] * (len(places) + 3),
        compiler_params=limit(4),
        cost_estimate=cost(1),
        name="finish_small",
    )(small, table, far, *after)
    return dict(zip(places, vectors)), b_expand, whole, done


def inner_join(info, parts):
    counts = (QUARTER // 2, QUARTER // 4)
    half = 4 * sum(counts)

    def body(info, *refs):
        whole = refs[-1]
        start, given = 0, 0
        for count in counts:
            for k, ref in enumerate(refs[:-1]):
                at = pl.multiple_of(lax.rem(info[3] + k, 4) * count, 16) + start
                whole[pl.ds(at, count)] = ref[given : given + count]
                whole[pl.ds(at + half, count)] = ref[given + count : given + 2 * count]
            start, given = start + 4 * count, given + 2 * count

    return small_kernel(body, "inner_join", [(2 * half, D)], parts, (), info)[0]


def cut(before, after_part, after=()):
    count = before.shape[0] // 2

    def body(before, after_part, right, left, both):
        right[...] = before[:count]
        left[...] = after_part[count:]
        both[: 2 * count] = before[...]
        both[2 * count :] = after_part[...]

    shapes = [(count, D), (count, D), (4 * count, D)]
    return small_kernel(body, "cut", shapes, (before, after_part), after)


OUT_SHAPES = ((FF, D), (D, FF)) + ((D, D),) * 4


def out_places(outs, source, half, core, quarter):
    pairs = []
    for block in range(2):
        part = source.at[block * QUARTER : (block + 1) * QUARTER]
        if half == 0:
            target = rows_at(outs[0], core * HALF + block * D + quarter * QUARTER, QUARTER)
        else:
            target = columns(
                rows_at(outs[1], quarter * QUARTER, QUARTER), (core * 2 + block) * D, D
            )
        pairs.append((None, part, target))
    part = source.at[2 * QUARTER :]
    for number in range(2):
        target = rows_at(outs[2 + 2 * number + half], quarter * QUARTER, QUARTER)
        pairs.append((core == number, part, target))
    return pairs


def settle(info, pieces, outs, name, after=()):
    shapes, count = OUT_SHAPES, 3 * QUARTER
    keys = tuple(pieces)
    arrays = [pieces[key] for key in keys]
    given = list(after) + list(outs or ())

    def kernel(info, *refs):
        parts, rest = refs[: len(keys)], refs[len(keys) + len(given) :]
        outs, rest = rest[: len(shapes)], rest[len(shapes) :]
        done, rest = rest[0], rest[1:]
        done[...] = jnp.zeros_like(done)
        wide_held, out_sems = rest[:-1], rest[-1]
        finish = []
        for index, (sibling, places) in enumerate(keys):
            core = 1 - info[0] if sibling else info[0]
            for number, (k, half) in enumerate(places):
                quarter = lax.rem((info[3] if sibling else info[1]) + k, 4)
                source = wide_held[index].at[number * count : (number + 1) * count]
                source[...] = parts[index][number * count : (number + 1) * count].astype(WIDE)
                for place, (condition, part, target) in enumerate(
                    out_places(outs, source, half, core, quarter)
                ):
                    copy = pltpu.make_async_copy(
                        part, target, out_sems.at[16 * index + 4 * number + place]
                    )
                    if condition is None:
                        copy.start()
                        finish.append(copy.wait)
                    else:
                        pl.when(condition)(copy.start)
                        finish.append(lambda c=copy, when=condition: pl.when(when)(c.wait))
        for action in finish:
            action()

    result = pl.pallas_call(
        kernel,
        out_shape=[shaped(shape, WIDE) for shape in shapes]
        + [TOKEN],
        in_specs=[SMEM] + [VMEM] * len(keys) + [ANY] * len(given),
        out_specs=[ANY] * len(shapes) + [VMEM],
        scratch_shapes=[pltpu.VMEM(array.shape, WIDE) for array in arrays]
        + [DMA((16 * len(keys),))],
        input_output_aliases={
            1 + len(keys) + len(after) + i: i for i in range(len(outs or ()))
        },
        compiler_params=limit(20),
        cost_estimate=cost(sum(array.size for array in arrays) * 2e-6 + 1),
        name=name,
    )(info, *arrays, *given)
    return result[:-1], result[-1]


PLANE = ("x", "y", "c")


def shift(value, axis, by):
    size = lax.axis_size(axis)
    return lax.ppermute(value, axis, [(i, (i + by) % size) for i in range(size)])


def send(value, by):
    return lax.ppermute(value, "s", [(0, 1)] if by > 0 else [(1, 0)])


def turn(value, outer, by):
    pairs = []
    for i in range(4):
        for j in range(4):
            for c in range(2):
                if (c == 0) == outer:
                    target = ((i + by) % 4, j)
                else:
                    target = (i, (j + by) % 4)
                pairs.append(((i * 4 + j) * 2 + c, (target[0] * 4 + target[1]) * 2 + c))
    return lax.ppermute(value, PLANE, pairs)


def place(outer):
    return jnp.where(
        (lax.axis_index("c") == 0) == outer, lax.axis_index("x"), lax.axis_index("y")
    )


def wide(value):
    return value.astype(WIDE)


def total_wide(*terms):
    return sum(wide(term) for term in terms)


def inner_turns(parts, sign):
    return [turn(part, False, sign * by) for part, by in zip(parts, (1, 2, -1))]


OWN, ACROSS = ((0, 0), (0, 1)), (((2, 0),), ((2, 1),))
NEAR = ((3, 0), (3, 1), (1, 0), (1, 1))


def both_cores(places, piece):
    return {(0, places): piece, (1, places): shift(piece, "c", 1)}


def on_device(
    content_in,
    query_in,
    content_cot,
    query_cot,
    order_rank,
    query_pos,
    group_tag,
    *rest,
):
    (
        w_query,
        b_query,
        w_key,
        w_value,
        b_value,
        w_out,
        b_out,
        norm1_gain,
        norm1_bias,
        w_expand,
        b_expand,
        w_contract,
        b_contract,
        norm2_gain,
        norm2_bias,
    ) = (argument[0] for argument in rest[:-1])
    rel_table = rest[-1]
    core = lax.axis_index("c")
    first_section = (lax.axis_index("s") == 0).astype(jnp.int32)
    info = jnp.stack([core, place(True), first_section, place(False)])
    picks = query_pos.shape[1]

    matrices = (w_query, w_key, w_value, w_out, w_expand, w_contract)
    w_out_held = w_out
    vec = jnp.stack(
        [b_query, b_value, b_out, norm1_gain, norm1_bias, b_contract, norm2_gain, norm2_bias]
    )
    ranks = jnp.concatenate([order_rank, group_tag, query_pos], axis=1)
    masks, spread, query_in, query_cot = prepare(
        ranks, rel_table.T, jnp.concatenate([query_in, query_cot]), picks, (vec, info)
    )
    b_expand = b_expand[None]

    fronts, arrived = [], []
    for seq in range(SEQS):
        given = (seq, info, content_in, query_in, matrices, masks, vec, b_expand)
        fronts.append(front(*given, tuple(fronts)) if fronts else front_parts(*given))
        arrived.append(send(fronts[seq], 1))
    output, early, pair, saved, grads = [], [], [], [], []
    for seq in range(SEQS):
        results = middle_forward(
            seq, info, content_in, query_in, arrived[seq], matrices, masks, vec, b_expand, tuple(grads)
        )
        for collected, result in zip((output, early, pair, saved), results):
            collected.append(result)
        grads.append(middle_back(seq, info, content_cot, query_cot, matrices, vec, saved[seq]))
    early = [shift(value, "c", 1) for value in early]
    grads = [send(value, -1) for value in grads]
    small = None
    total, branch, attended, own, late, pieces, pass_on = [], [], [], [], [], [], []
    for seq in range(SEQS):
        results = feed_back(
            seq,
            info,
            grads[seq],
            content_cot,
            query_cot,
            small,
            vec,
            matrices,
            saved[seq],
            tuple(pass_on),
        )
        small = results[3]
        for collected, result in zip(
            (total, branch, attended, own, late), results[:3] + results[4:]
        ):
            collected.append(result)
        late[seq] = shift(late[seq], "c", 1)
        results = attend_back(
            seq,
            info,
            attended[seq],
            small,
            spread,
            (),
            w_out_held,
            saved[seq],
        )
        small = results[2]
        pieces.append(results[0])
        pass_on.append(results[1])
    feed_terms = feed_grads(info, saved, branch, own, early, late, (small,))
    passed = [shift(value, "c", 1) for value in pass_on]

    def outer_step(terms):
        return (turn(terms[0], True, 1), turn(terms[1], True, -1))

    f_left, f_right = outer_step(feed_terms)
    *attend_terms, extra = attend_grads(info, pair, early, pieces, passed, small, (feed_terms[4],))
    a_left, a_right = outer_step(attend_terms)
    f_sent = ring_add(feed_terms[2], feed_terms[3], f_left, f_right, (extra,))
    f_outer = outer_step(f_sent)
    a_sent = ring_add(attend_terms[2], attend_terms[3], a_left, a_right)
    f_parts = ring_sum(info, feed_terms[4], *f_outer, f_left, f_right, (a_sent[0],))
    f_others = inner_turns(f_parts[1:], 1)
    a_parts = ring_sum(
        info, attend_terms[4], *outer_step(a_sent), a_left, a_right, (f_parts[0],), (extra,)
    )
    f_part = add_all("inner_sum", [f_parts[0]] + f_others, (a_parts[0],))
    f_far = shift(f_part, "z", 1)
    a_part = add_all("inner_sum", [a_parts[0]] + inner_turns(a_parts[1:], 1), (f_part,))
    a_far = shift(a_part, "z", 1)
    part, small, table = z_join(f_part, f_far, a_part, a_far)
    own = inner_join(info, [part] + inner_turns([part] * 3, -1))
    before, after_part = turn(own, True, 1), turn(own, True, -1)
    content_ends, query_ends, token = finish_rows(
        info, total, output, pieces, matrices, picks, (own,)
    )
    row, b_expand, table, small_token = finish_small(small, table, shift(table, "s", 1), (own,))
    outs, own_token = settle(info, both_cores(OWN, own), None, "own_out")
    to_right, to_left, near = cut(before, after_part, (token, small_token, own_token))
    across = (turn(to_right, True, 1), turn(to_left, True, -1))
    outs, near_token = settle(info, {(0, NEAR): near}, outs, "near_out")
    outs, far_token = settle(info, {(1, NEAR): shift(near, "c", 1)}, outs, "near_out")
    across = hand_on(across, (near_token, far_token))
    own = {(0, places): piece for places, piece in zip(ACROSS, across)}
    far = {(1, places): shift(piece, "c", 1) for places, piece in zip(ACROSS, across)}
    outs, _ = settle(info, own, outs, "across_out")
    outs, _ = settle(info, far, outs, "across_out")
    contract, expand, g_query, g_key, g_out, g_value = outs
    return (
        content_ends[None],
        query_ends.transpose(1, 0, 2),
        g_query[None],
        row[S_QUERY],
        g_key[None],
        g_value[None],
        row[S_VALUE],
        g_out[None],
        row[S_OUT],
        row[S_GAIN1],
        row[S_SHIFT1],
        expand[None],
        b_expand,
        contract[None],
        row[S_CONTRACT],
        row[S_GAIN2],
        row[S_SHIFT2],
        table.T,
    )


DP = ("z", "x", "y", "c")


def solution(mesh):
    mesh = jax.sharding.Mesh(mesh.devices.reshape(2, 2, 4, 4, 2), ("s",) + DP)
    layer_specs = tuple(
        P("s", *([None] * (rank - 1))) for rank in (3, 2, 3, 3, 2, 3, 2, 2, 2, 3, 2, 3, 2, 2, 2)
    )
    in_specs = (P(DP, None),) * 7 + layer_specs + (P(),)
    out_specs = (P("s", DP, None),) * 2 + layer_specs + (P(),)
    return jax.shard_map(
        on_device, mesh=mesh, in_specs=in_specs, out_specs=out_specs, check_vma=False
    )
```

```python
import jax
import jax.numpy as jnp
from jax import lax
from jax.experimental import pallas as pl
from jax.experimental.pallas import tpu as pltpu
from jax.sharding import PartitionSpec as P

D = 768
H = 12
HD = 64
FF = 3072
NB = 32
L = 128
PAIRS = H // 2
SEQS = 2
PICKS = 32
ROWS = L + PICKS
EPSILON = 1e-05
SCALE = HD ** (-0.5)
TILE = 1536
LOW = jnp.bfloat16
WIDE = jnp.float32
HALF = FF // 2
QUARTER = D // 4
EARLY = 3 * D + HALF
LATE = D + HALF
SMALL = 16
ALL_ROWS = SEQS * ROWS
ALL_CONTENT = SEQS * L
PIECE = ALL_ROWS + ALL_CONTENT


def nn(former, latter):
    return lax.dot_general(
        former, latter, (((1,), (0,)), ((), ())), preferred_element_type=WIDE
    )


def nt(former, latter):
    return lax.dot_general(
        former, latter, (((1,), (1,)), ((), ())), preferred_element_type=WIDE
    )


def tn(former, latter):
    return lax.dot_general(
        former, latter, (((0,), (0,)), ((), ())), preferred_element_type=WIDE
    )


def halves(value):
    even = lax.broadcasted_iota(jnp.int32, value.shape, 1) < HD
    zero = jnp.zeros_like(value)
    return jnp.concatenate([jnp.where(even, value, zero), jnp.where(even, zero, value)])


def side(value):
    count = value.shape[0] // 2
    return jnp.concatenate([value[:count], value[count:]], axis=1)


def norm_rows(values):
    centered = values - jnp.mean(values, axis=-1, keepdims=True)
    variance = jnp.mean(centered * centered, axis=-1, keepdims=True)
    root = lax.rsqrt(variance + EPSILON)
    return (centered * root, root)


def norm_rows_back(scaled, normed, root):
    return root * (
        scaled
        - jnp.mean(scaled, axis=-1, keepdims=True)
        - normed * jnp.mean(scaled * normed, axis=-1, keepdims=True)
    )


B_QUERY, B_VALUE, B_OUT, GAIN1, SHIFT1, B_CONTRACT, GAIN2, SHIFT2 = range(8)
S_QUERY, S_VALUE, S_OUT, S_GAIN1, S_SHIFT1, S_EXPAND = range(6)
S_CONTRACT, S_GAIN2, S_SHIFT2, S_TABLE = 9, 10, 11, 12
LIMITS = (12, 16, 23, 32, 46, 64, 91)


def bucket_of(relative):
    distance = jnp.abs(relative)
    beyond = 8 + sum((distance >= limit).astype(jnp.int32) for limit in LIMITS)
    within = jnp.where(distance < 8, distance, beyond)
    return within + 16 * (relative > 0).astype(jnp.int32)


def forward_attend(x, w, vec, masks, s, keep):
    row = lambda k: vec[k : k + 1, :]
    s.query[...] = (nn(x[...], w.query[...]) + row(B_QUERY)).astype(LOW)
    s.key[...] = nn(x[:L], w.key[...]).astype(LOW)
    s.value[...] = (nn(x[:L], w.value[...]) + row(B_VALUE)).astype(LOW)
    for pair in range(PAIRS):
        lanes = slice(pair * 128, (pair + 1) * 128)
        scores = nt(halves(s.query[:, lanes]), s.key[:, lanes]) * SCALE + masks[pair]
        shifted = jnp.exp(scores - jnp.max(scores, axis=-1, keepdims=True))
        probs = (shifted / jnp.sum(shifted, axis=-1, keepdims=True)).astype(LOW)
        if keep:
            s.probs[pair] = probs
        s.mixed[:, lanes] = nn(side(probs), halves(s.value[:, lanes])).astype(LOW)
    total = x[...].astype(WIDE) + nn(s.mixed[...], w.out[...]) + row(B_OUT)
    normed, root = norm_rows(total)
    first = normed * row(GAIN1) + row(SHIFT1)
    s.first_low[...] = first.astype(LOW)
    s.total[...] = first + row(B_CONTRACT)
    if keep:
        s.normed1[...] = normed
        s.root1[...] = jnp.broadcast_to(root, (ROWS, 128))


def forward_feed(w, vec, b_expand, s, keep):
    row = lambda k: vec[k : k + 1, :]
    for tile in range(FF // TILE):
        tile = slice(tile * TILE, (tile + 1) * TILE)
        expanded = nn(s.first_low[...], w.expand[:, tile]) + b_expand[:, tile]
        cumulative = 0.5 * (1.0 + lax.erf(expanded * 0.7071067811865476))
        activated = (expanded * cumulative).astype(LOW)
        if keep:
            s.slope[:, tile] = (
                cumulative + expanded * jnp.exp(-0.5 * expanded * expanded) * 0.3989422804014327
            ).astype(LOW)
            s.activated[:, tile] = activated
        s.total[...] += nn(activated, w.contract[tile, :])
    normed, root = norm_rows(s.total[...])
    if keep:
        s.normed2[...] = normed
        s.root2[...] = jnp.broadcast_to(root, (ROWS, 128))
    s.out[...] = (normed * row(GAIN2) + row(SHIFT2)).astype(s.out.dtype)


def column_sum(value):
    return jnp.sum(value.astype(WIDE), axis=0, keepdims=True)


def back_second_norm(grad, vec, s, add=None):
    upper = grad.astype(WIDE)
    normed = s.normed2[...]
    lower = norm_rows_back(upper * vec[GAIN2 : GAIN2 + 1, :], normed, s.root2[:, :1])
    s.total[...] = lower
    s.branch[...] = lower.astype(LOW)
    if add is not None:
        add(S_GAIN2, column_sum(upper * normed))
        add(S_SHIFT2, column_sum(upper))
        add(S_CONTRACT, column_sum(lower.astype(LOW)))


def back_feed(w, vec, s, add=None):
    for tile in range(FF // TILE):
        tile = slice(tile * TILE, (tile + 1) * TILE)
        lower = (nt(s.branch[...], w.contract[tile, :]) * s.slope[:, tile].astype(WIDE)).astype(LOW)
        s.expanded[:, tile] = lower
        if add is not None:
            part = column_sum(lower)
            for column in range(TILE // D):
                add(
                    S_EXPAND + tile.start // D + column,
                    part[:, column * D : (column + 1) * D],
                )
        s.total[...] += nt(lower, w.expand[:, tile])
    upper = s.total[...]
    normed = s.normed1[...]
    lower = norm_rows_back(upper * vec[GAIN1 : GAIN1 + 1, :], normed, s.root1[:, :1])
    s.total[...] = lower
    s.attended[...] = lower.astype(LOW)
    if add is not None:
        add(S_GAIN1, column_sum(upper * normed))
        add(S_SHIFT1, column_sum(upper))
        add(S_OUT, column_sum(lower.astype(LOW)))


def back_attend(s, table=None):
    for pair in range(PAIRS):
        lanes = slice(pair * 128, (pair + 1) * 128)
        probs = s.probs[pair]
        below = halves(s.dmixed[:, lanes])
        dprobs = nt(below, s.value[:, lanes])
        s.dvalue[:, lanes] = tn(probs, below).astype(LOW)
        weight = probs.astype(WIDE)
        dscores = (
            weight * (dprobs - jnp.sum(weight * dprobs, axis=-1, keepdims=True))
        ).astype(LOW)
        s.dquery[:, lanes] = (nn(side(dscores), halves(s.key[:, lanes])) * SCALE).astype(LOW)
        s.dkey[:, lanes] = (tn(dscores, halves(s.query[:, lanes])) * SCALE).astype(LOW)
        if table is not None:
            table(pair, dscores)


class Names:
    def __init__(self, **named):
        self.__dict__.update(named)


MATRICES = ("query", "key", "value", "out", "expand", "contract")
MATRIX_SHAPES = {
    "query": (D, D),
    "key": (D, D),
    "value": (D, D),
    "out": (D, D),
    "expand": (D, FF),
    "contract": (FF, D),
}
MASK_SHAPE = (PAIRS, 2 * ROWS, L)
KEPT = {
    "query": ((ROWS, D), LOW),
    "key": ((L, D), LOW),
    "value": ((L, D), LOW),
    "probs": (MASK_SHAPE, LOW),
    "mixed": ((ROWS, D), LOW),
    "normed1": ((ROWS, D), WIDE),
    "root1": ((ROWS, 128), WIDE),
    "first_low": ((ROWS, D), LOW),
    "slope": ((ROWS, FF), LOW),
    "activated": ((ROWS, FF), LOW),
    "normed2": ((ROWS, D), WIDE),
    "root2": ((ROWS, 128), WIDE),
}
SAVED = tuple(name for name in KEPT if name != "mixed")
ANY = pl.BlockSpec(memory_space=pl.ANY)
HBM = pl.BlockSpec(memory_space=pltpu.HBM)
VMEM = pl.BlockSpec(memory_space=pltpu.VMEM)
SMEM = pl.BlockSpec(memory_space=pltpu.SMEM)


def limit(megabytes):
    return pltpu.CompilerParams(vmem_limit_bytes=megabytes * 1024 * 1024)


DMA = pltpu.SemaphoreType.DMA


def cost(microseconds):
    return pl.CostEstimate(flops=0, bytes_accessed=int(microseconds * 3.2e6), transcendentals=0)


def shaped(shape, kind):
    return jax.ShapeDtypeStruct(shape, kind)


TOKEN = shaped((8, 128), WIDE)


def columns(ref, start, size):
    return ref.at[:, pl.ds(pl.multiple_of(start, 128), size)]


def rows_at(ref, start, size):
    return ref.at[pl.ds(pl.multiple_of(start, 64), size)]


def start_all(pairs, sems, base=0):
    copies = [
        pltpu.make_async_copy(source, target, sems.at[base + index])
        for index, (source, target) in enumerate(pairs)
    ]
    for copy in copies:
        copy.start()
    return copies


def wait_all(copies):
    for copy in copies:
        copy.wait()


def fetcher(names, sources, targets, sems, base=0):
    copies = dict(zip(names, start_all(list(zip(sources, targets)), sems, base)))
    return lambda name: copies[name].wait()


def prepare(ranks, table, queries, picks, after):
    def kernel(ranks, table, queries, *refs):
        masks, spread, rows_in, rows_cot = refs[len(after) :]
        order, tag, pos = ranks[:, :L], ranks[:, L : 2 * L], ranks[:, 2 * L : 2 * L + picks]
        values = queries[...].astype(WIDE)
        blank = jnp.zeros((PICKS - picks, D), WIDE)
        for index, target in enumerate((rows_in, rows_cot)):
            own = values[2 * index * picks : 2 * (index + 1) * picks]
            target[...] = jnp.concatenate([own[:picks], blank, own[picks:], blank]).astype(LOW)
        lane = lax.broadcasted_iota(jnp.int32, (L, L), 1)
        level = lax.broadcasted_iota(jnp.int32, (L, L), 0)
        lane_q = lax.broadcasted_iota(jnp.int32, (PICKS, L), 1)
        upright = lambda row: jnp.sum(jnp.where(lane == level, row, 0.0), axis=1, keepdims=True)
        distance = lax.broadcasted_iota(jnp.int32, (2 * L, NB), 0) - (L - 1)
        bucket = lax.broadcasted_iota(jnp.int32, (2 * L, NB), 1)
        by_distance = lax.dot_general(
            table[...],
            (bucket_of(distance) == bucket).astype(WIDE),
            (((1,), (1,)), ((), ())),
            precision=lax.Precision.HIGHEST,
            preferred_element_type=WIDE,
        )
        allowed, hot = [], []
        for seq in range(SEQS):
            own_rank = order[seq : seq + 1, :].astype(WIDE)
            own_tag = tag[seq : seq + 1, :].astype(WIDE)
            own_pos = pos[seq : seq + 1, :].astype(WIDE)
            number = lax.broadcasted_iota(jnp.int32, (PICKS, picks), 0)
            same = number == lax.broadcasted_iota(jnp.int32, (PICKS, picks), 1)
            place = jnp.sum(jnp.where(same, own_pos, 0.0), axis=1, keepdims=True)
            filled = lax.broadcasted_iota(jnp.int32, (PICKS, 1), 0) < picks
            place = jnp.where(filled, place, -1.0).astype(jnp.int32)
            matches = place == lane_q
            marks = jnp.where(matches, 1.0, 0.0)
            predicted = jnp.max(marks, axis=0, keepdims=True)
            rank = jnp.sum(jnp.where(matches, own_rank, 0.0), axis=1, keepdims=True)
            group = jnp.sum(jnp.where(matches, own_tag, 0.0), axis=1, keepdims=True)
            earlier = (upright(predicted) > 0) & (own_rank <= upright(own_rank))
            content = (upright(own_tag) == own_tag) & ((predicted == 0) | earlier)
            query = (group == own_tag) & ((predicted == 0) | (own_rank + 1 <= rank))
            allowed.append((content, query))
            hot.append(marks)
            spread[seq, :L] = jnp.where(lane == L - 1 - level, 1.0, 0.0).astype(LOW)
            spread[seq, L:] = jnp.where(lane_q == L - 1 - place, 1.0, 0.0).astype(LOW)
        hot = jnp.concatenate(hot)
        for head in range(H):
            row = jnp.broadcast_to(by_distance[head : head + 1], (L, 2 * L))
            bias = pltpu.roll(row, L + 1, 1, stride=1, stride_axis=0)[:, :L]
            bias_q = lax.dot_general(
                hot,
                bias,
                (((1,), (0,)), ((), ())),
                precision=lax.Precision.HIGHEST,
                preferred_element_type=WIDE,
            )
            base = head % 2 * ROWS
            for seq in range(SEQS):
                content, query = allowed[seq]
                masks[seq, head // 2, base : base + L] = jnp.where(content, bias, -1e30)
                masks[seq, head // 2, base + L : base + ROWS] = jnp.where(
                    query, bias_q[seq * PICKS : (seq + 1) * PICKS], -1e30
                )

    return pl.pallas_call(
        kernel,
        out_shape=[
            shaped((SEQS,) + MASK_SHAPE, WIDE),
            shaped((SEQS, ROWS, L), LOW),
            shaped((SEQS * PICKS, D), LOW),
            shaped((SEQS * PICKS, D), LOW),
        ],
        in_specs=[VMEM] * 3 + [ANY] * len(after),
        out_specs=[VMEM] * 4,
        compiler_params=limit(8),
        cost_estimate=pl.CostEstimate(flops=int(3e10), bytes_accessed=0, transcendentals=0),
        name="prepare",
    )(ranks, table, queries, *after)


def only(condition, work, *outs):
    pl.when(condition)(work)

    @pl.when(jnp.logical_not(condition))
    def _():
        for out in outs:
            out[...] = jnp.zeros_like(out)


def take_rows(content, picks, seq, target):
    target[:L] = content[seq * L : (seq + 1) * L]
    target[L:] = picks[seq * PICKS : (seq + 1) * PICKS]


def front(seq, info, content, picks, matrices, masks, vec, b_expand, after=()):
    def kernel(info, content, picks, masks, vec, b_expand, *refs):
        w = Names(**dict(zip(MATRICES, refs[:6])))
        out, x, query, key, value, mixed, first_low, total = refs[6 + len(after) :]
        s = Names(
            query=query,
            key=key,
            value=value,
            mixed=mixed,
            first_low=first_low,
            total=total,
            out=out,
        )

        def work():
            take_rows(content, picks, seq, x)
            forward_attend(x, w, vec, masks.at[seq], s, False)
            forward_feed(w, vec, b_expand, s, False)

        only(info[2] == 1, work, out)

    return pl.pallas_call(
        kernel,
        out_shape=shaped((ROWS, D), LOW),
        in_specs=[SMEM] + [VMEM] * 11 + [ANY] * len(after),
        out_specs=VMEM,
        scratch_shapes=[pltpu.VMEM((ROWS, D), LOW)]
        + [pltpu.VMEM(*KEPT[n]) for n in ("query", "key", "value", "mixed", "first_low")]
        + [pltpu.VMEM((ROWS, D), WIDE)],
        compiler_params=limit(12),
        cost_estimate=cost(5),
        name="front",
    )(info, content, picks, masks, vec, b_expand, *matrices, *after)


def front_parts(seq, info, content, picks, matrices, masks, vec, b_expand):
    def first(info, content, picks, masks, vec, *refs):
        w = Names(**dict(zip(MATRICES[:4], refs[:4])))
        first_low, total, x, query, key, value, mixed = refs[4:]
        s = Names(
            query=query, key=key, value=value, mixed=mixed, first_low=first_low, total=total
        )

        def work():
            take_rows(content, picks, seq, x)
            forward_attend(x, w, vec, masks.at[seq], s, False)

        only(info[2] == 1, work, first_low, total)

    def second(info, first_low, total_in, vec, b_expand, expand, contract, out, total):
        s = Names(first_low=first_low, total=total, out=out)

        def work():
            total[...] = total_in[...]
            forward_feed(Names(expand=expand, contract=contract), vec, b_expand, s, False)

        only(info[2] == 1, work, out)

    first_low, total = pl.pallas_call(
        first,
        out_shape=[shaped((ROWS, D), LOW), shaped((ROWS, D), WIDE)],
        in_specs=[SMEM] + [VMEM] * 8,
        out_specs=[VMEM] * 2,
        scratch_shapes=[pltpu.VMEM((ROWS, D), LOW)]
        + [pltpu.VMEM(*KEPT[n]) for n in ("query", "key", "value", "mixed")],
        compiler_params=limit(8),
        cost_estimate=pl.CostEstimate(flops=int(1e10), bytes_accessed=0, transcendentals=0),
        name="front_attend",
    )(info, content, picks, masks, vec, *matrices[:4])
    return pl.pallas_call(
        second,
        out_shape=shaped((ROWS, D), LOW),
        in_specs=[SMEM] + [VMEM] * 6,
        out_specs=VMEM,
        scratch_shapes=[pltpu.VMEM((ROWS, D), WIDE)],
        compiler_params=limit(12),
        cost_estimate=cost(2),
        name="front_feed",
    )(info, first_low, total, vec, b_expand, *matrices[4:])


def middle_forward(seq, info, content, picks, arrived, matrices, masks, vec, b_expand, after=()):
    def kernel(info, arrived, content, picks, masks, vec, b_expand, *refs):
        w, rest = Names(**dict(zip(MATRICES, refs[:6]))), refs[6 + len(after) :]
        (out, early, pair), kept = rest[:3], rest[3 : 3 + len(SAVED)]
        mixed, total = rest[3 + len(SAVED) :]
        x = pair.at[0]
        s = Names(total=total, out=out, mixed=mixed, **dict(zip(SAVED, kept)))
        take_rows(content, picks, seq, x)
        x[...] = jnp.where(info[2] == 1, x[...], arrived[...])
        early[:, :D] = x[...]
        forward_attend(x, w, vec, masks.at[seq], s, True)
        forward_feed(w, vec, b_expand, s, True)
        pair[1] = mixed[...]
        early[:, D : 2 * D] = mixed[...]
        early[:, 2 * D : 3 * D] = s.first_low[...]
        early[:, 3 * D :] = columns(s.activated, (1 - info[0]) * HALF, HALF)[...]

    out, early, pair, *saved = pl.pallas_call(
        kernel,
        out_shape=[
            shaped((ROWS, D), WIDE),
            shaped((ROWS, EARLY), LOW),
            shaped((2, ROWS, D), LOW),
        ]
        + [shaped(*KEPT[n]) for n in SAVED],
        in_specs=[SMEM] + [VMEM] * 12 + [ANY] * len(after),
        out_specs=[VMEM] * (3 + len(SAVED)),
        scratch_shapes=[pltpu.VMEM(*KEPT["mixed"]), pltpu.VMEM((ROWS, D), WIDE)],
        compiler_params=limit(16),
        cost_estimate=cost(6),
        name="middle_forward",
    )(info, arrived, content, picks, masks, vec, b_expand, *matrices, *after)
    return (out, early, pair, dict(zip(SAVED, saved)))


FEED_SAVED = ("normed2", "root2", "slope", "normed1", "root1")
ATTEND_SAVED = ("value", "probs", "key", "query")


def middle_back(seq, info, content, picks, matrices, vec, saved):
    names = FEED_SAVED + ATTEND_SAVED

    def kernel(info, content, picks, vec, *refs):
        w, rest = Names(**dict(zip(MATRICES, refs[:6]))), refs[6:]
        kept, grad, rest = rest[: len(names)], rest[len(names)], rest[len(names) + 1 :]
        cot, total, branch, expanded, attended, dmixed, dvalue, dquery, dkey = rest
        s = Names(
            total=total,
            branch=branch,
            expanded=expanded,
            attended=attended,
            dmixed=dmixed,
            dvalue=dvalue,
            dquery=dquery,
            dkey=dkey,
            **dict(zip(names, kept)),
        )
        take_rows(content, picks, seq, cot)
        back_second_norm(cot[...], vec, s)
        back_feed(w, vec, s)
        dmixed[...] = nt(attended[...], w.out[...]).astype(LOW)
        back_attend(s)
        lower = total[...] + nt(dquery[...], w.query[...])
        upper = nt(dkey[...], w.key[...]) + nt(dvalue[...], w.value[...])
        grad[:L] = (lower[:L] + upper).astype(LOW)
        grad[L:] = lower[L:].astype(LOW)

    return pl.pallas_call(
        kernel,
        out_shape=shaped((ROWS, D), LOW),
        in_specs=[SMEM] + [VMEM] * (9 + len(names)),
        out_specs=VMEM,
        scratch_shapes=[
            pltpu.VMEM((ROWS, D), LOW),
            pltpu.VMEM((ROWS, D), WIDE),
            pltpu.VMEM((ROWS, D), LOW),
            pltpu.VMEM((ROWS, FF), LOW),
            pltpu.VMEM((ROWS, D), LOW),
            pltpu.VMEM((ROWS, D), LOW),
            pltpu.VMEM((L, D), LOW),
            pltpu.VMEM((ROWS, D), LOW),
            pltpu.VMEM((L, D), LOW),
        ],
        compiler_params=limit(12),
        cost_estimate=cost(7),
        name="middle_back",
    )(info, content, picks, vec, *matrices, *(saved[n] for n in names))


def feed_back(seq, info, arrived, content, picks, small_in, vec, matrices, saved, after=()):
    given = [] if small_in is None else [small_in]

    def kernel(info, arrived, content, picks, vec, expand, contract, *refs):
        kept, rest = refs[:5], refs[5 + len(given) + len(after) :]
        total, branch, attended, small, own, late, upper, expanded = rest
        w = Names(expand=expand, contract=contract)
        s = Names(
            total=total,
            branch=branch,
            attended=attended,
            expanded=expanded,
            **dict(zip(FEED_SAVED, kept)),
        )
        small[...] = refs[5][...] if given else jnp.zeros_like(small)

        def add(place, value):
            small[place : place + 1, :] += value

        take_rows(content, picks, seq, upper)
        back_second_norm(jnp.where(info[2] == 1, arrived[...], upper[...]), vec, s, add)
        late[:, :D] = branch[...]
        back_feed(w, vec, s, add)
        own[...] = columns(expanded, info[0] * HALF, HALF)[...]
        late[:, D:] = columns(expanded, (1 - info[0]) * HALF, HALF)[...]

    return pl.pallas_call(
        kernel,
        out_shape=[
            shaped((ROWS, D), WIDE),
            shaped((ROWS, D), LOW),
            shaped((ROWS, D), LOW),
            shaped((SMALL, D), WIDE),
            shaped((ROWS, HALF), LOW),
            shaped((ROWS, LATE), LOW),
        ],
        in_specs=[SMEM] + [VMEM] * (11 + len(given)) + [ANY] * len(after),
        out_specs=[VMEM] * 6,
        scratch_shapes=[pltpu.VMEM((ROWS, D), LOW), pltpu.VMEM((ROWS, FF), LOW)],
        compiler_params=limit(12),
        cost_estimate=cost(4),
        name="feed_back",
    )(
        info,
        arrived,
        content,
        picks,
        vec,
        matrices[4],
        matrices[5],
        *(saved[n] for n in FEED_SAVED),
        *given,
        *after,
    )


PLACES = {
    (2, 0): (0, 0),
    (1, 1): (0, 1),
    (2, 1): (1, 0),
    (3, 0): (1, 1),
    (1, 0): (2, 0),
    (3, 1): (3, 0),
    (0, 0): (4, 0),
    (0, 1): (4, 1),
}


def term_shapes(count, extra=0):
    rows = (2 * count + extra, 2 * count + extra, count, count, 2 * count)
    return [shaped((n, D), LOW) for n in rows]


def feed_grads(info, mine, branch, own, early, late, after=()):
    def kernel(info, *refs):
        acts, lows, branches, owns, earlies, lates = (refs[2 * i : 2 * i + 2] for i in range(6))
        refs = refs[:12] + refs[12 + len(after) :]
        outs, (a_act, a_first, b_branch, b_own, stage, out_sems) = refs[12:17], refs[17:]
        core, place = info[0], info[1]
        own_at = [slice(seq * ROWS, (seq + 1) * ROWS) for seq in range(SEQS)]
        far_at = [slice((2 + seq) * ROWS, (3 + seq) * ROWS) for seq in range(SEQS)]
        for seq in range(SEQS):
            at, far = own_at[seq], far_at[seq]
            a_act[at] = columns(acts[seq], core * HALF, HALF)[...]
            a_act[far] = earlies[seq][:, 3 * D :]
            b_branch[at] = branches[seq][...]
            b_branch[far] = lates[seq][:, :D]
        sent = []

        def send(block):
            for k in range(4):
                quarter = lax.rem(place + k, 4)
                index, part = PLACES[k, block // 2]
                start = (2 * part + block % 2) * QUARTER
                sent.extend(
                    start_all(
                        [
                            (
                                rows_at(stage.at[block], quarter * QUARTER, QUARTER),
                                outs[index].at[start : start + QUARTER],
                            )
                        ],
                        out_sems,
                        block * 4 + k,
                    )
                )

        for block in range(2):
            for part in range(3):
                start = block * D + part * 256
                stage[block, part * 256 : (part + 1) * 256] = tn(
                    a_act[:, start : start + 256], b_branch[...]
                ).astype(LOW)
            send(block)
        for seq in range(SEQS):
            at, far = own_at[seq], far_at[seq]
            a_first[at] = lows[seq][...]
            a_first[far] = earlies[seq][:, 2 * D : 3 * D]
            b_own[at] = owns[seq][...]
            b_own[far] = lates[seq][:, D:]
        for block in range(2):
            for part in range(3):
                stage[2 + block, part * 256 : (part + 1) * 256] = tn(
                    a_first[:, part * 256 : (part + 1) * 256], b_own[:, block * D : (block + 1) * D]
                ).astype(LOW)
            send(2 + block)
        wait_all(sent)

    acts = [saved["activated"] for saved in mine]
    lows = [saved["first_low"] for saved in mine]
    return pl.pallas_call(
        kernel,
        out_shape=term_shapes(2 * QUARTER),
        in_specs=[SMEM] + [VMEM] * 12 + [ANY] * len(after),
        out_specs=[ANY] * 5,
        scratch_shapes=[
            pltpu.VMEM((2 * ALL_ROWS, HALF), LOW),
            pltpu.VMEM((2 * ALL_ROWS, D), LOW),
            pltpu.VMEM((2 * ALL_ROWS, D), LOW),
            pltpu.VMEM((2 * ALL_ROWS, HALF), LOW),
            pltpu.VMEM((4, D, D), LOW),
            DMA((16,)),
        ],
        compiler_params=limit(16),
        cost_estimate=cost(8),
        name="feed_grads",
    )(info, *acts, *lows, *branch, *own, *early, *late, *after)


def attend_back(seq, info, attended, small_in, spread, after, w_out, saved):
    def kernel(info, attended, small_in, spread, w_out, *refs):
        kept, (pieces, send, small, dmixed, sums) = refs[:4], refs[4 + len(after) :]
        small[...] = small_in[...]
        pieces[1, :ROWS] = attended[...]
        dmixed[...] = nt(attended[...], w_out[...]).astype(LOW)
        s = Names(
            dmixed=dmixed,
            dquery=pieces.at[0, :ROWS],
            dkey=pieces.at[0, ROWS:],
            dvalue=pieces.at[1, ROWS:],
            **dict(zip(ATTEND_SAVED, kept)),
        )
        sums[...] = jnp.zeros_like(sums)

        def table_sum(pair, dscores):
            for odd in range(2):
                part = tn(spread[seq], dscores[odd * ROWS : (odd + 1) * ROWS])
                both = jnp.concatenate([part, jnp.zeros((L, L), WIDE)], axis=1)
                turned = pltpu.roll(both, 0, 1, stride=1, stride_axis=0)
                head = 2 * pair + odd
                sums[head : head + 1, :] = jnp.sum(turned, axis=0, keepdims=True)

        back_attend(s, table_sum)
        send[: ROWS + L] = pieces[1 - info[0]]
        small[S_QUERY : S_QUERY + 1, :] += column_sum(pieces[0, :ROWS])
        small[S_VALUE : S_VALUE + 1, :] += column_sum(pieces[1, ROWS:])
        distance = lax.broadcasted_iota(jnp.int32, (2 * L, L), 0) - (L - 1)
        bucket = lax.broadcasted_iota(jnp.int32, (2 * L, L), 1)
        table = lax.dot_general(
            sums[...],
            (bucket_of(distance) == bucket).astype(WIDE),
            (((1,), (0,)), ((), ())),
            precision=lax.Precision.HIGHEST,
            preferred_element_type=WIDE,
        )
        for column in range(H // 4):
            lanes = slice(column * L, (column + 1) * L)
            small[S_TABLE : S_TABLE + 4, lanes] += table[4 * column : 4 * column + 4]
        send[ROWS + L :] = small[...].astype(LOW)

    return pl.pallas_call(
        kernel,
        out_shape=[
            shaped((2, ROWS + L, D), LOW),
            shaped((ROWS + L + SMALL, D), LOW),
            shaped((SMALL, D), WIDE),
        ],
        in_specs=[SMEM] + [VMEM] * 8 + [ANY] * len(after),
        out_specs=[VMEM] * 3,
        scratch_shapes=[pltpu.VMEM((ROWS, D), LOW), pltpu.VMEM((16, 2 * L), WIDE)],
        compiler_params=limit(12),
        cost_estimate=cost(4),
        name="attend_back",
    )(info, attended, small_in, spread, w_out, *(saved[n] for n in ATTEND_SAVED), *after)


def finish_rows(info, total, output, pieces, matrices, picks, after):
    def kernel(info, *refs):
        totals, outputs, pieces = refs[0:2], refs[2:4], refs[4:6]
        (query, key, value), refs = refs[6:9], refs[9 + len(after) :]
        content_ends, query_ends, done = refs
        done[...] = jnp.zeros_like(done)
        first = info[2] == 1
        for seq in range(SEQS):
            lower = totals[seq][...] + nt(pieces[seq][0, :ROWS], query[...])
            upper = nt(pieces[seq][0, ROWS:], key[...]) + nt(pieces[seq][1, ROWS:], value[...])
            content_ends[seq * L : (seq + 1) * L] = jnp.where(
                first, lower[:L] + upper, outputs[seq][:L]
            )
            ends = jnp.where(first, lower[L : L + picks], outputs[seq][L : L + picks])
            for row in range(picks):
                query_ends[seq * picks + row] = ends[row : row + 1]

    return pl.pallas_call(
        kernel,
        out_shape=[shaped((ALL_CONTENT, D), WIDE), shaped((SEQS * picks, 1, D), WIDE), TOKEN],
        in_specs=[SMEM] + [VMEM] * 9 + [ANY] * len(after),
        out_specs=[VMEM] * 3,
        compiler_params=limit(12),
        cost_estimate=cost(3),
        name="finish_rows",
    )(info, *total, *output, *pieces, *matrices[:3], *after)


def attend_grads(info, pair, early, mine, arrived, small, after=()):
    def kernel(info, small, *refs):
        pairs_in, earlies, mines, arriveds = (refs[2 * i : 2 * i + 2] for i in range(4))
        refs = refs[8 + len(after) :]
        outs, extra, rest = refs[:5], refs[5], refs[6:]
        a_rows, a_content, b_rows, b_content, stage, out_sems = rest
        core, place = info[0], info[1]
        for seq in range(SEQS):
            at = slice(seq * ROWS, (seq + 1) * ROWS)
            far = slice((2 + seq) * ROWS, (3 + seq) * ROWS)
            a_rows[at] = pairs_in[seq][core]
            a_rows[far] = columns(earlies[seq], core * D, D)[...]
            b_rows[at] = mines[seq][core, :ROWS]
            b_rows[far] = arriveds[seq][:ROWS]
            at = slice(seq * L, (seq + 1) * L)
            far = slice((2 + seq) * L, (3 + seq) * L)
            a_content[at] = pairs_in[seq][0, :L]
            a_content[far] = earlies[seq][:L, :D]
            b_content[at] = mines[seq][core, ROWS:]
            b_content[far] = arriveds[seq][ROWS : ROWS + L]
        far_small = arriveds[1][ROWS + L :]
        extra[...] = (small[...] + far_small.astype(WIDE)).astype(LOW)
        sent = start_all([(extra, outs[i].at[2 * QUARTER :]) for i in range(2)], out_sems, 8)
        for block, (former, latter) in enumerate(((a_rows, b_rows), (a_content, b_content))):
            for part in range(3):
                stage[block, part * 256 : (part + 1) * 256] = tn(
                    former[:, part * 256 : (part + 1) * 256], latter[...]
                ).astype(LOW)
            for k in range(4):
                quarter = lax.rem(place + k, 4)
                index, part = PLACES[k, block]
                start = part * QUARTER
                sent += start_all(
                    [
                        (
                            rows_at(stage.at[block], quarter * QUARTER, QUARTER),
                            outs[index].at[start : start + QUARTER],
                        )
                    ],
                    out_sems,
                    block * 4 + k,
                )
        wait_all(sent)

    return pl.pallas_call(
        kernel,
        out_shape=term_shapes(QUARTER, SMALL) + [shaped((SMALL, D), LOW)],
        in_specs=[SMEM] + [VMEM] * 9 + [ANY] * len(after),
        out_specs=[ANY] * 5 + [VMEM],
        scratch_shapes=[
            pltpu.VMEM((2 * ALL_ROWS, D), LOW),
            pltpu.VMEM((2 * ALL_CONTENT, D), LOW),
            pltpu.VMEM((2 * ALL_ROWS, D), LOW),
            pltpu.VMEM((2 * ALL_CONTENT, D), LOW),
            pltpu.VMEM((2, D, D), LOW),
            DMA((10,)),
        ],
        compiler_params=limit(12),
        cost_estimate=cost(5),
        name="attend_grads",
    )(info, small, *pair, *early, *mine, *arrived, *after)


def small_kernel(body, name, shapes, inputs, after=(), info=None, through=()):
    first = [] if info is None else [info]
    given = len(first) + len(inputs)

    def kernel(*refs):
        outs = refs[given + len(after) + len(through) :]
        body(*refs[:given], *outs[: len(shapes)])

    return pl.pallas_call(
        kernel,
        out_shape=[shaped(shape, LOW) for shape in shapes]
        + [shaped(array.shape, array.dtype) for array in through],
        in_specs=[SMEM] * len(first)
        + [VMEM] * len(inputs)
        + [ANY] * (len(after) + len(through)),
        out_specs=[VMEM] * len(shapes) + [ANY] * len(through),
        input_output_aliases={
            given + len(after) + i: len(shapes) + i for i in range(len(through))
        },
        compiler_params=limit(8),
        cost_estimate=cost(1),
        name=name,
    )(*first, *inputs, *after, *through)


def total_of(*terms):
    return sum(term.astype(WIDE) for term in terms).astype(LOW)


def ring_add(after0, before1, from_left, from_right, after=()):
    count = after0.shape[0]
    extra = from_left.shape[0] - 2 * count

    def body(after0, before1, from_left, from_right, right, left):
        right[:count] = total_of(after0[...], from_left[:count])
        left[:count] = total_of(before1[...], from_right[:count])
        if extra:
            right[count:] = from_left[2 * count :]
            left[count:] = from_right[2 * count :]

    return small_kernel(
        body,
        "ring_add",
        [(count + extra, D)] * 2,
        (after0, before1, from_left, from_right),
        after,
    )


def ring_sum(info, own, left, right, from_left, from_right, after=(), small=()):
    count = own.shape[0] // 2
    part = count // 4
    extra = sum(array.shape[0] for array in small)

    def body(info, own, left, right, from_left, from_right, *outs):
        if extra:
            small, outs = outs[0], outs[1:]
            total = total_of(
                small[...], from_left[2 * count :], from_right[2 * count :], left[count:]
            )
        for k, out in enumerate(outs):
            at = pl.multiple_of(lax.rem(info[3] + k, 4) * part, 16)
            low, high = pl.ds(at, part), pl.ds(at + count, part)
            out[:part] = total_of(own[low], left[low], from_right[high])
            out[part : 2 * part] = total_of(own[high], from_left[high], right[low])
            if extra:
                out[2 * part :] = total

    return small_kernel(
        body,
        "ring_sum",
        [(2 * part + extra, D)] * 4,
        (own, left, right, from_left, from_right, *small),
        after,
        info,
    )


def add_all(name, terms, after=()):
    def body(*refs):
        refs[-1][...] = total_of(*(ref[...] for ref in refs[:-1]))

    return small_kernel(body, name, [terms[0].shape], terms, after)[0]


def hand_on(arrays, after):
    return small_kernel(lambda *refs: None, "hand_on", [], (), after, None, arrays)


def z_join(feed, feed_far, attend, attend_far):
    first = feed.shape[0]
    count = attend.shape[0] - SMALL

    def body(feed, feed_far, attend, attend_far, whole, small, table):
        whole[:first] = total_of(feed[...], feed_far[...])
        total = total_of(attend[...], attend_far[...])
        whole[first:] = total[:count]
        small[...] = total[count : count + S_TABLE]
        table[...] = total[count + S_TABLE :]

    shapes = [(first + count, D), (S_TABLE, D), (SMALL - S_TABLE, D)]
    return small_kernel(body, "z_join", shapes, (feed, feed_far, attend, attend_far))


def finish_small(small, table, far, after=()):
    places = [n for n in range(S_TABLE) if not S_EXPAND <= n < S_EXPAND + 4]

    def kernel(small, table, far, *refs):
        vectors, (b_expand, whole, done) = refs[len(after) : -3], refs[-3:]
        done[...] = jnp.zeros_like(done)
        values = small[...].astype(WIDE)
        for place, vector in zip(places, vectors):
            vector[...] = values[place : place + 1]
        for column in range(4):
            lanes = slice(column * D, (column + 1) * D)
            b_expand[:, lanes] = values[S_EXPAND + column : S_EXPAND + column + 1]
        total = table[...].astype(WIDE) + far[...].astype(WIDE)
        heads = [total[:, column * L : (column + 1) * L] for column in range(4)]
        whole[...] = jnp.concatenate(heads)[:H, :NB]

    *vectors, b_expand, whole, done = pl.pallas_call(
        kernel,
        out_shape=[shaped((1, D), WIDE)] * len(places)
        + [shaped((1, FF), WIDE), shaped((H, NB), WIDE), TOKEN],
        in_specs=[VMEM] * 3 + [ANY] * len(after),
        out_specs=[VMEM] * (len(places) + 3),
        compiler_params=limit(4),
        cost_estimate=cost(1),
        name="finish_small",
    )(small, table, far, *after)
    return dict(zip(places, vectors)), b_expand, whole, done


def inner_join(info, parts):
    counts = (QUARTER // 2, QUARTER // 4)
    half = 4 * sum(counts)

    def body(info, *refs):
        refs, (whole, right, left) = refs[:-3], refs[-3:]
        start, given = 0, 0
        for count in counts:
            for k, ref in enumerate(refs):
                at = pl.multiple_of(lax.rem(info[3] + k, 4) * count, 16) + start
                whole[pl.ds(at, count)] = ref[given : given + count]
                whole[pl.ds(at + half, count)] = ref[given + count : given + 2 * count]
            start, given = start + 4 * count, given + 2 * count
        kept = pl.multiple_of((1 - info[4]) * QUARTER, QUARTER)
        right[:half] = whole[:half]
        right[half : half + QUARTER] = whole[pl.ds(kept + half, QUARTER)]
        right[half + QUARTER :] = whole[half + 2 * QUARTER :]
        left[:QUARTER] = whole[pl.ds(kept, QUARTER)]
        left[QUARTER:] = whole[2 * QUARTER :]

    shapes = [(2 * half, D)] + [(2 * half - QUARTER, D)] * 2
    return small_kernel(body, "inner_join", shapes, parts, (), info)


def cut(before, after_part, after=()):
    rows = before.shape[0]
    half = 3 * QUARTER

    def body(before, after_part, right, left, blocks, both):
        right[...] = before[:half]
        left[...] = after_part[2 * QUARTER :]
        blocks[:QUARTER] = before[half : half + QUARTER]
        blocks[QUARTER:] = after_part[:QUARTER]
        both[:rows] = before[...]
        both[rows:] = after_part[...]

    shapes = [(half, D), (half, D), (2 * QUARTER, D), (2 * rows, D)]
    return small_kernel(body, "cut", shapes, (before, after_part), after)


OUT_SHAPES = ((FF, D), (D, FF)) + ((D, D),) * 4


KEPT_BLOCK, LEFT_BLOCK, SQUARE = 2, 3, 4


def half_places(k, half, blocks=(0, 1)):
    return tuple((k, half, block) for block in (*blocks, SQUARE))


OWN = half_places(0, 0) + half_places(0, 1)
NEAR = (
    half_places(3, 0)
    + half_places(3, 1, (KEPT_BLOCK,))
    + half_places(1, 0, (KEPT_BLOCK,))
    + half_places(1, 1)
)
ACROSS = (half_places(2, 0), half_places(2, 1))
BLOCKS = ((3, 1, LEFT_BLOCK), (1, 0, LEFT_BLOCK))


def out_places(outs, part, half, block, core, quarter, plane):
    if block == SQUARE:
        return [
            (
                core == number,
                part,
                rows_at(outs[2 + 2 * number + half], quarter * QUARTER, QUARTER),
            )
            for number in range(2)
        ]
    if block >= KEPT_BLOCK:
        block = 1 - plane if block == KEPT_BLOCK else plane
    if half == 0:
        start = core * HALF + block * D + quarter * QUARTER
        return [(None, part, rows_at(outs[0], start, QUARTER))]
    rows = rows_at(outs[1], quarter * QUARTER, QUARTER)
    return [(None, part, columns(rows, (core * 2 + block) * D, D))]


def settle(info, pieces, outs, name, after=()):
    shapes = OUT_SHAPES
    keys = tuple(pieces)
    arrays = [pieces[key] for key in keys]
    given = list(after) + list(outs or ())

    def kernel(info, *refs):
        parts, rest = refs[: len(keys)], refs[len(keys) + len(given) :]
        outs, rest = rest[: len(shapes)], rest[len(shapes) :]
        done, rest = rest[0], rest[1:]
        done[...] = jnp.zeros_like(done)
        wide_held, out_sems = rest[:-1], rest[-1]
        finish = []
        for index, (sibling, places) in enumerate(keys):
            core = 1 - info[0] if sibling else info[0]
            for number, (k, half, block) in enumerate(places):
                quarter = lax.rem((info[3] if sibling else info[1]) + k, 4)
                at = slice(number * QUARTER, (number + 1) * QUARTER)
                source = wide_held[index].at[at]
                source[...] = parts[index][at].astype(WIDE)
                targets = out_places(outs, source, half, block, core, quarter, info[4])
                for condition, part, target in targets:
                    copy = pltpu.make_async_copy(part, target, out_sems.at[16 * index + number])
                    if condition is None:
                        copy.start()
                        finish.append(copy.wait)
                    else:
                        pl.when(condition)(copy.start)
                        finish.append(lambda c=copy, when=condition: pl.when(when)(c.wait))
        for action in finish:
            action()

    result = pl.pallas_call(
        kernel,
        out_shape=[shaped(shape, WIDE) for shape in shapes]
        + [TOKEN],
        in_specs=[SMEM] + [VMEM] * len(keys) + [ANY] * len(given),
        out_specs=[ANY] * len(shapes) + [VMEM],
        scratch_shapes=[pltpu.VMEM(array.shape, WIDE) for array in arrays]
        + [DMA((16 * len(keys),))],
        input_output_aliases={
            1 + len(keys) + len(after) + i: i for i in range(len(outs or ()))
        },
        compiler_params=limit(20),
        cost_estimate=cost(sum(array.size for array in arrays) * 2e-6 + 1),
        name=name,
    )(info, *arrays, *given)
    return result[:-1], result[-1]


PLANE = ("x", "y", "c")


def shift(value, axis, by):
    size = lax.axis_size(axis)
    return lax.ppermute(value, axis, [(i, (i + by) % size) for i in range(size)])


def send(value, by):
    return lax.ppermute(value, "s", [(0, 1)] if by > 0 else [(1, 0)])


def turn(value, outer, by):
    pairs = []
    for i in range(4):
        for j in range(4):
            for c in range(2):
                if (c == 0) == outer:
                    target = ((i + by) % 4, j)
                else:
                    target = (i, (j + by) % 4)
                pairs.append(((i * 4 + j) * 2 + c, (target[0] * 4 + target[1]) * 2 + c))
    return lax.ppermute(value, PLANE, pairs)


def place(outer):
    return jnp.where(
        (lax.axis_index("c") == 0) == outer, lax.axis_index("x"), lax.axis_index("y")
    )


def wide(value):
    return value.astype(WIDE)


def total_wide(*terms):
    return sum(wide(term) for term in terms)


def inner_turns(parts, sign):
    return [turn(part, False, sign * by) for part, by in zip(parts, (1, 2, -1))]


def both_cores(places, piece):
    return {(0, places): piece, (1, places): shift(piece, "c", 1)}


def on_device(
    content_in,
    query_in,
    content_cot,
    query_cot,
    order_rank,
    query_pos,
    group_tag,
    *rest,
):
    (
        w_query,
        b_query,
        w_key,
        w_value,
        b_value,
        w_out,
        b_out,
        norm1_gain,
        norm1_bias,
        w_expand,
        b_expand,
        w_contract,
        b_contract,
        norm2_gain,
        norm2_bias,
    ) = (argument[0] for argument in rest[:-1])
    rel_table = rest[-1]
    core = lax.axis_index("c")
    first_section = (lax.axis_index("s") == 0).astype(jnp.int32)
    info = jnp.stack([core, place(True), first_section, place(False), lax.axis_index("z")])
    picks = query_pos.shape[1]

    matrices = (w_query, w_key, w_value, w_out, w_expand, w_contract)
    w_out_held = w_out
    vec = jnp.stack(
        [b_query, b_value, b_out, norm1_gain, norm1_bias, b_contract, norm2_gain, norm2_bias]
    )
    ranks = jnp.concatenate([order_rank, group_tag, query_pos], axis=1)
    masks, spread, query_in, query_cot = prepare(
        ranks, rel_table.T, jnp.concatenate([query_in, query_cot]), picks, (vec, info)
    )
    b_expand = b_expand[None]

    fronts, arrived = [], []
    for seq in range(SEQS):
        given = (seq, info, content_in, query_in, matrices, masks, vec, b_expand)
        fronts.append(front(*given, tuple(fronts)) if fronts else front_parts(*given))
        arrived.append(send(fronts[seq], 1))
    output, early, pair, saved, grads = [], [], [], [], []
    for seq in range(SEQS):
        results = middle_forward(
            seq, info, content_in, query_in, arrived[seq], matrices, masks, vec, b_expand, tuple(grads)
        )
        for collected, result in zip((output, early, pair, saved), results):
            collected.append(result)
        grads.append(middle_back(seq, info, content_cot, query_cot, matrices, vec, saved[seq]))
    early = [shift(value, "c", 1) for value in early]
    grads = [send(value, -1) for value in grads]
    small = None
    total, branch, attended, own, late, pieces, pass_on = [], [], [], [], [], [], []
    for seq in range(SEQS):
        results = feed_back(
            seq,
            info,
            grads[seq],
            content_cot,
            query_cot,
            small,
            vec,
            matrices,
            saved[seq],
            tuple(pass_on),
        )
        small = results[3]
        for collected, result in zip(
            (total, branch, attended, own, late), results[:3] + results[4:]
        ):
            collected.append(result)
        late[seq] = shift(late[seq], "c", 1)
        results = attend_back(
            seq,
            info,
            attended[seq],
            small,
            spread,
            (),
            w_out_held,
            saved[seq],
        )
        small = results[2]
        pieces.append(results[0])
        pass_on.append(results[1])
    feed_terms = feed_grads(info, saved, branch, own, early, late, (small,))
    passed = [shift(value, "c", 1) for value in pass_on]

    def outer_step(terms):
        return (turn(terms[0], True, 1), turn(terms[1], True, -1))

    f_left, f_right = outer_step(feed_terms)
    *attend_terms, extra = attend_grads(info, pair, early, pieces, passed, small, (feed_terms[4],))
    a_left, a_right = outer_step(attend_terms)
    f_sent = ring_add(feed_terms[2], feed_terms[3], f_left, f_right, (extra,))
    f_outer = outer_step(f_sent)
    a_sent = ring_add(attend_terms[2], attend_terms[3], a_left, a_right)
    f_parts = ring_sum(info, feed_terms[4], *f_outer, f_left, f_right, (a_sent[0],))
    f_others = inner_turns(f_parts[1:], 1)
    a_parts = ring_sum(
        info, attend_terms[4], *outer_step(a_sent), a_left, a_right, (f_parts[0],), (extra,)
    )
    f_part = add_all("inner_sum", [f_parts[0]] + f_others, (a_parts[0],))
    f_far = shift(f_part, "z", 1)
    a_part = add_all("inner_sum", [a_parts[0]] + inner_turns(a_parts[1:], 1), (f_part,))
    a_far = shift(a_part, "z", 1)
    part, small, table = z_join(f_part, f_far, a_part, a_far)
    own, to_right, to_left = inner_join(info, [part] + inner_turns([part] * 3, -1))
    before, after_part = turn(to_right, True, 1), turn(to_left, True, -1)
    content_ends, query_ends, token = finish_rows(
        info, total, output, pieces, matrices, picks, (own,)
    )
    row, b_expand, table, small_token = finish_small(small, table, shift(table, "s", 1), (own,))
    outs, own_token = settle(info, both_cores(OWN, own), None, "own_out")
    to_right, to_left, blocks, near = cut(before, after_part, (token, small_token, own_token))
    last = (turn(to_right, True, 1), turn(to_left, True, -1), shift(blocks, "z", 1))
    outs, near_token = settle(info, {(0, NEAR): near}, outs, "near_out")
    outs, far_token = settle(info, {(1, NEAR): shift(near, "c", 1)}, outs, "near_out")
    last = dict(zip((*ACROSS, BLOCKS), hand_on(last, (near_token, far_token))))
    own = {(0, places): piece for places, piece in last.items()}
    far = {(1, places): shift(piece, "c", 1) for places, piece in last.items()}
    outs, _ = settle(info, own, outs, "last_out")
    outs, _ = settle(info, far, outs, "last_out")
    contract, expand, g_query, g_key, g_out, g_value = outs
    return (
        content_ends[None],
        query_ends.transpose(1, 0, 2),
        g_query[None],
        row[S_QUERY],
        g_key[None],
        g_value[None],
        row[S_VALUE],
        g_out[None],
        row[S_OUT],
        row[S_GAIN1],
        row[S_SHIFT1],
        expand[None],
        b_expand,
        contract[None],
        row[S_CONTRACT],
        row[S_GAIN2],
        row[S_SHIFT2],
        table.T,
    )


DP = ("z", "x", "y", "c")


def solution(mesh):
    mesh = jax.sharding.Mesh(mesh.devices.reshape(2, 2, 4, 4, 2), ("s",) + DP)
    layer_specs = tuple(
        P("s", *([None] * (rank - 1))) for rank in (3, 2, 3, 3, 2, 3, 2, 2, 2, 3, 2, 3, 2, 2, 2)
    )
    in_specs = (P(DP, None),) * 7 + layer_specs + (P(),)
    out_specs = (P("s", DP, None),) * 2 + layer_specs + (P(),)
    return jax.shard_map(
        on_device, mesh=mesh, in_specs=in_specs, out_specs=out_specs, check_vma=False
    )
```

```python
import jax
import jax.numpy as jnp
from jax import lax
from jax.experimental import pallas as pl
from jax.experimental.pallas import tpu as pltpu
from jax.sharding import PartitionSpec as P

D = 768
H = 12
HD = 64
FF = 3072
NB = 32
L = 128
PAIRS = H // 2
SEQS = 2
PICKS = 32
ROWS = L + PICKS
EPSILON = 1e-05
SCALE = HD ** (-0.5)
TILE = 1536
LOW = jnp.bfloat16
WIDE = jnp.float32
HALF = FF // 2
QUARTER = D // 4
EARLY = 3 * D + HALF
LATE = D + HALF
SMALL = 16
ALL_ROWS = SEQS * ROWS
ALL_CONTENT = SEQS * L
PIECE = ALL_ROWS + ALL_CONTENT


def nn(former, latter):
    return lax.dot_general(
        former, latter, (((1,), (0,)), ((), ())), preferred_element_type=WIDE
    )


def nt(former, latter):
    return lax.dot_general(
        former, latter, (((1,), (1,)), ((), ())), preferred_element_type=WIDE
    )


def tn(former, latter):
    return lax.dot_general(
        former, latter, (((0,), (0,)), ((), ())), preferred_element_type=WIDE
    )


def halves(value):
    even = lax.broadcasted_iota(jnp.int32, value.shape, 1) < HD
    zero = jnp.zeros_like(value)
    return jnp.concatenate([jnp.where(even, value, zero), jnp.where(even, zero, value)])


def side(value):
    count = value.shape[0] // 2
    return jnp.concatenate([value[:count], value[count:]], axis=1)


def norm_rows(values):
    centered = values - jnp.mean(values, axis=-1, keepdims=True)
    variance = jnp.mean(centered * centered, axis=-1, keepdims=True)
    root = lax.rsqrt(variance + EPSILON)
    return (centered * root, root)


def norm_rows_back(scaled, normed, root):
    return root * (
        scaled
        - jnp.mean(scaled, axis=-1, keepdims=True)
        - normed * jnp.mean(scaled * normed, axis=-1, keepdims=True)
    )


B_QUERY, B_VALUE, B_OUT, GAIN1, SHIFT1, B_CONTRACT, GAIN2, SHIFT2 = range(8)
S_QUERY, S_VALUE, S_OUT, S_GAIN1, S_SHIFT1, S_EXPAND = range(6)
S_CONTRACT, S_GAIN2, S_SHIFT2, S_TABLE = 9, 10, 11, 12
LIMITS = (12, 16, 23, 32, 46, 64, 91)


def bucket_of(relative):
    distance = jnp.abs(relative)
    beyond = 8 + sum((distance >= limit).astype(jnp.int32) for limit in LIMITS)
    within = jnp.where(distance < 8, distance, beyond)
    return within + 16 * (relative > 0).astype(jnp.int32)


def forward_attend(x, w, vec, masks, s, keep):
    row = lambda k: vec[k : k + 1, :]
    s.query[...] = (nn(x[...], w.query[...]) + row(B_QUERY)).astype(LOW)
    s.key[...] = nn(x[:L], w.key[...]).astype(LOW)
    s.value[...] = (nn(x[:L], w.value[...]) + row(B_VALUE)).astype(LOW)
    for pair in range(PAIRS):
        lanes = slice(pair * 128, (pair + 1) * 128)
        scores = nt(halves(s.query[:, lanes]), s.key[:, lanes]) * SCALE + masks[pair]
        shifted = jnp.exp(scores - jnp.max(scores, axis=-1, keepdims=True))
        probs = (shifted / jnp.sum(shifted, axis=-1, keepdims=True)).astype(LOW)
        if keep:
            s.probs[pair] = probs
        s.mixed[:, lanes] = nn(side(probs), halves(s.value[:, lanes])).astype(LOW)
    total = x[...].astype(WIDE) + nn(s.mixed[...], w.out[...]) + row(B_OUT)
    normed, root = norm_rows(total)
    first = normed * row(GAIN1) + row(SHIFT1)
    s.first_low[...] = first.astype(LOW)
    s.total[...] = first + row(B_CONTRACT)
    if keep:
        s.normed1[...] = normed
        s.root1[...] = jnp.broadcast_to(root, (ROWS, 128))


def forward_feed(w, vec, b_expand, s, keep):
    row = lambda k: vec[k : k + 1, :]
    for tile in range(FF // TILE):
        tile = slice(tile * TILE, (tile + 1) * TILE)
        expanded = nn(s.first_low[...], w.expand[:, tile]) + b_expand[:, tile]
        cumulative = 0.5 * (1.0 + lax.erf(expanded * 0.7071067811865476))
        activated = (expanded * cumulative).astype(LOW)
        if keep:
            s.slope[:, tile] = (
                cumulative + expanded * jnp.exp(-0.5 * expanded * expanded) * 0.3989422804014327
            ).astype(LOW)
            s.activated[:, tile] = activated
        s.total[...] += nn(activated, w.contract[tile, :])
    normed, root = norm_rows(s.total[...])
    if keep:
        s.normed2[...] = normed
        s.root2[...] = jnp.broadcast_to(root, (ROWS, 128))
    s.out[...] = (normed * row(GAIN2) + row(SHIFT2)).astype(s.out.dtype)


def column_sum(value):
    return jnp.sum(value.astype(WIDE), axis=0, keepdims=True)


def back_second_norm(grad, vec, s, add=None):
    upper = grad.astype(WIDE)
    normed = s.normed2[...]
    lower = norm_rows_back(upper * vec[GAIN2 : GAIN2 + 1, :], normed, s.root2[:, :1])
    s.total[...] = lower
    s.branch[...] = lower.astype(LOW)
    if add is not None:
        add(S_GAIN2, column_sum(upper * normed))
        add(S_SHIFT2, column_sum(upper))
        add(S_CONTRACT, column_sum(lower.astype(LOW)))


def back_feed(w, vec, s, add=None):
    for tile in range(FF // TILE):
        tile = slice(tile * TILE, (tile + 1) * TILE)
        lower = (nt(s.branch[...], w.contract[tile, :]) * s.slope[:, tile].astype(WIDE)).astype(LOW)
        s.expanded[:, tile] = lower
        if add is not None:
            part = column_sum(lower)
            for column in range(TILE // D):
                add(
                    S_EXPAND + tile.start // D + column,
                    part[:, column * D : (column + 1) * D],
                )
        s.total[...] += nt(lower, w.expand[:, tile])
    upper = s.total[...]
    normed = s.normed1[...]
    lower = norm_rows_back(upper * vec[GAIN1 : GAIN1 + 1, :], normed, s.root1[:, :1])
    s.total[...] = lower
    s.attended[...] = lower.astype(LOW)
    if add is not None:
        add(S_GAIN1, column_sum(upper * normed))
        add(S_SHIFT1, column_sum(upper))
        add(S_OUT, column_sum(lower.astype(LOW)))


def back_attend(s, table=None):
    for pair in range(PAIRS):
        lanes = slice(pair * 128, (pair + 1) * 128)
        probs = s.probs[pair]
        below = halves(s.dmixed[:, lanes])
        dprobs = nt(below, s.value[:, lanes])
        s.dvalue[:, lanes] = tn(probs, below).astype(LOW)
        weight = probs.astype(WIDE)
        dscores = (
            weight * (dprobs - jnp.sum(weight * dprobs, axis=-1, keepdims=True))
        ).astype(LOW)
        s.dquery[:, lanes] = (nn(side(dscores), halves(s.key[:, lanes])) * SCALE).astype(LOW)
        s.dkey[:, lanes] = (tn(dscores, halves(s.query[:, lanes])) * SCALE).astype(LOW)
        if table is not None:
            table(pair, dscores)


class Names:
    def __init__(self, **named):
        self.__dict__.update(named)


MATRICES = ("query", "key", "value", "out", "expand", "contract")
MATRIX_SHAPES = {
    "query": (D, D),
    "key": (D, D),
    "value": (D, D),
    "out": (D, D),
    "expand": (D, FF),
    "contract": (FF, D),
}
MASK_SHAPE = (PAIRS, 2 * ROWS, L)
KEPT = {
    "query": ((ROWS, D), LOW),
    "key": ((L, D), LOW),
    "value": ((L, D), LOW),
    "probs": (MASK_SHAPE, LOW),
    "mixed": ((ROWS, D), LOW),
    "normed1": ((ROWS, D), WIDE),
    "root1": ((ROWS, 128), WIDE),
    "first_low": ((ROWS, D), LOW),
    "slope": ((ROWS, FF), LOW),
    "activated": ((ROWS, FF), LOW),
    "normed2": ((ROWS, D), WIDE),
    "root2": ((ROWS, 128), WIDE),
}
SAVED = tuple(name for name in KEPT if name != "mixed")
ANY = pl.BlockSpec(memory_space=pl.ANY)
HBM = pl.BlockSpec(memory_space=pltpu.HBM)
VMEM = pl.BlockSpec(memory_space=pltpu.VMEM)


def limit(megabytes):
    return pltpu.CompilerParams(vmem_limit_bytes=megabytes * 1024 * 1024)


DMA = pltpu.SemaphoreType.DMA


def position():
    core, x, y = (lax.axis_index(axis) for axis in ("c", "x", "y"))
    first = core == 0
    return (
        core,
        jnp.where(first, x, y),
        lax.axis_index("s") == 0,
        jnp.where(first, y, x),
        lax.axis_index("z"),
    )


def cost(microseconds):
    return pl.CostEstimate(flops=0, bytes_accessed=int(microseconds * 3.2e6), transcendentals=0)


def shaped(shape, kind):
    return jax.ShapeDtypeStruct(shape, kind)


TOKEN = shaped((8, 128), WIDE)


def columns(ref, start, size):
    return ref.at[:, pl.ds(pl.multiple_of(start, 128), size)]


def rows_at(ref, start, size):
    return ref.at[pl.ds(pl.multiple_of(start, 64), size)]


def start_all(pairs, sems, base=0):
    copies = [
        pltpu.make_async_copy(source, target, sems.at[base + index])
        for index, (source, target) in enumerate(pairs)
    ]
    for copy in copies:
        copy.start()
    return copies


def wait_all(copies):
    for copy in copies:
        copy.wait()


def fetcher(names, sources, targets, sems, base=0):
    copies = dict(zip(names, start_all(list(zip(sources, targets)), sems, base)))
    return lambda name: copies[name].wait()


def prepare(ranks, table, queries, picks, after):
    def kernel(ranks, table, queries, *refs):
        masks, spread, rows_in, rows_cot = refs[len(after) :]
        order, tag, pos = ranks[:, :L], ranks[:, L : 2 * L], ranks[:, 2 * L : 2 * L + picks]
        values = queries[...].astype(WIDE)
        blank = jnp.zeros((PICKS - picks, D), WIDE)
        for index, target in enumerate((rows_in, rows_cot)):
            own = values[2 * index * picks : 2 * (index + 1) * picks]
            target[...] = jnp.concatenate([own[:picks], blank, own[picks:], blank]).astype(LOW)
        lane = lax.broadcasted_iota(jnp.int32, (L, L), 1)
        level = lax.broadcasted_iota(jnp.int32, (L, L), 0)
        lane_q = lax.broadcasted_iota(jnp.int32, (PICKS, L), 1)
        upright = lambda row: jnp.sum(jnp.where(lane == level, row, 0.0), axis=1, keepdims=True)
        distance = lax.broadcasted_iota(jnp.int32, (2 * L, NB), 0) - (L - 1)
        bucket = lax.broadcasted_iota(jnp.int32, (2 * L, NB), 1)
        by_distance = lax.dot_general(
            table[...],
            (bucket_of(distance) == bucket).astype(WIDE),
            (((1,), (1,)), ((), ())),
            precision=lax.Precision.HIGHEST,
            preferred_element_type=WIDE,
        )
        allowed, hot = [], []
        for seq in range(SEQS):
            own_rank = order[seq : seq + 1, :].astype(WIDE)
            own_tag = tag[seq : seq + 1, :].astype(WIDE)
            own_pos = pos[seq : seq + 1, :].astype(WIDE)
            number = lax.broadcasted_iota(jnp.int32, (PICKS, picks), 0)
            same = number == lax.broadcasted_iota(jnp.int32, (PICKS, picks), 1)
            place = jnp.sum(jnp.where(same, own_pos, 0.0), axis=1, keepdims=True)
            filled = lax.broadcasted_iota(jnp.int32, (PICKS, 1), 0) < picks
            place = jnp.where(filled, place, -1.0).astype(jnp.int32)
            matches = place == lane_q
            marks = jnp.where(matches, 1.0, 0.0)
            predicted = jnp.max(marks, axis=0, keepdims=True)
            rank = jnp.sum(jnp.where(matches, own_rank, 0.0), axis=1, keepdims=True)
            group = jnp.sum(jnp.where(matches, own_tag, 0.0), axis=1, keepdims=True)
            earlier = (upright(predicted) > 0) & (own_rank <= upright(own_rank))
            content = (upright(own_tag) == own_tag) & ((predicted == 0) | earlier)
            query = (group == own_tag) & ((predicted == 0) | (own_rank + 1 <= rank))
            allowed.append((content, query))
            hot.append(marks)
            spread[seq, :L] = jnp.where(lane == L - 1 - level, 1.0, 0.0).astype(LOW)
            spread[seq, L:] = jnp.where(lane_q == L - 1 - place, 1.0, 0.0).astype(LOW)
        hot = jnp.concatenate(hot)
        for head in range(H):
            row = jnp.broadcast_to(by_distance[head : head + 1], (L, 2 * L))
            bias = pltpu.roll(row, L + 1, 1, stride=1, stride_axis=0)[:, :L]
            bias_q = lax.dot_general(
                hot,
                bias,
                (((1,), (0,)), ((), ())),
                precision=lax.Precision.HIGHEST,
                preferred_element_type=WIDE,
            )
            base = head % 2 * ROWS
            for seq in range(SEQS):
                content, query = allowed[seq]
                masks[seq, head // 2, base : base + L] = jnp.where(content, bias, -1e30)
                masks[seq, head // 2, base + L : base + ROWS] = jnp.where(
                    query, bias_q[seq * PICKS : (seq + 1) * PICKS], -1e30
                )

    return pl.pallas_call(
        kernel,
        out_shape=[
            shaped((SEQS,) + MASK_SHAPE, WIDE),
            shaped((SEQS, ROWS, L), LOW),
            shaped((SEQS * PICKS, D), LOW),
            shaped((SEQS * PICKS, D), LOW),
        ],
        in_specs=[VMEM] * 3 + [ANY] * len(after),
        out_specs=[VMEM] * 4,
        compiler_params=limit(8),
        cost_estimate=pl.CostEstimate(flops=int(3e10), bytes_accessed=0, transcendentals=0),
        name="prepare",
    )(ranks, table, queries, *after)


def only(condition, work, *outs):
    pl.when(condition)(work)

    @pl.when(jnp.logical_not(condition))
    def _():
        for out in outs:
            out[...] = jnp.zeros_like(out)


def take_rows(content, picks, seq, target):
    target[:L] = content[seq * L : (seq + 1) * L]
    target[L:] = picks[seq * PICKS : (seq + 1) * PICKS]


def front(seq, content, picks, matrices, masks, vec, b_expand, after=()):
    def kernel(content, picks, masks, vec, b_expand, *refs):
        info = position()
        w = Names(**dict(zip(MATRICES, refs[:6])))
        out, x, query, key, value, mixed, first_low, total = refs[6 + len(after) :]
        s = Names(
            query=query,
            key=key,
            value=value,
            mixed=mixed,
            first_low=first_low,
            total=total,
            out=out,
        )

        def work():
            take_rows(content, picks, seq, x)
            forward_attend(x, w, vec, masks.at[seq], s, False)
            forward_feed(w, vec, b_expand, s, False)

        only(info[2], work, out)

    return pl.pallas_call(
        kernel,
        out_shape=shaped((ROWS, D), LOW),
        in_specs=[VMEM] * 11 + [ANY] * len(after),
        out_specs=VMEM,
        scratch_shapes=[pltpu.VMEM((ROWS, D), LOW)]
        + [pltpu.VMEM(*KEPT[n]) for n in ("query", "key", "value", "mixed", "first_low")]
        + [pltpu.VMEM((ROWS, D), WIDE)],
        compiler_params=limit(12),
        cost_estimate=cost(5),
        name="front",
    )(content, picks, masks, vec, b_expand, *matrices, *after)


def front_parts(seq, content, picks, matrices, masks, vec, b_expand):
    def first(content, picks, masks, vec, *refs):
        info = position()
        w = Names(**dict(zip(MATRICES[:4], refs[:4])))
        first_low, total, x, query, key, value, mixed = refs[4:]
        s = Names(
            query=query, key=key, value=value, mixed=mixed, first_low=first_low, total=total
        )

        def work():
            take_rows(content, picks, seq, x)
            forward_attend(x, w, vec, masks.at[seq], s, False)

        only(info[2], work, first_low, total)

    def second(first_low, total_in, vec, b_expand, expand, contract, out, total):
        info = position()
        s = Names(first_low=first_low, total=total, out=out)

        def work():
            total[...] = total_in[...]
            forward_feed(Names(expand=expand, contract=contract), vec, b_expand, s, False)

        only(info[2], work, out)

    first_low, total = pl.pallas_call(
        first,
        out_shape=[shaped((ROWS, D), LOW), shaped((ROWS, D), WIDE)],
        in_specs=[VMEM] * 8,
        out_specs=[VMEM] * 2,
        scratch_shapes=[pltpu.VMEM((ROWS, D), LOW)]
        + [pltpu.VMEM(*KEPT[n]) for n in ("query", "key", "value", "mixed")],
        compiler_params=limit(8),
        cost_estimate=pl.CostEstimate(flops=int(1e10), bytes_accessed=0, transcendentals=0),
        name="front_attend",
    )(content, picks, masks, vec, *matrices[:4])
    return pl.pallas_call(
        second,
        out_shape=shaped((ROWS, D), LOW),
        in_specs=[VMEM] * 6,
        out_specs=VMEM,
        scratch_shapes=[pltpu.VMEM((ROWS, D), WIDE)],
        compiler_params=limit(12),
        cost_estimate=cost(2),
        name="front_feed",
    )(first_low, total, vec, b_expand, *matrices[4:])


def middle_forward(seq, content, picks, arrived, matrices, masks, vec, b_expand, after=()):
    def kernel(arrived, content, picks, masks, vec, b_expand, *refs):
        info = position()
        w, rest = Names(**dict(zip(MATRICES, refs[:6]))), refs[6 + len(after) :]
        (out, early, pair), kept = rest[:3], rest[3 : 3 + len(SAVED)]
        mixed, total = rest[3 + len(SAVED) :]
        x = pair.at[0]
        s = Names(total=total, out=out, mixed=mixed, **dict(zip(SAVED, kept)))
        take_rows(content, picks, seq, x)
        x[...] = jnp.where(info[2], x[...], arrived[...])
        early[:, :D] = x[...]
        forward_attend(x, w, vec, masks.at[seq], s, True)
        forward_feed(w, vec, b_expand, s, True)
        pair[1] = mixed[...]
        early[:, D : 2 * D] = mixed[...]
        early[:, 2 * D : 3 * D] = s.first_low[...]
        early[:, 3 * D :] = columns(s.activated, (1 - info[0]) * HALF, HALF)[...]

    out, early, pair, *saved = pl.pallas_call(
        kernel,
        out_shape=[
            shaped((ROWS, D), WIDE),
            shaped((ROWS, EARLY), LOW),
            shaped((2, ROWS, D), LOW),
        ]
        + [shaped(*KEPT[n]) for n in SAVED],
        in_specs=[VMEM] * 12 + [ANY] * len(after),
        out_specs=[VMEM] * (3 + len(SAVED)),
        scratch_shapes=[pltpu.VMEM(*KEPT["mixed"]), pltpu.VMEM((ROWS, D), WIDE)],
        compiler_params=limit(16),
        cost_estimate=cost(6),
        name="middle_forward",
    )(arrived, content, picks, masks, vec, b_expand, *matrices, *after)
    return (out, early, pair, dict(zip(SAVED, saved)))


FEED_SAVED = ("normed2", "root2", "slope", "normed1", "root1")
ATTEND_SAVED = ("value", "probs", "key", "query")


def middle_back(seq, content, picks, matrices, vec, saved):
    names = FEED_SAVED + ATTEND_SAVED

    def kernel(content, picks, vec, *refs):
        w, rest = Names(**dict(zip(MATRICES, refs[:6]))), refs[6:]
        kept, grad, rest = rest[: len(names)], rest[len(names)], rest[len(names) + 1 :]
        cot, total, branch, expanded, attended, dmixed, dvalue, dquery, dkey = rest
        s = Names(
            total=total,
            branch=branch,
            expanded=expanded,
            attended=attended,
            dmixed=dmixed,
            dvalue=dvalue,
            dquery=dquery,
            dkey=dkey,
            **dict(zip(names, kept)),
        )
        take_rows(content, picks, seq, cot)
        back_second_norm(cot[...], vec, s)
        back_feed(w, vec, s)
        dmixed[...] = nt(attended[...], w.out[...]).astype(LOW)
        back_attend(s)
        lower = total[...] + nt(dquery[...], w.query[...])
        upper = nt(dkey[...], w.key[...]) + nt(dvalue[...], w.value[...])
        grad[:L] = (lower[:L] + upper).astype(LOW)
        grad[L:] = lower[L:].astype(LOW)

    return pl.pallas_call(
        kernel,
        out_shape=shaped((ROWS, D), LOW),
        in_specs=[VMEM] * (9 + len(names)),
        out_specs=VMEM,
        scratch_shapes=[
            pltpu.VMEM((ROWS, D), LOW),
            pltpu.VMEM((ROWS, D), WIDE),
            pltpu.VMEM((ROWS, D), LOW),
            pltpu.VMEM((ROWS, FF), LOW),
            pltpu.VMEM((ROWS, D), LOW),
            pltpu.VMEM((ROWS, D), LOW),
            pltpu.VMEM((L, D), LOW),
            pltpu.VMEM((ROWS, D), LOW),
            pltpu.VMEM((L, D), LOW),
        ],
        compiler_params=limit(12),
        cost_estimate=cost(7),
        name="middle_back",
    )(content, picks, vec, *matrices, *(saved[n] for n in names))


def feed_back(seq, arrived, content, picks, small_in, vec, matrices, saved, after=()):
    given = [] if small_in is None else [small_in]

    def kernel(arrived, content, picks, vec, expand, contract, *refs):
        info = position()
        kept, rest = refs[:5], refs[5 + len(given) + len(after) :]
        total, branch, attended, small, own, late, upper, expanded = rest
        w = Names(expand=expand, contract=contract)
        s = Names(
            total=total,
            branch=branch,
            attended=attended,
            expanded=expanded,
            **dict(zip(FEED_SAVED, kept)),
        )
        small[...] = refs[5][...] if given else jnp.zeros_like(small)

        def add(place, value):
            small[place : place + 1, :] += value

        take_rows(content, picks, seq, upper)
        back_second_norm(jnp.where(info[2], arrived[...], upper[...]), vec, s, add)
        late[:, :D] = branch[...]
        back_feed(w, vec, s, add)
        own[...] = columns(expanded, info[0] * HALF, HALF)[...]
        late[:, D:] = columns(expanded, (1 - info[0]) * HALF, HALF)[...]

    return pl.pallas_call(
        kernel,
        out_shape=[
            shaped((ROWS, D), WIDE),
            shaped((ROWS, D), LOW),
            shaped((ROWS, D), LOW),
            shaped((SMALL, D), WIDE),
            shaped((ROWS, HALF), LOW),
            shaped((ROWS, LATE), LOW),
        ],
        in_specs=[VMEM] * (11 + len(given)) + [ANY] * len(after),
        out_specs=[VMEM] * 6,
        scratch_shapes=[pltpu.VMEM((ROWS, D), LOW), pltpu.VMEM((ROWS, FF), LOW)],
        compiler_params=limit(12),
        cost_estimate=cost(4),
        name="feed_back",
    )(
        arrived,
        content,
        picks,
        vec,
        matrices[4],
        matrices[5],
        *(saved[n] for n in FEED_SAVED),
        *given,
        *after,
    )


PLACES = {
    (2, 0): (0, 0),
    (1, 1): (0, 1),
    (2, 1): (1, 0),
    (3, 0): (1, 1),
    (1, 0): (2, 0),
    (3, 1): (3, 0),
    (0, 0): (4, 0),
    (0, 1): (4, 1),
}


def term_shapes(count, extra=0):
    rows = (2 * count + extra, 2 * count + extra, count, count, 2 * count)
    return [shaped((n, D), LOW) for n in rows]


def feed_grads(mine, branch, own, early, late, after=()):
    def kernel(*refs):
        info = position()
        acts, lows, branches, owns, earlies, lates = (refs[2 * i : 2 * i + 2] for i in range(6))
        refs = refs[:12] + refs[12 + len(after) :]
        outs, (a_act, a_first, b_branch, b_own, stage, out_sems) = refs[12:17], refs[17:]
        core, place = info[0], info[1]
        own_at = [slice(seq * ROWS, (seq + 1) * ROWS) for seq in range(SEQS)]
        far_at = [slice((2 + seq) * ROWS, (3 + seq) * ROWS) for seq in range(SEQS)]
        for seq in range(SEQS):
            at, far = own_at[seq], far_at[seq]
            a_act[at] = columns(acts[seq], core * HALF, HALF)[...]
            a_act[far] = earlies[seq][:, 3 * D :]
            b_branch[at] = branches[seq][...]
            b_branch[far] = lates[seq][:, :D]
        sent = []

        def send(block):
            for k in range(4):
                quarter = lax.rem(place + k, 4)
                index, part = PLACES[k, block // 2]
                start = (2 * part + block % 2) * QUARTER
                sent.extend(
                    start_all(
                        [
                            (
                                rows_at(stage.at[block], quarter * QUARTER, QUARTER),
                                outs[index].at[start : start + QUARTER],
                            )
                        ],
                        out_sems,
                        block * 4 + k,
                    )
                )

        for block in range(2):
            for part in range(3):
                start = block * D + part * 256
                stage[block, part * 256 : (part + 1) * 256] = tn(
                    a_act[:, start : start + 256], b_branch[...]
                ).astype(LOW)
            send(block)
        for seq in range(SEQS):
            at, far = own_at[seq], far_at[seq]
            a_first[at] = lows[seq][...]
            a_first[far] = earlies[seq][:, 2 * D : 3 * D]
            b_own[at] = owns[seq][...]
            b_own[far] = lates[seq][:, D:]
        for block in range(2):
            for part in range(3):
                stage[2 + block, part * 256 : (part + 1) * 256] = tn(
                    a_first[:, part * 256 : (part + 1) * 256], b_own[:, block * D : (block + 1) * D]
                ).astype(LOW)
            send(2 + block)
        wait_all(sent)

    acts = [saved["activated"] for saved in mine]
    lows = [saved["first_low"] for saved in mine]
    return pl.pallas_call(
        kernel,
        out_shape=term_shapes(2 * QUARTER),
        in_specs=[VMEM] * 12 + [ANY] * len(after),
        out_specs=[ANY] * 5,
        scratch_shapes=[
            pltpu.VMEM((2 * ALL_ROWS, HALF), LOW),
            pltpu.VMEM((2 * ALL_ROWS, D), LOW),
            pltpu.VMEM((2 * ALL_ROWS, D), LOW),
            pltpu.VMEM((2 * ALL_ROWS, HALF), LOW),
            pltpu.VMEM((4, D, D), LOW),
            DMA((16,)),
        ],
        compiler_params=limit(16),
        cost_estimate=cost(8),
        name="feed_grads",
    )(*acts, *lows, *branch, *own, *early, *late, *after)


def attend_back(seq, attended, small_in, spread, after, w_out, saved):
    def kernel(attended, small_in, spread, w_out, *refs):
        info = position()
        kept, (pieces, send, small, dmixed, sums) = refs[:4], refs[4 + len(after) :]
        small[...] = small_in[...]
        pieces[1, :ROWS] = attended[...]
        dmixed[...] = nt(attended[...], w_out[...]).astype(LOW)
        s = Names(
            dmixed=dmixed,
            dquery=pieces.at[0, :ROWS],
            dkey=pieces.at[0, ROWS:],
            dvalue=pieces.at[1, ROWS:],
            **dict(zip(ATTEND_SAVED, kept)),
        )
        sums[...] = jnp.zeros_like(sums)

        def table_sum(pair, dscores):
            for odd in range(2):
                part = tn(spread[seq], dscores[odd * ROWS : (odd + 1) * ROWS])
                both = jnp.concatenate([part, jnp.zeros((L, L), WIDE)], axis=1)
                turned = pltpu.roll(both, 0, 1, stride=1, stride_axis=0)
                head = 2 * pair + odd
                sums[head : head + 1, :] = jnp.sum(turned, axis=0, keepdims=True)

        back_attend(s, table_sum)
        send[: ROWS + L] = pieces[1 - info[0]]
        small[S_QUERY : S_QUERY + 1, :] += column_sum(pieces[0, :ROWS])
        small[S_VALUE : S_VALUE + 1, :] += column_sum(pieces[1, ROWS:])
        distance = lax.broadcasted_iota(jnp.int32, (2 * L, L), 0) - (L - 1)
        bucket = lax.broadcasted_iota(jnp.int32, (2 * L, L), 1)
        table = lax.dot_general(
            sums[...],
            (bucket_of(distance) == bucket).astype(WIDE),
            (((1,), (0,)), ((), ())),
            precision=lax.Precision.HIGHEST,
            preferred_element_type=WIDE,
        )
        for column in range(H // 4):
            lanes = slice(column * L, (column + 1) * L)
            small[S_TABLE : S_TABLE + 4, lanes] += table[4 * column : 4 * column + 4]
        send[ROWS + L :] = small[...].astype(LOW)

    return pl.pallas_call(
        kernel,
        out_shape=[
            shaped((2, ROWS + L, D), LOW),
            shaped((ROWS + L + SMALL, D), LOW),
            shaped((SMALL, D), WIDE),
        ],
        in_specs=[VMEM] * 8 + [ANY] * len(after),
        out_specs=[VMEM] * 3,
        scratch_shapes=[pltpu.VMEM((ROWS, D), LOW), pltpu.VMEM((16, 2 * L), WIDE)],
        compiler_params=limit(12),
        cost_estimate=cost(4),
        name="attend_back",
    )(attended, small_in, spread, w_out, *(saved[n] for n in ATTEND_SAVED), *after)


def finish_rows(total, output, pieces, matrices, picks, after):
    def kernel(*refs):
        info = position()
        totals, outputs, pieces = refs[0:2], refs[2:4], refs[4:6]
        (query, key, value), refs = refs[6:9], refs[9 + len(after) :]
        content_ends, query_ends, done = refs
        done[...] = jnp.zeros_like(done)
        first = info[2]
        for seq in range(SEQS):
            lower = totals[seq][...] + nt(pieces[seq][0, :ROWS], query[...])
            upper = nt(pieces[seq][0, ROWS:], key[...]) + nt(pieces[seq][1, ROWS:], value[...])
            content_ends[seq * L : (seq + 1) * L] = jnp.where(
                first, lower[:L] + upper, outputs[seq][:L]
            )
            ends = jnp.where(first, lower[L : L + picks], outputs[seq][L : L + picks])
            for row in range(picks):
                query_ends[seq * picks + row] = ends[row : row + 1]

    return pl.pallas_call(
        kernel,
        out_shape=[shaped((ALL_CONTENT, D), WIDE), shaped((SEQS * picks, 1, D), WIDE), TOKEN],
        in_specs=[VMEM] * 9 + [ANY] * len(after),
        out_specs=[VMEM] * 3,
        compiler_params=limit(12),
        cost_estimate=cost(3),
        name="finish_rows",
    )(*total, *output, *pieces, *matrices[:3], *after)


def attend_grads(pair, early, mine, arrived, small, after=()):
    def kernel(small, *refs):
        info = position()
        pairs_in, earlies, mines, arriveds = (refs[2 * i : 2 * i + 2] for i in range(4))
        refs = refs[8 + len(after) :]
        outs, extra, rest = refs[:5], refs[5], refs[6:]
        a_rows, a_content, b_rows, b_content, stage, out_sems = rest
        core, place = info[0], info[1]
        for seq in range(SEQS):
            at = slice(seq * ROWS, (seq + 1) * ROWS)
            far = slice((2 + seq) * ROWS, (3 + seq) * ROWS)
            a_rows[at] = pairs_in[seq][core]
            a_rows[far] = columns(earlies[seq], core * D, D)[...]
            b_rows[at] = mines[seq][core, :ROWS]
            b_rows[far] = arriveds[seq][:ROWS]
            at = slice(seq * L, (seq + 1) * L)
            far = slice((2 + seq) * L, (3 + seq) * L)
            a_content[at] = pairs_in[seq][0, :L]
            a_content[far] = earlies[seq][:L, :D]
            b_content[at] = mines[seq][core, ROWS:]
            b_content[far] = arriveds[seq][ROWS : ROWS + L]
        far_small = arriveds[1][ROWS + L :]
        extra[...] = (small[...] + far_small.astype(WIDE)).astype(LOW)
        sent = start_all([(extra, outs[i].at[2 * QUARTER :]) for i in range(2)], out_sems, 8)
        for block, (former, latter) in enumerate(((a_rows, b_rows), (a_content, b_content))):
            for part in range(3):
                stage[block, part * 256 : (part + 1) * 256] = tn(
                    former[:, part * 256 : (part + 1) * 256], latter[...]
                ).astype(LOW)
            for k in range(4):
                quarter = lax.rem(place + k, 4)
                index, part = PLACES[k, block]
                start = part * QUARTER
                sent += start_all(
                    [
                        (
                            rows_at(stage.at[block], quarter * QUARTER, QUARTER),
                            outs[index].at[start : start + QUARTER],
                        )
                    ],
                    out_sems,
                    block * 4 + k,
                )
        wait_all(sent)

    return pl.pallas_call(
        kernel,
        out_shape=term_shapes(QUARTER, SMALL) + [shaped((SMALL, D), LOW)],
        in_specs=[VMEM] * 9 + [ANY] * len(after),
        out_specs=[ANY] * 5 + [VMEM],
        scratch_shapes=[
            pltpu.VMEM((2 * ALL_ROWS, D), LOW),
            pltpu.VMEM((2 * ALL_CONTENT, D), LOW),
            pltpu.VMEM((2 * ALL_ROWS, D), LOW),
            pltpu.VMEM((2 * ALL_CONTENT, D), LOW),
            pltpu.VMEM((2, D, D), LOW),
            DMA((10,)),
        ],
        compiler_params=limit(12),
        cost_estimate=cost(5),
        name="attend_grads",
    )(small, *pair, *early, *mine, *arrived, *after)


def small_kernel(body, name, shapes, inputs, after=(), through=()):
    given = len(inputs)

    def kernel(*refs):
        outs = refs[given + len(after) + len(through) :]
        body(*refs[:given], *outs[: len(shapes)])

    return pl.pallas_call(
        kernel,
        out_shape=[shaped(shape, LOW) for shape in shapes]
        + [shaped(array.shape, array.dtype) for array in through],
        in_specs=[VMEM] * len(inputs) + [ANY] * (len(after) + len(through)),
        out_specs=[VMEM] * len(shapes) + [ANY] * len(through),
        input_output_aliases={
            given + len(after) + i: len(shapes) + i for i in range(len(through))
        },
        compiler_params=limit(8),
        cost_estimate=cost(1),
        name=name,
    )(*inputs, *after, *through)


def total_of(*terms):
    return sum(term.astype(WIDE) for term in terms).astype(LOW)


def ring_add(after0, before1, from_left, from_right, after=()):
    count = after0.shape[0]
    extra = from_left.shape[0] - 2 * count

    def body(after0, before1, from_left, from_right, right, left):
        right[:count] = total_of(after0[...], from_left[:count])
        left[:count] = total_of(before1[...], from_right[:count])
        if extra:
            right[count:] = from_left[2 * count :]
            left[count:] = from_right[2 * count :]

    return small_kernel(
        body,
        "ring_add",
        [(count + extra, D)] * 2,
        (after0, before1, from_left, from_right),
        after,
    )


def ring_sum(own, left, right, from_left, from_right, after=(), small=()):
    count = own.shape[0] // 2
    part = count // 4
    extra = sum(array.shape[0] for array in small)

    def body(own, left, right, from_left, from_right, *outs):
        info = position()
        if extra:
            small, outs = outs[0], outs[1:]
            total = total_of(
                small[...], from_left[2 * count :], from_right[2 * count :], left[count:]
            )
        for k, out in enumerate(outs):
            at = pl.multiple_of(lax.rem(info[3] + k, 4) * part, 16)
            low, high = pl.ds(at, part), pl.ds(at + count, part)
            out[:part] = total_of(own[low], left[low], from_right[high])
            out[part : 2 * part] = total_of(own[high], from_left[high], right[low])
            if extra:
                out[2 * part :] = total

    return small_kernel(
        body,
        "ring_sum",
        [(2 * part + extra, D)] * 4,
        (own, left, right, from_left, from_right, *small),
        after,
    )


def add_all(name, terms, after=()):
    def body(*refs):
        refs[-1][...] = total_of(*(ref[...] for ref in refs[:-1]))

    return small_kernel(body, name, [terms[0].shape], terms, after)[0]


def hand_on(arrays, after):
    return small_kernel(lambda *refs: None, "hand_on", [], (), after, arrays)


def z_join(feed, feed_far, attend, attend_far):
    first = feed.shape[0]
    count = attend.shape[0] - SMALL

    def body(feed, feed_far, attend, attend_far, whole, small, table):
        whole[:first] = total_of(feed[...], feed_far[...])
        total = total_of(attend[...], attend_far[...])
        whole[first:] = total[:count]
        small[...] = total[count : count + S_TABLE]
        table[...] = total[count + S_TABLE :]

    shapes = [(first + count, D), (S_TABLE, D), (SMALL - S_TABLE, D)]
    return small_kernel(body, "z_join", shapes, (feed, feed_far, attend, attend_far))


def finish_small(small, table, far, after=()):
    places = [n for n in range(S_TABLE) if not S_EXPAND <= n < S_EXPAND + 4]

    def kernel(small, table, far, *refs):
        vectors, (b_expand, whole, done) = refs[len(after) : -3], refs[-3:]
        done[...] = jnp.zeros_like(done)
        values = small[...].astype(WIDE)
        for place, vector in zip(places, vectors):
            vector[...] = values[place : place + 1]
        for column in range(4):
            lanes = slice(column * D, (column + 1) * D)
            b_expand[:, lanes] = values[S_EXPAND + column : S_EXPAND + column + 1]
        total = table[...].astype(WIDE) + far[...].astype(WIDE)
        heads = [total[:, column * L : (column + 1) * L] for column in range(4)]
        whole[...] = jnp.concatenate(heads)[:H, :NB]

    *vectors, b_expand, whole, done = pl.pallas_call(
        kernel,
        out_shape=[shaped((1, D), WIDE)] * len(places)
        + [shaped((1, FF), WIDE), shaped((H, NB), WIDE), TOKEN],
        in_specs=[VMEM] * 3 + [ANY] * len(after),
        out_specs=[VMEM] * (len(places) + 3),
        compiler_params=limit(4),
        cost_estimate=cost(1),
        name="finish_small",
    )(small, table, far, *after)
    return dict(zip(places, vectors)), b_expand, whole, done


def inner_join(parts):
    counts = (QUARTER // 2, QUARTER // 4)
    half = 4 * sum(counts)

    def body(*refs):
        info = position()
        refs, (whole, right, left) = refs[:-3], refs[-3:]
        start, given = 0, 0
        for count in counts:
            for k, ref in enumerate(refs):
                at = pl.multiple_of(lax.rem(info[3] + k, 4) * count, 16) + start
                whole[pl.ds(at, count)] = ref[given : given + count]
                whole[pl.ds(at + half, count)] = ref[given + count : given + 2 * count]
            start, given = start + 4 * count, given + 2 * count
        kept = pl.multiple_of((1 - info[4]) * QUARTER, QUARTER)
        right[:half] = whole[:half]
        right[half : half + QUARTER] = whole[pl.ds(kept + half, QUARTER)]
        right[half + QUARTER :] = whole[half + 2 * QUARTER :]
        left[:QUARTER] = whole[pl.ds(kept, QUARTER)]
        left[QUARTER:] = whole[2 * QUARTER :]

    shapes = [(2 * half, D)] + [(2 * half - QUARTER, D)] * 2
    return small_kernel(body, "inner_join", shapes, parts)


def cut(before, after_part, after=()):
    rows = before.shape[0]
    half = 3 * QUARTER

    def body(before, after_part, right, left, blocks, both):
        right[...] = before[:half]
        left[...] = after_part[2 * QUARTER :]
        blocks[:QUARTER] = before[half : half + QUARTER]
        blocks[QUARTER:] = after_part[:QUARTER]
        both[:rows] = before[...]
        both[rows:] = after_part[...]

    shapes = [(half, D), (half, D), (2 * QUARTER, D), (2 * rows, D)]
    return small_kernel(body, "cut", shapes, (before, after_part), after)


OUT_SHAPES = ((FF, D), (D, FF)) + ((D, D),) * 4


KEPT_BLOCK, LEFT_BLOCK, SQUARE = 2, 3, 4


def half_places(k, half, blocks=(0, 1)):
    return tuple((k, half, block) for block in (*blocks, SQUARE))


OWN = half_places(0, 0) + half_places(0, 1)
NEAR = (
    half_places(3, 0)
    + half_places(3, 1, (KEPT_BLOCK,))
    + half_places(1, 0, (KEPT_BLOCK,))
    + half_places(1, 1)
)
ACROSS = (half_places(2, 0), half_places(2, 1))
BLOCKS = ((3, 1, LEFT_BLOCK), (1, 0, LEFT_BLOCK))


def out_places(outs, part, half, block, core, quarter, plane):
    if block == SQUARE:
        return [
            (
                core == number,
                part,
                rows_at(outs[2 + 2 * number + half], quarter * QUARTER, QUARTER),
            )
            for number in range(2)
        ]
    if block >= KEPT_BLOCK:
        block = 1 - plane if block == KEPT_BLOCK else plane
    if half == 0:
        start = core * HALF + block * D + quarter * QUARTER
        return [(None, part, rows_at(outs[0], start, QUARTER))]
    rows = rows_at(outs[1], quarter * QUARTER, QUARTER)
    return [(None, part, columns(rows, (core * 2 + block) * D, D))]


def settle(pieces, outs, name, after=()):
    shapes = OUT_SHAPES
    keys = tuple(pieces)
    arrays = [pieces[key] for key in keys]
    given = list(after) + list(outs or ())

    def kernel(*refs):
        info = position()
        parts, rest = refs[: len(keys)], refs[len(keys) + len(given) :]
        outs, rest = rest[: len(shapes)], rest[len(shapes) :]
        done, rest = rest[0], rest[1:]
        done[...] = jnp.zeros_like(done)
        wide_held, out_sems = rest[:-1], rest[-1]
        finish = []
        for index, (sibling, places) in enumerate(keys):
            core = 1 - info[0] if sibling else info[0]
            for number, (k, half, block) in enumerate(places):
                quarter = lax.rem((info[3] if sibling else info[1]) + k, 4)
                at = slice(number * QUARTER, (number + 1) * QUARTER)
                source = wide_held[index].at[at]
                source[...] = parts[index][at].astype(WIDE)
                targets = out_places(outs, source, half, block, core, quarter, info[4])
                for condition, part, target in targets:
                    copy = pltpu.make_async_copy(part, target, out_sems.at[16 * index + number])
                    if condition is None:
                        copy.start()
                        finish.append(copy.wait)
                    else:
                        pl.when(condition)(copy.start)
                        finish.append(lambda c=copy, when=condition: pl.when(when)(c.wait))
        for action in finish:
            action()

    result = pl.pallas_call(
        kernel,
        out_shape=[shaped(shape, WIDE) for shape in shapes]
        + [TOKEN],
        in_specs=[VMEM] * len(keys) + [ANY] * len(given),
        out_specs=[ANY] * len(shapes) + [VMEM],
        scratch_shapes=[pltpu.VMEM(array.shape, WIDE) for array in arrays]
        + [DMA((16 * len(keys),))],
        input_output_aliases={
            len(keys) + len(after) + i: i for i in range(len(outs or ()))
        },
        compiler_params=limit(20),
        cost_estimate=cost(sum(array.size for array in arrays) * 2e-6 + 1),
        name=name,
    )(*arrays, *given)
    return result[:-1], result[-1]


PLANE = ("x", "y", "c")


def shift(value, axis, by):
    size = lax.axis_size(axis)
    return lax.ppermute(value, axis, [(i, (i + by) % size) for i in range(size)])


def send(value, by):
    return lax.ppermute(value, "s", [(0, 1)] if by > 0 else [(1, 0)])


def turn(value, outer, by):
    pairs = []
    for i in range(4):
        for j in range(4):
            for c in range(2):
                if (c == 0) == outer:
                    target = ((i + by) % 4, j)
                else:
                    target = (i, (j + by) % 4)
                pairs.append(((i * 4 + j) * 2 + c, (target[0] * 4 + target[1]) * 2 + c))
    return lax.ppermute(value, PLANE, pairs)


def place(outer):
    return jnp.where(
        (lax.axis_index("c") == 0) == outer, lax.axis_index("x"), lax.axis_index("y")
    )


def wide(value):
    return value.astype(WIDE)


def total_wide(*terms):
    return sum(wide(term) for term in terms)


def inner_turns(parts, sign):
    return [turn(part, False, sign * by) for part, by in zip(parts, (1, 2, -1))]


def both_cores(places, piece):
    return {(0, places): piece, (1, places): shift(piece, "c", 1)}


def on_device(
    content_in,
    query_in,
    content_cot,
    query_cot,
    order_rank,
    query_pos,
    group_tag,
    *rest,
):
    (
        w_query,
        b_query,
        w_key,
        w_value,
        b_value,
        w_out,
        b_out,
        norm1_gain,
        norm1_bias,
        w_expand,
        b_expand,
        w_contract,
        b_contract,
        norm2_gain,
        norm2_bias,
    ) = (argument[0] for argument in rest[:-1])
    rel_table = rest[-1]
    picks = query_pos.shape[1]

    matrices = (w_query, w_key, w_value, w_out, w_expand, w_contract)
    w_out_held = w_out
    vec = jnp.stack(
        [b_query, b_value, b_out, norm1_gain, norm1_bias, b_contract, norm2_gain, norm2_bias]
    )
    ranks = jnp.concatenate([order_rank, group_tag, query_pos], axis=1)
    masks, spread, query_in, query_cot = prepare(
        ranks, rel_table.T, jnp.concatenate([query_in, query_cot]), picks, (vec,)
    )
    b_expand = b_expand[None]

    fronts, arrived = [], []
    for seq in range(SEQS):
        given = (seq, content_in, query_in, matrices, masks, vec, b_expand)
        fronts.append(front(*given, tuple(fronts)) if fronts else front_parts(*given))
        arrived.append(send(fronts[seq], 1))
    output, early, pair, saved, grads = [], [], [], [], []
    for seq in range(SEQS):
        results = middle_forward(
            seq, content_in, query_in, arrived[seq], matrices, masks, vec, b_expand, tuple(grads)
        )
        for collected, result in zip((output, early, pair, saved), results):
            collected.append(result)
        grads.append(middle_back(seq, content_cot, query_cot, matrices, vec, saved[seq]))
    early = [shift(value, "c", 1) for value in early]
    grads = [send(value, -1) for value in grads]
    small = None
    total, branch, attended, own, late, pieces, pass_on = [], [], [], [], [], [], []
    for seq in range(SEQS):
        results = feed_back(
            seq,
            grads[seq],
            content_cot,
            query_cot,
            small,
            vec,
            matrices,
            saved[seq],
            tuple(pass_on),
        )
        small = results[3]
        for collected, result in zip(
            (total, branch, attended, own, late), results[:3] + results[4:]
        ):
            collected.append(result)
        late[seq] = shift(late[seq], "c", 1)
        results = attend_back(
            seq,
            attended[seq],
            small,
            spread,
            (),
            w_out_held,
            saved[seq],
        )
        small = results[2]
        pieces.append(results[0])
        pass_on.append(results[1])
    feed_terms = feed_grads(saved, branch, own, early, late, (small,))
    passed = [shift(value, "c", 1) for value in pass_on]

    def outer_step(terms):
        return (turn(terms[0], True, 1), turn(terms[1], True, -1))

    f_left, f_right = outer_step(feed_terms)
    *attend_terms, extra = attend_grads(pair, early, pieces, passed, small, (feed_terms[4],))
    a_left, a_right = outer_step(attend_terms)
    f_sent = ring_add(feed_terms[2], feed_terms[3], f_left, f_right, (extra,))
    f_outer = outer_step(f_sent)
    a_sent = ring_add(attend_terms[2], attend_terms[3], a_left, a_right)
    f_parts = ring_sum(feed_terms[4], *f_outer, f_left, f_right, (a_sent[0],))
    f_others = inner_turns(f_parts[1:], 1)
    a_parts = ring_sum(
        attend_terms[4], *outer_step(a_sent), a_left, a_right, (f_parts[0],), (extra,)
    )
    f_part = add_all("inner_sum", [f_parts[0]] + f_others, (a_parts[0],))
    f_far = shift(f_part, "z", 1)
    a_part = add_all("inner_sum", [a_parts[0]] + inner_turns(a_parts[1:], 1), (f_part,))
    a_far = shift(a_part, "z", 1)
    part, small, table = z_join(f_part, f_far, a_part, a_far)
    own, to_right, to_left = inner_join([part] + inner_turns([part] * 3, -1))
    before, after_part = turn(to_right, True, 1), turn(to_left, True, -1)
    content_ends, query_ends, token = finish_rows(
        total, output, pieces, matrices, picks, (own,)
    )
    row, b_expand, table, small_token = finish_small(small, table, shift(table, "s", 1), (own,))
    outs, own_token = settle(both_cores(OWN, own), None, "own_out")
    to_right, to_left, blocks, near = cut(before, after_part, (token, small_token, own_token))
    blocks = shift(blocks, "z", 1)
    last = (blocks, turn(to_right, True, 1), turn(to_left, True, -1))
    outs, near_token = settle({(0, NEAR): near}, outs, "near_out")
    outs, far_token = settle({(1, NEAR): shift(near, "c", 1)}, outs, "near_out")
    last = dict(zip((BLOCKS, *ACROSS), hand_on(last, (near_token, far_token))))
    own = {(0, places): piece for places, piece in last.items()}
    far = {(1, places): shift(piece, "c", 1) for places, piece in last.items()}
    outs, _ = settle(own, outs, "last_out")
    outs, _ = settle(far, outs, "last_out")
    contract, expand, g_query, g_key, g_out, g_value = outs
    return (
        content_ends[None],
        query_ends.transpose(1, 0, 2),
        g_query[None],
        row[S_QUERY],
        g_key[None],
        g_value[None],
        row[S_VALUE],
        g_out[None],
        row[S_OUT],
        row[S_GAIN1],
        row[S_SHIFT1],
        expand[None],
        b_expand,
        contract[None],
        row[S_CONTRACT],
        row[S_GAIN2],
        row[S_SHIFT2],
        table.T,
    )


DP = ("z", "x", "y", "c")


def solution(mesh):
    mesh = jax.sharding.Mesh(mesh.devices.reshape(2, 2, 4, 4, 2), ("s",) + DP)
    layer_specs = tuple(
        P("s", *([None] * (rank - 1))) for rank in (3, 2, 3, 3, 2, 3, 2, 2, 2, 3, 2, 3, 2, 2, 2)
    )
    in_specs = (P(DP, None),) * 7 + layer_specs + (P(),)
    out_specs = (P("s", DP, None),) * 2 + layer_specs + (P(),)
    return jax.shard_map(
        on_device, mesh=mesh, in_specs=in_specs, out_specs=out_specs, check_vma=False
    )
```

```python
import jax
import jax.numpy as jnp
from jax import lax
from jax.experimental import pallas as pl
from jax.experimental.pallas import tpu as pltpu
from jax.sharding import PartitionSpec as P

D = 768
H = 12
HD = 64
FF = 3072
NB = 32
L = 128
PAIRS = H // 2
SEQS = 2
PICKS = 32
ROWS = L + PICKS
EPSILON = 1e-05
SCALE = HD ** (-0.5)
TILE = 1536
LOW = jnp.bfloat16
WIDE = jnp.float32
HALF = FF // 2
QUARTER = D // 4
EARLY = 3 * D + HALF
LATE = D + HALF
SMALL = 16
ALL_ROWS = SEQS * ROWS
ALL_CONTENT = SEQS * L
PIECE = ALL_ROWS + ALL_CONTENT


def nn(former, latter):
    return lax.dot_general(
        former, latter, (((1,), (0,)), ((), ())), preferred_element_type=WIDE
    )


def nt(former, latter):
    return lax.dot_general(
        former, latter, (((1,), (1,)), ((), ())), preferred_element_type=WIDE
    )


def tn(former, latter):
    return lax.dot_general(
        former, latter, (((0,), (0,)), ((), ())), preferred_element_type=WIDE
    )


def halves(value):
    even = lax.broadcasted_iota(jnp.int32, value.shape, 1) < HD
    zero = jnp.zeros_like(value)
    return jnp.concatenate([jnp.where(even, value, zero), jnp.where(even, zero, value)])


def side(value):
    count = value.shape[0] // 2
    return jnp.concatenate([value[:count], value[count:]], axis=1)


def norm_rows(values):
    centered = values - jnp.mean(values, axis=-1, keepdims=True)
    variance = jnp.mean(centered * centered, axis=-1, keepdims=True)
    root = lax.rsqrt(variance + EPSILON)
    return (centered * root, root)


def norm_rows_back(scaled, normed, root):
    return root * (
        scaled
        - jnp.mean(scaled, axis=-1, keepdims=True)
        - normed * jnp.mean(scaled * normed, axis=-1, keepdims=True)
    )


B_QUERY, B_VALUE, B_OUT, GAIN1, SHIFT1, B_CONTRACT, GAIN2, SHIFT2 = range(8)
S_QUERY, S_VALUE, S_OUT, S_GAIN1, S_SHIFT1, S_EXPAND = range(6)
S_CONTRACT, S_GAIN2, S_SHIFT2, S_TABLE = 9, 10, 11, 12
LIMITS = (12, 16, 23, 32, 46, 64, 91)


def bucket_of(relative):
    distance = jnp.abs(relative)
    beyond = 8 + sum((distance >= limit).astype(jnp.int32) for limit in LIMITS)
    within = jnp.where(distance < 8, distance, beyond)
    return within + 16 * (relative > 0).astype(jnp.int32)


def forward_attend(x, w, vec, masks, s, keep):
    row = lambda k: vec[k : k + 1, :]
    s.query[...] = (nn(x[...], w.query[...]) + row(B_QUERY)).astype(LOW)
    s.key[...] = nn(x[:L], w.key[...]).astype(LOW)
    s.value[...] = (nn(x[:L], w.value[...]) + row(B_VALUE)).astype(LOW)
    for pair in range(PAIRS):
        lanes = slice(pair * 128, (pair + 1) * 128)
        scores = nt(halves(s.query[:, lanes]), s.key[:, lanes]) * SCALE + masks[pair]
        shifted = jnp.exp(scores - jnp.max(scores, axis=-1, keepdims=True))
        probs = (shifted / jnp.sum(shifted, axis=-1, keepdims=True)).astype(LOW)
        if keep:
            s.probs[pair] = probs
        s.mixed[:, lanes] = nn(side(probs), halves(s.value[:, lanes])).astype(LOW)
    total = x[...].astype(WIDE) + nn(s.mixed[...], w.out[...]) + row(B_OUT)
    normed, root = norm_rows(total)
    first = normed * row(GAIN1) + row(SHIFT1)
    s.first_low[...] = first.astype(LOW)
    s.total[...] = first + row(B_CONTRACT)
    if keep:
        s.normed1[...] = normed
        s.root1[...] = jnp.broadcast_to(root, (ROWS, 128))


def forward_feed(w, vec, b_expand, s, keep):
    row = lambda k: vec[k : k + 1, :]
    for tile in range(FF // TILE):
        tile = slice(tile * TILE, (tile + 1) * TILE)
        expanded = nn(s.first_low[...], w.expand[:, tile]) + b_expand[:, tile]
        cumulative = 0.5 * (1.0 + lax.erf(expanded * 0.7071067811865476))
        activated = (expanded * cumulative).astype(LOW)
        if keep:
            s.slope[:, tile] = (
                cumulative + expanded * jnp.exp(-0.5 * expanded * expanded) * 0.3989422804014327
            ).astype(LOW)
            s.activated[:, tile] = activated
        s.total[...] += nn(activated, w.contract[tile, :])
    normed, root = norm_rows(s.total[...])
    if keep:
        s.normed2[...] = normed
        s.root2[...] = jnp.broadcast_to(root, (ROWS, 128))
    s.out[...] = (normed * row(GAIN2) + row(SHIFT2)).astype(s.out.dtype)


def column_sum(value):
    return jnp.sum(value.astype(WIDE), axis=0, keepdims=True)


def back_second_norm(grad, vec, s, add=None):
    upper = grad.astype(WIDE)
    normed = s.normed2[...]
    lower = norm_rows_back(upper * vec[GAIN2 : GAIN2 + 1, :], normed, s.root2[:, :1])
    s.total[...] = lower
    s.branch[...] = lower.astype(LOW)
    if add is not None:
        add(S_GAIN2, column_sum(upper * normed))
        add(S_SHIFT2, column_sum(upper))
        add(S_CONTRACT, column_sum(lower.astype(LOW)))


def back_feed(w, vec, s, add=None):
    for tile in range(FF // TILE):
        tile = slice(tile * TILE, (tile + 1) * TILE)
        lower = (nt(s.branch[...], w.contract[tile, :]) * s.slope[:, tile].astype(WIDE)).astype(LOW)
        s.expanded[:, tile] = lower
        if add is not None:
            part = column_sum(lower)
            for column in range(TILE // D):
                add(
                    S_EXPAND + tile.start // D + column,
                    part[:, column * D : (column + 1) * D],
                )
        s.total[...] += nt(lower, w.expand[:, tile])
    upper = s.total[...]
    normed = s.normed1[...]
    lower = norm_rows_back(upper * vec[GAIN1 : GAIN1 + 1, :], normed, s.root1[:, :1])
    s.total[...] = lower
    s.attended[...] = lower.astype(LOW)
    if add is not None:
        add(S_GAIN1, column_sum(upper * normed))
        add(S_SHIFT1, column_sum(upper))
        add(S_OUT, column_sum(lower.astype(LOW)))


def back_attend(s, table=None):
    for pair in range(PAIRS):
        lanes = slice(pair * 128, (pair + 1) * 128)
        probs = s.probs[pair]
        below = halves(s.dmixed[:, lanes])
        dprobs = nt(below, s.value[:, lanes])
        s.dvalue[:, lanes] = tn(probs, below).astype(LOW)
        weight = probs.astype(WIDE)
        dscores = (
            weight * (dprobs - jnp.sum(weight * dprobs, axis=-1, keepdims=True))
        ).astype(LOW)
        s.dquery[:, lanes] = (nn(side(dscores), halves(s.key[:, lanes])) * SCALE).astype(LOW)
        s.dkey[:, lanes] = (tn(dscores, halves(s.query[:, lanes])) * SCALE).astype(LOW)
        if table is not None:
            table(pair, dscores)


class Names:
    def __init__(self, **named):
        self.__dict__.update(named)


MATRICES = ("query", "key", "value", "out", "expand", "contract")
MATRIX_SHAPES = {
    "query": (D, D),
    "key": (D, D),
    "value": (D, D),
    "out": (D, D),
    "expand": (D, FF),
    "contract": (FF, D),
}
MASK_SHAPE = (PAIRS, 2 * ROWS, L)
KEPT = {
    "query": ((ROWS, D), LOW),
    "key": ((L, D), LOW),
    "value": ((L, D), LOW),
    "probs": (MASK_SHAPE, LOW),
    "mixed": ((ROWS, D), LOW),
    "normed1": ((ROWS, D), WIDE),
    "root1": ((ROWS, 128), WIDE),
    "first_low": ((ROWS, D), LOW),
    "slope": ((ROWS, FF), LOW),
    "activated": ((ROWS, FF), LOW),
    "normed2": ((ROWS, D), WIDE),
    "root2": ((ROWS, 128), WIDE),
}
SAVED = tuple(name for name in KEPT if name != "mixed")
ANY = pl.BlockSpec(memory_space=pl.ANY)
HBM = pl.BlockSpec(memory_space=pltpu.HBM)
VMEM = pl.BlockSpec(memory_space=pltpu.VMEM)


def limit(megabytes):
    return pltpu.CompilerParams(vmem_limit_bytes=megabytes * 1024 * 1024)


DMA = pltpu.SemaphoreType.DMA


def position():
    core, x, y = (lax.axis_index(axis) for axis in ("c", "x", "y"))
    first = core == 0
    return (
        core,
        jnp.where(first, x, y),
        lax.axis_index("s") == 0,
        jnp.where(first, y, x),
        lax.axis_index("z"),
    )


def cost(microseconds):
    return pl.CostEstimate(flops=0, bytes_accessed=int(microseconds * 3.2e6), transcendentals=0)


def shaped(shape, kind):
    return jax.ShapeDtypeStruct(shape, kind)


TOKEN = shaped((8, 128), WIDE)


def columns(ref, start, size):
    return ref.at[:, pl.ds(pl.multiple_of(start, 128), size)]


def rows_at(ref, start, size):
    return ref.at[pl.ds(pl.multiple_of(start, 64), size)]


def start_all(pairs, sems, base=0):
    copies = [
        pltpu.make_async_copy(source, target, sems.at[base + index])
        for index, (source, target) in enumerate(pairs)
    ]
    for copy in copies:
        copy.start()
    return copies


def wait_all(copies):
    for copy in copies:
        copy.wait()


def fetcher(names, sources, targets, sems, base=0):
    copies = dict(zip(names, start_all(list(zip(sources, targets)), sems, base)))
    return lambda name: copies[name].wait()


def prepare(ranks, table, queries, picks, after):
    def kernel(ranks, table, queries, *refs):
        masks, spread, rows_in, rows_cot = refs[len(after) :]
        order, tag, pos = ranks[:, :L], ranks[:, L : 2 * L], ranks[:, 2 * L : 2 * L + picks]
        values = queries[...].astype(WIDE)
        blank = jnp.zeros((PICKS - picks, D), WIDE)
        for index, target in enumerate((rows_in, rows_cot)):
            own = values[2 * index * picks : 2 * (index + 1) * picks]
            target[...] = jnp.concatenate([own[:picks], blank, own[picks:], blank]).astype(LOW)
        lane = lax.broadcasted_iota(jnp.int32, (L, L), 1)
        level = lax.broadcasted_iota(jnp.int32, (L, L), 0)
        lane_q = lax.broadcasted_iota(jnp.int32, (PICKS, L), 1)
        upright = lambda row: jnp.sum(jnp.where(lane == level, row, 0.0), axis=1, keepdims=True)
        distance = lax.broadcasted_iota(jnp.int32, (2 * L, NB), 0) - (L - 1)
        bucket = lax.broadcasted_iota(jnp.int32, (2 * L, NB), 1)
        by_distance = lax.dot_general(
            table[...],
            (bucket_of(distance) == bucket).astype(WIDE),
            (((1,), (1,)), ((), ())),
            precision=lax.Precision.HIGHEST,
            preferred_element_type=WIDE,
        )
        allowed, hot = [], []
        for seq in range(SEQS):
            own_rank = order[seq : seq + 1, :].astype(WIDE)
            own_tag = tag[seq : seq + 1, :].astype(WIDE)
            own_pos = pos[seq : seq + 1, :].astype(WIDE)
            number = lax.broadcasted_iota(jnp.int32, (PICKS, picks), 0)
            same = number == lax.broadcasted_iota(jnp.int32, (PICKS, picks), 1)
            place = jnp.sum(jnp.where(same, own_pos, 0.0), axis=1, keepdims=True)
            filled = lax.broadcasted_iota(jnp.int32, (PICKS, 1), 0) < picks
            place = jnp.where(filled, place, -1.0).astype(jnp.int32)
            matches = place == lane_q
            marks = jnp.where(matches, 1.0, 0.0)
            predicted = jnp.max(marks, axis=0, keepdims=True)
            rank = jnp.sum(jnp.where(matches, own_rank, 0.0), axis=1, keepdims=True)
            group = jnp.sum(jnp.where(matches, own_tag, 0.0), axis=1, keepdims=True)
            earlier = (upright(predicted) > 0) & (own_rank <= upright(own_rank))
            content = (upright(own_tag) == own_tag) & ((predicted == 0) | earlier)
            query = (group == own_tag) & ((predicted == 0) | (own_rank + 1 <= rank))
            allowed.append((content, query))
            hot.append(marks)
            spread[seq, :L] = jnp.where(lane == L - 1 - level, 1.0, 0.0).astype(LOW)
            spread[seq, L:] = jnp.where(lane_q == L - 1 - place, 1.0, 0.0).astype(LOW)
        hot = jnp.concatenate(hot)
        for head in range(H):
            row = jnp.broadcast_to(by_distance[head : head + 1], (L, 2 * L))
            bias = pltpu.roll(row, L + 1, 1, stride=1, stride_axis=0)[:, :L]
            bias_q = lax.dot_general(
                hot,
                bias,
                (((1,), (0,)), ((), ())),
                precision=lax.Precision.HIGHEST,
                preferred_element_type=WIDE,
            )
            base = head % 2 * ROWS
            for seq in range(SEQS):
                content, query = allowed[seq]
                masks[seq, head // 2, base : base + L] = jnp.where(content, bias, -1e30)
                masks[seq, head // 2, base + L : base + ROWS] = jnp.where(
                    query, bias_q[seq * PICKS : (seq + 1) * PICKS], -1e30
                )

    return pl.pallas_call(
        kernel,
        out_shape=[
            shaped((SEQS,) + MASK_SHAPE, WIDE),
            shaped((SEQS, ROWS, L), LOW),
            shaped((SEQS * PICKS, D), LOW),
            shaped((SEQS * PICKS, D), LOW),
        ],
        in_specs=[VMEM] * 3 + [ANY] * len(after),
        out_specs=[VMEM] * 4,
        compiler_params=limit(8),
        cost_estimate=pl.CostEstimate(flops=int(3e10), bytes_accessed=0, transcendentals=0),
        name="prepare",
    )(ranks, table, queries, *after)


def only(condition, work, *outs):
    pl.when(condition)(work)

    @pl.when(jnp.logical_not(condition))
    def _():
        for out in outs:
            out[...] = jnp.zeros_like(out)


def take_rows(content, picks, seq, target):
    target[:L] = content[seq * L : (seq + 1) * L]
    target[L:] = picks[seq * PICKS : (seq + 1) * PICKS]


def front(seq, content, picks, matrices, masks, vec, b_expand, after=()):
    def kernel(content, picks, masks, vec, b_expand, *refs):
        info = position()
        w = Names(**dict(zip(MATRICES, refs[:6])))
        out, x, query, key, value, mixed, first_low, total = refs[6 + len(after) :]
        s = Names(
            query=query,
            key=key,
            value=value,
            mixed=mixed,
            first_low=first_low,
            total=total,
            out=out,
        )

        def work():
            take_rows(content, picks, seq, x)
            forward_attend(x, w, vec, masks.at[seq], s, False)
            forward_feed(w, vec, b_expand, s, False)

        only(info[2], work, out)

    return pl.pallas_call(
        kernel,
        out_shape=shaped((ROWS, D), LOW),
        in_specs=[VMEM] * 11 + [ANY] * len(after),
        out_specs=VMEM,
        scratch_shapes=[pltpu.VMEM((ROWS, D), LOW)]
        + [pltpu.VMEM(*KEPT[n]) for n in ("query", "key", "value", "mixed", "first_low")]
        + [pltpu.VMEM((ROWS, D), WIDE)],
        compiler_params=limit(12),
        cost_estimate=cost(5),
        name="front",
    )(content, picks, masks, vec, b_expand, *matrices, *after)


def front_parts(seq, content, picks, matrices, masks, vec, b_expand):
    def first(content, picks, masks, vec, *refs):
        info = position()
        w = Names(**dict(zip(MATRICES[:4], refs[:4])))
        first_low, total, x, query, key, value, mixed = refs[4:]
        s = Names(
            query=query, key=key, value=value, mixed=mixed, first_low=first_low, total=total
        )

        def work():
            take_rows(content, picks, seq, x)
            forward_attend(x, w, vec, masks.at[seq], s, False)

        only(info[2], work, first_low, total)

    def second(first_low, total_in, vec, b_expand, expand, contract, out, total):
        info = position()
        s = Names(first_low=first_low, total=total, out=out)

        def work():
            total[...] = total_in[...]
            forward_feed(Names(expand=expand, contract=contract), vec, b_expand, s, False)

        only(info[2], work, out)

    first_low, total = pl.pallas_call(
        first,
        out_shape=[shaped((ROWS, D), LOW), shaped((ROWS, D), WIDE)],
        in_specs=[VMEM] * 8,
        out_specs=[VMEM] * 2,
        scratch_shapes=[pltpu.VMEM((ROWS, D), LOW)]
        + [pltpu.VMEM(*KEPT[n]) for n in ("query", "key", "value", "mixed")],
        compiler_params=limit(8),
        cost_estimate=pl.CostEstimate(flops=int(1e10), bytes_accessed=0, transcendentals=0),
        name="front_attend",
    )(content, picks, masks, vec, *matrices[:4])
    return pl.pallas_call(
        second,
        out_shape=shaped((ROWS, D), LOW),
        in_specs=[VMEM] * 6,
        out_specs=VMEM,
        scratch_shapes=[pltpu.VMEM((ROWS, D), WIDE)],
        compiler_params=limit(12),
        cost_estimate=cost(2),
        name="front_feed",
    )(first_low, total, vec, b_expand, *matrices[4:])


def middle_forward(seq, content, picks, arrived, matrices, masks, vec, b_expand, after=()):
    def kernel(arrived, content, picks, masks, vec, b_expand, *refs):
        info = position()
        w, rest = Names(**dict(zip(MATRICES, refs[:6]))), refs[6 + len(after) :]
        (out, early, pair), kept = rest[:3], rest[3 : 3 + len(SAVED)]
        mixed, total = rest[3 + len(SAVED) :]
        x = pair.at[0]
        s = Names(total=total, out=out, mixed=mixed, **dict(zip(SAVED, kept)))
        take_rows(content, picks, seq, x)
        x[...] = jnp.where(info[2], x[...], arrived[...])
        early[:, :D] = x[...]
        forward_attend(x, w, vec, masks.at[seq], s, True)
        forward_feed(w, vec, b_expand, s, True)
        pair[1] = mixed[...]
        early[:, D : 2 * D] = mixed[...]
        early[:, 2 * D : 3 * D] = s.first_low[...]
        early[:, 3 * D :] = columns(s.activated, (1 - info[0]) * HALF, HALF)[...]

    out, early, pair, *saved = pl.pallas_call(
        kernel,
        out_shape=[
            shaped((ROWS, D), WIDE),
            shaped((ROWS, EARLY), LOW),
            shaped((2, ROWS, D), LOW),
        ]
        + [shaped(*KEPT[n]) for n in SAVED],
        in_specs=[VMEM] * 12 + [ANY] * len(after),
        out_specs=[VMEM] * (3 + len(SAVED)),
        scratch_shapes=[pltpu.VMEM(*KEPT["mixed"]), pltpu.VMEM((ROWS, D), WIDE)],
        compiler_params=limit(16),
        cost_estimate=cost(6),
        name="middle_forward",
    )(arrived, content, picks, masks, vec, b_expand, *matrices, *after)
    return (out, early, pair, dict(zip(SAVED, saved)))


FEED_SAVED = ("normed2", "root2", "slope", "normed1", "root1")
ATTEND_SAVED = ("value", "probs", "key", "query")


def middle_back(seq, content, picks, matrices, vec, saved):
    names = FEED_SAVED + ATTEND_SAVED

    def kernel(content, picks, vec, *refs):
        w, rest = Names(**dict(zip(MATRICES, refs[:6]))), refs[6:]
        kept, grad, rest = rest[: len(names)], rest[len(names)], rest[len(names) + 1 :]
        cot, total, branch, expanded, attended, dmixed, dvalue, dquery, dkey = rest
        s = Names(
            total=total,
            branch=branch,
            expanded=expanded,
            attended=attended,
            dmixed=dmixed,
            dvalue=dvalue,
            dquery=dquery,
            dkey=dkey,
            **dict(zip(names, kept)),
        )
        take_rows(content, picks, seq, cot)
        back_second_norm(cot[...], vec, s)
        back_feed(w, vec, s)
        dmixed[...] = nt(attended[...], w.out[...]).astype(LOW)
        back_attend(s)
        lower = total[...] + nt(dquery[...], w.query[...])
        upper = nt(dkey[...], w.key[...]) + nt(dvalue[...], w.value[...])
        grad[:L] = (lower[:L] + upper).astype(LOW)
        grad[L:] = lower[L:].astype(LOW)

    return pl.pallas_call(
        kernel,
        out_shape=shaped((ROWS, D), LOW),
        in_specs=[VMEM] * (9 + len(names)),
        out_specs=VMEM,
        scratch_shapes=[
            pltpu.VMEM((ROWS, D), LOW),
            pltpu.VMEM((ROWS, D), WIDE),
            pltpu.VMEM((ROWS, D), LOW),
            pltpu.VMEM((ROWS, FF), LOW),
            pltpu.VMEM((ROWS, D), LOW),
            pltpu.VMEM((ROWS, D), LOW),
            pltpu.VMEM((L, D), LOW),
            pltpu.VMEM((ROWS, D), LOW),
            pltpu.VMEM((L, D), LOW),
        ],
        compiler_params=limit(12),
        cost_estimate=cost(7),
        name="middle_back",
    )(content, picks, vec, *matrices, *(saved[n] for n in names))


def feed_back(seq, arrived, content, picks, small_in, vec, matrices, saved, after=()):
    given = [] if small_in is None else [small_in]

    def kernel(arrived, content, picks, vec, expand, contract, *refs):
        info = position()
        kept, rest = refs[:5], refs[5 + len(given) + len(after) :]
        total, branch, attended, small, own, late, upper, expanded = rest
        w = Names(expand=expand, contract=contract)
        s = Names(
            total=total,
            branch=branch,
            attended=attended,
            expanded=expanded,
            **dict(zip(FEED_SAVED, kept)),
        )
        small[...] = refs[5][...] if given else jnp.zeros_like(small)

        def add(place, value):
            small[place : place + 1, :] += value

        take_rows(content, picks, seq, upper)
        back_second_norm(jnp.where(info[2], arrived[...], upper[...]), vec, s, add)
        late[:, :D] = branch[...]
        back_feed(w, vec, s, add)
        own[...] = columns(expanded, info[0] * HALF, HALF)[...]
        late[:, D:] = columns(expanded, (1 - info[0]) * HALF, HALF)[...]

    return pl.pallas_call(
        kernel,
        out_shape=[
            shaped((ROWS, D), WIDE),
            shaped((ROWS, D), LOW),
            shaped((ROWS, D), LOW),
            shaped((SMALL, D), WIDE),
            shaped((ROWS, HALF), LOW),
            shaped((ROWS, LATE), LOW),
        ],
        in_specs=[VMEM] * (11 + len(given)) + [ANY] * len(after),
        out_specs=[VMEM] * 6,
        scratch_shapes=[pltpu.VMEM((ROWS, D), LOW), pltpu.VMEM((ROWS, FF), LOW)],
        compiler_params=limit(12),
        cost_estimate=cost(4),
        name="feed_back",
    )(
        arrived,
        content,
        picks,
        vec,
        matrices[4],
        matrices[5],
        *(saved[n] for n in FEED_SAVED),
        *given,
        *after,
    )


PLACES = {
    (2, 0): (0, 0),
    (1, 1): (0, 1),
    (2, 1): (1, 0),
    (3, 0): (1, 1),
    (1, 0): (2, 0),
    (3, 1): (3, 0),
    (0, 0): (4, 0),
    (0, 1): (4, 1),
}


def term_shapes(count, extra=0):
    rows = (2 * count + extra, 2 * count + extra, count, count, 2 * count)
    return [shaped((n, D), LOW) for n in rows]


def feed_grads(mine, branch, own, early, late, after=()):
    def kernel(*refs):
        info = position()
        acts, lows, branches, owns, earlies, lates = (refs[2 * i : 2 * i + 2] for i in range(6))
        refs = refs[:12] + refs[12 + len(after) :]
        outs, (a_act, a_first, b_branch, b_own, stage, out_sems) = refs[12:17], refs[17:]
        core, place = info[0], info[1]
        own_at = [slice(seq * ROWS, (seq + 1) * ROWS) for seq in range(SEQS)]
        far_at = [slice((2 + seq) * ROWS, (3 + seq) * ROWS) for seq in range(SEQS)]
        for seq in range(SEQS):
            at, far = own_at[seq], far_at[seq]
            a_act[at] = columns(acts[seq], core * HALF, HALF)[...]
            a_act[far] = earlies[seq][:, 3 * D :]
            b_branch[at] = branches[seq][...]
            b_branch[far] = lates[seq][:, :D]
        sent = []

        def send(block):
            for k in range(4):
                quarter = lax.rem(place + k, 4)
                index, part = PLACES[k, block // 2]
                start = (2 * part + block % 2) * QUARTER
                sent.extend(
                    start_all(
                        [
                            (
                                rows_at(stage.at[block], quarter * QUARTER, QUARTER),
                                outs[index].at[start : start + QUARTER],
                            )
                        ],
                        out_sems,
                        block * 4 + k,
                    )
                )

        for block in range(2):
            for part in range(3):
                start = block * D + part * 256
                stage[block, part * 256 : (part + 1) * 256] = tn(
                    a_act[:, start : start + 256], b_branch[...]
                ).astype(LOW)
            send(block)
        for seq in range(SEQS):
            at, far = own_at[seq], far_at[seq]
            a_first[at] = lows[seq][...]
            a_first[far] = earlies[seq][:, 2 * D : 3 * D]
            b_own[at] = owns[seq][...]
            b_own[far] = lates[seq][:, D:]
        for block in range(2):
            for part in range(3):
                stage[2 + block, part * 256 : (part + 1) * 256] = tn(
                    a_first[:, part * 256 : (part + 1) * 256], b_own[:, block * D : (block + 1) * D]
                ).astype(LOW)
            send(2 + block)
        wait_all(sent)

    acts = [saved["activated"] for saved in mine]
    lows = [saved["first_low"] for saved in mine]
    return pl.pallas_call(
        kernel,
        out_shape=term_shapes(2 * QUARTER),
        in_specs=[VMEM] * 12 + [ANY] * len(after),
        out_specs=[ANY] * 5,
        scratch_shapes=[
            pltpu.VMEM((2 * ALL_ROWS, HALF), LOW),
            pltpu.VMEM((2 * ALL_ROWS, D), LOW),
            pltpu.VMEM((2 * ALL_ROWS, D), LOW),
            pltpu.VMEM((2 * ALL_ROWS, HALF), LOW),
            pltpu.VMEM((4, D, D), LOW),
            DMA((16,)),
        ],
        compiler_params=limit(16),
        cost_estimate=cost(8),
        name="feed_grads",
    )(*acts, *lows, *branch, *own, *early, *late, *after)


def attend_back(seq, attended, small_in, spread, after, w_out, saved):
    def kernel(attended, small_in, spread, w_out, *refs):
        info = position()
        kept, (pieces, send, small, dmixed, sums) = refs[:4], refs[4 + len(after) :]
        small[...] = small_in[...]
        pieces[1, :ROWS] = attended[...]
        dmixed[...] = nt(attended[...], w_out[...]).astype(LOW)
        s = Names(
            dmixed=dmixed,
            dquery=pieces.at[0, :ROWS],
            dkey=pieces.at[0, ROWS:],
            dvalue=pieces.at[1, ROWS:],
            **dict(zip(ATTEND_SAVED, kept)),
        )
        sums[...] = jnp.zeros_like(sums)

        def table_sum(pair, dscores):
            for odd in range(2):
                part = tn(spread[seq], dscores[odd * ROWS : (odd + 1) * ROWS])
                both = jnp.concatenate([part, jnp.zeros((L, L), WIDE)], axis=1)
                turned = pltpu.roll(both, 0, 1, stride=1, stride_axis=0)
                head = 2 * pair + odd
                sums[head : head + 1, :] = jnp.sum(turned, axis=0, keepdims=True)

        back_attend(s, table_sum)
        send[: ROWS + L] = pieces[1 - info[0]]
        small[S_QUERY : S_QUERY + 1, :] += column_sum(pieces[0, :ROWS])
        small[S_VALUE : S_VALUE + 1, :] += column_sum(pieces[1, ROWS:])
        distance = lax.broadcasted_iota(jnp.int32, (2 * L, L), 0) - (L - 1)
        bucket = lax.broadcasted_iota(jnp.int32, (2 * L, L), 1)
        table = lax.dot_general(
            sums[...],
            (bucket_of(distance) == bucket).astype(WIDE),
            (((1,), (0,)), ((), ())),
            precision=lax.Precision.HIGHEST,
            preferred_element_type=WIDE,
        )
        for column in range(H // 4):
            lanes = slice(column * L, (column + 1) * L)
            small[S_TABLE : S_TABLE + 4, lanes] += table[4 * column : 4 * column + 4]
        send[ROWS + L :] = small[...].astype(LOW)

    return pl.pallas_call(
        kernel,
        out_shape=[
            shaped((2, ROWS + L, D), LOW),
            shaped((ROWS + L + SMALL, D), LOW),
            shaped((SMALL, D), WIDE),
        ],
        in_specs=[VMEM] * 8 + [ANY] * len(after),
        out_specs=[VMEM] * 3,
        scratch_shapes=[pltpu.VMEM((ROWS, D), LOW), pltpu.VMEM((16, 2 * L), WIDE)],
        compiler_params=limit(12),
        cost_estimate=cost(4),
        name="attend_back",
    )(attended, small_in, spread, w_out, *(saved[n] for n in ATTEND_SAVED), *after)


def finish_rows(total, output, pieces, matrices, picks, after):
    def kernel(*refs):
        info = position()
        totals, outputs, pieces = refs[0:2], refs[2:4], refs[4:6]
        (query, key, value), refs = refs[6:9], refs[9 + len(after) :]
        content_ends, query_ends, done = refs
        done[...] = jnp.zeros_like(done)
        first = info[2]
        for seq in range(SEQS):
            lower = totals[seq][...] + nt(pieces[seq][0, :ROWS], query[...])
            upper = nt(pieces[seq][0, ROWS:], key[...]) + nt(pieces[seq][1, ROWS:], value[...])
            content_ends[seq * L : (seq + 1) * L] = jnp.where(
                first, lower[:L] + upper, outputs[seq][:L]
            )
            ends = jnp.where(first, lower[L : L + picks], outputs[seq][L : L + picks])
            for row in range(picks):
                query_ends[seq * picks + row] = ends[row : row + 1]

    return pl.pallas_call(
        kernel,
        out_shape=[shaped((ALL_CONTENT, D), WIDE), shaped((SEQS * picks, 1, D), WIDE), TOKEN],
        in_specs=[VMEM] * 9 + [ANY] * len(after),
        out_specs=[VMEM] * 3,
        compiler_params=limit(12),
        cost_estimate=cost(3),
        name="finish_rows",
    )(*total, *output, *pieces, *matrices[:3], *after)


def attend_grads(pair, early, mine, arrived, small, after=()):
    def kernel(small, *refs):
        info = position()
        pairs_in, earlies, mines, arriveds = (refs[2 * i : 2 * i + 2] for i in range(4))
        refs = refs[8 + len(after) :]
        outs, extra, rest = refs[:5], refs[5], refs[6:]
        a_rows, a_content, b_rows, b_content, stage, out_sems = rest
        core, place = info[0], info[1]
        for seq in range(SEQS):
            at = slice(seq * ROWS, (seq + 1) * ROWS)
            far = slice((2 + seq) * ROWS, (3 + seq) * ROWS)
            a_rows[at] = pairs_in[seq][core]
            a_rows[far] = columns(earlies[seq], core * D, D)[...]
            b_rows[at] = mines[seq][core, :ROWS]
            b_rows[far] = arriveds[seq][:ROWS]
            at = slice(seq * L, (seq + 1) * L)
            far = slice((2 + seq) * L, (3 + seq) * L)
            a_content[at] = pairs_in[seq][0, :L]
            a_content[far] = earlies[seq][:L, :D]
            b_content[at] = mines[seq][core, ROWS:]
            b_content[far] = arriveds[seq][ROWS : ROWS + L]
        far_small = arriveds[1][ROWS + L :]
        extra[...] = (small[...] + far_small.astype(WIDE)).astype(LOW)
        sent = start_all([(extra, outs[i].at[2 * QUARTER :]) for i in range(2)], out_sems, 8)
        for block, (former, latter) in enumerate(((a_rows, b_rows), (a_content, b_content))):
            for part in range(3):
                stage[block, part * 256 : (part + 1) * 256] = tn(
                    former[:, part * 256 : (part + 1) * 256], latter[...]
                ).astype(LOW)
            for k in range(4):
                quarter = lax.rem(place + k, 4)
                index, part = PLACES[k, block]
                start = part * QUARTER
                sent += start_all(
                    [
                        (
                            rows_at(stage.at[block], quarter * QUARTER, QUARTER),
                            outs[index].at[start : start + QUARTER],
                        )
                    ],
                    out_sems,
                    block * 4 + k,
                )
        wait_all(sent)

    return pl.pallas_call(
        kernel,
        out_shape=term_shapes(QUARTER, SMALL) + [shaped((SMALL, D), LOW)],
        in_specs=[VMEM] * 9 + [ANY] * len(after),
        out_specs=[ANY] * 5 + [VMEM],
        scratch_shapes=[
            pltpu.VMEM((2 * ALL_ROWS, D), LOW),
            pltpu.VMEM((2 * ALL_CONTENT, D), LOW),
            pltpu.VMEM((2 * ALL_ROWS, D), LOW),
            pltpu.VMEM((2 * ALL_CONTENT, D), LOW),
            pltpu.VMEM((2, D, D), LOW),
            DMA((10,)),
        ],
        compiler_params=limit(12),
        cost_estimate=cost(5),
        name="attend_grads",
    )(small, *pair, *early, *mine, *arrived, *after)


def small_kernel(body, name, shapes, inputs, after=(), through=()):
    given = len(inputs)

    def kernel(*refs):
        outs = refs[given + len(after) + len(through) :]
        body(*refs[:given], *outs[: len(shapes)])

    return pl.pallas_call(
        kernel,
        out_shape=[shaped(shape, LOW) for shape in shapes]
        + [shaped(array.shape, array.dtype) for array in through],
        in_specs=[VMEM] * len(inputs) + [ANY] * (len(after) + len(through)),
        out_specs=[VMEM] * len(shapes) + [ANY] * len(through),
        input_output_aliases={
            given + len(after) + i: len(shapes) + i for i in range(len(through))
        },
        compiler_params=limit(8),
        cost_estimate=cost(1),
        name=name,
    )(*inputs, *after, *through)


def total_of(*terms):
    return sum(term.astype(WIDE) for term in terms).astype(LOW)


def ring_add(after0, before1, from_left, from_right, after=()):
    count = after0.shape[0]
    extra = from_left.shape[0] - 2 * count

    def body(after0, before1, from_left, from_right, right, left):
        right[:count] = total_of(after0[...], from_left[:count])
        left[:count] = total_of(before1[...], from_right[:count])
        if extra:
            right[count:] = from_left[2 * count :]
            left[count:] = from_right[2 * count :]

    return small_kernel(
        body,
        "ring_add",
        [(count + extra, D)] * 2,
        (after0, before1, from_left, from_right),
        after,
    )


def ring_sum(own, left, right, from_left, from_right, after=(), small=()):
    count = own.shape[0] // 2
    part = count // 4
    extra = sum(array.shape[0] for array in small)

    def body(own, left, right, from_left, from_right, *outs):
        info = position()
        if extra:
            small, outs = outs[0], outs[1:]
            total = total_of(
                small[...], from_left[2 * count :], from_right[2 * count :], left[count:]
            )
        for k, out in enumerate(outs):
            at = pl.multiple_of(lax.rem(info[3] + k, 4) * part, 16)
            low, high = pl.ds(at, part), pl.ds(at + count, part)
            out[:part] = total_of(own[low], left[low], from_right[high])
            out[part : 2 * part] = total_of(own[high], from_left[high], right[low])
            if extra:
                out[2 * part :] = total

    return small_kernel(
        body,
        "ring_sum",
        [(2 * part + extra, D)] * 4,
        (own, left, right, from_left, from_right, *small),
        after,
    )


def add_all(name, terms, after=()):
    def body(*refs):
        refs[-1][...] = total_of(*(ref[...] for ref in refs[:-1]))

    return small_kernel(body, name, [terms[0].shape], terms, after)[0]


def hand_on(arrays, after):
    return small_kernel(lambda *refs: None, "hand_on", [], (), after, arrays)


def z_join(feed, feed_far, attend, attend_far):
    first = feed.shape[0]
    count = attend.shape[0] - SMALL

    def body(feed, feed_far, attend, attend_far, whole, small, table):
        whole[:first] = total_of(feed[...], feed_far[...])
        total = total_of(attend[...], attend_far[...])
        whole[first:] = total[:count]
        small[...] = total[count : count + S_TABLE]
        table[...] = total[count + S_TABLE :]

    shapes = [(first + count, D), (S_TABLE, D), (SMALL - S_TABLE, D)]
    return small_kernel(body, "z_join", shapes, (feed, feed_far, attend, attend_far))


def finish_small(small, table, far, after=()):
    places = [n for n in range(S_TABLE) if not S_EXPAND <= n < S_EXPAND + 4]

    def kernel(small, table, far, *refs):
        vectors, (b_expand, whole, done) = refs[len(after) : -3], refs[-3:]
        done[...] = jnp.zeros_like(done)
        values = small[...].astype(WIDE)
        for place, vector in zip(places, vectors):
            vector[...] = values[place : place + 1]
        for column in range(4):
            lanes = slice(column * D, (column + 1) * D)
            b_expand[:, lanes] = values[S_EXPAND + column : S_EXPAND + column + 1]
        total = table[...].astype(WIDE) + far[...].astype(WIDE)
        heads = [total[:, column * L : (column + 1) * L] for column in range(4)]
        whole[...] = jnp.concatenate(heads)[:H, :NB]

    *vectors, b_expand, whole, done = pl.pallas_call(
        kernel,
        out_shape=[shaped((1, D), WIDE)] * len(places)
        + [shaped((1, FF), WIDE), shaped((H, NB), WIDE), TOKEN],
        in_specs=[VMEM] * 3 + [ANY] * len(after),
        out_specs=[VMEM] * (len(places) + 3),
        compiler_params=limit(4),
        cost_estimate=cost(1),
        name="finish_small",
    )(small, table, far, *after)
    return dict(zip(places, vectors)), b_expand, whole, done


def inner_join(parts):
    counts = (QUARTER // 2, QUARTER // 4)
    half = 4 * sum(counts)

    def body(*refs):
        info = position()
        refs, (whole, right, left) = refs[:-3], refs[-3:]
        start, given = 0, 0
        for count in counts:
            for k, ref in enumerate(refs):
                at = pl.multiple_of(lax.rem(info[3] + k, 4) * count, 16) + start
                whole[pl.ds(at, count)] = ref[given : given + count]
                whole[pl.ds(at + half, count)] = ref[given + count : given + 2 * count]
            start, given = start + 4 * count, given + 2 * count
        kept = pl.multiple_of((1 - info[4]) * QUARTER, QUARTER)
        right[:half] = whole[:half]
        right[half : half + QUARTER] = whole[pl.ds(kept + half, QUARTER)]
        right[half + QUARTER :] = whole[half + 2 * QUARTER :]
        left[:QUARTER] = whole[pl.ds(kept, QUARTER)]
        left[QUARTER:] = whole[2 * QUARTER :]

    shapes = [(2 * half, D)] + [(2 * half - QUARTER, D)] * 2
    return small_kernel(body, "inner_join", shapes, parts)


def cut(before, after_part, after=()):
    rows = before.shape[0]
    half = 3 * QUARTER

    def body(before, after_part, right, left, blocks, both):
        right[...] = before[:half]
        left[...] = after_part[2 * QUARTER :]
        blocks[:QUARTER] = before[half : half + QUARTER]
        blocks[QUARTER:] = after_part[:QUARTER]
        both[:rows] = before[...]
        both[rows:] = after_part[...]

    shapes = [(half, D), (half, D), (2 * QUARTER, D), (2 * rows, D)]
    return small_kernel(body, "cut", shapes, (before, after_part), after)


OUT_SHAPES = ((FF, D), (D, FF)) + ((D, D),) * 4


KEPT_BLOCK, LEFT_BLOCK, SQUARE = 2, 3, 4


def half_places(k, half, blocks=(0, 1)):
    return tuple((k, half, block) for block in (*blocks, SQUARE))


OWN = half_places(0, 0) + half_places(0, 1)
NEAR = (
    half_places(3, 0)
    + half_places(3, 1, (KEPT_BLOCK,))
    + half_places(1, 0, (KEPT_BLOCK,))
    + half_places(1, 1)
)
ACROSS = (half_places(2, 0), half_places(2, 1))
BLOCKS = ((3, 1, LEFT_BLOCK), (1, 0, LEFT_BLOCK))


def out_places(outs, part, half, block, core, quarter, plane):
    if block == SQUARE:
        return [
            (
                core == number,
                part,
                rows_at(outs[2 + 2 * number + half], quarter * QUARTER, QUARTER),
            )
            for number in range(2)
        ]
    if block >= KEPT_BLOCK:
        block = 1 - plane if block == KEPT_BLOCK else plane
    if half == 0:
        start = core * HALF + block * D + quarter * QUARTER
        return [(None, part, rows_at(outs[0], start, QUARTER))]
    rows = rows_at(outs[1], quarter * QUARTER, QUARTER)
    return [(None, part, columns(rows, (core * 2 + block) * D, D))]


def settle(pieces, outs, name, after=()):
    shapes = OUT_SHAPES
    keys = tuple(pieces)
    arrays = [pieces[key] for key in keys]
    given = list(after) + list(outs or ())

    def kernel(*refs):
        info = position()
        parts, rest = refs[: len(keys)], refs[len(keys) + len(given) :]
        outs, rest = rest[: len(shapes)], rest[len(shapes) :]
        done, rest = rest[0], rest[1:]
        done[...] = jnp.zeros_like(done)
        wide_held, out_sems = rest[:-1], rest[-1]
        finish = []
        for index, (sibling, places) in enumerate(keys):
            core = 1 - info[0] if sibling else info[0]
            for number, (k, half, block) in enumerate(places):
                quarter = lax.rem((info[3] if sibling else info[1]) + k, 4)
                at = slice(number * QUARTER, (number + 1) * QUARTER)
                source = wide_held[index].at[at]
                source[...] = parts[index][at].astype(WIDE)
                targets = out_places(outs, source, half, block, core, quarter, info[4])
                for condition, part, target in targets:
                    copy = pltpu.make_async_copy(part, target, out_sems.at[16 * index + number])
                    if condition is None:
                        copy.start()
                        finish.append(copy.wait)
                    else:
                        pl.when(condition)(copy.start)
                        finish.append(lambda c=copy, when=condition: pl.when(when)(c.wait))
        for action in finish:
            action()

    result = pl.pallas_call(
        kernel,
        out_shape=[shaped(shape, WIDE) for shape in shapes]
        + [TOKEN],
        in_specs=[VMEM] * len(keys) + [ANY] * len(given),
        out_specs=[ANY] * len(shapes) + [VMEM],
        scratch_shapes=[pltpu.VMEM(array.shape, WIDE) for array in arrays]
        + [DMA((16 * len(keys),))],
        input_output_aliases={
            len(keys) + len(after) + i: i for i in range(len(outs or ()))
        },
        compiler_params=limit(20),
        cost_estimate=cost(sum(array.size for array in arrays) * 2e-6 + 1),
        name=name,
    )(*arrays, *given)
    return result[:-1], result[-1]


PLANE = ("x", "y", "c")


def shift(value, axis, by):
    size = lax.axis_size(axis)
    return lax.ppermute(value, axis, [(i, (i + by) % size) for i in range(size)])


def send(value, by):
    return lax.ppermute(value, "s", [(0, 1)] if by > 0 else [(1, 0)])


def turn(value, outer, by):
    pairs = []
    for i in range(4):
        for j in range(4):
            for c in range(2):
                if (c == 0) == outer:
                    target = ((i + by) % 4, j)
                else:
                    target = (i, (j + by) % 4)
                pairs.append(((i * 4 + j) * 2 + c, (target[0] * 4 + target[1]) * 2 + c))
    return lax.ppermute(value, PLANE, pairs)


def place(outer):
    return jnp.where(
        (lax.axis_index("c") == 0) == outer, lax.axis_index("x"), lax.axis_index("y")
    )


def wide(value):
    return value.astype(WIDE)


def total_wide(*terms):
    return sum(wide(term) for term in terms)


def inner_turns(parts, sign):
    return [turn(part, False, sign * by) for part, by in zip(parts, (1, 2, -1))]


def both_cores(places, piece):
    return {(0, places): piece, (1, places): shift(piece, "c", 1)}


def on_device(
    content_in,
    query_in,
    content_cot,
    query_cot,
    order_rank,
    query_pos,
    group_tag,
    *rest,
):
    (
        w_query,
        b_query,
        w_key,
        w_value,
        b_value,
        w_out,
        b_out,
        norm1_gain,
        norm1_bias,
        w_expand,
        b_expand,
        w_contract,
        b_contract,
        norm2_gain,
        norm2_bias,
    ) = (argument[0] for argument in rest[:-1])
    rel_table = rest[-1]
    picks = query_pos.shape[1]

    matrices = (w_query, w_key, w_value, w_out, w_expand, w_contract)
    w_out_held = w_out
    vec = jnp.stack(
        [b_query, b_value, b_out, norm1_gain, norm1_bias, b_contract, norm2_gain, norm2_bias]
    )
    ranks = jnp.concatenate([order_rank, group_tag, query_pos], axis=1)
    masks, spread, query_in, query_cot = prepare(
        ranks, rel_table.T, jnp.concatenate([query_in, query_cot]), picks, (vec,)
    )
    b_expand = b_expand[None]

    fronts, arrived = [], []
    for seq in range(SEQS):
        given = (seq, content_in, query_in, matrices, masks, vec, b_expand)
        fronts.append(front(*given, tuple(fronts)) if fronts else front_parts(*given))
        arrived.append(send(fronts[seq], 1))
    output, early, pair, saved, grads = [], [], [], [], []
    for seq in range(SEQS):
        results = middle_forward(
            seq, content_in, query_in, arrived[seq], matrices, masks, vec, b_expand, tuple(grads)
        )
        for collected, result in zip((output, early, pair, saved), results):
            collected.append(result)
        grads.append(middle_back(seq, content_cot, query_cot, matrices, vec, saved[seq]))
    early = [shift(value, "c", 1) for value in early]
    grads = [send(value, -1) for value in grads]
    small = None
    total, branch, attended, own, late, pieces, pass_on = [], [], [], [], [], [], []
    for seq in range(SEQS):
        results = feed_back(
            seq,
            grads[seq],
            content_cot,
            query_cot,
            small,
            vec,
            matrices,
            saved[seq],
            tuple(pass_on),
        )
        small = results[3]
        for collected, result in zip(
            (total, branch, attended, own, late), results[:3] + results[4:]
        ):
            collected.append(result)
        late[seq] = shift(late[seq], "c", 1)
        results = attend_back(
            seq,
            attended[seq],
            small,
            spread,
            (),
            w_out_held,
            saved[seq],
        )
        small = results[2]
        pieces.append(results[0])
        pass_on.append(results[1])
    feed_terms = feed_grads(saved, branch, own, early, late, (small,))
    passed = [shift(value, "c", 1) for value in pass_on]

    def outer_step(terms):
        return (turn(terms[0], True, 1), turn(terms[1], True, -1))

    f_left, f_right = outer_step(feed_terms)
    *attend_terms, extra = attend_grads(pair, early, pieces, passed, small, (feed_terms[4],))
    a_left, a_right = outer_step(attend_terms)
    f_sent = ring_add(feed_terms[2], feed_terms[3], f_left, f_right, (extra,))
    f_outer = outer_step(f_sent)
    a_sent = ring_add(attend_terms[2], attend_terms[3], a_left, a_right)
    f_parts = ring_sum(feed_terms[4], *f_outer, f_left, f_right, (a_sent[0],))
    f_others = inner_turns(f_parts[1:], 1)
    a_parts = ring_sum(
        attend_terms[4], *outer_step(a_sent), a_left, a_right, (f_parts[0],), (extra,)
    )
    f_part = add_all("inner_sum", [f_parts[0]] + f_others, (a_parts[0],))
    f_far = shift(f_part, "z", 1)
    a_part = add_all("inner_sum", [a_parts[0]] + inner_turns(a_parts[1:], 1), (f_part,))
    a_far = shift(a_part, "z", 1)
    part, small, table = z_join(f_part, f_far, a_part, a_far)
    own, to_right, to_left = inner_join([part] + inner_turns([part] * 3, -1))
    before, after_part = turn(to_right, True, 1), turn(to_left, True, -1)
    content_ends, query_ends, token = finish_rows(
        total, output, pieces, matrices, picks, (own,)
    )
    row, b_expand, table, small_token = finish_small(small, table, shift(table, "s", 1), (own,))
    outs, own_token = settle(both_cores(OWN, own), None, "own_out")
    to_right, to_left, blocks, near = cut(before, after_part, (token, small_token, own_token))
    blocks = shift(blocks, "z", 1)
    across = (turn(to_right, True, 1), turn(to_left, True, -1))
    outs, near_token = settle({(0, NEAR): near}, outs, "near_out")
    outs, far_token = settle({(1, NEAR): shift(near, "c", 1)}, outs, "near_out")
    tokens = (near_token, far_token)
    across = hand_on(across, tokens)
    far = {(1, places): shift(piece, "c", 1) for places, piece in zip(ACROSS, across)}
    own = {(0, places): piece for places, piece in zip(ACROSS, across)}
    outs, token = settle(own, outs, "across_out")
    (blocks,) = hand_on((blocks,), (token,))
    outs, _ = settle(far | both_cores(BLOCKS, blocks), outs, "last_out")
    contract, expand, g_query, g_key, g_out, g_value = outs
    return (
        content_ends[None],
        query_ends.transpose(1, 0, 2),
        g_query[None],
        row[S_QUERY],
        g_key[None],
        g_value[None],
        row[S_VALUE],
        g_out[None],
        row[S_OUT],
        row[S_GAIN1],
        row[S_SHIFT1],
        expand[None],
        b_expand,
        contract[None],
        row[S_CONTRACT],
        row[S_GAIN2],
        row[S_SHIFT2],
        table.T,
    )


DP = ("z", "x", "y", "c")


def solution(mesh):
    mesh = jax.sharding.Mesh(mesh.devices.reshape(2, 2, 4, 4, 2), ("s",) + DP)
    layer_specs = tuple(
        P("s", *([None] * (rank - 1))) for rank in (3, 2, 3, 3, 2, 3, 2, 2, 2, 3, 2, 3, 2, 2, 2)
    )
    in_specs = (P(DP, None),) * 7 + layer_specs + (P(),)
    out_specs = (P("s", DP, None),) * 2 + layer_specs + (P(),)
    return jax.shard_map(
        on_device, mesh=mesh, in_specs=in_specs, out_specs=out_specs, check_vma=False
    )
```
